32 devices in a mesh: dp: 16 (over z, y, core), branch: 2 (over x).
Axes of the slice: x: 2, y: 2, z: 4, core: 2. Of those that a mesh axis runs over, the one named last changes fastest.
Arguments:
- tokens: bfloat16 [8192, 512], P(('dp', 'branch')), may hold values from -6 to 6
- wavlm: bfloat16 [8192, 1024], P('dp'), may hold values from -6 to 6
- cotangent: bfloat16 [8192, 512], P(('dp', 'branch')), may hold values from -6 to 6
- lengths: int32 [32, 4], P(('dp', 'branch')), may hold values from 1 to 128, 256 in all within a row
- codes: int32 [8192, 8], P('dp'), may hold values from 0 to 2047
- enc_qkv: bfloat16 [512, 1536], replicated, may hold values from -0.25 to 0.25
- enc_out: bfloat16 [512, 512], replicated, may hold values from -1 to 1
- enc_up: bfloat16 [512, 2048], replicated, may hold values from -0.25 to 0.25
- enc_down: bfloat16 [2048, 512], replicated, may hold values from -0.125 to 0.125
- dec_qkv: bfloat16 [512, 1536], replicated, may hold values from -0.25 to 0.25
- dec_out: bfloat16 [512, 512], replicated, may hold values from -1 to 1
- dec_up: bfloat16 [512, 2048], replicated, may hold values from -0.25 to 0.25
- dec_down: bfloat16 [2048, 512], replicated, may hold values from -0.125 to 0.125
- vectors: float32 [2, 4, 512], replicated, may hold values from 0.25 to 1.75
- proj_in: bfloat16 [2, 512, 256], P('branch'), may hold values from -0.25 to 0.25
- proj_out: bfloat16 [2, 256, 512], P('branch'), may hold values from -0.375 to 0.375
- codebooks: bfloat16 [8, 2048, 256], replicated, may hold values from -6 to 6
- distill_proj: bfloat16 [256, 1024], replicated, may hold values from -0.375 to 0.375
Outputs:
- decoded: bfloat16 [8192, 512], P(('dp', 'branch'))
- input_grad: float32 [8192, 512], P(('dp', 'branch'))
- enc_qkv_grad: float32 [786432], P(('dp', 'branch'))
- enc_out_grad: float32 [262144], P(('dp', 'branch'))
- enc_up_grad: float32 [1048576], P(('dp', 'branch'))
- enc_down_grad: float32 [1048576], P(('dp', 'branch'))
- dec_qkv_grad: float32 [786432], P(('dp', 'branch'))
- dec_out_grad: float32 [262144], P(('dp', 'branch'))
- dec_up_grad: float32 [1048576], P(('dp', 'branch'))
- dec_down_grad: float32 [1048576], P(('dp', 'branch'))
- vectors_grad: float32 [4096], P(('dp', 'branch'))
- proj_in_grad: float32 [262144], P(('dp', 'branch'))
- proj_out_grad: float32 [262144], P(('dp', 'branch'))
- codebooks_grad: float32 [4194304], P(('dp', 'branch'))
- distill_grad: float32 [262144], P(('dp', 'branch'))
The draws below stay inside these ranges and needn't reach their ends.
Inputs may be any that keep to these rules, and one draw needn't show every extreme that they name: `lengths`: each row holds the frame counts of the clips packed on one device, in order; they sum to 256, and the longest clip of each row has 128 frames.
All inputs are finite; a program needn't handle non-finite values.
Results may differ from the reference program's by a relative error of at most 0.025.
Values may be sent and summed in bfloat16 or wider, within the bound.
A program may use at most 192 MiB of HBM per device.

```python
import math
import jax
import jax.numpy as jnp
import numpy as np
from jax import lax

D = 512
HEADS = 8
FF = 2048
CB = 2048
CODE = 256
WAVLM = 1024
LEVELS = 8
WINDOW = 250
TOK_DEV = 256
CLIPS_DEV = 4
MOST = 128
TOKENS = 8192
N_DP = 16
N_BRANCH = 2


def place_ends(entries, key, low, high):
    dims = entries.shape
    index_at = [jax.random.randint(jax.random.fold_in(key, axis), (), 0, dims[axis]) for axis in range(len(dims))]
    entries = entries.at[tuple(index_at)].set(low)
    longest = dims.index(max(dims))
    index_at[longest] = (index_at[longest] + 1) % dims[longest]
    return entries.at[tuple(index_at)].set(high)


def level_of(key, shape, cuts, low, largest):
    def one(dim, blocks):
        heights = jax.random.uniform(jax.random.fold_in(jax.random.fold_in(key, 6), dim), (blocks,), jnp.float32, low / len(cuts), largest / len(cuts))
        return jnp.repeat(jnp.exp(heights), shape[dim] // blocks).reshape((-1,) + (1,) * (len(shape) - dim - 1))

    gain = one(*cuts[0])
    for cut in cuts[1:]:
        gain = gain * one(*cut)
    return gain


def length_profile(count, total, limit, skew):
    weights = [(1 << 20) // math.isqrt(grade ** skew) + 1 for grade in range(2, count + 1)]
    surplus, given = total - limit - (count - 1), [1] * (count - 1)
    while surplus > 0:
        candidates = [i for i in range(count - 1) if given[i] < limit]
        mass, budget = sum([weights[i] for i in candidates]), surplus
        for i in candidates:
            more = min(limit - given[i], max(1, budget * weights[i] // mass), surplus)
            given[i] = given[i] + more
            surplus = surplus - more
    return np.array([limit] + given)


def ragged(own_key, amount, total, limit, lean):
    if amount == 2:
        one = jax.random.randint(own_key, (), max(1, total - limit), min(limit, total - 1) + 1)
        return jnp.stack([one, total - one])
    sizes = jnp.asarray(length_profile(amount, total, limit, lean), jnp.int32)
    couples = (amount - 1) // 2
    source_of, receiver = sizes[1:1 + 2 * couples:2], sizes[2:2 + 2 * couples:2]
    slack = jnp.minimum(source_of - 1, limit - receiver)
    moved = jax.random.randint(jax.random.fold_in(own_key, 1), (couples,), 0, 1 << 20) % (slack + 1)
    sizes = sizes.at[1:1 + 2 * couples:2].set(source_of - moved).at[2:2 + 2 * couples:2].set(receiver + moved)
    return sizes[jax.random.permutation(jax.random.fold_in(own_key, 2), amount)]


def bell_draw(stream_key, shape, spread, bound, cuts=(), kind=jnp.bfloat16):
    result = jax.random.normal(stream_key, shape, jnp.float32) * spread
    if len(cuts) > 0:
        result = level_of(stream_key, shape, cuts, -0.22, 0.18) * result
    return jnp.clip(result, min=-bound, max=bound).astype(kind)


def setup_inputs(seed: int = 0) -> dict:
    key_of = jax.random.split(jax.random.key(seed), 19)
    tokens = bell_draw(key_of[0], (TOKENS, D), 1.0, 6.0, ((0, 32),))
    wavlm = bell_draw(key_of[1], (TOKENS, WAVLM), 1.0, 6.0, ((0, 16),))
    cotangent = bell_draw(key_of[2], (TOKENS, D), 1.0, 6.0, ((0, 32),))
    lengths = jax.vmap(lambda own: ragged(own, CLIPS_DEV, TOK_DEV, MOST, 2))(jax.random.split(key_of[3], (N_DP * N_BRANCH))).reshape((N_DP * N_BRANCH, CLIPS_DEV)).astype(jnp.int32)
    codes = place_ends(jax.random.randint(key_of[4], (TOKENS, LEVELS), 0, CB), jax.random.fold_in(key_of[4], 1), 0, CB - 1).astype(jnp.int32)
    enc_qkv = bell_draw(key_of[5], (D, 3 * D), D ** -0.5, 0.25)
    enc_out = bell_draw(key_of[6], (D, D), (D // 16) ** -0.5, 1.0)
    enc_up = bell_draw(key_of[7], (D, FF), D ** -0.5, 0.25)
    enc_down = bell_draw(key_of[8], (FF, D), FF ** -0.5, 0.125)
    dec_qkv = bell_draw(key_of[9], (D, 3 * D), D ** -0.5, 0.25)
    dec_out = bell_draw(key_of[10], (D, D), (D // 16) ** -0.5, 1.0)
    dec_up = bell_draw(key_of[11], (D, FF), D ** -0.5, 0.25)
    dec_down = bell_draw(key_of[12], (FF, D), FF ** -0.5, 0.125)
    vectors = jnp.clip(1.0 + 0.15 * jax.random.normal(key_of[13], (2, 4, D), jnp.float32), 0.25, 1.75)
    proj_in = bell_draw(key_of[14], (N_BRANCH, D, CODE), D ** -0.5, 0.25, ((0, 2),))
    proj_out = bell_draw(key_of[15], (N_BRANCH, CODE, D), CODE ** -0.5, 0.375, ((0, 2),))
    codebooks = bell_draw(key_of[16], (LEVELS, CB, CODE), 1.0, 6.0)
    distill_proj = bell_draw(key_of[17], (CODE, WAVLM), CODE ** -0.5, 0.375)
    return dict(tokens=tokens, wavlm=wavlm, cotangent=cotangent, lengths=lengths, codes=codes, enc_qkv=enc_qkv, enc_out=enc_out, enc_up=enc_up, enc_down=enc_down, dec_qkv=dec_qkv, dec_out=dec_out, dec_up=dec_up, dec_down=dec_down, vectors=vectors, proj_in=proj_in, proj_out=proj_out, codebooks=codebooks, distill_proj=distill_proj)


@jax.custom_vjp
def low(v):
    return lax.optimization_barrier(v.astype(jnp.bfloat16)).astype(jnp.float32)

@jax.custom_vjp
def low_back(v):
    return v

def low_keep(v):
    return (low(v), None)

def low_pass(kept, grad):
    return (grad,)

def back_keep(v):
    return (v, None)

def back_low(kept, grad):
    return (low(grad),)
low.defvjp(low_keep, low_pass)
low_back.defvjp(back_keep, back_low)
EPS_NORM = 1e-05
EPS_COS = 1e-06
BETA = 0.25
DISTILL = 10.0
ROPE_BASE = 10000.0
HIGH = lax.Precision.HIGHEST

def widen(array):
    return array.astype(jnp.float32)

def project(left, right):
    return jnp.einsum('...d,de->...e', left, right, precision=HIGH)

def clip_layout(clip_lengths, row_count):
    clip_ends = jnp.cumsum(clip_lengths).astype(jnp.int32)
    clip_starts = clip_ends - clip_lengths
    position = jnp.arange(row_count, dtype=jnp.int32)
    inside = (position[:, None] >= clip_starts[None, :]) & (position[:, None] < clip_ends[None, :])
    numbers = jnp.arange(clip_lengths.shape[0], dtype=jnp.int32)
    clip_id = lax.optimization_barrier(jnp.sum(jnp.where(inside, numbers[None, :], 0), axis=1)).astype(jnp.int32)
    offset = position - lax.optimization_barrier(jnp.sum(jnp.where(inside, clip_starts[None, :], 0), axis=1)).astype(jnp.int32)
    return (clip_id, offset)

def rope_tables(offset, head_width):
    half_width = head_width // 2
    inverse_rate = ROPE_BASE ** (-jnp.arange(half_width, dtype=jnp.float32) / half_width)
    angle = offset.astype(jnp.float32)[..., None] * inverse_rate
    return (jnp.cos(angle)[..., None, :], jnp.sin(angle)[..., None, :])

def rotate(stream, cos_table, sin_table):
    half_width = stream.shape[-1] // 2
    front_half = stream[..., :half_width]
    back_half = stream[..., half_width:]
    return jnp.concatenate([front_half * cos_table - back_half * sin_table, front_half * sin_table + back_half * cos_table], axis=-1)

def norm_scale(stream):
    return lax.rsqrt(lax.optimization_barrier(jnp.mean(stream * stream, axis=-1, keepdims=True)) + EPS_NORM)

def attend_pack(packed):
    query_rows, key_rows, value_rows, clip_id = packed
    row_count = query_rows.shape[0]
    scaling = query_rows.shape[-1] ** (-0.5)
    scores = low_back(jnp.einsum('qhd,khd->hqk', query_rows, key_rows, precision=HIGH) * scaling)
    position = jnp.arange(row_count, dtype=jnp.int32)
    allowed = (clip_id[:, None] == clip_id[None, :]) & (position[None, :] <= position[:, None]) & (position[:, None] - position[None, :] < WINDOW)
    scores = jnp.where(allowed[None], scores, -1e+30)
    peak_score = lax.optimization_barrier(jnp.max(scores, axis=-1, keepdims=True))
    weights = jnp.exp(scores - peak_score)
    attention = low(weights / lax.optimization_barrier(jnp.sum(weights, axis=-1, keepdims=True)))
    return jnp.einsum('hqk,khd->qhd', attention, value_rows, precision=HIGH)

def block_layer(stream, matrices, gains, clip_id, offset):
    w_qkv, w_out, w_up, w_down = matrices
    blocks, row_count, width = stream.shape
    head_shape = (blocks, row_count, HEADS, width // HEADS)
    h_one = low(stream * norm_scale(stream) * gains[0])
    qkv = low_back(project(h_one, w_qkv))
    query_rows, key_rows, value_rows = jnp.split(qkv, 3, axis=-1)
    cos_table, sin_table = rope_tables(offset, width // HEADS)
    query_rows = low(rotate(query_rows.reshape(head_shape), cos_table, sin_table))
    key_rows = low(rotate(key_rows.reshape(head_shape), cos_table, sin_table))
    value_rows = low(value_rows.reshape(head_shape))
    mixed = lax.map(jax.checkpoint(attend_pack), (query_rows, key_rows, value_rows, clip_id))
    mixed = low(low_back(mixed.reshape(blocks, row_count, width)))
    attn_out = low_back(project(mixed, w_out))
    stream_two = stream + gains[1] * attn_out
    h_two = low(stream_two * norm_scale(stream_two) * gains[2])
    pre_act = low_back(project(h_two, w_up))
    ffn_out = low_back(project(low(jax.nn.gelu(pre_act)), w_down))
    return stream_two + gains[3] * ffn_out

def reference(tokens, wavlm, cotangent, lengths, codes, enc_qkv, enc_out, enc_up, enc_down, dec_qkv, dec_out, dec_up, dec_down, vectors, proj_in, proj_out, codebooks, distill_proj):
    blocks = lengths.shape[0]
    row_count = tokens.shape[0] // blocks
    width = tokens.shape[1]
    groups = blocks // N_BRANCH
    pair_rows = N_BRANCH * row_count
    clip_id, offset = jax.vmap(clip_layout, in_axes=(0, None))(lengths, row_count)
    stream = widen(tokens).reshape(blocks, row_count, width)
    enc_mats = (widen(enc_qkv), widen(enc_out), widen(enc_up), widen(enc_down))
    dec_mats = (widen(dec_qkv), widen(dec_out), widen(dec_up), widen(dec_down))
    gain_all = widen(vectors)
    pin = widen(proj_in)
    pout = widen(proj_out)
    books = widen(codebooks)
    distill_w = widen(distill_proj)
    code_rows = codes.reshape(groups, pair_rows, LEVELS)
    target = widen(wavlm).reshape(groups, pair_rows, -1)

    def encode(stream_in, mats_in, gains_in):
        return block_layer(stream_in, mats_in, gains_in[0], clip_id, offset)
    latent, encode_back = jax.vjp(encode, stream, enc_mats, gain_all)
    latent_value = low(latent).reshape(groups, pair_rows, width)
    anchor_sem = project(latent_value, pin[0])
    anchor_ac = project(latent_value, pin[1])

    def rest(latent_in, mats_in, gains_in, pin_in, pout_in, books_in, distill_in):
        pair = low(latent_in).reshape(groups, pair_rows, width)
        sem_proj = low_back(project(pair, pin_in[0]))
        ac_proj = low_back(project(pair, pin_in[1]))
        chosen = books_in[0][code_rows[..., 0]]
        commit = jnp.sum((sem_proj - chosen) ** 2)
        sem_code = low(sem_proj + (chosen - anchor_sem))
        residual = ac_proj
        picked = jnp.zeros_like(ac_proj)
        for level in range(1, LEVELS):
            chosen = books_in[level][code_rows[..., level]]
            commit = commit + jnp.sum((residual - chosen) ** 2)
            residual = residual - chosen
            picked = picked + chosen
        ac_code = low(ac_proj + (picked - anchor_ac))
        prediction = low_back(project(sem_code, distill_in))
        pred_norm = jnp.sqrt(lax.optimization_barrier(jnp.sum(prediction * prediction, axis=-1)) + EPS_COS)
        target_norm = jnp.sqrt(lax.optimization_barrier(jnp.sum(target * target, axis=-1)) + EPS_COS)
        cosine = lax.optimization_barrier(jnp.sum(prediction * target, axis=-1)) / (pred_norm * target_norm)
        loss_value = BETA * commit + DISTILL * jnp.sum(1.0 - cosine)
        quant = project(sem_code, pout_in[0]) + project(ac_code, pout_in[1])
        quant = low_back(quant.reshape(blocks, row_count, width))
        decoded = block_layer(quant, mats_in, gains_in[1], clip_id, offset)
        return (decoded, loss_value)
    (decoded, loss_value), rest_back = jax.vjp(rest, latent, dec_mats, gain_all, pin, pout, books, distill_w)
    grad_latent, grad_dec, gain_rest, grad_pin, grad_pout, grad_books, grad_distill = rest_back((widen(cotangent).reshape(blocks, row_count, width), jnp.ones_like(loss_value)))
    grad_stream, grad_enc, gain_enc = encode_back(grad_latent)
    return (decoded.reshape(-1, width).astype(jnp.bfloat16), grad_stream.reshape(-1, width), grad_enc[0].reshape(-1), grad_enc[1].reshape(-1), grad_enc[2].reshape(-1), grad_enc[3].reshape(-1), grad_dec[0].reshape(-1), grad_dec[1].reshape(-1), grad_dec[2].reshape(-1), grad_dec[3].reshape(-1), (gain_rest + gain_enc).reshape(-1), grad_pin.reshape(-1), grad_pout.reshape(-1), grad_books.reshape(-1), grad_distill.reshape(-1))
```

```python
import functools

import jax
import jax.numpy as jnp
from jax import lax
from jax.experimental import pallas as pl
from jax.experimental.pallas import tpu as pltpu
from jax.sharding import PartitionSpec as P

MESH = pl.DeviceIdType.MESH

HEADS = 8
WINDOW = 250


EPS_NORM = 1e-05
EPS_COS = 1e-06
BETA = 0.25
DISTILL = 10.0
ROPE_BASE = 10000.0


def contract_rows(left, right):
    return lax.dot_general(
        left, right, (((0,), (0,)), ((), ())), preferred_element_type=jnp.float32
    )


def times_transpose(left, right):
    return lax.dot_general(
        left, right, (((1,), (1,)), ((), ())), preferred_element_type=jnp.float32
    )


def clip_layout(clip_lengths, row_count):
    clip_ends = jnp.cumsum(clip_lengths)
    clip_starts = clip_ends - clip_lengths
    position = jnp.arange(row_count, dtype=jnp.int32)
    inside = (position[:, None] >= clip_starts[None, :]) & (position[:, None] < clip_ends[None, :])
    numbers = jnp.arange(clip_lengths.shape[0], dtype=jnp.int32)
    clip_id = jnp.sum(jnp.where(inside, numbers[None, :], 0), axis=1)
    offset = position - jnp.sum(jnp.where(inside, clip_starts[None, :], 0), axis=1)
    return (clip_id, offset)


def rope_tables(offset, head_width):
    half_width = head_width // 2
    inverse_rate = ROPE_BASE ** (-jnp.arange(half_width, dtype=jnp.float32) / half_width)
    angle = offset.astype(jnp.float32)[..., None] * inverse_rate
    return (jnp.cos(angle)[..., None, :], jnp.sin(angle)[..., None, :])


def rotate(stream, cos_table, sin_table):
    half_width = stream.shape[-1] // 2
    front_half = stream[..., :half_width]
    back_half = stream[..., half_width:]
    return jnp.concatenate(
        [
            front_half * cos_table - back_half * sin_table,
            front_half * sin_table + back_half * cos_table,
        ],
        axis=-1,
    )


def norm_scale(stream):
    return lax.rsqrt(jnp.mean(stream * stream, axis=-1, keepdims=True) + EPS_NORM)


def norm_back(stream, inverse, grad_in):
    return inverse * grad_in - stream * (inverse * inverse * inverse) * jnp.mean(
        grad_in * stream, axis=-1, keepdims=True
    )


def masked_scores(query_rows, key_rows, scaling, allowed):
    scores = (
        jnp.einsum("qhd,khd->hqk", query_rows, key_rows, preferred_element_type=jnp.float32)
        * scaling
    )
    return jnp.where(allowed[None], scores, -1e30)


def layer_forward(stream, matrices, gains, cos_table, sin_table, allowed):
    w_qkv, w_out, w_up, w_down = matrices
    row_count, width = stream.shape
    head_shape = (row_count, HEADS, width // HEADS)
    scaling = (width // HEADS) ** (-0.5)
    inverse_one = norm_scale(stream)
    h_one = (stream * inverse_one * gains[0]).astype(jnp.bfloat16)
    qkv = jnp.dot(h_one, w_qkv, preferred_element_type=jnp.float32)
    query_rows, key_rows, value_rows = jnp.split(qkv, 3, axis=1)
    query_rows = rotate(query_rows.reshape(head_shape), cos_table, sin_table).astype(jnp.bfloat16)
    key_rows = rotate(key_rows.reshape(head_shape), cos_table, sin_table).astype(jnp.bfloat16)
    value_rows = value_rows.reshape(head_shape).astype(jnp.bfloat16)
    scores = masked_scores(query_rows, key_rows, scaling, allowed)
    peak_score = jnp.max(scores, axis=-1, keepdims=True)
    weights = jnp.exp(scores - peak_score)
    total = jnp.sum(weights, axis=-1, keepdims=True)
    attention = (weights / total).astype(jnp.bfloat16)
    log_total = peak_score + jnp.log(total)
    mixed = jnp.einsum("hqk,khd->qhd", attention, value_rows, preferred_element_type=jnp.float32)
    mixed = mixed.reshape(row_count, width).astype(jnp.bfloat16)
    attn_out = jnp.dot(mixed, w_out, preferred_element_type=jnp.float32)
    stream_two = stream + gains[1] * attn_out
    inverse_two = norm_scale(stream_two)
    h_two = (stream_two * inverse_two * gains[2]).astype(jnp.bfloat16)
    pre_act = jnp.dot(h_two, w_up, preferred_element_type=jnp.float32)
    activated = jax.nn.gelu(pre_act).astype(jnp.bfloat16)
    ffn_out = jnp.dot(activated, w_down, preferred_element_type=jnp.float32)
    result = stream_two + gains[3] * ffn_out
    kept = (
        stream,
        inverse_one,
        h_one,
        query_rows,
        key_rows,
        value_rows,
        log_total,
        mixed,
        attn_out,
        stream_two,
        inverse_two,
        h_two,
        pre_act,
        activated,
        ffn_out,
    )
    return (result, kept)


def layer_backward(grad_out, kept, matrices, gains, cos_table, sin_table, allowed):
    w_qkv, w_out, w_up, w_down = matrices
    (
        stream,
        inverse_one,
        h_one,
        query_rows,
        key_rows,
        value_rows,
        log_total,
        mixed,
        attn_out,
        stream_two,
        inverse_two,
        h_two,
        pre_act,
        activated,
        ffn_out,
    ) = kept
    row_count, width = stream.shape
    head_shape = (row_count, HEADS, width // HEADS)
    scaling = (width // HEADS) ** (-0.5)
    scale_two = jnp.sum(grad_out * ffn_out, axis=0)
    grad_ffn = (gains[3] * grad_out).astype(jnp.bfloat16)
    grad_down = contract_rows(activated, grad_ffn)
    grad_act = times_transpose(grad_ffn, w_down)
    gelu_back = jax.vjp(jax.nn.gelu, pre_act)[1]
    grad_pre = gelu_back(grad_act)[0].astype(jnp.bfloat16)
    grad_up = contract_rows(h_two, grad_pre)
    grad_htwo = times_transpose(grad_pre, w_up)
    gain_two = jnp.sum(grad_htwo * stream_two * inverse_two, axis=0)
    grad_stream = grad_out + norm_back(stream_two, inverse_two, grad_htwo * gains[2])
    scale_one = jnp.sum(grad_stream * attn_out, axis=0)
    grad_attn = (gains[1] * grad_stream).astype(jnp.bfloat16)
    grad_wout = contract_rows(mixed, grad_attn)
    grad_mixed = times_transpose(grad_attn, w_out).astype(jnp.bfloat16).reshape(head_shape)
    scores = masked_scores(query_rows, key_rows, scaling, allowed)
    attention = jnp.exp(scores - log_total)
    grad_value = jnp.einsum(
        "hqk,qhd->khd",
        attention.astype(jnp.bfloat16),
        grad_mixed,
        preferred_element_type=jnp.float32,
    )
    grad_weights = jnp.einsum(
        "qhd,khd->hqk", grad_mixed, value_rows, preferred_element_type=jnp.float32
    )
    grad_scores = attention * (
        grad_weights - jnp.sum(attention * grad_weights, axis=-1, keepdims=True)
    )
    grad_scores = grad_scores.astype(jnp.bfloat16)
    grad_query = (
        jnp.einsum("hqk,khd->qhd", grad_scores, key_rows, preferred_element_type=jnp.float32)
        * scaling
    )
    grad_key = (
        jnp.einsum("hqk,qhd->khd", grad_scores, query_rows, preferred_element_type=jnp.float32)
        * scaling
    )
    grad_qkv = jnp.concatenate(
        [
            rotate(grad_query, cos_table, -sin_table).reshape(row_count, width),
            rotate(grad_key, cos_table, -sin_table).reshape(row_count, width),
            grad_value.reshape(row_count, width),
        ],
        axis=1,
    ).astype(jnp.bfloat16)
    grad_wqkv = contract_rows(h_one, grad_qkv)
    grad_hone = times_transpose(grad_qkv, w_qkv)
    gain_one = jnp.sum(grad_hone * stream * inverse_one, axis=0)
    grad_input = grad_stream + norm_back(stream, inverse_one, grad_hone * gains[0])
    gain_grads = jnp.stack([gain_one, scale_one, gain_two, scale_two])
    return (grad_input, (grad_wqkv, grad_wout, grad_up, grad_down), gain_grads)


def plan_events(sizes, orders, bits):
    core = bits - 2
    free = {}
    done = {}
    ready = [(0.0, k, 0) for k in range(len(sizes))]
    events = []
    while ready:
        ready.sort()
        best = None
        for at, k, s in ready:
            dim = orders[k][s]
            begin = max(at, free.get(link_of(dim, bits), 0.0))
            if best is None or begin < best[0]:
                best = (begin, k, s)
        begin, k, s = best
        ready = [r for r in ready if r[1:] != (k, s)]
        dim = orders[k][s]
        rate = 600e3 if dim == core else 50e3
        took = sizes[k] / 2 ** (s + 1) / rate * (2 if dim < bits - 4 else 1)
        free[link_of(dim, bits)] = begin + took
        done[(k, s)] = begin + took + 1.5
        if s + 1 < bits:
            ready.append((begin + took + 1.5, k, s + 1))
    return sorted(done, key=lambda e: (done[e], e))


def link_of(dim, bits):
    return "z" if dim < bits - 3 else dim


def other_half(ref, position, index):
    return ref.at[(slice(None),) * position + (index,)]


def coordinates(step, count):
    return [step // 2 ** (count - 1 - i) % 2 for i in range(count)]


def store_flat(out_ref, value, folded):
    rows, columns = value.shape
    if folded:
        rows, columns = rows // folded, columns
        blocks = columns // 128
        for part in range(folded):
            for i in range(blocks):
                out_ref[pl.ds(part * blocks + i, rows, stride=folded * blocks), :] = value[
                    part * rows : (part + 1) * rows, i * 128 : (i + 1) * 128
                ]
        return
    blocks = columns // 128
    if blocks == 1:
        out_ref[...] = value[: out_ref.shape[0]]
        return
    for i in range(blocks):
        out_ref[pl.ds(i, rows, stride=blocks), :] = value[:, i * 128 : (i + 1) * 128]


def scatter_kernel(orders, folds, views, events, bits, n_in, *refs):
    count = len(orders)
    in_refs = refs[:n_in]
    out_refs = refs[n_in : 2 * n_in]
    own = refs[2 * n_in : 2 * n_in + count]
    recv = [refs[2 * n_in + count + k * bits : 2 * n_in + count + (k + 1) * bits] for k in range(count)]
    send_sem, recv_sem, own_sem = refs[2 * n_in + count + count * bits :]
    dp = lax.axis_index("dp")
    branch = lax.axis_index("branch")
    mine, partner = [], []
    for dim in range(bits - 1):
        weight = 2 ** (bits - 2 - dim)
        bit = dp // weight % 2
        mine.append(bit)
        partner.append({"dp": dp + weight * (1 - 2 * bit), "branch": branch})
    mine.append(branch)
    partner.append({"dp": dp, "branch": 1 - branch})

    barrier = pltpu.get_barrier_semaphore()
    for target in partner:
        pl.semaphore_signal(barrier, inc=1, device_id=target, device_id_type=MESH)
    pl.semaphore_wait(barrier, bits)

    def source(k):
        which, part = views[k]
        ref = in_refs[which]
        return ref if part is None else ref.at[(slice(None),) * bits + (part,)]

    copies = {}
    own_copies = {}

    def remaining(k, stage):
        return [d for d in range(bits) if d not in orders[k][:stage]]

    def start(k, stage):
        dim = orders[k][stage]
        ref = source(k) if stage == 0 else recv[k][stage - 1]
        position = remaining(k, stage).index(dim)
        copies[(k, stage)] = pltpu.make_async_remote_copy(
            src_ref=other_half(ref, position, 1 - mine[dim]),
            dst_ref=recv[k][stage],
            send_sem=send_sem.at[k, stage],
            recv_sem=recv_sem.at[k, stage],
            device_id=partner[dim],
            device_id_type=MESH,
        )
        copies[(k, stage)].start()

    def finish(k, stage):
        dim = orders[k][stage]
        left = remaining(k, stage)
        position = left.index(dim)
        copies[(k, stage)].wait_recv()
        got = recv[k][stage]
        depth = bits - 1 - stage
        if stage == 0:
            own_copies[k].wait()

        def have(where):
            if stage == 0:
                return own[k][tuple(where)]
            return recv[k][stage - 1][tuple(where[:position] + [mine[dim]] + where[position:])]

        if stage == bits - 1:
            total = have([]).astype(jnp.float32) + got[...].astype(jnp.float32)
            which, part = views[k]
            out_ref = out_refs[which]
            if part is not None:
                out_ref = out_ref.at[part]
            store_flat(out_ref, total, folds[k])
            return

        def add(step, carry):
            where = coordinates(step, depth)
            got[tuple(where)] = got[tuple(where)] + have(where)
            return carry

        lax.fori_loop(0, 2**depth, add, 0)

    for k in range(count):
        start(k, 0)
        dim = orders[k][0]
        own_copies[k] = pltpu.make_async_copy(
            other_half(source(k), remaining(k, 0).index(dim), mine[dim]), own[k], own_sem.at[k]
        )
        own_copies[k].start()
    for k, stage in events:
        finish(k, stage)
        if stage + 1 < bits:
            start(k, stage + 1)
    for copy in copies.values():
        copy.wait_send()


def scatter_sums(parts, devices):
    bits = devices.bit_length() - 1
    core, x = bits - 2, bits - 1
    y, z = bits - 3, list(range(bits - 3))[::-1]
    kinds = {
        "x": [core, x, y] + z,
        "y": [core, y, x] + z,
        "z": [core] + z + [x, y],
        "w": [core] + z + [y, x],
    }
    ins, outs, orders, folds, views, shapes = [], [], [], [], [], []
    for which, (array, fold, kind) in enumerate(parts):
        ins.append(array.reshape((2,) * bits + array.shape[1:]))
        rows, columns = array.shape[-2:]
        if array.ndim == 4:
            outs.append(jax.ShapeDtypeStruct((array.shape[1], rows * columns // 128, 128), jnp.float32))
            for part in range(array.shape[1]):
                orders.append(kinds[kind[part]])
                folds.append(fold)
                views.append((which, part))
                shapes.append((rows, columns))
        else:
            flat = rows * columns // 128 if columns > 128 else 1
            outs.append(jax.ShapeDtypeStruct((flat, 128), jnp.float32))
            orders.append(kinds[kind])
            folds.append(fold)
            views.append((which, None))
            shapes.append((rows, columns))
    count = len(orders)
    sizes = [devices * rows * columns * 2 for rows, columns in shapes]
    events = plan_events(sizes, orders, bits)
    scratch = [pltpu.VMEM((2,) * (bits - 1) + shape, jnp.bfloat16) for shape in shapes]
    for shape in shapes:
        for stage in range(bits):
            scratch.append(pltpu.VMEM((2,) * (bits - 1 - stage) + shape, jnp.bfloat16))
    scratch += [
        pltpu.SemaphoreType.DMA((count, bits)),
        pltpu.SemaphoreType.DMA((count, bits)),
        pltpu.SemaphoreType.DMA((count,)),
    ]
    return pl.pallas_call(
        functools.partial(scatter_kernel, orders, folds, views, events, bits, len(ins)),
        out_shape=outs,
        in_specs=[pl.BlockSpec(memory_space=pl.ANY)] * len(ins),
        out_specs=[pl.BlockSpec(memory_space=pltpu.VMEM)] * len(ins),
        scratch_shapes=scratch,
        compiler_params=pltpu.CompilerParams(
            collective_id=0, has_side_effects=True, vmem_limit_bytes=56 * 2**20
        ),
    )(*ins)


def body(
    tokens,
    wavlm,
    cotangent,
    lengths,
    codes,
    enc_qkv,
    enc_out,
    enc_up,
    enc_down,
    dec_qkv,
    dec_out,
    dec_up,
    dec_down,
    vectors,
    proj_in,
    proj_out,
    codebooks,
    distill_proj,
):
    row_count, width = tokens.shape
    branches = lax.axis_size("branch")
    devices = lax.axis_size("dp") * branches
    branch = lax.axis_index("branch")
    swap = [(i, branches - 1 - i) for i in range(branches)]
    swapped = lax.ppermute(jnp.concatenate([proj_in[0], proj_out[0].reshape(width, -1)], axis=1), "branch", swap)
    code_width = proj_in.shape[2]
    other_in = swapped[:, :code_width]
    other_out = swapped[:, code_width:].reshape(proj_out.shape[1:])
    first = branch == 0
    in_sem = jnp.where(first, proj_in[0], other_in)
    in_ac = jnp.where(first, other_in, proj_in[0])
    out_sem = jnp.where(first, proj_out[0], other_out)
    out_ac = jnp.where(first, other_out, proj_out[0])

    clip_id, offset = clip_layout(lengths[0], row_count)
    cos_table, sin_table = rope_tables(offset, width // HEADS)
    position = jnp.arange(row_count, dtype=jnp.int32)
    allowed = (
        (clip_id[:, None] == clip_id[None, :])
        & (position[None, :] <= position[:, None])
        & (position[:, None] - position[None, :] < WINDOW)
    )
    enc_mats = (enc_qkv, enc_out, enc_up, enc_down)
    dec_mats = (dec_qkv, dec_out, dec_up, dec_down)
    own_codes = lax.dynamic_slice_in_dim(codes, branch * row_count, row_count, axis=0)
    target = lax.dynamic_slice_in_dim(wavlm, branch * row_count, row_count, axis=0).astype(jnp.float32)

    levels = jnp.arange(codebooks.shape[0], dtype=jnp.int32)
    chosen = codebooks[levels[None, :], own_codes].astype(jnp.float32)
    sem_code = chosen[:, 0].astype(jnp.bfloat16)
    ac_code = jnp.sum(chosen[:, 1:], axis=1).astype(jnp.bfloat16)
    quant = jnp.dot(sem_code, out_sem, preferred_element_type=jnp.float32) + jnp.dot(
        ac_code, out_ac, preferred_element_type=jnp.float32
    )
    decoded, dec_kept = layer_forward(quant, dec_mats, vectors[1], cos_table, sin_table, allowed)
    grad_quant, dec_grads, dec_gains = layer_backward(
        cotangent.astype(jnp.float32), dec_kept, dec_mats, vectors[1], cos_table, sin_table, allowed
    )
    grad_quant = grad_quant.astype(jnp.bfloat16)

    latent, enc_kept = layer_forward(
        tokens.astype(jnp.float32), enc_mats, vectors[0], cos_table, sin_table, allowed
    )
    latent_low = latent.astype(jnp.bfloat16)
    proj_sem = jnp.dot(latent_low, in_sem, preferred_element_type=jnp.float32)
    proj_ac = jnp.dot(latent_low, in_ac, preferred_element_type=jnp.float32)
    grad_out_sem = contract_rows(sem_code, grad_quant)
    grad_out_ac = contract_rows(ac_code, grad_quant)

    prediction = jnp.dot(sem_code, distill_proj, preferred_element_type=jnp.float32)
    pred_norm = jnp.sqrt(jnp.sum(prediction * prediction, axis=-1, keepdims=True) + EPS_COS)
    target_norm = jnp.sqrt(jnp.sum(target * target, axis=-1, keepdims=True) + EPS_COS)
    cosine = jnp.sum(prediction * target, axis=-1, keepdims=True) / (pred_norm * target_norm)
    grad_pred = (
        -DISTILL
        * (target / (pred_norm * target_norm) - cosine * prediction / (pred_norm * pred_norm))
    ).astype(jnp.bfloat16)
    distill_grad = contract_rows(sem_code, grad_pred)
    grad_sem = times_transpose(grad_quant, out_sem) + times_transpose(grad_pred, distill_proj)
    commit = 2.0 * BETA * (proj_sem - chosen[:, 0])
    row_grads = [grad_sem - commit]
    grad_proj_sem = (grad_sem + commit).astype(jnp.bfloat16)

    grad_ac = times_transpose(grad_quant, out_ac)
    residual = proj_ac
    commits = []
    for level in range(1, codebooks.shape[0]):
        residual = residual - chosen[:, level]
        commits.append(2.0 * BETA * residual)
    carry = jnp.zeros_like(proj_ac)
    ac_rows = []
    for commit in commits[::-1]:
        carry = carry + commit
        ac_rows.append(grad_ac - carry)
    row_grads = jnp.stack(row_grads + ac_rows[::-1]).astype(jnp.bfloat16)
    grad_proj_ac = (carry + grad_ac).astype(jnp.bfloat16)
    picks = (own_codes.T[:, :, None] == jnp.arange(codebooks.shape[1], dtype=jnp.int32)).astype(jnp.bfloat16)
    book_grads = lax.dot_general(
        picks, row_grads, (((1,), (1,)), ((0,), (0,))), preferred_element_type=jnp.float32
    )

    grad_in_sem = contract_rows(latent_low, grad_proj_sem)
    grad_in_ac = contract_rows(latent_low, grad_proj_ac)
    grad_latent = times_transpose(grad_proj_sem, in_sem) + times_transpose(grad_proj_ac, in_ac)
    grad_tokens, enc_grads, enc_gains = layer_backward(
        grad_latent, enc_kept, enc_mats, vectors[0], cos_table, sin_table, allowed
    )
    gain_flat = jnp.stack([enc_gains, dec_gains]).reshape(-1)
    sums = [
        *enc_grads,
        *dec_grads,
        gain_flat,
        jnp.stack([grad_in_sem, grad_in_ac]),
        jnp.stack([grad_out_sem, grad_out_ac]),
        book_grads,
        distill_grad,
    ]
    if width // devices % 16 == 0:
        low = [s.astype(jnp.bfloat16) for s in sums]

        def rows_of(k, columns):
            return low[k].reshape(devices, -1, columns)

        vector_rows = jnp.pad(low[8].reshape(devices, 1, -1), ((0, 0), (0, 15), (0, 0)))
        books = low[11].reshape(devices, 4, -1, code_width)
        distill = low[12].reshape(devices, -1, 2, width).transpose(0, 2, 1, 3).reshape(devices, -1, width)
        ff = enc_up.shape[1]
        done = scatter_sums(
            [
                (rows_of(4, 3 * width), 0, "x"),
                (rows_of(5, width), 0, "x"),
                (rows_of(6, ff), 0, "y"),
                (rows_of(7, width), 0, "z"),
                (books, 0, "xyzx"),
                (rows_of(0, 3 * width), 0, "y"),
                (rows_of(1, width), 0, "y"),
                (rows_of(2, ff), 0, "w"),
                (rows_of(3, width), 0, "x"),
                (rows_of(9, code_width), 0, "y"),
                (rows_of(10, width), 0, "y"),
                (distill, 2, "y"),
                (vector_rows, 0, "y"),
            ],
            devices,
        )
        done = [d.reshape(-1) for d in done]
        sums = done[5:9] + done[0:4] + [done[12], done[9], done[10], done[4], done[11]]
    else:
        sums = [
            lax.psum_scatter(s.reshape(-1), ("dp", "branch"), scatter_dimension=0, tiled=True)
            for s in sums
        ]
    return (decoded.astype(jnp.bfloat16), grad_tokens, *sums)


def solution(mesh):
    placed = (
        P(("dp", "branch"), None),
        P("dp", None),
        P(("dp", "branch"), None),
        P(("dp", "branch"), None),
        P("dp", None),
        P(),
        P(),
        P(),
        P(),
        P(),
        P(),
        P(),
        P(),
        P(),
        P("branch", None, None),
        P("branch", None, None),
        P(),
        P(),
    )
    return jax.shard_map(
        body,
        mesh=mesh,
        in_specs=placed,
        out_specs=(
            P(("dp", "branch"), None),
            P(("dp", "branch"), None),
            P(("dp", "branch")),
            P(("dp", "branch")),
            P(("dp", "branch")),
            P(("dp", "branch")),
            P(("dp", "branch")),
            P(("dp", "branch")),
            P(("dp", "branch")),
            P(("dp", "branch")),
            P(("dp", "branch")),
            P(("dp", "branch")),
            P(("dp", "branch")),
            P(("dp", "branch")),
            P(("dp", "branch")),
        ),
        check_vma=False,
    )
```

```python
import functools
import math

import jax
import jax.numpy as jnp
from jax import lax
from jax.experimental import pallas as pl
from jax.experimental.pallas import tpu as pltpu
from jax.sharding import PartitionSpec as P

HEADS = 8
WINDOW = 250
EPS_NORM = 1e-05
EPS_COS = 1e-06
BETA = 0.25
DISTILL = 10.0
ROPE_BASE = 10000.0

MESH = pl.DeviceIdType.MESH
F32 = jnp.float32
BF16 = jnp.bfloat16
TILE = 512
PAIR = 128


def dot(left, right):
    return lax.dot_general(left, right, (((1,), (0,)), ((), ())), preferred_element_type=F32)


def dot_t(left, right):
    return lax.dot_general(left, right, (((1,), (1,)), ((), ())), preferred_element_type=F32)


def t_dot(left, right):
    return lax.dot_general(left, right, (((0,), (0,)), ((), ())), preferred_element_type=F32)


def iota(shape, dim):
    return lax.broadcasted_iota(jnp.int32, shape, dim)


def aligned(index, size):
    return pl.ds(pl.multiple_of(index * size, size), size)


class Refs(dict):
    __getattr__ = dict.__getitem__
    __setattr__ = dict.__setitem__


class Moves:
    def __init__(self, semaphores):
        self.semaphores, self.count = semaphores, 0

    def start(self, source, target):
        move = pltpu.make_async_copy(source, target, self.semaphores.at[self.count])
        self.count += 1
        move.start()
        return move


def layer_scratch(rows, width, ff):
    return Refs(
        x=pltpu.VMEM((rows, width), F32),
        s1=pltpu.VMEM((rows, 1), F32),
        h1=pltpu.VMEM((rows, width), BF16),
        qkv=pltpu.VMEM((rows, 3 * width), BF16),
        att=pltpu.VMEM((HEADS, rows, rows), BF16),
        mix=pltpu.VMEM((rows, width), BF16),
        ao=pltpu.VMEM((rows, width), F32),
        x2=pltpu.VMEM((rows, width), F32),
        s2=pltpu.VMEM((rows, 1), F32),
        h2=pltpu.VMEM((rows, width), BF16),
        act=pltpu.VMEM((rows, ff), BF16),
        dg=pltpu.VMEM((rows, ff), BF16),
        fo=pltpu.VMEM((rows, width), F32),
        grad=pltpu.VMEM((rows, width), BF16),
        gx=pltpu.VMEM((rows, width), F32),
        acc=pltpu.VMEM((rows, width), F32),
        w_qkv_v=pltpu.VMEM((width, 3 * width), BF16),
        w_out_v=pltpu.VMEM((width, width), BF16),
        w_up_v=pltpu.VMEM((width, ff), BF16),
        w_down_v=pltpu.VMEM((ff, width), BF16),
    )


def shaped(shape, kind):
    return jax.ShapeDtypeStruct(shape, kind)


def frame_tables(lengths_ref, cos_ref, sin_ref, bias_ref):
    rows = cos_ref.shape[0]
    place = iota((rows, PAIR), 0)
    query, key = iota((rows, rows), 0), iota((rows, rows), 1)
    begin, begin_query = jnp.zeros_like(place), jnp.zeros_like(query)
    edge = 0
    for clip in range(lengths_ref.shape[1] - 1):
        edge = edge + lengths_ref[0, clip]
        begin = jnp.where(place >= edge, edge, begin)
        begin_query = jnp.where(query >= edge, edge, begin_query)
    allowed = (key >= begin_query) & (key <= query) & (query - key < WINDOW)
    bias_ref[...] = jnp.where(allowed, 0.0, -1e30)
    lane = iota((rows, PAIR), 1)
    rate = jnp.exp((lane % 32).astype(F32) * (-math.log(ROPE_BASE) / 32))
    angle = (place - begin).astype(F32) * rate
    cos_ref[...] = jnp.cos(angle)
    sine = jnp.sin(angle)
    sin_ref[...] = jnp.where(lane % 64 < 32, -sine, sine)


def rotated(value, cosine, sine):
    lane = iota(value.shape, 1)
    swapped = jnp.where(lane % 64 < 32, pltpu.roll(value, PAIR - 32, 1), pltpu.roll(value, 32, 1))
    return value * cosine + swapped * sine


def head_masks(rows):
    low = iota((rows, PAIR), 1) < 64
    return (jnp.where(low, 1.0, 0.0).astype(BF16), jnp.where(low, 0.0, 1.0).astype(BF16))


def attention_forward(r, w_qkv, w_out, gain):
    rows, width = r.x.shape
    x = r.x[...]
    s1 = lax.rsqrt(jnp.mean(x * x, axis=1, keepdims=True) + EPS_NORM)
    r.s1[...] = s1
    r.h1[...] = (x * s1 * gain(0)).astype(BF16)

    def project(part, carry):
        value = dot(r.h1[...], w_qkv[:, aligned(part, width)])
        turn = jnp.where(part < 2, 1.0, 0.0)
        scale = jnp.where(part == 0, 0.125, 1.0)
        cosine = r.cos[...] * turn + (1.0 - turn)
        sine = r.sin[...] * turn
        for p in range(width // PAIR):
            low = rotated(value[:, p * PAIR : (p + 1) * PAIR], cosine, sine).astype(BF16)
            where = pl.ds(pl.multiple_of(part * width + p * PAIR, PAIR), PAIR)
            r.qkv[:, where] = (low.astype(F32) * scale).astype(BF16)
        return carry

    lax.fori_loop(0, 3, project, 0)
    masks = head_masks(rows)

    def pair(p, carry):
        query = r.qkv[:, aligned(p, PAIR)]
        key = r.qkv[:, aligned(p + width // PAIR, PAIR)]
        value = r.qkv[:, aligned(p + 2 * (width // PAIR), PAIR)]
        out = None
        for h in range(2):
            scores = dot_t(query * masks[h], key) + r.bias[...]
            weights = jnp.exp(scores - jnp.max(scores, axis=1, keepdims=True))
            total = jnp.sum(weights, axis=1, keepdims=True)
            attention = (weights * (1.0 / total)).astype(BF16)
            r.att[2 * p + h] = attention
            part = dot(attention, value * masks[h])
            out = part if out is None else out + part
        r.mix[:, aligned(p, PAIR)] = out.astype(BF16)
        return carry

    lax.fori_loop(0, width // PAIR, pair, 0)
    ao = dot(r.mix[...], w_out[...])
    r.ao[...] = ao
    x2 = r.x[...] + gain(1) * ao
    r.x2[...] = x2
    s2 = lax.rsqrt(jnp.mean(x2 * x2, axis=1, keepdims=True) + EPS_NORM)
    r.s2[...] = s2
    r.h2[...] = (x2 * s2 * gain(2)).astype(BF16)


def ffn_forward(r, w_up, w_down):
    r.fo[...] = jnp.zeros_like(r.fo)
    slope = math.sqrt(2.0 / math.pi)

    def tile(t, carry):
        cols = aligned(t, TILE)
        pre = dot(r.h2[...], w_up[:, cols])
        square = pre * pre
        bent = jnp.tanh(slope * pre * (1.0 + 0.044715 * square))
        half = 0.5 * (1.0 + bent)
        act = (pre * half).astype(BF16)
        r.act[:, cols] = act
        turn = 0.5 * pre * (1.0 - bent * bent) * slope * (1.0 + 3.0 * 0.044715 * square)
        r.dg[:, cols] = (half + turn).astype(BF16)
        r.fo[...] += dot(act, w_down[cols, :])
        return carry

    lax.fori_loop(0, w_up.shape[1] // TILE, tile, 0)


def norm_back(stream, inverse, grad):
    mean = jnp.mean(grad * stream, axis=1, keepdims=True)
    return inverse * grad - stream * (inverse * inverse * inverse * mean)


def column_sum(value):
    return jnp.sum(value, axis=0, keepdims=True)


def put_columns(target, value, start):
    shape = target.shape
    value = value.astype(target.dtype).reshape(shape[:-1] + (value.shape[1],))
    target[(slice(None),) * (len(shape) - 1) + (pl.ds(start, value.shape[-1]),)] = value


def put_rows(target, value, tile):
    shape = target.shape
    value = value.astype(target.dtype)
    if len(shape) == 2:
        target[aligned(tile, value.shape[0]), :] = value
    else:
        target[tile // 2, tile % 2] = value.reshape(shape[2:])


def ffn_backward(r, w_up, w_down, gain, gy_ref, grad_up, grad_down, gain_out):
    gy = gy_ref[...].astype(F32)
    gain_out[3:4, :] = column_sum(gy * r.fo[...])
    r.grad[...] = (gain(3) * gy).astype(BF16)
    r.acc[...] = jnp.zeros_like(r.acc)

    def tile(t, carry):
        cols = aligned(t, TILE)
        put_rows(grad_down, t_dot(r.act[:, cols], r.grad[...]), t)
        grad_pre = (dot_t(r.grad[...], w_down[cols, :]) * r.dg[:, cols].astype(F32)).astype(BF16)
        put_columns(grad_up, t_dot(r.h2[...], grad_pre), pl.multiple_of(t * TILE, TILE))
        r.acc[...] += dot_t(grad_pre, w_up[:, cols])
        return carry

    lax.fori_loop(0, w_up.shape[1] // TILE, tile, 0)
    back = r.acc[...]
    x2, s2 = r.x2[...], r.s2[...]
    gain_out[2:3, :] = column_sum(back * x2 * s2)
    r.gx[...] = gy_ref[...].astype(F32) + norm_back(x2, s2, back * gain(2))


def attention_backward(r, w_qkv, w_out, gain, grad_qkv, grad_out, gain_out):
    rows, width = r.x.shape
    gx = r.gx[...]
    gain_out[1:2, :] = column_sum(gx * r.ao[...])
    grad_attn = (gain(1) * gx).astype(BF16)
    put_columns(grad_out, t_dot(r.mix[...], grad_attn), 0)
    r.grad[...] = dot_t(grad_attn, w_out[...]).astype(BF16)
    masks = head_masks(rows)
    pairs = width // PAIR

    def pair(p, carry):
        query = r.qkv[:, aligned(p, PAIR)]
        key = r.qkv[:, aligned(p + pairs, PAIR)]
        value = r.qkv[:, aligned(p + 2 * pairs, PAIR)]
        grad_mixed = r.grad[:, aligned(p, PAIR)]
        to_query = to_key = to_value = 0.0
        for h in range(2):
            attention = r.att[2 * p + h]
            mixed = grad_mixed * masks[h]
            to_value = to_value + t_dot(attention, mixed)
            weights = dot_t(mixed, value)
            wide = attention.astype(F32)
            mean = jnp.sum(wide * weights, axis=1, keepdims=True)
            scores = (wide * (weights - mean)).astype(BF16)
            to_query = to_query + dot(scores, key * masks[h])
            to_key = to_key + t_dot(scores, query * masks[h])
        cosine, sine = r.cos[...], -r.sin[...]
        r.qkv[:, aligned(p, PAIR)] = rotated(to_query * 0.125, cosine, sine).astype(BF16)
        r.qkv[:, aligned(p + pairs, PAIR)] = rotated(to_key, cosine, sine).astype(BF16)
        r.qkv[:, aligned(p + 2 * pairs, PAIR)] = to_value.astype(BF16)
        return carry

    lax.fori_loop(0, pairs, pair, 0)
    r.acc[...] = jnp.zeros_like(r.acc)

    def part(t, carry):
        cols = aligned(t, TILE)
        put_columns(grad_qkv, t_dot(r.h1[...], r.qkv[:, cols]), pl.multiple_of(t * TILE, TILE))
        r.acc[...] += dot_t(r.qkv[:, cols], w_qkv[:, cols])
        return carry

    lax.fori_loop(0, w_qkv.shape[1] // TILE, part, 0)
    back = r.acc[...]
    x, s1 = r.x[...], r.s1[...]
    gain_out[0:1, :] = column_sum(back * x * s1)
    r.gx[...] = r.gx[...] + norm_back(x, s1, back * gain(0))


def decoder_kernel(ins, outs, scratch):
    r = Refs({**ins, **outs, **scratch})
    branch = lax.axis_index("branch")
    rows, width = r.decoded.shape
    levels, entries, code_width = r.books.shape
    moves = Moves(r.sem_move)

    def book(level):
        return pltpu.make_async_copy(r.books.at[level], r.books_v.at[level], r.sem_book.at[level])

    for level in range(levels):
        book(level).start()
    got_pout = [
        moves.start(r.pout_own.at[0], r.pout_v.at[branch]),
        moves.start(r.pout_other.at[0], r.pout_v.at[1 - branch]),
    ]
    got_qkv = moves.start(r.w_qkv, r.w_qkv_v)
    got_out = moves.start(r.w_out, r.w_out_v)
    got_up = moves.start(r.w_up, r.w_up_v)
    got_down = moves.start(r.w_down, r.w_down_v)

    frame_tables(r.lengths, r.cos, r.sin, r.bias)
    own_codes = r.codes[pl.ds(pl.multiple_of(branch * rows, rows), rows), :].astype(F32)
    level_lane = iota(own_codes.shape, 1)
    lane = iota((rows, PAIR), 1)
    entry = iota((rows, entries), 1)
    r.ac_sum[...] = jnp.zeros_like(r.ac_sum)
    r.code_cols[...] = jnp.zeros_like(r.code_cols)

    def pick(level, carry):
        code = jnp.sum(jnp.where(level_lane == level, own_codes, 0.0), axis=1, keepdims=True)
        r.code_cols[...] += jnp.where(lane == level, code, 0.0)
        one_hot = jnp.where(entry == code.astype(jnp.int32), 1.0, 0.0).astype(BF16)
        book(level).wait()
        got = dot(one_hot, r.books_v[level])
        r.chosen[level] = got.astype(BF16)
        r.ac_sum[...] += jnp.where(level > 0, got, 0.0)
        return carry

    lax.fori_loop(0, levels, pick, 0)
    r.codes_t[...] = r.code_cols[...].T[:levels].astype(jnp.int32)
    ac = r.ac_sum[...].astype(BF16)
    r.ac[...] = ac
    got_pout[0].wait()
    got_pout[1].wait()
    r.x[...] = dot(r.chosen[0], r.pout_v[0]) + dot(ac, r.pout_v[1])

    def gain(i):
        return r.vectors[1, i : i + 1, :]

    got_qkv.wait()
    got_out.wait()
    attention_forward(r, r.w_qkv_v, r.w_out_v, gain)
    got_up.wait()
    got_down.wait()
    ffn_forward(r, r.w_up_v, r.w_down_v)
    r.decoded[...] = (r.x2[...] + gain(3) * r.fo[...]).astype(BF16)
    ffn_backward(r, r.w_up_v, r.w_down_v, gain, r.cotangent, r.t_up_v, r.t_down_v, r.gains)
    stored = [moves.start(r.t_up_v, r.t_up), moves.start(r.t_down_v, r.t_down)]
    attention_backward(r, r.w_qkv_v, r.w_out_v, gain, r.t_qkv_v, r.t_out_v, r.gains)
    stored += [moves.start(r.t_qkv_v, r.t_qkv), moves.start(r.t_out_v, r.t_out)]
    r.gquant[...] = r.gx[...].astype(BF16)
    for move in stored:
        move.wait()


def decoder(given):
    rows, width = given.cotangent.shape
    ff = given.w_up.shape[1]
    levels, entries, code_width = given.books.shape
    vmem, hbm = pl.BlockSpec(memory_space=pltpu.VMEM), pl.BlockSpec(memory_space=pl.ANY)
    scratch = layer_scratch(rows, width, ff)
    scratch.t_qkv_v = pltpu.VMEM(given.w_qkv.shape, BF16)
    scratch.t_out_v = pltpu.VMEM(given.w_out.shape, BF16)
    scratch.t_up_v = pltpu.VMEM(given.w_up.shape, BF16)
    scratch.t_down_v = pltpu.VMEM(given.w_down.shape, BF16)
    scratch.books_v = pltpu.VMEM(given.books.shape, BF16)
    scratch.pout_v = pltpu.VMEM((2, code_width, width), BF16)
    scratch.ac_sum = pltpu.VMEM((rows, code_width), F32)
    scratch.code_cols = pltpu.VMEM((rows, PAIR), F32)
    scratch.sem_move = pltpu.SemaphoreType.DMA((10,))
    scratch.sem_book = pltpu.SemaphoreType.DMA((levels,))
    in_specs = dict.fromkeys(given, hbm)
    in_specs.update(
        lengths=pl.BlockSpec(memory_space=pltpu.SMEM), codes=vmem, vectors=vmem, cotangent=vmem
    )
    outs = dict(
        decoded=shaped((rows, width), BF16),
        t_qkv=shaped(given.w_qkv.shape, BF16),
        t_out=shaped(given.w_out.shape, BF16),
        t_up=shaped(given.w_up.shape, BF16),
        t_down=shaped(given.w_down.shape, BF16),
        gains=shaped((4, width), F32),
        gquant=shaped((rows, width), BF16),
        chosen=shaped((levels, rows, code_width), BF16),
        ac=shaped((rows, code_width), BF16),
        codes_t=shaped((levels, rows), jnp.int32),
        cos=shaped((rows, PAIR), F32),
        sin=shaped((rows, PAIR), F32),
        bias=shaped((rows, rows), F32),
    )
    out_specs = dict.fromkeys(outs, vmem)
    out_specs.update(t_qkv=hbm, t_out=hbm, t_up=hbm, t_down=hbm)
    got = pl.pallas_call(
        decoder_kernel,
        out_shape=outs,
        in_specs=[in_specs],
        out_specs=out_specs,
        scratch_shapes=[dict(scratch)],
        compiler_params=pltpu.CompilerParams(vmem_limit_bytes=56 * 2**20),
        name="decoder",
    )(dict(given))
    return Refs(got)


FROM_DECODER, BOOK, HERE = range(3)


class Chunk:
    def __init__(self, phase, rows, columns, order, source=HERE, part=0, kind=BF16, fold=0):
        self.phase, self.rows, self.columns, self.order = phase, rows, columns, order
        self.source, self.part, self.kind, self.fold = source, part, kind, fold

    def shape(self, leading):
        return (2,) * leading + (self.rows, self.columns)

    def flat(self):
        return (self.rows * self.columns // 128, 128) if self.columns > 128 else (1, 128)

    def size(self, bits):
        return 2**bits * self.rows * self.columns * (2 if self.kind == BF16 else 4)


def plan(chunks, phases, bits):
    core = bits - 2
    free, pending, done = {}, [], []
    now = 0.0

    def begin(name, stage):
        chunk = chunks[name]
        dim = chunk.order[stage]
        link = 0 if dim < bits - 3 else dim
        rate = 500e3 if dim == core else 45e3
        took = chunk.size(bits) / 2 ** (stage + 1) / rate * (2 if dim < bits - 4 else 1)
        free[link] = max(now, free.get(link, 0.0)) + took
        pending.append((free[link] + 1.5, name, stage))

    def finish(limit):
        nonlocal now
        acts = []
        while pending:
            pending.sort()
            if pending[0][0] > limit:
                break
            at, name, stage = pending.pop(0)
            now = max(now, at) + 0.3
            acts.append((name, stage))
            if stage + 1 < bits:
                begin(name, stage + 1)
        return acts

    for phase, took in enumerate(phases):
        now += took
        for name in chunks:
            if chunks[name].phase == phase:
                begin(name, 0)
        done.append(finish(now))
    done.append(finish(math.inf))
    return done


def coordinates(step, count):
    return [step // 2 ** (count - 1 - i) % 2 for i in range(count)]


def store_flat(out_ref, value, fold):
    rows, columns = value.shape
    blocks = columns // 128
    if blocks == 1:
        out_ref[...] = value[: out_ref.shape[0]]
        return
    folds = max(fold, 1)
    rows = rows // folds
    for part in range(folds):
        for i in range(blocks):
            out_ref[pl.ds(part * blocks + i, rows, stride=folds * blocks), :] = value[
                part * rows : (part + 1) * rows, i * 128 : (i + 1) * 128
            ]


class Halving:
    def __init__(self, chunks, bits, recv, outs, send_sem, recv_sem):
        self.chunks = {name: (i, chunks[name]) for i, name in enumerate(chunks)}
        self.bits, self.recv, self.outs = bits, recv, outs
        self.send_sem, self.recv_sem = send_sem, recv_sem
        self.copies = {}
        dp, branch = lax.axis_index("dp"), lax.axis_index("branch")
        self.mine, self.partner = [], []
        for dim in range(bits - 1):
            weight = 2 ** (bits - 2 - dim)
            bit = dp // weight % 2
            self.mine.append(bit)
            self.partner.append({"dp": dp + weight * (1 - 2 * bit), "branch": branch})
        self.mine.append(branch)
        self.partner.append({"dp": dp, "branch": 1 - branch})

    def barrier(self):
        semaphore = pltpu.get_barrier_semaphore()
        for target in self.partner:
            pl.semaphore_signal(semaphore, inc=1, device_id=target, device_id_type=MESH)
        pl.semaphore_wait(semaphore, self.bits)

    def left(self, name, stage):
        return [d for d in range(self.bits) if d not in self.chunks[name][1].order[:stage]]

    def half(self, ref, name, stage, index):
        position = self.left(name, stage).index(self.chunks[name][1].order[stage])
        return ref.at[(slice(None),) * position + (index,)]

    def send(self, name, stage, source):
        k, chunk = self.chunks[name]
        self.copies[name, stage] = pltpu.make_async_remote_copy(
            src_ref=source,
            dst_ref=self.recv[name][stage],
            send_sem=self.send_sem.at[k, stage],
            recv_sem=self.recv_sem.at[k, stage],
            device_id=self.partner[chunk.order[stage]],
            device_id_type=MESH,
        )
        self.copies[name, stage].start()

    def send_half(self, name, stage, ref):
        dim = self.chunks[name][1].order[stage]
        self.send(name, stage, self.half(ref, name, stage, 1 - self.mine[dim]))

    def arrived(self, name, stage):
        self.copies[name, stage].wait_recv()

    def add(self, name, stage, own):
        _, chunk = self.chunks[name]
        got = self.recv[name][stage]
        depth = self.bits - 1 - stage
        if stage == self.bits - 1:
            store_flat(self.outs[name], own[...].astype(F32) + got[...].astype(F32), chunk.fold)
            return

        def step(i, carry):
            where = tuple(coordinates(i, depth))
            got[where] = got[where] + own[where]
            return carry

        lax.fori_loop(0, 2**depth, step, 0)

    def finish(self, name, stage, own=None):
        _, chunk = self.chunks[name]
        self.arrived(name, stage)
        if own is None:
            dim = chunk.order[stage]
            own = self.half(self.recv[name][stage - 1], name, stage, self.mine[dim])
        self.add(name, stage, own)
        self.follow(name, stage)

    def follow(self, name, stage):
        if stage + 1 < self.bits:
            self.send_half(name, stage + 1, self.recv[name][stage])

    def drain(self):
        for copy in self.copies.values():
            copy.wait_send()


BOOK_PARTS = 4


def quantizer_latent(r):
    branch = lax.axis_index("branch")
    rows, width = r.x.shape
    levels = r.chosen.shape[0]
    latent = r.latent[...]
    sem_code, ac_code = r.chosen[0], r.ac[...]
    gquant = r.gquant[...]
    prediction = dot(sem_code, r.distill_v[...])
    target = r.wavlm_v[...].astype(F32)
    pred_norm = lax.rsqrt(jnp.sum(prediction * prediction, axis=1, keepdims=True) + EPS_COS)
    target_norm = lax.rsqrt(jnp.sum(target * target, axis=1, keepdims=True) + EPS_COS)
    cosine = jnp.sum(prediction * target, axis=1, keepdims=True) * (pred_norm * target_norm)
    grad_pred = (
        target * (-DISTILL * pred_norm * target_norm) + prediction * (DISTILL * cosine * pred_norm * pred_norm)
    ).astype(BF16)
    put_distill(r.t.distill, t_dot(sem_code, grad_pred))
    grad_sem = dot_t(gquant, r.pout_v[0]) + dot_t(grad_pred, r.distill_v[...])
    put_group(r.t.pout, 0, t_dot(sem_code, gquant))
    put_group(r.t.pout, 1, t_dot(ac_code, gquant))
    commit = 2.0 * BETA * (dot(latent, r.pin_v[0]) - sem_code.astype(F32))
    r.g_rows[0] = (grad_sem - commit).astype(BF16)
    to_sem = (grad_sem + commit).astype(BF16)

    grad_ac = dot_t(gquant, r.pout_v[1])
    residual = dot(latent, r.pin_v[1])
    for level in range(1, levels):
        residual = residual - r.chosen[level].astype(F32)
    carry = jnp.zeros_like(residual)
    for level in range(levels - 1, 0, -1):
        carry = carry + 2.0 * BETA * residual
        r.g_rows[level] = (grad_ac - carry).astype(BF16)
        residual = residual + r.chosen[level].astype(F32)
    to_ac = (grad_ac + carry).astype(BF16)
    put_group(r.t.pin, 0, t_dot(latent, to_sem))
    put_group(r.t.pin, 1, t_dot(latent, to_ac))
    r.gy[...] = dot_t(to_sem, r.pin_v[0]) + dot_t(to_ac, r.pin_v[1])


def put_group(target, group, value):
    if len(target.shape) == 2:
        target[group * value.shape[0] : (group + 1) * value.shape[0], :] = value.astype(target.dtype)
    else:
        target[group] = value.astype(target.dtype).reshape(target.shape[1:])


def put_distill(target, value):
    if len(target.shape) == 2:
        target[...] = value.astype(target.dtype)
        return
    columns = target.shape[-1]
    devices = math.prod(target.shape[:-2])
    value = value.reshape(devices, -1, value.shape[1])
    folded = [value[:, :, i : i + columns] for i in range(0, value.shape[2], columns)]
    target[...] = jnp.concatenate(folded, axis=1).astype(target.dtype).reshape(target.shape)


def book_rows(r, level, first, count, span, stride):
    row = iota((count, r.codes_t.shape[1]), 0)
    for step in range(1, count // span):
        row = jnp.where(iota(row.shape, 0) >= step * span, iota(row.shape, 0) + step * (stride - span), row)
    one_hot = jnp.where(r.codes_t[pl.ds(level, 1), :] == row + first, 1.0, 0.0).astype(BF16)
    return dot(one_hot, r.g_rows[level])


def encoder_kernel(chunks, bits, ins, outs, scratch):
    r = Refs({**ins, **outs, **scratch})
    t = r.t = Refs(r.t)
    branch = lax.axis_index("branch")
    rows, width = r.tokens.shape
    levels = r.chosen.shape[0]
    moves = Moves(r.sem_move)
    got_qkv = moves.start(r.w_qkv, r.w_qkv_v)
    got_out = moves.start(r.w_out, r.w_out_v)
    got_up = moves.start(r.w_up, r.w_up_v)
    got_down = moves.start(r.w_down, r.w_down_v)
    got_rest = [
        moves.start(r.wavlm.at[pl.ds(pl.multiple_of(branch * rows, rows), rows)], r.wavlm_v),
        moves.start(r.distill, r.distill_v),
        moves.start(r.pin_own.at[0], r.pin_v.at[branch]),
        moves.start(r.pin_other.at[0], r.pin_v.at[1 - branch]),
        moves.start(r.pout_own.at[0], r.pout_v.at[branch]),
        moves.start(r.pout_other.at[0], r.pout_v.at[1 - branch]),
    ]

    def gain(i):
        return r.vectors[0, i : i + 1, :]

    if chunks:
        sums = Halving(chunks, bits, r.recv, r.sums, r.send_sem, r.recv_sem)
        mine = sums.mine[bits - 2]
        sums.barrier()
        own_dec = {}
        places = dict(dec_down=t.enc_down, dec_up=t.enc_up, dec_qkv=t.enc_qkv, dec_out=t.enc_out)
        for name, place in places.items():
            sums.send_half(name, 0, r.t_dec[name])
            own = sums.half(place, name, 0, 0)
            own_dec[name] = (own, moves.start(sums.half(r.t_dec[name], name, 0, mine), own))

    def book_part(j, core, put):
        span = t.books[0].shape[-2]

        def one(level, carry):
            value = book_rows(r, level, core * (2 * BOOK_PARTS * span) + j * span, 2 * span, span, BOOK_PARTS * span)
            put(tuple(coordinates(level, bits - 2)), value)
            return carry

        lax.fori_loop(0, levels, one, 0)

    def start_books(j, name):
        def put(where, value):
            t.books[j][where] = value.astype(BF16).reshape(t.books[j].shape[bits - 2 :])

        book_part(j, 1 - mine, put)
        sums.send(name, 0, t.books[j])

    def finish_books(j, name):
        got = r.recv[name][0]

        def put(where, value):
            got[where] = (got[where].astype(F32) + value.reshape(got.shape[bits - 2 :])).astype(BF16)

        sums.arrived(name, 0)
        book_part(j, mine, put)
        sums.follow(name, 0)

    def finish(name, stage):
        if stage > 0:
            sums.finish(name, stage)
        elif chunks[name].source == FROM_DECODER:
            own, move = own_dec[name]
            move.wait()
            sums.finish(name, 0, own)
        elif chunks[name].source == BOOK:
            finish_books(chunks[name].part, name)
        else:
            sums.finish(name, 0, sums.half(t[name], name, 0, mine))

    def forward_attention():
        r.x[...] = r.tokens[...].astype(F32)
        got_qkv.wait()
        got_out.wait()
        attention_forward(r, r.w_qkv_v, r.w_out_v, gain)

    def forward_ffn():
        got_up.wait()
        got_down.wait()
        ffn_forward(r, r.w_up_v, r.w_down_v)
        r.latent[...] = (r.x2[...] + gain(3) * r.fo[...]).astype(BF16)

    def quantizer():
        for move in got_rest:
            move.wait()
        quantizer_latent(r)

    def all_books():
        tiles = t.books.shape[1] // TILE

        def one(step, carry):
            value = book_rows(r, step // tiles, step % tiles * TILE, TILE, TILE, TILE)
            t.books[step // tiles, aligned(step % tiles, TILE), :] = value.astype(BF16)
            return carry

        lax.fori_loop(0, levels * tiles, one, 0)

    def backward_ffn():
        ffn_backward(r, r.w_up_v, r.w_down_v, gain, r.gy, t.enc_up, t.enc_down, r.gains)

    def backward_attention():
        attention_backward(r, r.w_qkv_v, r.w_out_v, gain, t.enc_qkv, t.enc_out, r.gains)
        r.grad_tokens[...] = r.gx[...]

    def spread_gains():
        for layer, ref in enumerate((r.gains, r.dec_gains)):
            for row in range(4):
                for block in range(width // 128):
                    owner = (layer * 4 + row) * (width // 128) + block
                    where = tuple(owner // 2 ** (bits - 1 - i) % 2 for i in range(bits))
                    t.vec[where] = jnp.broadcast_to(
                        ref[row : row + 1, block * 128 : (block + 1) * 128], t.vec.shape[bits:]
                    )

    if not chunks:
        for run in (forward_attention, forward_ffn, quantizer, all_books, backward_ffn, backward_attention):
            run()
        return
    books = [name for name in chunks if chunks[name].source == BOOK]
    work = [(0.0, lambda: None), (6.0, forward_attention), (5.0, forward_ffn), (4.0, quantizer)]
    work += [(1.5, functools.partial(start_books, chunks[name].part, name)) for name in books]
    work += [(6.0, backward_ffn), (8.0, backward_attention), (0.2, spread_gains)]
    actions = plan(chunks, [took for took, _ in work], bits)
    early = [act for acts in actions[: 4 + len(books)] for act in acts]
    assert all((name, 0) in early for name in own_dec)
    for phase, (_, run) in enumerate(work):
        run()
        for name in chunks:
            if chunks[name].phase == phase and chunks[name].source == HERE:
                sums.send_half(name, 0, t[name])
        for name, stage in actions[phase]:
            finish(name, stage)
    for name, stage in actions[-1]:
        finish(name, stage)
    sums.drain()


def encoder(given, dec_parts, entries, devices, with_sums):
    rows, width = given.tokens.shape
    ff = given.w_up.shape[1]
    levels, _, code_width = given.chosen.shape
    bits = devices.bit_length() - 1
    vmem, hbm = pl.BlockSpec(memory_space=pltpu.VMEM), pl.BlockSpec(memory_space=pl.ANY)
    scratch = layer_scratch(rows, width, ff)
    scratch.gy = pltpu.VMEM((rows, width), F32)
    scratch.latent = pltpu.VMEM((rows, width), BF16)
    scratch.g_rows = pltpu.VMEM((levels, rows, code_width), BF16)
    scratch.pin_v = pltpu.VMEM((2, width, code_width), BF16)
    scratch.pout_v = pltpu.VMEM((2, code_width, width), BF16)
    scratch.distill_v = pltpu.VMEM(given.distill.shape, BF16)
    scratch.wavlm_v = pltpu.VMEM((rows, given.wavlm.shape[1]), BF16)
    scratch.sem_move = pltpu.SemaphoreType.DMA((14,))
    outs = Refs(grad_tokens=shaped((rows, width), F32))
    chunks = {}
    params = dict(vmem_limit_bytes=61 * 2**20)
    if with_sums:
        params.update(collective_id=0, has_side_effects=True)
        core, x, y = bits - 2, bits - 1, bits - 3
        z = list(range(bits - 3))[::-1]
        via_x, via_y = [core, x, y] + z, [core, y, x] + z
        via_z, via_w = [core] + z + [x, y], [core] + z + [y, x]
        share = width // devices
        chunks = dict(
            dec_down=Chunk(0, ff // devices, width, via_z, FROM_DECODER),
            dec_up=Chunk(0, share, ff, via_y, FROM_DECODER),
            dec_qkv=Chunk(0, share, 3 * width, via_x, FROM_DECODER),
            dec_out=Chunk(0, share, width, via_x, FROM_DECODER),
            distill=Chunk(3, 16, width, via_y, fold=2),
            pout=Chunk(3, share, width, via_y),
            pin=Chunk(3, 2 * share, code_width, via_y),
            books0=Chunk(4, 128, code_width, via_x, BOOK, 0),
            books1=Chunk(5, 128, code_width, via_y, BOOK, 1),
            books2=Chunk(6, 128, code_width, via_z, BOOK, 2),
            books3=Chunk(7, 128, code_width, via_x, BOOK, 3),
            enc_down=Chunk(8, ff // devices, width, via_x),
            enc_up=Chunk(8, share, ff, via_w),
            enc_out=Chunk(9, share, width, via_y),
            enc_qkv=Chunk(9, share, 3 * width, via_y),
            vec=Chunk(10, 8, 128, via_x, kind=F32),
        )
        t, recv = {}, {}
        for name, c in chunks.items():
            recv[name] = [pltpu.VMEM(c.shape(bits - 1 - stage), c.kind) for stage in range(bits)]
            if c.source == HERE:
                t[name] = pltpu.VMEM(c.shape(bits), c.kind)
        t.update(books=[pltpu.VMEM(c.shape(bits - 1), c.kind) for c in chunks.values() if c.source == BOOK])
        scratch.update(t=t, recv=recv, gains=pltpu.VMEM((4, width), F32))
        scratch.send_sem = pltpu.SemaphoreType.DMA((len(chunks), bits))
        scratch.recv_sem = pltpu.SemaphoreType.DMA((len(chunks), bits))
        outs.sums = {name: shaped(c.flat(), F32) for name, c in chunks.items()}
        given.t_dec = {name: part.reshape(chunks[name].shape(bits)) for name, part in dec_parts.items()}
    else:
        outs.gains = shaped((4, width), F32)
        outs.t = dict(
            enc_qkv=shaped(given.w_qkv.shape, BF16),
            enc_out=shaped(given.w_out.shape, BF16),
            enc_up=shaped(given.w_up.shape, BF16),
            enc_down=shaped(given.w_down.shape, BF16),
            pin=shaped((2 * width, code_width), BF16),
            pout=shaped((2 * code_width, width), BF16),
            books=shaped((levels, entries, code_width), BF16),
            distill=shaped(given.distill.shape, BF16),
        )
    in_specs = dict.fromkeys(given, vmem)
    in_specs.update(wavlm=hbm, distill=hbm, pin_own=hbm, pin_other=hbm, pout_own=hbm, pout_other=hbm)
    in_specs.update(w_qkv=hbm, w_out=hbm, w_up=hbm, w_down=hbm)
    if with_sums:
        in_specs.update(t_dec=dict.fromkeys(given.t_dec, hbm))
    got = pl.pallas_call(
        functools.partial(encoder_kernel, chunks, bits),
        out_shape=dict(outs),
        in_specs=[in_specs],
        out_specs=jax.tree.map(lambda _: vmem, dict(outs)),
        scratch_shapes=[dict(scratch)],
        compiler_params=pltpu.CompilerParams(**params),
        name="encoder",
    )(dict(given))
    return Refs(got)


def body(
    tokens,
    wavlm,
    cotangent,
    lengths,
    codes,
    enc_qkv,
    enc_out,
    enc_up,
    enc_down,
    dec_qkv,
    dec_out,
    dec_up,
    dec_down,
    vectors,
    proj_in,
    proj_out,
    codebooks,
    distill_proj,
):
    width = tokens.shape[1]
    devices = lax.axis_size("dp") * lax.axis_size("branch")
    swap = [(0, 1), (1, 0)]
    pout_other = lax.ppermute(proj_out, "branch", swap)
    pin_other = lax.ppermute(proj_in, "branch", swap)
    dec = decoder(
        Refs(
            lengths=lengths,
            codes=codes,
            vectors=vectors,
            cotangent=cotangent,
            pout_own=proj_out,
            pout_other=pout_other,
            books=codebooks,
            w_qkv=dec_qkv,
            w_out=dec_out,
            w_up=dec_up,
            w_down=dec_down,
        )
    )
    given = Refs(
        tokens=tokens,
        vectors=vectors,
        chosen=dec.chosen,
        ac=dec.ac,
        gquant=dec.gquant,
        codes_t=dec.codes_t,
        cos=dec.cos,
        sin=dec.sin,
        bias=dec.bias,
        dec_gains=dec.gains,
        wavlm=wavlm,
        distill=distill_proj,
        pin_own=proj_in,
        pin_other=pin_other,
        pout_own=proj_out,
        pout_other=pout_other,
        w_qkv=enc_qkv,
        w_out=enc_out,
        w_up=enc_up,
        w_down=enc_down,
    )
    dec_parts = dict(dec_qkv=dec.t_qkv, dec_out=dec.t_out, dec_up=dec.t_up, dec_down=dec.t_down)
    with_sums = devices == 4 * codebooks.shape[0] and width // devices % 16 == 0
    enc = encoder(given, dec_parts, codebooks.shape[1], devices, with_sums)
    if with_sums:
        s = Refs(enc.sums)
        books = jnp.concatenate([s.books0, s.books1, s.books2, s.books3])
        sums = [s.enc_qkv, s.enc_out, s.enc_up, s.enc_down, s.dec_qkv, s.dec_out, s.dec_up, s.dec_down]
        sums = [part.reshape(-1) for part in sums + [s.vec, s.pin, s.pout, books, s.distill]]
    else:
        t = Refs(enc.t)
        gains = jnp.concatenate([enc.gains, dec.gains])
        local = [t.enc_qkv, t.enc_out, t.enc_up, t.enc_down, dec.t_qkv, dec.t_out, dec.t_up, dec.t_down]
        local += [gains, t.pin, t.pout, t.books, t.distill]
        sums = [
            lax.psum_scatter(part.astype(F32).reshape(-1), ("dp", "branch"), scatter_dimension=0, tiled=True)
            for part in local
        ]
    return (dec.decoded, enc.grad_tokens, *sums)


def solution(mesh):
    rows, whole = P(("dp", "branch"), None), P()
    placed = (rows, P("dp", None), rows, rows, P("dp", None)) + (whole,) * 9
    placed += (P("branch", None, None),) * 2 + (whole,) * 2
    return jax.shard_map(
        body,
        mesh=mesh,
        in_specs=placed,
        out_specs=(rows, rows) + (P(("dp", "branch")),) * 13,
        check_vma=False,
    )
```

```python
import functools
import math

import jax
import jax.numpy as jnp
from jax import lax
from jax.experimental import pallas as pl
from jax.experimental.pallas import tpu as pltpu
from jax.sharding import PartitionSpec as P

HEADS = 8
WINDOW = 250
EPS_NORM = 1e-05
EPS_COS = 1e-06
BETA = 0.25
DISTILL = 10.0
ROPE_BASE = 10000.0

MESH = pl.DeviceIdType.MESH
F32 = jnp.float32
BF16 = jnp.bfloat16
TILE = 512
PAIR = 128


def dot(left, right):
    return lax.dot_general(left, right, (((1,), (0,)), ((), ())), preferred_element_type=F32)


def dot_t(left, right):
    return lax.dot_general(left, right, (((1,), (1,)), ((), ())), preferred_element_type=F32)


def t_dot(left, right):
    return lax.dot_general(left, right, (((0,), (0,)), ((), ())), preferred_element_type=F32)


def iota(shape, dim):
    return lax.broadcasted_iota(jnp.int32, shape, dim)


def aligned(index, size):
    return pl.ds(pl.multiple_of(index * size, size), size)


class Refs(dict):
    __getattr__ = dict.__getitem__
    __setattr__ = dict.__setitem__


class Moves:
    def __init__(self, semaphores):
        self.semaphores, self.count = semaphores, 0

    def start(self, source, target):
        move = pltpu.make_async_copy(source, target, self.semaphores.at[self.count])
        self.count += 1
        move.start()
        return move


def layer_scratch(rows, width, ff):
    return Refs(
        x=pltpu.VMEM((rows, width), F32),
        s1=pltpu.VMEM((rows, 1), F32),
        h1=pltpu.VMEM((rows, width), BF16),
        qkv=pltpu.VMEM((rows, 3 * width), BF16),
        mix=pltpu.VMEM((rows, width), BF16),
        ao=pltpu.VMEM((rows, width), F32),
        x2=pltpu.VMEM((rows, width), F32),
        s2=pltpu.VMEM((rows, 1), F32),
        h2=pltpu.VMEM((rows, width), BF16),
        act=pltpu.VMEM((rows, ff), BF16),
        dg=pltpu.VMEM((rows, ff), BF16),
        fo=pltpu.VMEM((rows, width), F32),
        grad=pltpu.VMEM((rows, width), BF16),
        gx=pltpu.VMEM((rows, width), F32),
        acc=pltpu.VMEM((rows, width), F32),
        w_qkv_v=pltpu.VMEM((width, 3 * width), BF16),
        w_out_v=pltpu.VMEM((width, width), BF16),
        w_up_v=pltpu.VMEM((width, ff), BF16),
        w_down_v=pltpu.VMEM((ff, width), BF16),
    )


def shaped(shape, kind):
    return jax.ShapeDtypeStruct(shape, kind)


def frame_tables(r):
    rows = r.cos.shape[0]
    place = iota((rows, PAIR), 0)
    query, key = iota((rows, rows), 0), iota((rows, rows), 1)
    begin, begin_query = jnp.zeros_like(place), jnp.zeros_like(query)
    edge = 0
    for clip in range(r.lengths.shape[1] - 1):
        edge = edge + r.lengths[0, clip]
        begin = jnp.where(place >= edge, edge, begin)
        begin_query = jnp.where(query >= edge, edge, begin_query)
    allowed = (key >= begin_query) & (key <= query) & (query - key < WINDOW)
    r.bias[...] = jnp.where(allowed, 0.0, -1e30)
    lane = iota((rows, PAIR), 1)
    rate = jnp.exp((lane % 32).astype(F32) * (-math.log(ROPE_BASE) / 32))
    angle = (place - begin).astype(F32) * rate
    r.cos[...] = jnp.cos(angle)
    sine = jnp.sin(angle)
    r.sin[...] = jnp.where(lane % 64 < 32, -sine, sine)


def rotated(value, cosine, sine):
    lane = iota(value.shape, 1)
    swapped = jnp.where(lane % 64 < 32, pltpu.roll(value, PAIR - 32, 1), pltpu.roll(value, 32, 1))
    return value * cosine + swapped * sine


def head_masks(rows):
    low = iota((rows, PAIR), 1) < 64
    return (jnp.where(low, 1.0, 0.0).astype(BF16), jnp.where(low, 0.0, 1.0).astype(BF16))


def attention_project(r, w_qkv, gain):
    width = r.x.shape[1]
    x = r.x[...]
    s1 = lax.rsqrt(jnp.mean(x * x, axis=1, keepdims=True) + EPS_NORM)
    r.s1[...] = s1
    r.h1[...] = (x * s1 * gain(0)).astype(BF16)

    def project(part, carry):
        value = dot(r.h1[...], w_qkv[:, aligned(part, width)])
        turn = jnp.where(part < 2, 1.0, 0.0)
        scale = jnp.where(part == 0, 0.125, 1.0)
        cosine = r.cos[...] * turn + (1.0 - turn)
        sine = r.sin[...] * turn
        for p in range(width // PAIR):
            low = rotated(value[:, p * PAIR : (p + 1) * PAIR], cosine, sine).astype(BF16)
            where = pl.ds(pl.multiple_of(part * width + p * PAIR, PAIR), PAIR)
            r.qkv[:, where] = (low.astype(F32) * scale).astype(BF16)
        return carry

    lax.fori_loop(0, 3, project, 0)


def attention_mix(r, w_out, gain):
    rows, width = r.x.shape
    masks = head_masks(rows)

    def pair(p, carry):
        query = r.qkv[:, aligned(p, PAIR)]
        key = r.qkv[:, aligned(p + width // PAIR, PAIR)]
        value = r.qkv[:, aligned(p + 2 * (width // PAIR), PAIR)]
        out = None
        for h in range(2):
            scores = dot_t(query * masks[h], key) + r.bias[...]
            weights = jnp.exp(scores - jnp.max(scores, axis=1, keepdims=True))
            total = jnp.sum(weights, axis=1, keepdims=True)
            attention = (weights * (1.0 / total)).astype(BF16)
            r.att[2 * p + h] = attention
            part = dot(attention, value * masks[h])
            out = part if out is None else out + part
        r.mix[:, aligned(p, PAIR)] = out.astype(BF16)
        return carry

    lax.fori_loop(0, width // PAIR, pair, 0)
    ao = dot(r.mix[...], w_out[...])
    r.ao[...] = ao
    x2 = r.x[...] + gain(1) * ao
    r.x2[...] = x2
    s2 = lax.rsqrt(jnp.mean(x2 * x2, axis=1, keepdims=True) + EPS_NORM)
    r.s2[...] = s2
    r.h2[...] = (x2 * s2 * gain(2)).astype(BF16)


def ffn_forward(r, w_up, w_down, grad_down=None):
    r.fo[...] = jnp.zeros_like(r.fo)
    slope = math.sqrt(2.0 / math.pi)

    def tile(t, carry):
        cols = aligned(t, TILE)
        pre = dot(r.h2[...], w_up[:, cols])
        square = pre * pre
        bent = jnp.tanh(slope * pre * (1.0 + 0.044715 * square))
        half = 0.5 * (1.0 + bent)
        act = (pre * half).astype(BF16)
        r.act[:, cols] = act
        turn = 0.5 * pre * (1.0 - bent * bent) * slope * (1.0 + 3.0 * 0.044715 * square)
        r.dg[:, cols] = (half + turn).astype(BF16)
        r.fo[...] += dot(act, w_down[cols, :])
        if grad_down is not None:
            put_rows(grad_down, t_dot(act, r.grad[...]), t)
        return carry

    lax.fori_loop(0, w_up.shape[1] // TILE, tile, 0)


def norm_back(stream, inverse, grad):
    mean = jnp.mean(grad * stream, axis=1, keepdims=True)
    return inverse * grad - stream * (inverse * inverse * inverse * mean)


def column_sum(value):
    return jnp.sum(value, axis=0, keepdims=True)


def put_columns(target, value, start):
    shape = target.shape
    value = value.astype(target.dtype).reshape(shape[:-1] + (value.shape[1],))
    target[(slice(None),) * (len(shape) - 1) + (pl.ds(start, value.shape[-1]),)] = value


def put_rows(target, value, tile):
    shape = target.shape
    value = value.astype(target.dtype)
    if len(shape) == 2:
        target[aligned(tile, value.shape[0]), :] = value
    else:
        target[tile // 2, tile % 2] = value.reshape(shape[2:])


def ffn_backward_begin(r, gain, gy_ref):
    r.grad[...] = (gain(3) * gy_ref[...].astype(F32)).astype(BF16)


def ffn_backward_tiles(r, w_up, w_down, grad_up, grad_down, first, last):
    if first == 0:
        r.acc[...] = jnp.zeros_like(r.acc)

    def tile(t, carry):
        cols = aligned(t, TILE)
        if grad_down is not None:
            put_rows(grad_down, t_dot(r.act[:, cols], r.grad[...]), t)
        grad_pre = (dot_t(r.grad[...], w_down[cols, :]) * r.dg[:, cols].astype(F32)).astype(BF16)
        put_columns(grad_up, t_dot(r.h2[...], grad_pre), pl.multiple_of(t * TILE, TILE))
        r.acc[...] += dot_t(grad_pre, w_up[:, cols])
        return carry

    lax.fori_loop(first, last, tile, 0)


def ffn_backward_end(r, gain, gy_ref, gain_out):
    gy = gy_ref[...].astype(F32)
    gain_out[3:4, :] = column_sum(gy * r.fo[...])
    back = r.acc[...]
    x2, s2 = r.x2[...], r.s2[...]
    gain_out[2:3, :] = column_sum(back * x2 * s2)
    r.gx[...] = gy + norm_back(x2, s2, back * gain(2))


def attention_backward_out(r, w_out, gain, grad_out, gain_out):
    gx = r.gx[...]
    gain_out[1:2, :] = column_sum(gx * r.ao[...])
    grad_attn = (gain(1) * gx).astype(BF16)
    put_columns(grad_out, t_dot(r.mix[...], grad_attn), 0)
    r.grad[...] = dot_t(grad_attn, w_out[...]).astype(BF16)


def attention_backward_pairs(r, first, last):
    rows, width = r.x.shape
    masks = head_masks(rows)
    pairs = width // PAIR

    def pair(p, carry):
        query = r.qkv[:, aligned(p, PAIR)]
        key = r.qkv[:, aligned(p + pairs, PAIR)]
        value = r.qkv[:, aligned(p + 2 * pairs, PAIR)]
        grad_mixed = r.grad[:, aligned(p, PAIR)]
        to_query = to_key = to_value = 0.0
        for h in range(2):
            attention = r.att[2 * p + h]
            mixed = grad_mixed * masks[h]
            to_value = to_value + t_dot(attention, mixed)
            weights = dot_t(mixed, value)
            wide = attention.astype(F32)
            mean = jnp.sum(wide * weights, axis=1, keepdims=True)
            scores = (wide * (weights - mean)).astype(BF16)
            to_query = to_query + dot(scores, key * masks[h])
            to_key = to_key + t_dot(scores, query * masks[h])
        cosine, sine = r.cos[...], -r.sin[...]
        r.qkv[:, aligned(p, PAIR)] = rotated(to_query * 0.125, cosine, sine).astype(BF16)
        r.qkv[:, aligned(p + pairs, PAIR)] = rotated(to_key, cosine, sine).astype(BF16)
        r.qkv[:, aligned(p + 2 * pairs, PAIR)] = to_value.astype(BF16)
        return carry

    lax.fori_loop(first, last, pair, 0)


def attention_backward_in(r, w_qkv, gain, grad_qkv, gain_out):
    r.acc[...] = jnp.zeros_like(r.acc)

    def part(t, carry):
        cols = aligned(t, TILE)
        put_columns(grad_qkv, t_dot(r.h1[...], r.qkv[:, cols]), pl.multiple_of(t * TILE, TILE))
        r.acc[...] += dot_t(r.qkv[:, cols], w_qkv[:, cols])
        return carry

    lax.fori_loop(0, w_qkv.shape[1] // TILE, part, 0)
    back = r.acc[...]
    x, s1 = r.x[...], r.s1[...]
    gain_out[0:1, :] = column_sum(back * x * s1)
    r.gx[...] = r.gx[...] + norm_back(x, s1, back * gain(0))


class Chunk:
    def __init__(self, rows, columns, order, kind=BF16, fold=0):
        self.rows, self.columns, self.order, self.kind, self.fold = rows, columns, order, kind, fold

    def shape(self, leading):
        return (2,) * leading + (self.rows, self.columns)

    def flat_rows(self):
        return self.rows * self.columns // 128 if self.columns > 128 else 8

    def bytes(self, bits):
        return 2**bits * self.rows * self.columns * (2 if self.kind == BF16 else 4)


def plan(chunks, work, bits, book_bytes):
    core, x, y = bits - 2, bits - 1, bits - 3
    free, pending, done = {}, [], []
    now = 0.0

    def carry(link, took):
        free[link] = max(now, free.get(link, 0.0)) + took
        return free[link]

    def begin(name, stage):
        if name == BOOKS:
            hops = 2 ** (bits - 3)
            if stage == 0:
                there = max(carry(y, hops * book_bytes / 40e3), carry(0, 1.5 * hops * book_bytes / 40e3))
            else:
                there = carry((None, core, x)[stage], (0, 4, 2)[stage] * book_bytes / (1, 400e3, 40e3)[stage])
            pending.append((there + 1.5, name, stage))
            return
        dim = chunks[name].order[stage]
        size = chunks[name].bytes(bits) / 2 ** (stage + 1)
        if dim == core:
            there = carry(core, size / 400e3)
        else:
            there = carry(max(dim, y - 1), size / 40e3)
            if dim < y - 1:
                there += size / 40e3
        pending.append((there + 1.5, name, stage))

    def finish(limit):
        nonlocal now
        acts = []
        while pending:
            pending.sort(key=lambda p: p[0])
            if pending[0][0] > limit:
                break
            at, name, stage = pending.pop(0)
            now = max(now, at) + (2.5 if name == BOOKS and stage < 2 else 0.4)
            acts.append((name, stage))
            if stage + 1 < (3 if name == BOOKS else bits):
                begin(name, stage + 1)
        return acts

    for took, _, names in work:
        now += took
        for name in names:
            begin(name, 0)
        done.append(finish(now))
    done.append(finish(math.inf))
    return done


def coordinates(step, count):
    return [step // 2 ** (count - 1 - i) % 2 for i in range(count)]


def store_flat(out_ref, value, fold):
    rows, columns = value.shape
    blocks = columns // 128
    if blocks == 1:
        out_ref[...] = value
        return
    folds = max(fold, 1)
    rows = rows // folds
    for part in range(folds):
        for i in range(blocks):
            out_ref[pl.ds(part * blocks + i, rows, stride=folds * blocks), :] = value[
                part * rows : (part + 1) * rows, i * 128 : (i + 1) * 128
            ]


class Halving:
    def __init__(self, chunks, bits, recv, outs, send_sem, recv_sem):
        self.chunks = chunks
        self.bits, self.recv, self.outs = bits, recv, outs
        self.send_sem, self.recv_sem = send_sem, recv_sem
        self.copies = {}
        dp, branch = lax.axis_index("dp"), lax.axis_index("branch")
        self.mine, self.partner = [], []
        for dim in range(bits - 1):
            weight = 2 ** (bits - 2 - dim)
            bit = dp // weight % 2
            self.mine.append(bit)
            self.partner.append({"dp": dp + weight * (1 - 2 * bit), "branch": branch})
        self.mine.append(branch)
        self.partner.append({"dp": dp, "branch": 1 - branch})

    def near_level(self, other):
        dp = lax.axis_index("dp")
        for i in range(self.bits - 2):
            if other >> i & 1:
                dp = dp + 2 ** (i + 1) * (1 - 2 * self.mine[self.bits - 3 - i])
        return {"dp": dp, "branch": lax.axis_index("branch")}

    def barrier(self):
        semaphore = pltpu.get_barrier_semaphore()
        levels = 2 ** (self.bits - 2)
        targets = self.partner[self.bits - 2 :] + [self.near_level(other) for other in range(1, levels)]
        for target in targets:
            pl.semaphore_signal(semaphore, inc=1, device_id=target, device_id_type=MESH)
        pl.semaphore_wait(semaphore, len(targets))

    def left(self, name, stage):
        return [d for d in range(self.bits) if d not in self.chunks[name].order[:stage]]

    def half(self, ref, name, stage, index):
        position = self.left(name, stage).index(self.chunks[name].order[stage])
        return ref.at[(slice(None),) * position + (index,)]

    def remote(self, source, target, device, *key):
        slot = len(self.copies)
        self.copies[key] = pltpu.make_async_remote_copy(
            src_ref=source,
            dst_ref=target,
            send_sem=self.send_sem.at[slot],
            recv_sem=self.recv_sem.at[slot],
            device_id=device,
            device_id_type=MESH,
        )
        self.copies[key].start()

    def send(self, name, stage, source):
        dim = self.chunks[name].order[stage]
        self.remote(source, self.recv[name][stage], self.partner[dim], name, stage)

    def send_half(self, name, stage, ref):
        dim = self.chunks[name].order[stage]
        self.send(name, stage, self.half(ref, name, stage, 1 - self.mine[dim]))

    def arrived(self, *key):
        self.copies[key].wait_recv()

    def add(self, name, stage, own):
        chunk = self.chunks[name]
        got = self.recv[name][stage]
        depth = self.bits - 1 - stage
        if stage == self.bits - 1:
            store_flat(self.outs(name), own[...].astype(F32) + got[...].astype(F32), chunk.fold)
            return

        def step(i, carry):
            where = tuple(coordinates(i, depth))
            got[where] = got[where] + own[where]
            return carry

        lax.fori_loop(0, 2**depth, step, 0)

    def finish(self, name, stage, own=None):
        chunk = self.chunks[name]
        self.arrived(name, stage)
        if own is None:
            dim = chunk.order[stage]
            own = self.half(self.recv[name][stage - 1], name, stage, self.mine[dim])
        self.add(name, stage, own)
        self.follow(name, stage)

    def follow(self, name, stage):
        if stage + 1 < self.bits:
            self.send_half(name, stage + 1, self.recv[name][stage])

    def drain(self):
        for copy in self.copies.values():
            copy.wait_send()


BOOKS = 0


def quantizer_latent(r):
    branch = lax.axis_index("branch")
    rows, width = r.x.shape
    levels = r.chosen.shape[0]
    latent = r.latent[...]
    sem_code, ac_code = r.chosen[0], r.ac[...]
    gquant = r.gquant[...]
    prediction = dot(sem_code, r.distill_v[...])
    target = r.wavlm_v[...].astype(F32)
    pred_norm = lax.rsqrt(jnp.sum(prediction * prediction, axis=1, keepdims=True) + EPS_COS)
    target_norm = lax.rsqrt(jnp.sum(target * target, axis=1, keepdims=True) + EPS_COS)
    cosine = jnp.sum(prediction * target, axis=1, keepdims=True) * (pred_norm * target_norm)
    grad_pred = (
        target * (-DISTILL * pred_norm * target_norm) + prediction * (DISTILL * cosine * pred_norm * pred_norm)
    ).astype(BF16)
    put_distill(r.t.distill, t_dot(sem_code, grad_pred))
    grad_sem = dot_t(gquant, r.pout_v[0]) + dot_t(grad_pred, r.distill_v[...])
    put_group(r.t.pout, 0, t_dot(sem_code, gquant))
    put_group(r.t.pout, 1, t_dot(ac_code, gquant))
    commit = 2.0 * BETA * (dot(latent, r.pin_v[0]) - sem_code.astype(F32))
    r.g_rows[0] = (grad_sem - commit).astype(BF16)
    to_sem = (grad_sem + commit).astype(BF16)

    grad_ac = dot_t(gquant, r.pout_v[1])
    residual = dot(latent, r.pin_v[1])
    for level in range(1, levels):
        residual = residual - r.chosen[level].astype(F32)
    carry = jnp.zeros_like(residual)
    for level in range(levels - 1, 0, -1):
        carry = carry + 2.0 * BETA * residual
        r.g_rows[level] = (grad_ac - carry).astype(BF16)
        residual = residual + r.chosen[level].astype(F32)
    to_ac = (grad_ac + carry).astype(BF16)
    put_group(r.t.pin, 0, t_dot(latent, to_sem))
    put_group(r.t.pin, 1, t_dot(latent, to_ac))
    r.gy[...] = dot_t(to_sem, r.pin_v[0]) + dot_t(to_ac, r.pin_v[1])


def put_group(target, group, value):
    if len(target.shape) == 2:
        target[group * value.shape[0] : (group + 1) * value.shape[0], :] = value.astype(target.dtype)
    else:
        target[group] = value.astype(target.dtype).reshape(target.shape[1:])


def put_distill(target, value):
    if len(target.shape) == 2:
        target[...] = value.astype(target.dtype)
        return
    columns = target.shape[-1]
    devices = math.prod(target.shape[:-2])
    value = value.reshape(devices, -1, value.shape[1])
    folded = [value[:, :, i : i + columns] for i in range(0, value.shape[2], columns)]
    target[...] = jnp.concatenate(folded, axis=1).astype(target.dtype).reshape(target.shape)


def one_hot_rows(codes, first, count):
    row = iota((count, codes.shape[1]), 0)
    return jnp.where(codes - first == row, 1.0, 0.0).astype(BF16)


def pick_codes(r):
    levels, _, entries, code_width = r.books.shape
    entries = entries * r.books.shape[1]
    rows = r.cos.shape[0]
    slots = r.ring.shape[0]
    branch = lax.axis_index("branch")
    own = r.codes[:, pl.ds(pl.multiple_of(branch * rows, rows), rows)]
    r.code_rows[...] = jnp.broadcast_to(own[:, None, :], r.code_rows.shape)
    columns = jnp.concatenate([own.astype(F32), jnp.zeros((PAIR - levels, rows), F32)], axis=0).T
    lane = iota(columns.shape, 1)
    entry = iota((rows, entries), 1)
    r.code_cols[...] = columns
    r.ac_sum[...] = jnp.zeros_like(r.ac_sum)

    def book(level):
        slot = level % slots
        return pltpu.make_async_copy(r.books.at[level], r.ring.at[slot], r.sem_book.at[slot])

    def pick(level, carry):
        code = jnp.sum(jnp.where(lane == level, r.code_cols[...], 0.0), axis=1, keepdims=True)
        one_hot = jnp.where(entry == code.astype(jnp.int32), 1.0, 0.0).astype(BF16)
        book(level).wait()
        got = dot(one_hot, r.ring[level % slots].reshape(entries, code_width))
        r.chosen[level] = got.astype(BF16)
        r.ac_sum[...] += jnp.where(level > 0, got, 0.0)

        @pl.when(level + slots < levels)
        def _():
            book(level + slots).start()

        return carry

    def begin():
        for level in range(slots):
            book(level).start()

    def run():
        lax.fori_loop(0, levels, pick, 0)
        r.ac[...] = r.ac_sum[...].astype(BF16)

    return begin, run


def step_kernel(chunks, bits, ins, outs, scratch):
    r = Refs({**ins, **outs, **scratch})
    t = r.t = Refs(r.t)
    r.att, r.g_rows = r.ring.at[0], r.ring.at[1]
    branch = lax.axis_index("branch")
    rows, width = r.tokens.shape
    levels, parts, entries, code_width = r.books.shape
    entries = entries * parts
    tiles = r.w_up_v.shape[1] // TILE
    pairs = width // PAIR
    moves = Moves(r.sem_move)
    begin_pick, run_pick = pick_codes(r)
    begin_pick()
    got_pout = [moves.start(r.pout_own.at[0], r.pout_v.at[branch])]
    got_pin = [moves.start(r.pin_own.at[0], r.pin_v.at[branch])]
    got_attention = [moves.start(r.dec_qkv, r.w_qkv_v), moves.start(r.dec_out, r.w_out_v)]
    got_ffn = [moves.start(r.dec_up, r.w_up_v), moves.start(r.dec_down, r.w_down_v)]
    got_attention_two = [moves.start(r.enc_qkv, r.w_qkv_e), moves.start(r.enc_out, r.w_out_e)]
    got_rest = [
        moves.start(r.wavlm.at[pl.ds(pl.multiple_of(branch * rows, rows), rows)], r.wavlm_v),
        moves.start(r.distill, r.distill_v),
    ]
    frame_tables(r)
    if chunks:
        sums = Halving(chunks, bits, r.recv, None, r.send_sem, r.recv_sem)
        mine, level = sums.mine[bits - 2], lax.axis_index("dp") // 2
        begin_row, begins = 0, {}
        for name in chunks:
            begins[name] = begin_row
            begin_row += chunks[name].flat_rows()
        sums.outs = lambda name: r.packed.at[pl.ds(begins[name], chunks[name].flat_rows())]
        sums.barrier()
        sums.remote(r.pout_own.at[0], r.pout_v.at[branch], sums.partner[bits - 1], POUT)
        sums.remote(r.pin_own.at[0], r.pin_v.at[branch], sums.partner[bits - 1], PIN)
    else:
        got_pout.append(moves.start(r.pout_other.at[0], r.pout_v.at[1 - branch]))
        got_pin.append(moves.start(r.pin_other.at[0], r.pin_v.at[1 - branch]))

    def wait(moves, other=None):
        for move in moves:
            move.wait()
        if chunks and other is not None:
            sums.arrived(other)

    def dec_gain(i):
        return r.vectors[1, i : i + 1, :]

    def enc_gain(i):
        return r.vectors[0, i : i + 1, :]

    def pick():
        run_pick()
        wait(got_pout, POUT)
        r.x[...] = dot(r.chosen[0], r.pout_v[0]) + dot(r.ac[...], r.pout_v[1])
        if chunks:
            for other in range(1, levels):
                target = sums.near_level(other)
                sums.remote(r.code_rows.at[target_level(target)], r.code_got.at[other], target, CODES, other)
            r.code_got[0] = r.code_rows[level]

    def target_level(target):
        return next(iter(target.values())) // 2

    def dec_project():
        wait(got_attention)
        attention_project(r, r.w_qkv_v, dec_gain)

    def dec_mix():
        attention_mix(r, r.w_out_v, dec_gain)

    def dec_ffn():
        wait(got_ffn)
        ffn_backward_begin(r, dec_gain, r.cotangent)
        ffn_forward(r, r.w_up_v, r.w_down_v, t.dec_down)
        r.decoded[...] = (r.x2[...] + dec_gain(3) * r.fo[...]).astype(BF16)

    def dec_ffn_back():
        ffn_backward_tiles(r, r.w_up_v, r.w_down_v, t.dec_up, None, 0, tiles)
        ffn_backward_end(r, dec_gain, r.cotangent, r.dec_gains)
        got_ffn[:] = [moves.start(r.enc_up, r.w_up_v), moves.start(r.enc_down, r.w_down_v)]

    def dec_out():
        attention_backward_out(r, r.w_out_v, dec_gain, t.dec_out, r.dec_gains)

    def attention_pairs(first, last):
        return lambda: attention_backward_pairs(r, first, last)

    def dec_in():
        attention_backward_in(r, r.w_qkv_v, dec_gain, t.dec_qkv, r.dec_gains)
        r.gquant[...] = r.gx[...].astype(BF16)

    def enc_project():
        r.x[...] = r.tokens[...].astype(F32)
        wait(got_attention_two)
        attention_project(r, r.w_qkv_e, enc_gain)

    def enc_mix():
        attention_mix(r, r.w_out_e, enc_gain)

    def enc_ffn():
        wait(got_ffn)
        ffn_forward(r, r.w_up_v, r.w_down_v)
        r.latent[...] = (r.x2[...] + enc_gain(3) * r.fo[...]).astype(BF16)

    def quantizer():
        wait(got_rest)
        wait(got_pin, PIN)
        quantizer_latent(r)
        if chunks:
            for other in range(1, levels):
                target = sums.near_level(other)
                sums.remote(r.g_rows.at[target_level(target)], r.g_got.at[other], target, BOOKS, 0, other)
            r.g_got[0] = r.g_rows[level]
        else:
            ffn_backward_begin(r, enc_gain, r.gy)

    def book_half(core, put):
        quarter = entries // 4
        for side in range(2):
            r.book_sum[...] = jnp.zeros_like(r.book_sum)
            first = (core * 2 + side) * quarter

            def add(source, carry):
                one_hot = one_hot_rows(r.code_got[source, 0:1, :], first, quarter)
                r.book_sum[...] += dot(one_hot, r.g_got[source])
                return carry

            lax.fori_loop(0, levels, add, 0)
            put(side, r.book_sum[...])

    def finish_books(stage):
        other_core, other_side = sums.partner[bits - 2], sums.partner[bits - 1]
        if stage == 0:
            for other in range(1, levels):
                sums.arrived(CODES, other)
                sums.arrived(BOOKS, 0, other)

            def put(side, value):
                r.book_send[side] = value.astype(BF16)

            book_half(1 - mine, put)
            sums.remote(r.book_send, r.book_got, other_core, BOOKS, 1)
        elif stage == 1:
            sums.arrived(BOOKS, 1)

            def put(side, value):
                r.book_got[side] = (value + r.book_got[side].astype(F32)).astype(BF16)

            book_half(mine, put)
            sums.remote(r.book_got.at[1 - branch], r.book_last, other_side, BOOKS, 2)
        else:
            sums.arrived(BOOKS, 2)
            total = r.book_got[branch].astype(F32) + r.book_last[...].astype(F32)
            store_flat(r.packed.at[pl.ds(begin_row, entries // 4 * code_width // 128)], total, 0)

    def all_books():
        parts = entries // TILE

        def one(step, carry):
            at = step // parts
            one_hot = one_hot_rows(r.code_rows[at, 0:1, :], step % parts * TILE, TILE)
            t.books[at, aligned(step % parts, TILE), :] = dot(one_hot, r.g_rows[at]).astype(BF16)
            return carry

        lax.fori_loop(0, levels * parts, one, 0)

    def enc_ffn_back(first, last):
        def run():
            if first == 0:
                ffn_backward_begin(r, enc_gain, r.gy)
            ffn_backward_tiles(r, r.w_up_v, r.w_down_v, t.enc_up, t.enc_down, first, last)
            if last == tiles:
                ffn_backward_end(r, enc_gain, r.gy, r.gains)

        return run

    def enc_out():
        attention_backward_out(r, r.w_out_e, enc_gain, t.enc_out, r.gains)

    def enc_in():
        attention_backward_in(r, r.w_qkv_e, enc_gain, t.enc_qkv, r.gains)
        r.grad_tokens[...] = r.gx[...]

    def spread_gains():
        for layer, ref in enumerate((r.gains, r.dec_gains)):
            for row in range(4):
                for block in range(width // 128):
                    owner = (layer * 4 + row) * (width // 128) + block
                    where = tuple(owner // 2 ** (bits - 1 - i) % 2 for i in range(bits))
                    t.vec[where] = jnp.broadcast_to(
                        ref[row : row + 1, block * 128 : (block + 1) * 128], t.vec.shape[bits:]
                    )

    names = list(chunks) if chunks else [None] * 12
    n_dec_down, n_dec_up, n_dec_out, n_dec_qkv, n_distill, n_pout, n_pin = names[:7]
    n_enc_down, n_enc_up, n_enc_out, n_enc_qkv, n_vec = names[7:]
    work = [
        (7.0, pick, ()),
        (2.0, dec_project, ()),
        (3.0, dec_mix, ()),
        (4.0, dec_ffn, (n_dec_down,)),
        (3.0, dec_ffn_back, (n_dec_up,)),
        (1.5, dec_out, (n_dec_out,)),
        (2.0, attention_pairs(0, pairs // 2), ()),
        (2.0, attention_pairs(pairs // 2, pairs), ()),
        (2.0, dec_in, (n_dec_qkv,)),
        (2.0, enc_project, ()),
        (3.0, enc_mix, ()),
        (3.0, enc_ffn, ()),
        (4.0, quantizer, (BOOKS, n_distill, n_pout, n_pin)),
        (2.5, enc_ffn_back(0, tiles // 2), ()),
        (2.5, enc_ffn_back(tiles // 2, tiles), (n_enc_down, n_enc_up)),
        (1.5, enc_out, (n_enc_out,)),
        (2.0, attention_pairs(0, pairs // 2), ()),
        (2.0, attention_pairs(pairs // 2, pairs), ()),
        (2.0, enc_in, (n_enc_qkv,)),
        (0.3, spread_gains, (n_vec,)),
    ]
    if not chunks:
        for _, run, _ in work[:13]:
            run()
        all_books()
        for _, run, _ in work[13:-1]:
            run()
        return
    actions = plan(chunks, work, bits, rows * code_width * 2)

    def finish(name, stage):
        if name == BOOKS:
            finish_books(stage)
        elif stage == 0:
            sums.finish(name, 0, sums.half(t[name], name, 0, mine))
        else:
            sums.finish(name, stage)

    for (_, run, made), acts in zip(work, actions):
        run()
        for name in made:
            if name != BOOKS:
                sums.send_half(name, 0, t[name])
        for name, stage in acts:
            finish(name, stage)
    for name, stage in actions[-1]:
        finish(name, stage)
    sums.drain()


POUT, PIN, CODES = 1, 2, 3


def step(given, devices, with_sums):
    rows, width = given.tokens.shape
    ff = given.enc_up.shape[1]
    levels, entries, code_width = given.books.shape
    given.books = given.books.reshape(levels, -1, rows, code_width)
    bits = devices.bit_length() - 1
    vmem, hbm = pl.BlockSpec(memory_space=pltpu.VMEM), pl.BlockSpec(memory_space=pl.ANY)
    scratch = layer_scratch(rows, width, ff)
    scratch.update(
        w_qkv_e=pltpu.VMEM((width, 3 * width), BF16),
        w_out_e=pltpu.VMEM((width, width), BF16),
        cos=pltpu.VMEM((rows, PAIR), F32),
        sin=pltpu.VMEM((rows, PAIR), F32),
        bias=pltpu.VMEM((rows, rows), F32),
        ring=pltpu.VMEM((4,) + given.books.shape[1:], BF16),
        code_rows=pltpu.VMEM((levels, 8, rows), jnp.int32),
        code_cols=pltpu.VMEM((rows, PAIR), F32),
        chosen=pltpu.VMEM((levels, rows, code_width), BF16),
        ac_sum=pltpu.VMEM((rows, code_width), F32),
        ac=pltpu.VMEM((rows, code_width), BF16),
        gquant=pltpu.VMEM((rows, width), BF16),
        gy=pltpu.VMEM((rows, width), F32),
        latent=pltpu.VMEM((rows, width), BF16),
        pin_v=pltpu.VMEM((2, width, code_width), BF16),
        pout_v=pltpu.VMEM((2, code_width, width), BF16),
        distill_v=pltpu.VMEM(given.distill.shape, BF16),
        wavlm_v=pltpu.VMEM((rows, given.wavlm.shape[1]), BF16),
        sem_move=pltpu.SemaphoreType.DMA((14,)),
        sem_book=pltpu.SemaphoreType.DMA((4,)),
    )
    outs = Refs(decoded=shaped((rows, width), BF16), grad_tokens=shaped((rows, width), F32))
    chunks = {}
    params = dict(vmem_limit_bytes=61 * 2**20)
    if with_sums:
        params.update(collective_id=0, has_side_effects=True)
        c, x, y = bits - 2, bits - 1, bits - 3
        b, a = range(y)
        share = width // devices
        chunks = dict(
            dec_down=Chunk(ff // devices, width, [c, a, y, b, x]),
            dec_up=Chunk(share, ff, [c, y, x, a, b]),
            dec_out=Chunk(share, width, [c, a, x, b, y]),
            dec_qkv=Chunk(share, 3 * width, [c, x, y, a, b]),
            distill=Chunk(16, width, [c, a, x, b, y], fold=2),
            pout=Chunk(share, width, [c, x, a, y, b]),
            pin=Chunk(2 * share, code_width, [c, y, x, a, b]),
            enc_down=Chunk(ff // devices, width, [c, x, y, a, b]),
            enc_up=Chunk(share, ff, [c, y, x, a, b]),
            enc_out=Chunk(share, width, [c, a, x, b, y]),
            enc_qkv=Chunk(share, 3 * width, [c, x, a, y, b]),
            vec=Chunk(8, 128, [c, x, y, a, b], kind=F32),
        )
        copies = len(chunks) * bits + 2 * levels + 2
        scratch.update(
            t={name: pltpu.VMEM(c.shape(bits), c.kind) for name, c in chunks.items()},
            recv={
                name: [pltpu.VMEM(c.shape(bits - 1 - stage), c.kind) for stage in range(bits)]
                for name, c in chunks.items()
            },
            gains=pltpu.VMEM((4, width), F32),
            dec_gains=pltpu.VMEM((4, width), F32),
            code_got=pltpu.VMEM((levels, 8, rows), jnp.int32),
            g_got=pltpu.VMEM((levels, rows, code_width), BF16),
            book_sum=pltpu.VMEM((entries // 4, code_width), F32),
            book_send=pltpu.VMEM((2, entries // 4, code_width), BF16),
            book_got=pltpu.VMEM((2, entries // 4, code_width), BF16),
            book_last=pltpu.VMEM((entries // 4, code_width), BF16),
            send_sem=pltpu.SemaphoreType.DMA((copies,)),
            recv_sem=pltpu.SemaphoreType.DMA((copies,)),
        )
        parts = {name: c.flat_rows() for name, c in chunks.items()}
        parts.update(books=entries // 4 * code_width // 128)
        outs.packed = shaped((sum(parts.values()), 128), F32)
    else:
        outs.update(gains=shaped((4, width), F32), dec_gains=shaped((4, width), F32))
        outs.t = dict(
            enc_qkv=shaped(given.enc_qkv.shape, BF16),
            enc_out=shaped(given.enc_out.shape, BF16),
            enc_up=shaped(given.enc_up.shape, BF16),
            enc_down=shaped(given.enc_down.shape, BF16),
            dec_qkv=shaped(given.enc_qkv.shape, BF16),
            dec_out=shaped(given.enc_out.shape, BF16),
            dec_up=shaped(given.enc_up.shape, BF16),
            dec_down=shaped(given.enc_down.shape, BF16),
            pin=shaped((2 * width, code_width), BF16),
            pout=shaped((2 * code_width, width), BF16),
            books=shaped((levels, entries, code_width), BF16),
            distill=shaped(given.distill.shape, BF16),
        )
    in_specs = dict.fromkeys(given, hbm)
    in_specs.update(
        lengths=pl.BlockSpec(memory_space=pltpu.SMEM), codes=vmem, vectors=vmem, tokens=vmem, cotangent=vmem
    )
    got = pl.pallas_call(
        functools.partial(step_kernel, chunks, bits),
        out_shape=dict(outs),
        in_specs=[in_specs],
        out_specs=jax.tree.map(lambda _: vmem, dict(outs)),
        scratch_shapes=[dict(scratch)],
        compiler_params=pltpu.CompilerParams(**params),
        name="step",
    )(dict(given))
    got = Refs(got)
    if not with_sums:
        return got
    def hand_on(ins, outs, semaphores):
        moves = Moves(semaphores)
        begin, started = 0, []
        for name, rows in parts.items():
            target = outs[name]
            started.append(moves.start(ins.packed.at[pl.ds(begin, target.shape[0])], target))
            begin += rows
        started.append(moves.start(ins.decoded, outs.decoded))
        started.append(moves.start(ins.grad_tokens, outs.grad_tokens))
        for move in started:
            move.wait()

    last = {name: shaped((rows, 128), F32) for name, rows in parts.items()}
    last.update(decoded=outs.decoded, grad_tokens=outs.grad_tokens)
    done = pl.pallas_call(
        lambda ins, outs, semaphores: hand_on(Refs(ins), Refs(outs), semaphores),
        out_shape=last,
        in_specs=[dict.fromkeys(got, hbm)],
        out_specs=dict.fromkeys(last, hbm),
        scratch_shapes=[pltpu.SemaphoreType.DMA((len(last),))],
        name="results",
    )(dict(got))
    return Refs(done)


def body(
    tokens,
    wavlm,
    cotangent,
    lengths,
    codes,
    enc_qkv,
    enc_out,
    enc_up,
    enc_down,
    dec_qkv,
    dec_out,
    dec_up,
    dec_down,
    vectors,
    proj_in,
    proj_out,
    codebooks,
    distill_proj,
):
    width = tokens.shape[1]
    devices = lax.axis_size("dp") * lax.axis_size("branch")
    with_sums = devices == 4 * codebooks.shape[0] and width // devices % 16 == 0
    given = Refs(
        tokens=tokens,
        wavlm=wavlm,
        cotangent=cotangent,
        lengths=lengths,
        codes=codes.T,
        enc_qkv=enc_qkv,
        enc_out=enc_out,
        enc_up=enc_up,
        enc_down=enc_down,
        dec_qkv=dec_qkv,
        dec_out=dec_out,
        dec_up=dec_up,
        dec_down=dec_down,
        vectors=vectors,
        pin_own=proj_in,
        pout_own=proj_out,
        books=codebooks,
        distill=distill_proj,
    )
    if with_sums:
        s = step(given, devices, True)
        sums = [s.enc_qkv, s.enc_out, s.enc_up, s.enc_down, s.dec_qkv, s.dec_out, s.dec_up, s.dec_down]
        sums = [part.reshape(-1) for part in sums + [s.vec[0], s.pin, s.pout, s.books, s.distill]]
    else:
        swap = [(0, 1), (1, 0)]
        given.pin_other = lax.ppermute(proj_in, "branch", swap)
        given.pout_other = lax.ppermute(proj_out, "branch", swap)
        s = step(given, devices, False)
        t = Refs(s.t)
        gains = jnp.concatenate([s.gains, s.dec_gains])
        local = [t.enc_qkv, t.enc_out, t.enc_up, t.enc_down, t.dec_qkv, t.dec_out, t.dec_up, t.dec_down]
        local += [gains, t.pin, t.pout, t.books, t.distill]
        sums = [
            lax.psum_scatter(part.astype(F32).reshape(-1), ("dp", "branch"), scatter_dimension=0, tiled=True)
            for part in local
        ]
    return (s.decoded, s.grad_tokens, *sums)


def solution(mesh):
    rows, whole = P(("dp", "branch"), None), P()
    placed = (rows, P("dp", None), rows, rows, P("dp", None)) + (whole,) * 9
    placed += (P("branch", None, None),) * 2 + (whole,) * 2
    return jax.shard_map(
        body,
        mesh=mesh,
        in_specs=placed,
        out_specs=(rows, rows) + (P(("dp", "branch")),) * 13,
        check_vma=False,
    )
```

```python
import functools
import math

import jax
import jax.numpy as jnp
from jax import lax
from jax.experimental import pallas as pl
from jax.experimental.pallas import tpu as pltpu
from jax.sharding import PartitionSpec as P

HEADS = 8
WINDOW = 250
EPS_NORM = 1e-05
EPS_COS = 1e-06
BETA = 0.25
DISTILL = 10.0
ROPE_BASE = 10000.0

MESH = pl.DeviceIdType.MESH
F32 = jnp.float32
BF16 = jnp.bfloat16
TILE = 512
PAIR = 128


def dot(left, right):
    return lax.dot_general(left, right, (((1,), (0,)), ((), ())), preferred_element_type=F32)


def dot_t(left, right):
    return lax.dot_general(left, right, (((1,), (1,)), ((), ())), preferred_element_type=F32)


def t_dot(left, right):
    return lax.dot_general(left, right, (((0,), (0,)), ((), ())), preferred_element_type=F32)


def iota(shape, dim):
    return lax.broadcasted_iota(jnp.int32, shape, dim)


def aligned(index, size):
    return pl.ds(pl.multiple_of(index * size, size), size)


class Refs(dict):
    __getattr__ = dict.__getitem__
    __setattr__ = dict.__setitem__


class Moves:
    def __init__(self, semaphores):
        self.semaphores, self.count = semaphores, 0

    def start(self, source, target):
        move = pltpu.make_async_copy(source, target, self.semaphores.at[self.count])
        self.count += 1
        move.start()
        return move


def layer_scratch(rows, width, ff):
    return Refs(
        x=pltpu.VMEM((rows, width), F32),
        s1=pltpu.VMEM((rows, 1), F32),
        h1=pltpu.VMEM((rows, width), BF16),
        qkv=pltpu.VMEM((rows, 3 * width), BF16),
        mix=pltpu.VMEM((rows, width), BF16),
        ao=pltpu.VMEM((rows, width), F32),
        x2=pltpu.VMEM((rows, width), F32),
        s2=pltpu.VMEM((rows, 1), F32),
        h2=pltpu.VMEM((rows, width), BF16),
        act=pltpu.VMEM((rows, ff), BF16),
        dg=pltpu.VMEM((rows, ff), BF16),
        fo=pltpu.VMEM((rows, width), F32),
        grad=pltpu.VMEM((rows, width), BF16),
        gx=pltpu.VMEM((rows, width), F32),
        acc=pltpu.VMEM((rows, width), F32),
        w_qkv_v=pltpu.VMEM((width, 3 * width), BF16),
        w_out_v=pltpu.VMEM((width, width), BF16),
        w_up_v=pltpu.VMEM((width, ff), BF16),
        w_down_v=pltpu.VMEM((ff, width), BF16),
    )


def shaped(shape, kind):
    return jax.ShapeDtypeStruct(shape, kind)


def frame_tables(r):
    rows = r.cos.shape[0]
    place = iota((rows, PAIR), 0)
    query, key = iota((rows, rows), 0), iota((rows, rows), 1)
    begin, begin_query = jnp.zeros_like(place), jnp.zeros_like(query)
    edge = 0
    for clip in range(r.lengths.shape[1] - 1):
        edge = edge + r.lengths[0, clip]
        begin = jnp.where(place >= edge, edge, begin)
        begin_query = jnp.where(query >= edge, edge, begin_query)
    allowed = (key >= begin_query) & (key <= query) & (query - key < WINDOW)
    r.bias[...] = jnp.where(allowed, 0.0, -1e30)
    lane = iota((rows, PAIR), 1)
    rate = jnp.exp((lane % 32).astype(F32) * (-math.log(ROPE_BASE) / 32))
    angle = (place - begin).astype(F32) * rate
    r.cos[...] = jnp.cos(angle)
    sine = jnp.sin(angle)
    r.sin[...] = jnp.where(lane % 64 < 32, -sine, sine)


def rotated(value, cosine, sine):
    lane = iota(value.shape, 1)
    swapped = jnp.where(lane % 64 < 32, pltpu.roll(value, PAIR - 32, 1), pltpu.roll(value, 32, 1))
    return value * cosine + swapped * sine


def head_masks(rows):
    low = iota((rows, PAIR), 1) < 64
    return (jnp.where(low, 1.0, 0.0).astype(BF16), jnp.where(low, 0.0, 1.0).astype(BF16))


def attention_project(r, w_qkv, gain):
    width = r.x.shape[1]
    x = r.x[...]
    s1 = lax.rsqrt(jnp.mean(x * x, axis=1, keepdims=True) + EPS_NORM)
    r.s1[...] = s1
    r.h1[...] = (x * s1 * gain(0)).astype(BF16)

    def project(part, carry):
        value = dot(r.h1[...], w_qkv[:, aligned(part, width)])
        turn = jnp.where(part < 2, 1.0, 0.0)
        scale = jnp.where(part == 0, 0.125, 1.0)
        cosine = r.cos[...] * turn + (1.0 - turn)
        sine = r.sin[...] * turn
        for p in range(width // PAIR):
            low = rotated(value[:, p * PAIR : (p + 1) * PAIR], cosine, sine).astype(BF16)
            where = pl.ds(pl.multiple_of(part * width + p * PAIR, PAIR), PAIR)
            r.qkv[:, where] = (low.astype(F32) * scale).astype(BF16)
        return carry

    lax.fori_loop(0, 3, project, 0)


def attention_mix(r, w_out, gain):
    rows, width = r.x.shape
    masks = head_masks(rows)

    def pair(p, carry):
        query = r.qkv[:, aligned(p, PAIR)]
        key = r.qkv[:, aligned(p + width // PAIR, PAIR)]
        value = r.qkv[:, aligned(p + 2 * (width // PAIR), PAIR)]
        out = None
        for h in range(2):
            scores = dot_t(query * masks[h], key) + r.bias[...]
            weights = jnp.exp(scores - jnp.max(scores, axis=1, keepdims=True))
            total = jnp.sum(weights, axis=1, keepdims=True)
            attention = (weights * (1.0 / total)).astype(BF16)
            r.att[2 * p + h] = attention
            part = dot(attention, value * masks[h])
            out = part if out is None else out + part
        r.mix[:, aligned(p, PAIR)] = out.astype(BF16)
        return carry

    lax.fori_loop(0, width // PAIR, pair, 0)
    ao = dot(r.mix[...], w_out[...])
    r.ao[...] = ao
    x2 = r.x[...] + gain(1) * ao
    r.x2[...] = x2
    s2 = lax.rsqrt(jnp.mean(x2 * x2, axis=1, keepdims=True) + EPS_NORM)
    r.s2[...] = s2
    r.h2[...] = (x2 * s2 * gain(2)).astype(BF16)


def ffn_forward(r, w_up, w_down, grad_down=None):
    r.fo[...] = jnp.zeros_like(r.fo)
    slope = math.sqrt(2.0 / math.pi)

    def tile(t, carry):
        cols = aligned(t, TILE)
        pre = dot(r.h2[...], w_up[:, cols])
        square = pre * pre
        bent = jnp.tanh(slope * pre * (1.0 + 0.044715 * square))
        half = 0.5 * (1.0 + bent)
        act = (pre * half).astype(BF16)
        r.act[:, cols] = act
        turn = 0.5 * pre * (1.0 - bent * bent) * slope * (1.0 + 3.0 * 0.044715 * square)
        r.dg[:, cols] = (half + turn).astype(BF16)
        r.fo[...] += dot(act, w_down[cols, :])
        if grad_down is not None:
            put_rows(grad_down, t_dot(act, r.grad[...]), t)
        return carry

    lax.fori_loop(0, w_up.shape[1] // TILE, tile, 0)


def norm_back(stream, inverse, grad):
    mean = jnp.mean(grad * stream, axis=1, keepdims=True)
    return inverse * grad - stream * (inverse * inverse * inverse * mean)


def column_sum(value):
    return jnp.sum(value, axis=0, keepdims=True)


class Place:
    def __init__(self, ref, col=0):
        self.ref, self.col = ref, col

    def shift(self, by):
        return Place(self.ref, self.col + by)

    def put(self, value):
        shape = self.ref.shape
        value = value.astype(self.ref.dtype).reshape(shape[:-1] + (value.shape[1],))
        self.ref[(slice(None),) * (len(shape) - 1) + (pl.ds(self.col, value.shape[-1]),)] = value


def put_rows(targets, value, tile):
    value = value.astype(BF16)
    columns = value.shape[1] // len(targets)
    for i, target in enumerate(targets):
        shape = target.shape
        part = value[:, i * columns : (i + 1) * columns]
        if len(shape) == 2:
            target[aligned(tile, value.shape[0]), :] = part
        else:
            target[tile // 2, tile % 2] = part.reshape(shape[2:])


def ffn_backward_begin(r, gain, gy_ref):
    r.grad[...] = (gain(3) * gy_ref[...].astype(F32)).astype(BF16)


def ffn_backward_tiles(r, w_up, w_down, grad_up, grad_down, first, last):
    if first == 0:
        r.acc[...] = jnp.zeros_like(r.acc)

    def tile(t, carry):
        cols = aligned(t, TILE)
        if grad_down is not None:
            put_rows(grad_down, t_dot(r.act[:, cols], r.grad[...]), t)
        grad_pre = (dot_t(r.grad[...], w_down[cols, :]) * r.dg[:, cols].astype(F32)).astype(BF16)
        grad_up.shift(pl.multiple_of((t - first) * TILE, TILE)).put(t_dot(r.h2[...], grad_pre))
        r.acc[...] += dot_t(grad_pre, w_up[:, cols])
        return carry

    lax.fori_loop(first, last, tile, 0)


def ffn_backward_end(r, gain, gy_ref, gain_out):
    gy = gy_ref[...].astype(F32)
    gain_out[3:4, :] = column_sum(gy * r.fo[...])
    back = r.acc[...]
    x2, s2 = r.x2[...], r.s2[...]
    gain_out[2:3, :] = column_sum(back * x2 * s2)
    r.gx[...] = gy + norm_back(x2, s2, back * gain(2))


def attention_backward_out(r, w_out, gain, grad_out, gain_out):
    gx = r.gx[...]
    gain_out[1:2, :] = column_sum(gx * r.ao[...])
    grad_attn = (gain(1) * gx).astype(BF16)
    grad_out.put(t_dot(r.mix[...], grad_attn))
    r.grad[...] = dot_t(grad_attn, w_out[...]).astype(BF16)


def attention_backward_pairs(r, first, last):
    rows, width = r.x.shape
    masks = head_masks(rows)
    pairs = width // PAIR

    def pair(p, carry):
        query = r.qkv[:, aligned(p, PAIR)]
        key = r.qkv[:, aligned(p + pairs, PAIR)]
        value = r.qkv[:, aligned(p + 2 * pairs, PAIR)]
        grad_mixed = r.grad[:, aligned(p, PAIR)]
        to_query = to_key = to_value = 0.0
        for h in range(2):
            attention = r.att[2 * p + h]
            mixed = grad_mixed * masks[h]
            to_value = to_value + t_dot(attention, mixed)
            weights = dot_t(mixed, value)
            wide = attention.astype(F32)
            mean = jnp.sum(wide * weights, axis=1, keepdims=True)
            scores = (wide * (weights - mean)).astype(BF16)
            to_query = to_query + dot(scores, key * masks[h])
            to_key = to_key + t_dot(scores, query * masks[h])
        cosine, sine = r.cos[...], -r.sin[...]
        r.qkv[:, aligned(p, PAIR)] = rotated(to_query * 0.125, cosine, sine).astype(BF16)
        r.qkv[:, aligned(p + pairs, PAIR)] = rotated(to_key, cosine, sine).astype(BF16)
        r.qkv[:, aligned(p + 2 * pairs, PAIR)] = to_value.astype(BF16)
        return carry

    lax.fori_loop(first, last, pair, 0)


def attention_backward_in(r, w_qkv, grad_qkv, part):
    width = r.x.shape[1]
    grad = r.qkv[:, part * width : (part + 1) * width]
    grad_qkv.put(t_dot(r.h1[...], grad))
    back = dot_t(grad, w_qkv[:, part * width : (part + 1) * width])
    r.acc[...] = back if part == 0 else r.acc[...] + back


def attention_backward_end(r, gain, gain_out):
    back = r.acc[...]
    x, s1 = r.x[...], r.s1[...]
    gain_out[0:1, :] = column_sum(back * x * s1)
    r.gx[...] = r.gx[...] + norm_back(x, s1, back * gain(0))


class Segment:
    def __init__(self, result, base, stride, col, blocks, row, rows):
        self.result, self.base, self.stride, self.col, self.blocks = result, base, stride, col, blocks
        self.row, self.rows = row, rows


class Chunk:
    def __init__(self, rows, columns, order, segments):
        self.rows, self.columns, self.order, self.segments = rows, columns, order, segments

    def shape(self, leading):
        return (2,) * leading + (self.rows, self.columns)

    def bytes(self, bits):
        return 2**bits * self.rows * self.columns * 2


def plan(chunks, work, bits, book_bytes):
    core, x, y = bits - 2, bits - 1, bits - 3
    free, pending, done = {}, [], []
    now = 0.0

    def carry(link, took):
        free[link] = max(now, free.get(link, 0.0)) + took
        return free[link]

    def begin(name, stage):
        if name == BOOKS:
            hops = 2 ** (bits - 3)
            if stage == 0:
                there = max(carry(y, hops * book_bytes / 40e3), carry(0, 1.5 * hops * book_bytes / 40e3))
            else:
                there = carry((None, core, x)[stage], (0, 4, 2)[stage] * book_bytes / (1, 400e3, 40e3)[stage])
            pending.append((there + 1.5, name, stage))
            return
        dim = chunks[name].order[stage]
        size = chunks[name].bytes(bits) / 2 ** (stage + 1)
        if dim == core:
            there = carry(core, size / 400e3)
        else:
            there = carry(max(dim, y - 1), size / 40e3)
            if dim < y - 1:
                there += size / 40e3
        pending.append((there + 1.5, name, stage))

    def finish(limit):
        nonlocal now
        acts = []
        while pending:
            pending.sort(key=lambda p: p[0])
            if pending[0][0] > limit:
                break
            at, name, stage = pending.pop(0)
            now = max(now, at) + (2.5 if name == BOOKS and stage < 2 else 0.4)
            acts.append((name, stage))
            if stage + 1 < (3 if name == BOOKS else bits):
                begin(name, stage + 1)
        return acts

    for took, _, names in work:
        now += took
        for name in names:
            begin(name, 0)
        done.append(finish(now))
    done.append(finish(math.inf))
    return done


def coordinates(step, count):
    return [step // 2 ** (count - 1 - i) % 2 for i in range(count)]


def store_segment(packed, first, segment, value):
    for i in range(segment.blocks):
        where = pl.ds(first + segment.base + i, segment.rows, stride=segment.stride)
        packed[where, :] = value[
            segment.row : segment.row + segment.rows, segment.col + i * 128 : segment.col + (i + 1) * 128
        ]


class Halving:
    def __init__(self, chunks, bits, recv, packed, first, send_sem, recv_sem):
        self.chunks = chunks
        self.bits, self.recv, self.packed, self.first = bits, recv, packed, first
        self.send_sem, self.recv_sem = send_sem, recv_sem
        self.copies = {}
        dp, branch = lax.axis_index("dp"), lax.axis_index("branch")
        self.mine, self.partner = [], []
        for dim in range(bits - 1):
            weight = 2 ** (bits - 2 - dim)
            bit = dp // weight % 2
            self.mine.append(bit)
            self.partner.append({"dp": dp + weight * (1 - 2 * bit), "branch": branch})
        self.mine.append(branch)
        self.partner.append({"dp": dp, "branch": 1 - branch})

    def near_level(self, other):
        dp = lax.axis_index("dp")
        for i in range(self.bits - 2):
            if other >> i & 1:
                dp = dp + 2 ** (i + 1) * (1 - 2 * self.mine[self.bits - 3 - i])
        return {"dp": dp, "branch": lax.axis_index("branch")}

    def barrier(self):
        semaphore = pltpu.get_barrier_semaphore()
        levels = 2 ** (self.bits - 2)
        targets = self.partner[self.bits - 2 :] + [self.near_level(other) for other in range(1, levels)]
        for target in targets:
            pl.semaphore_signal(semaphore, inc=1, device_id=target, device_id_type=MESH)
        pl.semaphore_wait(semaphore, len(targets))

    def left(self, name, stage):
        return [d for d in range(self.bits) if d not in self.chunks[name].order[:stage]]

    def half(self, ref, name, stage, index):
        position = self.left(name, stage).index(self.chunks[name].order[stage])
        return ref.at[(slice(None),) * position + (index,)]

    def remote(self, source, target, device, *key):
        slot = len(self.copies)
        self.copies[key] = pltpu.make_async_remote_copy(
            src_ref=source,
            dst_ref=target,
            send_sem=self.send_sem.at[slot],
            recv_sem=self.recv_sem.at[slot],
            device_id=device,
            device_id_type=MESH,
        )
        self.copies[key].start()

    def send(self, name, stage, source):
        dim = self.chunks[name].order[stage]
        self.remote(source, self.recv[name][stage], self.partner[dim], name, stage)

    def send_half(self, name, stage, ref):
        dim = self.chunks[name].order[stage]
        self.send(name, stage, self.half(ref, name, stage, 1 - self.mine[dim]))

    def arrived(self, *key):
        self.copies[key].wait_recv()

    def add(self, name, stage, own):
        chunk = self.chunks[name]
        got = self.recv[name][stage]
        depth = self.bits - 1 - stage
        if stage == self.bits - 1:
            value = own[...].astype(F32) + got[...].astype(F32)
            for segment in chunk.segments:
                store_segment(self.packed, self.first[segment.result], segment, value)
            return

        outer = max(depth - 2, 0)

        def step(i, carry):
            where = tuple(coordinates(i, outer))
            got[where] = got[where] + own[where]
            return carry

        lax.fori_loop(0, 2**outer, step, 0)

    def finish(self, name, stage, own=None):
        chunk = self.chunks[name]
        self.arrived(name, stage)
        if own is None:
            dim = chunk.order[stage]
            own = self.half(self.recv[name][stage - 1], name, stage, self.mine[dim])
        self.add(name, stage, own)
        self.follow(name, stage)

    def follow(self, name, stage):
        if stage + 1 < self.bits:
            self.send_half(name, stage + 1, self.recv[name][stage])

    def drain(self):
        for copy in self.copies.values():
            copy.wait_send()


BOOKS = "books"


def quantizer_latent(r):
    branch = lax.axis_index("branch")
    rows, width = r.x.shape
    levels = r.chosen.shape[0]
    latent = r.latent[...]
    sem_code, ac_code = r.chosen[0], r.ac[...]
    gquant = r.gquant[...]
    prediction = dot(sem_code, r.distill_v[...])
    target = r.wavlm_v[...].astype(F32)
    pred_norm = lax.rsqrt(jnp.sum(prediction * prediction, axis=1, keepdims=True) + EPS_COS)
    target_norm = lax.rsqrt(jnp.sum(target * target, axis=1, keepdims=True) + EPS_COS)
    cosine = jnp.sum(prediction * target, axis=1, keepdims=True) * (pred_norm * target_norm)
    grad_pred = (
        target * (-DISTILL * pred_norm * target_norm) + prediction * (DISTILL * cosine * pred_norm * pred_norm)
    ).astype(BF16)
    put_distill(r.places.distill, t_dot(sem_code, grad_pred))
    grad_sem = dot_t(gquant, r.pout_v[0]) + dot_t(grad_pred, r.distill_v[...])
    put_group(r.places.pout, 0, t_dot(sem_code, gquant))
    put_group(r.places.pout, 1, t_dot(ac_code, gquant))
    commit = 2.0 * BETA * (dot(latent, r.pin_v[0]) - sem_code.astype(F32))
    r.g_rows[0] = (grad_sem - commit).astype(BF16)
    to_sem = (grad_sem + commit).astype(BF16)

    grad_ac = dot_t(gquant, r.pout_v[1])
    residual = dot(latent, r.pin_v[1])
    for level in range(1, levels):
        residual = residual - r.chosen[level].astype(F32)
    carry = jnp.zeros_like(residual)
    for level in range(levels - 1, 0, -1):
        carry = carry + 2.0 * BETA * residual
        r.g_rows[level] = (grad_ac - carry).astype(BF16)
        residual = residual + r.chosen[level].astype(F32)
    to_ac = (grad_ac + carry).astype(BF16)
    put_group(r.places.pin, 0, t_dot(latent, to_sem))
    put_group(r.places.pin, 1, t_dot(latent, to_ac))
    r.gy[...] = dot_t(to_sem, r.pin_v[0]) + dot_t(to_ac, r.pin_v[1])


def put_group(place, group, value):
    target, rows = place.ref, value.shape[0]
    value = value.astype(target.dtype)
    if len(target.shape) == 2:
        target[group * rows : (group + 1) * rows, :] = value
        return
    lead, height = target.shape[1:-2], target.shape[-2]
    value = value.reshape(math.prod(lead), -1, height, value.shape[1])
    value = jnp.concatenate([value[:, i] for i in range(value.shape[1])], axis=2)
    columns = value.shape[2]
    where = (group,) + (slice(None),) * (len(lead) + 1) + (pl.ds(place.col, columns),)
    target[where] = value.reshape(lead + (height, columns))


def put_distill(place, value):
    target = place.ref
    if len(target.shape) == 2:
        target[...] = value.astype(target.dtype)
        return
    height = target.shape[-2]
    value = value.reshape(math.prod(target.shape[:-2]), -1, value.shape[1])
    columns = value.shape[2] * value.shape[1] // height
    value = jnp.concatenate([value[:, :, i : i + columns] for i in range(0, value.shape[2], columns)], axis=1)
    where = (slice(None),) * (len(target.shape) - 1) + (pl.ds(place.col, columns),)
    target[where] = value.astype(target.dtype).reshape(target.shape[:-1] + (columns,))


def one_hot_rows(codes, first, count):
    row = iota((count, codes.shape[1]), 0)
    return jnp.where(codes - first == row, 1.0, 0.0).astype(BF16)


def pick_codes(r):
    levels, _, entries, code_width = r.books.shape
    entries = entries * r.books.shape[1]
    rows = r.cos.shape[0]
    slots = r.ring.shape[0]
    branch = lax.axis_index("branch")
    own = r.codes[:, pl.ds(pl.multiple_of(branch * rows, rows), rows)]
    r.code_rows[...] = jnp.broadcast_to(own[:, None, :], r.code_rows.shape)
    columns = jnp.concatenate([own.astype(F32), jnp.zeros((PAIR - levels, rows), F32)], axis=0).T
    lane = iota(columns.shape, 1)
    entry = iota((rows, entries), 1)
    r.code_cols[...] = columns
    r.ac_sum[...] = jnp.zeros_like(r.ac_sum)

    def book(level):
        slot = level % slots
        return pltpu.make_async_copy(r.books.at[level], r.ring.at[slot], r.sem_book.at[slot])

    def pick(level, carry):
        code = jnp.sum(jnp.where(lane == level, r.code_cols[...], 0.0), axis=1, keepdims=True)
        one_hot = jnp.where(entry == code.astype(jnp.int32), 1.0, 0.0).astype(BF16)
        book(level).wait()
        got = dot(one_hot, r.ring[level % slots].reshape(entries, code_width))
        r.chosen[level] = got.astype(BF16)
        r.ac_sum[...] += jnp.where(level > 0, got, 0.0)

        @pl.when(level + slots < levels)
        def _():
            book(level + slots).start()

        return carry

    def begin():
        for level in range(slots):
            book(level).start()

    def run():
        lax.fori_loop(0, levels, pick, 0)
        r.ac[...] = r.ac_sum[...].astype(BF16)

    return begin, run


def step_kernel(chunks, first_rows, bits, ins, outs, scratch):
    r = Refs({**ins, **outs, **scratch})
    t = r.t = Refs(r.t)
    r.att, r.g_rows = r.ring.at[0], r.ring.at[1]
    branch = lax.axis_index("branch")
    rows, width = r.tokens.shape
    levels, parts, entries, code_width = r.books.shape
    entries = entries * parts
    tiles = r.w_up_v.shape[1] // TILE
    pairs = width // PAIR
    moves = Moves(r.sem_move)
    begin_pick, run_pick = pick_codes(r)
    begin_pick()
    got_pout = [moves.start(r.pout_own.at[0], r.pout_v.at[branch])]
    got_pin = [moves.start(r.pin_own.at[0], r.pin_v.at[branch])]
    got_attention = [moves.start(r.dec_qkv, r.w_qkv_v), moves.start(r.dec_out, r.w_out_v)]
    got_ffn = [moves.start(r.dec_up, r.w_up_v), moves.start(r.dec_down, r.w_down_v)]
    got_attention_two = [moves.start(r.enc_qkv, r.w_qkv_e), moves.start(r.enc_out, r.w_out_e)]
    got_rest = [
        moves.start(r.wavlm.at[pl.ds(pl.multiple_of(branch * rows, rows), rows)], r.wavlm_v),
        moves.start(r.distill, r.distill_v),
    ]
    frame_tables(r)
    if chunks:
        sums = Halving(chunks, bits, r.recv, r.packed, first_rows, r.send_sem, r.recv_sem)
        mine, level = sums.mine[bits - 2], lax.axis_index("dp") // 2
        sums.barrier()
        sums.remote(r.pout_own.at[0], r.pout_v.at[branch], sums.partner[bits - 1], POUT)
        sums.remote(r.pin_own.at[0], r.pin_v.at[branch], sums.partner[bits - 1], PIN)
    else:
        got_pout.append(moves.start(r.pout_other.at[0], r.pout_v.at[1 - branch]))
        got_pin.append(moves.start(r.pin_other.at[0], r.pin_v.at[1 - branch]))

    if chunks:
        down = dict(dec=[t.dd0, t.dd1], enc=[t.ed0, t.ed1])
        place = r.places = Refs(
            dec_up=[Place(t.du0), Place(t.du1)],
            dec_out=Place(t.da0),
            dec_qkv=[Place(t.da0, width), Place(t.da1), Place(t.da1, width)],
            enc_up=[Place(t.eu0), Place(t.eu1)],
            enc_out=Place(t.ea0),
            enc_qkv=[Place(t.ea0, width), Place(t.ea1), Place(t.ea2)],
            distill=Place(t.misc),
            pout=Place(t.misc, width),
            pin=Place(t.misc, 2 * width),
        )
    else:
        down = dict(dec=[t.dec_down], enc=[t.enc_down])
        place = r.places = Refs(
            dec_up=[Place(t.dec_up, i * tiles // 2 * TILE) for i in range(2)],
            dec_out=Place(t.dec_out),
            dec_qkv=[Place(t.dec_qkv, i * width) for i in range(3)],
            enc_up=[Place(t.enc_up, i * tiles // 2 * TILE) for i in range(2)],
            enc_out=Place(t.enc_out),
            enc_qkv=[Place(t.enc_qkv, i * width) for i in range(3)],
            distill=Place(t.distill),
            pout=Place(t.pout),
            pin=Place(t.pin),
        )
    dec_down, enc_down = down["dec"], down["enc"]

    def wait(moves, other=None):
        for move in moves:
            move.wait()
        if chunks and other is not None:
            sums.arrived(other)

    def dec_gain(i):
        return r.vectors[1, i : i + 1, :]

    def enc_gain(i):
        return r.vectors[0, i : i + 1, :]

    def pick():
        run_pick()
        wait(got_pout, POUT)
        r.x[...] = dot(r.chosen[0], r.pout_v[0]) + dot(r.ac[...], r.pout_v[1])
        if chunks:
            for other in range(1, levels):
                target = sums.near_level(other)
                sums.remote(r.code_rows.at[target_level(target)], r.code_got.at[other], target, CODES, other)
            r.code_got[0] = r.code_rows[level]

    def target_level(target):
        return next(iter(target.values())) // 2

    def dec_project():
        wait(got_attention)
        attention_project(r, r.w_qkv_v, dec_gain)

    def dec_mix():
        attention_mix(r, r.w_out_v, dec_gain)

    def dec_ffn():
        wait(got_ffn)
        ffn_backward_begin(r, dec_gain, r.cotangent)
        ffn_forward(r, r.w_up_v, r.w_down_v, dec_down)
        r.decoded[...] = (r.x2[...] + dec_gain(3) * r.fo[...]).astype(BF16)

    def dec_ffn_back(half):
        def run():
            first, last = half * tiles // 2, (half + 1) * tiles // 2
            ffn_backward_tiles(r, r.w_up_v, r.w_down_v, place.dec_up[half], None, first, last)
            if half == 1:
                ffn_backward_end(r, dec_gain, r.cotangent, r.dec_gains)
                got_ffn[:] = [moves.start(r.enc_up, r.w_up_v), moves.start(r.enc_down, r.w_down_v)]

        return run

    def dec_out():
        attention_backward_out(r, r.w_out_v, dec_gain, place.dec_out, r.dec_gains)

    def attention_pairs(first, last):
        return lambda: attention_backward_pairs(r, first, last)

    def dec_in(part):
        def run():
            attention_backward_in(r, r.w_qkv_v, place.dec_qkv[part], part)
            if part == 2:
                attention_backward_end(r, dec_gain, r.dec_gains)
                r.gquant[...] = r.gx[...].astype(BF16)

        return run

    def enc_project():
        r.x[...] = r.tokens[...].astype(F32)
        wait(got_attention_two)
        attention_project(r, r.w_qkv_e, enc_gain)

    def enc_mix():
        attention_mix(r, r.w_out_e, enc_gain)

    def enc_ffn():
        wait(got_ffn)
        ffn_forward(r, r.w_up_v, r.w_down_v)
        r.latent[...] = (r.x2[...] + enc_gain(3) * r.fo[...]).astype(BF16)

    def quantizer():
        wait(got_rest)
        wait(got_pin, PIN)
        quantizer_latent(r)
        if chunks:
            for other in range(1, levels):
                target = sums.near_level(other)
                sums.remote(r.g_rows.at[target_level(target)], r.g_got.at[other], target, BOOKS, 0, other)
            r.g_got[0] = r.g_rows[level]

    def book_half(core, put):
        quarter = entries // 4
        for side in range(2):
            r.book_sum[...] = jnp.zeros_like(r.book_sum)
            first = (core * 2 + side) * quarter

            def add(source, carry):
                one_hot = one_hot_rows(r.code_got[source, 0:1, :], first, quarter)
                r.book_sum[...] += dot(one_hot, r.g_got[source])
                return carry

            lax.fori_loop(0, levels, add, 0)
            put(side, r.book_sum[...])

    def finish_books(stage):
        other_core, other_side = sums.partner[bits - 2], sums.partner[bits - 1]
        if stage == 0:
            for other in range(1, levels):
                sums.arrived(CODES, other)
                sums.arrived(BOOKS, 0, other)

            def put(side, value):
                r.book_send[side] = value.astype(BF16)

            book_half(1 - mine, put)
            sums.remote(r.book_send, r.book_got, other_core, BOOKS, 1)
        elif stage == 1:
            sums.arrived(BOOKS, 1)

            def put(side, value):
                r.book_got[side] = (value + r.book_got[side].astype(F32)).astype(BF16)

            book_half(mine, put)
            sums.remote(r.book_got.at[1 - branch], r.book_last, other_side, BOOKS, 2)
        else:
            sums.arrived(BOOKS, 2)
            total = r.book_got[branch].astype(F32) + r.book_last[...].astype(F32)
            blocks = code_width // 128
            store_segment(r.packed, first_rows[BOOKS], Segment(BOOKS, 0, blocks, 0, blocks, 0, entries // 4), total)

    def all_books():
        parts = entries // TILE

        def one(step, carry):
            at = step // parts
            one_hot = one_hot_rows(r.code_rows[at, 0:1, :], step % parts * TILE, TILE)
            t.books[at, aligned(step % parts, TILE), :] = dot(one_hot, r.g_rows[at]).astype(BF16)
            return carry

        lax.fori_loop(0, levels * parts, one, 0)

    def enc_ffn_back(half):
        def run():
            first, last = half * tiles // 2, (half + 1) * tiles // 2
            if half == 0:
                ffn_backward_begin(r, enc_gain, r.gy)
            ffn_backward_tiles(r, r.w_up_v, r.w_down_v, place.enc_up[half], enc_down, first, last)
            if half == 1:
                ffn_backward_end(r, enc_gain, r.gy, r.gains)

        return run

    def enc_out():
        attention_backward_out(r, r.w_out_e, enc_gain, place.enc_out, r.gains)

    def enc_in(part):
        def run():
            attention_backward_in(r, r.w_qkv_e, place.enc_qkv[part], part)
            if part == 2:
                attention_backward_end(r, enc_gain, r.gains)
                r.grad_tokens[...] = r.gx[...]
                if chunks:
                    spread_gains()

        return run

    def spread_gains():
        lanes = pl.ds(width, 128)
        for layer, ref in enumerate((r.gains, r.dec_gains)):
            for row in range(4):
                for block in range(width // 128):
                    owner = (layer * 4 + row) * (width // 128) + block
                    where = tuple(owner // 2 ** (bits - 1 - i) % 2 for i in range(bits))
                    value = ref[row : row + 1, block * 128 : (block + 1) * 128]
                    rows_here = t.ea2.shape[bits]
                    t.ea2[where + (slice(None), lanes)] = jnp.broadcast_to(value, (rows_here, 128)).astype(BF16)

    work = [
        (9.0, pick, ()),
        (2.0, dec_project, ()),
        (3.0, dec_mix, ()),
        (4.0, dec_ffn, (DD0, DD1)),
        (1.5, dec_ffn_back(0), (DU0,)),
        (1.5, dec_ffn_back(1), (DU1,)),
        (1.5, dec_out, ()),
        (2.0, attention_pairs(0, pairs // 2), ()),
        (2.0, attention_pairs(pairs // 2, pairs), ()),
        (0.7, dec_in(0), (DA0,)),
        (0.7, dec_in(1), ()),
        (0.9, dec_in(2), (DA1,)),
        (2.0, enc_project, ()),
        (3.0, enc_mix, ()),
        (3.0, enc_ffn, ()),
        (4.0, quantizer, (BOOKS, MISC)),
        (2.5, enc_ffn_back(0), (EU0,)),
        (2.5, enc_ffn_back(1), (EU1, ED0, ED1)),
        (1.5, enc_out, ()),
        (2.0, attention_pairs(0, pairs // 2), ()),
        (2.0, attention_pairs(pairs // 2, pairs), ()),
        (0.7, enc_in(0), (EA0,)),
        (0.7, enc_in(1), (EA1,)),
        (1.2, enc_in(2), (EA2,)),
    ]
    if not chunks:
        for _, run, _ in work:
            run()
            if run is quantizer:
                all_books()
        return
    actions = plan(chunks, work, bits, rows * code_width * 2)

    def finish(name, stage):
        if name == BOOKS:
            finish_books(stage)
        elif stage == 0:
            sums.finish(name, 0, sums.half(t[name], name, 0, mine))
        else:
            sums.finish(name, stage)

    for (_, run, made), acts in zip(work, actions):
        run()
        for name in made:
            if name != BOOKS:
                sums.send_half(name, 0, t[name])
        for name, stage in acts:
            finish(name, stage)
    for name, stage in actions[-1]:
        finish(name, stage)
    sums.drain()


POUT, PIN, CODES = 1, 2, 3
DD0, DD1, DU0, DU1, DA0, DA1, MISC = "dd0", "dd1", "du0", "du1", "da0", "da1", "misc"
EU0, EU1, ED0, ED1, EA0, EA1, EA2 = "eu0", "eu1", "ed0", "ed1", "ea0", "ea1", "ea2"


def step(given, devices, with_sums):
    rows, width = given.tokens.shape
    ff = given.enc_up.shape[1]
    levels, entries, code_width = given.books.shape
    given.books = given.books.reshape(levels, -1, rows, code_width)
    bits = devices.bit_length() - 1
    vmem, hbm = pl.BlockSpec(memory_space=pltpu.VMEM), pl.BlockSpec(memory_space=pl.ANY)
    scratch = layer_scratch(rows, width, ff)
    scratch.update(
        w_qkv_e=pltpu.VMEM((width, 3 * width), BF16),
        w_out_e=pltpu.VMEM((width, width), BF16),
        cos=pltpu.VMEM((rows, PAIR), F32),
        sin=pltpu.VMEM((rows, PAIR), F32),
        bias=pltpu.VMEM((rows, rows), F32),
        ring=pltpu.VMEM((4,) + given.books.shape[1:], BF16),
        code_rows=pltpu.VMEM((levels, 8, rows), jnp.int32),
        code_cols=pltpu.VMEM((rows, PAIR), F32),
        chosen=pltpu.VMEM((levels, rows, code_width), BF16),
        ac_sum=pltpu.VMEM((rows, code_width), F32),
        ac=pltpu.VMEM((rows, code_width), BF16),
        gquant=pltpu.VMEM((rows, width), BF16),
        gy=pltpu.VMEM((rows, width), F32),
        latent=pltpu.VMEM((rows, width), BF16),
        pin_v=pltpu.VMEM((2, width, code_width), BF16),
        pout_v=pltpu.VMEM((2, code_width, width), BF16),
        distill_v=pltpu.VMEM(given.distill.shape, BF16),
        wavlm_v=pltpu.VMEM((rows, given.wavlm.shape[1]), BF16),
        sem_move=pltpu.SemaphoreType.DMA((14,)),
        sem_book=pltpu.SemaphoreType.DMA((4,)),
    )
    outs = Refs(decoded=shaped((rows, width), BF16), grad_tokens=shaped((rows, width), F32))
    chunks, first_rows = {}, {}
    params = dict(vmem_limit_bytes=61 * 2**20)
    if with_sums:
        params.update(collective_id=0, has_side_effects=True)
        c, x, y = bits - 2, bits - 1, bits - 3
        b, a = range(y)
        share = width // devices
        low, high = ff // devices, share
        wide, half, blocks = ff // 128, ff // 256, width // 128
        chunks = dict(
            dd0=Chunk(low, width // 2, [c, x, a, b, y], [Segment(3, 0, blocks, 0, blocks // 2, 0, low)]),
            dd1=Chunk(low, width // 2, [c, a, b, x, y], [Segment(3, blocks // 2, blocks, 0, blocks // 2, 0, low)]),
            du0=Chunk(high, ff // 2, [c, x, a, y, b], [Segment(2, 0, wide, 0, half, 0, high)]),
            du1=Chunk(high, ff // 2, [c, y, a, b, x], [Segment(2, half, wide, 0, half, 0, high)]),
            da0=Chunk(
                high,
                2 * width,
                [c, y, x, a, b],
                [
                    Segment(1, 0, blocks, 0, blocks, 0, high),
                    Segment(0, 0, 3 * blocks, width, blocks, 0, high),
                ],
            ),
            da1=Chunk(high, 2 * width, [c, x, y, a, b], [Segment(0, blocks, 3 * blocks, 0, 2 * blocks, 0, high)]),
            misc=Chunk(
                high,
                3 * width,
                [c, x, y, a, b],
                [
                    Segment(8, 0, 2 * blocks, 0, blocks, 0, high // 2),
                    Segment(8, blocks, 2 * blocks, 0, blocks, high // 2, high // 2),
                    Segment(9, 0, blocks, width, blocks, 0, high),
                    Segment(10, 0, blocks // 2, 2 * width, blocks // 2, 0, high),
                    Segment(10, high * blocks // 2, blocks // 2, 2 * width + code_width, blocks // 2, 0, high),
                ],
            ),
            eu0=Chunk(high, ff // 2, [c, x, y, a, b], [Segment(6, 0, wide, 0, half, 0, high)]),
            eu1=Chunk(high, ff // 2, [c, x, a, y, b], [Segment(6, half, wide, 0, half, 0, high)]),
            ed0=Chunk(low, width // 2, [c, y, x, a, b], [Segment(7, 0, blocks, 0, blocks // 2, 0, low)]),
            ed1=Chunk(low, width // 2, [c, x, a, y, b], [Segment(7, blocks // 2, blocks, 0, blocks // 2, 0, low)]),
            ea0=Chunk(
                high,
                2 * width,
                [c, x, y, a, b],
                [
                    Segment(5, 0, blocks, 0, blocks, 0, high),
                    Segment(4, 0, 3 * blocks, width, blocks, 0, high),
                ],
            ),
            ea1=Chunk(high, width, [c, a, y, b, x], [Segment(4, blocks, 3 * blocks, 0, blocks, 0, high)]),
            ea2=Chunk(
                high,
                width + 128,
                [c, y, a, x, b],
                [
                    Segment(4, 2 * blocks, 3 * blocks, 0, blocks, 0, high),
                    Segment(11, 0, 1, width, 1, 0, 8),
                ],
            ),
        )
        rows_of = [high * 3 * blocks, high * blocks, high * wide, low * blocks] * 2
        rows_of += [high * blocks, high * blocks, high * blocks, 8, entries // 4 * code_width // 128]
        first_rows = {i: sum(rows_of[:i]) for i in range(len(rows_of))}
        first_rows[BOOKS] = first_rows[len(rows_of) - 1]
        copies = len(chunks) * bits + 2 * levels + 2
        scratch.update(
            t={name: pltpu.VMEM(c.shape(bits), BF16) for name, c in chunks.items()},
            recv={
                name: [pltpu.VMEM(c.shape(bits - 1 - stage), BF16) for stage in range(bits)]
                for name, c in chunks.items()
            },
            gains=pltpu.VMEM((4, width), F32),
            dec_gains=pltpu.VMEM((4, width), F32),
            code_got=pltpu.VMEM((levels, 8, rows), jnp.int32),
            g_got=pltpu.VMEM((levels, rows, code_width), BF16),
            book_sum=pltpu.VMEM((entries // 4, code_width), F32),
            book_send=pltpu.VMEM((2, entries // 4, code_width), BF16),
            book_got=pltpu.VMEM((2, entries // 4, code_width), BF16),
            book_last=pltpu.VMEM((entries // 4, code_width), BF16),
            send_sem=pltpu.SemaphoreType.DMA((copies,)),
            recv_sem=pltpu.SemaphoreType.DMA((copies,)),
        )
        outs.packed = shaped((sum(rows_of), 128), F32)
    else:
        outs.update(gains=shaped((4, width), F32), dec_gains=shaped((4, width), F32))
        outs.t = dict(
            enc_qkv=shaped(given.enc_qkv.shape, BF16),
            enc_out=shaped(given.enc_out.shape, BF16),
            enc_up=shaped(given.enc_up.shape, BF16),
            enc_down=shaped(given.enc_down.shape, BF16),
            dec_qkv=shaped(given.enc_qkv.shape, BF16),
            dec_out=shaped(given.enc_out.shape, BF16),
            dec_up=shaped(given.enc_up.shape, BF16),
            dec_down=shaped(given.enc_down.shape, BF16),
            pin=shaped((2 * width, code_width), BF16),
            pout=shaped((2 * code_width, width), BF16),
            books=shaped((levels, entries, code_width), BF16),
            distill=shaped(given.distill.shape, BF16),
        )
    in_specs = dict.fromkeys(given, hbm)
    in_specs.update(
        lengths=pl.BlockSpec(memory_space=pltpu.SMEM), codes=vmem, vectors=vmem, tokens=vmem, cotangent=vmem
    )
    got = pl.pallas_call(
        functools.partial(step_kernel, chunks, first_rows, bits),
        out_shape=dict(outs),
        in_specs=[in_specs],
        out_specs=jax.tree.map(lambda _: vmem, dict(outs)),
        scratch_shapes=[dict(scratch)],
        compiler_params=pltpu.CompilerParams(**params),
        name="step",
    )(dict(given))
    got = Refs(got)
    if not with_sums:
        return got
    last = [shaped((rows, 128), F32) for rows in rows_of]
    last[11] = shaped((1, 128), F32)

    def hand_on(packed_ref, decoded_ref, grad_ref, *out_refs):
        for i, ref in enumerate(out_refs[:-2]):
            ref[...] = packed_ref[pl.ds(first_rows[i], ref.shape[0]), :]
        out_refs[-2][...] = decoded_ref[...]
        out_refs[-1][...] = grad_ref[...]

    return pl.pallas_call(
        hand_on,
        out_shape=last + [outs.decoded, outs.grad_tokens],
        in_specs=[vmem] * 3,
        out_specs=[vmem] * (len(last) + 2),
        compiler_params=pltpu.CompilerParams(vmem_limit_bytes=32 * 2**20),
        name="results",
    )(got.packed, got.decoded, got.grad_tokens)


def body(
    tokens,
    wavlm,
    cotangent,
    lengths,
    codes,
    enc_qkv,
    enc_out,
    enc_up,
    enc_down,
    dec_qkv,
    dec_out,
    dec_up,
    dec_down,
    vectors,
    proj_in,
    proj_out,
    codebooks,
    distill_proj,
):
    width = tokens.shape[1]
    devices = lax.axis_size("dp") * lax.axis_size("branch")
    with_sums = devices == 4 * codebooks.shape[0] and width // devices % 16 == 0
    given = Refs(
        tokens=tokens,
        wavlm=wavlm,
        cotangent=cotangent,
        lengths=lengths,
        codes=codes.T,
        enc_qkv=enc_qkv,
        enc_out=enc_out,
        enc_up=enc_up,
        enc_down=enc_down,
        dec_qkv=dec_qkv,
        dec_out=dec_out,
        dec_up=dec_up,
        dec_down=dec_down,
        vectors=vectors,
        pin_own=proj_in,
        pout_own=proj_out,
        books=codebooks,
        distill=distill_proj,
    )
    if with_sums:
        *sums, decoded, grad_tokens = step(given, devices, True)
        sums = [part.reshape(-1) for part in sums]
        order = (4, 5, 6, 7, 0, 1, 2, 3, 11, 10, 9, 12, 8)
        return (decoded, grad_tokens, *[sums[i] for i in order])
    swap = [(0, 1), (1, 0)]
    given.pin_other = lax.ppermute(proj_in, "branch", swap)
    given.pout_other = lax.ppermute(proj_out, "branch", swap)
    s = step(given, devices, False)
    t = Refs(s.t)
    gains = jnp.concatenate([s.gains, s.dec_gains])
    local = [t.enc_qkv, t.enc_out, t.enc_up, t.enc_down, t.dec_qkv, t.dec_out, t.dec_up, t.dec_down]
    local += [gains, t.pin, t.pout, t.books, t.distill]
    sums = [
        lax.psum_scatter(part.astype(F32).reshape(-1), ("dp", "branch"), scatter_dimension=0, tiled=True)
        for part in local
    ]
    return (s.decoded, s.grad_tokens, *sums)


def solution(mesh):
    rows, whole = P(("dp", "branch"), None), P()
    placed = (rows, P("dp", None), rows, rows, P("dp", None)) + (whole,) * 9
    placed += (P("branch", None, None),) * 2 + (whole,) * 2
    return jax.shard_map(
        body,
        mesh=mesh,
        in_specs=placed,
        out_specs=(rows, rows) + (P(("dp", "branch")),) * 13,
        check_vma=False,
    )
```

```python
import functools
import math

import jax
import jax.numpy as jnp
from jax import lax
from jax.experimental import pallas as pl
from jax.experimental.pallas import tpu as pltpu
from jax.sharding import PartitionSpec as P

HEADS = 8
WINDOW = 250
EPS_NORM = 1e-05
EPS_COS = 1e-06
BETA = 0.25
DISTILL = 10.0
ROPE_BASE = 10000.0

MESH = pl.DeviceIdType.MESH
F32 = jnp.float32
BF16 = jnp.bfloat16
TILE = 512
PAIR = 128


def dot(left, right):
    return lax.dot_general(left, right, (((1,), (0,)), ((), ())), preferred_element_type=F32)


def dot_t(left, right):
    return lax.dot_general(left, right, (((1,), (1,)), ((), ())), preferred_element_type=F32)


def t_dot(left, right):
    return lax.dot_general(left, right, (((0,), (0,)), ((), ())), preferred_element_type=F32)


def iota(shape, dim):
    return lax.broadcasted_iota(jnp.int32, shape, dim)


def aligned(index, size):
    return pl.ds(pl.multiple_of(index * size, size), size)


class Refs(dict):
    __getattr__ = dict.__getitem__
    __setattr__ = dict.__setitem__


class Moves:
    def __init__(self, semaphores):
        self.semaphores, self.count = semaphores, 0

    def start(self, source, target):
        move = pltpu.make_async_copy(source, target, self.semaphores.at[self.count])
        self.count += 1
        move.start()
        return move


def layer_scratch(rows, width, ff):
    return Refs(
        x=pltpu.VMEM((rows, width), F32),
        s1=pltpu.VMEM((rows, 1), F32),
        h=pltpu.VMEM((rows, width), BF16),
        h1t=pltpu.VMEM((width, rows), BF16),
        h2t=pltpu.VMEM((width, rows), BF16),
        rinv=pltpu.VMEM((rows, width), F32),
        qkv=pltpu.VMEM((rows, 3 * width), BF16),
        mix=pltpu.VMEM((rows, width), BF16),
        ao=pltpu.VMEM((rows, width), F32),
        x2=pltpu.VMEM((rows, width), F32),
        s2=pltpu.VMEM((rows, 1), F32),
        act=pltpu.VMEM((rows, ff), BF16),
        dg=pltpu.VMEM((rows, ff), BF16),
        fo=pltpu.VMEM((rows, width), F32),
        grad=pltpu.VMEM((rows, width), BF16),
        gx=pltpu.VMEM((rows, width), F32),
        acc=pltpu.VMEM((rows, width), F32),
        w_qkv_v=pltpu.VMEM((width, 3 * width), BF16),
        w_out_v=pltpu.VMEM((width, width), BF16),
        w_up_v=pltpu.VMEM((width, ff), BF16),
        w_down_v=pltpu.VMEM((ff, width), BF16),
    )


def shaped(shape, kind):
    return jax.ShapeDtypeStruct(shape, kind)


def frame_tables(r):
    rows = r.cos.shape[0]
    place = iota((rows, PAIR), 0)
    query, key = iota((rows, rows), 0), iota((rows, rows), 1)
    begin, begin_query = jnp.zeros_like(place), jnp.zeros_like(query)
    edge = 0
    for clip in range(r.lengths.shape[1] - 1):
        edge = edge + r.lengths[0, clip]
        begin = jnp.where(place >= edge, edge, begin)
        begin_query = jnp.where(query >= edge, edge, begin_query)
    allowed = (key >= begin_query) & (key <= query) & (query - key < WINDOW)
    r.bias[...] = jnp.where(allowed, 0.0, -1e30)
    lane = iota((rows, PAIR), 1)
    rate = jnp.exp((lane % 32).astype(F32) * (-math.log(ROPE_BASE) / 32))
    angle = (place - begin).astype(F32) * rate
    r.cos[...] = jnp.cos(angle)
    sine = jnp.sin(angle)
    r.sin[...] = jnp.where(lane % 64 < 32, -sine, sine)


def rotated(value, cosine, sine):
    lane = iota(value.shape, 1)
    swapped = jnp.where(lane % 64 < 32, pltpu.roll(value, PAIR - 32, 1), pltpu.roll(value, 32, 1))
    return value * cosine + swapped * sine


def head_masks(rows):
    low = iota((rows, PAIR), 1) < 64
    return (jnp.where(low, 1.0, 0.0).astype(BF16), jnp.where(low, 0.0, 1.0).astype(BF16))


def attention_project(r, w_qkv, gain):
    width = r.x.shape[1]
    x = r.x[...]
    s1 = lax.rsqrt(jnp.mean(x * x, axis=1, keepdims=True) + EPS_NORM)
    r.s1[...] = s1
    h = (x * s1 * gain(0)).astype(BF16)
    r.h[...] = h
    r.h1t[...] = h.T

    def project(part, carry):
        value = dot(r.h[...], w_qkv[:, aligned(part, width)])
        turn = jnp.where(part < 2, 1.0, 0.0)
        scale = jnp.where(part == 0, 0.125, 1.0)
        cosine = r.cos[...] * turn + (1.0 - turn)
        sine = r.sin[...] * turn
        for p in range(width // PAIR):
            low = rotated(value[:, p * PAIR : (p + 1) * PAIR], cosine, sine).astype(BF16)
            where = pl.ds(pl.multiple_of(part * width + p * PAIR, PAIR), PAIR)
            r.qkv[:, where] = (low.astype(F32) * scale).astype(BF16)
        return carry

    lax.fori_loop(0, 3, project, 0)


def attention_mix(r, w_out, gain):
    rows, width = r.x.shape
    masks = head_masks(rows)
    low = iota((rows, PAIR), 1) < 64

    def pair(p, carry):
        query = r.qkv[:, aligned(p, PAIR)]
        key = r.qkv[:, aligned(p + width // PAIR, PAIR)]
        value = r.qkv[:, aligned(p + 2 * (width // PAIR), PAIR)]
        outs = []
        for h in range(2):
            scores = dot_t(query * masks[h], key) + r.bias[...]
            weights = jnp.exp(scores - jnp.max(scores, axis=1, keepdims=True)).astype(BF16)
            r.att[2 * p + h] = weights
            outs.append(dot(weights, value * masks[h] + masks[1 - h]))
        inverse = 1.0 / pltpu.roll(jnp.where(low, outs[1], outs[0]), 64, 1)
        r.rinv[:, aligned(p, PAIR)] = inverse
        r.mix[:, aligned(p, PAIR)] = (jnp.where(low, outs[0], outs[1]) * inverse).astype(BF16)
        return carry

    lax.fori_loop(0, width // PAIR, pair, 0)
    ao = dot(r.mix[...], w_out[...])
    r.ao[...] = ao
    x2 = r.x[...] + gain(1) * ao
    r.x2[...] = x2
    s2 = lax.rsqrt(jnp.mean(x2 * x2, axis=1, keepdims=True) + EPS_NORM)
    r.s2[...] = s2
    h = (x2 * s2 * gain(2)).astype(BF16)
    r.h[...] = h
    r.h2t[...] = h.T


def ffn_forward(r, w_up, w_down, grad_down=None):
    r.fo[...] = jnp.zeros_like(r.fo)
    slope = math.sqrt(2.0 / math.pi)

    def tile(t, carry):
        cols = aligned(t, TILE)
        pre = dot(r.h[...], w_up[:, cols])
        square = pre * pre
        bent = jnp.tanh(slope * pre * (1.0 + 0.044715 * square))
        half = 0.5 * (1.0 + bent)
        act = (pre * half).astype(BF16)
        r.act[:, cols] = act
        turn = 0.5 * pre * (1.0 - bent * bent) * slope * (1.0 + 3.0 * 0.044715 * square)
        r.dg[:, cols] = (half + turn).astype(BF16)
        r.fo[...] += dot(act, w_down[cols, :])
        if grad_down is not None:
            put_rows(grad_down, t_dot(act, r.grad[...]), t)
        return carry

    lax.fori_loop(0, w_up.shape[1] // TILE, tile, 0)


def norm_back(stream, inverse, grad):
    mean = jnp.mean(grad * stream, axis=1, keepdims=True)
    return inverse * grad - stream * (inverse * inverse * inverse * mean)


def column_sum(value):
    return jnp.sum(value, axis=0, keepdims=True)


class Place:
    def __init__(self, ref, col=0):
        self.ref, self.col = ref, col

    def shift(self, by):
        return Place(self.ref, self.col + by)

    def put(self, value):
        shape = self.ref.shape
        value = value.astype(self.ref.dtype).reshape(shape[:-1] + (value.shape[1],))
        self.ref[(slice(None),) * (len(shape) - 1) + (pl.ds(self.col, value.shape[-1]),)] = value


def put_rows(targets, value, tile):
    value = value.astype(BF16)
    columns = value.shape[1] // len(targets)
    for i, target in enumerate(targets):
        shape = target.shape
        part = value[:, i * columns : (i + 1) * columns]
        if len(shape) == 2:
            target[aligned(tile, value.shape[0]), :] = part
        else:
            target[tile // 2, tile % 2] = part.reshape(shape[2:])


def ffn_backward_begin(r, gain, gy_ref):
    r.grad[...] = (gain(3) * gy_ref[...].astype(F32)).astype(BF16)


def ffn_backward_tiles(r, w_up, w_down, grad_up, grad_down, first, last):
    if first == 0:
        r.acc[...] = jnp.zeros_like(r.acc)

    def tile(t, carry):
        cols = aligned(t, TILE)
        if grad_down is not None:
            put_rows(grad_down, t_dot(r.act[:, cols], r.grad[...]), t)
        grad_pre = (dot_t(r.grad[...], w_down[cols, :]) * r.dg[:, cols].astype(F32)).astype(BF16)
        grad_up.shift(pl.multiple_of((t - first) * TILE, TILE)).put(dot(r.h2t[...], grad_pre))
        r.acc[...] += dot_t(grad_pre, w_up[:, cols])
        return carry

    lax.fori_loop(first, last, tile, 0)


def ffn_backward_end(r, gain, gy_ref, gain_out):
    gy = gy_ref[...].astype(F32)
    gain_out[3:4, :] = column_sum(gy * r.fo[...])
    back = r.acc[...]
    x2, s2 = r.x2[...], r.s2[...]
    gain_out[2:3, :] = column_sum(back * x2 * s2)
    r.gx[...] = gy + norm_back(x2, s2, back * gain(2))


def attention_backward_out(r, w_out, gain, grad_out, gain_out):
    gx = r.gx[...]
    gain_out[1:2, :] = column_sum(gx * r.ao[...])
    grad_attn = (gain(1) * gx).astype(BF16)
    grad_out.put(t_dot(r.mix[...], grad_attn))
    r.grad[...] = dot_t(grad_attn, w_out[...]).astype(BF16)


def attention_backward_pairs(r, first, last):
    rows, width = r.x.shape
    masks = head_masks(rows)
    masks_t = [jnp.where((iota((PAIR, rows), 0) < 64) == (h == 0), 1.0, 0.0).astype(BF16) for h in range(2)]
    pairs = width // PAIR

    def pair(p, carry):
        query = r.qkv[:, aligned(p, PAIR)]
        key = r.qkv[:, aligned(p + pairs, PAIR)]
        value = r.qkv[:, aligned(p + 2 * pairs, PAIR)]
        grad_mixed = (r.grad[:, aligned(p, PAIR)].astype(F32) * r.rinv[:, aligned(p, PAIR)]).astype(BF16)
        product = (grad_mixed.astype(F32) * r.mix[:, aligned(p, PAIR)].astype(F32)).astype(BF16)
        beside = jnp.concatenate([value, jnp.full(value.shape, -1.0, BF16)], axis=1)
        query_t, grad_t = query.T, grad_mixed.T
        to_query = to_key = to_value = 0.0
        for h in range(2):
            weights = r.att[2 * p + h]
            change = dot_t(jnp.concatenate([grad_mixed * masks[h], product * masks[h]], axis=1), beside)
            scores = (weights.astype(F32) * change).astype(BF16)
            to_query = to_query + dot(scores, key * masks[h])
            to_key = to_key + dot(query_t * masks_t[h], scores)
            to_value = to_value + dot(grad_t * masks_t[h], weights)
        cosine, sine = r.cos[...], -r.sin[...]
        r.qkv[:, aligned(p, PAIR)] = rotated(to_query * 0.125, cosine, sine).astype(BF16)
        r.qkv[:, aligned(p + pairs, PAIR)] = rotated(to_key.T, cosine, sine).astype(BF16)
        r.qkv[:, aligned(p + 2 * pairs, PAIR)] = to_value.T.astype(BF16)
        return carry

    lax.fori_loop(first, last, pair, 0)


def attention_backward_in(r, w_qkv, grad_qkv, part):
    width = r.x.shape[1]
    grad = r.qkv[:, part * width : (part + 1) * width]
    grad_qkv.put(dot(r.h1t[...], grad))
    back = dot_t(grad, w_qkv[:, part * width : (part + 1) * width])
    r.acc[...] = back if part == 0 else r.acc[...] + back


def attention_backward_end(r, gain, gain_out):
    back = r.acc[...]
    x, s1 = r.x[...], r.s1[...]
    gain_out[0:1, :] = column_sum(back * x * s1)
    r.gx[...] = r.gx[...] + norm_back(x, s1, back * gain(0))


class Segment:
    def __init__(self, result, base, stride, col, blocks, row, rows):
        self.result, self.base, self.stride, self.col, self.blocks = result, base, stride, col, blocks
        self.row, self.rows = row, rows


class Chunk:
    def __init__(self, rows, columns, order, segments):
        self.rows, self.columns, self.order, self.segments = rows, columns, order, segments

    def shape(self, leading):
        return (2,) * leading + (self.rows, self.columns)

    def bytes(self, bits):
        return 2**bits * self.rows * self.columns * 2


def plan(chunks, work, bits, book_bytes):
    core, x, y = bits - 2, bits - 1, bits - 3
    free, pending, done = {}, [], []
    now = 0.0

    def carry(link, took):
        free[link] = max(now, free.get(link, 0.0)) + took
        return free[link]

    def begin(name, stage):
        if name == BOOKS:
            hops = 2 ** (bits - 3)
            if stage == 0:
                there = max(carry(y, hops * book_bytes / 40e3), carry(0, 1.5 * hops * book_bytes / 40e3))
            else:
                there = carry((None, core, x)[stage], (0, 4, 2)[stage] * book_bytes / (1, 400e3, 40e3)[stage])
            pending.append((there + 1.5, name, stage))
            return
        dim = chunks[name].order[stage]
        size = chunks[name].bytes(bits) / 2 ** (stage + 1)
        if dim == core:
            there = carry(core, size / 400e3)
        else:
            there = carry(max(dim, y - 1), size / 40e3)
            if dim < y - 1:
                there += size / 40e3
        pending.append((there + 1.5, name, stage))

    def finish(limit):
        nonlocal now
        acts = []
        while pending:
            pending.sort(key=lambda p: p[0])
            if pending[0][0] > limit:
                break
            at, name, stage = pending.pop(0)
            now = max(now, at) + (2.5 if name == BOOKS and stage < 2 else 0.4)
            acts.append((name, stage))
            if stage + 1 < (3 if name == BOOKS else bits):
                begin(name, stage + 1)
        return acts

    for took, _, names in work:
        now += took
        for name in names:
            begin(name, 0)
        done.append(finish(now))
    done.append(finish(math.inf))
    return done


def coordinates(step, count):
    return [step // 2 ** (count - 1 - i) % 2 for i in range(count)]


def store_segment(packed, first, segment, value):
    for i in range(segment.blocks):
        where = pl.ds(first + segment.base + i, segment.rows, stride=segment.stride)
        packed[where, :] = value[
            segment.row : segment.row + segment.rows, segment.col + i * 128 : segment.col + (i + 1) * 128
        ]


class Halving:
    def __init__(self, chunks, bits, recv, packed, first, send_sem, recv_sem):
        self.chunks = chunks
        self.bits, self.recv, self.packed, self.first = bits, recv, packed, first
        self.send_sem, self.recv_sem = send_sem, recv_sem
        self.copies = {}
        dp, branch = lax.axis_index("dp"), lax.axis_index("branch")
        self.mine, self.partner = [], []
        for dim in range(bits - 1):
            weight = 2 ** (bits - 2 - dim)
            bit = dp // weight % 2
            self.mine.append(bit)
            self.partner.append({"dp": dp + weight * (1 - 2 * bit), "branch": branch})
        self.mine.append(branch)
        self.partner.append({"dp": dp, "branch": 1 - branch})

    def near_level(self, other):
        dp = lax.axis_index("dp")
        for i in range(self.bits - 2):
            if other >> i & 1:
                dp = dp + 2 ** (i + 1) * (1 - 2 * self.mine[self.bits - 3 - i])
        return {"dp": dp, "branch": lax.axis_index("branch")}

    def barrier(self):
        semaphore = pltpu.get_barrier_semaphore()
        levels = 2 ** (self.bits - 2)
        targets = self.partner[self.bits - 2 :] + [self.near_level(other) for other in range(1, levels)]
        for target in targets:
            pl.semaphore_signal(semaphore, inc=1, device_id=target, device_id_type=MESH)
        return lambda: pl.semaphore_wait(semaphore, len(targets))

    def left(self, name, stage):
        return [d for d in range(self.bits) if d not in self.chunks[name].order[:stage]]

    def half(self, ref, name, stage, index):
        position = self.left(name, stage).index(self.chunks[name].order[stage])
        return ref.at[(slice(None),) * position + (index,)]

    def remote(self, source, target, device, *key):
        slot = len(self.copies)
        self.copies[key] = pltpu.make_async_remote_copy(
            src_ref=source,
            dst_ref=target,
            send_sem=self.send_sem.at[slot],
            recv_sem=self.recv_sem.at[slot],
            device_id=device,
            device_id_type=MESH,
        )
        self.copies[key].start()

    def send(self, name, stage, source):
        dim = self.chunks[name].order[stage]
        self.remote(source, self.recv[name][stage], self.partner[dim], name, stage)

    def send_half(self, name, stage, ref):
        dim = self.chunks[name].order[stage]
        self.send(name, stage, self.half(ref, name, stage, 1 - self.mine[dim]))

    def arrived(self, *key):
        self.copies[key].wait_recv()

    def add(self, name, stage, own):
        chunk = self.chunks[name]
        got = self.recv[name][stage]
        depth = self.bits - 1 - stage
        if stage == self.bits - 1:
            value = own[...].astype(F32) + got[...].astype(F32)
            for segment in chunk.segments:
                store_segment(self.packed, self.first[segment.result], segment, value)
            return

        outer = max(depth - 2, 0)

        def step(i, carry):
            where = tuple(coordinates(i, outer))
            got[where] = got[where] + own[where]
            return carry

        lax.fori_loop(0, 2**outer, step, 0)

    def finish(self, name, stage, own=None):
        chunk = self.chunks[name]
        self.arrived(name, stage)
        if own is None:
            dim = chunk.order[stage]
            own = self.half(self.recv[name][stage - 1], name, stage, self.mine[dim])
        self.add(name, stage, own)
        self.follow(name, stage)

    def follow(self, name, stage):
        if stage + 1 < self.bits:
            self.send_half(name, stage + 1, self.recv[name][stage])

    def drain(self):
        for copy in self.copies.values():
            copy.wait_send()


BOOKS = "books"


def quantizer_latent(r):
    branch = lax.axis_index("branch")
    rows, width = r.x.shape
    levels = r.chosen.shape[0]
    latent = r.latent[...]
    sem_code, ac_code = r.chosen[0], r.ac[...]
    gquant = r.gquant[...]
    sem_t, latent_t = sem_code.T, latent.T
    prediction = dot(sem_code, r.distill_v[...])
    target = r.wavlm_v[...].astype(F32)
    pred_norm = lax.rsqrt(jnp.sum(prediction * prediction, axis=1, keepdims=True) + EPS_COS)
    target_norm = lax.rsqrt(jnp.sum(target * target, axis=1, keepdims=True) + EPS_COS)
    cosine = jnp.sum(prediction * target, axis=1, keepdims=True) * (pred_norm * target_norm)
    grad_pred = (
        target * (-DISTILL * pred_norm * target_norm) + prediction * (DISTILL * cosine * pred_norm * pred_norm)
    ).astype(BF16)
    put_distill(r.places.distill, dot(sem_t, grad_pred))
    grad_sem = dot_t(gquant, r.pout_v[0]) + dot_t(grad_pred, r.distill_v[...])
    put_group(r.places.pout, 0, dot(sem_t, gquant))
    put_group(r.places.pout, 1, t_dot(ac_code, gquant))
    commit = 2.0 * BETA * (dot(latent, r.pin_v[0]) - sem_code.astype(F32))
    r.g_rows[0] = (grad_sem - commit).astype(BF16)
    to_sem = (grad_sem + commit).astype(BF16)

    grad_ac = dot_t(gquant, r.pout_v[1])
    residual = dot(latent, r.pin_v[1])
    for level in range(1, levels):
        residual = residual - r.chosen[level].astype(F32)
    carry = jnp.zeros_like(residual)
    for level in range(levels - 1, 0, -1):
        carry = carry + 2.0 * BETA * residual
        r.g_rows[level] = (grad_ac - carry).astype(BF16)
        residual = residual + r.chosen[level].astype(F32)
    to_ac = (grad_ac + carry).astype(BF16)
    put_group(r.places.pin, 0, dot(latent_t, to_sem))
    put_group(r.places.pin, 1, dot(latent_t, to_ac))
    r.gy[...] = dot_t(to_sem, r.pin_v[0]) + dot_t(to_ac, r.pin_v[1])


def put_group(place, group, value):
    target, rows = place.ref, value.shape[0]
    value = value.astype(target.dtype)
    if len(target.shape) == 2:
        target[group * rows : (group + 1) * rows, :] = value
        return
    lead, height = target.shape[1:-2], target.shape[-2]
    value = value.reshape(math.prod(lead), -1, height, value.shape[1])
    value = jnp.concatenate([value[:, i] for i in range(value.shape[1])], axis=2)
    columns = value.shape[2]
    where = (group,) + (slice(None),) * (len(lead) + 1) + (pl.ds(place.col, columns),)
    target[where] = value.reshape(lead + (height, columns))


def put_distill(place, value):
    target = place.ref
    if len(target.shape) == 2:
        target[...] = value.astype(target.dtype)
        return
    height = target.shape[-2]
    value = value.reshape(math.prod(target.shape[:-2]), -1, value.shape[1])
    columns = value.shape[2] * value.shape[1] // height
    value = jnp.concatenate([value[:, :, i : i + columns] for i in range(0, value.shape[2], columns)], axis=1)
    where = (slice(None),) * (len(target.shape) - 1) + (pl.ds(place.col, columns),)
    target[where] = value.astype(target.dtype).reshape(target.shape[:-1] + (columns,))


def one_hot_rows(codes, first, count):
    row = iota((count, codes.shape[1]), 0)
    return jnp.where(codes - first == row, 1.0, 0.0).astype(BF16)


def pick_codes(r):
    levels, _, entries, code_width = r.books.shape
    entries = entries * r.books.shape[1]
    rows = r.cos.shape[0]
    slots = r.ring.shape[0]
    branch = lax.axis_index("branch")
    own = r.codes[:, pl.ds(pl.multiple_of(branch * rows, rows), rows)]
    r.code_rows[...] = jnp.broadcast_to(own[:, None, :], r.code_rows.shape)
    columns = jnp.concatenate([own.astype(F32), jnp.zeros((PAIR - levels, rows), F32)], axis=0).T
    lane = iota(columns.shape, 1)
    entry = iota((rows, entries), 1)
    r.code_cols[...] = columns
    r.ac_sum[...] = jnp.zeros(r.ac_sum.shape, F32)

    def book(level):
        slot = level % slots
        return pltpu.make_async_copy(r.books.at[level], r.ring.at[slot], r.sem_book.at[slot])

    def pick(level, carry):
        code = jnp.sum(jnp.where(lane == level, r.code_cols[...], 0.0), axis=1, keepdims=True)
        one_hot = jnp.where(entry == code.astype(jnp.int32), 1.0, 0.0).astype(BF16)
        book(level).wait()
        got = dot(one_hot, r.ring[level % slots].reshape(entries, code_width))
        r.chosen[level] = got.astype(BF16)
        r.ac_sum[...] += jnp.where(level > 0, got, 0.0)

        @pl.when(level + slots < levels)
        def _():
            book(level + slots).start()

        return carry

    def begin():
        for level in range(slots):
            book(level).start()

    def run():
        lax.fori_loop(0, levels, pick, 0)
        r.ac[...] = r.ac_sum[...].astype(BF16)

    return begin, run


def step_kernel(chunks, first_rows, bits, ins, outs, scratch):
    r = Refs({**ins, **outs, **scratch})
    t = r.t = Refs(r.t)
    r.att, r.g_rows, r.g_got = r.ring.at[0], r.ring.at[1], r.ring.at[2]
    r.ac_sum, r.code_cols = r.acc.at[:, : r.ac.shape[1]], r.gx.at[:, :PAIR]
    branch = lax.axis_index("branch")
    rows, width = r.tokens.shape
    levels, parts, entries, code_width = r.books.shape
    entries = entries * parts
    tiles = r.w_up_v.shape[1] // TILE
    pairs = width // PAIR
    if chunks:
        sums = Halving(chunks, bits, r.recv, r.packed, first_rows, r.send_sem, r.recv_sem)
        mine, level = sums.mine[bits - 2], lax.axis_index("dp") // 2
        wait_barrier = sums.barrier()
    moves = Moves(r.sem_move)
    begin_pick, run_pick = pick_codes(r)
    begin_pick()
    got_pout = [moves.start(r.pout_own.at[0], r.pout_v.at[branch])]
    got_pin = [moves.start(r.pin_own.at[0], r.pin_v.at[branch])]
    got_attention = [moves.start(r.dec_qkv, r.w_qkv_v), moves.start(r.dec_out, r.w_out_v)]
    got_ffn = [moves.start(r.dec_up, r.w_up_v), moves.start(r.dec_down, r.w_down_v)]
    got_attention_two = [moves.start(r.enc_qkv, r.w_qkv_e), moves.start(r.enc_out, r.w_out_e)]
    got_rest = [
        moves.start(r.wavlm.at[pl.ds(pl.multiple_of(branch * rows, rows), rows)], r.wavlm_v),
        moves.start(r.distill, r.distill_v),
    ]
    frame_tables(r)
    if chunks:
        wait_barrier()
        sums.remote(r.pout_own.at[0], r.pout_v.at[branch], sums.partner[bits - 1], POUT)
        sums.remote(r.pin_own.at[0], r.pin_v.at[branch], sums.partner[bits - 1], PIN)
    else:
        got_pout.append(moves.start(r.pout_other.at[0], r.pout_v.at[1 - branch]))
        got_pin.append(moves.start(r.pin_other.at[0], r.pin_v.at[1 - branch]))

    if chunks:
        down = dict(dec=[t.dd0, t.dd1], enc=[t.ed0, t.ed1])
        place = r.places = Refs(
            dec_up=[Place(t.du0), Place(t.du1)],
            dec_out=Place(t.da0),
            dec_qkv=[Place(t.da0, width), Place(t.da1), Place(t.da1, width)],
            enc_up=[Place(t.eu0), Place(t.eu1)],
            enc_out=Place(t.ea0),
            enc_qkv=[Place(t.ea0, width), Place(t.ea1), Place(t.ea2)],
            distill=Place(t.misc),
            pout=Place(t.misc, width),
            pin=Place(t.misc, 2 * width),
        )
    else:
        down = dict(dec=[t.dec_down], enc=[t.enc_down])
        place = r.places = Refs(
            dec_up=[Place(t.dec_up, i * tiles // 2 * TILE) for i in range(2)],
            dec_out=Place(t.dec_out),
            dec_qkv=[Place(t.dec_qkv, i * width) for i in range(3)],
            enc_up=[Place(t.enc_up, i * tiles // 2 * TILE) for i in range(2)],
            enc_out=Place(t.enc_out),
            enc_qkv=[Place(t.enc_qkv, i * width) for i in range(3)],
            distill=Place(t.distill),
            pout=Place(t.pout),
            pin=Place(t.pin),
        )
    dec_down, enc_down = down["dec"], down["enc"]

    def wait(moves, other=None):
        for move in moves:
            move.wait()
        if chunks and other is not None:
            sums.arrived(other)

    def dec_gain(i):
        return r.vectors[1, i : i + 1, :]

    def enc_gain(i):
        return r.vectors[0, i : i + 1, :]

    def pick():
        run_pick()
        wait(got_pout, POUT)
        r.x[...] = dot(r.chosen[0], r.pout_v[0]) + dot(r.ac[...], r.pout_v[1])
        if chunks:
            for other in range(1, levels):
                target = sums.near_level(other)
                sums.remote(r.code_rows.at[target_level(target)], r.code_got.at[other], target, CODES, other)
            r.code_got[0] = r.code_rows[level]

    def target_level(target):
        return next(iter(target.values())) // 2

    def dec_project():
        wait(got_attention)
        attention_project(r, r.w_qkv_v, dec_gain)

    def dec_mix():
        attention_mix(r, r.w_out_v, dec_gain)

    def dec_ffn():
        wait(got_ffn)
        ffn_backward_begin(r, dec_gain, r.cotangent)
        ffn_forward(r, r.w_up_v, r.w_down_v, dec_down)
        r.decoded[...] = (r.x2[...] + dec_gain(3) * r.fo[...]).astype(BF16)

    def dec_ffn_back(half):
        def run():
            first, last = half * tiles // 2, (half + 1) * tiles // 2
            ffn_backward_tiles(r, r.w_up_v, r.w_down_v, place.dec_up[half], None, first, last)
            if half == 1:
                ffn_backward_end(r, dec_gain, r.cotangent, r.dec_gains)
                got_ffn[:] = [moves.start(r.enc_up, r.w_up_v), moves.start(r.enc_down, r.w_down_v)]

        return run

    def dec_out():
        attention_backward_out(r, r.w_out_v, dec_gain, place.dec_out, r.dec_gains)

    def attention_pairs(first, last):
        return lambda: attention_backward_pairs(r, first, last)

    def dec_in(part):
        def run():
            attention_backward_in(r, r.w_qkv_v, place.dec_qkv[part], part)
            if part == 2:
                attention_backward_end(r, dec_gain, r.dec_gains)
                r.gquant[...] = r.gx[...].astype(BF16)

        return run

    def enc_project():
        r.x[...] = r.tokens[...].astype(F32)
        wait(got_attention_two)
        attention_project(r, r.w_qkv_e, enc_gain)

    def enc_mix():
        attention_mix(r, r.w_out_e, enc_gain)

    def enc_ffn():
        wait(got_ffn)
        ffn_forward(r, r.w_up_v, r.w_down_v)
        r.latent[...] = (r.x2[...] + enc_gain(3) * r.fo[...]).astype(BF16)

    def quantizer():
        wait(got_rest)
        wait(got_pin, PIN)
        quantizer_latent(r)
        if chunks:
            for other in range(1, levels):
                target = sums.near_level(other)
                sums.arrived(CODES, other)
                sums.remote(r.g_rows.at[target_level(target)], r.g_got.at[other], target, BOOKS, 0, other)
            r.g_got[0] = r.g_rows[level]

    def book_half(core, put):
        quarter = entries // 4
        for side in range(2):
            r.book_sum[...] = jnp.zeros_like(r.book_sum)
            first = (core * 2 + side) * quarter

            def add(source, carry):
                one_hot = one_hot_rows(r.code_got[source, 0:1, :], first, quarter)
                r.book_sum[...] += dot(one_hot, r.g_got[source])
                return carry

            lax.fori_loop(0, levels, add, 0)
            put(side, r.book_sum[...])

    def finish_books(stage):
        other_core, other_side = sums.partner[bits - 2], sums.partner[bits - 1]
        if stage == 0:
            for other in range(1, levels):
                sums.arrived(BOOKS, 0, other)

            def put(side, value):
                r.book_send[side] = value.astype(BF16)

            book_half(1 - mine, put)
            sums.remote(r.book_send, r.book_got, other_core, BOOKS, 1)
        elif stage == 1:
            sums.arrived(BOOKS, 1)

            def put(side, value):
                r.book_got[side] = (value + r.book_got[side].astype(F32)).astype(BF16)

            book_half(mine, put)
            sums.remote(r.book_got.at[1 - branch], r.book_last, other_side, BOOKS, 2)
        else:
            sums.arrived(BOOKS, 2)
            total = r.book_got[branch].astype(F32) + r.book_last[...].astype(F32)
            blocks = code_width // 128
            store_segment(r.packed, first_rows[BOOKS], Segment(BOOKS, 0, blocks, 0, blocks, 0, entries // 4), total)

    def all_books():
        parts = entries // TILE

        def one(step, carry):
            at = step // parts
            one_hot = one_hot_rows(r.code_rows[at, 0:1, :], step % parts * TILE, TILE)
            t.books[at, aligned(step % parts, TILE), :] = dot(one_hot, r.g_rows[at]).astype(BF16)
            return carry

        lax.fori_loop(0, levels * parts, one, 0)

    def enc_ffn_back(half):
        def run():
            first, last = half * tiles // 2, (half + 1) * tiles // 2
            if half == 0:
                ffn_backward_begin(r, enc_gain, r.gy)
            ffn_backward_tiles(r, r.w_up_v, r.w_down_v, place.enc_up[half], enc_down, first, last)
            if half == 1:
                ffn_backward_end(r, enc_gain, r.gy, r.gains)

        return run

    def enc_out():
        attention_backward_out(r, r.w_out_e, enc_gain, place.enc_out, r.gains)

    def enc_in(part):
        def run():
            attention_backward_in(r, r.w_qkv_e, place.enc_qkv[part], part)
            if part == 2:
                attention_backward_end(r, enc_gain, r.gains)
                r.grad_tokens[...] = r.gx[...]
                if chunks:
                    spread_gains()

        return run

    def spread_gains():
        lanes = pl.ds(width, 128)
        for layer, ref in enumerate((r.gains, r.dec_gains)):
            for row in range(4):
                for block in range(width // 128):
                    owner = (layer * 4 + row) * (width // 128) + block
                    where = tuple(owner // 2 ** (bits - 1 - i) % 2 for i in range(bits))
                    value = ref[row : row + 1, block * 128 : (block + 1) * 128]
                    rows_here = t.ea2.shape[bits]
                    t.ea2[where + (slice(None), lanes)] = jnp.broadcast_to(value, (rows_here, 128)).astype(BF16)

    work = [
        (9.0, pick, ()),
        (2.0, dec_project, ()),
        (3.0, dec_mix, ()),
        (4.0, dec_ffn, (DD0, DD1)),
        (1.5, dec_ffn_back(0), (DU0,)),
        (1.5, dec_ffn_back(1), (DU1,)),
        (1.5, dec_out, ()),
        (2.0, attention_pairs(0, pairs // 2), ()),
        (2.0, attention_pairs(pairs // 2, pairs), ()),
        (0.7, dec_in(0), (DA0,)),
        (0.7, dec_in(1), ()),
        (0.9, dec_in(2), (DA1,)),
        (2.0, enc_project, ()),
        (3.0, enc_mix, ()),
        (3.0, enc_ffn, ()),
        (4.0, quantizer, (BOOKS, MISC)),
        (2.5, enc_ffn_back(0), (EU0,)),
        (2.5, enc_ffn_back(1), (EU1, ED0, ED1)),
        (1.5, enc_out, ()),
        (2.0, attention_pairs(0, pairs // 2), ()),
        (2.0, attention_pairs(pairs // 2, pairs), ()),
        (0.7, enc_in(0), (EA0,)),
        (0.7, enc_in(1), (EA1,)),
        (1.2, enc_in(2), (EA2,)),
    ]
    if not chunks:
        for _, run, _ in work:
            run()
            if run is quantizer:
                all_books()
        return
    actions = plan(chunks, work, bits, rows * code_width * 2)

    def finish(name, stage):
        if name == BOOKS:
            finish_books(stage)
        elif stage == 0:
            sums.finish(name, 0, sums.half(t[name], name, 0, mine))
        else:
            sums.finish(name, stage)

    for (_, run, made), acts in zip(work, actions):
        run()
        for name in made:
            if name != BOOKS:
                sums.send_half(name, 0, t[name])
        for name, stage in acts:
            finish(name, stage)
    for name, stage in actions[-1]:
        finish(name, stage)
    sums.drain()


POUT, PIN, CODES = 1, 2, 3
DD0, DD1, DU0, DU1, DA0, DA1, MISC = "dd0", "dd1", "du0", "du1", "da0", "da1", "misc"
EU0, EU1, ED0, ED1, EA0, EA1, EA2 = "eu0", "eu1", "ed0", "ed1", "ea0", "ea1", "ea2"


def step(given, devices, with_sums):
    rows, width = given.tokens.shape
    ff = given.enc_up.shape[1]
    levels, entries, code_width = given.books.shape
    given.books = given.books.reshape(levels, -1, rows, code_width)
    bits = devices.bit_length() - 1
    vmem, hbm = pl.BlockSpec(memory_space=pltpu.VMEM), pl.BlockSpec(memory_space=pl.ANY)
    scratch = layer_scratch(rows, width, ff)
    scratch.update(
        w_qkv_e=pltpu.VMEM((width, 3 * width), BF16),
        w_out_e=pltpu.VMEM((width, width), BF16),
        cos=pltpu.VMEM((rows, PAIR), F32),
        sin=pltpu.VMEM((rows, PAIR), F32),
        bias=pltpu.VMEM((rows, rows), F32),
        ring=pltpu.VMEM((4,) + given.books.shape[1:], BF16),
        code_rows=pltpu.VMEM((levels, 8, rows), jnp.int32),
        chosen=pltpu.VMEM((levels, rows, code_width), BF16),
        ac=pltpu.VMEM((rows, code_width), BF16),
        gquant=pltpu.VMEM((rows, width), BF16),
        gy=pltpu.VMEM((rows, width), F32),
        latent=pltpu.VMEM((rows, width), BF16),
        pin_v=pltpu.VMEM((2, width, code_width), BF16),
        pout_v=pltpu.VMEM((2, code_width, width), BF16),
        distill_v=pltpu.VMEM(given.distill.shape, BF16),
        wavlm_v=pltpu.VMEM((rows, given.wavlm.shape[1]), BF16),
        sem_move=pltpu.SemaphoreType.DMA((14,)),
        sem_book=pltpu.SemaphoreType.DMA((4,)),
    )
    outs = Refs(decoded=shaped((rows, width), BF16), grad_tokens=shaped((rows, width), F32))
    chunks, first_rows = {}, {}
    params = dict(vmem_limit_bytes=61 * 2**20)
    if with_sums:
        params.update(collective_id=0, has_side_effects=True)
        c, x, y = bits - 2, bits - 1, bits - 3
        b, a = range(y)
        share = width // devices
        low, high = ff // devices, share
        wide, half, blocks = ff // 128, ff // 256, width // 128
        chunks = dict(
            dd0=Chunk(low, width // 2, [c, x, a, b, y], [Segment(3, 0, blocks, 0, blocks // 2, 0, low)]),
            dd1=Chunk(low, width // 2, [c, a, b, x, y], [Segment(3, blocks // 2, blocks, 0, blocks // 2, 0, low)]),
            du0=Chunk(high, ff // 2, [c, x, a, y, b], [Segment(2, 0, wide, 0, half, 0, high)]),
            du1=Chunk(high, ff // 2, [c, y, a, b, x], [Segment(2, half, wide, 0, half, 0, high)]),
            da0=Chunk(
                high,
                2 * width,
                [c, y, x, a, b],
                [
                    Segment(1, 0, blocks, 0, blocks, 0, high),
                    Segment(0, 0, 3 * blocks, width, blocks, 0, high),
                ],
            ),
            da1=Chunk(high, 2 * width, [c, x, y, a, b], [Segment(0, blocks, 3 * blocks, 0, 2 * blocks, 0, high)]),
            misc=Chunk(
                high,
                3 * width,
                [c, x, y, a, b],
                [
                    Segment(8, 0, 2 * blocks, 0, blocks, 0, high // 2),
                    Segment(8, blocks, 2 * blocks, 0, blocks, high // 2, high // 2),
                    Segment(9, 0, blocks, width, blocks, 0, high),
                    Segment(10, 0, blocks // 2, 2 * width, blocks // 2, 0, high),
                    Segment(10, high * blocks // 2, blocks // 2, 2 * width + code_width, blocks // 2, 0, high),
                ],
            ),
            eu0=Chunk(high, ff // 2, [c, x, y, a, b], [Segment(6, 0, wide, 0, half, 0, high)]),
            eu1=Chunk(high, ff // 2, [c, x, a, y, b], [Segment(6, half, wide, 0, half, 0, high)]),
            ed0=Chunk(low, width // 2, [c, y, x, a, b], [Segment(7, 0, blocks, 0, blocks // 2, 0, low)]),
            ed1=Chunk(low, width // 2, [c, x, a, y, b], [Segment(7, blocks // 2, blocks, 0, blocks // 2, 0, low)]),
            ea0=Chunk(
                high,
                2 * width,
                [c, x, y, a, b],
                [
                    Segment(5, 0, blocks, 0, blocks, 0, high),
                    Segment(4, 0, 3 * blocks, width, blocks, 0, high),
                ],
            ),
            ea1=Chunk(high, width, [c, a, y, b, x], [Segment(4, blocks, 3 * blocks, 0, blocks, 0, high)]),
            ea2=Chunk(
                high,
                width + 128,
                [c, y, a, x, b],
                [
                    Segment(4, 2 * blocks, 3 * blocks, 0, blocks, 0, high),
                    Segment(11, 0, 1, width, 1, 0, 8),
                ],
            ),
        )
        rows_of = [high * 3 * blocks, high * blocks, high * wide, low * blocks] * 2
        rows_of += [high * blocks, high * blocks, high * blocks, 8, entries // 4 * code_width // 128]
        first_rows = {i: sum(rows_of[:i]) for i in range(len(rows_of))}
        first_rows[BOOKS] = first_rows[len(rows_of) - 1]
        copies = len(chunks) * bits + 2 * levels + 2
        scratch.update(
            t={name: pltpu.VMEM(c.shape(bits), BF16) for name, c in chunks.items()},
            recv={
                name: [pltpu.VMEM(c.shape(bits - 1 - stage), BF16) for stage in range(bits)]
                for name, c in chunks.items()
            },
            gains=pltpu.VMEM((4, width), F32),
            dec_gains=pltpu.VMEM((4, width), F32),
            code_got=pltpu.VMEM((levels, 8, rows), jnp.int32),
                book_sum=pltpu.VMEM((entries // 4, code_width), F32),
            book_send=pltpu.VMEM((2, entries // 4, code_width), BF16),
            book_got=pltpu.VMEM((2, entries // 4, code_width), BF16),
            book_last=pltpu.VMEM((entries // 4, code_width), BF16),
            send_sem=pltpu.SemaphoreType.DMA((copies,)),
            recv_sem=pltpu.SemaphoreType.DMA((copies,)),
        )
        outs.packed = shaped((sum(rows_of), 128), F32)
    else:
        outs.update(gains=shaped((4, width), F32), dec_gains=shaped((4, width), F32))
        outs.t = dict(
            enc_qkv=shaped(given.enc_qkv.shape, BF16),
            enc_out=shaped(given.enc_out.shape, BF16),
            enc_up=shaped(given.enc_up.shape, BF16),
            enc_down=shaped(given.enc_down.shape, BF16),
            dec_qkv=shaped(given.enc_qkv.shape, BF16),
            dec_out=shaped(given.enc_out.shape, BF16),
            dec_up=shaped(given.enc_up.shape, BF16),
            dec_down=shaped(given.enc_down.shape, BF16),
            pin=shaped((2 * width, code_width), BF16),
            pout=shaped((2 * code_width, width), BF16),
            books=shaped((levels, entries, code_width), BF16),
            distill=shaped(given.distill.shape, BF16),
        )
    in_specs = dict.fromkeys(given, hbm)
    in_specs.update(
        lengths=pl.BlockSpec(memory_space=pltpu.SMEM), codes=vmem, vectors=vmem, tokens=vmem, cotangent=vmem
    )
    got = pl.pallas_call(
        functools.partial(step_kernel, chunks, first_rows, bits),
        out_shape=dict(outs),
        in_specs=[in_specs],
        out_specs=jax.tree.map(lambda _: vmem, dict(outs)),
        scratch_shapes=[dict(scratch)],
        compiler_params=pltpu.CompilerParams(**params),
        name="step",
    )(dict(given))
    got = Refs(got)
    if not with_sums:
        return got
    last = [shaped((rows, 128), F32) for rows in rows_of]
    last[11] = shaped((1, 128), F32)

    def hand_on(packed, decoded, grad, *refs):
        outs, places, semaphores = refs[: len(last) + 2], refs[len(last) + 2 : -1], refs[-1]
        moves = Moves(semaphores)
        arriving = [moves.start(source, place) for source, place in zip((packed, decoded, grad), places)]
        arriving[0].wait()
        leaving = []
        for i, ref in enumerate(outs[:-2]):
            leaving.append(moves.start(places[0].at[pl.ds(first_rows[i], ref.shape[0])], ref))
        for move, place, ref in zip(arriving[1:], places[1:], outs[-2:]):
            move.wait()
            leaving.append(moves.start(place, ref))
        for move in leaving:
            move.wait()

    return pl.pallas_call(
        hand_on,
        out_shape=last + [outs.decoded, outs.grad_tokens],
        in_specs=[hbm] * 3,
        out_specs=[hbm] * (len(last) + 2),
        scratch_shapes=[
            pltpu.VMEM(got.packed.shape, F32),
            pltpu.VMEM(got.decoded.shape, BF16),
            pltpu.VMEM(got.grad_tokens.shape, F32),
            pltpu.SemaphoreType.DMA((len(last) + 5,)),
        ],
        compiler_params=pltpu.CompilerParams(vmem_limit_bytes=61 * 2**20),
        name="results",
    )(got.packed, got.decoded, got.grad_tokens)


def body(
    tokens,
    wavlm,
    cotangent,
    lengths,
    codes,
    enc_qkv,
    enc_out,
    enc_up,
    enc_down,
    dec_qkv,
    dec_out,
    dec_up,
    dec_down,
    vectors,
    proj_in,
    proj_out,
    codebooks,
    distill_proj,
):
    width = tokens.shape[1]
    devices = lax.axis_size("dp") * lax.axis_size("branch")
    with_sums = devices == 4 * codebooks.shape[0] and width // devices % 16 == 0
    given = Refs(
        tokens=tokens,
        wavlm=wavlm,
        cotangent=cotangent,
        lengths=lengths,
        codes=codes.T,
        enc_qkv=enc_qkv,
        enc_out=enc_out,
        enc_up=enc_up,
        enc_down=enc_down,
        dec_qkv=dec_qkv,
        dec_out=dec_out,
        dec_up=dec_up,
        dec_down=dec_down,
        vectors=vectors,
        pin_own=proj_in,
        pout_own=proj_out,
        books=codebooks,
        distill=distill_proj,
    )
    if with_sums:
        *sums, decoded, grad_tokens = step(given, devices, True)
        sums = [part.reshape(-1) for part in sums]
        order = (4, 5, 6, 7, 0, 1, 2, 3, 11, 10, 9, 12, 8)
        return (decoded, grad_tokens, *[sums[i] for i in order])
    swap = [(0, 1), (1, 0)]
    given.pin_other = lax.ppermute(proj_in, "branch", swap)
    given.pout_other = lax.ppermute(proj_out, "branch", swap)
    s = step(given, devices, False)
    t = Refs(s.t)
    gains = jnp.concatenate([s.gains, s.dec_gains])
    local = [t.enc_qkv, t.enc_out, t.enc_up, t.enc_down, t.dec_qkv, t.dec_out, t.dec_up, t.dec_down]
    local += [gains, t.pin, t.pout, t.books, t.distill]
    sums = [
        lax.psum_scatter(part.astype(F32).reshape(-1), ("dp", "branch"), scatter_dimension=0, tiled=True)
        for part in local
    ]
    return (s.decoded, s.grad_tokens, *sums)


def solution(mesh):
    rows, whole = P(("dp", "branch"), None), P()
    placed = (rows, P("dp", None), rows, rows, P("dp", None)) + (whole,) * 9
    placed += (P("branch", None, None),) * 2 + (whole,) * 2
    return jax.shard_map(
        body,
        mesh=mesh,
        in_specs=placed,
        out_specs=(rows, rows) + (P(("dp", "branch")),) * 13,
        check_vma=False,
    )
```

```python
import functools
import math

import jax
import jax.numpy as jnp
from jax import lax
from jax.experimental import pallas as pl
from jax.experimental.pallas import tpu as pltpu
from jax.sharding import PartitionSpec as P

HEADS = 8
WINDOW = 250
EPS_NORM = 1e-05
EPS_COS = 1e-06
BETA = 0.25
DISTILL = 10.0
ROPE_BASE = 10000.0

MESH = pl.DeviceIdType.MESH
F32 = jnp.float32
BF16 = jnp.bfloat16
TILE = 512
PAIR = 128


def dot(left, right):
    return lax.dot_general(left, right, (((1,), (0,)), ((), ())), preferred_element_type=F32)


def dot_t(left, right):
    return lax.dot_general(left, right, (((1,), (1,)), ((), ())), preferred_element_type=F32)


def t_dot(left, right):
    return lax.dot_general(left, right, (((0,), (0,)), ((), ())), preferred_element_type=F32)


def iota(shape, dim):
    return lax.broadcasted_iota(jnp.int32, shape, dim)


def aligned(index, size):
    return pl.ds(pl.multiple_of(index * size, size), size)


class Refs(dict):
    __getattr__ = dict.__getitem__
    __setattr__ = dict.__setitem__


class Moves:
    def __init__(self, semaphores):
        self.semaphores, self.count = semaphores, 0

    def start(self, source, target):
        move = pltpu.make_async_copy(source, target, self.semaphores.at[self.count])
        self.count += 1
        move.start()
        return move


def layer_scratch(rows, width, ff):
    return Refs(
        x=pltpu.VMEM((rows, width), F32),
        s1=pltpu.VMEM((rows, 1), F32),
        h=pltpu.VMEM((rows, width), BF16),
        h1t=pltpu.VMEM((width, rows), BF16),
        h2t=pltpu.VMEM((width, rows), BF16),
        rinv=pltpu.VMEM((rows, width), F32),
        qkv=pltpu.VMEM((rows, 3 * width), BF16),
        mix=pltpu.VMEM((rows, width), BF16),
        ao=pltpu.VMEM((rows, width), F32),
        x2=pltpu.VMEM((rows, width), F32),
        s2=pltpu.VMEM((rows, 1), F32),
        act=pltpu.VMEM((rows, ff), BF16),
        dg=pltpu.VMEM((rows, ff), BF16),
        fo=pltpu.VMEM((rows, width), F32),
        grad=pltpu.VMEM((rows, width), BF16),
        gx=pltpu.VMEM((rows, width), F32),
        acc=pltpu.VMEM((rows, width), F32),
        w_qkv_v=pltpu.VMEM((width, 3 * width), BF16),
        w_out_v=pltpu.VMEM((width, width), BF16),
        w_up_v=pltpu.VMEM((width, ff), BF16),
        w_down_v=pltpu.VMEM((ff, width), BF16),
    )


def shaped(shape, kind):
    return jax.ShapeDtypeStruct(shape, kind)


def frame_tables(r):
    rows = r.cos.shape[0]
    place = iota((rows, PAIR), 0)
    query, key = iota((rows, rows), 0), iota((rows, rows), 1)
    begin, begin_query = jnp.zeros_like(place), jnp.zeros_like(query)
    edge = 0
    for clip in range(r.lengths.shape[1] - 1):
        edge = edge + r.lengths[0, clip]
        begin = jnp.where(place >= edge, edge, begin)
        begin_query = jnp.where(query >= edge, edge, begin_query)
    allowed = (key >= begin_query) & (key <= query) & (query - key < WINDOW)
    r.bias[...] = jnp.where(allowed, 0.0, -1e30)
    lane = iota((rows, PAIR), 1)
    rate = jnp.exp((lane % 32).astype(F32) * (-math.log(ROPE_BASE) / 32))
    angle = (place - begin).astype(F32) * rate
    r.cos[...] = jnp.cos(angle)
    sine = jnp.sin(angle)
    r.sin[...] = jnp.where(lane % 64 < 32, -sine, sine)


def rotated(value, cosine, sine):
    lane = iota(value.shape, 1)
    swapped = jnp.where(lane % 64 < 32, pltpu.roll(value, PAIR - 32, 1), pltpu.roll(value, 32, 1))
    return value * cosine + swapped * sine


def head_masks(rows):
    low = iota((rows, PAIR), 1) < 64
    return (jnp.where(low, 1.0, 0.0).astype(BF16), jnp.where(low, 0.0, 1.0).astype(BF16))


def attention_project(r, w_qkv, gain):
    width = r.x.shape[1]
    x = r.x[...]
    s1 = lax.rsqrt(jnp.mean(x * x, axis=1, keepdims=True) + EPS_NORM)
    r.s1[...] = s1
    h = (x * s1 * gain(0)).astype(BF16)
    r.h[...] = h
    r.h1t[...] = h.T

    def project(part, carry):
        value = dot(r.h[...], w_qkv[:, aligned(part, width)])
        turn = jnp.where(part < 2, 1.0, 0.0)
        scale = jnp.where(part == 0, 0.125, 1.0)
        cosine = r.cos[...] * turn + (1.0 - turn)
        sine = r.sin[...] * turn
        for p in range(width // PAIR):
            low = rotated(value[:, p * PAIR : (p + 1) * PAIR], cosine, sine).astype(BF16)
            where = pl.ds(pl.multiple_of(part * width + p * PAIR, PAIR), PAIR)
            r.qkv[:, where] = (low.astype(F32) * scale).astype(BF16)
        return carry

    lax.fori_loop(0, 3, project, 0, unroll=True)


def attention_mix(r, w_out, gain):
    rows, width = r.x.shape
    masks = head_masks(rows)
    low = iota((rows, PAIR), 1) < 64

    def pair(p, carry):
        query = r.qkv[:, aligned(p, PAIR)]
        key = r.qkv[:, aligned(p + width // PAIR, PAIR)]
        value = r.qkv[:, aligned(p + 2 * (width // PAIR), PAIR)]
        outs = []
        for h in range(2):
            scores = dot_t(query * masks[h], key) + r.bias[...]
            weights = jnp.exp(scores - jnp.max(scores, axis=1, keepdims=True)).astype(BF16)
            r.att[2 * p + h] = weights
            outs.append(dot(weights, value * masks[h] + masks[1 - h]))
        inverse = 1.0 / pltpu.roll(jnp.where(low, outs[1], outs[0]), 64, 1)
        r.rinv[:, aligned(p, PAIR)] = inverse
        r.mix[:, aligned(p, PAIR)] = (jnp.where(low, outs[0], outs[1]) * inverse).astype(BF16)
        return carry

    lax.fori_loop(0, width // PAIR, pair, 0, unroll=True)
    ao = dot(r.mix[...], w_out[...])
    r.ao[...] = ao
    x2 = r.x[...] + gain(1) * ao
    r.x2[...] = x2
    s2 = lax.rsqrt(jnp.mean(x2 * x2, axis=1, keepdims=True) + EPS_NORM)
    r.s2[...] = s2
    h = (x2 * s2 * gain(2)).astype(BF16)
    r.h[...] = h
    r.h2t[...] = h.T


def ffn_forward(r, w_up, w_down, grad_down=None):
    r.fo[...] = jnp.zeros_like(r.fo)
    slope = math.sqrt(2.0 / math.pi)

    def tile(t, carry):
        cols = aligned(t, TILE)
        pre = dot(r.h[...], w_up[:, cols])
        square = pre * pre
        bent = jnp.tanh(slope * pre * (1.0 + 0.044715 * square))
        half = 0.5 * (1.0 + bent)
        act = (pre * half).astype(BF16)
        r.act[:, cols] = act
        turn = 0.5 * pre * (1.0 - bent * bent) * slope * (1.0 + 3.0 * 0.044715 * square)
        r.dg[:, cols] = (half + turn).astype(BF16)
        r.fo[...] += dot(act, w_down[cols, :])
        if grad_down is not None:
            put_rows(grad_down, t_dot(act, r.grad[...]), t)
        return carry

    lax.fori_loop(0, w_up.shape[1] // TILE, tile, 0, unroll=True)


def norm_back(stream, inverse, grad):
    mean = jnp.mean(grad * stream, axis=1, keepdims=True)
    return inverse * grad - stream * (inverse * inverse * inverse * mean)


def column_sum(value):
    return jnp.sum(value, axis=0, keepdims=True)


class Place:
    def __init__(self, ref, col=0):
        self.ref, self.col = ref, col

    def shift(self, by):
        return Place(self.ref, self.col + by)

    def put(self, value):
        shape = self.ref.shape
        value = value.astype(self.ref.dtype).reshape(shape[:-1] + (value.shape[1],))
        self.ref[(slice(None),) * (len(shape) - 1) + (pl.ds(self.col, value.shape[-1]),)] = value


def put_rows(targets, value, tile):
    value = value.astype(BF16)
    columns = value.shape[1] // len(targets)
    for i, target in enumerate(targets):
        shape = target.shape
        part = value[:, i * columns : (i + 1) * columns]
        if len(shape) == 2:
            target[aligned(tile, value.shape[0]), :] = part
        else:
            target[tile // 2, tile % 2] = part.reshape(shape[2:])


def ffn_backward_begin(r, gain, gy_ref):
    r.grad[...] = (gain(3) * gy_ref[...].astype(F32)).astype(BF16)


def ffn_backward_tiles(r, w_up, w_down, grad_up, grad_down, first, last):
    if first == 0:
        r.acc[...] = jnp.zeros_like(r.acc)

    def tile(t, carry):
        cols = aligned(t, TILE)
        if grad_down is not None:
            put_rows(grad_down, t_dot(r.act[:, cols], r.grad[...]), t)
        grad_pre = (dot_t(r.grad[...], w_down[cols, :]) * r.dg[:, cols].astype(F32)).astype(BF16)
        grad_up.shift(pl.multiple_of((t - first) * TILE, TILE)).put(dot(r.h2t[...], grad_pre))
        r.acc[...] += dot_t(grad_pre, w_up[:, cols])
        return carry

    lax.fori_loop(first, last, tile, 0, unroll=True)


def ffn_backward_end(r, gain, gy_ref, gain_out):
    gy = gy_ref[...].astype(F32)
    gain_out[3:4, :] = column_sum(gy * r.fo[...])
    back = r.acc[...]
    x2, s2 = r.x2[...], r.s2[...]
    gain_out[2:3, :] = column_sum(back * x2 * s2)
    r.gx[...] = gy + norm_back(x2, s2, back * gain(2))


def attention_backward_out(r, w_out, gain, grad_out, gain_out):
    gx = r.gx[...]
    gain_out[1:2, :] = column_sum(gx * r.ao[...])
    grad_attn = (gain(1) * gx).astype(BF16)
    grad_out.put(t_dot(r.mix[...], grad_attn))
    r.grad[...] = dot_t(grad_attn, w_out[...]).astype(BF16)


def attention_backward_pairs(r, first, last):
    rows, width = r.x.shape
    masks = head_masks(rows)
    masks_t = [jnp.where((iota((PAIR, rows), 0) < 64) == (h == 0), 1.0, 0.0).astype(BF16) for h in range(2)]
    pairs = width // PAIR

    def pair(p, carry):
        query = r.qkv[:, aligned(p, PAIR)]
        key = r.qkv[:, aligned(p + pairs, PAIR)]
        value = r.qkv[:, aligned(p + 2 * pairs, PAIR)]
        grad_mixed = (r.grad[:, aligned(p, PAIR)].astype(F32) * r.rinv[:, aligned(p, PAIR)]).astype(BF16)
        product = (grad_mixed.astype(F32) * r.mix[:, aligned(p, PAIR)].astype(F32)).astype(BF16)
        beside = jnp.concatenate([value, jnp.full(value.shape, -1.0, BF16)], axis=1)
        query_t, grad_t = query.T, grad_mixed.T
        to_query = to_key = to_value = 0.0
        for h in range(2):
            weights = r.att[2 * p + h]
            change = dot_t(jnp.concatenate([grad_mixed * masks[h], product * masks[h]], axis=1), beside)
            scores = (weights.astype(F32) * change).astype(BF16)
            to_query = to_query + dot(scores, key * masks[h])
            to_key = to_key + dot(query_t * masks_t[h], scores)
            to_value = to_value + dot(grad_t * masks_t[h], weights)
        cosine, sine = r.cos[...], -r.sin[...]
        r.qkv[:, aligned(p, PAIR)] = rotated(to_query * 0.125, cosine, sine).astype(BF16)
        r.qkv[:, aligned(p + pairs, PAIR)] = rotated(to_key.T, cosine, sine).astype(BF16)
        r.qkv[:, aligned(p + 2 * pairs, PAIR)] = to_value.T.astype(BF16)
        return carry

    lax.fori_loop(first, last, pair, 0, unroll=True)


def attention_backward_in(r, w_qkv, grad_qkv, part):
    width = r.x.shape[1]
    grad = r.qkv[:, part * width : (part + 1) * width]
    grad_qkv.put(dot(r.h1t[...], grad))
    back = dot_t(grad, w_qkv[:, part * width : (part + 1) * width])
    r.acc[...] = back if part == 0 else r.acc[...] + back


def attention_backward_end(r, gain, gain_out):
    back = r.acc[...]
    x, s1 = r.x[...], r.s1[...]
    gain_out[0:1, :] = column_sum(back * x * s1)
    r.gx[...] = r.gx[...] + norm_back(x, s1, back * gain(0))


class Segment:
    def __init__(self, result, base, stride, col, blocks, row, rows):
        self.result, self.base, self.stride, self.col, self.blocks = result, base, stride, col, blocks
        self.row, self.rows = row, rows


class Chunk:
    def __init__(self, rows, columns, order, segments):
        self.rows, self.columns, self.order, self.segments = rows, columns, order, segments

    def shape(self, leading):
        return (2,) * leading + (self.rows, self.columns)

    def bytes(self, bits):
        return 2**bits * self.rows * self.columns * 2


def plan(chunks, work, bits, book_bytes):
    core, x, y = bits - 2, bits - 1, bits - 3
    free, pending, done = {}, [], []
    now = 0.0

    def carry(link, took):
        free[link] = max(now, free.get(link, 0.0)) + took
        return free[link]

    def begin(name, stage):
        if name == BOOKS:
            hops = 2 ** (bits - 3)
            if stage == 0:
                there = max(carry(y, hops * book_bytes / 40e3), carry(0, 1.5 * hops * book_bytes / 40e3))
            else:
                there = carry((None, core, x)[stage], (0, 4, 2)[stage] * book_bytes / (1, 400e3, 40e3)[stage])
            pending.append((there + 1.5, name, stage))
            return
        dim = chunks[name].order[stage]
        size = chunks[name].bytes(bits) / 2 ** (stage + 1)
        if dim == core:
            there = carry(core, size / 400e3)
        else:
            there = carry(max(dim, y - 1), size / 40e3)
            if dim < y - 1:
                there += size / 40e3
        pending.append((there + 1.5, name, stage))

    def finish(limit):
        nonlocal now
        acts = []
        while pending:
            pending.sort(key=lambda p: p[0])
            if pending[0][0] > limit:
                break
            at, name, stage = pending.pop(0)
            now = max(now, at) + (6.0 if name == BOOKS and stage == 0 else 0.5)
            acts.append((name, stage))
            if stage + 1 < (3 if name == BOOKS else bits):
                begin(name, stage + 1)
        return acts

    for took, _, names in work:
        now += took
        for name in names:
            begin(name, 0)
        done.append(finish(now))
    done.append(finish(math.inf))
    return done


def coordinates(step, count):
    return [step // 2 ** (count - 1 - i) % 2 for i in range(count)]


def store_segment(packed, first, segment, value):
    for i in range(segment.blocks):
        where = pl.ds(first + segment.base + i, segment.rows, stride=segment.stride)
        packed[where, :] = value[
            segment.row : segment.row + segment.rows, segment.col + i * 128 : segment.col + (i + 1) * 128
        ]


class Halving:
    def __init__(self, chunks, bits, recv, packed, first, send_sem, recv_sem):
        self.chunks = chunks
        self.bits, self.recv, self.packed, self.first = bits, recv, packed, first
        self.send_sem, self.recv_sem = send_sem, recv_sem
        self.copies = {}
        dp, branch = lax.axis_index("dp"), lax.axis_index("branch")
        self.mine, self.partner = [], []
        for dim in range(bits - 1):
            weight = 2 ** (bits - 2 - dim)
            bit = dp // weight % 2
            self.mine.append(bit)
            self.partner.append({"dp": dp + weight * (1 - 2 * bit), "branch": branch})
        self.mine.append(branch)
        self.partner.append({"dp": dp, "branch": 1 - branch})

    def near_level(self, other):
        dp = lax.axis_index("dp")
        for i in range(self.bits - 2):
            if other >> i & 1:
                dp = dp + 2 ** (i + 1) * (1 - 2 * self.mine[self.bits - 3 - i])
        return {"dp": dp, "branch": lax.axis_index("branch")}

    def barrier(self):
        semaphore = pltpu.get_barrier_semaphore()
        levels = 2 ** (self.bits - 2)
        targets = self.partner[self.bits - 2 :] + [self.near_level(other) for other in range(1, levels)]
        for target in targets:
            pl.semaphore_signal(semaphore, inc=1, device_id=target, device_id_type=MESH)
        return lambda: pl.semaphore_wait(semaphore, len(targets))

    def left(self, name, stage):
        return [d for d in range(self.bits) if d not in self.chunks[name].order[:stage]]

    def half(self, ref, name, stage, index):
        position = self.left(name, stage).index(self.chunks[name].order[stage])
        return ref.at[(slice(None),) * position + (index,)]

    def remote(self, source, target, device, *key):
        slot = len(self.copies)
        self.copies[key] = pltpu.make_async_remote_copy(
            src_ref=source,
            dst_ref=target,
            send_sem=self.send_sem.at[slot],
            recv_sem=self.recv_sem.at[slot],
            device_id=device,
            device_id_type=MESH,
        )
        self.copies[key].start()

    def send(self, name, stage, source):
        dim = self.chunks[name].order[stage]
        self.remote(source, self.recv[name][stage], self.partner[dim], name, stage)

    def send_half(self, name, stage, ref):
        dim = self.chunks[name].order[stage]
        self.send(name, stage, self.half(ref, name, stage, 1 - self.mine[dim]))

    def arrived(self, *key):
        self.copies[key].wait_recv()

    def add(self, name, stage, own):
        chunk = self.chunks[name]
        got = self.recv[name][stage]
        depth = self.bits - 1 - stage
        if stage == self.bits - 1:
            value = own[...].astype(F32) + got[...].astype(F32)
            for segment in chunk.segments:
                store_segment(self.packed, self.first[segment.result], segment, value)
            return

        outer = max(depth - 2, 0)

        def step(i, carry):
            where = tuple(coordinates(i, outer))
            got[where] = got[where] + own[where]
            return carry

        lax.fori_loop(0, 2**outer, step, 0)

    def finish(self, name, stage, own=None):
        chunk = self.chunks[name]
        self.arrived(name, stage)
        if own is None:
            dim = chunk.order[stage]
            own = self.half(self.recv[name][stage - 1], name, stage, self.mine[dim])
        self.add(name, stage, own)
        self.follow(name, stage)

    def follow(self, name, stage):
        if stage + 1 < self.bits:
            self.send_half(name, stage + 1, self.recv[name][stage])

    def drain(self):
        for copy in self.copies.values():
            copy.wait_send()


BOOKS = "books"


def quantizer_latent(r):
    branch = lax.axis_index("branch")
    rows, width = r.x.shape
    levels = r.chosen.shape[0]
    latent = r.latent[...]
    sem_code, ac_code = r.chosen[0], r.ac[...]
    gquant = r.gquant[...]
    sem_t, latent_t = sem_code.T, latent.T
    prediction = dot(sem_code, r.distill_v[...])
    target = r.wavlm_v[...].astype(F32)
    pred_norm = lax.rsqrt(jnp.sum(prediction * prediction, axis=1, keepdims=True) + EPS_COS)
    target_norm = lax.rsqrt(jnp.sum(target * target, axis=1, keepdims=True) + EPS_COS)
    cosine = jnp.sum(prediction * target, axis=1, keepdims=True) * (pred_norm * target_norm)
    grad_pred = (
        target * (-DISTILL * pred_norm * target_norm) + prediction * (DISTILL * cosine * pred_norm * pred_norm)
    ).astype(BF16)
    put_distill(r.places.distill, dot(sem_t, grad_pred))
    grad_sem = dot_t(gquant, r.pout_v[0]) + dot_t(grad_pred, r.distill_v[...])
    put_group(r.places.pout, 0, dot(sem_t, gquant))
    put_group(r.places.pout, 1, t_dot(ac_code, gquant))
    commit = 2.0 * BETA * (dot(latent, r.pin_v[0]) - sem_code.astype(F32))
    r.g_rows[0] = (grad_sem - commit).astype(BF16)
    to_sem = (grad_sem + commit).astype(BF16)

    grad_ac = dot_t(gquant, r.pout_v[1])
    residual = dot(latent, r.pin_v[1])
    for level in range(1, levels):
        residual = residual - r.chosen[level].astype(F32)
    carry = jnp.zeros_like(residual)
    for level in range(levels - 1, 0, -1):
        carry = carry + 2.0 * BETA * residual
        r.g_rows[level] = (grad_ac - carry).astype(BF16)
        residual = residual + r.chosen[level].astype(F32)
    to_ac = (grad_ac + carry).astype(BF16)
    put_group(r.places.pin, 0, dot(latent_t, to_sem))
    put_group(r.places.pin, 1, dot(latent_t, to_ac))
    r.gy[...] = dot_t(to_sem, r.pin_v[0]) + dot_t(to_ac, r.pin_v[1])


def put_group(place, group, value):
    target, rows = place.ref, value.shape[0]
    value = value.astype(target.dtype)
    if len(target.shape) == 2:
        target[group * rows : (group + 1) * rows, :] = value
        return
    lead, height = target.shape[1:-2], target.shape[-2]
    value = value.reshape(math.prod(lead), -1, height, value.shape[1])
    value = jnp.concatenate([value[:, i] for i in range(value.shape[1])], axis=2)
    columns = value.shape[2]
    where = (group,) + (slice(None),) * (len(lead) + 1) + (pl.ds(place.col, columns),)
    target[where] = value.reshape(lead + (height, columns))


def put_distill(place, value):
    target = place.ref
    if len(target.shape) == 2:
        target[...] = value.astype(target.dtype)
        return
    height = target.shape[-2]
    value = value.reshape(math.prod(target.shape[:-2]), -1, value.shape[1])
    columns = value.shape[2] * value.shape[1] // height
    value = jnp.concatenate([value[:, :, i : i + columns] for i in range(0, value.shape[2], columns)], axis=1)
    where = (slice(None),) * (len(target.shape) - 1) + (pl.ds(place.col, columns),)
    target[where] = value.astype(target.dtype).reshape(target.shape[:-1] + (columns,))


def one_hot_rows(codes, first, count):
    row = iota((count, codes.shape[1]), 0)
    return jnp.where(codes - first == row, 1.0, 0.0).astype(BF16)


def pick_codes(r):
    levels, _, entries, code_width = r.books.shape
    entries = entries * r.books.shape[1]
    rows = r.cos.shape[0]
    slots = r.ring.shape[0]
    branch = lax.axis_index("branch")
    own = r.codes[:, pl.ds(pl.multiple_of(branch * rows, rows), rows)]
    r.code_rows[...] = jnp.broadcast_to(own[:, None, :], r.code_rows.shape)
    columns = jnp.concatenate([own.astype(F32), jnp.zeros((PAIR - levels, rows), F32)], axis=0).T
    lane = iota(columns.shape, 1)
    entry = iota((rows, entries), 1)
    r.code_cols[...] = columns
    r.ac_sum[...] = jnp.zeros(r.ac_sum.shape, F32)

    def book(level):
        slot = level % slots
        return pltpu.make_async_copy(r.books.at[level], r.ring.at[slot], r.sem_book.at[slot])

    def pick(level, carry):
        code = jnp.sum(jnp.where(lane == level, r.code_cols[...], 0.0), axis=1, keepdims=True)
        one_hot = jnp.where(entry == code.astype(jnp.int32), 1.0, 0.0).astype(BF16)
        book(level).wait()
        got = dot(one_hot, r.ring[level % slots].reshape(entries, code_width))
        r.chosen[level] = got.astype(BF16)
        r.ac_sum[...] += jnp.where(level > 0, got, 0.0)

        @pl.when(level + slots < levels)
        def _():
            book(level + slots).start()

        return carry

    def begin():
        for level in range(slots):
            book(level).start()

    def run():
        lax.fori_loop(0, levels, pick, 0)
        r.ac[...] = r.ac_sum[...].astype(BF16)

    return begin, run


def step_kernel(chunks, first_rows, bits, ins, outs, scratch):
    r = Refs({**ins, **outs, **scratch})
    t = r.t = Refs(r.t)
    r.att, r.g_rows, r.g_got, r.book_own = (r.ring.at[i] for i in range(4))
    r.ac_sum, r.code_cols = r.acc.at[:, : r.ac.shape[1]], r.gx.at[:, :PAIR]
    branch = lax.axis_index("branch")
    rows, width = r.tokens.shape
    levels, parts, entries, code_width = r.books.shape
    entries = entries * parts
    tiles = r.w_up_v.shape[1] // TILE
    pairs = width // PAIR
    if chunks:
        sums = Halving(chunks, bits, r.recv, r.packed, first_rows, r.send_sem, r.recv_sem)
        mine, level = sums.mine[bits - 2], lax.axis_index("dp") // 2
        wait_barrier = sums.barrier()
    moves = Moves(r.sem_move)
    begin_pick, run_pick = pick_codes(r)
    begin_pick()
    got_pout = [moves.start(r.pout_own.at[0], r.pout_v.at[branch])]
    got_pin = [moves.start(r.pin_own.at[0], r.pin_v.at[branch])]
    got_attention = [moves.start(r.dec_qkv, r.w_qkv_v), moves.start(r.dec_out, r.w_out_v)]
    got_ffn = [moves.start(r.dec_up, r.w_up_v), moves.start(r.dec_down, r.w_down_v)]
    got_attention_two = [moves.start(r.enc_qkv, r.w_qkv_e), moves.start(r.enc_out, r.w_out_e)]
    got_rest = [
        moves.start(r.wavlm.at[pl.ds(pl.multiple_of(branch * rows, rows), rows)], r.wavlm_v),
        moves.start(r.distill, r.distill_v),
    ]
    frame_tables(r)
    if chunks:
        wait_barrier()
        sums.remote(r.pout_own.at[0], r.pout_v.at[branch], sums.partner[bits - 1], POUT)
        sums.remote(r.pin_own.at[0], r.pin_v.at[branch], sums.partner[bits - 1], PIN)
    else:
        got_pout.append(moves.start(r.pout_other.at[0], r.pout_v.at[1 - branch]))
        got_pin.append(moves.start(r.pin_other.at[0], r.pin_v.at[1 - branch]))

    if chunks:
        down = dict(dec=[t.dd0, t.dd1], enc=[t.ed0, t.ed1])
        place = r.places = Refs(
            dec_up=[Place(t.du0), Place(t.du1)],
            dec_out=Place(t.da0),
            dec_qkv=[Place(t.da0, width), Place(t.da1), Place(t.da1, width)],
            enc_up=[Place(t.eu0), Place(t.eu1)],
            enc_out=Place(t.ea0),
            enc_qkv=[Place(t.ea0, width), Place(t.ea1), Place(t.ea2)],
            distill=Place(t.misc),
            pout=Place(t.misc, width),
            pin=Place(t.misc, 2 * width),
        )
    else:
        down = dict(dec=[t.dec_down], enc=[t.enc_down])
        place = r.places = Refs(
            dec_up=[Place(t.dec_up, i * tiles // 2 * TILE) for i in range(2)],
            dec_out=Place(t.dec_out),
            dec_qkv=[Place(t.dec_qkv, i * width) for i in range(3)],
            enc_up=[Place(t.enc_up, i * tiles // 2 * TILE) for i in range(2)],
            enc_out=Place(t.enc_out),
            enc_qkv=[Place(t.enc_qkv, i * width) for i in range(3)],
            distill=Place(t.distill),
            pout=Place(t.pout),
            pin=Place(t.pin),
        )
    dec_down, enc_down = down["dec"], down["enc"]

    def wait(moves, other=None):
        for move in moves:
            move.wait()
        if chunks and other is not None:
            sums.arrived(other)

    def dec_gain(i):
        return r.vectors[1, i : i + 1, :]

    def enc_gain(i):
        return r.vectors[0, i : i + 1, :]

    def pick():
        run_pick()
        wait(got_pout, POUT)
        r.x[...] = dot(r.chosen[0], r.pout_v[0]) + dot(r.ac[...], r.pout_v[1])
        if chunks:
            for other in range(1, levels):
                target = sums.near_level(other)
                sums.remote(r.code_rows.at[target_level(target)], r.code_got.at[other], target, CODES, other)
            r.code_got[0] = r.code_rows[level]

    def target_level(target):
        return next(iter(target.values())) // 2

    def dec_project():
        wait(got_attention)
        attention_project(r, r.w_qkv_v, dec_gain)

    def dec_mix():
        attention_mix(r, r.w_out_v, dec_gain)

    def dec_ffn():
        wait(got_ffn)
        ffn_backward_begin(r, dec_gain, r.cotangent)
        ffn_forward(r, r.w_up_v, r.w_down_v, dec_down)
        r.decoded[...] = (r.x2[...] + dec_gain(3) * r.fo[...]).astype(BF16)

    def dec_ffn_back(half):
        def run():
            first, last = half * tiles // 2, (half + 1) * tiles // 2
            ffn_backward_tiles(r, r.w_up_v, r.w_down_v, place.dec_up[half], None, first, last)
            if half == 1:
                ffn_backward_end(r, dec_gain, r.cotangent, r.dec_gains)
                got_ffn[:] = [moves.start(r.enc_up, r.w_up_v), moves.start(r.enc_down, r.w_down_v)]

        return run

    def dec_out():
        attention_backward_out(r, r.w_out_v, dec_gain, place.dec_out, r.dec_gains)

    def attention_pairs(first, last):
        return lambda: attention_backward_pairs(r, first, last)

    def dec_in(part):
        def run():
            attention_backward_in(r, r.w_qkv_v, place.dec_qkv[part], part)
            if part == 2:
                attention_backward_end(r, dec_gain, r.dec_gains)
                r.gquant[...] = r.gx[...].astype(BF16)

        return run

    def enc_project():
        r.x[...] = r.tokens[...].astype(F32)
        wait(got_attention_two)
        attention_project(r, r.w_qkv_e, enc_gain)

    def enc_mix():
        attention_mix(r, r.w_out_e, enc_gain)

    def enc_ffn():
        wait(got_ffn)
        ffn_forward(r, r.w_up_v, r.w_down_v)
        r.latent[...] = (r.x2[...] + enc_gain(3) * r.fo[...]).astype(BF16)

    def quantizer():
        wait(got_rest)
        wait(got_pin, PIN)
        quantizer_latent(r)
        if chunks:
            for other in reversed(range(1, levels)):
                target = sums.near_level(other)
                sums.arrived(CODES, other)
                sums.remote(r.g_rows.at[target_level(target)], r.g_got.at[other], target, BOOKS, 0, other)
            r.g_got[0] = r.g_rows[level]

    def book_half(core, put):
        quarter = entries // 4
        for side in range(2):
            r.book_sum[...] = jnp.zeros_like(r.book_sum)
            first = (core * 2 + side) * quarter

            def add(source, carry):
                one_hot = one_hot_rows(r.code_got[source, 0:1, :], first, quarter)
                r.book_sum[...] += dot(one_hot, r.g_got[source])
                return carry

            lax.fori_loop(0, levels, add, 0)
            put(side, r.book_sum[...])

    def finish_books(stage):
        blocks = entries // 4 // rows
        other_core, other_side = sums.partner[bits - 2], sums.partner[bits - 1]
        if stage == 0:
            for other in range(1, levels):
                sums.arrived(BOOKS, 0, other)

            def put(side, value):
                r.book_send[side] = value.astype(BF16)

            def keep(side, value):
                r.book_own[side * blocks : (side + 1) * blocks] = value.astype(BF16).reshape((blocks, rows, code_width))

            book_half(1 - mine, put)
            sums.remote(r.book_send, r.book_got, other_core, BOOKS, 1)
            book_half(mine, keep)
        elif stage == 1:
            sums.arrived(BOOKS, 1)
            for side in range(2):
                own = r.book_own[side * blocks : (side + 1) * blocks]
                r.book_got[side] = r.book_got[side] + own.reshape(r.book_got.shape[1:])
            sums.remote(r.book_got.at[1 - branch], r.book_last, other_side, BOOKS, 2)
        else:
            sums.arrived(BOOKS, 2)
            total = r.book_got[branch].astype(F32) + r.book_last[...].astype(F32)
            blocks = code_width // 128
            store_segment(r.packed, first_rows[BOOKS], Segment(BOOKS, 0, blocks, 0, blocks, 0, entries // 4), total)

    def all_books():
        parts = entries // TILE

        def one(step, carry):
            at = step // parts
            one_hot = one_hot_rows(r.code_rows[at, 0:1, :], step % parts * TILE, TILE)
            t.books[at, aligned(step % parts, TILE), :] = dot(one_hot, r.g_rows[at]).astype(BF16)
            return carry

        lax.fori_loop(0, levels * parts, one, 0)

    def enc_ffn_back(half):
        def run():
            first, last = half * tiles // 2, (half + 1) * tiles // 2
            if half == 0:
                ffn_backward_begin(r, enc_gain, r.gy)
            ffn_backward_tiles(r, r.w_up_v, r.w_down_v, place.enc_up[half], enc_down, first, last)
            if half == 1:
                ffn_backward_end(r, enc_gain, r.gy, r.gains)

        return run

    def enc_out():
        attention_backward_out(r, r.w_out_e, enc_gain, place.enc_out, r.gains)

    def enc_in(part):
        def run():
            attention_backward_in(r, r.w_qkv_e, place.enc_qkv[part], part)
            if part == 2:
                attention_backward_end(r, enc_gain, r.gains)
                r.grad_tokens[...] = r.gx[...]
                if chunks:
                    spread_gains()

        return run

    def spread_gains():
        lanes = pl.ds(width, 128)
        for layer, ref in enumerate((r.gains, r.dec_gains)):
            for row in range(4):
                for block in range(width // 128):
                    owner = (layer * 4 + row) * (width // 128) + block
                    where = tuple(owner // 2 ** (bits - 1 - i) % 2 for i in range(bits))
                    value = ref[row : row + 1, block * 128 : (block + 1) * 128]
                    rows_here = t.ea2.shape[bits]
                    t.ea2[where + (slice(None), lanes)] = jnp.broadcast_to(value, (rows_here, 128)).astype(BF16)

    work = [
        (9.0, pick, ()),
        (2.0, dec_project, ()),
        (3.0, dec_mix, ()),
        (4.0, dec_ffn, (DD0, DD1)),
        (1.5, dec_ffn_back(0), (DU0,)),
        (1.5, dec_ffn_back(1), (DU1,)),
        (1.5, dec_out, ()),
        (2.0, attention_pairs(0, pairs // 2), ()),
        (2.0, attention_pairs(pairs // 2, pairs), ()),
        (0.7, dec_in(0), (DA0,)),
        (0.7, dec_in(1), ()),
        (0.9, dec_in(2), (DA1,)),
        (2.0, enc_project, ()),
        (3.0, enc_mix, ()),
        (3.0, enc_ffn, ()),
        (4.0, quantizer, (BOOKS, MISC)),
        (2.5, enc_ffn_back(0), (EU0,)),
        (2.5, enc_ffn_back(1), (EU1, ED0, ED1)),
        (1.5, enc_out, ()),
        (2.0, attention_pairs(0, pairs // 2), ()),
        (2.0, attention_pairs(pairs // 2, pairs), ()),
        (0.7, enc_in(0), (EA0,)),
        (0.7, enc_in(1), (EA1,)),
        (1.2, enc_in(2), (EA2,)),
    ]
    if not chunks:
        for _, run, _ in work:
            run()
            if run is quantizer:
                all_books()
        return
    actions = plan(chunks, work, bits, rows * code_width * 2)

    def finish(name, stage):
        if name == BOOKS:
            finish_books(stage)
        elif stage == 0:
            sums.finish(name, 0, sums.half(t[name], name, 0, mine))
        else:
            sums.finish(name, stage)

    for (_, run, made), acts in zip(work, actions):
        run()
        for name in made:
            if name != BOOKS:
                sums.send_half(name, 0, t[name])
        for name, stage in acts:
            finish(name, stage)
    for name, stage in actions[-1]:
        finish(name, stage)
    sums.drain()


POUT, PIN, CODES = 1, 2, 3
DD0, DD1, DU0, DU1, DA0, DA1, MISC = "dd0", "dd1", "du0", "du1", "da0", "da1", "misc"
EU0, EU1, ED0, ED1, EA0, EA1, EA2 = "eu0", "eu1", "ed0", "ed1", "ea0", "ea1", "ea2"


def step(given, devices, with_sums):
    rows, width = given.tokens.shape
    ff = given.enc_up.shape[1]
    levels, entries, code_width = given.books.shape
    given.books = given.books.reshape(levels, -1, rows, code_width)
    bits = devices.bit_length() - 1
    vmem, hbm = pl.BlockSpec(memory_space=pltpu.VMEM), pl.BlockSpec(memory_space=pl.ANY)
    scratch = layer_scratch(rows, width, ff)
    scratch.update(
        w_qkv_e=pltpu.VMEM((width, 3 * width), BF16),
        w_out_e=pltpu.VMEM((width, width), BF16),
        cos=pltpu.VMEM((rows, PAIR), F32),
        sin=pltpu.VMEM((rows, PAIR), F32),
        bias=pltpu.VMEM((rows, rows), F32),
        ring=pltpu.VMEM((4,) + given.books.shape[1:], BF16),
        code_rows=pltpu.VMEM((levels, 8, rows), jnp.int32),
        chosen=pltpu.VMEM((levels, rows, code_width), BF16),
        ac=pltpu.VMEM((rows, code_width), BF16),
        gquant=pltpu.VMEM((rows, width), BF16),
        gy=pltpu.VMEM((rows, width), F32),
        latent=pltpu.VMEM((rows, width), BF16),
        pin_v=pltpu.VMEM((2, width, code_width), BF16),
        pout_v=pltpu.VMEM((2, code_width, width), BF16),
        distill_v=pltpu.VMEM(given.distill.shape, BF16),
        wavlm_v=pltpu.VMEM((rows, given.wavlm.shape[1]), BF16),
        sem_move=pltpu.SemaphoreType.DMA((14,)),
        sem_book=pltpu.SemaphoreType.DMA((4,)),
    )
    outs = Refs(decoded=shaped((rows, width), BF16), grad_tokens=shaped((rows, width), F32))
    chunks, first_rows = {}, {}
    params = dict(vmem_limit_bytes=61 * 2**20)
    if with_sums:
        params.update(collective_id=0, has_side_effects=True)
        c, x, y = bits - 2, bits - 1, bits - 3
        b, a = range(y)
        share = width // devices
        low, high = ff // devices, share
        wide, half, blocks = ff // 128, ff // 256, width // 128
        chunks = dict(
            dd0=Chunk(low, width // 2, [c, x, a, b, y], [Segment(3, 0, blocks, 0, blocks // 2, 0, low)]),
            dd1=Chunk(low, width // 2, [c, a, b, x, y], [Segment(3, blocks // 2, blocks, 0, blocks // 2, 0, low)]),
            du0=Chunk(high, ff // 2, [c, x, a, y, b], [Segment(2, 0, wide, 0, half, 0, high)]),
            du1=Chunk(high, ff // 2, [c, y, a, b, x], [Segment(2, half, wide, 0, half, 0, high)]),
            da0=Chunk(
                high,
                2 * width,
                [c, y, x, a, b],
                [
                    Segment(1, 0, blocks, 0, blocks, 0, high),
                    Segment(0, 0, 3 * blocks, width, blocks, 0, high),
                ],
            ),
            da1=Chunk(high, 2 * width, [c, x, y, a, b], [Segment(0, blocks, 3 * blocks, 0, 2 * blocks, 0, high)]),
            misc=Chunk(
                high,
                3 * width,
                [c, x, y, a, b],
                [
                    Segment(8, 0, 2 * blocks, 0, blocks, 0, high // 2),
                    Segment(8, blocks, 2 * blocks, 0, blocks, high // 2, high // 2),
                    Segment(9, 0, blocks, width, blocks, 0, high),
                    Segment(10, 0, blocks // 2, 2 * width, blocks // 2, 0, high),
                    Segment(10, high * blocks // 2, blocks // 2, 2 * width + code_width, blocks // 2, 0, high),
                ],
            ),
            eu0=Chunk(high, ff // 2, [c, x, y, a, b], [Segment(6, 0, wide, 0, half, 0, high)]),
            eu1=Chunk(high, ff // 2, [c, x, a, y, b], [Segment(6, half, wide, 0, half, 0, high)]),
            ed0=Chunk(low, width // 2, [c, y, x, a, b], [Segment(7, 0, blocks, 0, blocks // 2, 0, low)]),
            ed1=Chunk(low, width // 2, [c, x, a, y, b], [Segment(7, blocks // 2, blocks, 0, blocks // 2, 0, low)]),
            ea0=Chunk(
                high,
                2 * width,
                [c, x, y, a, b],
                [
                    Segment(5, 0, blocks, 0, blocks, 0, high),
                    Segment(4, 0, 3 * blocks, width, blocks, 0, high),
                ],
            ),
            ea1=Chunk(high, width, [c, a, y, b, x], [Segment(4, blocks, 3 * blocks, 0, blocks, 0, high)]),
            ea2=Chunk(
                high,
                width + 128,
                [c, y, a, x, b],
                [
                    Segment(4, 2 * blocks, 3 * blocks, 0, blocks, 0, high),
                    Segment(11, 0, 1, width, 1, 0, 8),
                ],
            ),
        )
        rows_of = [high * 3 * blocks, high * blocks, high * wide, low * blocks] * 2
        rows_of += [high * blocks, high * blocks, high * blocks, 8, entries // 4 * code_width // 128]
        first_rows = {i: sum(rows_of[:i]) for i in range(len(rows_of))}
        first_rows[BOOKS] = first_rows[len(rows_of) - 1]
        copies = len(chunks) * bits + 2 * levels + 2
        scratch.update(
            t={name: pltpu.VMEM(c.shape(bits), BF16) for name, c in chunks.items()},
            recv={
                name: [pltpu.VMEM(c.shape(bits - 1 - stage), BF16) for stage in range(bits)]
                for name, c in chunks.items()
            },
            gains=pltpu.VMEM((4, width), F32),
            dec_gains=pltpu.VMEM((4, width), F32),
            code_got=pltpu.VMEM((levels, 8, rows), jnp.int32),
                book_sum=pltpu.VMEM((entries // 4, code_width), F32),
            book_send=pltpu.VMEM((2, entries // 4, code_width), BF16),
            book_got=pltpu.VMEM((2, entries // 4, code_width), BF16),
            book_last=pltpu.VMEM((entries // 4, code_width), BF16),
            send_sem=pltpu.SemaphoreType.DMA((copies,)),
            recv_sem=pltpu.SemaphoreType.DMA((copies,)),
        )
        outs.packed = shaped((sum(rows_of), 128), F32)
    else:
        outs.update(gains=shaped((4, width), F32), dec_gains=shaped((4, width), F32))
        outs.t = dict(
            enc_qkv=shaped(given.enc_qkv.shape, BF16),
            enc_out=shaped(given.enc_out.shape, BF16),
            enc_up=shaped(given.enc_up.shape, BF16),
            enc_down=shaped(given.enc_down.shape, BF16),
            dec_qkv=shaped(given.enc_qkv.shape, BF16),
            dec_out=shaped(given.enc_out.shape, BF16),
            dec_up=shaped(given.enc_up.shape, BF16),
            dec_down=shaped(given.enc_down.shape, BF16),
            pin=shaped((2 * width, code_width), BF16),
            pout=shaped((2 * code_width, width), BF16),
            books=shaped((levels, entries, code_width), BF16),
            distill=shaped(given.distill.shape, BF16),
        )
    in_specs = dict.fromkeys(given, hbm)
    in_specs.update(
        lengths=pl.BlockSpec(memory_space=pltpu.SMEM), codes=vmem, vectors=vmem, tokens=vmem, cotangent=vmem
    )
    got = pl.pallas_call(
        functools.partial(step_kernel, chunks, first_rows, bits),
        out_shape=dict(outs),
        in_specs=[in_specs],
        out_specs=jax.tree.map(lambda _: vmem, dict(outs)),
        scratch_shapes=[dict(scratch)],
        compiler_params=pltpu.CompilerParams(**params),
        name="step",
    )(dict(given))
    got = Refs(got)
    if not with_sums:
        return got
    last = [shaped((rows, 128), F32) for rows in rows_of]
    last[11] = shaped((1, 128), F32)

    def hand_on(packed, decoded, grad, *refs):
        outs, places, semaphores = refs[: len(last) + 2], refs[len(last) + 2 : -1], refs[-1]
        moves = Moves(semaphores)
        arriving = [moves.start(source, place) for source, place in zip((packed, decoded, grad), places)]
        arriving[0].wait()
        leaving = []
        for i, ref in enumerate(outs[:-2]):
            leaving.append(moves.start(places[0].at[pl.ds(first_rows[i], ref.shape[0])], ref))
        for move, place, ref in zip(arriving[1:], places[1:], outs[-2:]):
            move.wait()
            leaving.append(moves.start(place, ref))
        for move in leaving:
            move.wait()

    return pl.pallas_call(
        hand_on,
        out_shape=last + [outs.decoded, outs.grad_tokens],
        in_specs=[hbm] * 3,
        out_specs=[hbm] * (len(last) + 2),
        scratch_shapes=[
            pltpu.VMEM(got.packed.shape, F32),
            pltpu.VMEM(got.decoded.shape, BF16),
            pltpu.VMEM(got.grad_tokens.shape, F32),
            pltpu.SemaphoreType.DMA((len(last) + 5,)),
        ],
        compiler_params=pltpu.CompilerParams(vmem_limit_bytes=61 * 2**20),
        name="results",
    )(got.packed, got.decoded, got.grad_tokens)


def body(
    tokens,
    wavlm,
    cotangent,
    lengths,
    codes,
    enc_qkv,
    enc_out,
    enc_up,
    enc_down,
    dec_qkv,
    dec_out,
    dec_up,
    dec_down,
    vectors,
    proj_in,
    proj_out,
    codebooks,
    distill_proj,
):
    width = tokens.shape[1]
    devices = lax.axis_size("dp") * lax.axis_size("branch")
    with_sums = devices == 4 * codebooks.shape[0] and width // devices % 16 == 0
    given = Refs(
        tokens=tokens,
        wavlm=wavlm,
        cotangent=cotangent,
        lengths=lengths,
        codes=codes.T,
        enc_qkv=enc_qkv,
        enc_out=enc_out,
        enc_up=enc_up,
        enc_down=enc_down,
        dec_qkv=dec_qkv,
        dec_out=dec_out,
        dec_up=dec_up,
        dec_down=dec_down,
        vectors=vectors,
        pin_own=proj_in,
        pout_own=proj_out,
        books=codebooks,
        distill=distill_proj,
    )
    if with_sums:
        *sums, decoded, grad_tokens = step(given, devices, True)
        sums = [part.reshape(-1) for part in sums]
        order = (4, 5, 6, 7, 0, 1, 2, 3, 11, 10, 9, 12, 8)
        return (decoded, grad_tokens, *[sums[i] for i in order])
    swap = [(0, 1), (1, 0)]
    given.pin_other = lax.ppermute(proj_in, "branch", swap)
    given.pout_other = lax.ppermute(proj_out, "branch", swap)
    s = step(given, devices, False)
    t = Refs(s.t)
    gains = jnp.concatenate([s.gains, s.dec_gains])
    local = [t.enc_qkv, t.enc_out, t.enc_up, t.enc_down, t.dec_qkv, t.dec_out, t.dec_up, t.dec_down]
    local += [gains, t.pin, t.pout, t.books, t.distill]
    sums = [
        lax.psum_scatter(part.astype(F32).reshape(-1), ("dp", "branch"), scatter_dimension=0, tiled=True)
        for part in local
    ]
    return (s.decoded, s.grad_tokens, *sums)


def solution(mesh):
    rows, whole = P(("dp", "branch"), None), P()
    placed = (rows, P("dp", None), rows, rows, P("dp", None)) + (whole,) * 9
    placed += (P("branch", None, None),) * 2 + (whole,) * 2
    return jax.shard_map(
        body,
        mesh=mesh,
        in_specs=placed,
        out_specs=(rows, rows) + (P(("dp", "branch")),) * 13,
        check_vma=False,
    )
```

```python
import functools
import math

import jax
import jax.numpy as jnp
from jax import lax
from jax.experimental import pallas as pl
from jax.experimental.pallas import tpu as pltpu
from jax.sharding import PartitionSpec as P

HEADS = 8
WINDOW = 250
EPS_NORM = 1e-05
EPS_COS = 1e-06
BETA = 0.25
DISTILL = 10.0
ROPE_BASE = 10000.0

MESH = pl.DeviceIdType.MESH
F32 = jnp.float32
BF16 = jnp.bfloat16
TILE = 512
PAIR = 128


def dot(left, right):
    return lax.dot_general(left, right, (((1,), (0,)), ((), ())), preferred_element_type=F32)


def dot_t(left, right):
    return lax.dot_general(left, right, (((1,), (1,)), ((), ())), preferred_element_type=F32)


def t_dot(left, right):
    return lax.dot_general(left, right, (((0,), (0,)), ((), ())), preferred_element_type=F32)


def iota(shape, dim):
    return lax.broadcasted_iota(jnp.int32, shape, dim)


def aligned(index, size):
    return pl.ds(pl.multiple_of(index * size, size), size)


class Refs(dict):
    __getattr__ = dict.__getitem__
    __setattr__ = dict.__setitem__


class Moves:
    def __init__(self, semaphores):
        self.semaphores, self.count = semaphores, 0

    def start(self, source, target):
        move = pltpu.make_async_copy(source, target, self.semaphores.at[self.count])
        self.count += 1
        move.start()
        return move


def layer_scratch(rows, width, ff):
    return Refs(
        x=pltpu.VMEM((rows, width), F32),
        s1=pltpu.VMEM((rows, 1), F32),
        h=pltpu.VMEM((rows, width), BF16),
        h1t=pltpu.VMEM((width, rows), BF16),
        h2t=pltpu.VMEM((width, rows), BF16),
        rinv=pltpu.VMEM((rows, width), F32),
        qkv=pltpu.VMEM((rows, 3 * width), BF16),
        mix=pltpu.VMEM((rows, width), BF16),
        ao=pltpu.VMEM((rows, width), F32),
        x2=pltpu.VMEM((rows, width), F32),
        s2=pltpu.VMEM((rows, 1), F32),
        act=pltpu.VMEM((rows, ff), BF16),
        dg=pltpu.VMEM((rows, ff), BF16),
        fo=pltpu.VMEM((rows, width), F32),
        grad=pltpu.VMEM((rows, width), BF16),
        gx=pltpu.VMEM((rows, width), F32),
        acc=pltpu.VMEM((rows, width), F32),
        w_qkv_v=pltpu.VMEM((width, 3 * width), BF16),
        w_out_v=pltpu.VMEM((width, width), BF16),
        w_up_v=pltpu.VMEM((width, ff), BF16),
        w_down_v=pltpu.VMEM((ff, width), BF16),
    )


def shaped(shape, kind):
    return jax.ShapeDtypeStruct(shape, kind)


def frame_tables(r):
    rows = r.cos.shape[0]
    place = iota((rows, PAIR), 0)
    query, key = iota((rows, rows), 0), iota((rows, rows), 1)
    begin, begin_query = jnp.zeros_like(place), jnp.zeros_like(query)
    edge = 0
    for clip in range(r.lengths.shape[1] - 1):
        edge = edge + r.lengths[0, clip]
        begin = jnp.where(place >= edge, edge, begin)
        begin_query = jnp.where(query >= edge, edge, begin_query)
    allowed = (key >= begin_query) & (key <= query) & (query - key < WINDOW)
    r.bias[...] = jnp.where(allowed, 0.0, -1e30)
    lane = iota((rows, PAIR), 1)
    rate = jnp.exp((lane % 32).astype(F32) * (-math.log(ROPE_BASE) / 32))
    angle = (place - begin).astype(F32) * rate
    r.cos[...] = jnp.cos(angle)
    sine = jnp.sin(angle)
    r.sin[...] = jnp.where(lane % 64 < 32, -sine, sine)


def rotated(value, cosine, sine):
    lane = iota(value.shape, 1)
    swapped = jnp.where(lane % 64 < 32, pltpu.roll(value, PAIR - 32, 1), pltpu.roll(value, 32, 1))
    return value * cosine + swapped * sine


def head_masks(rows):
    low = iota((rows, PAIR), 1) < 64
    return (jnp.where(low, 1.0, 0.0).astype(BF16), jnp.where(low, 0.0, 1.0).astype(BF16))


def attention_project(r, w_qkv, gain):
    width = r.x.shape[1]
    x = r.x[...]
    s1 = lax.rsqrt(jnp.mean(x * x, axis=1, keepdims=True) + EPS_NORM)
    r.s1[...] = s1
    h = (x * s1 * gain(0)).astype(BF16)
    r.h[...] = h
    r.h1t[...] = h.T

    def project(part, carry):
        value = dot(r.h[...], w_qkv[:, aligned(part, width)])
        turn = jnp.where(part < 2, 1.0, 0.0)
        scale = jnp.where(part == 0, 0.125, 1.0)
        cosine = r.cos[...] * turn + (1.0 - turn)
        sine = r.sin[...] * turn
        for p in range(width // PAIR):
            low = rotated(value[:, p * PAIR : (p + 1) * PAIR], cosine, sine).astype(BF16)
            where = pl.ds(pl.multiple_of(part * width + p * PAIR, PAIR), PAIR)
            r.qkv[:, where] = (low.astype(F32) * scale).astype(BF16)
        return carry

    lax.fori_loop(0, 3, project, 0, unroll=True)


def attention_mix(r, w_out, gain):
    rows, width = r.x.shape
    masks = head_masks(rows)
    low = iota((rows, PAIR), 1) < 64

    def pair(p, carry):
        query = r.qkv[:, aligned(p, PAIR)]
        key = r.qkv[:, aligned(p + width // PAIR, PAIR)]
        value = r.qkv[:, aligned(p + 2 * (width // PAIR), PAIR)]
        outs = []
        for h in range(2):
            scores = dot_t(query * masks[h], key) + r.bias[...]
            weights = jnp.exp(scores - jnp.max(scores, axis=1, keepdims=True)).astype(BF16)
            r.att[2 * p + h] = weights
            outs.append(dot(weights, value * masks[h] + masks[1 - h]))
        inverse = 1.0 / pltpu.roll(jnp.where(low, outs[1], outs[0]), 64, 1)
        r.rinv[:, aligned(p, PAIR)] = inverse
        r.mix[:, aligned(p, PAIR)] = (jnp.where(low, outs[0], outs[1]) * inverse).astype(BF16)
        return carry

    lax.fori_loop(0, width // PAIR, pair, 0, unroll=True)
    ao = dot(r.mix[...], w_out[...])
    r.ao[...] = ao
    x2 = r.x[...] + gain(1) * ao
    r.x2[...] = x2
    s2 = lax.rsqrt(jnp.mean(x2 * x2, axis=1, keepdims=True) + EPS_NORM)
    r.s2[...] = s2
    h = (x2 * s2 * gain(2)).astype(BF16)
    r.h[...] = h
    r.h2t[...] = h.T


def ffn_forward(r, w_up, w_down, grad_down=None):
    r.fo[...] = jnp.zeros_like(r.fo)
    slope = math.sqrt(2.0 / math.pi)

    def tile(t, carry):
        cols = aligned(t, TILE)
        pre = dot(r.h[...], w_up[:, cols])
        square = pre * pre
        bent = jnp.tanh(slope * pre * (1.0 + 0.044715 * square))
        half = 0.5 * (1.0 + bent)
        act = (pre * half).astype(BF16)
        r.act[:, cols] = act
        turn = 0.5 * pre * (1.0 - bent * bent) * slope * (1.0 + 3.0 * 0.044715 * square)
        r.dg[:, cols] = (half + turn).astype(BF16)
        r.fo[...] += dot(act, w_down[cols, :])
        if grad_down is not None:
            put_rows(grad_down, t_dot(act, r.grad[...]), t)
        return carry

    lax.fori_loop(0, w_up.shape[1] // TILE, tile, 0, unroll=True)


def norm_back(stream, inverse, grad):
    mean = jnp.mean(grad * stream, axis=1, keepdims=True)
    return inverse * grad - stream * (inverse * inverse * inverse * mean)


def column_sum(value):
    return jnp.sum(value, axis=0, keepdims=True)


class Place:
    def __init__(self, ref, col=0):
        self.ref, self.col = ref, col

    def shift(self, by):
        return Place(self.ref, self.col + by)

    def put(self, value):
        shape = self.ref.shape
        value = value.astype(self.ref.dtype).reshape(shape[:-1] + (value.shape[1],))
        self.ref[(slice(None),) * (len(shape) - 1) + (pl.ds(self.col, value.shape[-1]),)] = value


def put_rows(targets, value, tile):
    value = value.astype(BF16)
    columns = value.shape[1] // len(targets)
    for i, target in enumerate(targets):
        shape = target.shape
        part = value[:, i * columns : (i + 1) * columns]
        if len(shape) == 2:
            target[aligned(tile, value.shape[0]), :] = part
        else:
            target[tile // 2, tile % 2] = part.reshape(shape[2:])


def ffn_backward_begin(r, gain, gy_ref):
    r.grad[...] = (gain(3) * gy_ref[...].astype(F32)).astype(BF16)


def ffn_backward_tiles(r, w_up, w_down, grad_up, grad_down, first, last):
    if first == 0:
        r.acc[...] = jnp.zeros_like(r.acc)

    def tile(t, carry):
        cols = aligned(t, TILE)
        if grad_down is not None:
            put_rows(grad_down, t_dot(r.act[:, cols], r.grad[...]), t)
        grad_pre = (dot_t(r.grad[...], w_down[cols, :]) * r.dg[:, cols].astype(F32)).astype(BF16)
        grad_up.shift(pl.multiple_of((t - first) * TILE, TILE)).put(dot(r.h2t[...], grad_pre))
        r.acc[...] += dot_t(grad_pre, w_up[:, cols])
        return carry

    lax.fori_loop(first, last, tile, 0, unroll=True)


def ffn_backward_end(r, gain, gy_ref, gain_out):
    gy = gy_ref[...].astype(F32)
    gain_out[3:4, :] = column_sum(gy * r.fo[...])
    back = r.acc[...]
    x2, s2 = r.x2[...], r.s2[...]
    gain_out[2:3, :] = column_sum(back * x2 * s2)
    r.gx[...] = gy + norm_back(x2, s2, back * gain(2))


def attention_backward_out(r, w_out, gain, grad_out, gain_out):
    gx = r.gx[...]
    gain_out[1:2, :] = column_sum(gx * r.ao[...])
    grad_attn = (gain(1) * gx).astype(BF16)
    grad_out.put(t_dot(r.mix[...], grad_attn))
    r.grad[...] = dot_t(grad_attn, w_out[...]).astype(BF16)


def attention_backward_pairs(r, first, last):
    rows, width = r.x.shape
    masks = head_masks(rows)
    masks_t = [jnp.where((iota((PAIR, rows), 0) < 64) == (h == 0), 1.0, 0.0).astype(BF16) for h in range(2)]
    pairs = width // PAIR

    def pair(p, carry):
        query = r.qkv[:, aligned(p, PAIR)]
        key = r.qkv[:, aligned(p + pairs, PAIR)]
        value = r.qkv[:, aligned(p + 2 * pairs, PAIR)]
        grad_mixed = (r.grad[:, aligned(p, PAIR)].astype(F32) * r.rinv[:, aligned(p, PAIR)]).astype(BF16)
        product = (grad_mixed.astype(F32) * r.mix[:, aligned(p, PAIR)].astype(F32)).astype(BF16)
        beside = jnp.concatenate([value, jnp.full(value.shape, -1.0, BF16)], axis=1)
        query_t, grad_t = query.T, grad_mixed.T
        to_query = to_key = to_value = 0.0
        for h in range(2):
            weights = r.att[2 * p + h]
            change = dot_t(jnp.concatenate([grad_mixed * masks[h], product * masks[h]], axis=1), beside)
            scores = (weights.astype(F32) * change).astype(BF16)
            to_query = to_query + dot(scores, key * masks[h])
            to_key = to_key + dot(query_t * masks_t[h], scores)
            to_value = to_value + dot(grad_t * masks_t[h], weights)
        cosine, sine = r.cos[...], -r.sin[...]
        r.qkv[:, aligned(p, PAIR)] = rotated(to_query * 0.125, cosine, sine).astype(BF16)
        r.qkv[:, aligned(p + pairs, PAIR)] = rotated(to_key.T, cosine, sine).astype(BF16)
        r.qkv[:, aligned(p + 2 * pairs, PAIR)] = to_value.T.astype(BF16)
        return carry

    lax.fori_loop(first, last, pair, 0, unroll=True)


def attention_backward_in(r, w_qkv, grad_qkv, part):
    width = r.x.shape[1]
    grad = r.qkv[:, part * width : (part + 1) * width]
    grad_qkv.put(dot(r.h1t[...], grad))
    back = dot_t(grad, w_qkv[:, part * width : (part + 1) * width])
    r.acc[...] = back if part == 0 else r.acc[...] + back


def attention_backward_end(r, gain, gain_out):
    back = r.acc[...]
    x, s1 = r.x[...], r.s1[...]
    gain_out[0:1, :] = column_sum(back * x * s1)
    r.gx[...] = r.gx[...] + norm_back(x, s1, back * gain(0))


class Segment:
    def __init__(self, result, base, stride, col, blocks, row, rows):
        self.result, self.base, self.stride, self.col, self.blocks = result, base, stride, col, blocks
        self.row, self.rows = row, rows


class Chunk:
    def __init__(self, rows, columns, order, segments):
        self.rows, self.columns, self.order, self.segments = rows, columns, order, segments

    def shape(self, leading):
        return (2,) * leading + (self.rows, self.columns)

    def bytes(self, bits):
        return 2**bits * self.rows * self.columns * 2


def plan(chunks, work, bits, book_bytes):
    core, x, y = bits - 2, bits - 1, bits - 3
    ends, middle = -1, -2
    free, pending, done = {}, [], []
    now = 0.0

    def carry(link, size, rate=40e3):
        free[link] = max(now, free.get(link, 0.0)) + size / rate
        return free[link]

    def begin(name, stage):
        if name == BOOKS:
            size = 1.2 * 2 ** (bits - 3) * book_bytes
            if stage == 0:
                there = max(carry(y, size), carry(ends, 1.5 * size), carry(middle, 2 * size))
            else:
                there = carry(core, 4 * book_bytes, 400e3) if stage == 1 else carry(x, 2 * book_bytes)
        else:
            dim = chunks[name].order[stage]
            size = chunks[name].bytes(bits) / 2 ** (stage + 1)
            if dim == core:
                there = carry(core, size, 400e3)
            elif dim == x or dim == y:
                there = carry(dim, size)
            else:
                there = carry(ends, size)
                if dim < y - 1:
                    there = max(there, carry(middle, 2 * size))
        pending.append((there + 1.5, name, stage))

    def finish(limit):
        nonlocal now
        acts = []
        while pending:
            pending.sort(key=lambda p: p[0])
            if pending[0][0] + (0.5 if limit < math.inf else 0.0) > limit:
                break
            at, name, stage = pending.pop(0)
            if name == BOOKS:
                cost = (6.0, 0.6, 0.3)[stage]
            else:
                cost = 0.25 + 0.3e-6 * chunks[name].bytes(bits) / 2 ** (stage + 1)
            now = max(now, at) + cost
            limit = max(limit, now)
            acts.append((name, stage))
            if stage + 1 < (3 if name == BOOKS else bits):
                begin(name, stage + 1)
        return acts

    for took, _, names in work:
        now += took
        for name in names:
            begin(name, 0)
        done.append(finish(now))
    done.append(finish(math.inf))
    return done


def coordinates(step, count):
    return [step // 2 ** (count - 1 - i) % 2 for i in range(count)]


def store_segment(packed, first, segment, value):
    for i in range(segment.blocks):
        where = pl.ds(first + segment.base + i, segment.rows, stride=segment.stride)
        packed[where, :] = value[
            segment.row : segment.row + segment.rows, segment.col + i * 128 : segment.col + (i + 1) * 128
        ]


class Halving:
    def __init__(self, chunks, bits, recv, packed, first, send_sem, recv_sem):
        self.chunks = chunks
        self.bits, self.recv, self.packed, self.first = bits, recv, packed, first
        self.send_sem, self.recv_sem = send_sem, recv_sem
        self.copies = {}
        dp, branch = lax.axis_index("dp"), lax.axis_index("branch")
        self.mine, self.partner = [], []
        for dim in range(bits - 1):
            weight = 2 ** (bits - 2 - dim)
            bit = dp // weight % 2
            self.mine.append(bit)
            self.partner.append({"dp": dp + weight * (1 - 2 * bit), "branch": branch})
        self.mine.append(branch)
        self.partner.append({"dp": dp, "branch": 1 - branch})

    def near_level(self, other):
        dp = lax.axis_index("dp")
        for i in range(self.bits - 2):
            if other >> i & 1:
                dp = dp + 2 ** (i + 1) * (1 - 2 * self.mine[self.bits - 3 - i])
        return {"dp": dp, "branch": lax.axis_index("branch")}

    def barrier(self):
        semaphore = pltpu.get_barrier_semaphore()
        levels = 2 ** (self.bits - 2)
        targets = self.partner[self.bits - 2 :] + [self.near_level(other) for other in range(1, levels)]
        for target in targets:
            pl.semaphore_signal(semaphore, inc=1, device_id=target, device_id_type=MESH)
        return lambda: pl.semaphore_wait(semaphore, len(targets))

    def left(self, name, stage):
        return [d for d in range(self.bits) if d not in self.chunks[name].order[:stage]]

    def half(self, ref, name, stage, index):
        position = self.left(name, stage).index(self.chunks[name].order[stage])
        return ref.at[(slice(None),) * position + (index,)]

    def remote(self, source, target, device, *key):
        slot = len(self.copies)
        self.copies[key] = pltpu.make_async_remote_copy(
            src_ref=source,
            dst_ref=target,
            send_sem=self.send_sem.at[slot],
            recv_sem=self.recv_sem.at[slot],
            device_id=device,
            device_id_type=MESH,
        )
        self.copies[key].start()

    def send(self, name, stage, source):
        dim = self.chunks[name].order[stage]
        self.remote(source, self.recv[name][stage], self.partner[dim], name, stage)

    def send_half(self, name, stage, ref):
        dim = self.chunks[name].order[stage]
        self.send(name, stage, self.half(ref, name, stage, 1 - self.mine[dim]))

    def arrived(self, *key):
        self.copies[key].wait_recv()

    def add(self, name, stage, own):
        chunk = self.chunks[name]
        got = self.recv[name][stage]
        depth = self.bits - 1 - stage
        if stage == self.bits - 1:
            value = own[...].astype(F32) + got[...].astype(F32)
            for segment in chunk.segments:
                store_segment(self.packed, self.first[segment.result], segment, value)
            return

        outer = max(depth - 2, 0)

        def step(i, carry):
            where = tuple(coordinates(i, outer))
            got[where] = got[where] + own[where]
            return carry

        lax.fori_loop(0, 2**outer, step, 0)

    def finish(self, name, stage, own=None):
        chunk = self.chunks[name]
        self.arrived(name, stage)
        if own is None:
            dim = chunk.order[stage]
            own = self.half(self.recv[name][stage - 1], name, stage, self.mine[dim])
        self.add(name, stage, own)
        self.follow(name, stage)

    def follow(self, name, stage):
        if stage + 1 < self.bits:
            self.send_half(name, stage + 1, self.recv[name][stage])

    def drain(self):
        for copy in self.copies.values():
            copy.wait_send()


BOOKS = "books"


def quantizer_semantic(r):
    sem_code = r.chosen[0]
    prediction = dot(sem_code, r.distill_v[...])
    target = r.wavlm_v[...].astype(F32)
    pred_norm = lax.rsqrt(jnp.sum(prediction * prediction, axis=1, keepdims=True) + EPS_COS)
    target_norm = lax.rsqrt(jnp.sum(target * target, axis=1, keepdims=True) + EPS_COS)
    cosine = jnp.sum(prediction * target, axis=1, keepdims=True) * (pred_norm * target_norm)
    grad_pred = (
        target * (-DISTILL * pred_norm * target_norm) + prediction * (DISTILL * cosine * pred_norm * pred_norm)
    ).astype(BF16)
    put_distill(r.places.distill, dot(sem_code.T, grad_pred))
    r.gy[:, : sem_code.shape[1]] = dot_t(grad_pred, r.distill_v[...])


def quantizer_latent(r):
    levels = r.chosen.shape[0]
    latent = r.latent[...]
    sem_code, ac_code = r.chosen[0], r.ac[...]
    gquant = r.gquant[...]
    latent_t = latent.T
    grad_sem = dot_t(gquant, r.pout_v[0]) + r.gy[:, : sem_code.shape[1]]
    put_group(r.places.pout, 0, dot(sem_code.T, gquant))
    put_group(r.places.pout, 1, t_dot(ac_code, gquant))
    commit = 2.0 * BETA * (dot(latent, r.pin_v[0]) - sem_code.astype(F32))
    r.g_rows[0] = (grad_sem - commit).astype(BF16)
    to_sem = (grad_sem + commit).astype(BF16)

    grad_ac = dot_t(gquant, r.pout_v[1])
    residual = dot(latent, r.pin_v[1])
    for level in range(1, levels):
        residual = residual - r.chosen[level].astype(F32)
    carry = jnp.zeros_like(residual)
    for level in range(levels - 1, 0, -1):
        carry = carry + 2.0 * BETA * residual
        r.g_rows[level] = (grad_ac - carry).astype(BF16)
        residual = residual + r.chosen[level].astype(F32)
    to_ac = (grad_ac + carry).astype(BF16)
    put_group(r.places.pin, 0, dot(latent_t, to_sem))
    put_group(r.places.pin, 1, dot(latent_t, to_ac))
    r.gy[...] = dot_t(to_sem, r.pin_v[0]) + dot_t(to_ac, r.pin_v[1])


def put_group(place, group, value):
    target, rows = place.ref, value.shape[0]
    value = value.astype(target.dtype)
    if len(target.shape) == 2:
        target[group * rows : (group + 1) * rows, :] = value
        return
    lead, height = target.shape[1:-2], target.shape[-2]
    value = value.reshape(math.prod(lead), -1, height, value.shape[1])
    value = jnp.concatenate([value[:, i] for i in range(value.shape[1])], axis=2)
    columns = value.shape[2]
    where = (group,) + (slice(None),) * (len(lead) + 1) + (pl.ds(place.col, columns),)
    target[where] = value.reshape(lead + (height, columns))


def put_distill(place, value):
    target = place.ref
    if len(target.shape) == 2:
        target[...] = value.astype(target.dtype)
        return
    height = target.shape[-2]
    value = value.reshape(math.prod(target.shape[:-2]), -1, value.shape[1])
    columns = value.shape[2] * value.shape[1] // height
    value = jnp.concatenate([value[:, :, i : i + columns] for i in range(0, value.shape[2], columns)], axis=1)
    where = (slice(None),) * (len(target.shape) - 1) + (pl.ds(place.col, columns),)
    target[where] = value.astype(target.dtype).reshape(target.shape[:-1] + (columns,))


def one_hot_rows(codes, first, count):
    row = iota((count, codes.shape[1]), 0)
    return jnp.where(codes - first == row, 1.0, 0.0).astype(BF16)


def pick_codes(r):
    levels, _, entries, code_width = r.books.shape
    entries = entries * r.books.shape[1]
    rows = r.cos.shape[0]
    slots = r.ring.shape[0]
    branch = lax.axis_index("branch")
    own = r.codes[:, pl.ds(pl.multiple_of(branch * rows, rows), rows)]
    r.code_rows[...] = jnp.broadcast_to(own[:, None, :], r.code_rows.shape)
    columns = jnp.concatenate([own.astype(F32), jnp.zeros((PAIR - levels, rows), F32)], axis=0).T
    lane = iota(columns.shape, 1)
    entry = iota((rows, entries), 1)
    r.code_cols[...] = columns
    r.ac_sum[...] = jnp.zeros(r.ac_sum.shape, F32)

    def book(level):
        slot = level % slots
        return pltpu.make_async_copy(r.books.at[level], r.ring.at[slot], r.sem_book.at[slot])

    def pick(level, carry):
        code = jnp.sum(jnp.where(lane == level, r.code_cols[...], 0.0), axis=1, keepdims=True)
        one_hot = jnp.where(entry == code.astype(jnp.int32), 1.0, 0.0).astype(BF16)
        book(level).wait()
        got = dot(one_hot, r.ring[level % slots].reshape(entries, code_width))
        r.chosen[level] = got.astype(BF16)
        r.ac_sum[...] += jnp.where(level > 0, got, 0.0)

        @pl.when(level + slots < levels)
        def _():
            book(level + slots).start()

        return carry

    def begin():
        for level in range(slots):
            book(level).start()

    def run():
        lax.fori_loop(0, levels, pick, 0, unroll=2)
        r.ac[...] = r.ac_sum[...].astype(BF16)

    return begin, run


def step_kernel(chunks, first_rows, bits, ins, outs, scratch):
    r = Refs({**ins, **outs, **scratch})
    t = r.t = Refs(r.t)
    r.att, r.g_rows, r.g_got, r.book_own = (r.ring.at[i] for i in range(4))
    r.ac_sum, r.code_cols = r.acc.at[:, : r.ac.shape[1]], r.gx.at[:, :PAIR]
    branch = lax.axis_index("branch")
    rows, width = r.tokens.shape
    levels, parts, entries, code_width = r.books.shape
    entries = entries * parts
    tiles = r.w_up_v.shape[1] // TILE
    pairs = width // PAIR
    if chunks:
        sums = Halving(chunks, bits, r.recv, r.packed, first_rows, r.send_sem, r.recv_sem)
        mine, level = sums.mine[bits - 2], lax.axis_index("dp") // 2
        wait_barrier = sums.barrier()
    moves = Moves(r.sem_move)
    begin_pick, run_pick = pick_codes(r)
    begin_pick()
    got_pout = [moves.start(r.pout_own.at[0], r.pout_v.at[branch])]
    got_pin = [moves.start(r.pin_own.at[0], r.pin_v.at[branch])]
    got_attention = [moves.start(r.dec_qkv, r.w_qkv_v), moves.start(r.dec_out, r.w_out_v)]
    got_ffn = [moves.start(r.dec_up, r.w_up_v), moves.start(r.dec_down, r.w_down_v)]
    got_attention_two = [moves.start(r.enc_qkv, r.w_qkv_e), moves.start(r.enc_out, r.w_out_e)]
    got_rest = [
        moves.start(r.wavlm.at[pl.ds(pl.multiple_of(branch * rows, rows), rows)], r.wavlm_v),
        moves.start(r.distill, r.distill_v),
    ]
    got_tokens = [moves.start(r.tokens, r.tokens_v)]
    got_cotangent = [moves.start(r.cotangent, r.cotangent_v)]
    frame_tables(r)
    if chunks:
        wait_barrier()
        sums.remote(r.pout_own.at[0], r.pout_v.at[branch], sums.partner[bits - 1], POUT)
        sums.remote(r.pin_own.at[0], r.pin_v.at[branch], sums.partner[bits - 1], PIN)
    else:
        got_pout.append(moves.start(r.pout_other.at[0], r.pout_v.at[1 - branch]))
        got_pin.append(moves.start(r.pin_other.at[0], r.pin_v.at[1 - branch]))

    if chunks:
        down = dict(dec=[t.dd0, t.dd1], enc=[t.ed0, t.ed1])
        place = r.places = Refs(
            dec_up=[Place(t.du0), Place(t.du1)],
            dec_out=Place(t.da0),
            dec_qkv=[Place(t.da0, width), Place(t.da1), Place(t.da1, width)],
            enc_up=[Place(t.eu0), Place(t.eu1)],
            enc_out=Place(t.ea0),
            enc_qkv=[Place(t.ea0, width), Place(t.ea1), Place(t.ea2)],
            distill=Place(t.di),
            pout=Place(t.misc),
            pin=Place(t.misc, width),
        )
    else:
        down = dict(dec=[t.dec_down], enc=[t.enc_down])
        place = r.places = Refs(
            dec_up=[Place(t.dec_up, i * tiles // 2 * TILE) for i in range(2)],
            dec_out=Place(t.dec_out),
            dec_qkv=[Place(t.dec_qkv, i * width) for i in range(3)],
            enc_up=[Place(t.enc_up, i * tiles // 2 * TILE) for i in range(2)],
            enc_out=Place(t.enc_out),
            enc_qkv=[Place(t.enc_qkv, i * width) for i in range(3)],
            distill=Place(t.distill),
            pout=Place(t.pout),
            pin=Place(t.pin),
        )
    dec_down, enc_down = down["dec"], down["enc"]

    def wait(moves, other=None):
        for move in moves:
            move.wait()
        if chunks and other is not None:
            sums.arrived(other)

    def dec_gain(i):
        return r.vectors[1, i : i + 1, :]

    def enc_gain(i):
        return r.vectors[0, i : i + 1, :]

    def pick():
        run_pick()

    def semantic():
        wait(got_rest)
        quantizer_semantic(r)

    def quant():
        wait(got_pout, POUT)
        r.x[...] = dot(r.chosen[0], r.pout_v[0]) + dot(r.ac[...], r.pout_v[1])
        if chunks:
            for other in range(1, levels):
                target = sums.near_level(other)
                sums.remote(r.code_rows.at[target_level(target)], r.code_got.at[other], target, CODES, other)
            r.code_got[0] = r.code_rows[level]

    def target_level(target):
        return next(iter(target.values())) // 2

    def dec_project():
        wait(got_attention)
        attention_project(r, r.w_qkv_v, dec_gain)

    def dec_mix():
        attention_mix(r, r.w_out_v, dec_gain)

    def dec_ffn():
        wait(got_ffn)
        wait(got_cotangent)
        ffn_backward_begin(r, dec_gain, r.cotangent_v)
        ffn_forward(r, r.w_up_v, r.w_down_v, dec_down)
        r.decoded[...] = (r.x2[...] + dec_gain(3) * r.fo[...]).astype(BF16)

    def dec_ffn_back(half):
        def run():
            first, last = half * tiles // 2, (half + 1) * tiles // 2
            ffn_backward_tiles(r, r.w_up_v, r.w_down_v, place.dec_up[half], None, first, last)
            if half == 1:
                ffn_backward_end(r, dec_gain, r.cotangent_v, r.dec_gains)
                got_ffn[:] = [moves.start(r.enc_up, r.w_up_v), moves.start(r.enc_down, r.w_down_v)]

        return run

    def dec_out():
        attention_backward_out(r, r.w_out_v, dec_gain, place.dec_out, r.dec_gains)

    def attention_pairs(first, last):
        return lambda: attention_backward_pairs(r, first, last)

    def dec_in(part):
        def run():
            attention_backward_in(r, r.w_qkv_v, place.dec_qkv[part], part)
            if part == 2:
                attention_backward_end(r, dec_gain, r.dec_gains)
                r.gquant[...] = r.gx[...].astype(BF16)

        return run

    def enc_project():
        wait(got_tokens)
        r.x[...] = r.tokens_v[...].astype(F32)
        wait(got_attention_two)
        attention_project(r, r.w_qkv_e, enc_gain)

    def enc_mix():
        attention_mix(r, r.w_out_e, enc_gain)

    def enc_ffn():
        wait(got_ffn)
        ffn_forward(r, r.w_up_v, r.w_down_v)
        r.latent[...] = (r.x2[...] + enc_gain(3) * r.fo[...]).astype(BF16)

    def quantizer():
        wait(got_pin, PIN)
        quantizer_latent(r)
        if chunks:
            for other in reversed(range(1, levels)):
                target = sums.near_level(other)
                sums.arrived(CODES, other)
                sums.remote(r.g_rows.at[target_level(target)], r.g_got.at[other], target, BOOKS, 0, other)
            r.g_got[0] = r.g_rows[level]

    def book_half(core, put):
        quarter = entries // 4
        for side in range(2):
            r.book_sum[...] = jnp.zeros_like(r.book_sum)
            first = (core * 2 + side) * quarter

            def add(source, carry):
                one_hot = one_hot_rows(r.code_got[source, 0:1, :], first, quarter)
                r.book_sum[...] += dot(one_hot, r.g_got[source])
                return carry

            lax.fori_loop(0, levels, add, 0, unroll=2)
            put(side, r.book_sum[...])

    def finish_books(stage):
        blocks = entries // 4 // rows
        other_core, other_side = sums.partner[bits - 2], sums.partner[bits - 1]
        if stage == 0:
            for other in range(1, levels):
                sums.arrived(BOOKS, 0, other)

            def put(side, value):
                r.book_send[side] = value.astype(BF16)

            def keep(side, value):
                r.book_own[side * blocks : (side + 1) * blocks] = value.astype(BF16).reshape((blocks, rows, code_width))

            book_half(1 - mine, put)
            sums.remote(r.book_send, r.book_got, other_core, BOOKS, 1)
            book_half(mine, keep)
        elif stage == 1:
            sums.arrived(BOOKS, 1)
            for side in range(2):
                own = r.book_own[side * blocks : (side + 1) * blocks]
                r.book_got[side] = r.book_got[side] + own.reshape(r.book_got.shape[1:])
            sums.remote(r.book_got.at[1 - branch], r.book_last, other_side, BOOKS, 2)
        else:
            sums.arrived(BOOKS, 2)
            total = r.book_got[branch].astype(F32) + r.book_last[...].astype(F32)
            blocks = code_width // 128
            store_segment(r.packed, first_rows[BOOKS], Segment(BOOKS, 0, blocks, 0, blocks, 0, entries // 4), total)

    def all_books():
        parts = entries // TILE

        def one(step, carry):
            at = step // parts
            one_hot = one_hot_rows(r.code_rows[at, 0:1, :], step % parts * TILE, TILE)
            t.books[at, aligned(step % parts, TILE), :] = dot(one_hot, r.g_rows[at]).astype(BF16)
            return carry

        lax.fori_loop(0, levels * parts, one, 0)

    def enc_ffn_back(half):
        def run():
            first, last = half * tiles // 2, (half + 1) * tiles // 2
            if half == 0:
                ffn_backward_begin(r, enc_gain, r.gy)
            ffn_backward_tiles(r, r.w_up_v, r.w_down_v, place.enc_up[half], enc_down, first, last)
            if half == 1:
                ffn_backward_end(r, enc_gain, r.gy, r.gains)

        return run

    def enc_out():
        attention_backward_out(r, r.w_out_e, enc_gain, place.enc_out, r.gains)

    def enc_in(part):
        def run():
            attention_backward_in(r, r.w_qkv_e, place.enc_qkv[part], part)
            if part == 2:
                attention_backward_end(r, enc_gain, r.gains)
                r.grad_tokens[...] = r.gx[...]
                if chunks:
                    spread_gains()

        return run

    def spread_gains():
        lanes = pl.ds(width, 128)
        for layer, ref in enumerate((r.gains, r.dec_gains)):
            for row in range(4):
                for block in range(width // 128):
                    owner = (layer * 4 + row) * (width // 128) + block
                    where = tuple(owner // 2 ** (bits - 1 - i) % 2 for i in range(bits))
                    value = ref[row : row + 1, block * 128 : (block + 1) * 128]
                    rows_here = t.ea2.shape[bits]
                    t.ea2[where + (slice(None), lanes)] = jnp.broadcast_to(value, (rows_here, 128)).astype(BF16)

    work = [
        (7.0, pick, ()),
        (2.0, semantic, (DISTILL_GRAD,)),
        (0.7, quant, ()),
        (1.5, dec_project, ()),
        (2.5, dec_mix, ()),
        (3.0, dec_ffn, (DD0, DD1)),
        (1.2, dec_ffn_back(0), (DU0,)),
        (1.2, dec_ffn_back(1), (DU1,)),
        (1.2, dec_out, ()),
        (1.6, attention_pairs(0, pairs // 2), ()),
        (1.6, attention_pairs(pairs // 2, pairs), ()),
        (0.6, dec_in(0), (DA0,)),
        (0.6, dec_in(1), ()),
        (0.8, dec_in(2), (DA1,)),
        (1.5, enc_project, ()),
        (2.5, enc_mix, ()),
        (2.2, enc_ffn, ()),
        (2.0, quantizer, (BOOKS, MISC)),
        (2.0, enc_ffn_back(0), (EU0,)),
        (2.0, enc_ffn_back(1), (EU1, ED0, ED1)),
        (1.2, enc_out, ()),
        (1.6, attention_pairs(0, pairs // 2), ()),
        (1.6, attention_pairs(pairs // 2, pairs), ()),
        (0.6, enc_in(0), (EA0,)),
        (0.6, enc_in(1), (EA1,)),
        (1.0, enc_in(2), (EA2,)),
    ]
    if not chunks:
        for _, run, _ in work:
            run()
            if run is quantizer:
                all_books()
        return
    actions = plan(chunks, work, bits, rows * code_width * 2)

    def finish(name, stage):
        if name == BOOKS:
            finish_books(stage)
        elif stage == 0:
            sums.finish(name, 0, sums.half(t[name], name, 0, mine))
        else:
            sums.finish(name, stage)

    for (_, run, made), acts in zip(work, actions):
        run()
        for name in made:
            if name != BOOKS:
                sums.send_half(name, 0, t[name])
        for name, stage in acts:
            finish(name, stage)
    for name, stage in actions[-1]:
        finish(name, stage)
    sums.drain()


POUT, PIN, CODES = 1, 2, 3
DISTILL_GRAD = "di"
DD0, DD1, DU0, DU1, DA0, DA1, MISC = "dd0", "dd1", "du0", "du1", "da0", "da1", "misc"
EU0, EU1, ED0, ED1, EA0, EA1, EA2 = "eu0", "eu1", "ed0", "ed1", "ea0", "ea1", "ea2"


def step(given, devices, with_sums):
    rows, width = given.tokens.shape
    ff = given.enc_up.shape[1]
    levels, entries, code_width = given.books.shape
    given.books = given.books.reshape(levels, -1, rows, code_width)
    bits = devices.bit_length() - 1
    vmem, hbm = pl.BlockSpec(memory_space=pltpu.VMEM), pl.BlockSpec(memory_space=pl.ANY)
    scratch = layer_scratch(rows, width, ff)
    scratch.update(
        w_qkv_e=pltpu.VMEM((width, 3 * width), BF16),
        w_out_e=pltpu.VMEM((width, width), BF16),
        cos=pltpu.VMEM((rows, PAIR), F32),
        sin=pltpu.VMEM((rows, PAIR), F32),
        bias=pltpu.VMEM((rows, rows), F32),
        ring=pltpu.VMEM((4,) + given.books.shape[1:], BF16),
        code_rows=pltpu.VMEM((levels, 8, rows), jnp.int32),
        chosen=pltpu.VMEM((levels, rows, code_width), BF16),
        ac=pltpu.VMEM((rows, code_width), BF16),
        gquant=pltpu.VMEM((rows, width), BF16),
        gy=pltpu.VMEM((rows, width), F32),
        latent=pltpu.VMEM((rows, width), BF16),
        pin_v=pltpu.VMEM((2, width, code_width), BF16),
        pout_v=pltpu.VMEM((2, code_width, width), BF16),
        distill_v=pltpu.VMEM(given.distill.shape, BF16),
        wavlm_v=pltpu.VMEM((rows, given.wavlm.shape[1]), BF16),
        tokens_v=pltpu.VMEM((rows, width), BF16),
        cotangent_v=pltpu.VMEM((rows, width), BF16),
        sem_move=pltpu.SemaphoreType.DMA((14,)),
        sem_book=pltpu.SemaphoreType.DMA((4,)),
    )
    outs = Refs(decoded=shaped((rows, width), BF16), grad_tokens=shaped((rows, width), F32))
    chunks, first_rows = {}, {}
    params = dict(vmem_limit_bytes=61 * 2**20)
    if with_sums:
        params.update(collective_id=0, has_side_effects=True)
        c, x, y = bits - 2, bits - 1, bits - 3
        b, a = range(y)
        share = width // devices
        low, high = ff // devices, share
        wide, half, blocks = ff // 128, ff // 256, width // 128
        chunks = dict(
            dd0=Chunk(low, width // 2, [c, a, x, b, y], [Segment(3, 0, blocks, 0, blocks // 2, 0, low)]),
            dd1=Chunk(low, width // 2, [c, y, a, x, b], [Segment(3, blocks // 2, blocks, 0, blocks // 2, 0, low)]),
            du0=Chunk(high, ff // 2, [c, a, x, y, b], [Segment(2, 0, wide, 0, half, 0, high)]),
            du1=Chunk(high, ff // 2, [c, x, a, b, y], [Segment(2, half, wide, 0, half, 0, high)]),
            da0=Chunk(
                high,
                2 * width,
                [c, y, x, a, b],
                [
                    Segment(1, 0, blocks, 0, blocks, 0, high),
                    Segment(0, 0, 3 * blocks, width, blocks, 0, high),
                ],
            ),
            da1=Chunk(high, 2 * width, [c, x, y, a, b], [Segment(0, blocks, 3 * blocks, 0, 2 * blocks, 0, high)]),
            di=Chunk(
                high,
                width,
                [c, a, x, y, b],
                [
                    Segment(8, 0, 2 * blocks, 0, blocks, 0, high // 2),
                    Segment(8, blocks, 2 * blocks, 0, blocks, high // 2, high // 2),
                ],
            ),
            misc=Chunk(
                high,
                2 * width,
                [c, x, y, a, b],
                [
                    Segment(9, 0, blocks, 0, blocks, 0, high),
                    Segment(10, 0, blocks // 2, width, blocks // 2, 0, high),
                    Segment(10, high * blocks // 2, blocks // 2, width + code_width, blocks // 2, 0, high),
                ],
            ),
            eu0=Chunk(high, ff // 2, [c, x, y, a, b], [Segment(6, 0, wide, 0, half, 0, high)]),
            eu1=Chunk(high, ff // 2, [c, x, a, y, b], [Segment(6, half, wide, 0, half, 0, high)]),
            ed0=Chunk(low, width // 2, [c, y, x, a, b], [Segment(7, 0, blocks, 0, blocks // 2, 0, low)]),
            ed1=Chunk(low, width // 2, [c, y, x, a, b], [Segment(7, blocks // 2, blocks, 0, blocks // 2, 0, low)]),
            ea0=Chunk(
                high,
                2 * width,
                [c, x, y, a, b],
                [
                    Segment(5, 0, blocks, 0, blocks, 0, high),
                    Segment(4, 0, 3 * blocks, width, blocks, 0, high),
                ],
            ),
            ea1=Chunk(high, width, [c, x, y, a, b], [Segment(4, blocks, 3 * blocks, 0, blocks, 0, high)]),
            ea2=Chunk(
                high,
                width + 128,
                [c, a, x, y, b],
                [
                    Segment(4, 2 * blocks, 3 * blocks, 0, blocks, 0, high),
                    Segment(11, 0, 1, width, 1, 0, 8),
                ],
            ),
        )
        rows_of = [high * 3 * blocks, high * blocks, high * wide, low * blocks] * 2
        rows_of += [high * blocks, high * blocks, high * blocks, 8, entries // 4 * code_width // 128]
        first_rows = {i: sum(rows_of[:i]) for i in range(len(rows_of))}
        first_rows[BOOKS] = first_rows[len(rows_of) - 1]
        copies = len(chunks) * bits + 2 * levels + 2
        scratch.update(
            t={name: pltpu.VMEM(c.shape(bits), BF16) for name, c in chunks.items()},
            recv={
                name: [pltpu.VMEM(c.shape(bits - 1 - stage), BF16) for stage in range(bits)]
                for name, c in chunks.items()
            },
            gains=pltpu.VMEM((4, width), F32),
            dec_gains=pltpu.VMEM((4, width), F32),
            code_got=pltpu.VMEM((levels, 8, rows), jnp.int32),
                book_sum=pltpu.VMEM((entries // 4, code_width), F32),
            book_send=pltpu.VMEM((2, entries // 4, code_width), BF16),
            book_got=pltpu.VMEM((2, entries // 4, code_width), BF16),
            book_last=pltpu.VMEM((entries // 4, code_width), BF16),
            send_sem=pltpu.SemaphoreType.DMA((copies,)),
            recv_sem=pltpu.SemaphoreType.DMA((copies,)),
        )
        outs.packed = shaped((sum(rows_of), 128), F32)
    else:
        outs.update(gains=shaped((4, width), F32), dec_gains=shaped((4, width), F32))
        outs.t = dict(
            enc_qkv=shaped(given.enc_qkv.shape, BF16),
            enc_out=shaped(given.enc_out.shape, BF16),
            enc_up=shaped(given.enc_up.shape, BF16),
            enc_down=shaped(given.enc_down.shape, BF16),
            dec_qkv=shaped(given.enc_qkv.shape, BF16),
            dec_out=shaped(given.enc_out.shape, BF16),
            dec_up=shaped(given.enc_up.shape, BF16),
            dec_down=shaped(given.enc_down.shape, BF16),
            pin=shaped((2 * width, code_width), BF16),
            pout=shaped((2 * code_width, width), BF16),
            books=shaped((levels, entries, code_width), BF16),
            distill=shaped(given.distill.shape, BF16),
        )
    in_specs = dict.fromkeys(given, hbm)
    in_specs.update(
        lengths=pl.BlockSpec(memory_space=pltpu.SMEM), codes=vmem, vectors=vmem
    )
    got = pl.pallas_call(
        functools.partial(step_kernel, chunks, first_rows, bits),
        out_shape=dict(outs),
        in_specs=[in_specs],
        out_specs=jax.tree.map(lambda _: vmem, dict(outs)),
        scratch_shapes=[dict(scratch)],
        compiler_params=pltpu.CompilerParams(**params),
        name="step",
    )(dict(given))
    got = Refs(got)
    if not with_sums:
        return got
    last = [shaped((rows, 128), F32) for rows in rows_of]
    last[11] = shaped((1, 128), F32)

    def hand_on(packed, decoded, grad, *refs):
        outs, places, semaphores = refs[: len(last) + 2], refs[len(last) + 2 : -1], refs[-1]
        moves = Moves(semaphores)
        arriving = [moves.start(source, place) for source, place in zip((packed, decoded, grad), places)]
        arriving[0].wait()
        leaving = []
        for i, ref in enumerate(outs[:-2]):
            leaving.append(moves.start(places[0].at[pl.ds(first_rows[i], ref.shape[0])], ref))
        for move, place, ref in zip(arriving[1:], places[1:], outs[-2:]):
            move.wait()
            leaving.append(moves.start(place, ref))
        for move in leaving:
            move.wait()

    return pl.pallas_call(
        hand_on,
        out_shape=last + [outs.decoded, outs.grad_tokens],
        in_specs=[hbm] * 3,
        out_specs=[hbm] * (len(last) + 2),
        scratch_shapes=[
            pltpu.VMEM(got.packed.shape, F32),
            pltpu.VMEM(got.decoded.shape, BF16),
            pltpu.VMEM(got.grad_tokens.shape, F32),
            pltpu.SemaphoreType.DMA((len(last) + 5,)),
        ],
        compiler_params=pltpu.CompilerParams(vmem_limit_bytes=61 * 2**20),
        name="results",
    )(got.packed, got.decoded, got.grad_tokens)


def body(
    tokens,
    wavlm,
    cotangent,
    lengths,
    codes,
    enc_qkv,
    enc_out,
    enc_up,
    enc_down,
    dec_qkv,
    dec_out,
    dec_up,
    dec_down,
    vectors,
    proj_in,
    proj_out,
    codebooks,
    distill_proj,
):
    width = tokens.shape[1]
    devices = lax.axis_size("dp") * lax.axis_size("branch")
    with_sums = devices == 4 * codebooks.shape[0] and width // devices % 16 == 0
    given = Refs(
        tokens=tokens,
        wavlm=wavlm,
        cotangent=cotangent,
        lengths=lengths,
        codes=codes.T,
        enc_qkv=enc_qkv,
        enc_out=enc_out,
        enc_up=enc_up,
        enc_down=enc_down,
        dec_qkv=dec_qkv,
        dec_out=dec_out,
        dec_up=dec_up,
        dec_down=dec_down,
        vectors=vectors,
        pin_own=proj_in,
        pout_own=proj_out,
        books=codebooks,
        distill=distill_proj,
    )
    if with_sums:
        *sums, decoded, grad_tokens = step(given, devices, True)
        sums = [part.reshape(-1) for part in sums]
        order = (4, 5, 6, 7, 0, 1, 2, 3, 11, 10, 9, 12, 8)
        return (decoded, grad_tokens, *[sums[i] for i in order])
    swap = [(0, 1), (1, 0)]
    given.pin_other = lax.ppermute(proj_in, "branch", swap)
    given.pout_other = lax.ppermute(proj_out, "branch", swap)
    s = step(given, devices, False)
    t = Refs(s.t)
    gains = jnp.concatenate([s.gains, s.dec_gains])
    local = [t.enc_qkv, t.enc_out, t.enc_up, t.enc_down, t.dec_qkv, t.dec_out, t.dec_up, t.dec_down]
    local += [gains, t.pin, t.pout, t.books, t.distill]
    sums = [
        lax.psum_scatter(part.astype(F32).reshape(-1), ("dp", "branch"), scatter_dimension=0, tiled=True)
        for part in local
    ]
    return (s.decoded, s.grad_tokens, *sums)


def solution(mesh):
    rows, whole = P(("dp", "branch"), None), P()
    placed = (rows, P("dp", None), rows, rows, P("dp", None)) + (whole,) * 9
    placed += (P("branch", None, None),) * 2 + (whole,) * 2
    return jax.shard_map(
        body,
        mesh=mesh,
        in_specs=placed,
        out_specs=(rows, rows) + (P(("dp", "branch")),) * 13,
        check_vma=False,
    )
```

```python
import functools
import math

import jax
import jax.numpy as jnp
from jax import lax
from jax.experimental import pallas as pl
from jax.experimental.pallas import tpu as pltpu
from jax.sharding import PartitionSpec as P

HEADS = 8
WINDOW = 250
EPS_NORM = 1e-05
EPS_COS = 1e-06
BETA = 0.25
DISTILL = 10.0
ROPE_BASE = 10000.0

MESH = pl.DeviceIdType.MESH
F32 = jnp.float32
BF16 = jnp.bfloat16
TILE = 512
PAIR = 128


def dot(left, right):
    return lax.dot_general(left, right, (((1,), (0,)), ((), ())), preferred_element_type=F32)


def dot_t(left, right):
    return lax.dot_general(left, right, (((1,), (1,)), ((), ())), preferred_element_type=F32)


def t_dot(left, right):
    return lax.dot_general(left, right, (((0,), (0,)), ((), ())), preferred_element_type=F32)


def iota(shape, dim):
    return lax.broadcasted_iota(jnp.int32, shape, dim)


def aligned(index, size):
    return pl.ds(pl.multiple_of(index * size, size), size)


class Refs(dict):
    __getattr__ = dict.__getitem__
    __setattr__ = dict.__setitem__


class Moves:
    def __init__(self, semaphores):
        self.semaphores, self.count = semaphores, 0

    def start(self, source, target):
        move = pltpu.make_async_copy(source, target, self.semaphores.at[self.count])
        self.count += 1
        move.start()
        return move


def layer_scratch(rows, width, ff):
    return Refs(
        x=pltpu.VMEM((rows, width), F32),
        s1=pltpu.VMEM((rows, 1), F32),
        h=pltpu.VMEM((rows, width), BF16),
        h1t=pltpu.VMEM((width, rows), BF16),
        h2t=pltpu.VMEM((width, rows), BF16),
        rinv=pltpu.VMEM((rows, width), F32),
        qkv=pltpu.VMEM((rows, 3 * width), BF16),
        mix=pltpu.VMEM((rows, width), BF16),
        ao=pltpu.VMEM((rows, width), F32),
        x2=pltpu.VMEM((rows, width), F32),
        s2=pltpu.VMEM((rows, 1), F32),
        act=pltpu.VMEM((rows, ff), BF16),
        dg=pltpu.VMEM((rows, ff), BF16),
        fo=pltpu.VMEM((rows, width), F32),
        grad=pltpu.VMEM((rows, width), BF16),
        gx=pltpu.VMEM((rows, width), F32),
        acc=pltpu.VMEM((rows, width), F32),
        w_qkv_v=pltpu.VMEM((width, 3 * width), BF16),
        w_out_v=pltpu.VMEM((width, width), BF16),
        w_up_v=pltpu.VMEM((width, ff), BF16),
        w_down_v=pltpu.VMEM((ff, width), BF16),
    )


def shaped(shape, kind):
    return jax.ShapeDtypeStruct(shape, kind)


def frame_tables(r):
    rows = r.cos.shape[0]
    place = iota((rows, PAIR), 0)
    query, key = iota((rows, rows), 0), iota((rows, rows), 1)
    begin, begin_query = jnp.zeros_like(place), jnp.zeros_like(query)
    edge = 0
    for clip in range(r.lengths.shape[1] - 1):
        edge = edge + r.lengths[0, clip]
        begin = jnp.where(place >= edge, edge, begin)
        begin_query = jnp.where(query >= edge, edge, begin_query)
    allowed = (key >= begin_query) & (key <= query) & (query - key < WINDOW)
    r.bias[...] = jnp.where(allowed, 0.0, -1e30)
    lane = iota((rows, PAIR), 1)
    rate = jnp.exp((lane % 32).astype(F32) * (-math.log(ROPE_BASE) / 32))
    angle = (place - begin).astype(F32) * rate
    r.cos[...] = jnp.cos(angle)
    sine = jnp.sin(angle)
    r.sin[...] = jnp.where(lane % 64 < 32, -sine, sine)


def rotated(value, cosine, sine):
    lane = iota(value.shape, 1)
    swapped = jnp.where(lane % 64 < 32, pltpu.roll(value, PAIR - 32, 1), pltpu.roll(value, 32, 1))
    return value * cosine + swapped * sine


def head_masks(rows):
    low = iota((rows, PAIR), 1) < 64
    return (jnp.where(low, 1.0, 0.0).astype(BF16), jnp.where(low, 0.0, 1.0).astype(BF16))


def attention_project(r, w_qkv, gain):
    width = r.x.shape[1]
    x = r.x[...]
    s1 = lax.rsqrt(jnp.mean(x * x, axis=1, keepdims=True) + EPS_NORM)
    r.s1[...] = s1
    h = (x * s1 * gain(0)).astype(BF16)
    r.h[...] = h
    r.h1t[...] = h.T

    def project(part, carry):
        value = dot(r.h[...], w_qkv[:, aligned(part, width)])
        turn = jnp.where(part < 2, 1.0, 0.0)
        scale = jnp.where(part == 0, 0.125, 1.0)
        cosine = r.cos[...] * turn + (1.0 - turn)
        sine = r.sin[...] * turn
        for p in range(width // PAIR):
            low = rotated(value[:, p * PAIR : (p + 1) * PAIR], cosine, sine).astype(BF16)
            where = pl.ds(pl.multiple_of(part * width + p * PAIR, PAIR), PAIR)
            r.qkv[:, where] = (low.astype(F32) * scale).astype(BF16)
        return carry

    lax.fori_loop(0, 3, project, 0, unroll=True)


def attention_mix(r, w_out, gain):
    rows, width = r.x.shape
    masks = head_masks(rows)
    low = iota((rows, PAIR), 1) < 64

    def pair(p, carry):
        query = r.qkv[:, aligned(p, PAIR)]
        key = r.qkv[:, aligned(p + width // PAIR, PAIR)]
        value = r.qkv[:, aligned(p + 2 * (width // PAIR), PAIR)]
        outs = []
        for h in range(2):
            scores = dot_t(query * masks[h], key) + r.bias[...]
            weights = jnp.exp(scores - jnp.max(scores, axis=1, keepdims=True)).astype(BF16)
            r.att[2 * p + h] = weights
            outs.append(dot(weights, value * masks[h] + masks[1 - h]))
        inverse = 1.0 / pltpu.roll(jnp.where(low, outs[1], outs[0]), 64, 1)
        r.rinv[:, aligned(p, PAIR)] = inverse
        r.mix[:, aligned(p, PAIR)] = (jnp.where(low, outs[0], outs[1]) * inverse).astype(BF16)
        return carry

    lax.fori_loop(0, width // PAIR, pair, 0, unroll=True)
    ao = dot(r.mix[...], w_out[...])
    r.ao[...] = ao
    x2 = r.x[...] + gain(1) * ao
    r.x2[...] = x2
    s2 = lax.rsqrt(jnp.mean(x2 * x2, axis=1, keepdims=True) + EPS_NORM)
    r.s2[...] = s2
    h = (x2 * s2 * gain(2)).astype(BF16)
    r.h[...] = h
    r.h2t[...] = h.T


def gelu_parts(pre):
    slope = math.sqrt(2.0 / math.pi)
    square = pre * pre
    bent = jnp.tanh(slope * pre * (1.0 + 0.044715 * square))
    half = 0.5 * (1.0 + bent)
    turn = 0.5 * pre * (1.0 - bent * bent) * slope * (1.0 + 3.0 * 0.044715 * square)
    return (pre * half).astype(BF16), half + turn


def ffn_forward(r, w_up, w_down):
    r.fo[...] = jnp.zeros_like(r.fo)

    def tile(t, carry):
        cols = aligned(t, TILE)
        act, slope = gelu_parts(dot(r.h[...], w_up[:, cols]))
        r.act[:, cols] = act
        r.dg[:, cols] = slope.astype(BF16)
        r.fo[...] += dot(act, w_down[cols, :])
        return carry

    lax.fori_loop(0, w_up.shape[1] // TILE, tile, 0, unroll=True)


def ffn_both(r, w_up, w_down, grad_up, grad_down, first, last):
    if first == 0:
        r.fo[...] = jnp.zeros_like(r.fo)
        r.acc[...] = jnp.zeros_like(r.acc)

    def tile(t, carry):
        cols = aligned(t, TILE)
        act, slope = gelu_parts(dot(r.h[...], w_up[:, cols]))
        grad_pre = (dot_t(r.grad[...], w_down[cols, :]) * slope).astype(BF16)
        grad_up.shift(pl.multiple_of((t - first) * TILE, TILE)).put(dot(r.h2t[...], grad_pre))
        put_rows(grad_down, t_dot(act, r.grad[...]), t)
        r.fo[...] += dot(act, w_down[cols, :])
        r.acc[...] += dot_t(grad_pre, w_up[:, cols])
        return carry

    lax.fori_loop(first, last, tile, 0, unroll=True)


def norm_back(stream, inverse, grad):
    mean = jnp.mean(grad * stream, axis=1, keepdims=True)
    return inverse * grad - stream * (inverse * inverse * inverse * mean)


def column_sum(value):
    return jnp.sum(value, axis=0, keepdims=True)


class Place:
    def __init__(self, ref, col=0):
        self.ref, self.col = ref, col

    def shift(self, by):
        return Place(self.ref, self.col + by)

    def put(self, value):
        shape = self.ref.shape
        value = value.astype(self.ref.dtype).reshape(shape[:-1] + (value.shape[1],))
        self.ref[(slice(None),) * (len(shape) - 1) + (pl.ds(self.col, value.shape[-1]),)] = value


def put_rows(targets, value, tile):
    value = value.astype(BF16)
    begin = 0
    for target in targets:
        shape = target.shape
        part = value[:, begin : begin + shape[-1]]
        begin += shape[-1]
        if len(shape) == 2:
            target[aligned(tile, value.shape[0]), :] = part
        else:
            target[tile // 2, tile % 2] = part.reshape(shape[2:])


def ffn_backward_begin(r, gain, gy_ref):
    r.grad[...] = (gain(3) * gy_ref[...].astype(F32)).astype(BF16)


def ffn_backward_tiles(r, w_up, w_down, grad_up, grad_down, first, last):
    if first == 0:
        r.acc[...] = jnp.zeros_like(r.acc)

    def tile(t, carry):
        cols = aligned(t, TILE)
        put_rows(grad_down, t_dot(r.act[:, cols], r.grad[...]), t)
        grad_pre = (dot_t(r.grad[...], w_down[cols, :]) * r.dg[:, cols].astype(F32)).astype(BF16)
        grad_up.shift(pl.multiple_of((t - first) * TILE, TILE)).put(dot(r.h2t[...], grad_pre))
        r.acc[...] += dot_t(grad_pre, w_up[:, cols])
        return carry

    lax.fori_loop(first, last, tile, 0, unroll=True)


def ffn_backward_end(r, gain, gy_ref, gain_out):
    gy = gy_ref[...].astype(F32)
    gain_out[3:4, :] = column_sum(gy * r.fo[...])
    back = r.acc[...]
    x2, s2 = r.x2[...], r.s2[...]
    gain_out[2:3, :] = column_sum(back * x2 * s2)
    r.gx[...] = gy + norm_back(x2, s2, back * gain(2))


def attention_backward_out(r, w_out, gain, grad_out, gain_out):
    gx = r.gx[...]
    gain_out[1:2, :] = column_sum(gx * r.ao[...])
    grad_attn = (gain(1) * gx).astype(BF16)
    grad_out.put(t_dot(r.mix[...], grad_attn))
    r.grad[...] = dot_t(grad_attn, w_out[...]).astype(BF16)


def attention_backward_pairs(r, first, last):
    rows, width = r.x.shape
    masks = head_masks(rows)
    masks_t = [jnp.where((iota((PAIR, rows), 0) < 64) == (h == 0), 1.0, 0.0).astype(BF16) for h in range(2)]
    pairs = width // PAIR

    def pair(p, carry):
        query = r.qkv[:, aligned(p, PAIR)]
        key = r.qkv[:, aligned(p + pairs, PAIR)]
        value = r.qkv[:, aligned(p + 2 * pairs, PAIR)]
        grad_mixed = (r.grad[:, aligned(p, PAIR)].astype(F32) * r.rinv[:, aligned(p, PAIR)]).astype(BF16)
        product = (grad_mixed.astype(F32) * r.mix[:, aligned(p, PAIR)].astype(F32)).astype(BF16)
        beside = jnp.concatenate([value, jnp.full(value.shape, -1.0, BF16)], axis=1)
        query_t, grad_t = query.T, grad_mixed.T
        to_query = to_key = to_value = 0.0
        for h in range(2):
            weights = r.att[2 * p + h]
            change = dot_t(jnp.concatenate([grad_mixed * masks[h], product * masks[h]], axis=1), beside)
            scores = (weights.astype(F32) * change).astype(BF16)
            to_query = to_query + dot(scores, key * masks[h])
            to_key = to_key + dot(query_t * masks_t[h], scores)
            to_value = to_value + dot(grad_t * masks_t[h], weights)
        cosine, sine = r.cos[...], -r.sin[...]
        r.qkv[:, aligned(p, PAIR)] = rotated(to_query * 0.125, cosine, sine).astype(BF16)
        r.qkv[:, aligned(p + pairs, PAIR)] = rotated(to_key.T, cosine, sine).astype(BF16)
        r.qkv[:, aligned(p + 2 * pairs, PAIR)] = to_value.T.astype(BF16)
        return carry

    lax.fori_loop(first, last, pair, 0, unroll=True)


def attention_backward_in(r, w_qkv, grad_qkv, part):
    width = r.x.shape[1]
    grad = r.qkv[:, part * width : (part + 1) * width]
    grad_qkv.put(dot(r.h1t[...], grad))
    back = dot_t(grad, w_qkv[:, part * width : (part + 1) * width])
    r.acc[...] = back if part == 0 else r.acc[...] + back


def attention_backward_end(r, gain, gain_out):
    back = r.acc[...]
    x, s1 = r.x[...], r.s1[...]
    gain_out[0:1, :] = column_sum(back * x * s1)
    r.gx[...] = r.gx[...] + norm_back(x, s1, back * gain(0))


class Segment:
    def __init__(self, result, base, stride, col, blocks, row, rows):
        self.result, self.base, self.stride, self.col, self.blocks = result, base, stride, col, blocks
        self.row, self.rows = row, rows


class Chunk:
    def __init__(self, rows, columns, order, segments):
        self.rows, self.columns, self.order, self.segments = rows, columns, order, segments

    def shape(self, leading):
        return (2,) * leading + (self.rows, self.columns)

    def bytes(self, bits):
        return 2**bits * self.rows * self.columns * 2


def plan(chunks, work, bits, book_bytes):
    core, x, y = bits - 2, bits - 1, bits - 3
    ends, middle = -1, -2
    free, pending, done = {}, [], []
    now = 0.0

    def carry(link, size, rate=42e3):
        free[link] = max(now, free.get(link, 0.0)) + size / rate
        return free[link]

    def begin(name, stage):
        if name == BOOKS:
            size = 1.2 * 2 ** (bits - 3) * book_bytes
            if stage == 0:
                there = max(carry(y, size), carry(ends, 1.5 * size), carry(middle, 2 * size))
            else:
                there = carry(core, 4 * book_bytes, 400e3) if stage == 1 else carry(x, 2 * book_bytes)
        else:
            dim = chunks[name].order[stage]
            size = chunks[name].bytes(bits) / 2 ** (stage + 1)
            if dim == core:
                there = carry(core, size, 400e3)
            elif dim == x or dim == y:
                there = carry(dim, size)
            else:
                there = carry(ends, size)
                if dim < y - 1:
                    there = max(there, carry(middle, 2 * size))
        pending.append((there + 1.5, name, stage))

    def finish(limit):
        nonlocal now
        acts = []
        while pending:
            pending.sort(key=lambda p: p[0])
            if pending[0][0] + (0.5 if limit < math.inf else 0.0) > limit:
                break
            at, name, stage = pending.pop(0)
            if name == BOOKS:
                cost = (6.0, 0.6, 0.3)[stage]
            else:
                cost = 0.25 + 0.3e-6 * chunks[name].bytes(bits) / 2 ** (stage + 1)
            now = max(now, at) + cost
            limit = max(limit, now)
            acts.append((name, stage))
            if stage + 1 < (3 if name == BOOKS else bits):
                begin(name, stage + 1)
        return acts

    for took, _, names in work:
        now += 0.95 * took
        for name in names:
            begin(name, 0)
        done.append(finish(now))
    done.append(finish(math.inf))
    return done


def coordinates(step, count):
    return [step // 2 ** (count - 1 - i) % 2 for i in range(count)]


def store_segment(packed, first, segment, value):
    for i in range(segment.blocks):
        where = pl.ds(first + segment.base + i, segment.rows, stride=segment.stride)
        packed[where, :] = value[
            segment.row : segment.row + segment.rows, segment.col + i * 128 : segment.col + (i + 1) * 128
        ]


class Halving:
    def __init__(self, chunks, bits, recv, packed, first, send_sem, recv_sem):
        self.chunks = chunks
        self.bits, self.recv, self.packed, self.first = bits, recv, packed, first
        self.send_sem, self.recv_sem = send_sem, recv_sem
        self.copies = {}
        dp, branch = lax.axis_index("dp"), lax.axis_index("branch")
        self.mine, self.partner = [], []
        for dim in range(bits - 1):
            weight = 2 ** (bits - 2 - dim)
            bit = dp // weight % 2
            self.mine.append(bit)
            self.partner.append({"dp": dp + weight * (1 - 2 * bit), "branch": branch})
        self.mine.append(branch)
        self.partner.append({"dp": dp, "branch": 1 - branch})

    def near_level(self, other):
        dp = lax.axis_index("dp")
        for i in range(self.bits - 2):
            if other >> i & 1:
                dp = dp + 2 ** (i + 1) * (1 - 2 * self.mine[self.bits - 3 - i])
        return {"dp": dp, "branch": lax.axis_index("branch")}

    def barrier(self):
        semaphore = pltpu.get_barrier_semaphore()
        levels = 2 ** (self.bits - 2)
        targets = self.partner[self.bits - 2 :] + [self.near_level(other) for other in range(1, levels)]
        for target in targets:
            pl.semaphore_signal(semaphore, inc=1, device_id=target, device_id_type=MESH)
        return lambda: pl.semaphore_wait(semaphore, len(targets))

    def left(self, name, stage):
        return [d for d in range(self.bits) if d not in self.chunks[name].order[:stage]]

    def half(self, ref, name, stage, index):
        position = self.left(name, stage).index(self.chunks[name].order[stage])
        return ref.at[(slice(None),) * position + (index,)]

    def remote(self, source, target, device, *key):
        slot = len(self.copies)
        self.copies[key] = pltpu.make_async_remote_copy(
            src_ref=source,
            dst_ref=target,
            send_sem=self.send_sem.at[slot],
            recv_sem=self.recv_sem.at[slot],
            device_id=device,
            device_id_type=MESH,
        )
        self.copies[key].start()

    def send(self, name, stage, source):
        dim = self.chunks[name].order[stage]
        self.remote(source, self.recv[name][stage], self.partner[dim], name, stage)

    def send_half(self, name, stage, ref):
        dim = self.chunks[name].order[stage]
        self.send(name, stage, self.half(ref, name, stage, 1 - self.mine[dim]))

    def arrived(self, *key):
        self.copies[key].wait_recv()

    def add(self, name, stage, own):
        chunk = self.chunks[name]
        got = self.recv[name][stage]
        depth = self.bits - 1 - stage
        if stage == self.bits - 1:
            value = own[...].astype(F32) + got[...].astype(F32)
            for segment in chunk.segments:
                store_segment(self.packed, self.first[segment.result], segment, value)
            return

        outer = max(depth - 2, 0)

        def step(i, carry):
            where = tuple(coordinates(i, outer))
            got[where] = got[where] + own[where]
            return carry

        lax.fori_loop(0, 2**outer, step, 0)

    def finish(self, name, stage, own=None):
        chunk = self.chunks[name]
        self.arrived(name, stage)
        if own is None:
            dim = chunk.order[stage]
            own = self.half(self.recv[name][stage - 1], name, stage, self.mine[dim])
        self.add(name, stage, own)
        self.follow(name, stage)

    def follow(self, name, stage):
        if stage + 1 < self.bits:
            self.send_half(name, stage + 1, self.recv[name][stage])

    def drain(self):
        for copy in self.copies.values():
            copy.wait_send()


BOOKS = "books"


def quantizer_semantic(r):
    sem_code = r.chosen[0]
    prediction = dot(sem_code, r.distill_v[...])
    target = r.wavlm_v[...].astype(F32)
    pred_norm = lax.rsqrt(jnp.sum(prediction * prediction, axis=1, keepdims=True) + EPS_COS)
    target_norm = lax.rsqrt(jnp.sum(target * target, axis=1, keepdims=True) + EPS_COS)
    cosine = jnp.sum(prediction * target, axis=1, keepdims=True) * (pred_norm * target_norm)
    grad_pred = (
        target * (-DISTILL * pred_norm * target_norm) + prediction * (DISTILL * cosine * pred_norm * pred_norm)
    ).astype(BF16)
    put_distill(r.places.distill, dot(sem_code.T, grad_pred))
    r.gy[:, : sem_code.shape[1]] = dot_t(grad_pred, r.distill_v[...])


def quantizer_latent(r):
    levels = r.chosen.shape[0]
    latent = r.latent[...]
    sem_code, ac_code = r.chosen[0], r.ac[...]
    gquant = r.gquant[...]
    latent_t = latent.T
    grad_sem = dot_t(gquant, r.pout_v[0]) + r.gy[:, : sem_code.shape[1]]
    put_group(r.places.pout, 0, dot(sem_code.T, gquant))
    put_group(r.places.pout, 1, t_dot(ac_code, gquant))
    commit = 2.0 * BETA * (dot(latent, r.pin_v[0]) - sem_code.astype(F32))
    r.g_rows[0] = (grad_sem - commit).astype(BF16)
    to_sem = (grad_sem + commit).astype(BF16)

    grad_ac = dot_t(gquant, r.pout_v[1])
    residual = dot(latent, r.pin_v[1])
    for level in range(1, levels):
        residual = residual - r.chosen[level].astype(F32)
    carry = jnp.zeros_like(residual)
    for level in range(levels - 1, 0, -1):
        carry = carry + 2.0 * BETA * residual
        r.g_rows[level] = (grad_ac - carry).astype(BF16)
        residual = residual + r.chosen[level].astype(F32)
    to_ac = (grad_ac + carry).astype(BF16)
    put_group(r.places.pin, 0, dot(latent_t, to_sem))
    put_group(r.places.pin, 1, dot(latent_t, to_ac))
    r.gy[...] = dot_t(to_sem, r.pin_v[0]) + dot_t(to_ac, r.pin_v[1])


def put_group(place, group, value):
    target, rows = place.ref, value.shape[0]
    value = value.astype(target.dtype)
    if len(target.shape) == 2:
        target[group * rows : (group + 1) * rows, :] = value
        return
    lead, height = target.shape[1:-2], target.shape[-2]
    value = value.reshape(math.prod(lead), -1, height, value.shape[1])
    value = jnp.concatenate([value[:, i] for i in range(value.shape[1])], axis=2)
    columns = value.shape[2]
    where = (group,) + (slice(None),) * (len(lead) + 1) + (pl.ds(place.col, columns),)
    target[where] = value.reshape(lead + (height, columns))


def put_distill(place, value):
    target = place.ref
    if len(target.shape) == 2:
        target[...] = value.astype(target.dtype)
        return
    height = target.shape[-2]
    value = value.reshape(math.prod(target.shape[:-2]), -1, value.shape[1])
    columns = value.shape[2] * value.shape[1] // height
    value = jnp.concatenate([value[:, :, i : i + columns] for i in range(0, value.shape[2], columns)], axis=1)
    where = (slice(None),) * (len(target.shape) - 1) + (pl.ds(place.col, columns),)
    target[where] = value.astype(target.dtype).reshape(target.shape[:-1] + (columns,))


def one_hot_rows(codes, first, count):
    row = iota((count, codes.shape[1]), 0)
    return jnp.where(codes - first == row, 1.0, 0.0).astype(BF16)


def pick_codes(r):
    levels, _, entries, code_width = r.books.shape
    entries = entries * r.books.shape[1]
    rows = r.cos.shape[0]
    slots = r.ring.shape[0]
    branch = lax.axis_index("branch")
    own = r.codes[:, pl.ds(pl.multiple_of(branch * rows, rows), rows)]
    r.code_rows[...] = jnp.broadcast_to(own[:, None, :], r.code_rows.shape)
    columns = jnp.concatenate([own.astype(F32), jnp.zeros((PAIR - levels, rows), F32)], axis=0).T
    lane = iota(columns.shape, 1)
    entry = iota((rows, entries), 1)
    r.code_cols[...] = columns
    r.ac_sum[...] = jnp.zeros(r.ac_sum.shape, F32)

    def book(level):
        slot = level % slots
        return pltpu.make_async_copy(r.books.at[level], r.ring.at[slot], r.sem_book.at[slot])

    def pick(level, carry):
        code = jnp.sum(jnp.where(lane == level, r.code_cols[...], 0.0), axis=1, keepdims=True)
        one_hot = jnp.where(entry == code.astype(jnp.int32), 1.0, 0.0).astype(BF16)
        book(level).wait()
        got = dot(one_hot, r.ring[level % slots].reshape(entries, code_width))
        r.chosen[level] = got.astype(BF16)
        r.ac_sum[...] += jnp.where(level > 0, got, 0.0)

        @pl.when(level + slots < levels)
        def _():
            book(level + slots).start()

        return carry

    def begin():
        for level in range(slots):
            book(level).start()

    def run():
        lax.fori_loop(0, levels, pick, 0, unroll=4)
        r.ac[...] = r.ac_sum[...].astype(BF16)

    return begin, run


def step_kernel(chunks, first_rows, bits, ins, outs, scratch):
    r = Refs({**ins, **outs, **scratch})
    t = r.t = Refs(r.t)
    r.att, r.g_rows, r.g_got, r.book_own = (r.ring.at[i] for i in range(4))
    r.ac_sum, r.code_cols = r.acc.at[:, : r.ac.shape[1]], r.gx.at[:, :PAIR]
    branch = lax.axis_index("branch")
    rows, width = r.tokens.shape
    levels, parts, entries, code_width = r.books.shape
    entries = entries * parts
    tiles = r.w_up_v.shape[1] // TILE
    pairs = width // PAIR
    if chunks:
        sums = Halving(chunks, bits, r.recv, r.packed, first_rows, r.send_sem, r.recv_sem)
        mine, level = sums.mine[bits - 2], lax.axis_index("dp") // 2
        wait_barrier = sums.barrier()
    moves = Moves(r.sem_move)
    begin_pick, run_pick = pick_codes(r)
    begin_pick()
    got_pout = [moves.start(r.pout_own.at[0], r.pout_v.at[branch])]
    frame_tables(r)
    if chunks:
        wait_barrier()
        sums.remote(r.pout_own.at[0], r.pout_v.at[branch], sums.partner[bits - 1], POUT)
    else:
        got_pout.append(moves.start(r.pout_other.at[0], r.pout_v.at[1 - branch]))
    got_rest = [
        moves.start(r.distill, r.distill_v),
        moves.start(r.wavlm.at[pl.ds(pl.multiple_of(branch * rows, rows), rows)], r.wavlm_v),
    ]
    got_attention = [moves.start(r.dec_qkv, r.w_qkv_v), moves.start(r.dec_out, r.w_out_v)]
    got_ffn = [moves.start(r.dec_up, r.w_up_v), moves.start(r.dec_down, r.w_down_v)]
    got_cotangent = [moves.start(r.cotangent, r.cotangent_v)]
    got_pin = [moves.start(r.pin_own.at[0], r.pin_v.at[branch])]
    if not chunks:
        got_pin.append(moves.start(r.pin_other.at[0], r.pin_v.at[1 - branch]))
    got_tokens = [moves.start(r.tokens, r.tokens_v)]
    got_attention_two = [moves.start(r.enc_qkv, r.w_qkv_e), moves.start(r.enc_out, r.w_out_e)]

    if chunks:
        down = dict(dec=[t.dd0, t.dd1], enc=[t.ed0, t.ed1, t.ed2])
        place = r.places = Refs(
            dec_up=[Place(t.du0), Place(t.du1)],
            dec_out=Place(t.da0),
            dec_qkv=[Place(t.da0, width), Place(t.da1), Place(t.da2)],
            enc_up=[Place(t.eu0), Place(t.eu1)],
            enc_out=Place(t.ea0),
            enc_qkv=[Place(t.ea1), Place(t.ea2), Place(t.ea3)],
            distill=Place(t.di),
            pout=Place(t.misc),
            pin=Place(t.misc, width),
        )
    else:
        down = dict(dec=[t.dec_down], enc=[t.enc_down])
        place = r.places = Refs(
            dec_up=[Place(t.dec_up, i * tiles // 2 * TILE) for i in range(2)],
            dec_out=Place(t.dec_out),
            dec_qkv=[Place(t.dec_qkv, i * width) for i in range(3)],
            enc_up=[Place(t.enc_up, i * tiles // 2 * TILE) for i in range(2)],
            enc_out=Place(t.enc_out),
            enc_qkv=[Place(t.enc_qkv, i * width) for i in range(3)],
            distill=Place(t.distill),
            pout=Place(t.pout),
            pin=Place(t.pin),
        )
    dec_down, enc_down = down["dec"], down["enc"]

    def wait(moves, other=None):
        for move in moves:
            move.wait()
        if chunks and other is not None:
            sums.arrived(other)

    def dec_gain(i):
        return r.vectors[1, i : i + 1, :]

    def enc_gain(i):
        return r.vectors[0, i : i + 1, :]

    def pick():
        run_pick()

    def semantic():
        wait(got_rest)
        quantizer_semantic(r)

    def quant():
        wait(got_pout, POUT)
        if chunks:
            sums.remote(r.pin_own.at[0], r.pin_v.at[branch], sums.partner[bits - 1], PIN)
        r.x[...] = dot(r.chosen[0], r.pout_v[0]) + dot(r.ac[...], r.pout_v[1])
        if chunks:
            for other in range(1, levels):
                target = sums.near_level(other)
                sums.remote(r.code_rows.at[target_level(target)], r.code_got.at[other], target, CODES, other)
            r.code_got[0] = r.code_rows[level]

    def target_level(target):
        return next(iter(target.values())) // 2

    def dec_project():
        wait(got_attention)
        attention_project(r, r.w_qkv_v, dec_gain)

    def dec_mix():
        attention_mix(r, r.w_out_v, dec_gain)

    def dec_ffn(half):
        def run():
            if half == 0:
                wait(got_ffn)
                wait(got_cotangent)
                ffn_backward_begin(r, dec_gain, r.cotangent_v)
            first, last = half * tiles // 2, (half + 1) * tiles // 2
            ffn_both(r, r.w_up_v, r.w_down_v, place.dec_up[half], dec_down, first, last)
            if half == 1:
                r.decoded[...] = (r.x2[...] + dec_gain(3) * r.fo[...]).astype(BF16)
                ffn_backward_end(r, dec_gain, r.cotangent_v, r.dec_gains)
                got_ffn[:] = [moves.start(r.enc_up, r.w_up_v), moves.start(r.enc_down, r.w_down_v)]

        return run

    def dec_out():
        attention_backward_out(r, r.w_out_v, dec_gain, place.dec_out, r.dec_gains)

    def attention_pairs(first, last):
        return lambda: attention_backward_pairs(r, first, last)

    def dec_in(part):
        def run():
            attention_backward_in(r, r.w_qkv_v, place.dec_qkv[part], part)
            if part == 2:
                attention_backward_end(r, dec_gain, r.dec_gains)
                r.gquant[...] = r.gx[...].astype(BF16)

        return run

    def enc_project():
        wait(got_tokens)
        r.x[...] = r.tokens_v[...].astype(F32)
        wait(got_attention_two)
        attention_project(r, r.w_qkv_e, enc_gain)

    def enc_mix():
        attention_mix(r, r.w_out_e, enc_gain)

    def enc_ffn():
        wait(got_ffn)
        ffn_forward(r, r.w_up_v, r.w_down_v)
        r.latent[...] = (r.x2[...] + enc_gain(3) * r.fo[...]).astype(BF16)

    def quantizer():
        wait(got_pin, PIN)
        quantizer_latent(r)
        if chunks:
            for other in reversed(range(1, levels)):
                target = sums.near_level(other)
                sums.arrived(CODES, other)
                sums.remote(r.g_rows.at[target_level(target)], r.g_got.at[other], target, BOOKS, 0, other)
            r.g_got[0] = r.g_rows[level]

    def book_half(core, put):
        quarter = entries // 4
        for side in range(2):
            r.book_sum[...] = jnp.zeros_like(r.book_sum)
            first = (core * 2 + side) * quarter

            def add(source, carry):
                one_hot = one_hot_rows(r.code_got[source, 0:1, :], first, quarter)
                r.book_sum[...] += dot(one_hot, r.g_got[source])
                return carry

            lax.fori_loop(0, levels, add, 0, unroll=4)
            put(side, r.book_sum[...])

    def finish_books(stage):
        blocks = entries // 4 // rows
        other_core, other_side = sums.partner[bits - 2], sums.partner[bits - 1]
        if stage == 0:
            for other in range(1, levels):
                sums.arrived(BOOKS, 0, other)

            def put(side, value):
                r.book_send[side] = value.astype(BF16)

            def keep(side, value):
                r.book_own[side * blocks : (side + 1) * blocks] = value.astype(BF16).reshape((blocks, rows, code_width))

            book_half(1 - mine, put)
            sums.remote(r.book_send, r.book_got, other_core, BOOKS, 1)
            book_half(mine, keep)
        elif stage == 1:
            sums.arrived(BOOKS, 1)
            for side in range(2):
                own = r.book_own[side * blocks : (side + 1) * blocks]
                r.book_got[side] = r.book_got[side] + own.reshape(r.book_got.shape[1:])
            sums.remote(r.book_got.at[1 - branch], r.book_last, other_side, BOOKS, 2)
        else:
            sums.arrived(BOOKS, 2)
            total = r.book_got[branch].astype(F32) + r.book_last[...].astype(F32)
            blocks = code_width // 128
            store_segment(r.packed, first_rows[BOOKS], Segment(BOOKS, 0, blocks, 0, blocks, 0, entries // 4), total)

    def all_books():
        parts = entries // TILE

        def one(step, carry):
            at = step // parts
            one_hot = one_hot_rows(r.code_rows[at, 0:1, :], step % parts * TILE, TILE)
            t.books[at, aligned(step % parts, TILE), :] = dot(one_hot, r.g_rows[at]).astype(BF16)
            return carry

        lax.fori_loop(0, levels * parts, one, 0)

    def enc_ffn_back(half):
        def run():
            first, last = half * tiles // 2, (half + 1) * tiles // 2
            if half == 0:
                ffn_backward_begin(r, enc_gain, r.gy)
            ffn_backward_tiles(r, r.w_up_v, r.w_down_v, place.enc_up[half], enc_down, first, last)
            if half == 1:
                ffn_backward_end(r, enc_gain, r.gy, r.gains)

        return run

    def enc_out():
        attention_backward_out(r, r.w_out_e, enc_gain, place.enc_out, r.gains)

    def enc_in(part):
        def run():
            attention_backward_in(r, r.w_qkv_e, place.enc_qkv[part], part)
            if part == 2:
                attention_backward_end(r, enc_gain, r.gains)
                r.grad_tokens[...] = r.gx[...]
                if chunks:
                    spread_gains()

        return run

    def spread_gains():
        lanes = pl.ds(width, 128)
        for layer, ref in enumerate((r.gains, r.dec_gains)):
            for row in range(4):
                for block in range(width // 128):
                    owner = (layer * 4 + row) * (width // 128) + block
                    where = tuple(owner // 2 ** (bits - 1 - i) % 2 for i in range(bits))
                    value = ref[row : row + 1, block * 128 : (block + 1) * 128]
                    rows_here = t.ea3.shape[bits]
                    t.ea3[where + (slice(None), lanes)] = jnp.broadcast_to(value, (rows_here, 128)).astype(BF16)

    work = [
        (6.5, pick, ()),
        (2.0, semantic, (DISTILL_GRAD,)),
        (0.7, quant, ()),
        (1.5, dec_project, ()),
        (2.5, dec_mix, ()),
        (2.6, dec_ffn(0), (DU0,)),
        (2.7, dec_ffn(1), (DD0, DD1, DU1)),
        (1.2, dec_out, ()),
        (1.6, attention_pairs(0, pairs // 2), ()),
        (1.6, attention_pairs(pairs // 2, pairs), ()),
        (0.6, dec_in(0), (DA0,)),
        (0.6, dec_in(1), (DA1,)),
        (0.8, dec_in(2), (DA2,)),
        (1.5, enc_project, ()),
        (2.5, enc_mix, ()),
        (2.2, enc_ffn, ()),
        (2.0, quantizer, (BOOKS, MISC)),
        (2.0, enc_ffn_back(0), (EU0,)),
        (2.0, enc_ffn_back(1), (EU1, ED0, ED1, ED2)),
        (1.2, enc_out, (EA0,)),
        (1.6, attention_pairs(0, pairs // 2), ()),
        (1.6, attention_pairs(pairs // 2, pairs), ()),
        (0.6, enc_in(0), (EA1,)),
        (0.6, enc_in(1), (EA2,)),
        (1.0, enc_in(2), (EA3,)),
    ]
    if not chunks:
        for _, run, _ in work:
            run()
            if run is quantizer:
                all_books()
        return
    actions = plan(chunks, work, bits, rows * code_width * 2)

    def finish(name, stage):
        if name == BOOKS:
            finish_books(stage)
        elif stage == 0:
            sums.finish(name, 0, sums.half(t[name], name, 0, mine))
        else:
            sums.finish(name, stage)

    for (_, run, made), acts in zip(work, actions):
        run()
        for name in made:
            if name != BOOKS:
                sums.send_half(name, 0, t[name])
        for name, stage in acts:
            finish(name, stage)
    for name, stage in actions[-1]:
        finish(name, stage)
    sums.drain()


POUT, PIN, CODES = 1, 2, 3
DISTILL_GRAD = "di"
DD0, DD1, DU0, DU1, DA0, DA1, DA2, MISC = "dd0", "dd1", "du0", "du1", "da0", "da1", "da2", "misc"
EU0, EU1, ED0, ED1, ED2 = "eu0", "eu1", "ed0", "ed1", "ed2"
EA0, EA1, EA2, EA3 = "ea0", "ea1", "ea2", "ea3"


def step(given, devices, with_sums):
    rows, width = given.tokens.shape
    ff = given.enc_up.shape[1]
    levels, entries, code_width = given.books.shape
    given.books = given.books.reshape(levels, -1, rows, code_width)
    bits = devices.bit_length() - 1
    vmem, hbm = pl.BlockSpec(memory_space=pltpu.VMEM), pl.BlockSpec(memory_space=pl.ANY)
    scratch = layer_scratch(rows, width, ff)
    scratch.update(
        w_qkv_e=pltpu.VMEM((width, 3 * width), BF16),
        w_out_e=pltpu.VMEM((width, width), BF16),
        cos=pltpu.VMEM((rows, PAIR), F32),
        sin=pltpu.VMEM((rows, PAIR), F32),
        bias=pltpu.VMEM((rows, rows), F32),
        ring=pltpu.VMEM((4,) + given.books.shape[1:], BF16),
        code_rows=pltpu.VMEM((levels, 8, rows), jnp.int32),
        chosen=pltpu.VMEM((levels, rows, code_width), BF16),
        ac=pltpu.VMEM((rows, code_width), BF16),
        gquant=pltpu.VMEM((rows, width), BF16),
        gy=pltpu.VMEM((rows, width), F32),
        latent=pltpu.VMEM((rows, width), BF16),
        pin_v=pltpu.VMEM((2, width, code_width), BF16),
        pout_v=pltpu.VMEM((2, code_width, width), BF16),
        distill_v=pltpu.VMEM(given.distill.shape, BF16),
        wavlm_v=pltpu.VMEM((rows, given.wavlm.shape[1]), BF16),
        tokens_v=pltpu.VMEM((rows, width), BF16),
        cotangent_v=pltpu.VMEM((rows, width), BF16),
        sem_move=pltpu.SemaphoreType.DMA((14,)),
        sem_book=pltpu.SemaphoreType.DMA((4,)),
    )
    outs = Refs(decoded=shaped((rows, width), BF16), grad_tokens=shaped((rows, width), F32))
    chunks, first_rows = {}, {}
    params = dict(vmem_limit_bytes=61 * 2**20)
    if with_sums:
        params.update(collective_id=0, has_side_effects=True)
        c, x, y = bits - 2, bits - 1, bits - 3
        b, a = range(y)
        share = width // devices
        low, high = ff // devices, share
        wide, half, blocks = ff // 128, ff // 256, width // 128
        third, quarter = 3 * blocks, blocks // 4
        chunks = dict(
            di=Chunk(
                high,
                width,
                [c, y, x, a, b],
                [
                    Segment(8, 0, 2 * blocks, 0, blocks, 0, high // 2),
                    Segment(8, blocks, 2 * blocks, 0, blocks, high // 2, high // 2),
                ],
            ),
            du0=Chunk(high, ff // 2, [c, y, a, x, b], [Segment(2, 0, wide, 0, half, 0, high)]),
            dd0=Chunk(low, width // 2, [c, a, y, b, x], [Segment(3, 0, blocks, 0, 2 * quarter, 0, low)]),
            dd1=Chunk(low, width // 2, [c, y, x, a, b], [Segment(3, 2 * quarter, blocks, 0, 2 * quarter, 0, low)]),
            du1=Chunk(high, ff // 2, [c, x, y, a, b], [Segment(2, half, wide, 0, half, 0, high)]),
            da0=Chunk(
                high,
                2 * width,
                [c, x, y, a, b],
                [Segment(1, 0, blocks, 0, blocks, 0, high), Segment(0, 0, third, width, blocks, 0, high)],
            ),
            da1=Chunk(high, width, [c, a, x, y, b], [Segment(0, blocks, third, 0, blocks, 0, high)]),
            da2=Chunk(high, width, [c, y, x, a, b], [Segment(0, 2 * blocks, third, 0, blocks, 0, high)]),
            misc=Chunk(
                high,
                2 * width,
                [c, x, y, a, b],
                [
                    Segment(9, 0, blocks, 0, blocks, 0, high),
                    Segment(10, 0, blocks // 2, width, blocks // 2, 0, high),
                    Segment(10, high * blocks // 2, blocks // 2, width + code_width, blocks // 2, 0, high),
                ],
            ),
            eu0=Chunk(high, ff // 2, [c, x, a, y, b], [Segment(6, 0, wide, 0, half, 0, high)]),
            eu1=Chunk(high, ff // 2, [c, x, y, a, b], [Segment(6, half, wide, 0, half, 0, high)]),
            ed0=Chunk(low, width // 2, [c, x, y, a, b], [Segment(7, 0, blocks, 0, 2 * quarter, 0, low)]),
            ed1=Chunk(low, width // 4, [c, y, x, a, b], [Segment(7, 2 * quarter, blocks, 0, quarter, 0, low)]),
            ed2=Chunk(low, width // 4, [c, y, a, b, x], [Segment(7, 3 * quarter, blocks, 0, quarter, 0, low)]),
            ea0=Chunk(high, width, [c, x, y, a, b], [Segment(5, 0, blocks, 0, blocks, 0, high)]),
            ea1=Chunk(high, width, [c, y, x, a, b], [Segment(4, 0, third, 0, blocks, 0, high)]),
            ea2=Chunk(high, width, [c, x, a, y, b], [Segment(4, blocks, third, 0, blocks, 0, high)]),
            ea3=Chunk(
                high,
                width + 128,
                [c, x, y, a, b],
                [Segment(4, 2 * blocks, third, 0, blocks, 0, high), Segment(11, 0, 1, width, 1, 0, 8)],
            ),
        )
        rows_of = [high * 3 * blocks, high * blocks, high * wide, low * blocks] * 2
        rows_of += [high * blocks, high * blocks, high * blocks, 8, entries // 4 * code_width // 128]
        first_rows = {i: sum(rows_of[:i]) for i in range(len(rows_of))}
        first_rows[BOOKS] = first_rows[len(rows_of) - 1]
        copies = len(chunks) * bits + 2 * levels + 2
        scratch.update(
            t={name: pltpu.VMEM(c.shape(bits), BF16) for name, c in chunks.items()},
            recv={
                name: [pltpu.VMEM(c.shape(bits - 1 - stage), BF16) for stage in range(bits)]
                for name, c in chunks.items()
            },
            gains=pltpu.VMEM((4, width), F32),
            dec_gains=pltpu.VMEM((4, width), F32),
            code_got=pltpu.VMEM((levels, 8, rows), jnp.int32),
                book_sum=pltpu.VMEM((entries // 4, code_width), F32),
            book_send=pltpu.VMEM((2, entries // 4, code_width), BF16),
            book_got=pltpu.VMEM((2, entries // 4, code_width), BF16),
            book_last=pltpu.VMEM((entries // 4, code_width), BF16),
            send_sem=pltpu.SemaphoreType.DMA((copies,)),
            recv_sem=pltpu.SemaphoreType.DMA((copies,)),
        )
        outs.packed = shaped((sum(rows_of), 128), F32)
    else:
        outs.update(gains=shaped((4, width), F32), dec_gains=shaped((4, width), F32))
        outs.t = dict(
            enc_qkv=shaped(given.enc_qkv.shape, BF16),
            enc_out=shaped(given.enc_out.shape, BF16),
            enc_up=shaped(given.enc_up.shape, BF16),
            enc_down=shaped(given.enc_down.shape, BF16),
            dec_qkv=shaped(given.enc_qkv.shape, BF16),
            dec_out=shaped(given.enc_out.shape, BF16),
            dec_up=shaped(given.enc_up.shape, BF16),
            dec_down=shaped(given.enc_down.shape, BF16),
            pin=shaped((2 * width, code_width), BF16),
            pout=shaped((2 * code_width, width), BF16),
            books=shaped((levels, entries, code_width), BF16),
            distill=shaped(given.distill.shape, BF16),
        )
    in_specs = dict.fromkeys(given, hbm)
    in_specs.update(
        lengths=pl.BlockSpec(memory_space=pltpu.SMEM), codes=vmem, vectors=vmem
    )
    got = pl.pallas_call(
        functools.partial(step_kernel, chunks, first_rows, bits),
        out_shape=dict(outs),
        in_specs=[in_specs],
        out_specs=jax.tree.map(lambda _: vmem, dict(outs)),
        scratch_shapes=[dict(scratch)],
        compiler_params=pltpu.CompilerParams(**params),
        name="step",
    )(dict(given))
    got = Refs(got)
    if not with_sums:
        return got
    last = [shaped((rows, 128), F32) for rows in rows_of]
    last[11] = shaped((1, 128), F32)

    def hand_on(packed, decoded, grad, *refs):
        outs, places, semaphores = refs[: len(last) + 2], refs[len(last) + 2 : -1], refs[-1]
        moves = Moves(semaphores)
        arriving = [moves.start(source, place) for source, place in zip((packed, decoded, grad), places)]
        arriving[0].wait()
        leaving = []
        for i, ref in enumerate(outs[:-2]):
            leaving.append(moves.start(places[0].at[pl.ds(first_rows[i], ref.shape[0])], ref))
        for move, place, ref in zip(arriving[1:], places[1:], outs[-2:]):
            move.wait()
            leaving.append(moves.start(place, ref))
        for move in leaving:
            move.wait()

    return pl.pallas_call(
        hand_on,
        out_shape=last + [outs.decoded, outs.grad_tokens],
        in_specs=[hbm] * 3,
        out_specs=[hbm] * (len(last) + 2),
        scratch_shapes=[
            pltpu.VMEM(got.packed.shape, F32),
            pltpu.VMEM(got.decoded.shape, BF16),
            pltpu.VMEM(got.grad_tokens.shape, F32),
            pltpu.SemaphoreType.DMA((len(last) + 5,)),
        ],
        compiler_params=pltpu.CompilerParams(vmem_limit_bytes=61 * 2**20),
        name="results",
    )(got.packed, got.decoded, got.grad_tokens)


def body(
    tokens,
    wavlm,
    cotangent,
    lengths,
    codes,
    enc_qkv,
    enc_out,
    enc_up,
    enc_down,
    dec_qkv,
    dec_out,
    dec_up,
    dec_down,
    vectors,
    proj_in,
    proj_out,
    codebooks,
    distill_proj,
):
    width = tokens.shape[1]
    devices = lax.axis_size("dp") * lax.axis_size("branch")
    with_sums = devices == 4 * codebooks.shape[0] and width // devices % 16 == 0
    given = Refs(
        tokens=tokens,
        wavlm=wavlm,
        cotangent=cotangent,
        lengths=lengths,
        codes=codes.T,
        enc_qkv=enc_qkv,
        enc_out=enc_out,
        enc_up=enc_up,
        enc_down=enc_down,
        dec_qkv=dec_qkv,
        dec_out=dec_out,
        dec_up=dec_up,
        dec_down=dec_down,
        vectors=vectors,
        pin_own=proj_in,
        pout_own=proj_out,
        books=codebooks,
        distill=distill_proj,
    )
    if with_sums:
        *sums, decoded, grad_tokens = step(given, devices, True)
        sums = [part.reshape(-1) for part in sums]
        order = (4, 5, 6, 7, 0, 1, 2, 3, 11, 10, 9, 12, 8)
        return (decoded, grad_tokens, *[sums[i] for i in order])
    swap = [(0, 1), (1, 0)]
    given.pin_other = lax.ppermute(proj_in, "branch", swap)
    given.pout_other = lax.ppermute(proj_out, "branch", swap)
    s = step(given, devices, False)
    t = Refs(s.t)
    gains = jnp.concatenate([s.gains, s.dec_gains])
    local = [t.enc_qkv, t.enc_out, t.enc_up, t.enc_down, t.dec_qkv, t.dec_out, t.dec_up, t.dec_down]
    local += [gains, t.pin, t.pout, t.books, t.distill]
    sums = [
        lax.psum_scatter(part.astype(F32).reshape(-1), ("dp", "branch"), scatter_dimension=0, tiled=True)
        for part in local
    ]
    return (s.decoded, s.grad_tokens, *sums)


def solution(mesh):
    rows, whole = P(("dp", "branch"), None), P()
    placed = (rows, P("dp", None), rows, rows, P("dp", None)) + (whole,) * 9
    placed += (P("branch", None, None),) * 2 + (whole,) * 2
    return jax.shard_map(
        body,
        mesh=mesh,
        in_specs=placed,
        out_specs=(rows, rows) + (P(("dp", "branch")),) * 13,
        check_vma=False,
    )
```

```python
import functools
import math

import jax
import jax.numpy as jnp
from jax import lax
from jax.experimental import pallas as pl
from jax.experimental.pallas import tpu as pltpu
from jax.sharding import PartitionSpec as P

HEADS = 8
WINDOW = 250
EPS_NORM = 1e-05
EPS_COS = 1e-06
BETA = 0.25
DISTILL = 10.0
ROPE_BASE = 10000.0

MESH = pl.DeviceIdType.MESH
F32 = jnp.float32
BF16 = jnp.bfloat16
TILE = 512
PAIR = 128


def dot(left, right):
    return lax.dot_general(left, right, (((1,), (0,)), ((), ())), preferred_element_type=F32)


def dot_t(left, right):
    return lax.dot_general(left, right, (((1,), (1,)), ((), ())), preferred_element_type=F32)


def t_dot(left, right):
    return lax.dot_general(left, right, (((0,), (0,)), ((), ())), preferred_element_type=F32)


def iota(shape, dim):
    return lax.broadcasted_iota(jnp.int32, shape, dim)


def aligned(index, size):
    return pl.ds(pl.multiple_of(index * size, size), size)


class Refs(dict):
    __getattr__ = dict.__getitem__
    __setattr__ = dict.__setitem__


class Moves:
    def __init__(self, semaphores):
        self.semaphores, self.count = semaphores, 0

    def start(self, source, target):
        move = pltpu.make_async_copy(source, target, self.semaphores.at[self.count])
        self.count += 1
        move.start()
        return move


def layer_scratch(rows, width, ff):
    return Refs(
        x=pltpu.VMEM((rows, width), F32),
        s1=pltpu.VMEM((rows, 1), F32),
        h=pltpu.VMEM((rows, width), BF16),
        h1t=pltpu.VMEM((width, rows), BF16),
        h2t=pltpu.VMEM((width, rows), BF16),
        rinv=pltpu.VMEM((rows, width), F32),
        qkv=pltpu.VMEM((rows, 3 * width), BF16),
        mix=pltpu.VMEM((rows, width), BF16),
        ao=pltpu.VMEM((rows, width), F32),
        x2=pltpu.VMEM((rows, width), F32),
        s2=pltpu.VMEM((rows, 1), F32),
        act=pltpu.VMEM((rows, ff), BF16),
        dg=pltpu.VMEM((rows, ff), BF16),
        fo=pltpu.VMEM((rows, width), F32),
        grad=pltpu.VMEM((rows, width), BF16),
        gx=pltpu.VMEM((rows, width), F32),
        acc=pltpu.VMEM((rows, width), F32),
        w_qkv_v=pltpu.VMEM((width, 3 * width), BF16),
        w_out_v=pltpu.VMEM((width, width), BF16),
        w_up_v=pltpu.VMEM((width, ff), BF16),
        w_down_v=pltpu.VMEM((ff, width), BF16),
    )


def shaped(shape, kind):
    return jax.ShapeDtypeStruct(shape, kind)


def frame_tables(r):
    rows = r.cos.shape[0]
    place = iota((rows, PAIR), 0)
    query, key = iota((rows, rows), 0), iota((rows, rows), 1)
    begin, begin_query = jnp.zeros_like(place), jnp.zeros_like(query)
    edge = 0
    for clip in range(r.lengths.shape[1] - 1):
        edge = edge + r.lengths[0, clip]
        begin = jnp.where(place >= edge, edge, begin)
        begin_query = jnp.where(query >= edge, edge, begin_query)
    allowed = (key >= begin_query) & (key <= query) & (query - key < WINDOW)
    r.bias[...] = jnp.where(allowed, 0.0, -1e30)
    lane = iota((rows, PAIR), 1)
    rate = jnp.exp((lane % 32).astype(F32) * (-math.log(ROPE_BASE) / 32))
    angle = (place - begin).astype(F32) * rate
    r.cos[...] = jnp.cos(angle)
    sine = jnp.sin(angle)
    r.sin[...] = jnp.where(lane % 64 < 32, -sine, sine)


def rotated(value, cosine, sine):
    lane = iota(value.shape, 1)
    swapped = jnp.where(lane % 64 < 32, pltpu.roll(value, PAIR - 32, 1), pltpu.roll(value, 32, 1))
    return value * cosine + swapped * sine


def head_masks(rows):
    low = iota((rows, PAIR), 1) < 64
    return (jnp.where(low, 1.0, 0.0).astype(BF16), jnp.where(low, 0.0, 1.0).astype(BF16))


def attention_project(r, w_qkv, gain):
    width = r.x.shape[1]
    x = r.x[...]
    s1 = lax.rsqrt(jnp.mean(x * x, axis=1, keepdims=True) + EPS_NORM)
    r.s1[...] = s1
    h = (x * s1 * gain(0)).astype(BF16)
    r.h[...] = h
    r.h1t[...] = h.T

    def project(part, carry):
        value = dot(r.h[...], w_qkv[:, aligned(part, width)])
        turn = jnp.where(part < 2, 1.0, 0.0)
        scale = jnp.where(part == 0, 0.125, 1.0)
        cosine = r.cos[...] * turn + (1.0 - turn)
        sine = r.sin[...] * turn
        for p in range(width // PAIR):
            low = rotated(value[:, p * PAIR : (p + 1) * PAIR], cosine, sine).astype(BF16)
            where = pl.ds(pl.multiple_of(part * width + p * PAIR, PAIR), PAIR)
            r.qkv[:, where] = (low.astype(F32) * scale).astype(BF16)
        return carry

    lax.fori_loop(0, 3, project, 0, unroll=True)


def attention_mix(r, w_out, gain):
    rows, width = r.x.shape
    masks = head_masks(rows)
    low = iota((rows, PAIR), 1) < 64

    def pair(p, carry):
        query = r.qkv[:, aligned(p, PAIR)]
        key = r.qkv[:, aligned(p + width // PAIR, PAIR)]
        value = r.qkv[:, aligned(p + 2 * (width // PAIR), PAIR)]
        outs = []
        for h in range(2):
            scores = dot_t(query * masks[h], key) + r.bias[...]
            weights = jnp.exp(scores - jnp.max(scores, axis=1, keepdims=True)).astype(BF16)
            r.att[2 * p + h] = weights
            outs.append(dot(weights, value * masks[h] + masks[1 - h]))
        inverse = 1.0 / pltpu.roll(jnp.where(low, outs[1], outs[0]), 64, 1)
        r.rinv[:, aligned(p, PAIR)] = inverse
        r.mix[:, aligned(p, PAIR)] = (jnp.where(low, outs[0], outs[1]) * inverse).astype(BF16)
        return carry

    lax.fori_loop(0, width // PAIR, pair, 0, unroll=True)
    ao = dot(r.mix[...], w_out[...])
    r.ao[...] = ao
    x2 = r.x[...] + gain(1) * ao
    r.x2[...] = x2
    s2 = lax.rsqrt(jnp.mean(x2 * x2, axis=1, keepdims=True) + EPS_NORM)
    r.s2[...] = s2
    h = (x2 * s2 * gain(2)).astype(BF16)
    r.h[...] = h
    r.h2t[...] = h.T


def gelu_parts(pre):
    slope = math.sqrt(2.0 / math.pi)
    square = pre * pre
    bent = jnp.tanh(slope * pre * (1.0 + 0.044715 * square))
    half = 0.5 * (1.0 + bent)
    turn = 0.5 * pre * (1.0 - bent * bent) * slope * (1.0 + 3.0 * 0.044715 * square)
    return (pre * half).astype(BF16), half + turn


def ffn_forward(r, w_up, w_down):
    r.fo[...] = jnp.zeros_like(r.fo)

    def tile(t, carry):
        cols = aligned(t, TILE)
        act, slope = gelu_parts(dot(r.h[...], w_up[:, cols]))
        r.act[:, cols] = act
        r.dg[:, cols] = slope.astype(BF16)
        r.fo[...] += dot(act, w_down[cols, :])
        return carry

    lax.fori_loop(0, w_up.shape[1] // TILE, tile, 0, unroll=True)


def ffn_both(r, w_up, w_down, grad_up, grad_down, t):
    cols = pl.ds(t * TILE, TILE)
    act, slope = gelu_parts(dot(r.h[...], w_up[:, cols]))
    grad_pre = (dot_t(r.grad[...], w_down[cols, :]) * slope).astype(BF16)
    grad_up.put(dot(r.h2t[...], grad_pre))
    put_rows(grad_down, t_dot(act, r.grad[...]), t)
    out, back = dot(act, w_down[cols, :]), dot_t(grad_pre, w_up[:, cols])
    r.fo[...] = out if t == 0 else r.fo[...] + out
    r.acc[...] = back if t == 0 else r.acc[...] + back


def norm_back(stream, inverse, grad):
    mean = jnp.mean(grad * stream, axis=1, keepdims=True)
    return inverse * grad - stream * (inverse * inverse * inverse * mean)


def column_sum(value):
    return jnp.sum(value, axis=0, keepdims=True)


class Place:
    def __init__(self, ref, col=0):
        self.ref, self.col = ref, col

    def shift(self, by):
        return Place(self.ref, self.col + by)

    def put(self, value):
        shape = self.ref.shape
        value = value.astype(self.ref.dtype).reshape(shape[:-1] + (value.shape[1],))
        self.ref[(slice(None),) * (len(shape) - 1) + (pl.ds(self.col, value.shape[-1]),)] = value


def put_rows(targets, value, tile):
    value = value.astype(BF16)
    begin = 0
    for target in targets:
        shape = target.shape
        part = value[:, begin : begin + shape[-1]]
        begin += shape[-1]
        if len(shape) == 2:
            target[aligned(tile, value.shape[0]), :] = part
        else:
            target[tile // 2, tile % 2] = part.reshape(shape[2:])


def ffn_backward_begin(r, gain, gy_ref):
    r.grad[...] = (gain(3) * gy_ref[...].astype(F32)).astype(BF16)


def ffn_backward_tile(r, w_up, w_down, grad_up, grad_down, t):
    cols = pl.ds(t * TILE, TILE)
    put_rows(grad_down, t_dot(r.act[:, cols], r.grad[...]), t)
    grad_pre = (dot_t(r.grad[...], w_down[cols, :]) * r.dg[:, cols].astype(F32)).astype(BF16)
    grad_up.put(dot(r.h2t[...], grad_pre))
    back = dot_t(grad_pre, w_up[:, cols])
    r.acc[...] = back if t == 0 else r.acc[...] + back


def ffn_backward_end(r, gain, gy_ref, gain_out):
    gy = gy_ref[...].astype(F32)
    gain_out[3:4, :] = column_sum(gy * r.fo[...])
    back = r.acc[...]
    x2, s2 = r.x2[...], r.s2[...]
    gain_out[2:3, :] = column_sum(back * x2 * s2)
    r.gx[...] = gy + norm_back(x2, s2, back * gain(2))


def attention_backward_out(r, w_out, gain, grad_out, gain_out):
    gx = r.gx[...]
    gain_out[1:2, :] = column_sum(gx * r.ao[...])
    grad_attn = (gain(1) * gx).astype(BF16)
    grad_out.put(t_dot(r.mix[...], grad_attn))
    r.grad[...] = dot_t(grad_attn, w_out[...]).astype(BF16)


def attention_backward_pairs(r, first, last):
    rows, width = r.x.shape
    masks = head_masks(rows)
    masks_t = [jnp.where((iota((PAIR, rows), 0) < 64) == (h == 0), 1.0, 0.0).astype(BF16) for h in range(2)]
    pairs = width // PAIR

    def pair(p, carry):
        query = r.qkv[:, aligned(p, PAIR)]
        key = r.qkv[:, aligned(p + pairs, PAIR)]
        value = r.qkv[:, aligned(p + 2 * pairs, PAIR)]
        grad_mixed = (r.grad[:, aligned(p, PAIR)].astype(F32) * r.rinv[:, aligned(p, PAIR)]).astype(BF16)
        product = (grad_mixed.astype(F32) * r.mix[:, aligned(p, PAIR)].astype(F32)).astype(BF16)
        beside = jnp.concatenate([value, jnp.full(value.shape, -1.0, BF16)], axis=1)
        query_t, grad_t = query.T, grad_mixed.T
        to_query = to_key = to_value = 0.0
        for h in range(2):
            weights = r.att[2 * p + h]
            change = dot_t(jnp.concatenate([grad_mixed * masks[h], product * masks[h]], axis=1), beside)
            scores = (weights.astype(F32) * change).astype(BF16)
            to_query = to_query + dot(scores, key * masks[h])
            to_key = to_key + dot(query_t * masks_t[h], scores)
            to_value = to_value + dot(grad_t * masks_t[h], weights)
        cosine, sine = r.cos[...], -r.sin[...]
        r.qkv[:, aligned(p, PAIR)] = rotated(to_query * 0.125, cosine, sine).astype(BF16)
        r.qkv[:, aligned(p + pairs, PAIR)] = rotated(to_key.T, cosine, sine).astype(BF16)
        r.qkv[:, aligned(p + 2 * pairs, PAIR)] = to_value.T.astype(BF16)
        return carry

    lax.fori_loop(first, last, pair, 0, unroll=True)


def attention_backward_in(r, w_qkv, grad_qkv, part):
    width = r.x.shape[1]
    grad = r.qkv[:, part * width : (part + 1) * width]
    grad_qkv.put(dot(r.h1t[...], grad))
    back = dot_t(grad, w_qkv[:, part * width : (part + 1) * width])
    r.acc[...] = back if part == 0 else r.acc[...] + back


def attention_backward_end(r, gain, gain_out):
    back = r.acc[...]
    x, s1 = r.x[...], r.s1[...]
    gain_out[0:1, :] = column_sum(back * x * s1)
    r.gx[...] = r.gx[...] + norm_back(x, s1, back * gain(0))


class Segment:
    def __init__(self, result, base, stride, col, blocks, row, rows):
        self.result, self.base, self.stride, self.col, self.blocks = result, base, stride, col, blocks
        self.row, self.rows = row, rows


class Chunk:
    def __init__(self, rows, columns, order, segments):
        self.rows, self.columns, self.order, self.segments = rows, columns, order, segments

    def shape(self, leading):
        return (2,) * leading + (self.rows, self.columns)

    def bytes(self, bits):
        return 2**bits * self.rows * self.columns * 2


def plan(chunks, work, bits, book_bytes):
    core, x, y = bits - 2, bits - 1, bits - 3
    ends, middle = -1, -2
    free, pending, done = {}, [], []
    now = 0.0

    def carry(link, size, rate=42e3):
        free[link] = max(now, free.get(link, 0.0)) + size / rate
        return free[link]

    def begin(name, stage):
        if name == BOOKS:
            size = 1.2 * 2 ** (bits - 3) * book_bytes
            if stage == 0:
                there = max(carry(y, size), carry(ends, 1.5 * size), carry(middle, 2 * size))
            else:
                there = carry(core, 4 * book_bytes, 400e3) if stage == 1 else carry(x, 2 * book_bytes)
        else:
            dim = chunks[name].order[stage]
            size = chunks[name].bytes(bits) / 2 ** (stage + 1)
            if dim == core:
                there = carry(core, size, 400e3)
            elif dim == x or dim == y:
                there = carry(dim, size)
            else:
                there = carry(ends, size)
                if dim < y - 1:
                    there = max(there, carry(middle, 2 * size))
        pending.append((there + 1.5, name, stage))

    def finish(limit):
        nonlocal now
        acts = []
        while pending:
            pending.sort(key=lambda p: p[0])
            if pending[0][0] + (0.3 if limit < math.inf else 0.0) > limit:
                break
            at, name, stage = pending.pop(0)
            if name == BOOKS:
                cost = (6.0, 0.6, 0.3)[stage]
            else:
                cost = 0.25 + 0.3e-6 * chunks[name].bytes(bits) / 2 ** (stage + 1)
            now = max(now, at) + cost
            limit = max(limit, now)
            acts.append((name, stage))
            if stage + 1 < (3 if name == BOOKS else bits):
                begin(name, stage + 1)
        return acts

    for took, _, names in work:
        now += 0.95 * took
        for name in names:
            begin(name, 0)
        done.append(finish(now))
    done.append(finish(math.inf))
    return done


def coordinates(step, count):
    return [step // 2 ** (count - 1 - i) % 2 for i in range(count)]


def store_segment(packed, first, segment, value):
    for i in range(segment.blocks):
        where = pl.ds(first + segment.base + i, segment.rows, stride=segment.stride)
        packed[where, :] = value[
            segment.row : segment.row + segment.rows, segment.col + i * 128 : segment.col + (i + 1) * 128
        ]


class Halving:
    def __init__(self, chunks, bits, recv, packed, first, send_sem, recv_sem):
        self.chunks = chunks
        self.bits, self.recv, self.packed, self.first = bits, recv, packed, first
        self.send_sem, self.recv_sem = send_sem, recv_sem
        self.copies = {}
        dp, branch = lax.axis_index("dp"), lax.axis_index("branch")
        self.mine, self.partner = [], []
        for dim in range(bits - 1):
            weight = 2 ** (bits - 2 - dim)
            bit = dp // weight % 2
            self.mine.append(bit)
            self.partner.append({"dp": dp + weight * (1 - 2 * bit), "branch": branch})
        self.mine.append(branch)
        self.partner.append({"dp": dp, "branch": 1 - branch})

    def near_level(self, other):
        dp = lax.axis_index("dp")
        for i in range(self.bits - 2):
            if other >> i & 1:
                dp = dp + 2 ** (i + 1) * (1 - 2 * self.mine[self.bits - 3 - i])
        return {"dp": dp, "branch": lax.axis_index("branch")}

    def barrier(self):
        semaphore = pltpu.get_barrier_semaphore()
        levels = 2 ** (self.bits - 2)
        targets = self.partner[self.bits - 2 :] + [self.near_level(other) for other in range(1, levels)]
        for target in targets:
            pl.semaphore_signal(semaphore, inc=1, device_id=target, device_id_type=MESH)
        return lambda: pl.semaphore_wait(semaphore, len(targets))

    def left(self, name, stage):
        return [d for d in range(self.bits) if d not in self.chunks[name].order[:stage]]

    def half(self, ref, name, stage, index):
        position = self.left(name, stage).index(self.chunks[name].order[stage])
        return ref.at[(slice(None),) * position + (index,)]

    def remote(self, source, target, device, *key):
        slot = len(self.copies)
        self.copies[key] = pltpu.make_async_remote_copy(
            src_ref=source,
            dst_ref=target,
            send_sem=self.send_sem.at[slot],
            recv_sem=self.recv_sem.at[slot],
            device_id=device,
            device_id_type=MESH,
        )
        self.copies[key].start()

    def send(self, name, stage, source):
        dim = self.chunks[name].order[stage]
        self.remote(source, self.recv[name][stage], self.partner[dim], name, stage)

    def send_half(self, name, stage, ref):
        dim = self.chunks[name].order[stage]
        self.send(name, stage, self.half(ref, name, stage, 1 - self.mine[dim]))

    def arrived(self, *key):
        self.copies[key].wait_recv()

    def add(self, name, stage, own):
        chunk = self.chunks[name]
        got = self.recv[name][stage]
        depth = self.bits - 1 - stage
        if stage == self.bits - 1:
            value = own[...].astype(F32) + got[...].astype(F32)
            for segment in chunk.segments:
                store_segment(self.packed, self.first[segment.result], segment, value)
            return

        outer = max(depth - 2, 0)

        def step(i, carry):
            where = tuple(coordinates(i, outer))
            got[where] = got[where] + own[where]
            return carry

        lax.fori_loop(0, 2**outer, step, 0)

    def finish(self, name, stage, own=None):
        chunk = self.chunks[name]
        self.arrived(name, stage)
        if own is None:
            dim = chunk.order[stage]
            own = self.half(self.recv[name][stage - 1], name, stage, self.mine[dim])
        self.add(name, stage, own)
        self.follow(name, stage)

    def follow(self, name, stage):
        if stage + 1 < self.bits:
            self.send_half(name, stage + 1, self.recv[name][stage])

    def drain(self):
        for copy in self.copies.values():
            copy.wait_send()


BOOKS = "books"


def quantizer_semantic(r):
    sem_code = r.chosen[0]
    prediction = dot(sem_code, r.distill_v[...])
    target = r.wavlm_v[...].astype(F32)
    pred_norm = lax.rsqrt(jnp.sum(prediction * prediction, axis=1, keepdims=True) + EPS_COS)
    target_norm = lax.rsqrt(jnp.sum(target * target, axis=1, keepdims=True) + EPS_COS)
    cosine = jnp.sum(prediction * target, axis=1, keepdims=True) * (pred_norm * target_norm)
    grad_pred = (
        target * (-DISTILL * pred_norm * target_norm) + prediction * (DISTILL * cosine * pred_norm * pred_norm)
    ).astype(BF16)
    put_distill(r.places.distill, dot(sem_code.T, grad_pred))
    r.gy[:, : sem_code.shape[1]] = dot_t(grad_pred, r.distill_v[...])


def quantizer_latent(r):
    levels = r.chosen.shape[0]
    latent = r.latent[...]
    sem_code, ac_code = r.chosen[0], r.ac[...]
    gquant = r.gquant[...]
    latent_t = latent.T
    grad_sem = dot_t(gquant, r.pout_v[0]) + r.gy[:, : sem_code.shape[1]]
    put_group(r.places.pout, 0, dot(sem_code.T, gquant))
    put_group(r.places.pout, 1, t_dot(ac_code, gquant))
    commit = 2.0 * BETA * (dot(latent, r.pin_v[0]) - sem_code.astype(F32))
    r.g_rows[0] = (grad_sem - commit).astype(BF16)
    to_sem = (grad_sem + commit).astype(BF16)

    grad_ac = dot_t(gquant, r.pout_v[1])
    residual = dot(latent, r.pin_v[1])
    for level in range(1, levels):
        residual = residual - r.chosen[level].astype(F32)
    carry = jnp.zeros_like(residual)
    for level in range(levels - 1, 0, -1):
        carry = carry + 2.0 * BETA * residual
        r.g_rows[level] = (grad_ac - carry).astype(BF16)
        residual = residual + r.chosen[level].astype(F32)
    to_ac = (grad_ac + carry).astype(BF16)
    put_group(r.places.pin, 0, dot(latent_t, to_sem))
    put_group(r.places.pin, 1, dot(latent_t, to_ac))
    r.gy[...] = dot_t(to_sem, r.pin_v[0]) + dot_t(to_ac, r.pin_v[1])


def put_group(place, group, value):
    target, rows = place.ref, value.shape[0]
    value = value.astype(target.dtype)
    if len(target.shape) == 2:
        target[group * rows : (group + 1) * rows, :] = value
        return
    lead, height = target.shape[1:-2], target.shape[-2]
    value = value.reshape(math.prod(lead), -1, height, value.shape[1])
    value = jnp.concatenate([value[:, i] for i in range(value.shape[1])], axis=2)
    columns = value.shape[2]
    where = (group,) + (slice(None),) * (len(lead) + 1) + (pl.ds(place.col, columns),)
    target[where] = value.reshape(lead + (height, columns))


def put_distill(place, value):
    target = place.ref
    if len(target.shape) == 2:
        target[...] = value.astype(target.dtype)
        return
    height = target.shape[-2]
    value = value.reshape(math.prod(target.shape[:-2]), -1, value.shape[1])
    columns = value.shape[2] * value.shape[1] // height
    value = jnp.concatenate([value[:, :, i : i + columns] for i in range(0, value.shape[2], columns)], axis=1)
    where = (slice(None),) * (len(target.shape) - 1) + (pl.ds(place.col, columns),)
    target[where] = value.astype(target.dtype).reshape(target.shape[:-1] + (columns,))


def one_hot_rows(codes, first, count):
    row = iota((count, codes.shape[1]), 0)
    return jnp.where(codes - first == row, 1.0, 0.0).astype(BF16)


def pick_codes(r):
    levels, _, entries, code_width = r.books.shape
    entries = entries * r.books.shape[1]
    rows = r.cos.shape[0]
    slots = r.ring.shape[0]
    branch = lax.axis_index("branch")
    own = r.codes[:, pl.ds(pl.multiple_of(branch * rows, rows), rows)]
    r.code_rows[...] = jnp.broadcast_to(own[:, None, :], r.code_rows.shape)
    columns = jnp.concatenate([own.astype(F32), jnp.zeros((PAIR - levels, rows), F32)], axis=0).T
    lane = iota(columns.shape, 1)
    entry = iota((rows, entries), 1)
    r.code_cols[...] = columns
    r.ac_sum[...] = jnp.zeros(r.ac_sum.shape, F32)

    def book(level):
        slot = level % slots
        return pltpu.make_async_copy(r.books.at[level], r.ring.at[slot], r.sem_book.at[slot])

    def pick(level, carry):
        code = jnp.sum(jnp.where(lane == level, r.code_cols[...], 0.0), axis=1, keepdims=True)
        one_hot = jnp.where(entry == code.astype(jnp.int32), 1.0, 0.0).astype(BF16)
        book(level).wait()
        got = dot(one_hot, r.ring[level % slots].reshape(entries, code_width))
        r.chosen[level] = got.astype(BF16)
        r.ac_sum[...] += jnp.where(level > 0, got, 0.0)

        @pl.when(level + slots < levels)
        def _():
            book(level + slots).start()

        return carry

    def begin():
        for level in range(slots):
            book(level).start()

    def run():
        lax.fori_loop(0, levels, pick, 0, unroll=4)
        r.ac[...] = r.ac_sum[...].astype(BF16)

    return begin, run


def step_kernel(chunks, first_rows, bits, ins, outs, scratch):
    r = Refs({**ins, **outs, **scratch})
    t = r.t = Refs(r.t)
    r.att, r.g_rows, r.g_got, r.book_own = (r.ring.at[i] for i in range(4))
    r.ac_sum, r.code_cols = r.acc.at[:, : r.ac.shape[1]], r.gx.at[:, :PAIR]
    branch = lax.axis_index("branch")
    rows, width = r.tokens.shape
    levels, parts, entries, code_width = r.books.shape
    entries = entries * parts
    tiles = r.w_up_v.shape[1] // TILE
    pairs = width // PAIR
    if chunks:
        sums = Halving(chunks, bits, r.recv, r.packed, first_rows, r.send_sem, r.recv_sem)
        mine, level = sums.mine[bits - 2], lax.axis_index("dp") // 2
        wait_barrier = sums.barrier()
    moves = Moves(r.sem_move)
    begin_pick, run_pick = pick_codes(r)
    begin_pick()
    got_pout = [moves.start(r.pout_own.at[0], r.pout_v.at[branch])]
    frame_tables(r)
    if chunks:
        wait_barrier()
        sums.remote(r.pout_own.at[0], r.pout_v.at[branch], sums.partner[bits - 1], POUT)
    else:
        got_pout.append(moves.start(r.pout_other.at[0], r.pout_v.at[1 - branch]))
    got_rest = [
        moves.start(r.distill, r.distill_v),
        moves.start(r.wavlm.at[pl.ds(pl.multiple_of(branch * rows, rows), rows)], r.wavlm_v),
    ]
    got_attention = [moves.start(r.dec_qkv, r.w_qkv_v), moves.start(r.dec_out, r.w_out_v)]
    got_ffn = [moves.start(r.dec_up, r.w_up_v), moves.start(r.dec_down, r.w_down_v)]
    got_cotangent = [moves.start(r.cotangent, r.cotangent_v)]
    got_pin = [moves.start(r.pin_own.at[0], r.pin_v.at[branch])]
    if not chunks:
        got_pin.append(moves.start(r.pin_other.at[0], r.pin_v.at[1 - branch]))
    got_tokens = [moves.start(r.tokens, r.tokens_v)]
    got_attention_two = [moves.start(r.enc_qkv, r.w_qkv_e), moves.start(r.enc_out, r.w_out_e)]

    if chunks:
        down = dict(dec=[t.dd0, t.dd1], enc=[t.ed0, t.ed1])
        place = r.places = Refs(
            dec_up=[Place(t.du0), Place(t.du1), Place(t.du2), Place(t.du2, TILE)],
            dec_out=Place(t.da0),
            dec_qkv=[Place(t.da0, width), Place(t.da1), Place(t.da1, width)],
            enc_up=[Place(t.eu0), Place(t.eu0, TILE), Place(t.eu1), Place(t.eu1, TILE)],
            enc_out=Place(t.ea0),
            enc_qkv=[Place(t.ea0, width), Place(t.ea1), Place(t.ea2)],
            distill=Place(t.di),
            pout=Place(t.misc),
            pin=Place(t.misc, width),
        )
    else:
        down = dict(dec=[t.dec_down], enc=[t.enc_down])
        place = r.places = Refs(
            dec_up=[Place(t.dec_up, i * TILE) for i in range(tiles)],
            dec_out=Place(t.dec_out),
            dec_qkv=[Place(t.dec_qkv, i * width) for i in range(3)],
            enc_up=[Place(t.enc_up, i * TILE) for i in range(tiles)],
            enc_out=Place(t.enc_out),
            enc_qkv=[Place(t.enc_qkv, i * width) for i in range(3)],
            distill=Place(t.distill),
            pout=Place(t.pout),
            pin=Place(t.pin),
        )
    dec_down, enc_down = down["dec"], down["enc"]

    def wait(moves, other=None):
        for move in moves:
            move.wait()
        if chunks and other is not None:
            sums.arrived(other)

    def dec_gain(i):
        return r.vectors[1, i : i + 1, :]

    def enc_gain(i):
        return r.vectors[0, i : i + 1, :]

    def pick():
        run_pick()

    def semantic():
        wait(got_rest)
        quantizer_semantic(r)

    def quant():
        wait(got_pout, POUT)
        if chunks:
            sums.remote(r.pin_own.at[0], r.pin_v.at[branch], sums.partner[bits - 1], PIN)
        r.x[...] = dot(r.chosen[0], r.pout_v[0]) + dot(r.ac[...], r.pout_v[1])
        if chunks:
            for other in range(1, levels):
                target = sums.near_level(other)
                sums.remote(r.code_rows.at[target_level(target)], r.code_got.at[other], target, CODES, other)
            r.code_got[0] = r.code_rows[level]

    def target_level(target):
        return next(iter(target.values())) // 2

    def dec_project():
        wait(got_attention)
        attention_project(r, r.w_qkv_v, dec_gain)

    def dec_mix():
        attention_mix(r, r.w_out_v, dec_gain)

    def dec_ffn(tile):
        def run():
            if tile == 0:
                wait(got_ffn)
                wait(got_cotangent)
                ffn_backward_begin(r, dec_gain, r.cotangent_v)
            ffn_both(r, r.w_up_v, r.w_down_v, place.dec_up[tile], dec_down, tile)
            if tile == tiles - 1:
                r.decoded[...] = (r.x2[...] + dec_gain(3) * r.fo[...]).astype(BF16)
                ffn_backward_end(r, dec_gain, r.cotangent_v, r.dec_gains)
                got_ffn[:] = [moves.start(r.enc_up, r.w_up_v), moves.start(r.enc_down, r.w_down_v)]

        return run

    def dec_out():
        attention_backward_out(r, r.w_out_v, dec_gain, place.dec_out, r.dec_gains)

    def attention_pair(pair):
        return lambda: attention_backward_pairs(r, pair, pair + 1)

    def dec_in(part):
        def run():
            attention_backward_in(r, r.w_qkv_v, place.dec_qkv[part], part)
            if part == 2:
                attention_backward_end(r, dec_gain, r.dec_gains)
                r.gquant[...] = r.gx[...].astype(BF16)

        return run

    def enc_project():
        wait(got_tokens)
        r.x[...] = r.tokens_v[...].astype(F32)
        wait(got_attention_two)
        attention_project(r, r.w_qkv_e, enc_gain)

    def enc_mix():
        attention_mix(r, r.w_out_e, enc_gain)

    def enc_ffn():
        wait(got_ffn)
        ffn_forward(r, r.w_up_v, r.w_down_v)
        r.latent[...] = (r.x2[...] + enc_gain(3) * r.fo[...]).astype(BF16)

    def quantizer():
        wait(got_pin, PIN)
        quantizer_latent(r)
        if chunks:
            for other in reversed(range(1, levels)):
                target = sums.near_level(other)
                sums.arrived(CODES, other)
                sums.remote(r.g_rows.at[target_level(target)], r.g_got.at[other], target, BOOKS, 0, other)
            r.g_got[0] = r.g_rows[level]

    def book_half(core, put):
        quarter = entries // 4
        for side in range(2):
            r.book_sum[...] = jnp.zeros_like(r.book_sum)
            first = (core * 2 + side) * quarter

            def add(source, carry):
                one_hot = one_hot_rows(r.code_got[source, 0:1, :], first, quarter)
                r.book_sum[...] += dot(one_hot, r.g_got[source])
                return carry

            lax.fori_loop(0, levels, add, 0, unroll=4)
            put(side, r.book_sum[...])

    def finish_books(stage):
        blocks = entries // 4 // rows
        other_core, other_side = sums.partner[bits - 2], sums.partner[bits - 1]
        if stage == 0:
            for other in range(1, levels):
                sums.arrived(BOOKS, 0, other)

            def put(side, value):
                r.book_send[side] = value.astype(BF16)

            def keep(side, value):
                r.book_own[side * blocks : (side + 1) * blocks] = value.astype(BF16).reshape((blocks, rows, code_width))

            book_half(1 - mine, put)
            sums.remote(r.book_send, r.book_got, other_core, BOOKS, 1)
            book_half(mine, keep)
        elif stage == 1:
            sums.arrived(BOOKS, 1)
            for side in range(2):
                own = r.book_own[side * blocks : (side + 1) * blocks]
                r.book_got[side] = r.book_got[side] + own.reshape(r.book_got.shape[1:])
            sums.remote(r.book_got.at[1 - branch], r.book_last, other_side, BOOKS, 2)
        else:
            sums.arrived(BOOKS, 2)
            total = r.book_got[branch].astype(F32) + r.book_last[...].astype(F32)
            blocks = code_width // 128
            store_segment(r.packed, first_rows[BOOKS], Segment(BOOKS, 0, blocks, 0, blocks, 0, entries // 4), total)

    def all_books():
        parts = entries // TILE

        def one(step, carry):
            at = step // parts
            one_hot = one_hot_rows(r.code_rows[at, 0:1, :], step % parts * TILE, TILE)
            t.books[at, aligned(step % parts, TILE), :] = dot(one_hot, r.g_rows[at]).astype(BF16)
            return carry

        lax.fori_loop(0, levels * parts, one, 0)

    def enc_ffn_back(tile):
        def run():
            if tile == 0:
                ffn_backward_begin(r, enc_gain, r.gy)
            ffn_backward_tile(r, r.w_up_v, r.w_down_v, place.enc_up[tile], enc_down, tile)
            if tile == tiles - 1:
                ffn_backward_end(r, enc_gain, r.gy, r.gains)

        return run

    def enc_out():
        attention_backward_out(r, r.w_out_e, enc_gain, place.enc_out, r.gains)

    def enc_in(part):
        def run():
            attention_backward_in(r, r.w_qkv_e, place.enc_qkv[part], part)
            if part == 2:
                attention_backward_end(r, enc_gain, r.gains)
                r.grad_tokens[...] = r.gx[...]
                if chunks:
                    spread_gains()

        return run

    def spread_gains():
        lanes = pl.ds(width, 128)
        for layer, ref in enumerate((r.gains, r.dec_gains)):
            for row in range(4):
                for block in range(width // 128):
                    owner = (layer * 4 + row) * (width // 128) + block
                    where = tuple(owner // 2 ** (bits - 1 - i) % 2 for i in range(bits))
                    value = ref[row : row + 1, block * 128 : (block + 1) * 128]
                    rows_here = t.ea2.shape[bits]
                    t.ea2[where + (slice(None), lanes)] = jnp.broadcast_to(value, (rows_here, 128)).astype(BF16)

    def pairs_of(seconds):
        return [(seconds, attention_pair(p), ()) for p in range(pairs)]

    work = [
        (6.5, pick, ()),
        (2.0, semantic, (DISTILL_GRAD,)),
        (0.7, quant, ()),
        (1.5, dec_project, ()),
        (2.5, dec_mix, ()),
        (1.3, dec_ffn(0), (DU0,)),
        (1.3, dec_ffn(1), (DU1,)),
        (1.3, dec_ffn(2), ()),
        (1.3, dec_ffn(3), (DD0, DD1, DU2)),
        (1.2, dec_out, ()),
        *pairs_of(0.8),
        (0.6, dec_in(0), (DA0,)),
        (0.6, dec_in(1), ()),
        (0.8, dec_in(2), (DA1,)),
        (1.5, enc_project, ()),
        (2.5, enc_mix, ()),
        (2.2, enc_ffn, ()),
        (2.0, quantizer, (BOOKS, MISC)),
        (1.0, enc_ffn_back(0), ()),
        (1.0, enc_ffn_back(1), (EU0,)),
        (1.0, enc_ffn_back(2), ()),
        (1.0, enc_ffn_back(3), (EU1, ED0, ED1)),
        (1.2, enc_out, ()),
        *pairs_of(0.8),
        (0.6, enc_in(0), (EA0,)),
        (0.6, enc_in(1), (EA1,)),
        (1.0, enc_in(2), (EA2,)),
    ]
    if not chunks:
        for _, run, _ in work:
            run()
            if run is quantizer:
                all_books()
        return
    actions = plan(chunks, work, bits, rows * code_width * 2)

    def finish(name, stage):
        if name == BOOKS:
            finish_books(stage)
        elif stage == 0:
            sums.finish(name, 0, sums.half(t[name], name, 0, mine))
        else:
            sums.finish(name, stage)

    for (_, run, made), acts in zip(work, actions):
        run()
        for name in made:
            if name != BOOKS:
                sums.send_half(name, 0, t[name])
        for name, stage in acts:
            finish(name, stage)
    for name, stage in actions[-1]:
        finish(name, stage)
    sums.drain()


POUT, PIN, CODES = 1, 2, 3
DISTILL_GRAD = "di"
DU0, DU1, DU2, DD0, DD1, DA0, DA1, MISC = "du0", "du1", "du2", "dd0", "dd1", "da0", "da1", "misc"
EU0, EU1, ED0, ED1, EA0, EA1, EA2 = "eu0", "eu1", "ed0", "ed1", "ea0", "ea1", "ea2"


def step(given, devices, with_sums):
    rows, width = given.tokens.shape
    ff = given.enc_up.shape[1]
    levels, entries, code_width = given.books.shape
    given.books = given.books.reshape(levels, -1, rows, code_width)
    bits = devices.bit_length() - 1
    vmem, hbm = pl.BlockSpec(memory_space=pltpu.VMEM), pl.BlockSpec(memory_space=pl.ANY)
    scratch = layer_scratch(rows, width, ff)
    scratch.update(
        w_qkv_e=pltpu.VMEM((width, 3 * width), BF16),
        w_out_e=pltpu.VMEM((width, width), BF16),
        cos=pltpu.VMEM((rows, PAIR), F32),
        sin=pltpu.VMEM((rows, PAIR), F32),
        bias=pltpu.VMEM((rows, rows), F32),
        ring=pltpu.VMEM((4,) + given.books.shape[1:], BF16),
        code_rows=pltpu.VMEM((levels, 8, rows), jnp.int32),
        chosen=pltpu.VMEM((levels, rows, code_width), BF16),
        ac=pltpu.VMEM((rows, code_width), BF16),
        gquant=pltpu.VMEM((rows, width), BF16),
        gy=pltpu.VMEM((rows, width), F32),
        latent=pltpu.VMEM((rows, width), BF16),
        pin_v=pltpu.VMEM((2, width, code_width), BF16),
        pout_v=pltpu.VMEM((2, code_width, width), BF16),
        distill_v=pltpu.VMEM(given.distill.shape, BF16),
        wavlm_v=pltpu.VMEM((rows, given.wavlm.shape[1]), BF16),
        tokens_v=pltpu.VMEM((rows, width), BF16),
        cotangent_v=pltpu.VMEM((rows, width), BF16),
        sem_move=pltpu.SemaphoreType.DMA((14,)),
        sem_book=pltpu.SemaphoreType.DMA((4,)),
    )
    outs = Refs(decoded=shaped((rows, width), BF16), grad_tokens=shaped((rows, width), F32))
    chunks, first_rows = {}, {}
    params = dict(vmem_limit_bytes=60 * 2**20)
    if with_sums:
        params.update(collective_id=0, has_side_effects=True)
        c, x, y = bits - 2, bits - 1, bits - 3
        b, a = range(y)
        share = width // devices
        low, high = ff // devices, share
        wide, half, blocks = ff // 128, ff // 256, width // 128
        third = 3 * blocks
        chunks = dict(
            di=Chunk(
                high,
                width,
                [c, a, b, x, y],
                [
                    Segment(8, 0, 2 * blocks, 0, blocks, 0, high // 2),
                    Segment(8, blocks, 2 * blocks, 0, blocks, high // 2, high // 2),
                ],
            ),
            du0=Chunk(high, ff // 4, [c, a, b, x, y], [Segment(2, 0, wide, 0, half // 2, 0, high)]),
            du1=Chunk(high, ff // 4, [c, x, a, b, y], [Segment(2, half // 2, wide, 0, half // 2, 0, high)]),
            dd0=Chunk(low, width // 2, [c, y, a, b, x], [Segment(3, 0, blocks, 0, blocks // 2, 0, low)]),
            dd1=Chunk(low, width // 2, [c, a, y, x, b], [Segment(3, blocks // 2, blocks, 0, blocks // 2, 0, low)]),
            du2=Chunk(high, ff // 2, [c, x, a, y, b], [Segment(2, half, wide, 0, half, 0, high)]),
            da0=Chunk(
                high,
                2 * width,
                [c, y, x, a, b],
                [Segment(1, 0, blocks, 0, blocks, 0, high), Segment(0, 0, third, width, blocks, 0, high)],
            ),
            da1=Chunk(high, 2 * width, [c, x, y, a, b], [Segment(0, blocks, third, 0, 2 * blocks, 0, high)]),
            misc=Chunk(
                high,
                2 * width,
                [c, y, a, x, b],
                [
                    Segment(9, 0, blocks, 0, blocks, 0, high),
                    Segment(10, 0, blocks // 2, width, blocks // 2, 0, high),
                    Segment(10, high * blocks // 2, blocks // 2, width + code_width, blocks // 2, 0, high),
                ],
            ),
            eu0=Chunk(high, ff // 2, [c, x, y, a, b], [Segment(6, 0, wide, 0, half, 0, high)]),
            eu1=Chunk(high, ff // 2, [c, x, a, b, y], [Segment(6, half, wide, 0, half, 0, high)]),
            ed0=Chunk(low, width // 2, [c, x, y, a, b], [Segment(7, 0, blocks, 0, blocks // 2, 0, low)]),
            ed1=Chunk(low, width // 2, [c, x, y, a, b], [Segment(7, blocks // 2, blocks, 0, blocks // 2, 0, low)]),
            ea0=Chunk(
                high,
                2 * width,
                [c, y, x, a, b],
                [Segment(5, 0, blocks, 0, blocks, 0, high), Segment(4, 0, third, width, blocks, 0, high)],
            ),
            ea1=Chunk(high, width, [c, x, a, y, b], [Segment(4, blocks, third, 0, blocks, 0, high)]),
            ea2=Chunk(
                high,
                width + 128,
                [c, x, y, a, b],
                [Segment(4, 2 * blocks, third, 0, blocks, 0, high), Segment(11, 0, 1, width, 1, 0, 8)],
            ),
        )
        rows_of = [high * 3 * blocks, high * blocks, high * wide, low * blocks] * 2
        rows_of += [high * blocks, high * blocks, high * blocks, 8, entries // 4 * code_width // 128]
        first_rows = {i: sum(rows_of[:i]) for i in range(len(rows_of))}
        first_rows[BOOKS] = first_rows[len(rows_of) - 1]
        copies = len(chunks) * bits + 2 * levels + 2
        scratch.update(
            t={name: pltpu.VMEM(c.shape(bits), BF16) for name, c in chunks.items()},
            recv={
                name: [pltpu.VMEM(c.shape(bits - 1 - stage), BF16) for stage in range(bits)]
                for name, c in chunks.items()
            },
            gains=pltpu.VMEM((4, width), F32),
            dec_gains=pltpu.VMEM((4, width), F32),
            code_got=pltpu.VMEM((levels, 8, rows), jnp.int32),
                book_sum=pltpu.VMEM((entries // 4, code_width), F32),
            book_send=pltpu.VMEM((2, entries // 4, code_width), BF16),
            book_got=pltpu.VMEM((2, entries // 4, code_width), BF16),
            book_last=pltpu.VMEM((entries // 4, code_width), BF16),
            send_sem=pltpu.SemaphoreType.DMA((copies,)),
            recv_sem=pltpu.SemaphoreType.DMA((copies,)),
        )
        outs.packed = shaped((sum(rows_of), 128), F32)
    else:
        outs.update(gains=shaped((4, width), F32), dec_gains=shaped((4, width), F32))
        outs.t = dict(
            enc_qkv=shaped(given.enc_qkv.shape, BF16),
            enc_out=shaped(given.enc_out.shape, BF16),
            enc_up=shaped(given.enc_up.shape, BF16),
            enc_down=shaped(given.enc_down.shape, BF16),
            dec_qkv=shaped(given.enc_qkv.shape, BF16),
            dec_out=shaped(given.enc_out.shape, BF16),
            dec_up=shaped(given.enc_up.shape, BF16),
            dec_down=shaped(given.enc_down.shape, BF16),
            pin=shaped((2 * width, code_width), BF16),
            pout=shaped((2 * code_width, width), BF16),
            books=shaped((levels, entries, code_width), BF16),
            distill=shaped(given.distill.shape, BF16),
        )
    in_specs = dict.fromkeys(given, hbm)
    in_specs.update(
        lengths=pl.BlockSpec(memory_space=pltpu.SMEM), codes=vmem, vectors=vmem
    )
    got = pl.pallas_call(
        functools.partial(step_kernel, chunks, first_rows, bits),
        out_shape={k: pltpu.VMEM(v.shape, v.dtype) for k, v in outs.items()} if with_sums else dict(outs),
        in_specs=[in_specs],
        out_specs=jax.tree.map(lambda _: vmem, dict(outs)),
        scratch_shapes=[dict(scratch)],
        compiler_params=pltpu.CompilerParams(**params),
        name="step",
    )(dict(given))
    got = Refs(got)
    if not with_sums:
        return got
    last = [shaped((rows, 128), F32) for rows in rows_of]
    last[11] = shaped((1, 128), F32)

    def hand_on(packed, decoded, grad, *refs):
        outs, moves = refs[:-1], Moves(refs[-1])
        parts = [packed.at[pl.ds(first_rows[i], ref.shape[0])] for i, ref in enumerate(outs[:-2])]
        leaving = [moves.start(part, ref) for part, ref in zip(parts + [decoded, grad], outs)]
        for move in leaving:
            move.wait()

    return pl.pallas_call(
        hand_on,
        out_shape=last + [outs.decoded, outs.grad_tokens],
        in_specs=[vmem] * 3,
        out_specs=[hbm] * (len(last) + 2),
        scratch_shapes=[pltpu.SemaphoreType.DMA((len(last) + 2,))],
        compiler_params=pltpu.CompilerParams(vmem_limit_bytes=16 * 2**20),
        name="results",
    )(got.packed, got.decoded, got.grad_tokens)


def body(
    tokens,
    wavlm,
    cotangent,
    lengths,
    codes,
    enc_qkv,
    enc_out,
    enc_up,
    enc_down,
    dec_qkv,
    dec_out,
    dec_up,
    dec_down,
    vectors,
    proj_in,
    proj_out,
    codebooks,
    distill_proj,
):
    width = tokens.shape[1]
    devices = lax.axis_size("dp") * lax.axis_size("branch")
    with_sums = devices == 4 * codebooks.shape[0] and width // devices % 16 == 0
    given = Refs(
        tokens=tokens,
        wavlm=wavlm,
        cotangent=cotangent,
        lengths=lengths,
        codes=codes.T,
        enc_qkv=enc_qkv,
        enc_out=enc_out,
        enc_up=enc_up,
        enc_down=enc_down,
        dec_qkv=dec_qkv,
        dec_out=dec_out,
        dec_up=dec_up,
        dec_down=dec_down,
        vectors=vectors,
        pin_own=proj_in,
        pout_own=proj_out,
        books=codebooks,
        distill=distill_proj,
    )
    if with_sums:
        *sums, decoded, grad_tokens = step(given, devices, True)
        sums = [part.reshape(-1) for part in sums]
        order = (4, 5, 6, 7, 0, 1, 2, 3, 11, 10, 9, 12, 8)
        return (decoded, grad_tokens, *[sums[i] for i in order])
    swap = [(0, 1), (1, 0)]
    given.pin_other = lax.ppermute(proj_in, "branch", swap)
    given.pout_other = lax.ppermute(proj_out, "branch", swap)
    s = step(given, devices, False)
    t = Refs(s.t)
    gains = jnp.concatenate([s.gains, s.dec_gains])
    local = [t.enc_qkv, t.enc_out, t.enc_up, t.enc_down, t.dec_qkv, t.dec_out, t.dec_up, t.dec_down]
    local += [gains, t.pin, t.pout, t.books, t.distill]
    sums = [
        lax.psum_scatter(part.astype(F32).reshape(-1), ("dp", "branch"), scatter_dimension=0, tiled=True)
        for part in local
    ]
    return (s.decoded, s.grad_tokens, *sums)


def solution(mesh):
    rows, whole = P(("dp", "branch"), None), P()
    placed = (rows, P("dp", None), rows, rows, P("dp", None)) + (whole,) * 9
    placed += (P("branch", None, None),) * 2 + (whole,) * 2
    return jax.shard_map(
        body,
        mesh=mesh,
        in_specs=placed,
        out_specs=(rows, rows) + (P(("dp", "branch")),) * 13,
        check_vma=False,
    )
```

```python
import functools
import math

import jax
import jax.numpy as jnp
from jax import lax
from jax.experimental import pallas as pl
from jax.experimental.pallas import tpu as pltpu
from jax.sharding import PartitionSpec as P

HEADS = 8
WINDOW = 250
EPS_NORM = 1e-05
EPS_COS = 1e-06
BETA = 0.25
DISTILL = 10.0
ROPE_BASE = 10000.0

MESH = pl.DeviceIdType.MESH
F32 = jnp.float32
BF16 = jnp.bfloat16
TILE = 512
PAIR = 128
HALF = 256


def dot(left, right):
    return lax.dot_general(left, right, (((1,), (0,)), ((), ())), preferred_element_type=F32)


def dot_t(left, right):
    return lax.dot_general(left, right, (((1,), (1,)), ((), ())), preferred_element_type=F32)


def t_dot(left, right):
    return lax.dot_general(left, right, (((0,), (0,)), ((), ())), preferred_element_type=F32)


def iota(shape, dim):
    return lax.broadcasted_iota(jnp.int32, shape, dim)


def aligned(index, size):
    return pl.ds(pl.multiple_of(index * size, size), size)


class Refs(dict):
    __getattr__ = dict.__getitem__
    __setattr__ = dict.__setitem__


class Moves:
    def __init__(self, semaphores):
        self.semaphores, self.count = semaphores, 0

    def start(self, source, target):
        move = pltpu.make_async_copy(source, target, self.semaphores.at[self.count])
        self.count += 1
        move.start()
        return move


def layer_scratch(rows, width, ff):
    return Refs(
        x=pltpu.VMEM((rows, width), F32),
        s1=pltpu.VMEM((rows, 1), F32),
        h=pltpu.VMEM((rows, width), BF16),
        h1t=pltpu.VMEM((width, rows), BF16),
        h2t=pltpu.VMEM((width, rows), BF16),
        rinv=pltpu.VMEM((rows, width), F32),
        qkv=pltpu.VMEM((rows, 3 * width), BF16),
        mix=pltpu.VMEM((rows, width), BF16),
        ao=pltpu.VMEM((rows, width), F32),
        x2=pltpu.VMEM((rows, width), F32),
        s2=pltpu.VMEM((rows, 1), F32),
        act=pltpu.VMEM((rows, ff), BF16),
        dg=pltpu.VMEM((rows, ff), BF16),
        fo=pltpu.VMEM((rows, width), F32),
        grad=pltpu.VMEM((rows, width), BF16),
        gx=pltpu.VMEM((rows, width), F32),
        acc=pltpu.VMEM((rows, width), F32),
        wide=pltpu.VMEM((4, rows, HALF), F32),
        change=pltpu.VMEM((2, rows, rows), BF16),
        w_qkv_v=pltpu.VMEM((width, 3 * width), BF16),
        w_out_v=pltpu.VMEM((width, width), BF16),
        w_up_v=pltpu.VMEM((width, ff), BF16),
        w_down_v=pltpu.VMEM((ff, width), BF16),
    )


def shaped(shape, kind):
    return jax.ShapeDtypeStruct(shape, kind)


def frame_tables(r):
    rows = r.cos.shape[0]
    place = iota((rows, PAIR), 0)
    query, key = iota((rows, rows), 0), iota((rows, rows), 1)
    begin, begin_query = jnp.zeros_like(place), jnp.zeros_like(query)
    edge = 0
    for clip in range(r.lengths.shape[1] - 1):
        edge = edge + r.lengths[0, clip]
        begin = jnp.where(place >= edge, edge, begin)
        begin_query = jnp.where(query >= edge, edge, begin_query)
    allowed = (key >= begin_query) & (key <= query) & (query - key < WINDOW)
    r.bias[...] = jnp.where(allowed, 0.0, -1e30)
    lane = iota((rows, PAIR), 1)
    rate = jnp.exp((lane % 32).astype(F32) * (-math.log(ROPE_BASE) / 32))
    angle = (place - begin).astype(F32) * rate
    r.cos[...] = jnp.cos(angle)
    sine = jnp.sin(angle)
    r.sin[...] = jnp.where(lane % 64 < 32, -sine, sine)


def rotated(value, cosine, sine):
    lane = iota(value.shape, 1)
    swapped = jnp.where(lane % 64 < 32, pltpu.roll(value, PAIR - 32, 1), pltpu.roll(value, 32, 1))
    return value * cosine + swapped * sine


def head_masks(rows):
    low = iota((rows, PAIR), 1) < 64
    return (jnp.where(low, 1.0, 0.0).astype(BF16), jnp.where(low, 0.0, 1.0).astype(BF16))


def row_blocks(rows, step):
    return [slice(i, i + step) for i in range(0, rows, step)]


def attention_project(r, w_qkv, gain):
    rows, width = r.x.shape
    scale = gain(0)
    for at in row_blocks(rows, 64):
        x = r.x[at, :]
        s1 = lax.rsqrt(jnp.mean(x * x, axis=1, keepdims=True) + EPS_NORM)
        r.s1[at, :] = s1
        r.h[at, :] = (x * s1 * scale).astype(BF16)
    for half in range(3 * width // HALF):
        slot, part = half % 4, half // (width // HALF)
        cols = slice(half * HALF, (half + 1) * HALF)
        r.wide[slot] = dot(r.h[...], w_qkv[:, cols])
        for at in row_blocks(rows, 64):
            for p in range(HALF // PAIR):
                value = r.wide[slot, at, p * PAIR : (p + 1) * PAIR]
                if part < 2:
                    value = rotated(value, r.cos[at, :], r.sin[at, :])
                low = value.astype(BF16)
                if part == 0:
                    low = (low.astype(F32) * 0.125).astype(BF16)
                r.qkv[at, half * HALF + p * PAIR : half * HALF + (p + 1) * PAIR] = low
    r.h1t[...] = r.h[...].T


def attention_mix(r, w_out, gain):
    rows, width = r.x.shape
    masks = head_masks(rows)
    low = iota((rows, PAIR), 1) < 64
    pairs = width // PAIR
    for p in range(pairs):
        query = r.qkv[:, p * PAIR : (p + 1) * PAIR]
        key = r.qkv[:, (p + pairs) * PAIR : (p + pairs + 1) * PAIR]
        value = r.qkv[:, (p + 2 * pairs) * PAIR : (p + 2 * pairs + 1) * PAIR]
        outs = []
        for h in range(2):
            head = 2 * p + h
            slot = head % 4
            r.wide[slot] = dot_t(query * masks[h], key)
            for at in row_blocks(rows, 64):
                seen = PAIR if at.stop <= PAIR else rows
                scores = r.wide[slot, at, :seen] + r.bias[at, :seen]
                weights = jnp.exp(scores - jnp.max(scores, axis=1, keepdims=True))
                r.att[head, at, :seen] = weights.astype(BF16)
                if seen < rows:
                    r.att[head, at, seen:] = jnp.zeros((64, rows - seen), BF16)
            outs.append(dot(r.att[head], value * masks[h] + masks[1 - h]))
        inverse = 1.0 / pltpu.roll(jnp.where(low, outs[1], outs[0]), 64, 1)
        r.rinv[:, p * PAIR : (p + 1) * PAIR] = inverse
        r.mix[:, p * PAIR : (p + 1) * PAIR] = (jnp.where(low, outs[0], outs[1]) * inverse).astype(BF16)
    r.ao[...] = dot(r.mix[...], w_out[...])
    scale_one, scale_two = gain(1), gain(2)
    for at in row_blocks(rows, 64):
        x2 = r.x[at, :] + scale_one * r.ao[at, :]
        r.x2[at, :] = x2
        s2 = lax.rsqrt(jnp.mean(x2 * x2, axis=1, keepdims=True) + EPS_NORM)
        r.s2[at, :] = s2
        r.h[at, :] = (x2 * s2 * scale_two).astype(BF16)
    r.h2t[...] = r.h[...].T


def gelu_parts(pre):
    slope = math.sqrt(2.0 / math.pi)
    square = pre * pre
    bent = jnp.tanh(slope * pre * (1.0 + 0.044715 * square))
    half = 0.5 * (1.0 + bent)
    turn = 0.5 * pre * (1.0 - bent * bent) * slope * (1.0 + 3.0 * 0.044715 * square)
    return (pre * half).astype(BF16), half + turn


def ffn_forward(r, w_up, w_down):
    rows, ff = r.act.shape
    for half in range(ff // HALF):
        slot, cols = half % 4, slice(half * HALF, (half + 1) * HALF)
        r.wide[slot] = dot(r.h[...], w_up[:, cols])
        for at in row_blocks(rows, 32):
            act, slope = gelu_parts(r.wide[slot, at, :])
            r.act[at, cols] = act
            r.dg[at, cols] = slope.astype(BF16)
    r.fo[...] = dot(r.act[...], w_down[...])


def ffn_both(r, w_up, w_down, grad_up, grad_down, first, last):
    rows = r.act.shape[0]
    for t in range(first, last):
        cols = slice(t * TILE, (t + 1) * TILE)
        for side in range(TILE // HALF):
            part = slice(t * TILE + side * HALF, t * TILE + (side + 1) * HALF)
            r.wide[side] = dot(r.h[...], w_up[:, part])
            r.wide[2 + side] = dot_t(r.grad[...], w_down[part, :])
            for at in row_blocks(rows, 32):
                act, slope = gelu_parts(r.wide[side, at, :])
                r.act[at, part] = act
                r.dg[at, part] = (r.wide[2 + side, at, :] * slope).astype(BF16)
        grad_up.shift((t - first) * TILE).put(dot(r.h2t[...], r.dg[:, cols]))
        put_rows(grad_down, t_dot(r.act[:, cols], r.grad[...]), t)


def ffn_back_sum(r, w_up):
    r.acc[...] = dot_t(r.dg[...], w_up[...])


def norm_back(stream, inverse, grad):
    mean = jnp.mean(grad * stream, axis=1, keepdims=True)
    return inverse * grad - stream * (inverse * inverse * inverse * mean)


def column_sum(value):
    return jnp.sum(value, axis=0, keepdims=True)


class Place:
    def __init__(self, ref, col=0):
        self.ref, self.col = ref, col

    def shift(self, by):
        return Place(self.ref, self.col + by)

    def put(self, value):
        shape = self.ref.shape
        value = value.astype(self.ref.dtype).reshape(shape[:-1] + (value.shape[1],))
        self.ref[(slice(None),) * (len(shape) - 1) + (pl.ds(self.col, value.shape[-1]),)] = value


def put_rows(targets, value, tile):
    value = value.astype(BF16)
    begin = 0
    for target in targets:
        shape = target.shape
        part = value[:, begin : begin + shape[-1]]
        begin += shape[-1]
        if len(shape) == 2:
            target[aligned(tile, value.shape[0]), :] = part
        else:
            target[tile // 2, tile % 2] = part.reshape(shape[2:])


def ffn_backward_begin(r, gain, gy_ref):
    scale = gain(3)
    for at in row_blocks(r.grad.shape[0], 64):
        r.grad[at, :] = (scale * gy_ref[at, :].astype(F32)).astype(BF16)


def ffn_backward_tiles(r, w_down, grad_up, grad_down, first, last):
    rows = r.act.shape[0]
    for t in range(first, last):
        cols = slice(t * TILE, (t + 1) * TILE)
        for side in range(TILE // HALF):
            part = slice(t * TILE + side * HALF, t * TILE + (side + 1) * HALF)
            slot = (2 * t + side) % 4
            r.wide[slot] = dot_t(r.grad[...], w_down[part, :])
            for at in row_blocks(rows, 64):
                r.dg[at, part] = (r.wide[slot, at, :] * r.dg[at, part].astype(F32)).astype(BF16)
        put_rows(grad_down, t_dot(r.act[:, cols], r.grad[...]), t)
        grad_up.shift((t - first) * TILE).put(dot(r.h2t[...], r.dg[:, cols]))


def ffn_backward_end(r, gain, gy_ref, gain_out):
    scale = gain(2)
    to_gain = to_scale = 0.0
    for at in row_blocks(r.x2.shape[0], 32):
        gy = gy_ref[at, :].astype(F32)
        to_scale = to_scale + column_sum(gy * r.fo[at, :])
        back, x2, s2 = r.acc[at, :], r.x2[at, :], r.s2[at, :]
        to_gain = to_gain + column_sum(back * x2 * s2)
        r.gx[at, :] = gy + norm_back(x2, s2, back * scale)
    gain_out[3:4, :] = to_scale
    gain_out[2:3, :] = to_gain


def attention_backward_out(r, w_out, gain, grad_out, gain_out):
    scale = gain(1)
    to_scale = 0.0
    for at in row_blocks(r.gx.shape[0], 64):
        gx = r.gx[at, :]
        to_scale = to_scale + column_sum(gx * r.ao[at, :])
        r.grad[at, :] = (scale * gx).astype(BF16)
    gain_out[1:2, :] = to_scale
    grad_out.put(t_dot(r.mix[...], r.grad[...]))
    r.grad[...] = dot_t(r.grad[...], w_out[...]).astype(BF16)


def attention_backward_pairs(r, first, last):
    rows, width = r.x.shape
    masks = head_masks(rows)
    masks_t = [jnp.where((iota((PAIR, rows), 0) < 64) == (h == 0), 1.0, 0.0).astype(BF16) for h in range(2)]
    pairs = width // PAIR
    for p in range(first, last):
        lanes = [slice((p + i * pairs) * PAIR, (p + i * pairs + 1) * PAIR) for i in range(3)]
        query, key, value = (r.qkv[:, at] for at in lanes)
        grad_mixed = (r.grad[:, lanes[0]].astype(F32) * r.rinv[:, lanes[0]]).astype(BF16)
        product = (grad_mixed.astype(F32) * r.mix[:, lanes[0]].astype(F32)).astype(BF16)
        beside = jnp.concatenate([value, jnp.full(value.shape, -1.0, BF16)], axis=1)
        query_t, grad_t = query.T, grad_mixed.T
        to_query = to_key = to_value = 0.0
        for h in range(2):
            head = 2 * p + h
            slot = head % 4
            both = jnp.concatenate([grad_mixed * masks[h], product * masks[h]], axis=1)
            r.wide[slot] = dot_t(both, beside)
            for at in row_blocks(rows, 64):
                r.change[h, at, :] = (r.att[head, at, :].astype(F32) * r.wide[slot, at, :]).astype(BF16)
            to_query = to_query + dot(r.change[h], key * masks[h])
            to_key = to_key + dot(query_t * masks_t[h], r.change[h])
            to_value = to_value + dot(grad_t * masks_t[h], r.att[head])
        cosine, sine = r.cos[...], -r.sin[...]
        r.qkv[:, lanes[0]] = rotated(to_query * 0.125, cosine, sine).astype(BF16)
        r.qkv[:, lanes[1]] = rotated(to_key.T, cosine, sine).astype(BF16)
        r.qkv[:, lanes[2]] = to_value.T.astype(BF16)


def attention_backward_in(r, grad_qkv, part):
    width = r.x.shape[1]
    grad_qkv.put(dot(r.h1t[...], r.qkv[:, part * width : (part + 1) * width]))


def attention_backward_end(r, w_qkv, gain, gain_out):
    r.acc[...] = dot_t(r.qkv[...], w_qkv[...])
    scale = gain(0)
    to_gain = 0.0
    for at in row_blocks(r.x.shape[0], 32):
        back, x, s1 = r.acc[at, :], r.x[at, :], r.s1[at, :]
        to_gain = to_gain + column_sum(back * x * s1)
        r.gx[at, :] = r.gx[at, :] + norm_back(x, s1, back * scale)
    gain_out[0:1, :] = to_gain


class Segment:
    def __init__(self, result, base, stride, col, blocks, row, rows):
        self.result, self.base, self.stride, self.col, self.blocks = result, base, stride, col, blocks
        self.row, self.rows = row, rows


class Chunk:
    def __init__(self, rows, columns, order, segments):
        self.rows, self.columns, self.order, self.segments = rows, columns, order, segments

    def shape(self, leading):
        return (2,) * leading + (self.rows, self.columns)

    def bytes(self, bits):
        return 2**bits * self.rows * self.columns * 2


def plan(chunks, work, bits, book_bytes):
    core, x, y = bits - 2, bits - 1, bits - 3
    ends, middle = -1, -2
    free, pending, done = {}, [], []
    now = 0.0

    def carry(link, size, rate=42e3):
        free[link] = max(now, free.get(link, 0.0)) + size / rate
        return free[link]

    def begin(name, stage):
        if name == BOOKS:
            size = 1.2 * 2 ** (bits - 3) * book_bytes
            if stage == 0:
                there = max(carry(y, size), carry(ends, 1.5 * size), carry(middle, 2 * size))
            else:
                there = carry(core, 4 * book_bytes, 400e3) if stage == 1 else carry(x, 2 * book_bytes)
        else:
            dim = chunks[name].order[stage]
            size = chunks[name].bytes(bits) / 2 ** (stage + 1)
            if dim == core:
                there = carry(core, size, 400e3)
            elif dim == x or dim == y:
                there = carry(dim, size)
            else:
                there = carry(ends, size)
                if dim < y - 1:
                    there = max(there, carry(middle, 2 * size))
        pending.append((there + 1.5, name, stage))

    def finish(limit):
        nonlocal now
        acts = []
        while pending:
            pending.sort(key=lambda p: p[0])
            if pending[0][0] + (0.5 if limit < math.inf else 0.0) > limit:
                break
            at, name, stage = pending.pop(0)
            if name == BOOKS:
                cost = (6.0, 0.6, 0.3)[stage]
            else:
                cost = 0.25 + 0.3e-6 * chunks[name].bytes(bits) / 2 ** (stage + 1)
            now = max(now, at) + cost
            limit = max(limit, now)
            acts.append((name, stage))
            if stage + 1 < (3 if name == BOOKS else bits):
                begin(name, stage + 1)
        return acts

    for took, _, names in work:
        now += 0.95 * took
        for name in names:
            begin(name, 0)
        done.append(finish(now))
    done.append(finish(math.inf))
    return done


def coordinates(step, count):
    return [step // 2 ** (count - 1 - i) % 2 for i in range(count)]


def store_segment(packed, first, segment, value):
    for i in range(segment.blocks):
        where = pl.ds(first + segment.base + i, segment.rows, stride=segment.stride)
        packed[where, :] = value[
            segment.row : segment.row + segment.rows, segment.col + i * 128 : segment.col + (i + 1) * 128
        ]


class Halving:
    def __init__(self, chunks, bits, recv, packed, first, send_sem, recv_sem):
        self.chunks = chunks
        self.bits, self.recv, self.packed, self.first = bits, recv, packed, first
        self.send_sem, self.recv_sem = send_sem, recv_sem
        self.copies = {}
        dp, branch = lax.axis_index("dp"), lax.axis_index("branch")
        self.mine, self.partner = [], []
        for dim in range(bits - 1):
            weight = 2 ** (bits - 2 - dim)
            bit = dp // weight % 2
            self.mine.append(bit)
            self.partner.append({"dp": dp + weight * (1 - 2 * bit), "branch": branch})
        self.mine.append(branch)
        self.partner.append({"dp": dp, "branch": 1 - branch})

    def near_level(self, other):
        dp = lax.axis_index("dp")
        for i in range(self.bits - 2):
            if other >> i & 1:
                dp = dp + 2 ** (i + 1) * (1 - 2 * self.mine[self.bits - 3 - i])
        return {"dp": dp, "branch": lax.axis_index("branch")}

    def barrier(self):
        semaphore = pltpu.get_barrier_semaphore()
        levels = 2 ** (self.bits - 2)
        targets = self.partner[self.bits - 2 :] + [self.near_level(other) for other in range(1, levels)]
        for target in targets:
            pl.semaphore_signal(semaphore, inc=1, device_id=target, device_id_type=MESH)
        return lambda: pl.semaphore_wait(semaphore, len(targets))

    def left(self, name, stage):
        return [d for d in range(self.bits) if d not in self.chunks[name].order[:stage]]

    def half(self, ref, name, stage, index):
        position = self.left(name, stage).index(self.chunks[name].order[stage])
        return ref.at[(slice(None),) * position + (index,)]

    def remote(self, source, target, device, *key):
        slot = len(self.copies)
        self.copies[key] = pltpu.make_async_remote_copy(
            src_ref=source,
            dst_ref=target,
            send_sem=self.send_sem.at[slot],
            recv_sem=self.recv_sem.at[slot],
            device_id=device,
            device_id_type=MESH,
        )
        self.copies[key].start()

    def send(self, name, stage, source):
        dim = self.chunks[name].order[stage]
        self.remote(source, self.recv[name][stage], self.partner[dim], name, stage)

    def send_half(self, name, stage, ref):
        dim = self.chunks[name].order[stage]
        self.send(name, stage, self.half(ref, name, stage, 1 - self.mine[dim]))

    def arrived(self, *key):
        self.copies[key].wait_recv()

    def add(self, name, stage, own):
        chunk = self.chunks[name]
        got = self.recv[name][stage]
        depth = self.bits - 1 - stage
        if stage == self.bits - 1:
            value = own[...].astype(F32) + got[...].astype(F32)
            for segment in chunk.segments:
                store_segment(self.packed, self.first[segment.result], segment, value)
            return

        outer = max(depth - 2, 0)

        def step(i, carry):
            where = tuple(coordinates(i, outer))
            got[where] = got[where] + own[where]
            return carry

        lax.fori_loop(0, 2**outer, step, 0)

    def finish(self, name, stage, own=None):
        chunk = self.chunks[name]
        self.arrived(name, stage)
        if own is None:
            dim = chunk.order[stage]
            own = self.half(self.recv[name][stage - 1], name, stage, self.mine[dim])
        self.add(name, stage, own)
        self.follow(name, stage)

    def follow(self, name, stage):
        if stage + 1 < self.bits:
            self.send_half(name, stage + 1, self.recv[name][stage])

    def drain(self):
        for copy in self.copies.values():
            copy.wait_send()


BOOKS = "books"


def quantizer_semantic(r):
    sem_code = r.chosen[0]
    rows, code_width = sem_code.shape
    columns = [slice(i * HALF, (i + 1) * HALF) for i in range(r.distill_v.shape[1] // HALF)]
    for i, cols in enumerate(columns):
        r.wide[i] = dot(sem_code, r.distill_v[:, cols])

    def row_sum(parts):
        return jnp.sum(sum(parts), axis=1, keepdims=True)

    for at in row_blocks(rows, 32):
        prediction = [r.wide[i, at, :] for i in range(len(columns))]
        target = [r.wavlm_v[at, cols].astype(F32) for cols in columns]
        pred_norm = lax.rsqrt(row_sum([p * p for p in prediction]) + EPS_COS)
        target_norm = lax.rsqrt(row_sum([w * w for w in target]) + EPS_COS)
        cosine = row_sum([p * w for p, w in zip(prediction, target)]) * (pred_norm * target_norm)
        from_target = -DISTILL * pred_norm * target_norm
        from_prediction = DISTILL * cosine * pred_norm * pred_norm
        for p, w, cols in zip(prediction, target, columns):
            r.act[at, cols] = (w * from_target + p * from_prediction).astype(BF16)
    grad_pred = r.act[:, : r.distill_v.shape[1]]
    put_distill(r.places.distill, dot(sem_code.T, grad_pred))
    r.gy[:, :code_width] = dot_t(grad_pred, r.distill_v[...])


def quantizer_latent(r):
    levels, rows, code_width = r.chosen.shape
    latent_t = r.latent[...].T
    r.wide[0] = dot_t(r.gquant[...], r.pout_v[0])
    r.wide[1] = dot(r.latent[...], r.pin_v[0])
    r.wide[2] = dot_t(r.gquant[...], r.pout_v[1])
    r.wide[3] = dot(r.latent[...], r.pin_v[1])
    put_group(r.places.pout, 0, t_dot(r.chosen[0], r.gquant[...]))
    put_group(r.places.pout, 1, t_dot(r.ac[...], r.gquant[...]))
    for at in row_blocks(rows, 32):
        grad_sem = r.wide[0, at, :] + r.gy[at, :code_width]
        commit = 2.0 * BETA * (r.wide[1, at, :] - r.chosen[0, at, :].astype(F32))
        r.g_rows[0, at, :] = (grad_sem - commit).astype(BF16)
        r.grad[at, :code_width] = (grad_sem + commit).astype(BF16)
        grad_ac, residual = r.wide[2, at, :], r.wide[3, at, :]
        for level in range(1, levels):
            residual = residual - r.chosen[level, at, :].astype(F32)
        carry = jnp.zeros_like(residual)
        for level in range(levels - 1, 0, -1):
            carry = carry + 2.0 * BETA * residual
            r.g_rows[level, at, :] = (grad_ac - carry).astype(BF16)
            residual = residual + r.chosen[level, at, :].astype(F32)
        r.grad[at, code_width:] = (grad_ac + carry).astype(BF16)
    put_group(r.places.pin, 0, dot(latent_t, r.grad[:, :code_width]))
    put_group(r.places.pin, 1, dot(latent_t, r.grad[:, code_width:]))
    r.gy[...] = dot_t(r.grad[...], jnp.concatenate([r.pin_v[0], r.pin_v[1]], axis=1))


def put_group(place, group, value):
    target, rows = place.ref, value.shape[0]
    value = value.astype(target.dtype)
    if len(target.shape) == 2:
        target[group * rows : (group + 1) * rows, :] = value
        return
    lead, height = target.shape[1:-2], target.shape[-2]
    value = value.reshape(math.prod(lead), -1, height, value.shape[1])
    value = jnp.concatenate([value[:, i] for i in range(value.shape[1])], axis=2)
    columns = value.shape[2]
    where = (group,) + (slice(None),) * (len(lead) + 1) + (pl.ds(place.col, columns),)
    target[where] = value.reshape(lead + (height, columns))


def put_distill(place, value):
    target = place.ref
    if len(target.shape) == 2:
        target[...] = value.astype(target.dtype)
        return
    height = target.shape[-2]
    value = value.reshape(math.prod(target.shape[:-2]), -1, value.shape[1])
    columns = value.shape[2] * value.shape[1] // height
    value = jnp.concatenate([value[:, :, i : i + columns] for i in range(0, value.shape[2], columns)], axis=1)
    where = (slice(None),) * (len(target.shape) - 1) + (pl.ds(place.col, columns),)
    target[where] = value.astype(target.dtype).reshape(target.shape[:-1] + (columns,))


def one_hot_rows(codes, first, count):
    row = iota((count, codes.shape[1]), 0)
    return jnp.where(codes - first == row, 1.0, 0.0).astype(BF16)


def pick_codes(r):
    levels, _, entries, code_width = r.books.shape
    entries = entries * r.books.shape[1]
    rows = r.cos.shape[0]
    slots = r.ring.shape[0]
    branch = lax.axis_index("branch")
    own = r.codes[:, pl.ds(pl.multiple_of(branch * rows, rows), rows)]
    r.code_rows[...] = jnp.broadcast_to(own[:, None, :], r.code_rows.shape)
    columns = jnp.concatenate([own.astype(F32), jnp.zeros((PAIR - levels, rows), F32)], axis=0).T
    lane = iota(columns.shape, 1)
    entry = iota((rows, entries), 1)
    r.code_cols[...] = columns
    r.ac_sum[...] = jnp.zeros(r.ac_sum.shape, F32)

    def book(level):
        slot = level % slots
        return pltpu.make_async_copy(r.books.at[level], r.ring.at[slot], r.sem_book.at[slot])

    def pick(level, carry):
        code = jnp.sum(jnp.where(lane == level, r.code_cols[...], 0.0), axis=1, keepdims=True)
        one_hot = jnp.where(entry == code.astype(jnp.int32), 1.0, 0.0).astype(BF16)
        book(level).wait()
        got = dot(one_hot, r.ring[level % slots].reshape(entries, code_width))
        r.chosen[level] = got.astype(BF16)
        r.ac_sum[...] += jnp.where(level > 0, got, 0.0)

        @pl.when(level + slots < levels)
        def _():
            book(level + slots).start()

        return carry

    def begin():
        for level in range(slots):
            book(level).start()

    def run():
        lax.fori_loop(0, levels, pick, 0, unroll=4)
        r.ac[...] = r.ac_sum[...].astype(BF16)

    return begin, run


def step_kernel(chunks, first_rows, bits, ins, outs, scratch):
    r = Refs({**ins, **outs, **scratch})
    t = r.t = Refs(r.t)
    r.att, r.g_rows, r.g_got, r.book_own = (r.ring.at[i] for i in range(4))
    r.ac_sum, r.code_cols = r.acc.at[:, : r.ac.shape[1]], r.gx.at[:, :PAIR]
    branch = lax.axis_index("branch")
    rows, width = r.tokens.shape
    levels, parts, entries, code_width = r.books.shape
    entries = entries * parts
    tiles = r.w_up_v.shape[1] // TILE
    pairs = width // PAIR
    if chunks:
        sums = Halving(chunks, bits, r.recv, r.packed, first_rows, r.send_sem, r.recv_sem)
        mine, level = sums.mine[bits - 2], lax.axis_index("dp") // 2
        wait_barrier = sums.barrier()
    moves = Moves(r.sem_move)
    begin_pick, run_pick = pick_codes(r)
    begin_pick()
    got_pout = [moves.start(r.pout_own.at[0], r.pout_v.at[branch])]
    frame_tables(r)
    if chunks:
        wait_barrier()
        sums.remote(r.pout_own.at[0], r.pout_v.at[branch], sums.partner[bits - 1], POUT)
    else:
        got_pout.append(moves.start(r.pout_other.at[0], r.pout_v.at[1 - branch]))
    got_rest = [
        moves.start(r.distill, r.distill_v),
        moves.start(r.wavlm.at[pl.ds(pl.multiple_of(branch * rows, rows), rows)], r.wavlm_v),
    ]
    got_attention = [moves.start(r.dec_qkv, r.w_qkv_v), moves.start(r.dec_out, r.w_out_v)]
    got_ffn = [moves.start(r.dec_up, r.w_up_v), moves.start(r.dec_down, r.w_down_v)]
    got_cotangent = [moves.start(r.cotangent, r.cotangent_v)]
    got_pin = [moves.start(r.pin_own.at[0], r.pin_v.at[branch])]
    if not chunks:
        got_pin.append(moves.start(r.pin_other.at[0], r.pin_v.at[1 - branch]))
    got_tokens = [moves.start(r.tokens, r.tokens_v)]
    got_attention_two = [moves.start(r.enc_qkv, r.w_qkv_e), moves.start(r.enc_out, r.w_out_e)]

    if chunks:
        down = dict(dec=[t.dd0, t.dd1], enc=[t.ed0, t.ed1, t.ed2])
        place = r.places = Refs(
            dec_up=[Place(t.du0), Place(t.du1)],
            dec_out=Place(t.da0),
            dec_qkv=[Place(t.da0, width), Place(t.da1), Place(t.da2)],
            enc_up=[Place(t.eu0), Place(t.eu1)],
            enc_out=Place(t.ea0),
            enc_qkv=[Place(t.ea1), Place(t.ea2), Place(t.ea3)],
            distill=Place(t.di),
            pout=Place(t.misc),
            pin=Place(t.misc, width),
        )
    else:
        down = dict(dec=[t.dec_down], enc=[t.enc_down])
        place = r.places = Refs(
            dec_up=[Place(t.dec_up, i * tiles // 2 * TILE) for i in range(2)],
            dec_out=Place(t.dec_out),
            dec_qkv=[Place(t.dec_qkv, i * width) for i in range(3)],
            enc_up=[Place(t.enc_up, i * tiles // 2 * TILE) for i in range(2)],
            enc_out=Place(t.enc_out),
            enc_qkv=[Place(t.enc_qkv, i * width) for i in range(3)],
            distill=Place(t.distill),
            pout=Place(t.pout),
            pin=Place(t.pin),
        )
    dec_down, enc_down = down["dec"], down["enc"]

    def wait(moves, other=None):
        for move in moves:
            move.wait()
        if chunks and other is not None:
            sums.arrived(other)

    def layer_value(target, gain):
        for at in row_blocks(rows, 64):
            target[at, :] = (r.x2[at, :] + gain(3) * r.fo[at, :]).astype(BF16)

    def dec_gain(i):
        return r.vectors[1, i : i + 1, :]

    def enc_gain(i):
        return r.vectors[0, i : i + 1, :]

    def pick():
        run_pick()

    def semantic():
        wait(got_rest)
        quantizer_semantic(r)

    def quant():
        wait(got_pout, POUT)
        if chunks:
            sums.remote(r.pin_own.at[0], r.pin_v.at[branch], sums.partner[bits - 1], PIN)
        r.x[...] = dot(jnp.concatenate([r.chosen[0], r.ac[...]], axis=1), r.pout_v[...].reshape(-1, width))
        if chunks:
            for other in range(1, levels):
                target = sums.near_level(other)
                sums.remote(r.code_rows.at[target_level(target)], r.code_got.at[other], target, CODES, other)
            r.code_got[0] = r.code_rows[level]

    def target_level(target):
        return next(iter(target.values())) // 2

    def dec_project():
        wait(got_attention)
        attention_project(r, r.w_qkv_v, dec_gain)

    def dec_mix():
        attention_mix(r, r.w_out_v, dec_gain)

    def dec_ffn(half):
        def run():
            if half == 0:
                wait(got_ffn)
                wait(got_cotangent)
                ffn_backward_begin(r, dec_gain, r.cotangent_v)
            first, last = half * tiles // 2, (half + 1) * tiles // 2
            ffn_both(r, r.w_up_v, r.w_down_v, place.dec_up[half], dec_down, first, last)
            if half == 1:
                r.fo[...] = dot(r.act[...], r.w_down_v[...])
                layer_value(r.decoded, dec_gain)
                ffn_back_sum(r, r.w_up_v)
                ffn_backward_end(r, dec_gain, r.cotangent_v, r.dec_gains)
                got_ffn[:] = [moves.start(r.enc_up, r.w_up_v), moves.start(r.enc_down, r.w_down_v)]

        return run

    def dec_out():
        attention_backward_out(r, r.w_out_v, dec_gain, place.dec_out, r.dec_gains)

    def attention_pairs(first, last):
        return lambda: attention_backward_pairs(r, first, last)

    def dec_in(part):
        def run():
            attention_backward_in(r, place.dec_qkv[part], part)
            if part == 2:
                attention_backward_end(r, r.w_qkv_v, dec_gain, r.dec_gains)
                r.gquant[...] = r.gx[...].astype(BF16)

        return run

    def enc_project():
        wait(got_tokens)
        r.x[...] = r.tokens_v[...].astype(F32)
        wait(got_attention_two)
        attention_project(r, r.w_qkv_e, enc_gain)

    def enc_mix():
        attention_mix(r, r.w_out_e, enc_gain)

    def enc_ffn():
        wait(got_ffn)
        ffn_forward(r, r.w_up_v, r.w_down_v)
        layer_value(r.latent, enc_gain)

    def quantizer():
        wait(got_pin, PIN)
        quantizer_latent(r)
        if chunks:
            for other in reversed(range(1, levels)):
                target = sums.near_level(other)
                sums.arrived(CODES, other)
                sums.remote(r.g_rows.at[target_level(target)], r.g_got.at[other], target, BOOKS, 0, other)
            r.g_got[0] = r.g_rows[level]

    def book_half(core, put):
        quarter = entries // 4
        for side in range(2):
            r.book_sum[...] = jnp.zeros_like(r.book_sum)
            first = (core * 2 + side) * quarter

            def add(source, carry):
                one_hot = one_hot_rows(r.code_got[source, 0:1, :], first, quarter)
                r.book_sum[...] += dot(one_hot, r.g_got[source])
                return carry

            lax.fori_loop(0, levels, add, 0, unroll=4)
            put(side, r.book_sum[...])

    def finish_books(stage):
        blocks = entries // 4 // rows
        other_core, other_side = sums.partner[bits - 2], sums.partner[bits - 1]
        if stage == 0:
            for other in range(1, levels):
                sums.arrived(BOOKS, 0, other)

            def put(side, value):
                r.book_send[side] = value.astype(BF16)

            def keep(side, value):
                r.book_own[side * blocks : (side + 1) * blocks] = value.astype(BF16).reshape((blocks, rows, code_width))

            book_half(1 - mine, put)
            sums.remote(r.book_send, r.book_got, other_core, BOOKS, 1)
            book_half(mine, keep)
        elif stage == 1:
            sums.arrived(BOOKS, 1)
            for side in range(2):
                own = r.book_own[side * blocks : (side + 1) * blocks]
                r.book_got[side] = r.book_got[side] + own.reshape(r.book_got.shape[1:])
            sums.remote(r.book_got.at[1 - branch], r.book_last, other_side, BOOKS, 2)
        else:
            sums.arrived(BOOKS, 2)
            total = r.book_got[branch].astype(F32) + r.book_last[...].astype(F32)
            blocks = code_width // 128
            store_segment(r.packed, first_rows[BOOKS], Segment(BOOKS, 0, blocks, 0, blocks, 0, entries // 4), total)

    def all_books():
        parts = entries // TILE

        def one(step, carry):
            at = step // parts
            one_hot = one_hot_rows(r.code_rows[at, 0:1, :], step % parts * TILE, TILE)
            t.books[at, aligned(step % parts, TILE), :] = dot(one_hot, r.g_rows[at]).astype(BF16)
            return carry

        lax.fori_loop(0, levels * parts, one, 0)

    def enc_ffn_back(half):
        def run():
            first, last = half * tiles // 2, (half + 1) * tiles // 2
            if half == 0:
                ffn_backward_begin(r, enc_gain, r.gy)
            ffn_backward_tiles(r, r.w_down_v, place.enc_up[half], enc_down, first, last)
            if half == 1:
                ffn_back_sum(r, r.w_up_v)
                ffn_backward_end(r, enc_gain, r.gy, r.gains)

        return run

    def enc_out():
        attention_backward_out(r, r.w_out_e, enc_gain, place.enc_out, r.gains)

    def enc_in(part):
        def run():
            attention_backward_in(r, place.enc_qkv[part], part)
            if part == 2:
                attention_backward_end(r, r.w_qkv_e, enc_gain, r.gains)
                r.grad_tokens[...] = r.gx[...]
                if chunks:
                    spread_gains()

        return run

    def spread_gains():
        lanes = pl.ds(width, 128)
        for layer, ref in enumerate((r.gains, r.dec_gains)):
            for row in range(4):
                for block in range(width // 128):
                    owner = (layer * 4 + row) * (width // 128) + block
                    where = tuple(owner // 2 ** (bits - 1 - i) % 2 for i in range(bits))
                    value = ref[row : row + 1, block * 128 : (block + 1) * 128]
                    rows_here = t.ea3.shape[bits]
                    t.ea3[where + (slice(None), lanes)] = jnp.broadcast_to(value, (rows_here, 128)).astype(BF16)

    work = [
        (6.5, pick, ()),
        (2.0, semantic, (DISTILL_GRAD,)),
        (0.7, quant, ()),
        (1.5, dec_project, ()),
        (2.5, dec_mix, ()),
        (2.6, dec_ffn(0), (DU0,)),
        (2.7, dec_ffn(1), (DD0, DD1, DU1)),
        (1.2, dec_out, ()),
        (1.6, attention_pairs(0, pairs // 2), ()),
        (1.6, attention_pairs(pairs // 2, pairs), ()),
        (0.6, dec_in(0), (DA0,)),
        (0.6, dec_in(1), (DA1,)),
        (0.8, dec_in(2), (DA2,)),
        (1.5, enc_project, ()),
        (2.5, enc_mix, ()),
        (2.2, enc_ffn, ()),
        (2.0, quantizer, (BOOKS, MISC)),
        (2.0, enc_ffn_back(0), (EU0,)),
        (2.0, enc_ffn_back(1), (EU1, ED0, ED1, ED2)),
        (1.2, enc_out, (EA0,)),
        (1.6, attention_pairs(0, pairs // 2), ()),
        (1.6, attention_pairs(pairs // 2, pairs), ()),
        (0.6, enc_in(0), (EA1,)),
        (0.6, enc_in(1), (EA2,)),
        (1.0, enc_in(2), (EA3,)),
    ]
    if not chunks:
        for _, run, _ in work:
            run()
            if run is quantizer:
                all_books()
        return
    actions = plan(chunks, work, bits, rows * code_width * 2)

    def finish(name, stage):
        if name == BOOKS:
            finish_books(stage)
        elif stage == 0:
            sums.finish(name, 0, sums.half(t[name], name, 0, mine))
        else:
            sums.finish(name, stage)

    for (_, run, made), acts in zip(work, actions):
        run()
        for name in made:
            if name != BOOKS:
                sums.send_half(name, 0, t[name])
        for name, stage in acts:
            finish(name, stage)
    for name, stage in actions[-1]:
        finish(name, stage)
    sums.drain()


POUT, PIN, CODES = 1, 2, 3
DISTILL_GRAD = "di"
DD0, DD1, DU0, DU1, DA0, DA1, DA2, MISC = "dd0", "dd1", "du0", "du1", "da0", "da1", "da2", "misc"
EU0, EU1, ED0, ED1, ED2 = "eu0", "eu1", "ed0", "ed1", "ed2"
EA0, EA1, EA2, EA3 = "ea0", "ea1", "ea2", "ea3"


def step(given, devices, with_sums):
    rows, width = given.tokens.shape
    ff = given.enc_up.shape[1]
    levels, entries, code_width = given.books.shape
    given.books = given.books.reshape(levels, -1, rows, code_width)
    bits = devices.bit_length() - 1
    vmem, hbm = pl.BlockSpec(memory_space=pltpu.VMEM), pl.BlockSpec(memory_space=pl.ANY)
    scratch = layer_scratch(rows, width, ff)
    scratch.update(
        w_qkv_e=pltpu.VMEM((width, 3 * width), BF16),
        w_out_e=pltpu.VMEM((width, width), BF16),
        cos=pltpu.VMEM((rows, PAIR), F32),
        sin=pltpu.VMEM((rows, PAIR), F32),
        bias=pltpu.VMEM((rows, rows), F32),
        ring=pltpu.VMEM((4,) + given.books.shape[1:], BF16),
        code_rows=pltpu.VMEM((levels, 8, rows), jnp.int32),
        chosen=pltpu.VMEM((levels, rows, code_width), BF16),
        ac=pltpu.VMEM((rows, code_width), BF16),
        gquant=pltpu.VMEM((rows, width), BF16),
        gy=pltpu.VMEM((rows, width), F32),
        latent=pltpu.VMEM((rows, width), BF16),
        pin_v=pltpu.VMEM((2, width, code_width), BF16),
        pout_v=pltpu.VMEM((2, code_width, width), BF16),
        distill_v=pltpu.VMEM(given.distill.shape, BF16),
        wavlm_v=pltpu.VMEM((rows, given.wavlm.shape[1]), BF16),
        tokens_v=pltpu.VMEM((rows, width), BF16),
        cotangent_v=pltpu.VMEM((rows, width), BF16),
        sem_move=pltpu.SemaphoreType.DMA((14,)),
        sem_book=pltpu.SemaphoreType.DMA((4,)),
    )
    outs = Refs(decoded=shaped((rows, width), BF16), grad_tokens=shaped((rows, width), F32))
    chunks, first_rows = {}, {}
    params = dict(vmem_limit_bytes=60 * 2**20)
    if with_sums:
        params.update(collective_id=0, has_side_effects=True)
        c, x, y = bits - 2, bits - 1, bits - 3
        b, a = range(y)
        share = width // devices
        low, high = ff // devices, share
        wide, half, blocks = ff // 128, ff // 256, width // 128
        third, quarter = 3 * blocks, blocks // 4
        chunks = dict(
            di=Chunk(
                high,
                width,
                [c, y, x, a, b],
                [
                    Segment(8, 0, 2 * blocks, 0, blocks, 0, high // 2),
                    Segment(8, blocks, 2 * blocks, 0, blocks, high // 2, high // 2),
                ],
            ),
            du0=Chunk(high, ff // 2, [c, y, a, x, b], [Segment(2, 0, wide, 0, half, 0, high)]),
            dd0=Chunk(low, width // 2, [c, a, y, b, x], [Segment(3, 0, blocks, 0, 2 * quarter, 0, low)]),
            dd1=Chunk(low, width // 2, [c, y, x, a, b], [Segment(3, 2 * quarter, blocks, 0, 2 * quarter, 0, low)]),
            du1=Chunk(high, ff // 2, [c, x, y, a, b], [Segment(2, half, wide, 0, half, 0, high)]),
            da0=Chunk(
                high,
                2 * width,
                [c, x, y, a, b],
                [Segment(1, 0, blocks, 0, blocks, 0, high), Segment(0, 0, third, width, blocks, 0, high)],
            ),
            da1=Chunk(high, width, [c, a, x, y, b], [Segment(0, blocks, third, 0, blocks, 0, high)]),
            da2=Chunk(high, width, [c, y, x, a, b], [Segment(0, 2 * blocks, third, 0, blocks, 0, high)]),
            misc=Chunk(
                high,
                2 * width,
                [c, x, y, a, b],
                [
                    Segment(9, 0, blocks, 0, blocks, 0, high),
                    Segment(10, 0, blocks // 2, width, blocks // 2, 0, high),
                    Segment(10, high * blocks // 2, blocks // 2, width + code_width, blocks // 2, 0, high),
                ],
            ),
            eu0=Chunk(high, ff // 2, [c, x, a, y, b], [Segment(6, 0, wide, 0, half, 0, high)]),
            eu1=Chunk(high, ff // 2, [c, x, y, a, b], [Segment(6, half, wide, 0, half, 0, high)]),
            ed0=Chunk(low, width // 2, [c, x, y, a, b], [Segment(7, 0, blocks, 0, 2 * quarter, 0, low)]),
            ed1=Chunk(low, width // 4, [c, y, x, a, b], [Segment(7, 2 * quarter, blocks, 0, quarter, 0, low)]),
            ed2=Chunk(low, width // 4, [c, y, a, b, x], [Segment(7, 3 * quarter, blocks, 0, quarter, 0, low)]),
            ea0=Chunk(high, width, [c, x, y, a, b], [Segment(5, 0, blocks, 0, blocks, 0, high)]),
            ea1=Chunk(high, width, [c, y, x, a, b], [Segment(4, 0, third, 0, blocks, 0, high)]),
            ea2=Chunk(high, width, [c, x, a, y, b], [Segment(4, blocks, third, 0, blocks, 0, high)]),
            ea3=Chunk(
                high,
                width + 128,
                [c, x, y, a, b],
                [Segment(4, 2 * blocks, third, 0, blocks, 0, high), Segment(11, 0, 1, width, 1, 0, 8)],
            ),
        )
        rows_of = [high * 3 * blocks, high * blocks, high * wide, low * blocks] * 2
        rows_of += [high * blocks, high * blocks, high * blocks, 8, entries // 4 * code_width // 128]
        first_rows = {i: sum(rows_of[:i]) for i in range(len(rows_of))}
        first_rows[BOOKS] = first_rows[len(rows_of) - 1]
        copies = len(chunks) * bits + 2 * levels + 2
        scratch.update(
            t={name: pltpu.VMEM(c.shape(bits), BF16) for name, c in chunks.items()},
            recv={
                name: [pltpu.VMEM(c.shape(bits - 1 - stage), BF16) for stage in range(bits)]
                for name, c in chunks.items()
            },
            gains=pltpu.VMEM((4, width), F32),
            dec_gains=pltpu.VMEM((4, width), F32),
            code_got=pltpu.VMEM((levels, 8, rows), jnp.int32),
                book_sum=pltpu.VMEM((entries // 4, code_width), F32),
            book_send=pltpu.VMEM((2, entries // 4, code_width), BF16),
            book_got=pltpu.VMEM((2, entries // 4, code_width), BF16),
            book_last=pltpu.VMEM((entries // 4, code_width), BF16),
            send_sem=pltpu.SemaphoreType.DMA((copies,)),
            recv_sem=pltpu.SemaphoreType.DMA((copies,)),
        )
        outs.packed = shaped((sum(rows_of), 128), F32)
    else:
        outs.update(gains=shaped((4, width), F32), dec_gains=shaped((4, width), F32))
        outs.t = dict(
            enc_qkv=shaped(given.enc_qkv.shape, BF16),
            enc_out=shaped(given.enc_out.shape, BF16),
            enc_up=shaped(given.enc_up.shape, BF16),
            enc_down=shaped(given.enc_down.shape, BF16),
            dec_qkv=shaped(given.enc_qkv.shape, BF16),
            dec_out=shaped(given.enc_out.shape, BF16),
            dec_up=shaped(given.enc_up.shape, BF16),
            dec_down=shaped(given.enc_down.shape, BF16),
            pin=shaped((2 * width, code_width), BF16),
            pout=shaped((2 * code_width, width), BF16),
            books=shaped((levels, entries, code_width), BF16),
            distill=shaped(given.distill.shape, BF16),
        )
    in_specs = dict.fromkeys(given, hbm)
    in_specs.update(
        lengths=pl.BlockSpec(memory_space=pltpu.SMEM), codes=vmem, vectors=vmem
    )
    got = pl.pallas_call(
        functools.partial(step_kernel, chunks, first_rows, bits),
        out_shape={k: pltpu.VMEM(v.shape, v.dtype) for k, v in outs.items()} if with_sums else dict(outs),
        in_specs=[in_specs],
        out_specs=jax.tree.map(lambda _: vmem, dict(outs)),
        scratch_shapes=[dict(scratch)],
        compiler_params=pltpu.CompilerParams(**params),
        name="step",
    )(dict(given))
    got = Refs(got)
    if not with_sums:
        return got
    last = [shaped((rows, 128), F32) for rows in rows_of]
    last[11] = shaped((1, 128), F32)

    def hand_on(packed, decoded, grad, *refs):
        outs, moves = refs[:-1], Moves(refs[-1])
        parts = [packed.at[pl.ds(first_rows[i], ref.shape[0])] for i, ref in enumerate(outs[:-2])]
        leaving = [moves.start(part, ref) for part, ref in zip(parts + [decoded, grad], outs)]
        for move in leaving:
            move.wait()

    return pl.pallas_call(
        hand_on,
        out_shape=last + [outs.decoded, outs.grad_tokens],
        in_specs=[vmem] * 3,
        out_specs=[hbm] * (len(last) + 2),
        scratch_shapes=[pltpu.SemaphoreType.DMA((len(last) + 2,))],
        compiler_params=pltpu.CompilerParams(vmem_limit_bytes=16 * 2**20),
        name="results",
    )(got.packed, got.decoded, got.grad_tokens)


def body(
    tokens,
    wavlm,
    cotangent,
    lengths,
    codes,
    enc_qkv,
    enc_out,
    enc_up,
    enc_down,
    dec_qkv,
    dec_out,
    dec_up,
    dec_down,
    vectors,
    proj_in,
    proj_out,
    codebooks,
    distill_proj,
):
    width = tokens.shape[1]
    devices = lax.axis_size("dp") * lax.axis_size("branch")
    with_sums = devices == 4 * codebooks.shape[0] and width // devices % 16 == 0
    given = Refs(
        tokens=tokens,
        wavlm=wavlm,
        cotangent=cotangent,
        lengths=lengths,
        codes=codes.T,
        enc_qkv=enc_qkv,
        enc_out=enc_out,
        enc_up=enc_up,
        enc_down=enc_down,
        dec_qkv=dec_qkv,
        dec_out=dec_out,
        dec_up=dec_up,
        dec_down=dec_down,
        vectors=vectors,
        pin_own=proj_in,
        pout_own=proj_out,
        books=codebooks,
        distill=distill_proj,
    )
    if with_sums:
        *sums, decoded, grad_tokens = step(given, devices, True)
        sums = [part.reshape(-1) for part in sums]
        order = (4, 5, 6, 7, 0, 1, 2, 3, 11, 10, 9, 12, 8)
        return (decoded, grad_tokens, *[sums[i] for i in order])
    swap = [(0, 1), (1, 0)]
    given.pin_other = lax.ppermute(proj_in, "branch", swap)
    given.pout_other = lax.ppermute(proj_out, "branch", swap)
    s = step(given, devices, False)
    t = Refs(s.t)
    gains = jnp.concatenate([s.gains, s.dec_gains])
    local = [t.enc_qkv, t.enc_out, t.enc_up, t.enc_down, t.dec_qkv, t.dec_out, t.dec_up, t.dec_down]
    local += [gains, t.pin, t.pout, t.books, t.distill]
    sums = [
        lax.psum_scatter(part.astype(F32).reshape(-1), ("dp", "branch"), scatter_dimension=0, tiled=True)
        for part in local
    ]
    return (s.decoded, s.grad_tokens, *sums)


def solution(mesh):
    rows, whole = P(("dp", "branch"), None), P()
    placed = (rows, P("dp", None), rows, rows, P("dp", None)) + (whole,) * 9
    placed += (P("branch", None, None),) * 2 + (whole,) * 2
    return jax.shard_map(
        body,
        mesh=mesh,
        in_specs=placed,
        out_specs=(rows, rows) + (P(("dp", "branch")),) * 13,
        check_vma=False,
    )
```

```python
import functools
import math

import jax
import jax.numpy as jnp
from jax import lax
from jax.experimental import pallas as pl
from jax.experimental.pallas import tpu as pltpu
from jax.sharding import PartitionSpec as P

HEADS = 8
WINDOW = 250
EPS_NORM = 1e-05
EPS_COS = 1e-06
BETA = 0.25
DISTILL = 10.0
ROPE_BASE = 10000.0

MESH = pl.DeviceIdType.MESH
F32 = jnp.float32
BF16 = jnp.bfloat16
TILE = 512
PAIR = 128
HALF = 256


def dot(left, right):
    return lax.dot_general(left, right, (((1,), (0,)), ((), ())), preferred_element_type=F32)


def dot_t(left, right):
    return lax.dot_general(left, right, (((1,), (1,)), ((), ())), preferred_element_type=F32)


def t_dot(left, right):
    return lax.dot_general(left, right, (((0,), (0,)), ((), ())), preferred_element_type=F32)


def iota(shape, dim):
    return lax.broadcasted_iota(jnp.int32, shape, dim)


def aligned(index, size):
    return pl.ds(pl.multiple_of(index * size, size), size)


class Refs(dict):
    __getattr__ = dict.__getitem__
    __setattr__ = dict.__setitem__


class Moves:
    def __init__(self, semaphores):
        self.semaphores, self.count = semaphores, 0

    def start(self, source, target):
        move = pltpu.make_async_copy(source, target, self.semaphores.at[self.count])
        self.count += 1
        move.start()
        return move


def layer_scratch(rows, width, ff):
    return Refs(
        x=pltpu.VMEM((rows, width), F32),
        s1=pltpu.VMEM((rows, 1), F32),
        h=pltpu.VMEM((rows, width), BF16),
        h1t=pltpu.VMEM((width, rows), BF16),
        h2t=pltpu.VMEM((width, rows), BF16),
        rinv=pltpu.VMEM((rows, width), F32),
        qkv=pltpu.VMEM((rows, 3 * width), BF16),
        mix=pltpu.VMEM((rows, width), BF16),
        ao=pltpu.VMEM((rows, width), F32),
        x2=pltpu.VMEM((rows, width), F32),
        s2=pltpu.VMEM((rows, 1), F32),
        act=pltpu.VMEM((rows, ff), BF16),
        dg=pltpu.VMEM((rows, ff), BF16),
        fo=pltpu.VMEM((rows, width), F32),
        grad=pltpu.VMEM((rows, width), BF16),
        gx=pltpu.VMEM((rows, width), F32),
        acc=pltpu.VMEM((rows, width), F32),
        wide=pltpu.VMEM((4, rows, HALF), F32),
        change=pltpu.VMEM((2, rows, rows), BF16),
        w_qkv_v=pltpu.VMEM((width, 3 * width), BF16),
        w_out_v=pltpu.VMEM((width, width), BF16),
        w_up_v=pltpu.VMEM((width, ff), BF16),
        w_down_v=pltpu.VMEM((ff, width), BF16),
    )


def shaped(shape, kind):
    return jax.ShapeDtypeStruct(shape, kind)


def frame_tables(r):
    rows = r.cos.shape[0]
    place = iota((rows, PAIR), 0)
    query, key = iota((rows, rows), 0), iota((rows, rows), 1)
    begin, begin_query = jnp.zeros_like(place), jnp.zeros_like(query)
    edge = 0
    for clip in range(r.lengths.shape[1] - 1):
        edge = edge + r.lengths[0, clip]
        begin = jnp.where(place >= edge, edge, begin)
        begin_query = jnp.where(query >= edge, edge, begin_query)
    allowed = (key >= begin_query) & (key <= query) & (query - key < WINDOW)
    r.bias[...] = jnp.where(allowed, 0.0, -1e30)
    lane = iota((rows, PAIR), 1)
    rate = jnp.exp((lane % 32).astype(F32) * (-math.log(ROPE_BASE) / 32))
    angle = (place - begin).astype(F32) * rate
    r.cos[...] = jnp.cos(angle)
    sine = jnp.sin(angle)
    r.sin[...] = jnp.where(lane % 64 < 32, -sine, sine)


def rotated(value, cosine, sine):
    lane = iota(value.shape, 1)
    swapped = jnp.where(lane % 64 < 32, pltpu.roll(value, PAIR - 32, 1), pltpu.roll(value, 32, 1))
    return value * cosine + swapped * sine


def head_masks(rows):
    low = iota((rows, PAIR), 1) < 64
    return (jnp.where(low, 1.0, 0.0).astype(BF16), jnp.where(low, 0.0, 1.0).astype(BF16))


def row_blocks(rows, step):
    return [slice(i, i + step) for i in range(0, rows, step)]


def attention_project(r, w_qkv, gain):
    rows, width = r.x.shape
    scale = gain(0)
    for at in row_blocks(rows, 64):
        x = r.x[at, :]
        s1 = lax.rsqrt(jnp.mean(x * x, axis=1, keepdims=True) + EPS_NORM)
        r.s1[at, :] = s1
        r.h[at, :] = (x * s1 * scale).astype(BF16)
    for half in range(3 * width // HALF):
        slot, part = half % 4, half // (width // HALF)
        cols = slice(half * HALF, (half + 1) * HALF)
        r.wide[slot] = dot(r.h[...], w_qkv[:, cols])
        for at in row_blocks(rows, 64):
            for p in range(HALF // PAIR):
                value = r.wide[slot, at, p * PAIR : (p + 1) * PAIR]
                if part < 2:
                    value = rotated(value, r.cos[at, :], r.sin[at, :])
                low = value.astype(BF16)
                if part == 0:
                    low = (low.astype(F32) * 0.125).astype(BF16)
                r.qkv[at, half * HALF + p * PAIR : half * HALF + (p + 1) * PAIR] = low
    r.h1t[...] = r.h[...].T


def attention_mix(r, w_out, gain):
    rows, width = r.x.shape
    masks = head_masks(rows)
    low = iota((rows, PAIR), 1) < 64
    pairs = width // PAIR
    for p in range(pairs):
        query = r.qkv[:, p * PAIR : (p + 1) * PAIR]
        key = r.qkv[:, (p + pairs) * PAIR : (p + pairs + 1) * PAIR]
        value = r.qkv[:, (p + 2 * pairs) * PAIR : (p + 2 * pairs + 1) * PAIR]
        outs = []
        for h in range(2):
            head = 2 * p + h
            slot = head % 4
            r.wide[slot] = dot_t(query * masks[h], key)
            for at in row_blocks(rows, 64):
                seen = PAIR if at.stop <= PAIR else rows
                scores = r.wide[slot, at, :seen] + r.bias[at, :seen]
                weights = jnp.exp(scores - jnp.max(scores, axis=1, keepdims=True))
                r.att[head, at, :seen] = weights.astype(BF16)
                if seen < rows:
                    r.att[head, at, seen:] = jnp.zeros((64, rows - seen), BF16)
            outs.append(dot(r.att[head], value * masks[h] + masks[1 - h]))
        inverse = 1.0 / pltpu.roll(jnp.where(low, outs[1], outs[0]), 64, 1)
        r.rinv[:, p * PAIR : (p + 1) * PAIR] = inverse
        r.mix[:, p * PAIR : (p + 1) * PAIR] = (jnp.where(low, outs[0], outs[1]) * inverse).astype(BF16)
    r.ao[...] = dot(r.mix[...], w_out[...])
    scale_one, scale_two = gain(1), gain(2)
    for at in row_blocks(rows, 64):
        x2 = r.x[at, :] + scale_one * r.ao[at, :]
        r.x2[at, :] = x2
        s2 = lax.rsqrt(jnp.mean(x2 * x2, axis=1, keepdims=True) + EPS_NORM)
        r.s2[at, :] = s2
        r.h[at, :] = (x2 * s2 * scale_two).astype(BF16)
    r.h2t[...] = r.h[...].T


def gelu_parts(pre):
    slope = math.sqrt(2.0 / math.pi)
    square = pre * pre
    bent = jnp.tanh(slope * pre * (1.0 + 0.044715 * square))
    half = 0.5 * (1.0 + bent)
    turn = 0.5 * pre * (1.0 - bent * bent) * slope * (1.0 + 3.0 * 0.044715 * square)
    return (pre * half).astype(BF16), half + turn


def ffn_forward(r, w_up, w_down):
    rows, ff = r.act.shape
    for half in range(ff // HALF):
        slot, cols = half % 4, slice(half * HALF, (half + 1) * HALF)
        r.wide[slot] = dot(r.h[...], w_up[:, cols])
        for at in row_blocks(rows, 32):
            act, slope = gelu_parts(r.wide[slot, at, :])
            r.act[at, cols] = act
            r.dg[at, cols] = slope.astype(BF16)
    r.fo[...] = dot(r.act[...], w_down[...])


def ffn_both(r, w_up, w_down, grad_up, grad_down, first, last):
    rows = r.act.shape[0]
    for t in range(first, last):
        cols = slice(t * TILE, (t + 1) * TILE)
        for side in range(TILE // HALF):
            part = slice(t * TILE + side * HALF, t * TILE + (side + 1) * HALF)
            r.wide[side] = dot(r.h[...], w_up[:, part])
            r.wide[2 + side] = dot_t(r.grad[...], w_down[part, :])
            for at in row_blocks(rows, 32):
                act, slope = gelu_parts(r.wide[side, at, :])
                r.act[at, part] = act
                r.dg[at, part] = (r.wide[2 + side, at, :] * slope).astype(BF16)
        grad_up[t].put(dot(r.h2t[...], r.dg[:, cols]))
        put_rows(grad_down, t_dot(r.act[:, cols], r.grad[...]), t)


def ffn_back_sum(r, w_up):
    r.acc[...] = dot_t(r.dg[...], w_up[...])


def norm_back(stream, inverse, grad):
    mean = jnp.mean(grad * stream, axis=1, keepdims=True)
    return inverse * grad - stream * (inverse * inverse * inverse * mean)


def column_sum(value):
    return jnp.sum(value, axis=0, keepdims=True)


class Place:
    def __init__(self, ref, col=0):
        self.ref, self.col = ref, col

    def shift(self, by):
        return Place(self.ref, self.col + by)

    def put(self, value):
        shape = self.ref.shape
        value = value.astype(self.ref.dtype).reshape(shape[:-1] + (value.shape[1],))
        self.ref[(slice(None),) * (len(shape) - 1) + (pl.ds(self.col, value.shape[-1]),)] = value


def put_rows(targets, value, tile):
    value = value.astype(BF16)
    begin = 0
    for target in targets:
        shape = target.shape
        part = value[:, begin : begin + shape[-1]]
        begin += shape[-1]
        if len(shape) == 2:
            target[aligned(tile, value.shape[0]), :] = part
        else:
            target[tile // 2, tile % 2] = part.reshape(shape[2:])


def ffn_backward_begin(r, gain, gy_ref):
    scale = gain(3)
    for at in row_blocks(r.grad.shape[0], 64):
        r.grad[at, :] = (scale * gy_ref[at, :].astype(F32)).astype(BF16)


def ffn_backward_tiles(r, w_down, grad_up, grad_down, first, last):
    rows = r.act.shape[0]
    for t in range(first, last):
        cols = slice(t * TILE, (t + 1) * TILE)
        for side in range(TILE // HALF):
            part = slice(t * TILE + side * HALF, t * TILE + (side + 1) * HALF)
            slot = (2 * t + side) % 4
            r.wide[slot] = dot_t(r.grad[...], w_down[part, :])
            for at in row_blocks(rows, 64):
                r.dg[at, part] = (r.wide[slot, at, :] * r.dg[at, part].astype(F32)).astype(BF16)
        put_rows(grad_down, t_dot(r.act[:, cols], r.grad[...]), t)
        grad_up.shift((t - first) * TILE).put(dot(r.h2t[...], r.dg[:, cols]))


def ffn_backward_end(r, gain, gy_ref, gain_out):
    scale = gain(2)
    to_gain = to_scale = 0.0
    for at in row_blocks(r.x2.shape[0], 32):
        gy = gy_ref[at, :].astype(F32)
        to_scale = to_scale + column_sum(gy * r.fo[at, :])
        back, x2, s2 = r.acc[at, :], r.x2[at, :], r.s2[at, :]
        to_gain = to_gain + column_sum(back * x2 * s2)
        r.gx[at, :] = gy + norm_back(x2, s2, back * scale)
    gain_out[3:4, :] = to_scale
    gain_out[2:3, :] = to_gain


def attention_backward_out(r, w_out, gain, grad_out, gain_out):
    scale = gain(1)
    to_scale = 0.0
    for at in row_blocks(r.gx.shape[0], 64):
        gx = r.gx[at, :]
        to_scale = to_scale + column_sum(gx * r.ao[at, :])
        r.grad[at, :] = (scale * gx).astype(BF16)
    gain_out[1:2, :] = to_scale
    grad_out.put(t_dot(r.mix[...], r.grad[...]))
    r.grad[...] = dot_t(r.grad[...], w_out[...]).astype(BF16)


def attention_backward_pairs(r, first, last):
    rows, width = r.x.shape
    masks = head_masks(rows)
    masks_t = [jnp.where((iota((PAIR, rows), 0) < 64) == (h == 0), 1.0, 0.0).astype(BF16) for h in range(2)]
    pairs = width // PAIR
    for p in range(first, last):
        lanes = [slice((p + i * pairs) * PAIR, (p + i * pairs + 1) * PAIR) for i in range(3)]
        query, key, value = (r.qkv[:, at] for at in lanes)
        grad_mixed = (r.grad[:, lanes[0]].astype(F32) * r.rinv[:, lanes[0]]).astype(BF16)
        product = (grad_mixed.astype(F32) * r.mix[:, lanes[0]].astype(F32)).astype(BF16)
        beside = jnp.concatenate([value, jnp.full(value.shape, -1.0, BF16)], axis=1)
        query_t, grad_t = query.T, grad_mixed.T
        to_query = to_key = to_value = 0.0
        for h in range(2):
            head = 2 * p + h
            slot = head % 4
            both = jnp.concatenate([grad_mixed * masks[h], product * masks[h]], axis=1)
            r.wide[slot] = dot_t(both, beside)
            for at in row_blocks(rows, 64):
                r.change[h, at, :] = (r.att[head, at, :].astype(F32) * r.wide[slot, at, :]).astype(BF16)
            to_query = to_query + dot(r.change[h], key * masks[h])
            to_key = to_key + dot(query_t * masks_t[h], r.change[h])
            to_value = to_value + dot(grad_t * masks_t[h], r.att[head])
        cosine, sine = r.cos[...], -r.sin[...]
        r.qkv[:, lanes[0]] = rotated(to_query * 0.125, cosine, sine).astype(BF16)
        r.qkv[:, lanes[1]] = rotated(to_key.T, cosine, sine).astype(BF16)
        r.qkv[:, lanes[2]] = to_value.T.astype(BF16)


def attention_backward_in(r, grad_qkv, part):
    width = r.x.shape[1]
    grad_qkv.put(dot(r.h1t[...], r.qkv[:, part * width : (part + 1) * width]))


def attention_backward_end(r, w_qkv, gain, gain_out):
    r.acc[...] = dot_t(r.qkv[...], w_qkv[...])
    scale = gain(0)
    to_gain = 0.0
    for at in row_blocks(r.x.shape[0], 32):
        back, x, s1 = r.acc[at, :], r.x[at, :], r.s1[at, :]
        to_gain = to_gain + column_sum(back * x * s1)
        r.gx[at, :] = r.gx[at, :] + norm_back(x, s1, back * scale)
    gain_out[0:1, :] = to_gain


class Segment:
    def __init__(self, result, base, stride, col, blocks, row, rows):
        self.result, self.base, self.stride, self.col, self.blocks = result, base, stride, col, blocks
        self.row, self.rows = row, rows


class Chunk:
    def __init__(self, rows, columns, order, segments):
        self.rows, self.columns, self.order, self.segments = rows, columns, order, segments

    def shape(self, leading):
        return (2,) * leading + (self.rows, self.columns)

    def bytes(self, bits):
        return 2**bits * self.rows * self.columns * 2


def plan(chunks, work, bits, book_bytes):
    core, x, y = bits - 2, bits - 1, bits - 3
    ends, middle = -1, -2
    free, pending, done = {}, [], []
    now = 0.0

    def carry(link, size, rate=42e3):
        free[link] = max(now, free.get(link, 0.0)) + size / rate
        return free[link]

    def begin(name, stage):
        if name == BOOKS:
            size = 1.2 * 2 ** (bits - 3) * book_bytes
            if stage == 0:
                there = max(carry(y, size), carry(ends, 1.5 * size), carry(middle, 2 * size))
            else:
                there = carry(core, 4 * book_bytes, 400e3) if stage == 1 else carry(x, 2 * book_bytes)
        else:
            dim = chunks[name].order[stage]
            size = chunks[name].bytes(bits) / 2 ** (stage + 1)
            if dim == core:
                there = carry(core, size, 400e3)
            elif dim == x or dim == y:
                there = carry(dim, size)
            else:
                there = carry(ends, size)
                if dim < y - 1:
                    there = max(there, carry(middle, 2 * size))
        pending.append((there + 1.5, name, stage))

    def finish(limit):
        nonlocal now
        acts = []
        while pending:
            pending.sort(key=lambda p: p[0])
            if pending[0][0] + (0.5 if limit < math.inf else 0.0) > limit:
                break
            at, name, stage = pending.pop(0)
            if name == BOOKS:
                cost = (6.0, 0.6, 0.3)[stage]
            else:
                cost = 0.25 + 0.3e-6 * chunks[name].bytes(bits) / 2 ** (stage + 1)
            now = max(now, at) + cost
            limit = max(limit, now)
            acts.append((name, stage))
            if stage + 1 < (3 if name == BOOKS else bits):
                begin(name, stage + 1)
        return acts

    for took, _, names in work:
        now += took
        for name in names:
            begin(name, 0)
        done.append(finish(now))
    done.append(finish(math.inf))
    return done


def coordinates(step, count):
    return [step // 2 ** (count - 1 - i) % 2 for i in range(count)]


def store_segment(packed, first, segment, value):
    for i in range(segment.blocks):
        where = pl.ds(first + segment.base + i, segment.rows, stride=segment.stride)
        packed[where, :] = value[
            segment.row : segment.row + segment.rows, segment.col + i * 128 : segment.col + (i + 1) * 128
        ]


class Halving:
    def __init__(self, chunks, bits, recv, packed, first, send_sem, recv_sem):
        self.chunks = chunks
        self.bits, self.recv, self.packed, self.first = bits, recv, packed, first
        self.send_sem, self.recv_sem = send_sem, recv_sem
        self.copies = {}
        dp, branch = lax.axis_index("dp"), lax.axis_index("branch")
        self.mine, self.partner = [], []
        for dim in range(bits - 1):
            weight = 2 ** (bits - 2 - dim)
            bit = dp // weight % 2
            self.mine.append(bit)
            self.partner.append({"dp": dp + weight * (1 - 2 * bit), "branch": branch})
        self.mine.append(branch)
        self.partner.append({"dp": dp, "branch": 1 - branch})

    def near_level(self, other):
        dp = lax.axis_index("dp")
        for i in range(self.bits - 2):
            if other >> i & 1:
                dp = dp + 2 ** (i + 1) * (1 - 2 * self.mine[self.bits - 3 - i])
        return {"dp": dp, "branch": lax.axis_index("branch")}

    def barrier(self):
        semaphore = pltpu.get_barrier_semaphore()
        levels = 2 ** (self.bits - 2)
        targets = self.partner[self.bits - 2 :] + [self.near_level(other) for other in range(1, levels)]
        for target in targets:
            pl.semaphore_signal(semaphore, inc=1, device_id=target, device_id_type=MESH)
        return lambda: pl.semaphore_wait(semaphore, len(targets))

    def left(self, name, stage):
        return [d for d in range(self.bits) if d not in self.chunks[name].order[:stage]]

    def half(self, ref, name, stage, index):
        position = self.left(name, stage).index(self.chunks[name].order[stage])
        return ref.at[(slice(None),) * position + (index,)]

    def remote(self, source, target, device, *key):
        slot = len(self.copies)
        self.copies[key] = pltpu.make_async_remote_copy(
            src_ref=source,
            dst_ref=target,
            send_sem=self.send_sem.at[slot],
            recv_sem=self.recv_sem.at[slot],
            device_id=device,
            device_id_type=MESH,
        )
        self.copies[key].start()

    def send(self, name, stage, source):
        dim = self.chunks[name].order[stage]
        self.remote(source, self.recv[name][stage], self.partner[dim], name, stage)

    def send_half(self, name, stage, ref):
        dim = self.chunks[name].order[stage]
        self.send(name, stage, self.half(ref, name, stage, 1 - self.mine[dim]))

    def arrived(self, *key):
        self.copies[key].wait_recv()

    def add(self, name, stage, own):
        chunk = self.chunks[name]
        got = self.recv[name][stage]
        depth = self.bits - 1 - stage
        if stage == self.bits - 1:
            value = own[...].astype(F32) + got[...].astype(F32)
            for segment in chunk.segments:
                store_segment(self.packed, self.first[segment.result], segment, value)
            return

        outer = max(depth - 2, 0)

        def step(i, carry):
            where = tuple(coordinates(i, outer))
            got[where] = got[where] + own[where]
            return carry

        lax.fori_loop(0, 2**outer, step, 0)

    def finish(self, name, stage, own=None):
        chunk = self.chunks[name]
        self.arrived(name, stage)
        if own is None:
            dim = chunk.order[stage]
            own = self.half(self.recv[name][stage - 1], name, stage, self.mine[dim])
        self.add(name, stage, own)
        self.follow(name, stage)

    def follow(self, name, stage):
        if stage + 1 < self.bits:
            self.send_half(name, stage + 1, self.recv[name][stage])

    def drain(self):
        for copy in self.copies.values():
            copy.wait_send()


BOOKS = "books"


def quantizer_semantic(r):
    sem_code = r.chosen[0]
    rows, code_width = sem_code.shape
    columns = [slice(i * HALF, (i + 1) * HALF) for i in range(r.distill_v.shape[1] // HALF)]
    for i, cols in enumerate(columns):
        r.wide[i] = dot(sem_code, r.distill_v[:, cols])

    def row_sum(parts):
        return jnp.sum(sum(parts), axis=1, keepdims=True)

    for at in row_blocks(rows, 32):
        prediction = [r.wide[i, at, :] for i in range(len(columns))]
        target = [r.wavlm_v[at, cols].astype(F32) for cols in columns]
        pred_norm = lax.rsqrt(row_sum([p * p for p in prediction]) + EPS_COS)
        target_norm = lax.rsqrt(row_sum([w * w for w in target]) + EPS_COS)
        cosine = row_sum([p * w for p, w in zip(prediction, target)]) * (pred_norm * target_norm)
        from_target = -DISTILL * pred_norm * target_norm
        from_prediction = DISTILL * cosine * pred_norm * pred_norm
        for p, w, cols in zip(prediction, target, columns):
            r.act[at, cols] = (w * from_target + p * from_prediction).astype(BF16)
    grad_pred = r.act[:, : r.distill_v.shape[1]]
    put_distill(r.places.distill, dot(sem_code.T, grad_pred))
    r.gy[:, :code_width] = dot_t(grad_pred, r.distill_v[...])


def quantizer_latent(r):
    levels, rows, code_width = r.chosen.shape
    latent_t = r.latent[...].T
    r.wide[0] = dot_t(r.gquant[...], r.pout_v[0])
    r.wide[1] = dot(r.latent[...], r.pin_v[0])
    r.wide[2] = dot_t(r.gquant[...], r.pout_v[1])
    r.wide[3] = dot(r.latent[...], r.pin_v[1])
    put_group(r.places.pout, 0, t_dot(r.chosen[0], r.gquant[...]))
    put_group(r.places.pout, 1, t_dot(r.ac[...], r.gquant[...]))
    for at in row_blocks(rows, 32):
        grad_sem = r.wide[0, at, :] + r.gy[at, :code_width]
        commit = 2.0 * BETA * (r.wide[1, at, :] - r.chosen[0, at, :].astype(F32))
        r.g_rows[0, at, :] = (grad_sem - commit).astype(BF16)
        r.grad[at, :code_width] = (grad_sem + commit).astype(BF16)
        grad_ac, residual = r.wide[2, at, :], r.wide[3, at, :]
        for level in range(1, levels):
            residual = residual - r.chosen[level, at, :].astype(F32)
        carry = jnp.zeros_like(residual)
        for level in range(levels - 1, 0, -1):
            carry = carry + 2.0 * BETA * residual
            r.g_rows[level, at, :] = (grad_ac - carry).astype(BF16)
            residual = residual + r.chosen[level, at, :].astype(F32)
        r.grad[at, code_width:] = (grad_ac + carry).astype(BF16)
    put_group(r.places.pin, 0, dot(latent_t, r.grad[:, :code_width]))
    put_group(r.places.pin, 1, dot(latent_t, r.grad[:, code_width:]))
    r.gy[...] = dot_t(r.grad[...], jnp.concatenate([r.pin_v[0], r.pin_v[1]], axis=1))


def put_group(place, group, value):
    target, rows = place.ref, value.shape[0]
    value = value.astype(target.dtype)
    if len(target.shape) == 2:
        target[group * rows : (group + 1) * rows, :] = value
        return
    lead, height = target.shape[1:-2], target.shape[-2]
    value = value.reshape(math.prod(lead), -1, height, value.shape[1])
    value = jnp.concatenate([value[:, i] for i in range(value.shape[1])], axis=2)
    columns = value.shape[2]
    where = (group,) + (slice(None),) * (len(lead) + 1) + (pl.ds(place.col, columns),)
    target[where] = value.reshape(lead + (height, columns))


def put_distill(place, value):
    target = place.ref
    if len(target.shape) == 2:
        target[...] = value.astype(target.dtype)
        return
    height = target.shape[-2]
    value = value.reshape(math.prod(target.shape[:-2]), -1, value.shape[1])
    columns = value.shape[2] * value.shape[1] // height
    value = jnp.concatenate([value[:, :, i : i + columns] for i in range(0, value.shape[2], columns)], axis=1)
    where = (slice(None),) * (len(target.shape) - 1) + (pl.ds(place.col, columns),)
    target[where] = value.astype(target.dtype).reshape(target.shape[:-1] + (columns,))


def one_hot_rows(codes, first, count):
    row = iota((count, codes.shape[1]), 0)
    return jnp.where(codes - first == row, 1.0, 0.0).astype(BF16)


def pick_codes(r):
    levels, _, entries, code_width = r.books.shape
    entries = entries * r.books.shape[1]
    rows = r.cos.shape[0]
    slots = r.ring.shape[0]
    branch = lax.axis_index("branch")
    own = r.codes[:, pl.ds(pl.multiple_of(branch * rows, rows), rows)]
    r.code_rows[...] = jnp.broadcast_to(own[:, None, :], r.code_rows.shape)
    columns = jnp.concatenate([own.astype(F32), jnp.zeros((PAIR - levels, rows), F32)], axis=0).T
    lane = iota(columns.shape, 1)
    entry = iota((rows, entries), 1)
    r.code_cols[...] = columns
    r.ac_sum[...] = jnp.zeros(r.ac_sum.shape, F32)

    def book(level):
        slot = level % slots
        return pltpu.make_async_copy(r.books.at[level], r.ring.at[slot], r.sem_book.at[slot])

    def pick(level, carry):
        code = jnp.sum(jnp.where(lane == level, r.code_cols[...], 0.0), axis=1, keepdims=True)
        one_hot = jnp.where(entry == code.astype(jnp.int32), 1.0, 0.0).astype(BF16)
        book(level).wait()
        got = dot(one_hot, r.ring[level % slots].reshape(entries, code_width))
        r.chosen[level] = got.astype(BF16)
        r.ac_sum[...] += jnp.where(level > 0, got, 0.0)

        @pl.when(level + slots < levels)
        def _():
            book(level + slots).start()

        return carry

    def begin():
        for level in range(slots):
            book(level).start()

    def run():
        lax.fori_loop(0, levels, pick, 0, unroll=4)
        r.ac[...] = r.ac_sum[...].astype(BF16)

    return begin, run


def step_kernel(chunks, first_rows, bits, ins, outs, scratch):
    r = Refs({**ins, **outs, **scratch})
    t = r.t = Refs(r.t)
    r.att, r.g_rows, r.g_got, r.book_own = (r.ring.at[i] for i in range(4))
    r.ac_sum, r.code_cols = r.acc.at[:, : r.ac.shape[1]], r.gx.at[:, :PAIR]
    branch = lax.axis_index("branch")
    rows, width = r.tokens.shape
    levels, parts, entries, code_width = r.books.shape
    entries = entries * parts
    tiles = r.w_up_v.shape[1] // TILE
    pairs = width // PAIR

    def core_rows(ref):
        half = ref.shape[0] // 2
        return ref.at[pl.ds(pl.multiple_of(mine * half, half), half)]

    def ask(own, target, key):
        sums.remote(core_rows(own.at[0]), core_rows(target.at[branch]), sums.partner[bits - 1], key)

    def relay(target, key):
        if chunks:
            sums.arrived(key)
            there = core_rows(target.at[1 - branch])
            sums.remote(there, there, sums.partner[bits - 2], key, 1)

    if chunks:
        sums = Halving(chunks, bits, r.recv, r.packed, first_rows, r.send_sem, r.recv_sem)
        mine, level = sums.mine[bits - 2], lax.axis_index("dp") // 2
        wait_barrier = sums.barrier()
    moves = Moves(r.sem_move)
    begin_pick, run_pick = pick_codes(r)
    begin_pick()
    got_pout = [moves.start(r.pout_own.at[0], r.pout_v.at[branch])]
    frame_tables(r)
    if chunks:
        wait_barrier()
        ask(r.pout_own, r.pout_v, POUT)
    else:
        got_pout.append(moves.start(r.pout_other.at[0], r.pout_v.at[1 - branch]))
    got_rest = [
        moves.start(r.distill, r.distill_v),
        moves.start(r.wavlm.at[pl.ds(pl.multiple_of(branch * rows, rows), rows)], r.wavlm_v),
    ]
    got_attention = [moves.start(r.dec_qkv, r.w_qkv_v), moves.start(r.dec_out, r.w_out_v)]
    got_ffn = [moves.start(r.dec_up, r.w_up_v), moves.start(r.dec_down, r.w_down_v)]
    got_cotangent = [moves.start(r.cotangent, r.cotangent_v)]
    got_pin = [moves.start(r.pin_own.at[0], r.pin_v.at[branch])]
    if not chunks:
        got_pin.append(moves.start(r.pin_other.at[0], r.pin_v.at[1 - branch]))
    got_tokens = [moves.start(r.tokens, r.tokens_v)]
    got_attention_two = [moves.start(r.enc_qkv, r.w_qkv_e), moves.start(r.enc_out, r.w_out_e)]

    if chunks:
        down = dict(dec=[t.dd0, t.dd1], enc=[t.ed0, t.ed1, t.ed2])
        place = r.places = Refs(
            dec_up=[Place(t.du0), Place(t.du1), Place(t.du2), Place(t.du2, TILE)],
            dec_out=Place(t.da0),
            dec_qkv=[Place(t.da0, width), Place(t.da1), Place(t.da2)],
            enc_up=[Place(t.eu0), Place(t.eu1)],
            enc_out=Place(t.ea0),
            enc_qkv=[Place(t.ea1), Place(t.ea2), Place(t.ea3)],
            distill=Place(t.di),
            pout=Place(t.misc),
            pin=Place(t.misc, width),
        )
    else:
        down = dict(dec=[t.dec_down], enc=[t.enc_down])
        place = r.places = Refs(
            dec_up=[Place(t.dec_up, i * TILE) for i in range(tiles)],
            dec_out=Place(t.dec_out),
            dec_qkv=[Place(t.dec_qkv, i * width) for i in range(3)],
            enc_up=[Place(t.enc_up, i * tiles // 2 * TILE) for i in range(2)],
            enc_out=Place(t.enc_out),
            enc_qkv=[Place(t.enc_qkv, i * width) for i in range(3)],
            distill=Place(t.distill),
            pout=Place(t.pout),
            pin=Place(t.pin),
        )
    dec_down, enc_down = down["dec"], down["enc"]

    def wait(moves, other=None):
        for move in moves:
            move.wait()
        if chunks and other is not None:
            sums.arrived(other, 1)

    def layer_value(target, gain):
        for at in row_blocks(rows, 64):
            target[at, :] = (r.x2[at, :] + gain(3) * r.fo[at, :]).astype(BF16)

    def dec_gain(i):
        return r.vectors[1, i : i + 1, :]

    def enc_gain(i):
        return r.vectors[0, i : i + 1, :]

    def pick():
        run_pick()

    def semantic():
        relay(r.pout_v, POUT)
        wait(got_rest)
        quantizer_semantic(r)

    def quant():
        wait(got_pout, POUT)
        if chunks:
            ask(r.pin_own, r.pin_v, PIN)
        r.x[...] = dot(jnp.concatenate([r.chosen[0], r.ac[...]], axis=1), r.pout_v[...].reshape(-1, width))
        if chunks:
            for other in range(1, levels):
                target = sums.near_level(other)
                sums.remote(r.code_rows.at[target_level(target)], r.code_got.at[other], target, CODES, other)
            r.code_got[0] = r.code_rows[level]

    def target_level(target):
        return next(iter(target.values())) // 2

    def dec_project():
        wait(got_attention)
        attention_project(r, r.w_qkv_v, dec_gain)

    def dec_mix():
        relay(r.pin_v, PIN)
        attention_mix(r, r.w_out_v, dec_gain)

    def dec_ffn(first, last):
        def run():
            if first == 0:
                wait(got_ffn)
                wait(got_cotangent)
                ffn_backward_begin(r, dec_gain, r.cotangent_v)
            ffn_both(r, r.w_up_v, r.w_down_v, place.dec_up, dec_down, first, last)
            if last == tiles:
                r.fo[...] = dot(r.act[...], r.w_down_v[...])
                layer_value(r.decoded, dec_gain)
                ffn_back_sum(r, r.w_up_v)
                ffn_backward_end(r, dec_gain, r.cotangent_v, r.dec_gains)
                got_ffn[:] = [moves.start(r.enc_up, r.w_up_v), moves.start(r.enc_down, r.w_down_v)]

        return run

    def dec_out():
        attention_backward_out(r, r.w_out_v, dec_gain, place.dec_out, r.dec_gains)

    def attention_pairs(first, last):
        return lambda: attention_backward_pairs(r, first, last)

    def dec_in(part):
        def run():
            attention_backward_in(r, place.dec_qkv[part], part)
            if part == 2:
                attention_backward_end(r, r.w_qkv_v, dec_gain, r.dec_gains)
                r.gquant[...] = r.gx[...].astype(BF16)

        return run

    def enc_project():
        wait(got_tokens)
        r.x[...] = r.tokens_v[...].astype(F32)
        wait(got_attention_two)
        attention_project(r, r.w_qkv_e, enc_gain)

    def enc_mix():
        attention_mix(r, r.w_out_e, enc_gain)

    def enc_ffn():
        wait(got_ffn)
        ffn_forward(r, r.w_up_v, r.w_down_v)
        layer_value(r.latent, enc_gain)

    def quantizer():
        wait(got_pin, PIN)
        quantizer_latent(r)
        if chunks:
            for other in reversed(range(1, levels)):
                target = sums.near_level(other)
                sums.arrived(CODES, other)
                sums.remote(r.g_rows.at[target_level(target)], r.g_got.at[other], target, BOOKS, 0, other)
            r.g_got[0] = r.g_rows[level]

    def book_half(core, put):
        quarter = entries // 4
        for side in range(2):
            r.book_sum[...] = jnp.zeros_like(r.book_sum)
            first = (core * 2 + side) * quarter

            def add(source, carry):
                one_hot = one_hot_rows(r.code_got[source, 0:1, :], first, quarter)
                r.book_sum[...] += dot(one_hot, r.g_got[source])
                return carry

            lax.fori_loop(0, levels, add, 0, unroll=4)
            put(side, r.book_sum[...])

    def finish_books(stage):
        blocks = entries // 4 // rows
        other_core, other_side = sums.partner[bits - 2], sums.partner[bits - 1]
        if stage == 0:
            for other in range(1, levels):
                sums.arrived(BOOKS, 0, other)

            def put(side, value):
                r.book_send[side] = value.astype(BF16)

            def keep(side, value):
                r.book_own[side * blocks : (side + 1) * blocks] = value.astype(BF16).reshape((blocks, rows, code_width))

            book_half(1 - mine, put)
            sums.remote(r.book_send, r.book_got, other_core, BOOKS, 1)
            book_half(mine, keep)
        elif stage == 1:
            sums.arrived(BOOKS, 1)
            for side in range(2):
                own = r.book_own[side * blocks : (side + 1) * blocks]
                r.book_got[side] = r.book_got[side] + own.reshape(r.book_got.shape[1:])
            sums.remote(r.book_got.at[1 - branch], r.book_last, other_side, BOOKS, 2)
        else:
            sums.arrived(BOOKS, 2)
            total = r.book_got[branch].astype(F32) + r.book_last[...].astype(F32)
            blocks = code_width // 128
            store_segment(r.packed, first_rows[BOOKS], Segment(BOOKS, 0, blocks, 0, blocks, 0, entries // 4), total)

    def all_books():
        parts = entries // TILE

        def one(step, carry):
            at = step // parts
            one_hot = one_hot_rows(r.code_rows[at, 0:1, :], step % parts * TILE, TILE)
            t.books[at, aligned(step % parts, TILE), :] = dot(one_hot, r.g_rows[at]).astype(BF16)
            return carry

        lax.fori_loop(0, levels * parts, one, 0)

    def enc_ffn_back(half):
        def run():
            first, last = half * tiles // 2, (half + 1) * tiles // 2
            if half == 0:
                ffn_backward_begin(r, enc_gain, r.gy)
            ffn_backward_tiles(r, r.w_down_v, place.enc_up[half], enc_down, first, last)
            if half == 1:
                ffn_back_sum(r, r.w_up_v)
                ffn_backward_end(r, enc_gain, r.gy, r.gains)

        return run

    def enc_out():
        attention_backward_out(r, r.w_out_e, enc_gain, place.enc_out, r.gains)

    def enc_in(part):
        def run():
            attention_backward_in(r, place.enc_qkv[part], part)
            if part == 2:
                attention_backward_end(r, r.w_qkv_e, enc_gain, r.gains)
                r.grad_tokens[...] = r.gx[...]
                if chunks:
                    spread_gains()

        return run

    def spread_gains():
        lanes = pl.ds(width, 128)
        for layer, ref in enumerate((r.gains, r.dec_gains)):
            for row in range(4):
                for block in range(width // 128):
                    owner = (layer * 4 + row) * (width // 128) + block
                    where = tuple(owner // 2 ** (bits - 1 - i) % 2 for i in range(bits))
                    value = ref[row : row + 1, block * 128 : (block + 1) * 128]
                    rows_here = t.ea3.shape[bits]
                    t.ea3[where + (slice(None), lanes)] = jnp.broadcast_to(value, (rows_here, 128)).astype(BF16)

    work = [
        (5.5, pick, ()),
        (1.5, semantic, (DISTILL_GRAD,)),
        (0.7, quant, ()),
        (1.2, dec_project, ()),
        (2.0, dec_mix, ()),
        (1.2, dec_ffn(0, 1), (DU0,)),
        (1.2, dec_ffn(1, 2), (DU1,)),
        (2.6, dec_ffn(2, tiles), (DD0, DD1, DU2)),
        (1.0, dec_out, ()),
        (1.4, attention_pairs(0, pairs // 2), ()),
        (1.4, attention_pairs(pairs // 2, pairs), ()),
        (0.5, dec_in(0), (DA0,)),
        (0.5, dec_in(1), (DA1,)),
        (0.9, dec_in(2), (DA2,)),
        (1.2, enc_project, ()),
        (2.0, enc_mix, ()),
        (2.2, enc_ffn, ()),
        (2.2, quantizer, (BOOKS, MISC)),
        (1.7, enc_ffn_back(0), (EU0,)),
        (2.0, enc_ffn_back(1), (EU1, ED0, ED1, ED2)),
        (1.0, enc_out, (EA0,)),
        (1.4, attention_pairs(0, pairs // 2), ()),
        (1.4, attention_pairs(pairs // 2, pairs), ()),
        (0.5, enc_in(0), (EA1,)),
        (0.5, enc_in(1), (EA2,)),
        (1.0, enc_in(2), (EA3,)),
    ]
    if not chunks:
        for _, run, _ in work:
            run()
            if run is quantizer:
                all_books()
        return
    actions = plan(chunks, work, bits, rows * code_width * 2)

    def finish(name, stage):
        if name == BOOKS:
            finish_books(stage)
        elif stage == 0:
            sums.finish(name, 0, sums.half(t[name], name, 0, mine))
        else:
            sums.finish(name, stage)

    for (_, run, made), acts in zip(work, actions):
        run()
        for name in made:
            if name != BOOKS:
                sums.send_half(name, 0, t[name])
        for name, stage in acts:
            finish(name, stage)
    for name, stage in actions[-1]:
        finish(name, stage)
    sums.drain()


POUT, PIN, CODES = 1, 2, 3
DISTILL_GRAD = "di"
DD0, DD1, DU0, DU1, DU2 = "dd0", "dd1", "du0", "du1", "du2"
DA0, DA1, DA2, MISC = "da0", "da1", "da2", "misc"
EU0, EU1, ED0, ED1, ED2 = "eu0", "eu1", "ed0", "ed1", "ed2"
EA0, EA1, EA2, EA3 = "ea0", "ea1", "ea2", "ea3"


def step(given, devices, with_sums):
    rows, width = given.tokens.shape
    ff = given.enc_up.shape[1]
    levels, entries, code_width = given.books.shape
    given.books = given.books.reshape(levels, -1, rows, code_width)
    bits = devices.bit_length() - 1
    vmem, hbm = pl.BlockSpec(memory_space=pltpu.VMEM), pl.BlockSpec(memory_space=pl.ANY)
    scratch = layer_scratch(rows, width, ff)
    scratch.update(
        w_qkv_e=pltpu.VMEM((width, 3 * width), BF16),
        w_out_e=pltpu.VMEM((width, width), BF16),
        cos=pltpu.VMEM((rows, PAIR), F32),
        sin=pltpu.VMEM((rows, PAIR), F32),
        bias=pltpu.VMEM((rows, rows), F32),
        ring=pltpu.VMEM((4,) + given.books.shape[1:], BF16),
        code_rows=pltpu.VMEM((levels, 8, rows), jnp.int32),
        chosen=pltpu.VMEM((levels, rows, code_width), BF16),
        ac=pltpu.VMEM((rows, code_width), BF16),
        gquant=pltpu.VMEM((rows, width), BF16),
        gy=pltpu.VMEM((rows, width), F32),
        latent=pltpu.VMEM((rows, width), BF16),
        pin_v=pltpu.VMEM((2, width, code_width), BF16),
        pout_v=pltpu.VMEM((2, code_width, width), BF16),
        distill_v=pltpu.VMEM(given.distill.shape, BF16),
        wavlm_v=pltpu.VMEM((rows, given.wavlm.shape[1]), BF16),
        tokens_v=pltpu.VMEM((rows, width), BF16),
        cotangent_v=pltpu.VMEM((rows, width), BF16),
        sem_move=pltpu.SemaphoreType.DMA((14,)),
        sem_book=pltpu.SemaphoreType.DMA((4,)),
    )
    outs = Refs(decoded=shaped((rows, width), BF16), grad_tokens=shaped((rows, width), F32))
    chunks, first_rows = {}, {}
    params = dict(vmem_limit_bytes=60 * 2**20)
    if with_sums:
        params.update(collective_id=0, has_side_effects=True)
        c, x, y = bits - 2, bits - 1, bits - 3
        b, a = range(y)
        share = width // devices
        low, high = ff // devices, share
        wide, half, blocks = ff // 128, ff // 256, width // 128
        third, quarter = 3 * blocks, blocks // 4
        chunks = dict(
            di=Chunk(
                high,
                width,
                [c, x, y, a, b],
                [
                    Segment(8, 0, 2 * blocks, 0, blocks, 0, high // 2),
                    Segment(8, blocks, 2 * blocks, 0, blocks, high // 2, high // 2),
                ],
            ),
            du0=Chunk(high, ff // 4, [c, y, x, a, b], [Segment(2, 0, wide, 0, half // 2, 0, high)]),
            du1=Chunk(high, ff // 4, [c, a, x, b, y], [Segment(2, half // 2, wide, 0, half // 2, 0, high)]),
            dd0=Chunk(low, width // 2, [c, x, a, b, y], [Segment(3, 0, blocks, 0, 2 * quarter, 0, low)]),
            dd1=Chunk(low, width // 2, [c, y, x, a, b], [Segment(3, 2 * quarter, blocks, 0, 2 * quarter, 0, low)]),
            du2=Chunk(high, ff // 2, [c, a, y, x, b], [Segment(2, half, wide, 0, half, 0, high)]),
            da0=Chunk(
                high,
                2 * width,
                [c, x, y, a, b],
                [Segment(1, 0, blocks, 0, blocks, 0, high), Segment(0, 0, third, width, blocks, 0, high)],
            ),
            da1=Chunk(high, width, [c, x, y, a, b], [Segment(0, blocks, third, 0, blocks, 0, high)]),
            da2=Chunk(high, width, [c, y, a, b, x], [Segment(0, 2 * blocks, third, 0, blocks, 0, high)]),
            misc=Chunk(
                high,
                2 * width,
                [c, x, y, a, b],
                [
                    Segment(9, 0, blocks, 0, blocks, 0, high),
                    Segment(10, 0, blocks // 2, width, blocks // 2, 0, high),
                    Segment(10, high * blocks // 2, blocks // 2, width + code_width, blocks // 2, 0, high),
                ],
            ),
            eu0=Chunk(high, ff // 2, [c, x, y, a, b], [Segment(6, 0, wide, 0, half, 0, high)]),
            eu1=Chunk(high, ff // 2, [c, y, x, a, b], [Segment(6, half, wide, 0, half, 0, high)]),
            ed0=Chunk(low, width // 2, [c, x, y, a, b], [Segment(7, 0, blocks, 0, 2 * quarter, 0, low)]),
            ed1=Chunk(low, width // 4, [c, x, a, y, b], [Segment(7, 2 * quarter, blocks, 0, quarter, 0, low)]),
            ed2=Chunk(low, width // 4, [c, x, y, a, b], [Segment(7, 3 * quarter, blocks, 0, quarter, 0, low)]),
            ea0=Chunk(high, width, [c, x, y, a, b], [Segment(5, 0, blocks, 0, blocks, 0, high)]),
            ea1=Chunk(high, width, [c, x, y, a, b], [Segment(4, 0, third, 0, blocks, 0, high)]),
            ea2=Chunk(high, width, [c, y, x, a, b], [Segment(4, blocks, third, 0, blocks, 0, high)]),
            ea3=Chunk(
                high,
                width + 128,
                [c, a, x, y, b],
                [Segment(4, 2 * blocks, third, 0, blocks, 0, high), Segment(11, 0, 1, width, 1, 0, 8)],
            ),
        )
        rows_of = [high * 3 * blocks, high * blocks, high * wide, low * blocks] * 2
        rows_of += [high * blocks, high * blocks, high * blocks, 8, entries // 4 * code_width // 128]
        first_rows = {i: sum(rows_of[:i]) for i in range(len(rows_of))}
        first_rows[BOOKS] = first_rows[len(rows_of) - 1]
        copies = len(chunks) * bits + 2 * levels + 4
        scratch.update(
            t={name: pltpu.VMEM(c.shape(bits), BF16) for name, c in chunks.items()},
            recv={
                name: [pltpu.VMEM(c.shape(bits - 1 - stage), BF16) for stage in range(bits)]
                for name, c in chunks.items()
            },
            gains=pltpu.VMEM((4, width), F32),
            dec_gains=pltpu.VMEM((4, width), F32),
            code_got=pltpu.VMEM((levels, 8, rows), jnp.int32),
                book_sum=pltpu.VMEM((entries // 4, code_width), F32),
            book_send=pltpu.VMEM((2, entries // 4, code_width), BF16),
            book_got=pltpu.VMEM((2, entries // 4, code_width), BF16),
            book_last=pltpu.VMEM((entries // 4, code_width), BF16),
            send_sem=pltpu.SemaphoreType.DMA((copies,)),
            recv_sem=pltpu.SemaphoreType.DMA((copies,)),
        )
        outs.packed = shaped((sum(rows_of), 128), F32)
    else:
        outs.update(gains=shaped((4, width), F32), dec_gains=shaped((4, width), F32))
        outs.t = dict(
            enc_qkv=shaped(given.enc_qkv.shape, BF16),
            enc_out=shaped(given.enc_out.shape, BF16),
            enc_up=shaped(given.enc_up.shape, BF16),
            enc_down=shaped(given.enc_down.shape, BF16),
            dec_qkv=shaped(given.enc_qkv.shape, BF16),
            dec_out=shaped(given.enc_out.shape, BF16),
            dec_up=shaped(given.enc_up.shape, BF16),
            dec_down=shaped(given.enc_down.shape, BF16),
            pin=shaped((2 * width, code_width), BF16),
            pout=shaped((2 * code_width, width), BF16),
            books=shaped((levels, entries, code_width), BF16),
            distill=shaped(given.distill.shape, BF16),
        )
    in_specs = dict.fromkeys(given, hbm)
    in_specs.update(
        lengths=pl.BlockSpec(memory_space=pltpu.SMEM), codes=vmem, vectors=vmem
    )
    got = pl.pallas_call(
        functools.partial(step_kernel, chunks, first_rows, bits),
        out_shape={k: pltpu.VMEM(v.shape, v.dtype) for k, v in outs.items()} if with_sums else dict(outs),
        in_specs=[in_specs],
        out_specs=jax.tree.map(lambda _: vmem, dict(outs)),
        scratch_shapes=[dict(scratch)],
        compiler_params=pltpu.CompilerParams(**params),
        name="step",
    )(dict(given))
    got = Refs(got)
    if not with_sums:
        return got
    last = [shaped((rows, 128), F32) for rows in rows_of]
    last[11] = shaped((1, 128), F32)

    def hand_on(packed, decoded, grad, *refs):
        outs, moves = refs[:-1], Moves(refs[-1])
        parts = [packed.at[pl.ds(first_rows[i], ref.shape[0])] for i, ref in enumerate(outs[:-2])]
        leaving = [moves.start(part, ref) for part, ref in zip(parts + [decoded, grad], outs)]
        for move in leaving:
            move.wait()

    return pl.pallas_call(
        hand_on,
        out_shape=last + [outs.decoded, outs.grad_tokens],
        in_specs=[vmem] * 3,
        out_specs=[hbm] * (len(last) + 2),
        scratch_shapes=[pltpu.SemaphoreType.DMA((len(last) + 2,))],
        compiler_params=pltpu.CompilerParams(vmem_limit_bytes=16 * 2**20),
        name="results",
    )(got.packed, got.decoded, got.grad_tokens)


def body(
    tokens,
    wavlm,
    cotangent,
    lengths,
    codes,
    enc_qkv,
    enc_out,
    enc_up,
    enc_down,
    dec_qkv,
    dec_out,
    dec_up,
    dec_down,
    vectors,
    proj_in,
    proj_out,
    codebooks,
    distill_proj,
):
    width = tokens.shape[1]
    devices = lax.axis_size("dp") * lax.axis_size("branch")
    with_sums = devices == 4 * codebooks.shape[0] and width // devices % 16 == 0
    given = Refs(
        tokens=tokens,
        wavlm=wavlm,
        cotangent=cotangent,
        lengths=lengths,
        codes=codes.T,
        enc_qkv=enc_qkv,
        enc_out=enc_out,
        enc_up=enc_up,
        enc_down=enc_down,
        dec_qkv=dec_qkv,
        dec_out=dec_out,
        dec_up=dec_up,
        dec_down=dec_down,
        vectors=vectors,
        pin_own=proj_in,
        pout_own=proj_out,
        books=codebooks,
        distill=distill_proj,
    )
    if with_sums:
        *sums, decoded, grad_tokens = step(given, devices, True)
        sums = [part.reshape(-1) for part in sums]
        order = (4, 5, 6, 7, 0, 1, 2, 3, 11, 10, 9, 12, 8)
        return (decoded, grad_tokens, *[sums[i] for i in order])
    swap = [(0, 1), (1, 0)]
    given.pin_other = lax.ppermute(proj_in, "branch", swap)
    given.pout_other = lax.ppermute(proj_out, "branch", swap)
    s = step(given, devices, False)
    t = Refs(s.t)
    gains = jnp.concatenate([s.gains, s.dec_gains])
    local = [t.enc_qkv, t.enc_out, t.enc_up, t.enc_down, t.dec_qkv, t.dec_out, t.dec_up, t.dec_down]
    local += [gains, t.pin, t.pout, t.books, t.distill]
    sums = [
        lax.psum_scatter(part.astype(F32).reshape(-1), ("dp", "branch"), scatter_dimension=0, tiled=True)
        for part in local
    ]
    return (s.decoded, s.grad_tokens, *sums)


def solution(mesh):
    rows, whole = P(("dp", "branch"), None), P()
    placed = (rows, P("dp", None), rows, rows, P("dp", None)) + (whole,) * 9
    placed += (P("branch", None, None),) * 2 + (whole,) * 2
    return jax.shard_map(
        body,
        mesh=mesh,
        in_specs=placed,
        out_specs=(rows, rows) + (P(("dp", "branch")),) * 13,
        check_vma=False,
    )
```

```python
import functools
import math

import jax
import jax.numpy as jnp
from jax import lax
from jax.experimental import pallas as pl
from jax.experimental.pallas import tpu as pltpu
from jax.sharding import PartitionSpec as P

HEADS = 8
WINDOW = 250
EPS_NORM = 1e-05
EPS_COS = 1e-06
BETA = 0.25
DISTILL = 10.0
ROPE_BASE = 10000.0

MESH = pl.DeviceIdType.MESH
F32 = jnp.float32
BF16 = jnp.bfloat16
TILE = 512
PAIR = 128
HALF = 256


def dot(left, right):
    return lax.dot_general(left, right, (((1,), (0,)), ((), ())), preferred_element_type=F32)


def dot_t(left, right):
    return lax.dot_general(left, right, (((1,), (1,)), ((), ())), preferred_element_type=F32)


def t_dot(left, right):
    return lax.dot_general(left, right, (((0,), (0,)), ((), ())), preferred_element_type=F32)


def iota(shape, dim):
    return lax.broadcasted_iota(jnp.int32, shape, dim)


def aligned(index, size):
    return pl.ds(pl.multiple_of(index * size, size), size)


class Refs(dict):
    __getattr__ = dict.__getitem__
    __setattr__ = dict.__setitem__


class Moves:
    def __init__(self, semaphores):
        self.semaphores, self.count = semaphores, 0

    def start(self, source, target):
        move = pltpu.make_async_copy(source, target, self.semaphores.at[self.count])
        self.count += 1
        move.start()
        return move


def layer_scratch(rows, width, ff):
    return Refs(
        x=pltpu.VMEM((rows, width), F32),
        s1=pltpu.VMEM((rows, 1), F32),
        h=pltpu.VMEM((rows, width), BF16),
        h1t=pltpu.VMEM((width, rows), BF16),
        h2t=pltpu.VMEM((width, rows), BF16),
        rinv=pltpu.VMEM((rows, width), F32),
        qkv=pltpu.VMEM((rows, 3 * width), BF16),
        mix=pltpu.VMEM((rows, width), BF16),
        ao=pltpu.VMEM((rows, width), F32),
        x2=pltpu.VMEM((rows, width), F32),
        s2=pltpu.VMEM((rows, 1), F32),
        act=pltpu.VMEM((rows, ff), BF16),
        dg=pltpu.VMEM((rows, ff), BF16),
        fo=pltpu.VMEM((rows, width), F32),
        grad=pltpu.VMEM((rows, width), BF16),
        gx=pltpu.VMEM((rows, width), F32),
        acc=pltpu.VMEM((rows, width), F32),
        wide=pltpu.VMEM((4, rows, HALF), F32),
        change=pltpu.VMEM((2, rows, rows), BF16),
        w_qkv_v=pltpu.VMEM((width, 3 * width), BF16),
        w_out_v=pltpu.VMEM((width, width), BF16),
        w_up_v=pltpu.VMEM((width, ff), BF16),
        w_down_v=pltpu.VMEM((ff, width), BF16),
    )


def shaped(shape, kind):
    return jax.ShapeDtypeStruct(shape, kind)


def frame_tables(r):
    rows = r.cos.shape[0]
    place = iota((rows, PAIR), 0)
    query, key = iota((rows, rows), 0), iota((rows, rows), 1)
    begin, begin_query = jnp.zeros_like(place), jnp.zeros_like(query)
    edge = 0
    for clip in range(r.lengths.shape[1] - 1):
        edge = edge + r.lengths[0, clip]
        begin = jnp.where(place >= edge, edge, begin)
        begin_query = jnp.where(query >= edge, edge, begin_query)
    allowed = (key >= begin_query) & (key <= query) & (query - key < WINDOW)
    r.bias[...] = jnp.where(allowed, 0.0, -1e30)
    lane = iota((rows, PAIR), 1)
    rate = jnp.exp((lane % 32).astype(F32) * (-math.log(ROPE_BASE) / 32))
    angle = (place - begin).astype(F32) * rate
    r.cos[...] = jnp.cos(angle)
    sine = jnp.sin(angle)
    r.sin[...] = jnp.where(lane % 64 < 32, -sine, sine)


def rotated(value, cosine, sine):
    lane = iota(value.shape, 1)
    swapped = jnp.where(lane % 64 < 32, pltpu.roll(value, PAIR - 32, 1), pltpu.roll(value, 32, 1))
    return value * cosine + swapped * sine


def head_masks(rows):
    low = iota((rows, PAIR), 1) < 64
    return (jnp.where(low, 1.0, 0.0).astype(BF16), jnp.where(low, 0.0, 1.0).astype(BF16))


def row_blocks(rows, step):
    return [slice(i, i + step) for i in range(0, rows, step)]


def attention_project(r, w_qkv, gain):
    rows, width = r.x.shape
    scale = gain(0)
    for at in row_blocks(rows, 64):
        x = r.x[at, :]
        s1 = lax.rsqrt(jnp.mean(x * x, axis=1, keepdims=True) + EPS_NORM)
        r.s1[at, :] = s1
        r.h[at, :] = (x * s1 * scale).astype(BF16)
    for half in range(3 * width // HALF):
        slot, part = half % 4, half // (width // HALF)
        cols = slice(half * HALF, (half + 1) * HALF)
        r.wide[slot] = dot(r.h[...], w_qkv[:, cols])
        for at in row_blocks(rows, 64):
            for p in range(HALF // PAIR):
                value = r.wide[slot, at, p * PAIR : (p + 1) * PAIR]
                if part < 2:
                    value = rotated(value, r.cos[at, :], r.sin[at, :])
                low = value.astype(BF16)
                if part == 0:
                    low = (low.astype(F32) * 0.125).astype(BF16)
                r.qkv[at, half * HALF + p * PAIR : half * HALF + (p + 1) * PAIR] = low
    r.h1t[...] = r.h[...].T


def attention_mix(r, w_out, gain):
    rows, width = r.x.shape
    masks = head_masks(rows)
    low = iota((rows, PAIR), 1) < 64
    pairs = width // PAIR
    for p in range(pairs):
        query = r.qkv[:, p * PAIR : (p + 1) * PAIR]
        key = r.qkv[:, (p + pairs) * PAIR : (p + pairs + 1) * PAIR]
        value = r.qkv[:, (p + 2 * pairs) * PAIR : (p + 2 * pairs + 1) * PAIR]
        outs = []
        for h in range(2):
            head = 2 * p + h
            slot = head % 4
            r.wide[slot] = dot_t(query * masks[h], key)
            for at in row_blocks(rows, 64):
                seen = PAIR if at.stop <= PAIR else rows
                scores = r.wide[slot, at, :seen] + r.bias[at, :seen]
                weights = jnp.exp(scores - jnp.max(scores, axis=1, keepdims=True))
                r.att[head, at, :seen] = weights.astype(BF16)
                if seen < rows:
                    r.att[head, at, seen:] = jnp.zeros((64, rows - seen), BF16)
            outs.append(dot(r.att[head], value * masks[h] + masks[1 - h]))
        inverse = 1.0 / pltpu.roll(jnp.where(low, outs[1], outs[0]), 64, 1)
        r.rinv[:, p * PAIR : (p + 1) * PAIR] = inverse
        r.mix[:, p * PAIR : (p + 1) * PAIR] = (jnp.where(low, outs[0], outs[1]) * inverse).astype(BF16)
    r.ao[...] = dot(r.mix[...], w_out[...])
    scale_one, scale_two = gain(1), gain(2)
    for at in row_blocks(rows, 64):
        x2 = r.x[at, :] + scale_one * r.ao[at, :]
        r.x2[at, :] = x2
        s2 = lax.rsqrt(jnp.mean(x2 * x2, axis=1, keepdims=True) + EPS_NORM)
        r.s2[at, :] = s2
        r.h[at, :] = (x2 * s2 * scale_two).astype(BF16)
    r.h2t[...] = r.h[...].T


def gelu_parts(pre):
    slope = math.sqrt(2.0 / math.pi)
    square = pre * pre
    bent = jnp.tanh(slope * pre * (1.0 + 0.044715 * square))
    half = 0.5 * (1.0 + bent)
    turn = 0.5 * pre * (1.0 - bent * bent) * slope * (1.0 + 3.0 * 0.044715 * square)
    return (pre * half).astype(BF16), half + turn


def ffn_forward(r, w_up, w_down):
    rows, ff = r.act.shape
    for half in range(ff // HALF):
        slot, cols = half % 4, slice(half * HALF, (half + 1) * HALF)
        r.wide[slot] = dot(r.h[...], w_up[:, cols])
        for at in row_blocks(rows, 32):
            act, slope = gelu_parts(r.wide[slot, at, :])
            r.act[at, cols] = act
            r.dg[at, cols] = slope.astype(BF16)
    r.fo[...] = dot(r.act[...], w_down[...])


def ffn_both(r, w_up, w_down, grad_up, grad_down, first, last):
    rows = r.act.shape[0]
    for t in range(first, last):
        cols = slice(t * TILE, (t + 1) * TILE)
        for side in range(TILE // HALF):
            part = slice(t * TILE + side * HALF, t * TILE + (side + 1) * HALF)
            r.wide[side] = dot(r.h[...], w_up[:, part])
            r.wide[2 + side] = dot_t(r.grad[...], w_down[part, :])
            for at in row_blocks(rows, 32):
                act, slope = gelu_parts(r.wide[side, at, :])
                r.act[at, part] = act
                r.dg[at, part] = (r.wide[2 + side, at, :] * slope).astype(BF16)
        grad_up.shift((t - first) * TILE).put(dot(r.h2t[...], r.dg[:, cols]))
        put_rows(grad_down, t_dot(r.act[:, cols], r.grad[...]), t)


def ffn_back_sum(r, w_up):
    r.acc[...] = dot_t(r.dg[...], w_up[...])


def norm_back(stream, inverse, grad):
    mean = jnp.mean(grad * stream, axis=1, keepdims=True)
    return inverse * grad - stream * (inverse * inverse * inverse * mean)


def column_sum(value):
    return jnp.sum(value, axis=0, keepdims=True)


class Place:
    def __init__(self, ref, col=0):
        self.ref, self.col = ref, col

    def shift(self, by):
        return Place(self.ref, self.col + by)

    def put(self, value):
        shape = self.ref.shape
        value = value.astype(self.ref.dtype).reshape(shape[:-1] + (value.shape[1],))
        self.ref[(slice(None),) * (len(shape) - 1) + (pl.ds(self.col, value.shape[-1]),)] = value


def put_rows(targets, value, tile):
    value = value.astype(BF16)
    begin = 0
    for target in targets:
        shape = target.shape
        part = value[:, begin : begin + shape[-1]]
        begin += shape[-1]
        if len(shape) == 2:
            target[aligned(tile, value.shape[0]), :] = part
        else:
            target[tile // 2, tile % 2] = part.reshape(shape[2:])


def ffn_backward_begin(r, gain, gy_ref):
    scale = gain(3)
    for at in row_blocks(r.grad.shape[0], 64):
        r.grad[at, :] = (scale * gy_ref[at, :].astype(F32)).astype(BF16)


def ffn_backward_tiles(r, w_down, grad_up, grad_down, first, last):
    rows = r.act.shape[0]
    for t in range(first, last):
        cols = slice(t * TILE, (t + 1) * TILE)
        for side in range(TILE // HALF):
            part = slice(t * TILE + side * HALF, t * TILE + (side + 1) * HALF)
            slot = (2 * t + side) % 4
            r.wide[slot] = dot_t(r.grad[...], w_down[part, :])
            for at in row_blocks(rows, 64):
                r.dg[at, part] = (r.wide[slot, at, :] * r.dg[at, part].astype(F32)).astype(BF16)
        put_rows(grad_down, t_dot(r.act[:, cols], r.grad[...]), t)
        grad_up.shift((t - first) * TILE).put(dot(r.h2t[...], r.dg[:, cols]))


def ffn_backward_end(r, gain, gy_ref, gain_out):
    scale = gain(2)
    to_gain = to_scale = 0.0
    for at in row_blocks(r.x2.shape[0], 32):
        gy = gy_ref[at, :].astype(F32)
        to_scale = to_scale + column_sum(gy * r.fo[at, :])
        back, x2, s2 = r.acc[at, :], r.x2[at, :], r.s2[at, :]
        to_gain = to_gain + column_sum(back * x2 * s2)
        r.gx[at, :] = gy + norm_back(x2, s2, back * scale)
    gain_out[3:4, :] = to_scale
    gain_out[2:3, :] = to_gain


def attention_backward_out(r, w_out, gain, grad_out, gain_out):
    scale = gain(1)
    to_scale = 0.0
    for at in row_blocks(r.gx.shape[0], 64):
        gx = r.gx[at, :]
        to_scale = to_scale + column_sum(gx * r.ao[at, :])
        r.grad[at, :] = (scale * gx).astype(BF16)
    gain_out[1:2, :] = to_scale
    grad_out.put(t_dot(r.mix[...], r.grad[...]))
    r.grad[...] = dot_t(r.grad[...], w_out[...]).astype(BF16)


def attention_backward_pairs(r, first, last):
    rows, width = r.x.shape
    masks = head_masks(rows)
    masks_t = [jnp.where((iota((PAIR, rows), 0) < 64) == (h == 0), 1.0, 0.0).astype(BF16) for h in range(2)]
    pairs = width // PAIR
    for p in range(first, last):
        lanes = [slice((p + i * pairs) * PAIR, (p + i * pairs + 1) * PAIR) for i in range(3)]
        query, key, value = (r.qkv[:, at] for at in lanes)
        grad_mixed = (r.grad[:, lanes[0]].astype(F32) * r.rinv[:, lanes[0]]).astype(BF16)
        product = (grad_mixed.astype(F32) * r.mix[:, lanes[0]].astype(F32)).astype(BF16)
        beside = jnp.concatenate([value, jnp.full(value.shape, -1.0, BF16)], axis=1)
        query_t, grad_t = query.T, grad_mixed.T
        to_query = to_key = to_value = 0.0
        for h in range(2):
            head = 2 * p + h
            slot = head % 4
            both = jnp.concatenate([grad_mixed * masks[h], product * masks[h]], axis=1)
            r.wide[slot] = dot_t(both, beside)
            for at in row_blocks(rows, 64):
                r.change[h, at, :] = (r.att[head, at, :].astype(F32) * r.wide[slot, at, :]).astype(BF16)
            to_query = to_query + dot(r.change[h], key * masks[h])
            to_key = to_key + dot(query_t * masks_t[h], r.change[h])
            to_value = to_value + dot(grad_t * masks_t[h], r.att[head])
        cosine, sine = r.cos[...], -r.sin[...]
        r.qkv[:, lanes[0]] = rotated(to_query * 0.125, cosine, sine).astype(BF16)
        r.qkv[:, lanes[1]] = rotated(to_key.T, cosine, sine).astype(BF16)
        r.qkv[:, lanes[2]] = to_value.T.astype(BF16)


def attention_backward_in(r, grad_qkv, part):
    width = r.x.shape[1]
    grad_qkv.put(dot(r.h1t[...], r.qkv[:, part * width : (part + 1) * width]))


def attention_backward_end(r, w_qkv, gain, gain_out):
    r.acc[...] = dot_t(r.qkv[...], w_qkv[...])
    scale = gain(0)
    to_gain = 0.0
    for at in row_blocks(r.x.shape[0], 32):
        back, x, s1 = r.acc[at, :], r.x[at, :], r.s1[at, :]
        to_gain = to_gain + column_sum(back * x * s1)
        r.gx[at, :] = r.gx[at, :] + norm_back(x, s1, back * scale)
    gain_out[0:1, :] = to_gain


class Segment:
    def __init__(self, result, base, stride, col, blocks, row, rows):
        self.result, self.base, self.stride, self.col, self.blocks = result, base, stride, col, blocks
        self.row, self.rows = row, rows


class Chunk:
    def __init__(self, rows, columns, order, segments):
        self.rows, self.columns, self.order, self.segments = rows, columns, order, segments

    def shape(self, leading):
        return (2,) * leading + (self.rows, self.columns)

    def bytes(self, bits):
        return 2**bits * self.rows * self.columns * 2


def plan(chunks, work, bits, book_bytes):
    core, x, y = bits - 2, bits - 1, bits - 3
    ends, middle = -1, -2
    free, pending, done = {}, [], []
    now = 0.0

    def carry(link, size, rate=42e3):
        free[link] = max(now, free.get(link, 0.0)) + size / rate
        return free[link]

    def begin(name, stage):
        if name == BOOKS:
            size = 1.2 * 2 ** (bits - 3) * book_bytes
            if stage == 0:
                there = max(carry(y, size), carry(ends, 1.5 * size), carry(middle, 2 * size))
            else:
                there = carry(core, 4 * book_bytes, 400e3) if stage == 1 else carry(x, 2 * book_bytes)
        else:
            dim = chunks[name].order[stage]
            size = chunks[name].bytes(bits) / 2 ** (stage + 1)
            if dim == core:
                there = carry(core, size, 400e3)
            elif dim == x or dim == y:
                there = carry(dim, size)
            else:
                there = carry(ends, size)
                if dim < y - 1:
                    there = max(there, carry(middle, 2 * size))
        pending.append((there + 1.5, name, stage))

    def finish(limit):
        nonlocal now
        acts = []
        while pending:
            pending.sort(key=lambda p: p[0])
            if pending[0][0] + (0.5 if limit < math.inf else 0.0) > limit:
                break
            at, name, stage = pending.pop(0)
            if name == BOOKS:
                cost = (6.0, 0.6, 0.3)[stage]
            else:
                cost = 0.25 + 0.3e-6 * chunks[name].bytes(bits) / 2 ** (stage + 1)
            now = max(now, at) + cost
            limit = max(limit, now)
            acts.append((name, stage))
            if stage + 1 < (3 if name == BOOKS else bits):
                begin(name, stage + 1)
        return acts

    for took, _, names in work:
        now += 0.95 * took
        for name in names:
            begin(name, 0)
        done.append(finish(now))
    done.append(finish(math.inf))
    return done


def coordinates(step, count):
    return [step // 2 ** (count - 1 - i) % 2 for i in range(count)]


def store_segment(packed, first, segment, value):
    for i in range(segment.blocks):
        where = pl.ds(first + segment.base + i, segment.rows, stride=segment.stride)
        packed[where, :] = value[
            segment.row : segment.row + segment.rows, segment.col + i * 128 : segment.col + (i + 1) * 128
        ]


class Halving:
    def __init__(self, chunks, bits, recv, packed, first, send_sem, recv_sem):
        self.chunks = chunks
        self.bits, self.recv, self.packed, self.first = bits, recv, packed, first
        self.send_sem, self.recv_sem = send_sem, recv_sem
        self.copies = {}
        dp, branch = lax.axis_index("dp"), lax.axis_index("branch")
        self.mine, self.partner = [], []
        for dim in range(bits - 1):
            weight = 2 ** (bits - 2 - dim)
            bit = dp // weight % 2
            self.mine.append(bit)
            self.partner.append({"dp": dp + weight * (1 - 2 * bit), "branch": branch})
        self.mine.append(branch)
        self.partner.append({"dp": dp, "branch": 1 - branch})

    def near_level(self, other):
        dp = lax.axis_index("dp")
        for i in range(self.bits - 2):
            if other >> i & 1:
                dp = dp + 2 ** (i + 1) * (1 - 2 * self.mine[self.bits - 3 - i])
        return {"dp": dp, "branch": lax.axis_index("branch")}

    def barrier(self):
        semaphore = pltpu.get_barrier_semaphore()
        levels = 2 ** (self.bits - 2)
        targets = self.partner[self.bits - 2 :] + [self.near_level(other) for other in range(1, levels)]
        for target in targets:
            pl.semaphore_signal(semaphore, inc=1, device_id=target, device_id_type=MESH)
        return lambda: pl.semaphore_wait(semaphore, len(targets))

    def left(self, name, stage):
        return [d for d in range(self.bits) if d not in self.chunks[name].order[:stage]]

    def half(self, ref, name, stage, index):
        position = self.left(name, stage).index(self.chunks[name].order[stage])
        return ref.at[(slice(None),) * position + (index,)]

    def remote(self, source, target, device, *key):
        slot = len(self.copies)
        self.copies[key] = pltpu.make_async_remote_copy(
            src_ref=source,
            dst_ref=target,
            send_sem=self.send_sem.at[slot],
            recv_sem=self.recv_sem.at[slot],
            device_id=device,
            device_id_type=MESH,
        )
        self.copies[key].start()

    def send(self, name, stage, source):
        dim = self.chunks[name].order[stage]
        self.remote(source, self.recv[name][stage], self.partner[dim], name, stage)

    def send_half(self, name, stage, ref):
        dim = self.chunks[name].order[stage]
        self.send(name, stage, self.half(ref, name, stage, 1 - self.mine[dim]))

    def arrived(self, *key):
        self.copies[key].wait_recv()

    def add(self, name, stage, own):
        chunk = self.chunks[name]
        got = self.recv[name][stage]
        depth = self.bits - 1 - stage
        if stage == self.bits - 1:
            value = own[...].astype(F32) + got[...].astype(F32)
            for segment in chunk.segments:
                store_segment(self.packed, self.first[segment.result], segment, value)
            return

        outer = max(depth - 2, 0)

        def step(i, carry):
            where = tuple(coordinates(i, outer))
            got[where] = got[where] + own[where]
            return carry

        lax.fori_loop(0, 2**outer, step, 0)

    def finish(self, name, stage, own=None):
        chunk = self.chunks[name]
        self.arrived(name, stage)
        if own is None:
            dim = chunk.order[stage]
            own = self.half(self.recv[name][stage - 1], name, stage, self.mine[dim])
        self.add(name, stage, own)
        self.follow(name, stage)

    def follow(self, name, stage):
        if stage + 1 < self.bits:
            self.send_half(name, stage + 1, self.recv[name][stage])

    def drain(self):
        for copy in self.copies.values():
            copy.wait_send()


BOOKS = "books"


def quantizer_semantic(r):
    sem_code = r.chosen[0]
    rows, code_width = sem_code.shape
    columns = [slice(i * HALF, (i + 1) * HALF) for i in range(r.distill_v.shape[1] // HALF)]
    for i, cols in enumerate(columns):
        r.wide[i] = dot(sem_code, r.distill_v[:, cols])

    def row_sum(parts):
        return jnp.sum(sum(parts), axis=1, keepdims=True)

    for at in row_blocks(rows, 32):
        prediction = [r.wide[i, at, :] for i in range(len(columns))]
        target = [r.wavlm_v[at, cols].astype(F32) for cols in columns]
        pred_norm = lax.rsqrt(row_sum([p * p for p in prediction]) + EPS_COS)
        target_norm = lax.rsqrt(row_sum([w * w for w in target]) + EPS_COS)
        cosine = row_sum([p * w for p, w in zip(prediction, target)]) * (pred_norm * target_norm)
        from_target = -DISTILL * pred_norm * target_norm
        from_prediction = DISTILL * cosine * pred_norm * pred_norm
        for p, w, cols in zip(prediction, target, columns):
            r.act[at, cols] = (w * from_target + p * from_prediction).astype(BF16)
    grad_pred = r.act[:, : r.distill_v.shape[1]]
    put_distill(r.places.distill, dot(sem_code.T, grad_pred))
    r.gy[:, :code_width] = dot_t(grad_pred, r.distill_v[...])


def quantizer_latent(r):
    levels, rows, code_width = r.chosen.shape
    latent_t = r.latent[...].T
    r.wide[0] = dot_t(r.gquant[...], r.pout_v[0])
    r.wide[1] = dot(r.latent[...], r.pin_v[0])
    r.wide[2] = dot_t(r.gquant[...], r.pout_v[1])
    r.wide[3] = dot(r.latent[...], r.pin_v[1])
    put_group(r.places.pout, 0, t_dot(r.chosen[0], r.gquant[...]))
    put_group(r.places.pout, 1, t_dot(r.ac[...], r.gquant[...]))
    for at in row_blocks(rows, 32):
        grad_sem = r.wide[0, at, :] + r.gy[at, :code_width]
        commit = 2.0 * BETA * (r.wide[1, at, :] - r.chosen[0, at, :].astype(F32))
        r.g_rows[0, at, :] = (grad_sem - commit).astype(BF16)
        r.grad[at, :code_width] = (grad_sem + commit).astype(BF16)
        grad_ac, residual = r.wide[2, at, :], r.wide[3, at, :]
        for level in range(1, levels):
            residual = residual - r.chosen[level, at, :].astype(F32)
        carry = jnp.zeros_like(residual)
        for level in range(levels - 1, 0, -1):
            carry = carry + 2.0 * BETA * residual
            r.g_rows[level, at, :] = (grad_ac - carry).astype(BF16)
            residual = residual + r.chosen[level, at, :].astype(F32)
        r.grad[at, code_width:] = (grad_ac + carry).astype(BF16)
    put_group(r.places.pin, 0, dot(latent_t, r.grad[:, :code_width]))
    put_group(r.places.pin, 1, dot(latent_t, r.grad[:, code_width:]))
    r.gy[...] = dot_t(r.grad[...], jnp.concatenate([r.pin_v[0], r.pin_v[1]], axis=1))


def put_group(place, group, value):
    target, rows = place.ref, value.shape[0]
    value = value.astype(target.dtype)
    if len(target.shape) == 2:
        target[group * rows : (group + 1) * rows, :] = value
        return
    lead, height = target.shape[1:-2], target.shape[-2]
    value = value.reshape(math.prod(lead), -1, height, value.shape[1])
    value = jnp.concatenate([value[:, i] for i in range(value.shape[1])], axis=2)
    columns = value.shape[2]
    where = (group,) + (slice(None),) * (len(lead) + 1) + (pl.ds(place.col, columns),)
    target[where] = value.reshape(lead + (height, columns))


def put_distill(place, value):
    target = place.ref
    if len(target.shape) == 2:
        target[...] = value.astype(target.dtype)
        return
    height = target.shape[-2]
    value = value.reshape(math.prod(target.shape[:-2]), -1, value.shape[1])
    columns = value.shape[2] * value.shape[1] // height
    value = jnp.concatenate([value[:, :, i : i + columns] for i in range(0, value.shape[2], columns)], axis=1)
    where = (slice(None),) * (len(target.shape) - 1) + (pl.ds(place.col, columns),)
    target[where] = value.astype(target.dtype).reshape(target.shape[:-1] + (columns,))


def one_hot_rows(codes, first, count):
    row = iota((count, codes.shape[1]), 0)
    return jnp.where(codes - first == row, 1.0, 0.0).astype(BF16)


def pick_codes(r):
    levels, _, entries, code_width = r.books.shape
    entries = entries * r.books.shape[1]
    rows = r.cos.shape[0]
    slots = r.ring.shape[0]
    branch = lax.axis_index("branch")
    own = r.codes[:, pl.ds(pl.multiple_of(branch * rows, rows), rows)]
    r.code_rows[...] = jnp.broadcast_to(own[:, None, :], r.code_rows.shape)
    columns = jnp.concatenate([own.astype(F32), jnp.zeros((PAIR - levels, rows), F32)], axis=0).T
    lane = iota(columns.shape, 1)
    entry = iota((rows, entries), 1)
    r.code_cols[...] = columns
    r.ac_sum[...] = jnp.zeros(r.ac_sum.shape, F32)

    def book(level):
        slot = level % slots
        return pltpu.make_async_copy(r.books.at[level], r.ring.at[slot], r.sem_book.at[slot])

    def pick(level, carry):
        code = jnp.sum(jnp.where(lane == level, r.code_cols[...], 0.0), axis=1, keepdims=True)
        one_hot = jnp.where(entry == code.astype(jnp.int32), 1.0, 0.0).astype(BF16)
        book(level).wait()
        got = dot(one_hot, r.ring[level % slots].reshape(entries, code_width))
        r.chosen[level] = got.astype(BF16)
        r.ac_sum[...] += jnp.where(level > 0, got, 0.0)

        @pl.when(level + slots < levels)
        def _():
            book(level + slots).start()

        return carry

    def begin():
        for level in range(slots):
            book(level).start()

    def run():
        lax.fori_loop(0, levels, pick, 0, unroll=4)
        r.ac[...] = r.ac_sum[...].astype(BF16)

    return begin, run


def step_kernel(chunks, first_rows, bits, ins, outs, scratch):
    r = Refs({**ins, **outs, **scratch})
    t = r.t = Refs(r.t)
    r.att, r.g_rows, r.g_got, r.book_own = (r.ring.at[i] for i in range(4))
    r.ac_sum, r.code_cols = r.acc.at[:, : r.ac.shape[1]], r.gx.at[:, :PAIR]
    branch = lax.axis_index("branch")
    rows, width = r.tokens.shape
    levels, parts, entries, code_width = r.books.shape
    entries = entries * parts
    tiles = r.w_up_v.shape[1] // TILE
    pairs = width // PAIR

    def core_rows(ref):
        half = ref.shape[0] // 2
        return ref.at[pl.ds(pl.multiple_of(mine * half, half), half)]

    def ask(own, target, key):
        sums.remote(core_rows(own.at[0]), core_rows(target.at[branch]), sums.partner[bits - 1], key)

    def relay(target, key):
        if chunks:
            sums.arrived(key)
            there = core_rows(target.at[1 - branch])
            sums.remote(there, there, sums.partner[bits - 2], key, 1)

    if chunks:
        sums = Halving(chunks, bits, r.recv, r.packed, first_rows, r.send_sem, r.recv_sem)
        mine, level = sums.mine[bits - 2], lax.axis_index("dp") // 2
        wait_barrier = sums.barrier()
    moves = Moves(r.sem_move)
    begin_pick, run_pick = pick_codes(r)
    begin_pick()
    got_pout = [moves.start(r.pout_own.at[0], r.pout_v.at[branch])]
    frame_tables(r)
    if chunks:
        wait_barrier()
        ask(r.pout_own, r.pout_v, POUT)
    else:
        got_pout.append(moves.start(r.pout_other.at[0], r.pout_v.at[1 - branch]))
    got_rest = [
        moves.start(r.distill, r.distill_v),
        moves.start(r.wavlm.at[pl.ds(pl.multiple_of(branch * rows, rows), rows)], r.wavlm_v),
    ]
    got_attention = [moves.start(r.dec_qkv, r.w_qkv_v), moves.start(r.dec_out, r.w_out_v)]
    got_ffn = [moves.start(r.dec_up, r.w_up_v), moves.start(r.dec_down, r.w_down_v)]
    got_cotangent = [moves.start(r.cotangent, r.cotangent_v)]
    got_pin = [moves.start(r.pin_own.at[0], r.pin_v.at[branch])]
    if not chunks:
        got_pin.append(moves.start(r.pin_other.at[0], r.pin_v.at[1 - branch]))
    got_tokens = [moves.start(r.tokens, r.tokens_v)]
    got_attention_two = [moves.start(r.enc_qkv, r.w_qkv_e), moves.start(r.enc_out, r.w_out_e)]

    if chunks:
        down = dict(dec=[t.dd0, t.dd1], enc=[t.ed0, t.ed1, t.ed2])
        place = r.places = Refs(
            dec_up=[Place(t.du0), Place(t.du1)],
            dec_out=Place(t.da0),
            dec_qkv=[Place(t.da0, width), Place(t.da1), Place(t.da2)],
            enc_up=[Place(t.eu0), Place(t.eu1)],
            enc_out=Place(t.ea0),
            enc_qkv=[Place(t.ea1), Place(t.ea2), Place(t.ea3)],
            distill=Place(t.di),
            pout=Place(t.misc),
            pin=Place(t.misc, width),
        )
    else:
        down = dict(dec=[t.dec_down], enc=[t.enc_down])
        place = r.places = Refs(
            dec_up=[Place(t.dec_up, i * tiles // 2 * TILE) for i in range(2)],
            dec_out=Place(t.dec_out),
            dec_qkv=[Place(t.dec_qkv, i * width) for i in range(3)],
            enc_up=[Place(t.enc_up, i * tiles // 2 * TILE) for i in range(2)],
            enc_out=Place(t.enc_out),
            enc_qkv=[Place(t.enc_qkv, i * width) for i in range(3)],
            distill=Place(t.distill),
            pout=Place(t.pout),
            pin=Place(t.pin),
        )
    dec_down, enc_down = down["dec"], down["enc"]

    def wait(moves, other=None):
        for move in moves:
            move.wait()
        if chunks and other is not None:
            sums.arrived(other, 1)

    def layer_value(target, gain):
        for at in row_blocks(rows, 64):
            target[at, :] = (r.x2[at, :] + gain(3) * r.fo[at, :]).astype(BF16)

    def dec_gain(i):
        return r.vectors[1, i : i + 1, :]

    def enc_gain(i):
        return r.vectors[0, i : i + 1, :]

    def pick():
        run_pick()

    def semantic():
        relay(r.pout_v, POUT)
        wait(got_rest)
        quantizer_semantic(r)

    def quant():
        wait(got_pout, POUT)
        if chunks:
            ask(r.pin_own, r.pin_v, PIN)
        r.x[...] = dot(jnp.concatenate([r.chosen[0], r.ac[...]], axis=1), r.pout_v[...].reshape(-1, width))
        if chunks:
            for other in range(1, levels):
                target = sums.near_level(other)
                sums.remote(r.code_rows.at[target_level(target)], r.code_got.at[other], target, CODES, other)
            r.code_got[0] = r.code_rows[level]

    def target_level(target):
        return next(iter(target.values())) // 2

    def dec_project():
        wait(got_attention)
        attention_project(r, r.w_qkv_v, dec_gain)

    def dec_mix():
        relay(r.pin_v, PIN)
        attention_mix(r, r.w_out_v, dec_gain)

    def dec_ffn(half):
        def run():
            if half == 0:
                wait(got_ffn)
                wait(got_cotangent)
                ffn_backward_begin(r, dec_gain, r.cotangent_v)
            first, last = half * tiles // 2, (half + 1) * tiles // 2
            ffn_both(r, r.w_up_v, r.w_down_v, place.dec_up[half], dec_down, first, last)
            if half == 1:
                r.fo[...] = dot(r.act[...], r.w_down_v[...])
                layer_value(r.decoded, dec_gain)
                ffn_back_sum(r, r.w_up_v)
                ffn_backward_end(r, dec_gain, r.cotangent_v, r.dec_gains)
                got_ffn[:] = [moves.start(r.enc_up, r.w_up_v), moves.start(r.enc_down, r.w_down_v)]

        return run

    def dec_out():
        attention_backward_out(r, r.w_out_v, dec_gain, place.dec_out, r.dec_gains)

    def attention_pairs(first, last):
        return lambda: attention_backward_pairs(r, first, last)

    def dec_in(part):
        def run():
            attention_backward_in(r, place.dec_qkv[part], part)
            if part == 2:
                attention_backward_end(r, r.w_qkv_v, dec_gain, r.dec_gains)
                r.gquant[...] = r.gx[...].astype(BF16)

        return run

    def enc_project():
        wait(got_tokens)
        r.x[...] = r.tokens_v[...].astype(F32)
        wait(got_attention_two)
        attention_project(r, r.w_qkv_e, enc_gain)

    def enc_mix():
        attention_mix(r, r.w_out_e, enc_gain)

    def enc_ffn():
        wait(got_ffn)
        ffn_forward(r, r.w_up_v, r.w_down_v)
        layer_value(r.latent, enc_gain)

    def quantizer():
        wait(got_pin, PIN)
        quantizer_latent(r)
        if chunks:
            for other in reversed(range(1, levels)):
                target = sums.near_level(other)
                sums.arrived(CODES, other)
                sums.remote(r.g_rows.at[target_level(target)], r.g_got.at[other], target, BOOKS, 0, other)
            r.g_got[0] = r.g_rows[level]

    def book_half(core, put):
        quarter = entries // 4
        for side in range(2):
            r.book_sum[...] = jnp.zeros_like(r.book_sum)
            first = (core * 2 + side) * quarter

            def add(source, carry):
                one_hot = one_hot_rows(r.code_got[source, 0:1, :], first, quarter)
                r.book_sum[...] += dot(one_hot, r.g_got[source])
                return carry

            lax.fori_loop(0, levels, add, 0, unroll=4)
            put(side, r.book_sum[...])

    def finish_books(stage):
        blocks = entries // 4 // rows
        other_core, other_side = sums.partner[bits - 2], sums.partner[bits - 1]
        if stage == 0:
            for other in range(1, levels):
                sums.arrived(BOOKS, 0, other)

            def put(side, value):
                r.book_send[side] = value.astype(BF16)

            def keep(side, value):
                r.book_own[side * blocks : (side + 1) * blocks] = value.astype(BF16).reshape((blocks, rows, code_width))

            book_half(1 - mine, put)
            sums.remote(r.book_send, r.book_got, other_core, BOOKS, 1)
            book_half(mine, keep)
        elif stage == 1:
            sums.arrived(BOOKS, 1)
            for side in range(2):
                own = r.book_own[side * blocks : (side + 1) * blocks]
                r.book_got[side] = r.book_got[side] + own.reshape(r.book_got.shape[1:])
            sums.remote(r.book_got.at[1 - branch], r.book_last, other_side, BOOKS, 2)
        else:
            sums.arrived(BOOKS, 2)
            total = r.book_got[branch].astype(F32) + r.book_last[...].astype(F32)
            blocks = code_width // 128
            store_segment(r.packed, first_rows[BOOKS], Segment(BOOKS, 0, blocks, 0, blocks, 0, entries // 4), total)

    def all_books():
        parts = entries // TILE

        def one(step, carry):
            at = step // parts
            one_hot = one_hot_rows(r.code_rows[at, 0:1, :], step % parts * TILE, TILE)
            t.books[at, aligned(step % parts, TILE), :] = dot(one_hot, r.g_rows[at]).astype(BF16)
            return carry

        lax.fori_loop(0, levels * parts, one, 0)

    def enc_ffn_back(half):
        def run():
            first, last = half * tiles // 2, (half + 1) * tiles // 2
            if half == 0:
                ffn_backward_begin(r, enc_gain, r.gy)
            ffn_backward_tiles(r, r.w_down_v, place.enc_up[half], enc_down, first, last)
            if half == 1:
                ffn_back_sum(r, r.w_up_v)
                ffn_backward_end(r, enc_gain, r.gy, r.gains)

        return run

    def enc_out():
        attention_backward_out(r, r.w_out_e, enc_gain, place.enc_out, r.gains)

    def enc_in(part):
        def run():
            attention_backward_in(r, place.enc_qkv[part], part)
            if part == 2:
                attention_backward_end(r, r.w_qkv_e, enc_gain, r.gains)
                r.grad_tokens[...] = r.gx[...]
                if chunks:
                    spread_gains()

        return run

    def spread_gains():
        lanes = pl.ds(width, 128)
        for layer, ref in enumerate((r.gains, r.dec_gains)):
            for row in range(4):
                for block in range(width // 128):
                    owner = (layer * 4 + row) * (width // 128) + block
                    where = tuple(owner // 2 ** (bits - 1 - i) % 2 for i in range(bits))
                    value = ref[row : row + 1, block * 128 : (block + 1) * 128]
                    rows_here = t.ea3.shape[bits]
                    t.ea3[where + (slice(None), lanes)] = jnp.broadcast_to(value, (rows_here, 128)).astype(BF16)

    work = [
        (6.5, pick, ()),
        (2.0, semantic, (DISTILL_GRAD,)),
        (0.7, quant, ()),
        (1.5, dec_project, ()),
        (2.5, dec_mix, ()),
        (2.6, dec_ffn(0), (DU0,)),
        (2.7, dec_ffn(1), (DD0, DD1, DU1)),
        (1.2, dec_out, ()),
        (1.6, attention_pairs(0, pairs // 2), ()),
        (1.6, attention_pairs(pairs // 2, pairs), ()),
        (0.6, dec_in(0), (DA0,)),
        (0.6, dec_in(1), (DA1,)),
        (0.8, dec_in(2), (DA2,)),
        (1.5, enc_project, ()),
        (2.5, enc_mix, ()),
        (2.2, enc_ffn, ()),
        (2.0, quantizer, (BOOKS, MISC)),
        (2.0, enc_ffn_back(0), (EU0,)),
        (2.0, enc_ffn_back(1), (EU1, ED0, ED1, ED2)),
        (1.2, enc_out, (EA0,)),
        (1.6, attention_pairs(0, pairs // 2), ()),
        (1.6, attention_pairs(pairs // 2, pairs), ()),
        (0.6, enc_in(0), (EA1,)),
        (0.6, enc_in(1), (EA2,)),
        (1.0, enc_in(2), (EA3,)),
    ]
    if not chunks:
        for _, run, _ in work:
            run()
            if run is quantizer:
                all_books()
        return
    actions = plan(chunks, work, bits, rows * code_width * 2)

    def finish(name, stage):
        if name == BOOKS:
            finish_books(stage)
        elif stage == 0:
            sums.finish(name, 0, sums.half(t[name], name, 0, mine))
        else:
            sums.finish(name, stage)

    for (_, run, made), acts in zip(work, actions):
        run()
        for name in made:
            if name != BOOKS:
                sums.send_half(name, 0, t[name])
        for name, stage in acts:
            finish(name, stage)
    for name, stage in actions[-1]:
        finish(name, stage)
    sums.drain()


POUT, PIN, CODES = 1, 2, 3
DISTILL_GRAD = "di"
DD0, DD1, DU0, DU1, DA0, DA1, DA2, MISC = "dd0", "dd1", "du0", "du1", "da0", "da1", "da2", "misc"
EU0, EU1, ED0, ED1, ED2 = "eu0", "eu1", "ed0", "ed1", "ed2"
EA0, EA1, EA2, EA3 = "ea0", "ea1", "ea2", "ea3"


def step(given, devices, with_sums):
    rows, width = given.tokens.shape
    ff = given.enc_up.shape[1]
    levels, entries, code_width = given.books.shape
    given.books = given.books.reshape(levels, -1, rows, code_width)
    bits = devices.bit_length() - 1
    vmem, hbm = pl.BlockSpec(memory_space=pltpu.VMEM), pl.BlockSpec(memory_space=pl.ANY)
    scratch = layer_scratch(rows, width, ff)
    scratch.update(
        w_qkv_e=pltpu.VMEM((width, 3 * width), BF16),
        w_out_e=pltpu.VMEM((width, width), BF16),
        cos=pltpu.VMEM((rows, PAIR), F32),
        sin=pltpu.VMEM((rows, PAIR), F32),
        bias=pltpu.VMEM((rows, rows), F32),
        ring=pltpu.VMEM((4,) + given.books.shape[1:], BF16),
        code_rows=pltpu.VMEM((levels, 8, rows), jnp.int32),
        chosen=pltpu.VMEM((levels, rows, code_width), BF16),
        ac=pltpu.VMEM((rows, code_width), BF16),
        gquant=pltpu.VMEM((rows, width), BF16),
        gy=pltpu.VMEM((rows, width), F32),
        latent=pltpu.VMEM((rows, width), BF16),
        pin_v=pltpu.VMEM((2, width, code_width), BF16),
        pout_v=pltpu.VMEM((2, code_width, width), BF16),
        distill_v=pltpu.VMEM(given.distill.shape, BF16),
        wavlm_v=pltpu.VMEM((rows, given.wavlm.shape[1]), BF16),
        tokens_v=pltpu.VMEM((rows, width), BF16),
        cotangent_v=pltpu.VMEM((rows, width), BF16),
        sem_move=pltpu.SemaphoreType.DMA((14,)),
        sem_book=pltpu.SemaphoreType.DMA((4,)),
    )
    outs = Refs(decoded=shaped((rows, width), BF16), grad_tokens=shaped((rows, width), F32))
    chunks, first_rows = {}, {}
    params = dict(vmem_limit_bytes=60 * 2**20)
    if with_sums:
        params.update(collective_id=0, has_side_effects=True)
        c, x, y = bits - 2, bits - 1, bits - 3
        b, a = range(y)
        share = width // devices
        low, high = ff // devices, share
        wide, half, blocks = ff // 128, ff // 256, width // 128
        third, quarter = 3 * blocks, blocks // 4
        chunks = dict(
            di=Chunk(
                high,
                width,
                [c, y, x, a, b],
                [
                    Segment(8, 0, 2 * blocks, 0, blocks, 0, high // 2),
                    Segment(8, blocks, 2 * blocks, 0, blocks, high // 2, high // 2),
                ],
            ),
            du0=Chunk(high, ff // 2, [c, y, a, x, b], [Segment(2, 0, wide, 0, half, 0, high)]),
            dd0=Chunk(low, width // 2, [c, a, y, b, x], [Segment(3, 0, blocks, 0, 2 * quarter, 0, low)]),
            dd1=Chunk(low, width // 2, [c, y, x, a, b], [Segment(3, 2 * quarter, blocks, 0, 2 * quarter, 0, low)]),
            du1=Chunk(high, ff // 2, [c, x, y, a, b], [Segment(2, half, wide, 0, half, 0, high)]),
            da0=Chunk(
                high,
                2 * width,
                [c, x, y, a, b],
                [Segment(1, 0, blocks, 0, blocks, 0, high), Segment(0, 0, third, width, blocks, 0, high)],
            ),
            da1=Chunk(high, width, [c, a, x, y, b], [Segment(0, blocks, third, 0, blocks, 0, high)]),
            da2=Chunk(high, width, [c, y, x, a, b], [Segment(0, 2 * blocks, third, 0, blocks, 0, high)]),
            misc=Chunk(
                high,
                2 * width,
                [c, x, y, a, b],
                [
                    Segment(9, 0, blocks, 0, blocks, 0, high),
                    Segment(10, 0, blocks // 2, width, blocks // 2, 0, high),
                    Segment(10, high * blocks // 2, blocks // 2, width + code_width, blocks // 2, 0, high),
                ],
            ),
            eu0=Chunk(high, ff // 2, [c, x, a, y, b], [Segment(6, 0, wide, 0, half, 0, high)]),
            eu1=Chunk(high, ff // 2, [c, x, y, a, b], [Segment(6, half, wide, 0, half, 0, high)]),
            ed0=Chunk(low, width // 2, [c, x, y, a, b], [Segment(7, 0, blocks, 0, 2 * quarter, 0, low)]),
            ed1=Chunk(low, width // 4, [c, y, x, a, b], [Segment(7, 2 * quarter, blocks, 0, quarter, 0, low)]),
            ed2=Chunk(low, width // 4, [c, y, a, b, x], [Segment(7, 3 * quarter, blocks, 0, quarter, 0, low)]),
            ea0=Chunk(high, width, [c, x, y, a, b], [Segment(5, 0, blocks, 0, blocks, 0, high)]),
            ea1=Chunk(high, width, [c, y, x, a, b], [Segment(4, 0, third, 0, blocks, 0, high)]),
            ea2=Chunk(high, width, [c, x, a, y, b], [Segment(4, blocks, third, 0, blocks, 0, high)]),
            ea3=Chunk(
                high,
                width + 128,
                [c, x, y, a, b],
                [Segment(4, 2 * blocks, third, 0, blocks, 0, high), Segment(11, 0, 1, width, 1, 0, 8)],
            ),
        )
        rows_of = [high * 3 * blocks, high * blocks, high * wide, low * blocks] * 2
        rows_of += [high * blocks, high * blocks, high * blocks, 8, entries // 4 * code_width // 128]
        first_rows = {i: sum(rows_of[:i]) for i in range(len(rows_of))}
        first_rows[BOOKS] = first_rows[len(rows_of) - 1]
        copies = len(chunks) * bits + 2 * levels + 4
        scratch.update(
            t={name: pltpu.VMEM(c.shape(bits), BF16) for name, c in chunks.items()},
            recv={
                name: [pltpu.VMEM(c.shape(bits - 1 - stage), BF16) for stage in range(bits)]
                for name, c in chunks.items()
            },
            gains=pltpu.VMEM((4, width), F32),
            dec_gains=pltpu.VMEM((4, width), F32),
            code_got=pltpu.VMEM((levels, 8, rows), jnp.int32),
                book_sum=pltpu.VMEM((entries // 4, code_width), F32),
            book_send=pltpu.VMEM((2, entries // 4, code_width), BF16),
            book_got=pltpu.VMEM((2, entries // 4, code_width), BF16),
            book_last=pltpu.VMEM((entries // 4, code_width), BF16),
            send_sem=pltpu.SemaphoreType.DMA((copies,)),
            recv_sem=pltpu.SemaphoreType.DMA((copies,)),
        )
        outs.packed = shaped((sum(rows_of), 128), F32)
    else:
        outs.update(gains=shaped((4, width), F32), dec_gains=shaped((4, width), F32))
        outs.t = dict(
            enc_qkv=shaped(given.enc_qkv.shape, BF16),
            enc_out=shaped(given.enc_out.shape, BF16),
            enc_up=shaped(given.enc_up.shape, BF16),
            enc_down=shaped(given.enc_down.shape, BF16),
            dec_qkv=shaped(given.enc_qkv.shape, BF16),
            dec_out=shaped(given.enc_out.shape, BF16),
            dec_up=shaped(given.enc_up.shape, BF16),
            dec_down=shaped(given.enc_down.shape, BF16),
            pin=shaped((2 * width, code_width), BF16),
            pout=shaped((2 * code_width, width), BF16),
            books=shaped((levels, entries, code_width), BF16),
            distill=shaped(given.distill.shape, BF16),
        )
    in_specs = dict.fromkeys(given, hbm)
    in_specs.update(
        lengths=pl.BlockSpec(memory_space=pltpu.SMEM), codes=vmem, vectors=vmem
    )
    got = pl.pallas_call(
        functools.partial(step_kernel, chunks, first_rows, bits),
        out_shape={k: pltpu.VMEM(v.shape, v.dtype) for k, v in outs.items()} if with_sums else dict(outs),
        in_specs=[in_specs],
        out_specs=jax.tree.map(lambda _: vmem, dict(outs)),
        scratch_shapes=[dict(scratch)],
        compiler_params=pltpu.CompilerParams(**params),
        name="step",
    )(dict(given))
    got = Refs(got)
    if not with_sums:
        return got
    last = [shaped((rows, 128), F32) for rows in rows_of]
    last[11] = shaped((1, 128), F32)

    def hand_on(packed, decoded, grad, *refs):
        outs, moves = refs[:-1], Moves(refs[-1])
        parts = [packed.at[pl.ds(first_rows[i], ref.shape[0])] for i, ref in enumerate(outs[:-2])]
        leaving = [moves.start(part, ref) for part, ref in zip(parts + [decoded, grad], outs)]
        for move in leaving:
            move.wait()

    return pl.pallas_call(
        hand_on,
        out_shape=last + [outs.decoded, outs.grad_tokens],
        in_specs=[vmem] * 3,
        out_specs=[hbm] * (len(last) + 2),
        scratch_shapes=[pltpu.SemaphoreType.DMA((len(last) + 2,))],
        compiler_params=pltpu.CompilerParams(vmem_limit_bytes=16 * 2**20),
        name="results",
    )(got.packed, got.decoded, got.grad_tokens)


def body(
    tokens,
    wavlm,
    cotangent,
    lengths,
    codes,
    enc_qkv,
    enc_out,
    enc_up,
    enc_down,
    dec_qkv,
    dec_out,
    dec_up,
    dec_down,
    vectors,
    proj_in,
    proj_out,
    codebooks,
    distill_proj,
):
    width = tokens.shape[1]
    devices = lax.axis_size("dp") * lax.axis_size("branch")
    with_sums = devices == 4 * codebooks.shape[0] and width // devices % 16 == 0
    given = Refs(
        tokens=tokens,
        wavlm=wavlm,
        cotangent=cotangent,
        lengths=lengths,
        codes=codes.T,
        enc_qkv=enc_qkv,
        enc_out=enc_out,
        enc_up=enc_up,
        enc_down=enc_down,
        dec_qkv=dec_qkv,
        dec_out=dec_out,
        dec_up=dec_up,
        dec_down=dec_down,
        vectors=vectors,
        pin_own=proj_in,
        pout_own=proj_out,
        books=codebooks,
        distill=distill_proj,
    )
    if with_sums:
        *sums, decoded, grad_tokens = step(given, devices, True)
        sums = [part.reshape(-1) for part in sums]
        order = (4, 5, 6, 7, 0, 1, 2, 3, 11, 10, 9, 12, 8)
        return (decoded, grad_tokens, *[sums[i] for i in order])
    swap = [(0, 1), (1, 0)]
    given.pin_other = lax.ppermute(proj_in, "branch", swap)
    given.pout_other = lax.ppermute(proj_out, "branch", swap)
    s = step(given, devices, False)
    t = Refs(s.t)
    gains = jnp.concatenate([s.gains, s.dec_gains])
    local = [t.enc_qkv, t.enc_out, t.enc_up, t.enc_down, t.dec_qkv, t.dec_out, t.dec_up, t.dec_down]
    local += [gains, t.pin, t.pout, t.books, t.distill]
    sums = [
        lax.psum_scatter(part.astype(F32).reshape(-1), ("dp", "branch"), scatter_dimension=0, tiled=True)
        for part in local
    ]
    return (s.decoded, s.grad_tokens, *sums)


def solution(mesh):
    rows, whole = P(("dp", "branch"), None), P()
    placed = (rows, P("dp", None), rows, rows, P("dp", None)) + (whole,) * 9
    placed += (P("branch", None, None),) * 2 + (whole,) * 2
    return jax.shard_map(
        body,
        mesh=mesh,
        in_specs=placed,
        out_specs=(rows, rows) + (P(("dp", "branch")),) * 13,
        check_vma=False,
    )
```

```python
import functools
import math

import jax
import jax.numpy as jnp
from jax import lax
from jax.experimental import pallas as pl
from jax.experimental.pallas import tpu as pltpu
from jax.sharding import PartitionSpec as P

HEADS = 8
WINDOW = 250
EPS_NORM = 1e-05
EPS_COS = 1e-06
BETA = 0.25
DISTILL = 10.0
ROPE_BASE = 10000.0

MESH = pl.DeviceIdType.MESH
F32 = jnp.float32
BF16 = jnp.bfloat16
TILE = 512
PAIR = 128
HALF = 256


def dot(left, right):
    return lax.dot_general(left, right, (((1,), (0,)), ((), ())), preferred_element_type=F32)


def dot_t(left, right):
    return lax.dot_general(left, right, (((1,), (1,)), ((), ())), preferred_element_type=F32)


def t_dot(left, right):
    return lax.dot_general(left, right, (((0,), (0,)), ((), ())), preferred_element_type=F32)


def iota(shape, dim):
    return lax.broadcasted_iota(jnp.int32, shape, dim)


def aligned(index, size):
    return pl.ds(pl.multiple_of(index * size, size), size)


class Refs(dict):
    __getattr__ = dict.__getitem__
    __setattr__ = dict.__setitem__


class Moves:
    def __init__(self, semaphores):
        self.semaphores, self.count = semaphores, 0

    def start(self, source, target):
        move = pltpu.make_async_copy(source, target, self.semaphores.at[self.count])
        self.count += 1
        move.start()
        return move


def layer_scratch(rows, width, ff):
    return Refs(
        x=pltpu.VMEM((rows, width), F32),
        s1=pltpu.VMEM((rows, 1), F32),
        h=pltpu.VMEM((rows, width), BF16),
        h1t=pltpu.VMEM((width, rows), BF16),
        h2t=pltpu.VMEM((width, rows), BF16),
        rinv=pltpu.VMEM((rows, width), F32),
        qkv=pltpu.VMEM((rows, 3 * width), BF16),
        mix=pltpu.VMEM((rows, width), BF16),
        ao=pltpu.VMEM((rows, width), F32),
        x2=pltpu.VMEM((rows, width), F32),
        s2=pltpu.VMEM((rows, 1), F32),
        act=pltpu.VMEM((rows, ff), BF16),
        dg=pltpu.VMEM((rows, ff), BF16),
        fo=pltpu.VMEM((rows, width), F32),
        grad=pltpu.VMEM((rows, width), BF16),
        gx=pltpu.VMEM((rows, width), F32),
        acc=pltpu.VMEM((rows, width), F32),
        wide=pltpu.VMEM((4, rows, HALF), F32),
        change=pltpu.VMEM((2, rows, rows), BF16),
        w_qkv_v=pltpu.VMEM((width, 3 * width), BF16),
        w_out_v=pltpu.VMEM((width, width), BF16),
        w_up_v=pltpu.VMEM((width, ff), BF16),
        w_down_v=pltpu.VMEM((ff, width), BF16),
    )


def shaped(shape, kind):
    return jax.ShapeDtypeStruct(shape, kind)


def frame_tables(r):
    rows = r.cos.shape[0]
    place = iota((rows, PAIR), 0)
    query, key = iota((rows, rows), 0), iota((rows, rows), 1)
    begin, begin_query = jnp.zeros_like(place), jnp.zeros_like(query)
    edge = 0
    for clip in range(r.lengths.shape[1] - 1):
        edge = edge + r.lengths[0, clip]
        begin = jnp.where(place >= edge, edge, begin)
        begin_query = jnp.where(query >= edge, edge, begin_query)
    allowed = (key >= begin_query) & (key <= query) & (query - key < WINDOW)
    r.bias[...] = jnp.where(allowed, 0.0, -1e30)
    lane = iota((rows, PAIR), 1)
    rate = jnp.exp((lane % 32).astype(F32) * (-math.log(ROPE_BASE) / 32))
    angle = (place - begin).astype(F32) * rate
    r.cos[...] = jnp.cos(angle)
    sine = jnp.sin(angle)
    r.sin[...] = jnp.where(lane % 64 < 32, -sine, sine)


def rotated(value, cosine, sine):
    lane = iota(value.shape, 1)
    swapped = jnp.where(lane % 64 < 32, pltpu.roll(value, PAIR - 32, 1), pltpu.roll(value, 32, 1))
    return value * cosine + swapped * sine


def head_masks(rows):
    low = iota((rows, PAIR), 1) < 64
    return (jnp.where(low, 1.0, 0.0).astype(BF16), jnp.where(low, 0.0, 1.0).astype(BF16))


def row_blocks(rows, step):
    return [slice(i, i + step) for i in range(0, rows, step)]


def attention_project(r, w_qkv, gain):
    rows, width = r.x.shape
    scale = gain(0)
    for at in row_blocks(rows, 64):
        x = r.x[at, :]
        s1 = lax.rsqrt(jnp.mean(x * x, axis=1, keepdims=True) + EPS_NORM)
        r.s1[at, :] = s1
        r.h[at, :] = (x * s1 * scale).astype(BF16)
    for half in range(3 * width // HALF):
        slot, part = half % 4, half // (width // HALF)
        cols = slice(half * HALF, (half + 1) * HALF)
        r.wide[slot] = dot(r.h[...], w_qkv[:, cols])
        for at in row_blocks(rows, 64):
            for p in range(HALF // PAIR):
                value = r.wide[slot, at, p * PAIR : (p + 1) * PAIR]
                if part < 2:
                    value = rotated(value, r.cos[at, :], r.sin[at, :])
                low = value.astype(BF16)
                if part == 0:
                    low = (low.astype(F32) * 0.125).astype(BF16)
                r.qkv[at, half * HALF + p * PAIR : half * HALF + (p + 1) * PAIR] = low
    r.h1t[...] = r.h[...].T


def attention_mix(r, w_out, gain):
    rows, width = r.x.shape
    masks = head_masks(rows)
    low = iota((rows, PAIR), 1) < 64
    pairs = width // PAIR
    for p in range(pairs):
        query = r.qkv[:, p * PAIR : (p + 1) * PAIR]
        key = r.qkv[:, (p + pairs) * PAIR : (p + pairs + 1) * PAIR]
        value = r.qkv[:, (p + 2 * pairs) * PAIR : (p + 2 * pairs + 1) * PAIR]
        outs = []
        for h in range(2):
            head = 2 * p + h
            slot = head % 4
            r.wide[slot] = dot_t(query * masks[h], key)
            for at in row_blocks(rows, 64):
                seen = PAIR if at.stop <= PAIR else rows
                scores = r.wide[slot, at, :seen] + r.bias[at, :seen]
                weights = jnp.exp(scores - jnp.max(scores, axis=1, keepdims=True))
                r.att[head, at, :seen] = weights.astype(BF16)
                if seen < rows:
                    r.att[head, at, seen:] = jnp.zeros((64, rows - seen), BF16)
            outs.append(dot(r.att[head], value * masks[h] + masks[1 - h]))
        inverse = 1.0 / pltpu.roll(jnp.where(low, outs[1], outs[0]), 64, 1)
        r.rinv[:, p * PAIR : (p + 1) * PAIR] = inverse
        r.mix[:, p * PAIR : (p + 1) * PAIR] = (jnp.where(low, outs[0], outs[1]) * inverse).astype(BF16)
    r.ao[...] = dot(r.mix[...], w_out[...])
    scale_one, scale_two = gain(1), gain(2)
    for at in row_blocks(rows, 64):
        x2 = r.x[at, :] + scale_one * r.ao[at, :]
        r.x2[at, :] = x2
        s2 = lax.rsqrt(jnp.mean(x2 * x2, axis=1, keepdims=True) + EPS_NORM)
        r.s2[at, :] = s2
        r.h[at, :] = (x2 * s2 * scale_two).astype(BF16)
    r.h2t[...] = r.h[...].T


def gelu_parts(pre):
    slope = math.sqrt(2.0 / math.pi)
    square = pre * pre
    bent = jnp.tanh(slope * pre * (1.0 + 0.044715 * square))
    half = 0.5 * (1.0 + bent)
    turn = 0.5 * pre * (1.0 - bent * bent) * slope * (1.0 + 3.0 * 0.044715 * square)
    return (pre * half).astype(BF16), half + turn


def ffn_forward(r, w_up, w_down):
    rows, ff = r.act.shape
    for half in range(ff // HALF):
        slot, cols = half % 4, slice(half * HALF, (half + 1) * HALF)
        r.wide[slot] = dot(r.h[...], w_up[:, cols])
        for at in row_blocks(rows, 32):
            act, slope = gelu_parts(r.wide[slot, at, :])
            r.act[at, cols] = act
            r.dg[at, cols] = slope.astype(BF16)
    r.fo[...] = dot(r.act[...], w_down[...])


def ffn_both(r, w_up, w_down, grad_up, grad_down, first, last):
    rows = r.act.shape[0]
    for t in range(first, last):
        cols = slice(t * TILE, (t + 1) * TILE)
        for side in range(TILE // HALF):
            part = slice(t * TILE + side * HALF, t * TILE + (side + 1) * HALF)
            r.wide[side] = dot(r.h[...], w_up[:, part])
            r.wide[2 + side] = dot_t(r.grad[...], w_down[part, :])
            for at in row_blocks(rows, 32):
                act, slope = gelu_parts(r.wide[side, at, :])
                r.act[at, part] = act
                r.dg[at, part] = (r.wide[2 + side, at, :] * slope).astype(BF16)
        grad_up.shift((t - first) * TILE).put(dot(r.h2t[...], r.dg[:, cols]))
        put_rows(grad_down, t_dot(r.act[:, cols], r.grad[...]), t)


def ffn_back_sum(r, w_up):
    r.acc[...] = dot_t(r.dg[...], w_up[...])


def norm_back(stream, inverse, grad):
    mean = jnp.mean(grad * stream, axis=1, keepdims=True)
    return inverse * grad - stream * (inverse * inverse * inverse * mean)


def column_sum(value):
    return jnp.sum(value, axis=0, keepdims=True)


class Place:
    def __init__(self, ref, col=0, chunk=None):
        self.ref, self.col, self.chunk = ref, col, chunk

    def shift(self, by):
        return Place(self.ref, self.col + by, self.chunk)

    def put(self, value):
        value = value.astype(BF16)
        cols = slice(self.col, self.col + value.shape[1])
        if self.chunk is None:
            self.ref[:, cols] = value
            return
        blocks, rows = self.ref.shape[:2]
        for owner in range(blocks):
            self.ref[self.chunk.index(owner), :, cols] = value[owner * rows : (owner + 1) * rows]


def put_rows(places, value, tile):
    value = value.astype(BF16)
    begin = 0
    for place in places:
        part = value[:, begin : begin + place.ref.shape[-1]]
        begin += place.ref.shape[-1]
        if place.chunk is None:
            place.ref[tile * TILE : tile * TILE + TILE, :] = part
            continue
        rows = place.ref.shape[1]
        for i in range(TILE // rows):
            place.ref[place.chunk.index(tile * (TILE // rows) + i)] = part[i * rows : (i + 1) * rows]


def ffn_backward_begin(r, gain, gy_ref):
    scale = gain(3)
    for at in row_blocks(r.grad.shape[0], 64):
        r.grad[at, :] = (scale * gy_ref[at, :].astype(F32)).astype(BF16)


def ffn_backward_tiles(r, w_down, grad_up, grad_down, first, last):
    rows = r.act.shape[0]
    for t in range(first, last):
        cols = slice(t * TILE, (t + 1) * TILE)
        for side in range(TILE // HALF):
            part = slice(t * TILE + side * HALF, t * TILE + (side + 1) * HALF)
            slot = (2 * t + side) % 4
            r.wide[slot] = dot_t(r.grad[...], w_down[part, :])
            for at in row_blocks(rows, 64):
                r.dg[at, part] = (r.wide[slot, at, :] * r.dg[at, part].astype(F32)).astype(BF16)
        put_rows(grad_down, t_dot(r.act[:, cols], r.grad[...]), t)
        grad_up.shift((t - first) * TILE).put(dot(r.h2t[...], r.dg[:, cols]))


def ffn_backward_end(r, gain, gy_ref, gain_out):
    scale = gain(2)
    to_gain = to_scale = 0.0
    for at in row_blocks(r.x2.shape[0], 32):
        gy = gy_ref[at, :].astype(F32)
        to_scale = to_scale + column_sum(gy * r.fo[at, :])
        back, x2, s2 = r.acc[at, :], r.x2[at, :], r.s2[at, :]
        to_gain = to_gain + column_sum(back * x2 * s2)
        r.gx[at, :] = gy + norm_back(x2, s2, back * scale)
    gain_out[3:4, :] = to_scale
    gain_out[2:3, :] = to_gain


def attention_backward_out(r, w_out, gain, grad_out, gain_out):
    scale = gain(1)
    to_scale = 0.0
    for at in row_blocks(r.gx.shape[0], 64):
        gx = r.gx[at, :]
        to_scale = to_scale + column_sum(gx * r.ao[at, :])
        r.grad[at, :] = (scale * gx).astype(BF16)
    gain_out[1:2, :] = to_scale
    grad_out.put(t_dot(r.mix[...], r.grad[...]))
    r.grad[...] = dot_t(r.grad[...], w_out[...]).astype(BF16)


def attention_backward_pairs(r, first, last):
    rows, width = r.x.shape
    masks = head_masks(rows)
    masks_t = [jnp.where((iota((PAIR, rows), 0) < 64) == (h == 0), 1.0, 0.0).astype(BF16) for h in range(2)]
    pairs = width // PAIR
    for p in range(first, last):
        lanes = [slice((p + i * pairs) * PAIR, (p + i * pairs + 1) * PAIR) for i in range(3)]
        query, key, value = (r.qkv[:, at] for at in lanes)
        grad_mixed = (r.grad[:, lanes[0]].astype(F32) * r.rinv[:, lanes[0]]).astype(BF16)
        product = (grad_mixed.astype(F32) * r.mix[:, lanes[0]].astype(F32)).astype(BF16)
        beside = jnp.concatenate([value, jnp.full(value.shape, -1.0, BF16)], axis=1)
        query_t, grad_t = query.T, grad_mixed.T
        to_query = to_key = to_value = 0.0
        for h in range(2):
            head = 2 * p + h
            slot = head % 4
            both = jnp.concatenate([grad_mixed * masks[h], product * masks[h]], axis=1)
            r.wide[slot] = dot_t(both, beside)
            for at in row_blocks(rows, 64):
                r.change[h, at, :] = (r.att[head, at, :].astype(F32) * r.wide[slot, at, :]).astype(BF16)
            to_query = to_query + dot(r.change[h], key * masks[h])
            to_key = to_key + dot(query_t * masks_t[h], r.change[h])
            to_value = to_value + dot(grad_t * masks_t[h], r.att[head])
        cosine, sine = r.cos[...], -r.sin[...]
        r.qkv[:, lanes[0]] = rotated(to_query * 0.125, cosine, sine).astype(BF16)
        r.qkv[:, lanes[1]] = rotated(to_key.T, cosine, sine).astype(BF16)
        r.qkv[:, lanes[2]] = to_value.T.astype(BF16)


def attention_backward_in(r, grad_qkv, part):
    width = r.x.shape[1]
    grad_qkv.put(dot(r.h1t[...], r.qkv[:, part * width : (part + 1) * width]))


def attention_backward_end(r, w_qkv, gain, gain_out):
    r.acc[...] = dot_t(r.qkv[...], w_qkv[...])
    scale = gain(0)
    to_gain = 0.0
    for at in row_blocks(r.x.shape[0], 32):
        back, x, s1 = r.acc[at, :], r.x[at, :], r.s1[at, :]
        to_gain = to_gain + column_sum(back * x * s1)
        r.gx[at, :] = r.gx[at, :] + norm_back(x, s1, back * scale)
    gain_out[0:1, :] = to_gain


class Segment:
    def __init__(self, result, base, stride, col, blocks, row, rows):
        self.result, self.base, self.stride, self.col, self.blocks = result, base, stride, col, blocks
        self.row, self.rows = row, rows


class Chunk:
    def __init__(self, rows, columns, order, segments):
        self.rows, self.columns, self.order, self.segments = rows, columns, order, segments

    def index(self, owner):
        bits = len(self.order)
        return sum((owner >> (bits - 1 - dim) & 1) << (bits - 1 - stage) for stage, dim in enumerate(self.order))

    def shape(self, leading):
        return (2**leading, self.rows, self.columns)

    def bytes(self, bits):
        return 2**bits * self.rows * self.columns * 2


def plan(chunks, work, bits, book_bytes):
    core, x, y = bits - 2, bits - 1, bits - 3
    ends, middle = -1, -2
    free, pending, done = {}, [], []
    now = 0.0

    def carry(link, size, rate=42e3):
        free[link] = max(now, free.get(link, 0.0)) + size / rate
        return free[link]

    def begin(name, stage):
        if name == BOOKS:
            size = 1.2 * 2 ** (bits - 3) * book_bytes
            if stage == 0:
                there = max(carry(y, size), carry(ends, 1.5 * size), carry(middle, 2 * size))
            else:
                there = carry(core, 4 * book_bytes, 400e3) if stage == 1 else carry(x, 2 * book_bytes)
        else:
            dim = chunks[name].order[stage]
            size = chunks[name].bytes(bits) / 2 ** (stage + 1)
            if dim == core:
                there = carry(core, size, 400e3)
            elif dim == x or dim == y:
                there = carry(dim, size)
            else:
                there = carry(ends, size)
                if dim < y - 1:
                    there = max(there, carry(middle, 2 * size))
        pending.append((there + 1.5, name, stage))

    def finish(limit):
        nonlocal now
        acts = []
        while pending:
            pending.sort(key=lambda p: p[0])
            if pending[0][0] + (0.5 if limit < math.inf else 0.0) > limit:
                break
            at, name, stage = pending.pop(0)
            if name == BOOKS:
                cost = (6.0, 0.6, 0.3)[stage]
            else:
                cost = 0.25 + 0.3e-6 * chunks[name].bytes(bits) / 2 ** (stage + 1)
            now = max(now, at) + cost
            limit = max(limit, now)
            acts.append((name, stage))
            if stage + 1 < (3 if name == BOOKS else bits):
                begin(name, stage + 1)
        return acts

    for took, _, names in work:
        now += 0.95 * took
        for name in names:
            begin(name, 0)
        done.append(finish(now))
    done.append(finish(math.inf))
    return done


def store_segment(packed, first, segment, value):
    for i in range(segment.blocks):
        where = pl.ds(first + segment.base + i, segment.rows, stride=segment.stride)
        packed[where, :] = value[
            segment.row : segment.row + segment.rows, segment.col + i * 128 : segment.col + (i + 1) * 128
        ]


class Halving:
    def __init__(self, chunks, bits, recv, packed, first, send_sem, recv_sem):
        self.chunks = chunks
        self.bits, self.recv, self.packed, self.first = bits, recv, packed, first
        self.send_sem, self.recv_sem = send_sem, recv_sem
        self.copies = {}
        dp, branch = lax.axis_index("dp"), lax.axis_index("branch")
        self.mine, self.partner = [], []
        for dim in range(bits - 1):
            weight = 2 ** (bits - 2 - dim)
            bit = dp // weight % 2
            self.mine.append(bit)
            self.partner.append({"dp": dp + weight * (1 - 2 * bit), "branch": branch})
        self.mine.append(branch)
        self.partner.append({"dp": dp, "branch": 1 - branch})

    def near_level(self, other):
        dp = lax.axis_index("dp")
        for i in range(self.bits - 2):
            if other >> i & 1:
                dp = dp + 2 ** (i + 1) * (1 - 2 * self.mine[self.bits - 3 - i])
        return {"dp": dp, "branch": lax.axis_index("branch")}

    def barrier(self):
        semaphore = pltpu.get_barrier_semaphore()
        levels = 2 ** (self.bits - 2)
        targets = self.partner[self.bits - 2 :] + [self.near_level(other) for other in range(1, levels)]
        for target in targets:
            pl.semaphore_signal(semaphore, inc=1, device_id=target, device_id_type=MESH)
        return lambda: pl.semaphore_wait(semaphore, len(targets))

    def half(self, ref, name, stage, other):
        mine = self.mine[self.chunks[name].order[stage]]
        count = 2 ** (self.bits - 1 - stage)
        return ref.at[pl.ds((1 - mine if other else mine) * count, count)]

    def remote(self, source, target, device, *key):
        slot = len(self.copies)
        self.copies[key] = pltpu.make_async_remote_copy(
            src_ref=source,
            dst_ref=target,
            send_sem=self.send_sem.at[slot],
            recv_sem=self.recv_sem.at[slot],
            device_id=device,
            device_id_type=MESH,
        )
        self.copies[key].start()

    def send(self, name, stage, source):
        dim = self.chunks[name].order[stage]
        self.remote(source, self.recv[name][stage], self.partner[dim], name, stage)

    def send_half(self, name, stage, ref):
        self.send(name, stage, self.half(ref, name, stage, True))

    def arrived(self, *key):
        self.copies[key].wait_recv()

    def add(self, name, stage, own):
        chunk = self.chunks[name]
        got = self.recv[name][stage]
        if stage == self.bits - 1:
            value = own[0].astype(F32) + got[0].astype(F32)
            for segment in chunk.segments:
                store_segment(self.packed, self.first[segment.result], segment, value)
            return
        count = 2 ** (self.bits - 1 - stage)
        step = min(count, 4)

        def some(i, carry):
            at = pl.ds(i * step, step)
            got[at] = got[at] + own[at]
            return carry

        lax.fori_loop(0, count // step, some, 0)

    def finish(self, name, stage, before):
        self.arrived(name, stage)
        self.add(name, stage, self.half(before, name, stage, False))
        if stage + 1 < self.bits:
            self.send_half(name, stage + 1, self.recv[name][stage])

    def drain(self):
        for copy in self.copies.values():
            copy.wait_send()


BOOKS = "books"


def quantizer_semantic(r):
    sem_code = r.chosen[0]
    rows, code_width = sem_code.shape
    columns = [slice(i * HALF, (i + 1) * HALF) for i in range(r.distill_v.shape[1] // HALF)]
    for i, cols in enumerate(columns):
        r.wide[i] = dot(sem_code, r.distill_v[:, cols])

    def row_sum(parts):
        return jnp.sum(sum(parts), axis=1, keepdims=True)

    for at in row_blocks(rows, 32):
        prediction = [r.wide[i, at, :] for i in range(len(columns))]
        target = [r.wavlm_v[at, cols].astype(F32) for cols in columns]
        pred_norm = lax.rsqrt(row_sum([p * p for p in prediction]) + EPS_COS)
        target_norm = lax.rsqrt(row_sum([w * w for w in target]) + EPS_COS)
        cosine = row_sum([p * w for p, w in zip(prediction, target)]) * (pred_norm * target_norm)
        from_target = -DISTILL * pred_norm * target_norm
        from_prediction = DISTILL * cosine * pred_norm * pred_norm
        for p, w, cols in zip(prediction, target, columns):
            r.act[at, cols] = (w * from_target + p * from_prediction).astype(BF16)
    grad_pred = r.act[:, : r.distill_v.shape[1]]
    put_distill(r.places.distill, dot(sem_code.T, grad_pred))
    r.gy[:, :code_width] = dot_t(grad_pred, r.distill_v[...])


def quantizer_latent(r):
    levels, rows, code_width = r.chosen.shape
    latent_t = r.latent[...].T
    r.wide[0] = dot_t(r.gquant[...], r.pout_v[0])
    r.wide[1] = dot(r.latent[...], r.pin_v[0])
    r.wide[2] = dot_t(r.gquant[...], r.pout_v[1])
    r.wide[3] = dot(r.latent[...], r.pin_v[1])
    put_group(r.places.pout, 0, t_dot(r.chosen[0], r.gquant[...]))
    put_group(r.places.pout, 1, t_dot(r.ac[...], r.gquant[...]))
    for at in row_blocks(rows, 32):
        grad_sem = r.wide[0, at, :] + r.gy[at, :code_width]
        commit = 2.0 * BETA * (r.wide[1, at, :] - r.chosen[0, at, :].astype(F32))
        r.g_rows[0, at, :] = (grad_sem - commit).astype(BF16)
        r.grad[at, :code_width] = (grad_sem + commit).astype(BF16)
        grad_ac, residual = r.wide[2, at, :], r.wide[3, at, :]
        for level in range(1, levels):
            residual = residual - r.chosen[level, at, :].astype(F32)
        carry = jnp.zeros_like(residual)
        for level in range(levels - 1, 0, -1):
            carry = carry + 2.0 * BETA * residual
            r.g_rows[level, at, :] = (grad_ac - carry).astype(BF16)
            residual = residual + r.chosen[level, at, :].astype(F32)
        r.grad[at, code_width:] = (grad_ac + carry).astype(BF16)
    put_group(r.places.pin, 0, dot(latent_t, r.grad[:, :code_width]))
    put_group(r.places.pin, 1, dot(latent_t, r.grad[:, code_width:]))
    r.gy[...] = dot_t(r.grad[...], jnp.concatenate([r.pin_v[0], r.pin_v[1]], axis=1))


def put_group(place, group, value):
    target, total = place.ref, value.shape[0]
    value = value.astype(BF16)
    if place.chunk is None:
        target[group * total : (group + 1) * total, :] = value
        return
    blocks, height, columns = target.shape[0] // 2, target.shape[1], value.shape[1]
    for i in range(blocks):
        for part in range(total // blocks // height):
            first = i * (total // blocks) + part * height
            cols = slice(place.col + part * columns, place.col + (part + 1) * columns)
            target[place.chunk.index(group * blocks + i), :, cols] = value[first : first + height]


def put_distill(place, value):
    target = place.ref
    if place.chunk is None:
        target[...] = value.astype(BF16)
        return
    blocks, height = target.shape[:2]
    rows = value.shape[0] // blocks
    columns = value.shape[1] * rows // height
    for i in range(blocks):
        part = value[i * rows : (i + 1) * rows]
        part = jnp.concatenate([part[:, at : at + columns] for at in range(0, value.shape[1], columns)], axis=0)
        target[place.chunk.index(i), :, place.col : place.col + columns] = part.astype(BF16)


def one_hot_rows(codes, first, count):
    row = iota((count, codes.shape[1]), 0)
    return jnp.where(codes - first == row, 1.0, 0.0).astype(BF16)


def pick_codes(r):
    levels, _, entries, code_width = r.books.shape
    entries = entries * r.books.shape[1]
    rows = r.cos.shape[0]
    slots = r.ring.shape[0]
    branch = lax.axis_index("branch")
    own = r.codes[:, pl.ds(pl.multiple_of(branch * rows, rows), rows)]
    r.code_rows[...] = jnp.broadcast_to(own[:, None, :], r.code_rows.shape)
    columns = jnp.concatenate([own.astype(F32), jnp.zeros((PAIR - levels, rows), F32)], axis=0).T
    lane = iota(columns.shape, 1)
    entry = iota((rows, entries), 1)
    r.code_cols[...] = columns
    r.ac_sum[...] = jnp.zeros(r.ac_sum.shape, F32)

    def book(level):
        slot = level % slots
        return pltpu.make_async_copy(r.books.at[level], r.ring.at[slot], r.sem_book.at[slot])

    def pick(level, carry):
        code = jnp.sum(jnp.where(lane == level, r.code_cols[...], 0.0), axis=1, keepdims=True)
        one_hot = jnp.where(entry == code.astype(jnp.int32), 1.0, 0.0).astype(BF16)
        book(level).wait()
        got = dot(one_hot, r.ring[level % slots].reshape(entries, code_width))
        r.chosen[level] = got.astype(BF16)
        r.ac_sum[...] += jnp.where(level > 0, got, 0.0)

        @pl.when(level + slots < levels)
        def _():
            book(level + slots).start()

        return carry

    def begin():
        for level in range(slots):
            book(level).start()

    def run():
        lax.fori_loop(0, levels, pick, 0, unroll=4)
        r.ac[...] = r.ac_sum[...].astype(BF16)

    return begin, run


def step_kernel(chunks, first_rows, bits, ins, outs, scratch):
    r = Refs({**ins, **outs, **scratch})
    t = r.t = Refs(r.t)
    r.att, r.g_rows, r.g_got, r.book_own = (r.ring.at[i] for i in range(4))
    r.ac_sum, r.code_cols = r.acc.at[:, : r.ac.shape[1]], r.gx.at[:, :PAIR]
    branch = lax.axis_index("branch")
    rows, width = r.tokens.shape
    levels, parts, entries, code_width = r.books.shape
    entries = entries * parts
    tiles = r.w_up_v.shape[1] // TILE
    pairs = width // PAIR
    if chunks:
        sums = Halving(chunks, bits, r.recv, r.packed, first_rows, r.send_sem, r.recv_sem)
        mine, level = sums.mine[bits - 2], lax.axis_index("dp") // 2
        wait_barrier = sums.barrier()
    moves = Moves(r.sem_move)
    begin_pick, run_pick = pick_codes(r)
    begin_pick()
    got_pout = [moves.start(r.pout_own.at[0], r.pout_v.at[branch])]
    frame_tables(r)
    if chunks:
        wait_barrier()
        sums.remote(r.pout_own.at[0], r.pout_v.at[branch], sums.partner[bits - 1], POUT)
    else:
        got_pout.append(moves.start(r.pout_other.at[0], r.pout_v.at[1 - branch]))
    got_rest = [
        moves.start(r.distill, r.distill_v),
        moves.start(r.wavlm.at[pl.ds(pl.multiple_of(branch * rows, rows), rows)], r.wavlm_v),
    ]
    got_attention = [moves.start(r.dec_qkv, r.w_qkv_v), moves.start(r.dec_out, r.w_out_v)]
    got_ffn = [moves.start(r.dec_up, r.w_up_v), moves.start(r.dec_down, r.w_down_v)]
    got_cotangent = [moves.start(r.cotangent, r.cotangent_v)]
    got_pin = [moves.start(r.pin_own.at[0], r.pin_v.at[branch])]
    if not chunks:
        got_pin.append(moves.start(r.pin_other.at[0], r.pin_v.at[1 - branch]))
    got_tokens = [moves.start(r.tokens, r.tokens_v)]
    got_attention_two = [moves.start(r.enc_qkv, r.w_qkv_e), moves.start(r.enc_out, r.w_out_e)]

    if chunks:
        def at(name, col=0):
            return Place(t[name], col, chunks[name])

        dec_down, enc_down = [at(DD0), at(DD1)], [at(ED0), at(ED1), at(ED2)]
        place = r.places = Refs(
            dec_up=[at(DU0), at(DU1)],
            dec_out=at(DA0),
            dec_qkv=[at(DA0, width), at(DA1), at(DA2)],
            enc_up=[at(EU0), at(EU1)],
            enc_out=at(EA0),
            enc_qkv=[at(EA1), at(EA2), at(EA3)],
            distill=at(DISTILL_GRAD),
            pout=at(MISC),
            pin=at(MISC, width),
        )
    else:
        dec_down, enc_down = [Place(t.dec_down)], [Place(t.enc_down)]
        place = r.places = Refs(
            dec_up=[Place(t.dec_up, i * tiles // 2 * TILE) for i in range(2)],
            dec_out=Place(t.dec_out),
            dec_qkv=[Place(t.dec_qkv, i * width) for i in range(3)],
            enc_up=[Place(t.enc_up, i * tiles // 2 * TILE) for i in range(2)],
            enc_out=Place(t.enc_out),
            enc_qkv=[Place(t.enc_qkv, i * width) for i in range(3)],
            distill=Place(t.distill),
            pout=Place(t.pout),
            pin=Place(t.pin),
        )

    def wait(moves, other=None):
        for move in moves:
            move.wait()
        if chunks and other is not None:
            sums.arrived(other)

    def layer_value(target, gain):
        for at in row_blocks(rows, 64):
            target[at, :] = (r.x2[at, :] + gain(3) * r.fo[at, :]).astype(BF16)

    def dec_gain(i):
        return r.vectors[1, i : i + 1, :]

    def enc_gain(i):
        return r.vectors[0, i : i + 1, :]

    def pick():
        run_pick()

    def semantic():
        wait(got_rest)
        quantizer_semantic(r)

    def quant():
        wait(got_pout, POUT)
        if chunks:
            sums.remote(r.pin_own.at[0], r.pin_v.at[branch], sums.partner[bits - 1], PIN)
        r.x[...] = dot(jnp.concatenate([r.chosen[0], r.ac[...]], axis=1), r.pout_v[...].reshape(-1, width))
        if chunks:
            for other in range(1, levels):
                target = sums.near_level(other)
                sums.remote(r.code_rows.at[target_level(target)], r.code_got.at[other], target, CODES, other)
            r.code_got[0] = r.code_rows[level]

    def target_level(target):
        return next(iter(target.values())) // 2

    def dec_project():
        wait(got_attention)
        attention_project(r, r.w_qkv_v, dec_gain)

    def dec_mix():
        attention_mix(r, r.w_out_v, dec_gain)

    def dec_ffn(half):
        def run():
            if half == 0:
                wait(got_ffn)
                wait(got_cotangent)
                ffn_backward_begin(r, dec_gain, r.cotangent_v)
            first, last = half * tiles // 2, (half + 1) * tiles // 2
            ffn_both(r, r.w_up_v, r.w_down_v, place.dec_up[half], dec_down, first, last)
            if half == 1:
                r.fo[...] = dot(r.act[...], r.w_down_v[...])
                layer_value(r.decoded, dec_gain)
                ffn_back_sum(r, r.w_up_v)
                ffn_backward_end(r, dec_gain, r.cotangent_v, r.dec_gains)
                got_ffn[:] = [moves.start(r.enc_up, r.w_up_v), moves.start(r.enc_down, r.w_down_v)]

        return run

    def dec_out():
        attention_backward_out(r, r.w_out_v, dec_gain, place.dec_out, r.dec_gains)

    def attention_pairs(first, last):
        return lambda: attention_backward_pairs(r, first, last)

    def dec_in(part):
        def run():
            attention_backward_in(r, place.dec_qkv[part], part)
            if part == 2:
                attention_backward_end(r, r.w_qkv_v, dec_gain, r.dec_gains)
                r.gquant[...] = r.gx[...].astype(BF16)

        return run

    def enc_project():
        wait(got_tokens)
        r.x[...] = r.tokens_v[...].astype(F32)
        wait(got_attention_two)
        attention_project(r, r.w_qkv_e, enc_gain)

    def enc_mix():
        attention_mix(r, r.w_out_e, enc_gain)

    def enc_ffn():
        wait(got_ffn)
        ffn_forward(r, r.w_up_v, r.w_down_v)
        layer_value(r.latent, enc_gain)

    def quantizer():
        wait(got_pin, PIN)
        quantizer_latent(r)
        if chunks:
            for other in reversed(range(1, levels)):
                target = sums.near_level(other)
                sums.arrived(CODES, other)
                sums.remote(r.g_rows.at[target_level(target)], r.g_got.at[other], target, BOOKS, 0, other)
            r.g_got[0] = r.g_rows[level]

    def book_half(core, put):
        quarter = entries // 4
        for side in range(2):
            r.book_sum[...] = jnp.zeros_like(r.book_sum)
            first = (core * 2 + side) * quarter

            def add(source, carry):
                one_hot = one_hot_rows(r.code_got[source, 0:1, :], first, quarter)
                r.book_sum[...] += dot(one_hot, r.g_got[source])
                return carry

            lax.fori_loop(0, levels, add, 0, unroll=4)
            put(side, r.book_sum[...])

    def finish_books(stage):
        blocks = entries // 4 // rows
        other_core, other_side = sums.partner[bits - 2], sums.partner[bits - 1]
        if stage == 0:
            for other in range(1, levels):
                sums.arrived(BOOKS, 0, other)

            def put(side, value):
                r.book_send[side] = value.astype(BF16)

            def keep(side, value):
                r.book_own[side * blocks : (side + 1) * blocks] = value.astype(BF16).reshape((blocks, rows, code_width))

            book_half(1 - mine, put)
            sums.remote(r.book_send, r.book_got, other_core, BOOKS, 1)
            book_half(mine, keep)
        elif stage == 1:
            sums.arrived(BOOKS, 1)
            for side in range(2):
                own = r.book_own[side * blocks : (side + 1) * blocks]
                r.book_got[side] = r.book_got[side] + own.reshape(r.book_got.shape[1:])
            sums.remote(r.book_got.at[1 - branch], r.book_last, other_side, BOOKS, 2)
        else:
            sums.arrived(BOOKS, 2)
            total = r.book_got[branch].astype(F32) + r.book_last[...].astype(F32)
            blocks = code_width // 128
            store_segment(r.packed, first_rows[BOOKS], Segment(BOOKS, 0, blocks, 0, blocks, 0, entries // 4), total)

    def all_books():
        parts = entries // TILE

        def one(step, carry):
            at = step // parts
            one_hot = one_hot_rows(r.code_rows[at, 0:1, :], step % parts * TILE, TILE)
            t.books[at, aligned(step % parts, TILE), :] = dot(one_hot, r.g_rows[at]).astype(BF16)
            return carry

        lax.fori_loop(0, levels * parts, one, 0)

    def enc_ffn_back(half):
        def run():
            first, last = half * tiles // 2, (half + 1) * tiles // 2
            if half == 0:
                ffn_backward_begin(r, enc_gain, r.gy)
            ffn_backward_tiles(r, r.w_down_v, place.enc_up[half], enc_down, first, last)
            if half == 1:
                ffn_back_sum(r, r.w_up_v)
                ffn_backward_end(r, enc_gain, r.gy, r.gains)

        return run

    def enc_out():
        attention_backward_out(r, r.w_out_e, enc_gain, place.enc_out, r.gains)

    def enc_in(part):
        def run():
            attention_backward_in(r, place.enc_qkv[part], part)
            if part == 2:
                attention_backward_end(r, r.w_qkv_e, enc_gain, r.gains)
                r.grad_tokens[...] = r.gx[...]
                if chunks:
                    spread_gains()

        return run

    def spread_gains():
        last, height = chunks[EA3], t.ea3.shape[1]
        for layer, ref in enumerate((r.gains, r.dec_gains)):
            for row in range(4):
                for block in range(width // 128):
                    owner = (layer * 4 + row) * (width // 128) + block
                    value = jnp.broadcast_to(ref[row : row + 1, block * 128 : (block + 1) * 128], (height, 128))
                    t.ea3[last.index(owner), :, width : width + 128] = value.astype(BF16)

    work = [
        (6.5, pick, ()),
        (2.0, semantic, (DISTILL_GRAD,)),
        (0.7, quant, ()),
        (1.5, dec_project, ()),
        (2.5, dec_mix, ()),
        (2.6, dec_ffn(0), (DU0,)),
        (2.7, dec_ffn(1), (DD0, DD1, DU1)),
        (1.2, dec_out, ()),
        (1.6, attention_pairs(0, pairs // 2), ()),
        (1.6, attention_pairs(pairs // 2, pairs), ()),
        (0.6, dec_in(0), (DA0,)),
        (0.6, dec_in(1), (DA1,)),
        (0.8, dec_in(2), (DA2,)),
        (1.5, enc_project, ()),
        (2.5, enc_mix, ()),
        (2.2, enc_ffn, ()),
        (2.0, quantizer, (BOOKS, MISC)),
        (2.0, enc_ffn_back(0), (EU0,)),
        (2.0, enc_ffn_back(1), (EU1, ED0, ED1, ED2)),
        (1.2, enc_out, (EA0,)),
        (1.6, attention_pairs(0, pairs // 2), ()),
        (1.6, attention_pairs(pairs // 2, pairs), ()),
        (0.6, enc_in(0), (EA1,)),
        (0.6, enc_in(1), (EA2,)),
        (1.0, enc_in(2), (EA3,)),
    ]
    if not chunks:
        for _, run, _ in work:
            run()
            if run is quantizer:
                all_books()
        return
    actions = plan(chunks, work, bits, rows * code_width * 2)

    def finish(name, stage):
        if name == BOOKS:
            finish_books(stage)
        else:
            sums.finish(name, stage, r.recv[name][stage - 1] if stage else t[name])

    for (_, run, made), acts in zip(work, actions):
        run()
        for name in made:
            if name != BOOKS:
                sums.send_half(name, 0, t[name])
        for name, stage in acts:
            finish(name, stage)
    for name, stage in actions[-1]:
        finish(name, stage)
    sums.drain()


POUT, PIN, CODES = 1, 2, 3
DISTILL_GRAD = "di"
DD0, DD1, DU0, DU1, DA0, DA1, DA2, MISC = "dd0", "dd1", "du0", "du1", "da0", "da1", "da2", "misc"
EU0, EU1, ED0, ED1, ED2 = "eu0", "eu1", "ed0", "ed1", "ed2"
EA0, EA1, EA2, EA3 = "ea0", "ea1", "ea2", "ea3"


def step(given, devices, with_sums):
    rows, width = given.tokens.shape
    ff = given.enc_up.shape[1]
    levels, entries, code_width = given.books.shape
    given.books = given.books.reshape(levels, -1, rows, code_width)
    bits = devices.bit_length() - 1
    vmem, hbm = pl.BlockSpec(memory_space=pltpu.VMEM), pl.BlockSpec(memory_space=pl.ANY)
    scratch = layer_scratch(rows, width, ff)
    scratch.update(
        w_qkv_e=pltpu.VMEM((width, 3 * width), BF16),
        w_out_e=pltpu.VMEM((width, width), BF16),
        cos=pltpu.VMEM((rows, PAIR), F32),
        sin=pltpu.VMEM((rows, PAIR), F32),
        bias=pltpu.VMEM((rows, rows), F32),
        ring=pltpu.VMEM((4,) + given.books.shape[1:], BF16),
        code_rows=pltpu.VMEM((levels, 8, rows), jnp.int32),
        chosen=pltpu.VMEM((levels, rows, code_width), BF16),
        ac=pltpu.VMEM((rows, code_width), BF16),
        gquant=pltpu.VMEM((rows, width), BF16),
        gy=pltpu.VMEM((rows, width), F32),
        latent=pltpu.VMEM((rows, width), BF16),
        pin_v=pltpu.VMEM((2, width, code_width), BF16),
        pout_v=pltpu.VMEM((2, code_width, width), BF16),
        distill_v=pltpu.VMEM(given.distill.shape, BF16),
        wavlm_v=pltpu.VMEM((rows, given.wavlm.shape[1]), BF16),
        tokens_v=pltpu.VMEM((rows, width), BF16),
        cotangent_v=pltpu.VMEM((rows, width), BF16),
        sem_move=pltpu.SemaphoreType.DMA((14,)),
        sem_book=pltpu.SemaphoreType.DMA((4,)),
    )
    outs = Refs(decoded=shaped((rows, width), BF16), grad_tokens=shaped((rows, width), F32))
    chunks, first_rows = {}, {}
    params = dict(vmem_limit_bytes=60 * 2**20)
    if with_sums:
        params.update(collective_id=0, has_side_effects=True)
        c, x, y = bits - 2, bits - 1, bits - 3
        b, a = range(y)
        share = width // devices
        low, high = ff // devices, share
        wide, half, blocks = ff // 128, ff // 256, width // 128
        third, quarter = 3 * blocks, blocks // 4
        chunks = dict(
            di=Chunk(
                high,
                width,
                [c, y, x, a, b],
                [
                    Segment(8, 0, 2 * blocks, 0, blocks, 0, high // 2),
                    Segment(8, blocks, 2 * blocks, 0, blocks, high // 2, high // 2),
                ],
            ),
            du0=Chunk(high, ff // 2, [c, y, a, x, b], [Segment(2, 0, wide, 0, half, 0, high)]),
            dd0=Chunk(low, width // 2, [c, a, y, b, x], [Segment(3, 0, blocks, 0, 2 * quarter, 0, low)]),
            dd1=Chunk(low, width // 2, [c, y, x, a, b], [Segment(3, 2 * quarter, blocks, 0, 2 * quarter, 0, low)]),
            du1=Chunk(high, ff // 2, [c, x, y, a, b], [Segment(2, half, wide, 0, half, 0, high)]),
            da0=Chunk(
                high,
                2 * width,
                [c, x, y, a, b],
                [Segment(1, 0, blocks, 0, blocks, 0, high), Segment(0, 0, third, width, blocks, 0, high)],
            ),
            da1=Chunk(high, width, [c, a, x, y, b], [Segment(0, blocks, third, 0, blocks, 0, high)]),
            da2=Chunk(high, width, [c, y, x, a, b], [Segment(0, 2 * blocks, third, 0, blocks, 0, high)]),
            misc=Chunk(
                high,
                2 * width,
                [c, x, y, a, b],
                [
                    Segment(9, 0, blocks, 0, blocks, 0, high),
                    Segment(10, 0, blocks // 2, width, blocks // 2, 0, high),
                    Segment(10, high * blocks // 2, blocks // 2, width + code_width, blocks // 2, 0, high),
                ],
            ),
            eu0=Chunk(high, ff // 2, [c, x, a, y, b], [Segment(6, 0, wide, 0, half, 0, high)]),
            eu1=Chunk(high, ff // 2, [c, x, y, a, b], [Segment(6, half, wide, 0, half, 0, high)]),
            ed0=Chunk(low, width // 2, [c, x, y, a, b], [Segment(7, 0, blocks, 0, 2 * quarter, 0, low)]),
            ed1=Chunk(low, width // 4, [c, y, x, a, b], [Segment(7, 2 * quarter, blocks, 0, quarter, 0, low)]),
            ed2=Chunk(low, width // 4, [c, y, a, b, x], [Segment(7, 3 * quarter, blocks, 0, quarter, 0, low)]),
            ea0=Chunk(high, width, [c, x, y, a, b], [Segment(5, 0, blocks, 0, blocks, 0, high)]),
            ea1=Chunk(high, width, [c, y, x, a, b], [Segment(4, 0, third, 0, blocks, 0, high)]),
            ea2=Chunk(high, width, [c, x, a, y, b], [Segment(4, blocks, third, 0, blocks, 0, high)]),
            ea3=Chunk(
                high,
                width + 128,
                [c, x, y, a, b],
                [Segment(4, 2 * blocks, third, 0, blocks, 0, high), Segment(11, 0, 1, width, 1, 0, 8)],
            ),
        )
        rows_of = [high * 3 * blocks, high * blocks, high * wide, low * blocks] * 2
        rows_of += [high * blocks, high * blocks, high * blocks, 8, entries // 4 * code_width // 128]
        first_rows = {i: sum(rows_of[:i]) for i in range(len(rows_of))}
        first_rows[BOOKS] = first_rows[len(rows_of) - 1]
        copies = len(chunks) * bits + 2 * levels + 2
        scratch.update(
            t={name: pltpu.VMEM(c.shape(bits), BF16) for name, c in chunks.items()},
            recv={
                name: [pltpu.VMEM(c.shape(bits - 1 - stage), BF16) for stage in range(bits)]
                for name, c in chunks.items()
            },
            gains=pltpu.VMEM((4, width), F32),
            dec_gains=pltpu.VMEM((4, width), F32),
            code_got=pltpu.VMEM((levels, 8, rows), jnp.int32),
                book_sum=pltpu.VMEM((entries // 4, code_width), F32),
            book_send=pltpu.VMEM((2, entries // 4, code_width), BF16),
            book_got=pltpu.VMEM((2, entries // 4, code_width), BF16),
            book_last=pltpu.VMEM((entries // 4, code_width), BF16),
            send_sem=pltpu.SemaphoreType.DMA((copies,)),
            recv_sem=pltpu.SemaphoreType.DMA((copies,)),
        )
        outs.packed = shaped((sum(rows_of), 128), F32)
    else:
        outs.update(gains=shaped((4, width), F32), dec_gains=shaped((4, width), F32))
        outs.t = dict(
            enc_qkv=shaped(given.enc_qkv.shape, BF16),
            enc_out=shaped(given.enc_out.shape, BF16),
            enc_up=shaped(given.enc_up.shape, BF16),
            enc_down=shaped(given.enc_down.shape, BF16),
            dec_qkv=shaped(given.enc_qkv.shape, BF16),
            dec_out=shaped(given.enc_out.shape, BF16),
            dec_up=shaped(given.enc_up.shape, BF16),
            dec_down=shaped(given.enc_down.shape, BF16),
            pin=shaped((2 * width, code_width), BF16),
            pout=shaped((2 * code_width, width), BF16),
            books=shaped((levels, entries, code_width), BF16),
            distill=shaped(given.distill.shape, BF16),
        )
    in_specs = dict.fromkeys(given, hbm)
    in_specs.update(
        lengths=pl.BlockSpec(memory_space=pltpu.SMEM), codes=vmem, vectors=vmem
    )
    got = pl.pallas_call(
        functools.partial(step_kernel, chunks, first_rows, bits),
        out_shape={k: pltpu.VMEM(v.shape, v.dtype) for k, v in outs.items()} if with_sums else dict(outs),
        in_specs=[in_specs],
        out_specs=jax.tree.map(lambda _: vmem, dict(outs)),
        scratch_shapes=[dict(scratch)],
        compiler_params=pltpu.CompilerParams(**params),
        name="step",
    )(dict(given))
    got = Refs(got)
    if not with_sums:
        return got
    last = [shaped((rows, 128), F32) for rows in rows_of]
    last[11] = shaped((1, 128), F32)

    def hand_on(packed, decoded, grad, *refs):
        outs, moves = refs[:-1], Moves(refs[-1])
        parts = [packed.at[pl.ds(first_rows[i], ref.shape[0])] for i, ref in enumerate(outs[:-2])]
        leaving = [moves.start(part, ref) for part, ref in zip(parts + [decoded, grad], outs)]
        for move in leaving:
            move.wait()

    return pl.pallas_call(
        hand_on,
        out_shape=last + [outs.decoded, outs.grad_tokens],
        in_specs=[vmem] * 3,
        out_specs=[hbm] * (len(last) + 2),
        scratch_shapes=[pltpu.SemaphoreType.DMA((len(last) + 2,))],
        compiler_params=pltpu.CompilerParams(vmem_limit_bytes=16 * 2**20),
        name="results",
    )(got.packed, got.decoded, got.grad_tokens)


def body(
    tokens,
    wavlm,
    cotangent,
    lengths,
    codes,
    enc_qkv,
    enc_out,
    enc_up,
    enc_down,
    dec_qkv,
    dec_out,
    dec_up,
    dec_down,
    vectors,
    proj_in,
    proj_out,
    codebooks,
    distill_proj,
):
    width = tokens.shape[1]
    devices = lax.axis_size("dp") * lax.axis_size("branch")
    with_sums = devices == 4 * codebooks.shape[0] and width // devices % 16 == 0
    given = Refs(
        tokens=tokens,
        wavlm=wavlm,
        cotangent=cotangent,
        lengths=lengths,
        codes=codes.T,
        enc_qkv=enc_qkv,
        enc_out=enc_out,
        enc_up=enc_up,
        enc_down=enc_down,
        dec_qkv=dec_qkv,
        dec_out=dec_out,
        dec_up=dec_up,
        dec_down=dec_down,
        vectors=vectors,
        pin_own=proj_in,
        pout_own=proj_out,
        books=codebooks,
        distill=distill_proj,
    )
    if with_sums:
        *sums, decoded, grad_tokens = step(given, devices, True)
        sums = [part.reshape(-1) for part in sums]
        order = (4, 5, 6, 7, 0, 1, 2, 3, 11, 10, 9, 12, 8)
        return (decoded, grad_tokens, *[sums[i] for i in order])
    swap = [(0, 1), (1, 0)]
    given.pin_other = lax.ppermute(proj_in, "branch", swap)
    given.pout_other = lax.ppermute(proj_out, "branch", swap)
    s = step(given, devices, False)
    t = Refs(s.t)
    gains = jnp.concatenate([s.gains, s.dec_gains])
    local = [t.enc_qkv, t.enc_out, t.enc_up, t.enc_down, t.dec_qkv, t.dec_out, t.dec_up, t.dec_down]
    local += [gains, t.pin, t.pout, t.books, t.distill]
    sums = [
        lax.psum_scatter(part.astype(F32).reshape(-1), ("dp", "branch"), scatter_dimension=0, tiled=True)
        for part in local
    ]
    return (s.decoded, s.grad_tokens, *sums)


def solution(mesh):
    rows, whole = P(("dp", "branch"), None), P()
    placed = (rows, P("dp", None), rows, rows, P("dp", None)) + (whole,) * 9
    placed += (P("branch", None, None),) * 2 + (whole,) * 2
    return jax.shard_map(
        body,
        mesh=mesh,
        in_specs=placed,
        out_specs=(rows, rows) + (P(("dp", "branch")),) * 13,
        check_vma=False,
    )
```

```python
import functools
import math

import jax
import jax.numpy as jnp
from jax import lax
from jax.experimental import pallas as pl
from jax.experimental.pallas import tpu as pltpu
from jax.sharding import PartitionSpec as P

HEADS = 8
WINDOW = 250
EPS_NORM = 1e-05
EPS_COS = 1e-06
BETA = 0.25
DISTILL = 10.0
ROPE_BASE = 10000.0

MESH = pl.DeviceIdType.MESH
F32 = jnp.float32
BF16 = jnp.bfloat16
TILE = 512
PAIR = 128
HALF = 256


def dot(left, right):
    return lax.dot_general(left, right, (((1,), (0,)), ((), ())), preferred_element_type=F32)


def dot_t(left, right):
    return lax.dot_general(left, right, (((1,), (1,)), ((), ())), preferred_element_type=F32)


def t_dot(left, right):
    return lax.dot_general(left, right, (((0,), (0,)), ((), ())), preferred_element_type=F32)


def iota(shape, dim):
    return lax.broadcasted_iota(jnp.int32, shape, dim)


def aligned(index, size):
    return pl.ds(pl.multiple_of(index * size, size), size)


class Refs(dict):
    __getattr__ = dict.__getitem__
    __setattr__ = dict.__setitem__


class Moves:
    def __init__(self, semaphores):
        self.semaphores, self.count = semaphores, 0

    def start(self, source, target):
        move = pltpu.make_async_copy(source, target, self.semaphores.at[self.count])
        self.count += 1
        move.start()
        return move


def layer_scratch(rows, width, ff):
    return Refs(
        x=pltpu.VMEM((rows, width), F32),
        s1=pltpu.VMEM((rows, 1), F32),
        h=pltpu.VMEM((rows, width), BF16),
        h1t=pltpu.VMEM((width, rows), BF16),
        h2t=pltpu.VMEM((width, rows), BF16),
        rinv=pltpu.VMEM((rows, width), F32),
        qkv=pltpu.VMEM((rows, 3 * width), BF16),
        mix=pltpu.VMEM((rows, width), BF16),
        ao=pltpu.VMEM((rows, width), F32),
        x2=pltpu.VMEM((rows, width), F32),
        s2=pltpu.VMEM((rows, 1), F32),
        act=pltpu.VMEM((rows, ff), BF16),
        dg=pltpu.VMEM((rows, ff), BF16),
        fo=pltpu.VMEM((rows, width), F32),
        grad=pltpu.VMEM((rows, width), BF16),
        gx=pltpu.VMEM((rows, width), F32),
        acc=pltpu.VMEM((rows, width), F32),
        wide=pltpu.VMEM((4, rows, HALF), F32),
        change=pltpu.VMEM((2, rows, rows), BF16),
        w_qkv_v=pltpu.VMEM((width, 3 * width), BF16),
        w_out_v=pltpu.VMEM((width, width), BF16),
        w_up_v=pltpu.VMEM((width, ff), BF16),
        w_down_v=pltpu.VMEM((ff, width), BF16),
    )


def shaped(shape, kind):
    return jax.ShapeDtypeStruct(shape, kind)


def frame_tables(r):
    rows = r.cos.shape[0]
    place = iota((rows, PAIR), 0)
    query, key = iota((rows, rows), 0), iota((rows, rows), 1)
    begin, begin_query = jnp.zeros_like(place), jnp.zeros_like(query)
    edge = 0
    for clip in range(r.lengths.shape[1] - 1):
        edge = edge + r.lengths[0, clip]
        begin = jnp.where(place >= edge, edge, begin)
        begin_query = jnp.where(query >= edge, edge, begin_query)
    allowed = (key >= begin_query) & (key <= query) & (query - key < WINDOW)
    r.bias[...] = jnp.where(allowed, 0.0, -1e30)
    lane = iota((rows, PAIR), 1)
    rate = jnp.exp((lane % 32).astype(F32) * (-math.log(ROPE_BASE) / 32))
    angle = (place - begin).astype(F32) * rate
    r.cos[...] = jnp.cos(angle)
    sine = jnp.sin(angle)
    r.sin[...] = jnp.where(lane % 64 < 32, -sine, sine)


def rotated(value, cosine, sine):
    lane = iota(value.shape, 1)
    swapped = jnp.where(lane % 64 < 32, pltpu.roll(value, PAIR - 32, 1), pltpu.roll(value, 32, 1))
    return value * cosine + swapped * sine


def head_masks(rows):
    low = iota((rows, PAIR), 1) < 64
    return (jnp.where(low, 1.0, 0.0).astype(BF16), jnp.where(low, 0.0, 1.0).astype(BF16))


def row_blocks(rows, step):
    return [slice(i, i + step) for i in range(0, rows, step)]


def attention_project(r, w_qkv, gain):
    rows, width = r.x.shape
    scale = gain(0)
    for at in row_blocks(rows, 64):
        x = r.x[at, :]
        s1 = lax.rsqrt(jnp.mean(x * x, axis=1, keepdims=True) + EPS_NORM)
        r.s1[at, :] = s1
        r.h[at, :] = (x * s1 * scale).astype(BF16)
    for half in range(3 * width // HALF):
        slot, part = half % 4, half // (width // HALF)
        cols = slice(half * HALF, (half + 1) * HALF)
        r.wide[slot] = dot(r.h[...], w_qkv[:, cols])
        for at in row_blocks(rows, 64):
            for p in range(HALF // PAIR):
                value = r.wide[slot, at, p * PAIR : (p + 1) * PAIR]
                if part < 2:
                    value = rotated(value, r.cos[at, :], r.sin[at, :])
                low = value.astype(BF16)
                if part == 0:
                    low = (low.astype(F32) * 0.125).astype(BF16)
                r.qkv[at, half * HALF + p * PAIR : half * HALF + (p + 1) * PAIR] = low
    r.h1t[...] = r.h[...].T


def attention_mix(r, w_out, gain):
    rows, width = r.x.shape
    masks = head_masks(rows)
    low = iota((rows, PAIR), 1) < 64
    pairs = width // PAIR
    for p in range(pairs):
        query = r.qkv[:, p * PAIR : (p + 1) * PAIR]
        key = r.qkv[:, (p + pairs) * PAIR : (p + pairs + 1) * PAIR]
        value = r.qkv[:, (p + 2 * pairs) * PAIR : (p + 2 * pairs + 1) * PAIR]
        outs = []
        for h in range(2):
            head = 2 * p + h
            slot = head % 4
            r.wide[slot] = dot_t(query * masks[h], key)
            for at in row_blocks(rows, 64):
                seen = PAIR if at.stop <= PAIR else rows
                scores = r.wide[slot, at, :seen] + r.bias[at, :seen]
                weights = jnp.exp(scores - jnp.max(scores, axis=1, keepdims=True))
                r.att[head, at, :seen] = weights.astype(BF16)
                if seen < rows:
                    r.att[head, at, seen:] = jnp.zeros((64, rows - seen), BF16)
            outs.append(dot(r.att[head], value * masks[h] + masks[1 - h]))
        inverse = 1.0 / pltpu.roll(jnp.where(low, outs[1], outs[0]), 64, 1)
        r.rinv[:, p * PAIR : (p + 1) * PAIR] = inverse
        r.mix[:, p * PAIR : (p + 1) * PAIR] = (jnp.where(low, outs[0], outs[1]) * inverse).astype(BF16)
    r.ao[...] = dot(r.mix[...], w_out[...])
    scale_one, scale_two = gain(1), gain(2)
    for at in row_blocks(rows, 64):
        x2 = r.x[at, :] + scale_one * r.ao[at, :]
        r.x2[at, :] = x2
        s2 = lax.rsqrt(jnp.mean(x2 * x2, axis=1, keepdims=True) + EPS_NORM)
        r.s2[at, :] = s2
        r.h[at, :] = (x2 * s2 * scale_two).astype(BF16)
    r.h2t[...] = r.h[...].T


def gelu_parts(pre):
    slope = math.sqrt(2.0 / math.pi)
    square = pre * pre
    bent = jnp.tanh(slope * pre * (1.0 + 0.044715 * square))
    half = 0.5 * (1.0 + bent)
    turn = 0.5 * pre * (1.0 - bent * bent) * slope * (1.0 + 3.0 * 0.044715 * square)
    return (pre * half).astype(BF16), half + turn


def ffn_forward(r, w_up, w_down):
    rows, ff = r.act.shape
    for half in range(ff // HALF):
        slot, cols = half % 4, slice(half * HALF, (half + 1) * HALF)
        r.wide[slot] = dot(r.h[...], w_up[:, cols])
        for at in row_blocks(rows, 32):
            act, slope = gelu_parts(r.wide[slot, at, :])
            r.act[at, cols] = act
            r.dg[at, cols] = slope.astype(BF16)
    r.fo[...] = dot(r.act[...], w_down[...])


def ffn_both(r, w_up, w_down, grad_up, grad_down, first, last):
    rows = r.act.shape[0]
    for t in range(first, last):
        cols = slice(t * TILE, (t + 1) * TILE)
        for side in range(TILE // HALF):
            part = slice(t * TILE + side * HALF, t * TILE + (side + 1) * HALF)
            r.wide[side] = dot(r.h[...], w_up[:, part])
            r.wide[2 + side] = dot_t(r.grad[...], w_down[part, :])
            for at in row_blocks(rows, 32):
                act, slope = gelu_parts(r.wide[side, at, :])
                r.act[at, part] = act
                r.dg[at, part] = (r.wide[2 + side, at, :] * slope).astype(BF16)
        grad_up.shift((t - first) * TILE).put(dot(r.h2t[...], r.dg[:, cols]))
        put_rows(grad_down, t_dot(r.act[:, cols], r.grad[...]), t)


def ffn_back_sum(r, w_up):
    r.acc[...] = dot_t(r.dg[...], w_up[...])


def norm_back(stream, inverse, grad):
    mean = jnp.mean(grad * stream, axis=1, keepdims=True)
    return inverse * grad - stream * (inverse * inverse * inverse * mean)


def column_sum(value):
    return jnp.sum(value, axis=0, keepdims=True)


class Place:
    def __init__(self, ref, col=0, chunk=None):
        self.ref, self.col, self.chunk = ref, col, chunk

    def shift(self, by):
        return Place(self.ref, self.col + by, self.chunk)

    def put(self, value):
        value = value.astype(BF16)
        cols = slice(self.col, self.col + value.shape[1])
        if self.chunk is None:
            self.ref[:, cols] = value
            return
        blocks, rows = self.ref.shape[:2]
        for owner in range(blocks):
            self.ref[self.chunk.index(owner), :, cols] = value[owner * rows : (owner + 1) * rows]


def put_rows(places, value, tile):
    value = value.astype(BF16)
    begin = 0
    for place in places:
        part = value[:, begin : begin + place.ref.shape[-1]]
        begin += place.ref.shape[-1]
        if place.chunk is None:
            place.ref[tile * TILE : tile * TILE + TILE, :] = part
            continue
        rows = place.ref.shape[1]
        for i in range(TILE // rows):
            place.ref[place.chunk.index(tile * (TILE // rows) + i)] = part[i * rows : (i + 1) * rows]


def ffn_backward_begin(r, gain, gy_ref):
    scale = gain(3)
    for at in row_blocks(r.grad.shape[0], 64):
        r.grad[at, :] = (scale * gy_ref[at, :].astype(F32)).astype(BF16)


def ffn_backward_tiles(r, w_down, grad_up, grad_down, first, last):
    rows = r.act.shape[0]
    for t in range(first, last):
        cols = slice(t * TILE, (t + 1) * TILE)
        for side in range(TILE // HALF):
            part = slice(t * TILE + side * HALF, t * TILE + (side + 1) * HALF)
            slot = (2 * t + side) % 4
            r.wide[slot] = dot_t(r.grad[...], w_down[part, :])
            for at in row_blocks(rows, 64):
                r.dg[at, part] = (r.wide[slot, at, :] * r.dg[at, part].astype(F32)).astype(BF16)
        put_rows(grad_down, t_dot(r.act[:, cols], r.grad[...]), t)
        grad_up.shift((t - first) * TILE).put(dot(r.h2t[...], r.dg[:, cols]))


def ffn_backward_end(r, gain, gy_ref, gain_out):
    scale = gain(2)
    to_gain = to_scale = 0.0
    for at in row_blocks(r.x2.shape[0], 32):
        gy = gy_ref[at, :].astype(F32)
        to_scale = to_scale + column_sum(gy * r.fo[at, :])
        back, x2, s2 = r.acc[at, :], r.x2[at, :], r.s2[at, :]
        to_gain = to_gain + column_sum(back * x2 * s2)
        r.gx[at, :] = gy + norm_back(x2, s2, back * scale)
    gain_out[3:4, :] = to_scale
    gain_out[2:3, :] = to_gain


def attention_backward_out(r, w_out, gain, grad_out, gain_out):
    scale = gain(1)
    to_scale = 0.0
    for at in row_blocks(r.gx.shape[0], 64):
        gx = r.gx[at, :]
        to_scale = to_scale + column_sum(gx * r.ao[at, :])
        r.grad[at, :] = (scale * gx).astype(BF16)
    gain_out[1:2, :] = to_scale
    grad_out.put(t_dot(r.mix[...], r.grad[...]))
    r.grad[...] = dot_t(r.grad[...], w_out[...]).astype(BF16)


def attention_backward_pairs(r, first, last):
    rows, width = r.x.shape
    masks = head_masks(rows)
    masks_t = [jnp.where((iota((PAIR, rows), 0) < 64) == (h == 0), 1.0, 0.0).astype(BF16) for h in range(2)]
    pairs = width // PAIR
    for p in range(first, last):
        lanes = [slice((p + i * pairs) * PAIR, (p + i * pairs + 1) * PAIR) for i in range(3)]
        query, key, value = (r.qkv[:, at] for at in lanes)
        grad_mixed = (r.grad[:, lanes[0]].astype(F32) * r.rinv[:, lanes[0]]).astype(BF16)
        product = (grad_mixed.astype(F32) * r.mix[:, lanes[0]].astype(F32)).astype(BF16)
        beside = jnp.concatenate([value, jnp.full(value.shape, -1.0, BF16)], axis=1)
        query_t, grad_t = query.T, grad_mixed.T
        to_query = to_key = to_value = 0.0
        for h in range(2):
            head = 2 * p + h
            slot = head % 4
            both = jnp.concatenate([grad_mixed * masks[h], product * masks[h]], axis=1)
            r.wide[slot] = dot_t(both, beside)
            for at in row_blocks(rows, 64):
                r.change[h, at, :] = (r.att[head, at, :].astype(F32) * r.wide[slot, at, :]).astype(BF16)
            to_query = to_query + dot(r.change[h], key * masks[h])
            to_key = to_key + dot(query_t * masks_t[h], r.change[h])
            to_value = to_value + dot(grad_t * masks_t[h], r.att[head])
        cosine, sine = r.cos[...], -r.sin[...]
        r.qkv[:, lanes[0]] = rotated(to_query * 0.125, cosine, sine).astype(BF16)
        r.qkv[:, lanes[1]] = rotated(to_key.T, cosine, sine).astype(BF16)
        r.qkv[:, lanes[2]] = to_value.T.astype(BF16)


def attention_backward_in(r, grad_qkv, part):
    width = r.x.shape[1]
    grad_qkv.put(dot(r.h1t[...], r.qkv[:, part * width : (part + 1) * width]))


def attention_backward_end(r, w_qkv, gain, gain_out):
    r.acc[...] = dot_t(r.qkv[...], w_qkv[...])
    scale = gain(0)
    to_gain = 0.0
    for at in row_blocks(r.x.shape[0], 32):
        back, x, s1 = r.acc[at, :], r.x[at, :], r.s1[at, :]
        to_gain = to_gain + column_sum(back * x * s1)
        r.gx[at, :] = r.gx[at, :] + norm_back(x, s1, back * scale)
    gain_out[0:1, :] = to_gain


class Segment:
    def __init__(self, result, base, stride, col, blocks, row, rows):
        self.result, self.base, self.stride, self.col, self.blocks = result, base, stride, col, blocks
        self.row, self.rows = row, rows


class Chunk:
    def __init__(self, rows, columns, order, segments):
        self.rows, self.columns, self.order, self.segments = rows, columns, order, segments

    def index(self, owner):
        bits = len(self.order)
        return sum((owner >> (bits - 1 - dim) & 1) << (bits - 1 - stage) for stage, dim in enumerate(self.order))

    def shape(self, leading):
        return (2**leading, self.rows, self.columns)

    def bytes(self, bits):
        return 2**bits * self.rows * self.columns * 2


def plan(chunks, work, bits, book_bytes):
    core, x, y = bits - 2, bits - 1, bits - 3
    ends, middle = -1, -2
    free, pending, done = {}, [], []
    now = 0.0

    def carry(link, size, rate=42e3):
        free[link] = max(now, free.get(link, 0.0)) + size / rate
        return free[link]

    def begin(name, stage):
        if name == BOOKS:
            size = 1.2 * 2 ** (bits - 3) * book_bytes
            if stage == 0:
                there = max(carry(y, size), carry(ends, 1.5 * size), carry(middle, 2 * size))
            else:
                there = carry(core, 4 * book_bytes, 400e3) if stage == 1 else carry(x, 2 * book_bytes)
        else:
            dim = chunks[name].order[stage]
            size = chunks[name].bytes(bits) / 2 ** (stage + 1)
            if dim == core:
                there = carry(core, size, 400e3)
            elif dim == x or dim == y:
                there = carry(dim, size)
            else:
                there = carry(ends, size)
                if dim < y - 1:
                    there = max(there, carry(middle, 2 * size))
        pending.append((there + 1.5, name, stage))

    def finish(limit):
        nonlocal now
        acts = []
        while pending:
            pending.sort(key=lambda p: p[0])
            if pending[0][0] + (0.5 if limit < math.inf else 0.0) > limit:
                break
            at, name, stage = pending.pop(0)
            if name == BOOKS:
                cost = (6.0, 0.6, 0.3)[stage]
            else:
                cost = 0.25 + 0.3e-6 * chunks[name].bytes(bits) / 2 ** (stage + 1)
            now = max(now, at) + cost
            limit = max(limit, now)
            acts.append((name, stage))
            if stage + 1 < (3 if name == BOOKS else bits):
                begin(name, stage + 1)
        return acts

    for took, _, names in work:
        now += 0.95 * took
        for name in names:
            begin(name, 0)
        done.append(finish(now))
    done.append(finish(math.inf))
    return done


def store_segment(packed, first, segment, value):
    for i in range(segment.blocks):
        where = pl.ds(first + segment.base + i, segment.rows, stride=segment.stride)
        packed[where, :] = value[
            segment.row : segment.row + segment.rows, segment.col + i * 128 : segment.col + (i + 1) * 128
        ]


class Halving:
    def __init__(self, chunks, bits, recv, packed, first, send_sem, recv_sem):
        self.chunks = chunks
        self.bits, self.recv, self.packed, self.first = bits, recv, packed, first
        self.send_sem, self.recv_sem = send_sem, recv_sem
        self.copies = {}
        dp, branch = lax.axis_index("dp"), lax.axis_index("branch")
        self.mine, self.partner = [], []
        for dim in range(bits - 1):
            weight = 2 ** (bits - 2 - dim)
            bit = dp // weight % 2
            self.mine.append(bit)
            self.partner.append({"dp": dp + weight * (1 - 2 * bit), "branch": branch})
        self.mine.append(branch)
        self.partner.append({"dp": dp, "branch": 1 - branch})

    def near_level(self, other):
        dp = lax.axis_index("dp")
        for i in range(self.bits - 2):
            if other >> i & 1:
                dp = dp + 2 ** (i + 1) * (1 - 2 * self.mine[self.bits - 3 - i])
        return {"dp": dp, "branch": lax.axis_index("branch")}

    def barrier(self):
        semaphore = pltpu.get_barrier_semaphore()
        levels = 2 ** (self.bits - 2)
        targets = self.partner[self.bits - 2 :] + [self.near_level(other) for other in range(1, levels)]
        for target in targets:
            pl.semaphore_signal(semaphore, inc=1, device_id=target, device_id_type=MESH)
        return lambda: pl.semaphore_wait(semaphore, len(targets))

    def half(self, ref, name, stage, other):
        mine = self.mine[self.chunks[name].order[stage]]
        count = 2 ** (self.bits - 1 - stage)
        return ref.at[pl.ds((1 - mine if other else mine) * count, count)]

    def remote(self, source, target, device, *key):
        slot = len(self.copies)
        self.copies[key] = pltpu.make_async_remote_copy(
            src_ref=source,
            dst_ref=target,
            send_sem=self.send_sem.at[slot],
            recv_sem=self.recv_sem.at[slot],
            device_id=device,
            device_id_type=MESH,
        )
        self.copies[key].start()

    def send(self, name, stage, source):
        dim = self.chunks[name].order[stage]
        self.remote(source, self.recv[name][stage], self.partner[dim], name, stage)

    def send_half(self, name, stage, ref):
        self.send(name, stage, self.half(ref, name, stage, True))

    def arrived(self, *key):
        self.copies[key].wait_recv()

    def add(self, name, stage, own):
        chunk = self.chunks[name]
        got = self.recv[name][stage]
        if stage == self.bits - 1:
            value = own[0].astype(F32) + got[0].astype(F32)
            for segment in chunk.segments:
                store_segment(self.packed, self.first[segment.result], segment, value)
            return
        count = 2 ** (self.bits - 1 - stage)
        step = min(count, 4)

        def some(i, carry):
            at = pl.ds(i * step, step)
            got[at] = got[at] + own[at]
            return carry

        lax.fori_loop(0, count // step, some, 0)

    def finish(self, name, stage, before):
        self.arrived(name, stage)
        self.add(name, stage, self.half(before, name, stage, False))
        if stage + 1 < self.bits:
            self.send_half(name, stage + 1, self.recv[name][stage])

    def drain(self):
        for copy in self.copies.values():
            copy.wait_send()


BOOKS = "books"


def quantizer_semantic(r):
    sem_code = r.chosen[0]
    rows, code_width = sem_code.shape
    columns = [slice(i * HALF, (i + 1) * HALF) for i in range(r.distill_v.shape[1] // HALF)]
    for i, cols in enumerate(columns):
        r.wide[i] = dot(sem_code, r.distill_v[:, cols])

    def row_sum(parts):
        return jnp.sum(sum(parts), axis=1, keepdims=True)

    for at in row_blocks(rows, 32):
        prediction = [r.wide[i, at, :] for i in range(len(columns))]
        target = [r.wavlm_v[at, cols].astype(F32) for cols in columns]
        pred_norm = lax.rsqrt(row_sum([p * p for p in prediction]) + EPS_COS)
        target_norm = lax.rsqrt(row_sum([w * w for w in target]) + EPS_COS)
        cosine = row_sum([p * w for p, w in zip(prediction, target)]) * (pred_norm * target_norm)
        from_target = -DISTILL * pred_norm * target_norm
        from_prediction = DISTILL * cosine * pred_norm * pred_norm
        for p, w, cols in zip(prediction, target, columns):
            r.act[at, cols] = (w * from_target + p * from_prediction).astype(BF16)
    grad_pred = r.act[:, : r.distill_v.shape[1]]
    put_distill(r.places.distill, dot(sem_code.T, grad_pred))
    r.gy[:, :code_width] = dot_t(grad_pred, r.distill_v[...])


def quantizer_latent(r):
    levels, rows, code_width = r.chosen.shape
    r.wide[0] = dot_t(r.gquant[...], r.pout_v[0])
    r.wide[1] = dot(r.latent[...], r.pin_v[0])
    r.wide[2] = dot_t(r.gquant[...], r.pout_v[1])
    r.wide[3] = dot(r.latent[...], r.pin_v[1])
    for at in row_blocks(rows, 32):
        grad_sem = r.wide[0, at, :] + r.gy[at, :code_width]
        commit = 2.0 * BETA * (r.wide[1, at, :] - r.chosen[0, at, :].astype(F32))
        r.g_rows[0, at, :] = (grad_sem - commit).astype(BF16)
        r.grad[at, :code_width] = (grad_sem + commit).astype(BF16)
        grad_ac, residual = r.wide[2, at, :], r.wide[3, at, :]
        for level in range(1, levels):
            residual = residual - r.chosen[level, at, :].astype(F32)
        carry = jnp.zeros_like(residual)
        for level in range(levels - 1, 0, -1):
            carry = carry + 2.0 * BETA * residual
            r.g_rows[level, at, :] = (grad_ac - carry).astype(BF16)
            residual = residual + r.chosen[level, at, :].astype(F32)
        r.grad[at, code_width:] = (grad_ac + carry).astype(BF16)


def quantizer_rest(r):
    code_width = r.ac.shape[1]
    latent_t = r.latent[...].T
    put_group(r.places.pout, 0, t_dot(r.chosen[0], r.gquant[...]))
    put_group(r.places.pout, 1, t_dot(r.ac[...], r.gquant[...]))
    put_group(r.places.pin, 0, dot(latent_t, r.grad[:, :code_width]))
    put_group(r.places.pin, 1, dot(latent_t, r.grad[:, code_width:]))
    r.gy[...] = dot_t(r.grad[...], jnp.concatenate([r.pin_v[0], r.pin_v[1]], axis=1))


def put_group(place, group, value):
    target, total = place.ref, value.shape[0]
    value = value.astype(BF16)
    if place.chunk is None:
        target[group * total : (group + 1) * total, :] = value
        return
    blocks, height, columns = target.shape[0] // 2, target.shape[1], value.shape[1]
    for i in range(blocks):
        for part in range(total // blocks // height):
            first = i * (total // blocks) + part * height
            cols = slice(place.col + part * columns, place.col + (part + 1) * columns)
            target[place.chunk.index(group * blocks + i), :, cols] = value[first : first + height]


def put_distill(place, value):
    target = place.ref
    if place.chunk is None:
        target[...] = value.astype(BF16)
        return
    blocks, height = target.shape[:2]
    rows = value.shape[0] // blocks
    columns = value.shape[1] * rows // height
    for i in range(blocks):
        part = value[i * rows : (i + 1) * rows]
        part = jnp.concatenate([part[:, at : at + columns] for at in range(0, value.shape[1], columns)], axis=0)
        target[place.chunk.index(i), :, place.col : place.col + columns] = part.astype(BF16)


def one_hot_rows(codes, first, count):
    row = iota((count, codes.shape[1]), 0)
    return jnp.where(codes - first == row, 1.0, 0.0).astype(BF16)


def pick_codes(r):
    levels, _, entries, code_width = r.books.shape
    entries = entries * r.books.shape[1]
    rows = r.cos.shape[0]
    slots = r.ring.shape[0]
    branch = lax.axis_index("branch")
    own = r.codes[:, pl.ds(pl.multiple_of(branch * rows, rows), rows)]
    r.code_rows[...] = jnp.broadcast_to(own[:, None, :], r.code_rows.shape)
    columns = jnp.concatenate([own.astype(F32), jnp.zeros((PAIR - levels, rows), F32)], axis=0).T
    lane = iota(columns.shape, 1)
    entry = iota((rows, entries), 1)
    r.code_cols[...] = columns
    r.ac_sum[...] = jnp.zeros(r.ac_sum.shape, F32)

    def book(level):
        slot = level % slots
        return pltpu.make_async_copy(r.books.at[level], r.ring.at[slot], r.sem_book.at[slot])

    def pick(level, carry):
        code = jnp.sum(jnp.where(lane == level, r.code_cols[...], 0.0), axis=1, keepdims=True)
        one_hot = jnp.where(entry == code.astype(jnp.int32), 1.0, 0.0).astype(BF16)
        book(level).wait()
        got = dot(one_hot, r.ring[level % slots].reshape(entries, code_width))
        r.chosen[level] = got.astype(BF16)
        r.ac_sum[...] += jnp.where(level > 0, got, 0.0)

        @pl.when(level + slots < levels)
        def _():
            book(level + slots).start()

        return carry

    def begin():
        for level in range(slots):
            book(level).start()

    def run():
        lax.fori_loop(0, levels, pick, 0, unroll=True)
        r.ac[...] = r.ac_sum[...].astype(BF16)

    return begin, run


def step_kernel(chunks, first_rows, bits, ins, outs, scratch):
    r = Refs({**ins, **outs, **scratch})
    t = r.t = Refs(r.t)
    r.att, r.g_rows, r.g_got, r.book_own = (r.ring.at[i] for i in range(4))
    r.ac_sum, r.code_cols = r.acc.at[:, : r.ac.shape[1]], r.gx.at[:, :PAIR]
    branch = lax.axis_index("branch")
    rows, width = r.tokens.shape
    levels, parts, entries, code_width = r.books.shape
    entries = entries * parts
    tiles = r.w_up_v.shape[1] // TILE
    pairs = width // PAIR
    if chunks:
        sums = Halving(chunks, bits, r.recv, r.packed, first_rows, r.send_sem, r.recv_sem)
        mine, level = sums.mine[bits - 2], lax.axis_index("dp") // 2
        wait_barrier = sums.barrier()
    moves = Moves(r.sem_move)
    begin_pick, run_pick = pick_codes(r)
    begin_pick()
    got_pout = [moves.start(r.pout_own.at[0], r.pout_v.at[branch])]
    frame_tables(r)
    if chunks:
        wait_barrier()
        sums.remote(r.pout_own.at[0], r.pout_v.at[branch], sums.partner[bits - 1], POUT)
    else:
        got_pout.append(moves.start(r.pout_other.at[0], r.pout_v.at[1 - branch]))
    got_rest = [
        moves.start(r.distill, r.distill_v),
        moves.start(r.wavlm.at[pl.ds(pl.multiple_of(branch * rows, rows), rows)], r.wavlm_v),
    ]
    got_attention = [moves.start(r.dec_qkv, r.w_qkv_v), moves.start(r.dec_out, r.w_out_v)]
    got_ffn = [moves.start(r.dec_up, r.w_up_v), moves.start(r.dec_down, r.w_down_v)]
    got_cotangent = [moves.start(r.cotangent, r.cotangent_v)]
    got_pin = [moves.start(r.pin_own.at[0], r.pin_v.at[branch])]
    if not chunks:
        got_pin.append(moves.start(r.pin_other.at[0], r.pin_v.at[1 - branch]))
    got_tokens = [moves.start(r.tokens, r.tokens_v)]
    got_attention_two = [moves.start(r.enc_qkv, r.w_qkv_e), moves.start(r.enc_out, r.w_out_e)]

    if chunks:
        def at(name, col=0):
            return Place(t[name], col, chunks[name])

        dec_down, enc_down = [at(DD0), at(DD1)], [at(ED0), at(ED1), at(ED2)]
        place = r.places = Refs(
            dec_up=[at(DU0), at(DU1)],
            dec_out=at(DA0),
            dec_qkv=[at(DA0, width), at(DA1), at(DA2)],
            enc_up=[at(EU0), at(EU1)],
            enc_out=at(EA0),
            enc_qkv=[at(EA1), at(EA2), at(EA3)],
            distill=at(DISTILL_GRAD),
            pout=at(MISC),
            pin=at(MISC, width),
        )
    else:
        dec_down, enc_down = [Place(t.dec_down)], [Place(t.enc_down)]
        place = r.places = Refs(
            dec_up=[Place(t.dec_up, i * tiles // 2 * TILE) for i in range(2)],
            dec_out=Place(t.dec_out),
            dec_qkv=[Place(t.dec_qkv, i * width) for i in range(3)],
            enc_up=[Place(t.enc_up, i * tiles // 2 * TILE) for i in range(2)],
            enc_out=Place(t.enc_out),
            enc_qkv=[Place(t.enc_qkv, i * width) for i in range(3)],
            distill=Place(t.distill),
            pout=Place(t.pout),
            pin=Place(t.pin),
        )

    def wait(moves, other=None):
        for move in moves:
            move.wait()
        if chunks and other is not None:
            sums.arrived(other)

    def layer_value(target, gain):
        for at in row_blocks(rows, 64):
            target[at, :] = (r.x2[at, :] + gain(3) * r.fo[at, :]).astype(BF16)

    def dec_gain(i):
        return r.vectors[1, i : i + 1, :]

    def enc_gain(i):
        return r.vectors[0, i : i + 1, :]

    def pick():
        run_pick()

    def semantic():
        wait(got_rest)
        quantizer_semantic(r)

    def quant():
        wait(got_pout, POUT)
        if chunks:
            sums.remote(r.pin_own.at[0], r.pin_v.at[branch], sums.partner[bits - 1], PIN)
        r.x[...] = dot(jnp.concatenate([r.chosen[0], r.ac[...]], axis=1), r.pout_v[...].reshape(-1, width))
        if chunks:
            for other in range(1, levels):
                target = sums.near_level(other)
                sums.remote(r.code_rows.at[target_level(target)], r.code_got.at[other], target, CODES, other)
            r.code_got[0] = r.code_rows[level]

    def target_level(target):
        return next(iter(target.values())) // 2

    def dec_project():
        wait(got_attention)
        attention_project(r, r.w_qkv_v, dec_gain)

    def dec_mix():
        attention_mix(r, r.w_out_v, dec_gain)

    def dec_ffn(half):
        def run():
            if half == 0:
                wait(got_ffn)
                wait(got_cotangent)
                ffn_backward_begin(r, dec_gain, r.cotangent_v)
            first, last = half * tiles // 2, (half + 1) * tiles // 2
            ffn_both(r, r.w_up_v, r.w_down_v, place.dec_up[half], dec_down, first, last)

        return run

    def dec_ffn_end():
        r.fo[...] = dot(r.act[...], r.w_down_v[...])
        layer_value(r.decoded, dec_gain)
        ffn_back_sum(r, r.w_up_v)
        ffn_backward_end(r, dec_gain, r.cotangent_v, r.dec_gains)
        got_ffn[:] = [moves.start(r.enc_up, r.w_up_v), moves.start(r.enc_down, r.w_down_v)]

    def dec_out():
        attention_backward_out(r, r.w_out_v, dec_gain, place.dec_out, r.dec_gains)

    def attention_pairs(first, last):
        return lambda: attention_backward_pairs(r, first, last)

    def dec_in(part):
        return lambda: attention_backward_in(r, place.dec_qkv[part], part)

    def dec_in_end():
        attention_backward_end(r, r.w_qkv_v, dec_gain, r.dec_gains)
        r.gquant[...] = r.gx[...].astype(BF16)

    def enc_project():
        wait(got_tokens)
        r.x[...] = r.tokens_v[...].astype(F32)
        wait(got_attention_two)
        attention_project(r, r.w_qkv_e, enc_gain)

    def enc_mix():
        attention_mix(r, r.w_out_e, enc_gain)

    def enc_ffn():
        wait(got_ffn)
        ffn_forward(r, r.w_up_v, r.w_down_v)
        layer_value(r.latent, enc_gain)

    def quantizer():
        wait(got_pin, PIN)
        quantizer_latent(r)
        if chunks:
            for other in reversed(range(1, levels)):
                target = sums.near_level(other)
                sums.arrived(CODES, other)
                sums.remote(r.g_rows.at[target_level(target)], r.g_got.at[other], target, BOOKS, 0, other)
            r.g_got[0] = r.g_rows[level]

    def quantizer_end():
        quantizer_rest(r)

    def book_half(core, put):
        quarter = entries // 4
        for side in range(2):
            r.book_sum[...] = jnp.zeros_like(r.book_sum)
            first = (core * 2 + side) * quarter

            def add(source, carry):
                one_hot = one_hot_rows(r.code_got[source, 0:1, :], first, quarter)
                r.book_sum[...] += dot(one_hot, r.g_got[source])
                return carry

            lax.fori_loop(0, levels, add, 0, unroll=4)
            put(side, r.book_sum[...])

    def finish_books(stage):
        blocks = entries // 4 // rows
        other_core, other_side = sums.partner[bits - 2], sums.partner[bits - 1]
        if stage == 0:
            for other in range(1, levels):
                sums.arrived(BOOKS, 0, other)

            def put(side, value):
                r.book_send[side] = value.astype(BF16)

            def keep(side, value):
                r.book_own[side * blocks : (side + 1) * blocks] = value.astype(BF16).reshape((blocks, rows, code_width))

            book_half(1 - mine, put)
            sums.remote(r.book_send, r.book_got, other_core, BOOKS, 1)
            book_half(mine, keep)
        elif stage == 1:
            sums.arrived(BOOKS, 1)
            for side in range(2):
                own = r.book_own[side * blocks : (side + 1) * blocks]
                r.book_got[side] = r.book_got[side] + own.reshape(r.book_got.shape[1:])
            sums.remote(r.book_got.at[1 - branch], r.book_last, other_side, BOOKS, 2)
        else:
            sums.arrived(BOOKS, 2)
            total = r.book_got[branch].astype(F32) + r.book_last[...].astype(F32)
            blocks = code_width // 128
            store_segment(r.packed, first_rows[BOOKS], Segment(BOOKS, 0, blocks, 0, blocks, 0, entries // 4), total)

    def all_books():
        parts = entries // TILE

        def one(step, carry):
            at = step // parts
            one_hot = one_hot_rows(r.code_rows[at, 0:1, :], step % parts * TILE, TILE)
            t.books[at, aligned(step % parts, TILE), :] = dot(one_hot, r.g_rows[at]).astype(BF16)
            return carry

        lax.fori_loop(0, levels * parts, one, 0)

    def enc_ffn_back(half):
        def run():
            first, last = half * tiles // 2, (half + 1) * tiles // 2
            if half == 0:
                ffn_backward_begin(r, enc_gain, r.gy)
            ffn_backward_tiles(r, r.w_down_v, place.enc_up[half], enc_down, first, last)

        return run

    def enc_ffn_back_end():
        ffn_back_sum(r, r.w_up_v)
        ffn_backward_end(r, enc_gain, r.gy, r.gains)

    def enc_out():
        attention_backward_out(r, r.w_out_e, enc_gain, place.enc_out, r.gains)

    def enc_in(part):
        def run():
            attention_backward_in(r, place.enc_qkv[part], part)
            if part == 2:
                attention_backward_end(r, r.w_qkv_e, enc_gain, r.gains)
                r.grad_tokens[...] = r.gx[...]
                if chunks:
                    spread_gains()

        return run

    def spread_gains():
        last, height = chunks[EA3], t.ea3.shape[1]
        for layer, ref in enumerate((r.gains, r.dec_gains)):
            for row in range(4):
                for block in range(width // 128):
                    owner = (layer * 4 + row) * (width // 128) + block
                    value = jnp.broadcast_to(ref[row : row + 1, block * 128 : (block + 1) * 128], (height, 128))
                    t.ea3[last.index(owner), :, width : width + 128] = value.astype(BF16)

    work = [
        (6.5, pick, ()),
        (0.7, quant, ()),
        (1.5, dec_project, ()),
        (2.5, dec_mix, ()),
        (2.6, dec_ffn(0), (DU0,)),
        (2.0, dec_ffn(1), (DD0, DD1, DU1)),
        (0.9, dec_ffn_end, ()),
        (1.8, semantic, (DISTILL_GRAD,)),
        (1.2, dec_out, ()),
        (1.6, attention_pairs(0, pairs // 2), ()),
        (1.6, attention_pairs(pairs // 2, pairs), ()),
        (0.6, dec_in(0), (DA0,)),
        (0.6, dec_in(1), (DA1,)),
        (0.5, dec_in(2), (DA2,)),
        (0.4, dec_in_end, ()),
        (1.5, enc_project, ()),
        (2.5, enc_mix, ()),
        (2.2, enc_ffn, ()),
        (1.2, quantizer, (BOOKS,)),
        (0.8, quantizer_end, (MISC,)),
        (2.0, enc_ffn_back(0), (EU0,)),
        (1.6, enc_ffn_back(1), (EU1, ED0, ED1, ED2)),
        (0.5, enc_ffn_back_end, ()),
        (1.2, enc_out, (EA0,)),
        (1.6, attention_pairs(0, pairs // 2), ()),
        (1.6, attention_pairs(pairs // 2, pairs), ()),
        (0.6, enc_in(0), (EA1,)),
        (0.6, enc_in(1), (EA2,)),
        (1.0, enc_in(2), (EA3,)),
    ]
    if not chunks:
        for _, run, _ in work:
            run()
            if run is quantizer:
                all_books()
        return
    actions = plan(chunks, work, bits, rows * code_width * 2)

    def finish(name, stage):
        if name == BOOKS:
            finish_books(stage)
        else:
            sums.finish(name, stage, r.recv[name][stage - 1] if stage else t[name])

    for (_, run, made), acts in zip(work, actions):
        run()
        for name in made:
            if name != BOOKS:
                sums.send_half(name, 0, t[name])
        for name, stage in acts:
            finish(name, stage)
    for name, stage in actions[-1]:
        finish(name, stage)
    sums.drain()


POUT, PIN, CODES = 1, 2, 3
DISTILL_GRAD = "di"
DD0, DD1, DU0, DU1, DA0, DA1, DA2, MISC = "dd0", "dd1", "du0", "du1", "da0", "da1", "da2", "misc"
EU0, EU1, ED0, ED1, ED2 = "eu0", "eu1", "ed0", "ed1", "ed2"
EA0, EA1, EA2, EA3 = "ea0", "ea1", "ea2", "ea3"


def step(given, devices, with_sums):
    rows, width = given.tokens.shape
    ff = given.enc_up.shape[1]
    levels, entries, code_width = given.books.shape
    given.books = given.books.reshape(levels, -1, rows, code_width)
    bits = devices.bit_length() - 1
    vmem, hbm = pl.BlockSpec(memory_space=pltpu.VMEM), pl.BlockSpec(memory_space=pl.ANY)
    scratch = layer_scratch(rows, width, ff)
    scratch.update(
        w_qkv_e=pltpu.VMEM((width, 3 * width), BF16),
        w_out_e=pltpu.VMEM((width, width), BF16),
        cos=pltpu.VMEM((rows, PAIR), F32),
        sin=pltpu.VMEM((rows, PAIR), F32),
        bias=pltpu.VMEM((rows, rows), F32),
        ring=pltpu.VMEM((4,) + given.books.shape[1:], BF16),
        code_rows=pltpu.VMEM((levels, 8, rows), jnp.int32),
        chosen=pltpu.VMEM((levels, rows, code_width), BF16),
        ac=pltpu.VMEM((rows, code_width), BF16),
        gquant=pltpu.VMEM((rows, width), BF16),
        gy=pltpu.VMEM((rows, width), F32),
        latent=pltpu.VMEM((rows, width), BF16),
        pin_v=pltpu.VMEM((2, width, code_width), BF16),
        pout_v=pltpu.VMEM((2, code_width, width), BF16),
        distill_v=pltpu.VMEM(given.distill.shape, BF16),
        wavlm_v=pltpu.VMEM((rows, given.wavlm.shape[1]), BF16),
        tokens_v=pltpu.VMEM((rows, width), BF16),
        cotangent_v=pltpu.VMEM((rows, width), BF16),
        sem_move=pltpu.SemaphoreType.DMA((14,)),
        sem_book=pltpu.SemaphoreType.DMA((4,)),
    )
    outs = Refs(decoded=shaped((rows, width), BF16), grad_tokens=shaped((rows, width), F32))
    chunks, first_rows = {}, {}
    params = dict(vmem_limit_bytes=60 * 2**20)
    if with_sums:
        params.update(collective_id=0, has_side_effects=True)
        c, x, y = bits - 2, bits - 1, bits - 3
        b, a = range(y)
        share = width // devices
        low, high = ff // devices, share
        wide, half, blocks = ff // 128, ff // 256, width // 128
        third, quarter = 3 * blocks, blocks // 4
        chunks = dict(
            di=Chunk(
                high,
                width,
                [c, y, x, a, b],
                [
                    Segment(8, 0, 2 * blocks, 0, blocks, 0, high // 2),
                    Segment(8, blocks, 2 * blocks, 0, blocks, high // 2, high // 2),
                ],
            ),
            du0=Chunk(high, ff // 2, [c, y, a, x, b], [Segment(2, 0, wide, 0, half, 0, high)]),
            dd0=Chunk(low, width // 2, [c, a, y, b, x], [Segment(3, 0, blocks, 0, 2 * quarter, 0, low)]),
            dd1=Chunk(low, width // 2, [c, y, x, a, b], [Segment(3, 2 * quarter, blocks, 0, 2 * quarter, 0, low)]),
            du1=Chunk(high, ff // 2, [c, x, y, a, b], [Segment(2, half, wide, 0, half, 0, high)]),
            da0=Chunk(
                high,
                2 * width,
                [c, x, y, a, b],
                [Segment(1, 0, blocks, 0, blocks, 0, high), Segment(0, 0, third, width, blocks, 0, high)],
            ),
            da1=Chunk(high, width, [c, a, x, y, b], [Segment(0, blocks, third, 0, blocks, 0, high)]),
            da2=Chunk(high, width, [c, y, x, a, b], [Segment(0, 2 * blocks, third, 0, blocks, 0, high)]),
            misc=Chunk(
                high,
                2 * width,
                [c, x, y, a, b],
                [
                    Segment(9, 0, blocks, 0, blocks, 0, high),
                    Segment(10, 0, blocks // 2, width, blocks // 2, 0, high),
                    Segment(10, high * blocks // 2, blocks // 2, width + code_width, blocks // 2, 0, high),
                ],
            ),
            eu0=Chunk(high, ff // 2, [c, x, a, y, b], [Segment(6, 0, wide, 0, half, 0, high)]),
            eu1=Chunk(high, ff // 2, [c, x, y, a, b], [Segment(6, half, wide, 0, half, 0, high)]),
            ed0=Chunk(low, width // 2, [c, x, y, a, b], [Segment(7, 0, blocks, 0, 2 * quarter, 0, low)]),
            ed1=Chunk(low, width // 4, [c, y, x, a, b], [Segment(7, 2 * quarter, blocks, 0, quarter, 0, low)]),
            ed2=Chunk(low, width // 4, [c, y, a, b, x], [Segment(7, 3 * quarter, blocks, 0, quarter, 0, low)]),
            ea0=Chunk(high, width, [c, x, y, a, b], [Segment(5, 0, blocks, 0, blocks, 0, high)]),
            ea1=Chunk(high, width, [c, y, x, a, b], [Segment(4, 0, third, 0, blocks, 0, high)]),
            ea2=Chunk(high, width, [c, x, a, y, b], [Segment(4, blocks, third, 0, blocks, 0, high)]),
            ea3=Chunk(
                high,
                width + 128,
                [c, x, y, a, b],
                [Segment(4, 2 * blocks, third, 0, blocks, 0, high), Segment(11, 0, 1, width, 1, 0, 8)],
            ),
        )
        rows_of = [high * 3 * blocks, high * blocks, high * wide, low * blocks] * 2
        rows_of += [high * blocks, high * blocks, high * blocks, 8, entries // 4 * code_width // 128]
        first_rows = {i: sum(rows_of[:i]) for i in range(len(rows_of))}
        first_rows[BOOKS] = first_rows[len(rows_of) - 1]
        copies = len(chunks) * bits + 2 * levels + 2
        scratch.update(
            t={name: pltpu.VMEM(c.shape(bits), BF16) for name, c in chunks.items()},
            recv={
                name: [pltpu.VMEM(c.shape(bits - 1 - stage), BF16) for stage in range(bits)]
                for name, c in chunks.items()
            },
            gains=pltpu.VMEM((4, width), F32),
            dec_gains=pltpu.VMEM((4, width), F32),
            code_got=pltpu.VMEM((levels, 8, rows), jnp.int32),
                book_sum=pltpu.VMEM((entries // 4, code_width), F32),
            book_send=pltpu.VMEM((2, entries // 4, code_width), BF16),
            book_got=pltpu.VMEM((2, entries // 4, code_width), BF16),
            book_last=pltpu.VMEM((entries // 4, code_width), BF16),
            send_sem=pltpu.SemaphoreType.DMA((copies,)),
            recv_sem=pltpu.SemaphoreType.DMA((copies,)),
        )
        outs.packed = shaped((sum(rows_of), 128), F32)
    else:
        outs.update(gains=shaped((4, width), F32), dec_gains=shaped((4, width), F32))
        outs.t = dict(
            enc_qkv=shaped(given.enc_qkv.shape, BF16),
            enc_out=shaped(given.enc_out.shape, BF16),
            enc_up=shaped(given.enc_up.shape, BF16),
            enc_down=shaped(given.enc_down.shape, BF16),
            dec_qkv=shaped(given.enc_qkv.shape, BF16),
            dec_out=shaped(given.enc_out.shape, BF16),
            dec_up=shaped(given.enc_up.shape, BF16),
            dec_down=shaped(given.enc_down.shape, BF16),
            pin=shaped((2 * width, code_width), BF16),
            pout=shaped((2 * code_width, width), BF16),
            books=shaped((levels, entries, code_width), BF16),
            distill=shaped(given.distill.shape, BF16),
        )
    in_specs = dict.fromkeys(given, hbm)
    in_specs.update(
        lengths=pl.BlockSpec(memory_space=pltpu.SMEM), codes=vmem, vectors=vmem
    )
    got = pl.pallas_call(
        functools.partial(step_kernel, chunks, first_rows, bits),
        out_shape={k: pltpu.VMEM(v.shape, v.dtype) for k, v in outs.items()} if with_sums else dict(outs),
        in_specs=[in_specs],
        out_specs=jax.tree.map(lambda _: vmem, dict(outs)),
        scratch_shapes=[dict(scratch)],
        compiler_params=pltpu.CompilerParams(**params),
        name="step",
    )(dict(given))
    got = Refs(got)
    if not with_sums:
        return got
    last = [shaped((rows, 128), F32) for rows in rows_of]
    last[11] = shaped((1, 128), F32)

    def hand_on(packed, decoded, grad, *refs):
        outs, moves = refs[:-1], Moves(refs[-1])
        parts = [packed.at[pl.ds(first_rows[i], ref.shape[0])] for i, ref in enumerate(outs[:-2])]
        leaving = [moves.start(part, ref) for part, ref in zip(parts + [decoded, grad], outs)]
        for move in leaving:
            move.wait()

    return pl.pallas_call(
        hand_on,
        out_shape=last + [outs.decoded, outs.grad_tokens],
        in_specs=[vmem] * 3,
        out_specs=[hbm] * (len(last) + 2),
        scratch_shapes=[pltpu.SemaphoreType.DMA((len(last) + 2,))],
        compiler_params=pltpu.CompilerParams(vmem_limit_bytes=16 * 2**20),
        name="results",
    )(got.packed, got.decoded, got.grad_tokens)


def body(
    tokens,
    wavlm,
    cotangent,
    lengths,
    codes,
    enc_qkv,
    enc_out,
    enc_up,
    enc_down,
    dec_qkv,
    dec_out,
    dec_up,
    dec_down,
    vectors,
    proj_in,
    proj_out,
    codebooks,
    distill_proj,
):
    width = tokens.shape[1]
    devices = lax.axis_size("dp") * lax.axis_size("branch")
    with_sums = devices == 4 * codebooks.shape[0] and width // devices % 16 == 0
    given = Refs(
        tokens=tokens,
        wavlm=wavlm,
        cotangent=cotangent,
        lengths=lengths,
        codes=codes.T,
        enc_qkv=enc_qkv,
        enc_out=enc_out,
        enc_up=enc_up,
        enc_down=enc_down,
        dec_qkv=dec_qkv,
        dec_out=dec_out,
        dec_up=dec_up,
        dec_down=dec_down,
        vectors=vectors,
        pin_own=proj_in,
        pout_own=proj_out,
        books=codebooks,
        distill=distill_proj,
    )
    if with_sums:
        *sums, decoded, grad_tokens = step(given, devices, True)
        sums = [part.reshape(-1) for part in sums]
        order = (4, 5, 6, 7, 0, 1, 2, 3, 11, 10, 9, 12, 8)
        return (decoded, grad_tokens, *[sums[i] for i in order])
    swap = [(0, 1), (1, 0)]
    given.pin_other = lax.ppermute(proj_in, "branch", swap)
    given.pout_other = lax.ppermute(proj_out, "branch", swap)
    s = step(given, devices, False)
    t = Refs(s.t)
    gains = jnp.concatenate([s.gains, s.dec_gains])
    local = [t.enc_qkv, t.enc_out, t.enc_up, t.enc_down, t.dec_qkv, t.dec_out, t.dec_up, t.dec_down]
    local += [gains, t.pin, t.pout, t.books, t.distill]
    sums = [
        lax.psum_scatter(part.astype(F32).reshape(-1), ("dp", "branch"), scatter_dimension=0, tiled=True)
        for part in local
    ]
    return (s.decoded, s.grad_tokens, *sums)


def solution(mesh):
    rows, whole = P(("dp", "branch"), None), P()
    placed = (rows, P("dp", None), rows, rows, P("dp", None)) + (whole,) * 9
    placed += (P("branch", None, None),) * 2 + (whole,) * 2
    return jax.shard_map(
        body,
        mesh=mesh,
        in_specs=placed,
        out_specs=(rows, rows) + (P(("dp", "branch")),) * 13,
        check_vma=False,
    )
```

```python
import functools
import math

import jax
import jax.numpy as jnp
from jax import lax
from jax.experimental import pallas as pl
from jax.experimental.pallas import tpu as pltpu
from jax.sharding import PartitionSpec as P

HEADS = 8
WINDOW = 250
EPS_NORM = 1e-05
EPS_COS = 1e-06
BETA = 0.25
DISTILL = 10.0
ROPE_BASE = 10000.0

MESH = pl.DeviceIdType.MESH
F32 = jnp.float32
BF16 = jnp.bfloat16
TILE = 512
PAIR = 128
HALF = 256


def dot(left, right):
    return lax.dot_general(left, right, (((1,), (0,)), ((), ())), preferred_element_type=F32)


def dot_t(left, right):
    return lax.dot_general(left, right, (((1,), (1,)), ((), ())), preferred_element_type=F32)


def t_dot(left, right):
    return lax.dot_general(left, right, (((0,), (0,)), ((), ())), preferred_element_type=F32)


def iota(shape, dim):
    return lax.broadcasted_iota(jnp.int32, shape, dim)


def aligned(index, size):
    return pl.ds(pl.multiple_of(index * size, size), size)


class Refs(dict):
    __getattr__ = dict.__getitem__
    __setattr__ = dict.__setitem__


class Moves:
    def __init__(self, semaphores):
        self.semaphores, self.count = semaphores, 0

    def start(self, source, target):
        move = pltpu.make_async_copy(source, target, self.semaphores.at[self.count])
        self.count += 1
        move.start()
        return move


def layer_scratch(rows, width, ff):
    return Refs(
        x=pltpu.VMEM((rows, width), F32),
        s1=pltpu.VMEM((rows, 1), F32),
        h=pltpu.VMEM((rows, width), BF16),
        h1t=pltpu.VMEM((width, rows), BF16),
        h2t=pltpu.VMEM((width, rows), BF16),
        rinv=pltpu.VMEM((rows, width), F32),
        qkv=pltpu.VMEM((rows, 3 * width), BF16),
        mix=pltpu.VMEM((rows, width), BF16),
        ao=pltpu.VMEM((rows, width), F32),
        x2=pltpu.VMEM((rows, width), F32),
        s2=pltpu.VMEM((rows, 1), F32),
        act=pltpu.VMEM((rows, ff), BF16),
        dg=pltpu.VMEM((rows, ff), BF16),
        fo=pltpu.VMEM((rows, width), F32),
        grad=pltpu.VMEM((rows, width), BF16),
        gx=pltpu.VMEM((rows, width), F32),
        acc=pltpu.VMEM((rows, width), F32),
        wide=pltpu.VMEM((4, rows, HALF), F32),
        change=pltpu.VMEM((2, rows, rows), BF16),
        w_qkv_v=pltpu.VMEM((width, 3 * width), BF16),
        w_out_v=pltpu.VMEM((width, width), BF16),
        w_up_v=pltpu.VMEM((width, ff), BF16),
        w_down_v=pltpu.VMEM((ff, width), BF16),
    )


def shaped(shape, kind):
    return jax.ShapeDtypeStruct(shape, kind)


def frame_tables(r):
    rows = r.cos.shape[0]
    place = iota((rows, PAIR), 0)
    query, key = iota((rows, rows), 0), iota((rows, rows), 1)
    begin, begin_query = jnp.zeros_like(place), jnp.zeros_like(query)
    edge = 0
    for clip in range(r.lengths.shape[1] - 1):
        edge = edge + r.lengths[0, clip]
        begin = jnp.where(place >= edge, edge, begin)
        begin_query = jnp.where(query >= edge, edge, begin_query)
    allowed = (key >= begin_query) & (key <= query) & (query - key < WINDOW)
    r.bias[...] = jnp.where(allowed, 0.0, -1e30)
    lane = iota((rows, PAIR), 1)
    rate = jnp.exp((lane % 32).astype(F32) * (-math.log(ROPE_BASE) / 32))
    angle = (place - begin).astype(F32) * rate
    r.cos[...] = jnp.cos(angle)
    sine = jnp.sin(angle)
    r.sin[...] = jnp.where(lane % 64 < 32, -sine, sine)


def rotated(value, cosine, sine):
    lane = iota(value.shape, 1)
    swapped = jnp.where(lane % 64 < 32, pltpu.roll(value, PAIR - 32, 1), pltpu.roll(value, 32, 1))
    return value * cosine + swapped * sine


def head_masks(rows):
    low = iota((rows, PAIR), 1) < 64
    return (jnp.where(low, 1.0, 0.0).astype(BF16), jnp.where(low, 0.0, 1.0).astype(BF16))


def row_blocks(rows, step):
    return [slice(i, i + step) for i in range(0, rows, step)]


def attention_project(r, w_qkv, gain):
    rows, width = r.x.shape
    scale = gain(0)
    for at in row_blocks(rows, 64):
        x = r.x[at, :]
        s1 = lax.rsqrt(jnp.mean(x * x, axis=1, keepdims=True) + EPS_NORM)
        r.s1[at, :] = s1
        r.h[at, :] = (x * s1 * scale).astype(BF16)
    for half in range(3 * width // HALF):
        slot, part = half % 4, half // (width // HALF)
        cols = slice(half * HALF, (half + 1) * HALF)
        r.wide[slot] = dot(r.h[...], w_qkv[:, cols])
        for at in row_blocks(rows, 64):
            for p in range(HALF // PAIR):
                value = r.wide[slot, at, p * PAIR : (p + 1) * PAIR]
                if part < 2:
                    value = rotated(value, r.cos[at, :], r.sin[at, :])
                low = value.astype(BF16)
                if part == 0:
                    low = (low.astype(F32) * 0.125).astype(BF16)
                r.qkv[at, half * HALF + p * PAIR : half * HALF + (p + 1) * PAIR] = low
    r.h1t[...] = r.h[...].T


def attention_mix(r, w_out, gain):
    rows, width = r.x.shape
    masks = head_masks(rows)
    low = iota((rows, PAIR), 1) < 64
    pairs = width // PAIR
    for p in range(pairs):
        query = r.qkv[:, p * PAIR : (p + 1) * PAIR]
        key = r.qkv[:, (p + pairs) * PAIR : (p + pairs + 1) * PAIR]
        value = r.qkv[:, (p + 2 * pairs) * PAIR : (p + 2 * pairs + 1) * PAIR]
        outs = []
        for h in range(2):
            head = 2 * p + h
            slot = head % 4
            r.wide[slot] = dot_t(query * masks[h], key)
            for at in row_blocks(rows, 64):
                seen = PAIR if at.stop <= PAIR else rows
                scores = r.wide[slot, at, :seen] + r.bias[at, :seen]
                weights = jnp.exp(scores - jnp.max(scores, axis=1, keepdims=True))
                r.att[head, at, :seen] = weights.astype(BF16)
                if seen < rows:
                    r.att[head, at, seen:] = jnp.zeros((64, rows - seen), BF16)
            outs.append(dot(r.att[head], value * masks[h] + masks[1 - h]))
        inverse = 1.0 / pltpu.roll(jnp.where(low, outs[1], outs[0]), 64, 1)
        r.rinv[:, p * PAIR : (p + 1) * PAIR] = inverse
        r.mix[:, p * PAIR : (p + 1) * PAIR] = (jnp.where(low, outs[0], outs[1]) * inverse).astype(BF16)
    r.ao[...] = dot(r.mix[...], w_out[...])
    scale_one, scale_two = gain(1), gain(2)
    for at in row_blocks(rows, 64):
        x2 = r.x[at, :] + scale_one * r.ao[at, :]
        r.x2[at, :] = x2
        s2 = lax.rsqrt(jnp.mean(x2 * x2, axis=1, keepdims=True) + EPS_NORM)
        r.s2[at, :] = s2
        r.h[at, :] = (x2 * s2 * scale_two).astype(BF16)
    r.h2t[...] = r.h[...].T


def gelu_parts(pre):
    slope = math.sqrt(2.0 / math.pi)
    square = pre * pre
    bent = jnp.tanh(slope * pre * (1.0 + 0.044715 * square))
    half = 0.5 * (1.0 + bent)
    turn = 0.5 * pre * (1.0 - bent * bent) * slope * (1.0 + 3.0 * 0.044715 * square)
    return (pre * half).astype(BF16), half + turn


def ffn_forward(r, w_up, w_down):
    rows, ff = r.act.shape
    for half in range(ff // HALF):
        slot, cols = half % 4, slice(half * HALF, (half + 1) * HALF)
        r.wide[slot] = dot(r.h[...], w_up[:, cols])
        for at in row_blocks(rows, 32):
            act, slope = gelu_parts(r.wide[slot, at, :])
            r.act[at, cols] = act
            r.dg[at, cols] = slope.astype(BF16)
    r.fo[...] = dot(r.act[...], w_down[...])


def ffn_both(r, w_up, w_down, grad_up, grad_down, first, last):
    rows = r.act.shape[0]
    for t in range(first, last):
        cols = slice(t * TILE, (t + 1) * TILE)
        for side in range(TILE // HALF):
            part = slice(t * TILE + side * HALF, t * TILE + (side + 1) * HALF)
            r.wide[side] = dot(r.h[...], w_up[:, part])
            r.wide[2 + side] = dot_t(r.grad[...], w_down[part, :])
            for at in row_blocks(rows, 32):
                act, slope = gelu_parts(r.wide[side, at, :])
                r.act[at, part] = act
                r.dg[at, part] = (r.wide[2 + side, at, :] * slope).astype(BF16)
        grad_up.shift((t - first) * TILE).put(dot(r.h2t[...], r.dg[:, cols]))
        put_rows(grad_down, t_dot(r.act[:, cols], r.grad[...]), t)


def ffn_back_sum(r, w_up):
    r.acc[...] = dot_t(r.dg[...], w_up[...])


def norm_back(stream, inverse, grad):
    mean = jnp.mean(grad * stream, axis=1, keepdims=True)
    return inverse * grad - stream * (inverse * inverse * inverse * mean)


def column_sum(value):
    return jnp.sum(value, axis=0, keepdims=True)


class Place:
    def __init__(self, ref, col=0, chunk=None):
        self.ref, self.col, self.chunk = ref, col, chunk

    def shift(self, by):
        return Place(self.ref, self.col + by, self.chunk)

    def put(self, value):
        value = value.astype(BF16)
        cols = slice(self.col, self.col + value.shape[1])
        if self.chunk is None:
            self.ref[:, cols] = value
            return
        blocks, rows = self.ref.shape[:2]
        for owner in range(blocks):
            self.ref[self.chunk.index(owner), :, cols] = value[owner * rows : (owner + 1) * rows]


def put_rows(places, value, tile):
    value = value.astype(BF16)
    begin = 0
    for place in places:
        part = value[:, begin : begin + place.ref.shape[-1]]
        begin += place.ref.shape[-1]
        if place.chunk is None:
            place.ref[tile * TILE : tile * TILE + TILE, :] = part
            continue
        rows = place.ref.shape[1]
        for i in range(TILE // rows):
            place.ref[place.chunk.index(tile * (TILE // rows) + i)] = part[i * rows : (i + 1) * rows]


def ffn_backward_begin(r, gain, gy_ref):
    scale = gain(3)
    for at in row_blocks(r.grad.shape[0], 64):
        r.grad[at, :] = (scale * gy_ref[at, :].astype(F32)).astype(BF16)


def ffn_backward_tiles(r, w_down, grad_up, grad_down, first, last):
    rows = r.act.shape[0]
    for t in range(first, last):
        cols = slice(t * TILE, (t + 1) * TILE)
        for side in range(TILE // HALF):
            part = slice(t * TILE + side * HALF, t * TILE + (side + 1) * HALF)
            slot = (2 * t + side) % 4
            r.wide[slot] = dot_t(r.grad[...], w_down[part, :])
            for at in row_blocks(rows, 64):
                r.dg[at, part] = (r.wide[slot, at, :] * r.dg[at, part].astype(F32)).astype(BF16)
        put_rows(grad_down, t_dot(r.act[:, cols], r.grad[...]), t)
        grad_up.shift((t - first) * TILE).put(dot(r.h2t[...], r.dg[:, cols]))


def ffn_backward_end(r, gain, gy_ref, gain_out):
    scale = gain(2)
    to_gain = to_scale = 0.0
    for at in row_blocks(r.x2.shape[0], 32):
        gy = gy_ref[at, :].astype(F32)
        to_scale = to_scale + column_sum(gy * r.fo[at, :])
        back, x2, s2 = r.acc[at, :], r.x2[at, :], r.s2[at, :]
        to_gain = to_gain + column_sum(back * x2 * s2)
        r.gx[at, :] = gy + norm_back(x2, s2, back * scale)
    gain_out[3:4, :] = to_scale
    gain_out[2:3, :] = to_gain


def attention_backward_out(r, w_out, gain, grad_out, gain_out):
    scale = gain(1)
    to_scale = 0.0
    for at in row_blocks(r.gx.shape[0], 64):
        gx = r.gx[at, :]
        to_scale = to_scale + column_sum(gx * r.ao[at, :])
        r.grad[at, :] = (scale * gx).astype(BF16)
    gain_out[1:2, :] = to_scale
    grad_out.put(t_dot(r.mix[...], r.grad[...]))
    r.grad[...] = dot_t(r.grad[...], w_out[...]).astype(BF16)


def attention_backward_pairs(r, first, last):
    rows, width = r.x.shape
    masks = head_masks(rows)
    masks_t = [jnp.where((iota((PAIR, rows), 0) < 64) == (h == 0), 1.0, 0.0).astype(BF16) for h in range(2)]
    pairs = width // PAIR
    for p in range(first, last):
        lanes = [slice((p + i * pairs) * PAIR, (p + i * pairs + 1) * PAIR) for i in range(3)]
        query, key, value = (r.qkv[:, at] for at in lanes)
        grad_mixed = (r.grad[:, lanes[0]].astype(F32) * r.rinv[:, lanes[0]]).astype(BF16)
        product = (grad_mixed.astype(F32) * r.mix[:, lanes[0]].astype(F32)).astype(BF16)
        beside = jnp.concatenate([value, jnp.full(value.shape, -1.0, BF16)], axis=1)
        query_t, grad_t = query.T, grad_mixed.T
        to_query = to_key = to_value = 0.0
        for h in range(2):
            head = 2 * p + h
            slot = head % 4
            both = jnp.concatenate([grad_mixed * masks[h], product * masks[h]], axis=1)
            r.wide[slot] = dot_t(both, beside)
            for at in row_blocks(rows, 64):
                r.change[h, at, :] = (r.att[head, at, :].astype(F32) * r.wide[slot, at, :]).astype(BF16)
            to_query = to_query + dot(r.change[h], key * masks[h])
            to_key = to_key + dot(query_t * masks_t[h], r.change[h])
            to_value = to_value + dot(grad_t * masks_t[h], r.att[head])
        cosine, sine = r.cos[...], -r.sin[...]
        r.qkv[:, lanes[0]] = rotated(to_query * 0.125, cosine, sine).astype(BF16)
        r.qkv[:, lanes[1]] = rotated(to_key.T, cosine, sine).astype(BF16)
        r.qkv[:, lanes[2]] = to_value.T.astype(BF16)


def attention_backward_in(r, grad_qkv, part):
    width = r.x.shape[1]
    grad_qkv.put(dot(r.h1t[...], r.qkv[:, part * width : (part + 1) * width]))


def attention_backward_end(r, w_qkv, gain, gain_out):
    r.acc[...] = dot_t(r.qkv[...], w_qkv[...])
    scale = gain(0)
    to_gain = 0.0
    for at in row_blocks(r.x.shape[0], 32):
        back, x, s1 = r.acc[at, :], r.x[at, :], r.s1[at, :]
        to_gain = to_gain + column_sum(back * x * s1)
        r.gx[at, :] = r.gx[at, :] + norm_back(x, s1, back * scale)
    gain_out[0:1, :] = to_gain


class Segment:
    def __init__(self, result, base, stride, col, blocks, row, rows):
        self.result, self.base, self.stride, self.col, self.blocks = result, base, stride, col, blocks
        self.row, self.rows = row, rows


class Chunk:
    def __init__(self, rows, columns, order, segments):
        self.rows, self.columns, self.order, self.segments = rows, columns, order, segments

    def index(self, owner):
        bits = len(self.order)
        x, core, y = bits - 1, bits - 2, bits - 3
        swap = {x: y, y: x} if owner >> (bits - 1 - core) & 1 else {}
        order = [swap.get(dim, dim) for dim in self.order]
        return sum((owner >> (bits - 1 - dim) & 1) << (bits - 1 - stage) for stage, dim in enumerate(order))

    def shape(self, leading):
        return (2**leading, self.rows, self.columns)

    def bytes(self, bits):
        return 2**bits * self.rows * self.columns * 2


def plan(chunks, work, bits, book_bytes):
    core, x, y = bits - 2, bits - 1, bits - 3
    ends, middle = -1, -2
    free, pending, done = {}, [], []
    now = 0.0

    def carry(link, size, rate=42e3):
        free[link] = max(now, free.get(link, 0.0)) + size / rate
        return free[link]

    def begin(name, stage):
        if name == BOOKS:
            size = 1.2 * 2 ** (bits - 3) * book_bytes
            if stage == 0:
                there = max(carry(x, size, 84e3), carry(ends, 1.5 * size), carry(middle, 2 * size))
            else:
                there = carry(core, 4 * book_bytes, 400e3) if stage == 1 else carry(x, 2 * book_bytes, 84e3)
        else:
            dim = chunks[name].order[stage]
            size = chunks[name].bytes(bits) / 2 ** (stage + 1)
            if dim == core:
                there = carry(core, size, 400e3)
            elif dim == x or dim == y:
                there = carry(x, size, 84e3)
            else:
                there = carry(ends, size)
                if dim < y - 1:
                    there = max(there, carry(middle, 2 * size))
        pending.append((there + 1.5, name, stage))

    def finish(limit):
        nonlocal now
        acts = []
        while pending:
            pending.sort(key=lambda p: p[0])
            if pending[0][0] + (0.5 if limit < math.inf else 0.0) > limit:
                break
            at, name, stage = pending.pop(0)
            if name == BOOKS:
                cost = (6.0, 0.6, 0.3)[stage]
            else:
                cost = 0.25 + 0.3e-6 * chunks[name].bytes(bits) / 2 ** (stage + 1)
            now = max(now, at) + cost
            limit = max(limit, now)
            acts.append((name, stage))
            if stage + 1 < (3 if name == BOOKS else bits):
                begin(name, stage + 1)
        return acts

    for took, _, names in work:
        now += 0.95 * took
        for name in names:
            begin(name, 0)
        done.append(finish(now))
    done.append(finish(math.inf))
    return done


def store_segment(packed, first, segment, value):
    for i in range(segment.blocks):
        where = pl.ds(first + segment.base + i, segment.rows, stride=segment.stride)
        packed[where, :] = value[
            segment.row : segment.row + segment.rows, segment.col + i * 128 : segment.col + (i + 1) * 128
        ]


class Halving:
    def __init__(self, chunks, bits, recv, packed, first, send_sem, recv_sem):
        self.chunks = chunks
        self.bits, self.recv, self.packed, self.first = bits, recv, packed, first
        self.send_sem, self.recv_sem = send_sem, recv_sem
        self.copies = {}
        dp, branch = lax.axis_index("dp"), lax.axis_index("branch")
        self.mine, self.partner = [], []
        for dim in range(bits - 1):
            weight = 2 ** (bits - 2 - dim)
            bit = dp // weight % 2
            self.mine.append(bit)
            self.partner.append({"dp": dp + weight * (1 - 2 * bit), "branch": branch})
        self.mine.append(branch)
        self.partner.append({"dp": dp, "branch": 1 - branch})
        x, core, y = bits - 1, self.mine[bits - 2], bits - 3
        step_y, step_x = 2 * (1 - 2 * self.mine[y]), 1 - 2 * branch
        self.side, self.target = list(self.mine), list(self.partner)
        self.side[x] = self.mine[x] + core * (self.mine[y] - self.mine[x])
        self.side[y] = self.mine[y] + core * (self.mine[x] - self.mine[y])
        self.target[x] = {"dp": dp + core * step_y, "branch": branch + (1 - core) * step_x}
        self.target[y] = {"dp": dp + (1 - core) * step_y, "branch": branch + core * step_x}

    def near_level(self, other):
        dp = lax.axis_index("dp")
        for i in range(self.bits - 2):
            if other >> i & 1:
                dp = dp + 2 ** (i + 1) * (1 - 2 * self.mine[self.bits - 3 - i])
        return {"dp": dp, "branch": lax.axis_index("branch")}

    def barrier(self):
        semaphore = pltpu.get_barrier_semaphore()
        levels = 2 ** (self.bits - 2)
        targets = self.partner[self.bits - 2 :] + [self.near_level(other) for other in range(1, levels)]
        for target in targets:
            pl.semaphore_signal(semaphore, inc=1, device_id=target, device_id_type=MESH)
        return lambda: pl.semaphore_wait(semaphore, len(targets))

    def half(self, ref, name, stage, other):
        mine = self.side[self.chunks[name].order[stage]]
        count = 2 ** (self.bits - 1 - stage)
        return ref.at[pl.ds((1 - mine if other else mine) * count, count)]

    def remote(self, source, target, device, *key):
        slot = len(self.copies)
        self.copies[key] = pltpu.make_async_remote_copy(
            src_ref=source,
            dst_ref=target,
            send_sem=self.send_sem.at[slot],
            recv_sem=self.recv_sem.at[slot],
            device_id=device,
            device_id_type=MESH,
        )
        self.copies[key].start()

    def send(self, name, stage, source):
        dim = self.chunks[name].order[stage]
        self.remote(source, self.recv[name][stage], self.target[dim], name, stage)

    def send_half(self, name, stage, ref):
        self.send(name, stage, self.half(ref, name, stage, True))

    def arrived(self, *key):
        self.copies[key].wait_recv()

    def add(self, name, stage, own):
        chunk = self.chunks[name]
        got = self.recv[name][stage]
        if stage == self.bits - 1:
            value = own[0].astype(F32) + got[0].astype(F32)
            for segment in chunk.segments:
                store_segment(self.packed, self.first[segment.result], segment, value)
            return
        count = 2 ** (self.bits - 1 - stage)
        step = min(count, 4)

        def some(i, carry):
            at = pl.ds(i * step, step)
            got[at] = got[at] + own[at]
            return carry

        lax.fori_loop(0, count // step, some, 0)

    def finish(self, name, stage, before):
        self.arrived(name, stage)
        self.add(name, stage, self.half(before, name, stage, False))
        if stage + 1 < self.bits:
            self.send_half(name, stage + 1, self.recv[name][stage])

    def drain(self):
        for copy in self.copies.values():
            copy.wait_send()


BOOKS = "books"


def quantizer_semantic(r):
    sem_code = r.chosen[0]
    rows, code_width = sem_code.shape
    columns = [slice(i * HALF, (i + 1) * HALF) for i in range(r.distill_v.shape[1] // HALF)]
    for i, cols in enumerate(columns):
        r.wide[i] = dot(sem_code, r.distill_v[:, cols])

    def row_sum(parts):
        return jnp.sum(sum(parts), axis=1, keepdims=True)

    for at in row_blocks(rows, 32):
        prediction = [r.wide[i, at, :] for i in range(len(columns))]
        target = [r.wavlm_v[at, cols].astype(F32) for cols in columns]
        pred_norm = lax.rsqrt(row_sum([p * p for p in prediction]) + EPS_COS)
        target_norm = lax.rsqrt(row_sum([w * w for w in target]) + EPS_COS)
        cosine = row_sum([p * w for p, w in zip(prediction, target)]) * (pred_norm * target_norm)
        from_target = -DISTILL * pred_norm * target_norm
        from_prediction = DISTILL * cosine * pred_norm * pred_norm
        for p, w, cols in zip(prediction, target, columns):
            r.act[at, cols] = (w * from_target + p * from_prediction).astype(BF16)
    grad_pred = r.act[:, : r.distill_v.shape[1]]
    put_distill(r.places.distill, dot(sem_code.T, grad_pred))
    r.gy[:, :code_width] = dot_t(grad_pred, r.distill_v[...])


def quantizer_latent(r):
    levels, rows, code_width = r.chosen.shape
    latent_t = r.latent[...].T
    r.wide[0] = dot_t(r.gquant[...], r.pout_v[0])
    r.wide[1] = dot(r.latent[...], r.pin_v[0])
    r.wide[2] = dot_t(r.gquant[...], r.pout_v[1])
    r.wide[3] = dot(r.latent[...], r.pin_v[1])
    put_group(r.places.pout, 0, t_dot(r.chosen[0], r.gquant[...]))
    put_group(r.places.pout, 1, t_dot(r.ac[...], r.gquant[...]))
    for at in row_blocks(rows, 32):
        grad_sem = r.wide[0, at, :] + r.gy[at, :code_width]
        commit = 2.0 * BETA * (r.wide[1, at, :] - r.chosen[0, at, :].astype(F32))
        r.g_rows[0, at, :] = (grad_sem - commit).astype(BF16)
        r.grad[at, :code_width] = (grad_sem + commit).astype(BF16)
        grad_ac, residual = r.wide[2, at, :], r.wide[3, at, :]
        for level in range(1, levels):
            residual = residual - r.chosen[level, at, :].astype(F32)
        carry = jnp.zeros_like(residual)
        for level in range(levels - 1, 0, -1):
            carry = carry + 2.0 * BETA * residual
            r.g_rows[level, at, :] = (grad_ac - carry).astype(BF16)
            residual = residual + r.chosen[level, at, :].astype(F32)
        r.grad[at, code_width:] = (grad_ac + carry).astype(BF16)
    put_group(r.places.pin, 0, dot(latent_t, r.grad[:, :code_width]))
    put_group(r.places.pin, 1, dot(latent_t, r.grad[:, code_width:]))
    r.gy[...] = dot_t(r.grad[...], jnp.concatenate([r.pin_v[0], r.pin_v[1]], axis=1))


def put_group(place, group, value):
    target, total = place.ref, value.shape[0]
    value = value.astype(BF16)
    if place.chunk is None:
        target[group * total : (group + 1) * total, :] = value
        return
    blocks, height, columns = target.shape[0] // 2, target.shape[1], value.shape[1]
    for i in range(blocks):
        for part in range(total // blocks // height):
            first = i * (total // blocks) + part * height
            cols = slice(place.col + part * columns, place.col + (part + 1) * columns)
            target[place.chunk.index(group * blocks + i), :, cols] = value[first : first + height]


def put_distill(place, value):
    target = place.ref
    if place.chunk is None:
        target[...] = value.astype(BF16)
        return
    blocks, height = target.shape[:2]
    rows = value.shape[0] // blocks
    columns = value.shape[1] * rows // height
    for i in range(blocks):
        part = value[i * rows : (i + 1) * rows]
        part = jnp.concatenate([part[:, at : at + columns] for at in range(0, value.shape[1], columns)], axis=0)
        target[place.chunk.index(i), :, place.col : place.col + columns] = part.astype(BF16)


def one_hot_rows(codes, first, count):
    row = iota((count, codes.shape[1]), 0)
    return jnp.where(codes - first == row, 1.0, 0.0).astype(BF16)


def pick_codes(r):
    levels, _, entries, code_width = r.books.shape
    entries = entries * r.books.shape[1]
    rows = r.cos.shape[0]
    slots = r.ring.shape[0]
    branch = lax.axis_index("branch")
    own = r.codes[:, pl.ds(pl.multiple_of(branch * rows, rows), rows)]
    r.code_rows[...] = jnp.broadcast_to(own[:, None, :], r.code_rows.shape)
    columns = jnp.concatenate([own.astype(F32), jnp.zeros((PAIR - levels, rows), F32)], axis=0).T
    lane = iota(columns.shape, 1)
    entry = iota((rows, entries), 1)
    r.code_cols[...] = columns
    r.ac_sum[...] = jnp.zeros(r.ac_sum.shape, F32)

    def book(level):
        slot = level % slots
        return pltpu.make_async_copy(r.books.at[level], r.ring.at[slot], r.sem_book.at[slot])

    def pick(level, carry):
        code = jnp.sum(jnp.where(lane == level, r.code_cols[...], 0.0), axis=1, keepdims=True)
        one_hot = jnp.where(entry == code.astype(jnp.int32), 1.0, 0.0).astype(BF16)
        book(level).wait()
        got = dot(one_hot, r.ring[level % slots].reshape(entries, code_width))
        r.chosen[level] = got.astype(BF16)
        r.ac_sum[...] += jnp.where(level > 0, got, 0.0)

        @pl.when(level + slots < levels)
        def _():
            book(level + slots).start()

        return carry

    def begin():
        for level in range(slots):
            book(level).start()

    def run():
        lax.fori_loop(0, levels, pick, 0, unroll=4)
        r.ac[...] = r.ac_sum[...].astype(BF16)

    return begin, run


def step_kernel(chunks, first_rows, bits, ins, outs, scratch):
    r = Refs({**ins, **outs, **scratch})
    t = r.t = Refs(r.t)
    r.att, r.g_rows, r.g_got, r.book_own = (r.ring.at[i] for i in range(4))
    r.ac_sum, r.code_cols = r.acc.at[:, : r.ac.shape[1]], r.gx.at[:, :PAIR]
    branch = lax.axis_index("branch")
    rows, width = r.tokens.shape
    levels, parts, entries, code_width = r.books.shape
    entries = entries * parts
    tiles = r.w_up_v.shape[1] // TILE
    pairs = width // PAIR
    if chunks:
        sums = Halving(chunks, bits, r.recv, r.packed, first_rows, r.send_sem, r.recv_sem)
        mine, level = sums.mine[bits - 2], lax.axis_index("dp") // 2
        wait_barrier = sums.barrier()
    moves = Moves(r.sem_move)
    begin_pick, run_pick = pick_codes(r)
    begin_pick()
    got_pout = [moves.start(r.pout_own.at[0], r.pout_v.at[branch])]
    frame_tables(r)
    if chunks:
        wait_barrier()
        sums.remote(r.pout_own.at[0], r.pout_v.at[branch], sums.partner[bits - 1], POUT)
    else:
        got_pout.append(moves.start(r.pout_other.at[0], r.pout_v.at[1 - branch]))
    got_rest = [
        moves.start(r.distill, r.distill_v),
        moves.start(r.wavlm.at[pl.ds(pl.multiple_of(branch * rows, rows), rows)], r.wavlm_v),
    ]
    got_attention = [moves.start(r.dec_qkv, r.w_qkv_v), moves.start(r.dec_out, r.w_out_v)]
    got_ffn = [moves.start(r.dec_up, r.w_up_v), moves.start(r.dec_down, r.w_down_v)]
    got_cotangent = [moves.start(r.cotangent, r.cotangent_v)]
    got_pin = [moves.start(r.pin_own.at[0], r.pin_v.at[branch])]
    if not chunks:
        got_pin.append(moves.start(r.pin_other.at[0], r.pin_v.at[1 - branch]))
    got_tokens = [moves.start(r.tokens, r.tokens_v)]
    got_attention_two = [moves.start(r.enc_qkv, r.w_qkv_e), moves.start(r.enc_out, r.w_out_e)]

    if chunks:
        def at(name, col=0):
            return Place(t[name], col, chunks[name])

        dec_down, enc_down = [at(DD0), at(DD1)], [at(ED0), at(ED1), at(ED2)]
        place = r.places = Refs(
            dec_up=[at(DU0), at(DU1)],
            dec_out=at(DA0),
            dec_qkv=[at(DA0, width), at(DA1), at(DA2)],
            enc_up=[at(EU0), at(EU1)],
            enc_out=at(EA0),
            enc_qkv=[at(EA1), at(EA2), at(EA3)],
            distill=at(DISTILL_GRAD),
            pout=at(MISC),
            pin=at(MISC, width),
        )
    else:
        dec_down, enc_down = [Place(t.dec_down)], [Place(t.enc_down)]
        place = r.places = Refs(
            dec_up=[Place(t.dec_up, i * tiles // 2 * TILE) for i in range(2)],
            dec_out=Place(t.dec_out),
            dec_qkv=[Place(t.dec_qkv, i * width) for i in range(3)],
            enc_up=[Place(t.enc_up, i * tiles // 2 * TILE) for i in range(2)],
            enc_out=Place(t.enc_out),
            enc_qkv=[Place(t.enc_qkv, i * width) for i in range(3)],
            distill=Place(t.distill),
            pout=Place(t.pout),
            pin=Place(t.pin),
        )

    def wait(moves, other=None):
        for move in moves:
            move.wait()
        if chunks and other is not None:
            sums.arrived(other)

    def layer_value(target, gain):
        for at in row_blocks(rows, 64):
            target[at, :] = (r.x2[at, :] + gain(3) * r.fo[at, :]).astype(BF16)

    def dec_gain(i):
        return r.vectors[1, i : i + 1, :]

    def enc_gain(i):
        return r.vectors[0, i : i + 1, :]

    def pick():
        run_pick()

    def semantic():
        wait(got_rest)
        quantizer_semantic(r)

    def quant():
        wait(got_pout, POUT)
        if chunks:
            sums.remote(r.pin_own.at[0], r.pin_v.at[branch], sums.partner[bits - 1], PIN)
        r.x[...] = dot(jnp.concatenate([r.chosen[0], r.ac[...]], axis=1), r.pout_v[...].reshape(-1, width))
        if chunks:
            for other in range(1, levels):
                target = sums.near_level(other)
                sums.remote(r.code_rows.at[target_level(target)], r.code_got.at[other], target, CODES, other)
            r.code_got[0] = r.code_rows[level]

    def target_level(target):
        return next(iter(target.values())) // 2

    def dec_project():
        wait(got_attention)
        attention_project(r, r.w_qkv_v, dec_gain)

    def dec_mix():
        attention_mix(r, r.w_out_v, dec_gain)

    def dec_ffn(half):
        def run():
            if half == 0:
                wait(got_ffn)
                wait(got_cotangent)
                ffn_backward_begin(r, dec_gain, r.cotangent_v)
            first, last = half * tiles // 2, (half + 1) * tiles // 2
            ffn_both(r, r.w_up_v, r.w_down_v, place.dec_up[half], dec_down, first, last)
            if half == 1:
                r.fo[...] = dot(r.act[...], r.w_down_v[...])
                layer_value(r.decoded, dec_gain)
                ffn_back_sum(r, r.w_up_v)
                ffn_backward_end(r, dec_gain, r.cotangent_v, r.dec_gains)
                got_ffn[:] = [moves.start(r.enc_up, r.w_up_v), moves.start(r.enc_down, r.w_down_v)]

        return run

    def dec_out():
        attention_backward_out(r, r.w_out_v, dec_gain, place.dec_out, r.dec_gains)

    def attention_pairs(first, last):
        return lambda: attention_backward_pairs(r, first, last)

    def dec_in(part):
        def run():
            attention_backward_in(r, place.dec_qkv[part], part)
            if part == 2:
                attention_backward_end(r, r.w_qkv_v, dec_gain, r.dec_gains)
                r.gquant[...] = r.gx[...].astype(BF16)

        return run

    def enc_project():
        wait(got_tokens)
        r.x[...] = r.tokens_v[...].astype(F32)
        wait(got_attention_two)
        attention_project(r, r.w_qkv_e, enc_gain)

    def enc_mix():
        attention_mix(r, r.w_out_e, enc_gain)

    def enc_ffn():
        wait(got_ffn)
        ffn_forward(r, r.w_up_v, r.w_down_v)
        layer_value(r.latent, enc_gain)

    def quantizer():
        wait(got_pin, PIN)
        quantizer_latent(r)
        if chunks:
            for other in reversed(range(1, levels)):
                target = sums.near_level(other)
                sums.arrived(CODES, other)
                sums.remote(r.g_rows.at[target_level(target)], r.g_got.at[other], target, BOOKS, 0, other)
            r.g_got[0] = r.g_rows[level]

    def book_half(core, put):
        quarter = entries // 4
        for side in range(2):
            r.book_sum[...] = jnp.zeros_like(r.book_sum)
            first = (core * 2 + side) * quarter

            def add(source, carry):
                one_hot = one_hot_rows(r.code_got[source, 0:1, :], first, quarter)
                r.book_sum[...] += dot(one_hot, r.g_got[source])
                return carry

            lax.fori_loop(0, levels, add, 0, unroll=4)
            put(side, r.book_sum[...])

    def finish_books(stage):
        blocks = entries // 4 // rows
        other_core, other_side = sums.partner[bits - 2], sums.partner[bits - 1]
        if stage == 0:
            for other in range(1, levels):
                sums.arrived(BOOKS, 0, other)

            def put(side, value):
                r.book_send[side] = value.astype(BF16)

            def keep(side, value):
                r.book_own[side * blocks : (side + 1) * blocks] = value.astype(BF16).reshape((blocks, rows, code_width))

            book_half(1 - mine, put)
            sums.remote(r.book_send, r.book_got, other_core, BOOKS, 1)
            book_half(mine, keep)
        elif stage == 1:
            sums.arrived(BOOKS, 1)
            for side in range(2):
                own = r.book_own[side * blocks : (side + 1) * blocks]
                r.book_got[side] = r.book_got[side] + own.reshape(r.book_got.shape[1:])
            sums.remote(r.book_got.at[1 - branch], r.book_last, other_side, BOOKS, 2)
        else:
            sums.arrived(BOOKS, 2)
            total = r.book_got[branch].astype(F32) + r.book_last[...].astype(F32)
            blocks = code_width // 128
            store_segment(r.packed, first_rows[BOOKS], Segment(BOOKS, 0, blocks, 0, blocks, 0, entries // 4), total)

    def all_books():
        parts = entries // TILE

        def one(step, carry):
            at = step // parts
            one_hot = one_hot_rows(r.code_rows[at, 0:1, :], step % parts * TILE, TILE)
            t.books[at, aligned(step % parts, TILE), :] = dot(one_hot, r.g_rows[at]).astype(BF16)
            return carry

        lax.fori_loop(0, levels * parts, one, 0)

    def enc_ffn_back(half):
        def run():
            first, last = half * tiles // 2, (half + 1) * tiles // 2
            if half == 0:
                ffn_backward_begin(r, enc_gain, r.gy)
            ffn_backward_tiles(r, r.w_down_v, place.enc_up[half], enc_down, first, last)
            if half == 1:
                ffn_back_sum(r, r.w_up_v)
                ffn_backward_end(r, enc_gain, r.gy, r.gains)

        return run

    def enc_out():
        attention_backward_out(r, r.w_out_e, enc_gain, place.enc_out, r.gains)

    def enc_in(part):
        def run():
            attention_backward_in(r, place.enc_qkv[part], part)
            if part == 2:
                attention_backward_end(r, r.w_qkv_e, enc_gain, r.gains)
                r.grad_tokens[...] = r.gx[...]
                if chunks:
                    spread_gains()

        return run

    def spread_gains():
        last, height = chunks[EA3], t.ea3.shape[1]
        for layer, ref in enumerate((r.gains, r.dec_gains)):
            for row in range(4):
                for block in range(width // 128):
                    owner = (layer * 4 + row) * (width // 128) + block
                    value = jnp.broadcast_to(ref[row : row + 1, block * 128 : (block + 1) * 128], (height, 128))
                    t.ea3[last.index(owner), :, width : width + 128] = value.astype(BF16)

    work = [
        (6.5, pick, ()),
        (2.0, semantic, (DISTILL_GRAD,)),
        (0.7, quant, ()),
        (1.5, dec_project, ()),
        (2.5, dec_mix, ()),
        (2.6, dec_ffn(0), (DU0,)),
        (2.7, dec_ffn(1), (DD0, DD1, DU1)),
        (1.2, dec_out, ()),
        (1.6, attention_pairs(0, pairs // 2), ()),
        (1.6, attention_pairs(pairs // 2, pairs), ()),
        (0.6, dec_in(0), (DA0,)),
        (0.6, dec_in(1), (DA1,)),
        (0.8, dec_in(2), (DA2,)),
        (1.5, enc_project, ()),
        (2.5, enc_mix, ()),
        (2.2, enc_ffn, ()),
        (2.0, quantizer, (BOOKS, MISC)),
        (2.0, enc_ffn_back(0), (EU0,)),
        (2.0, enc_ffn_back(1), (EU1, ED0, ED1, ED2)),
        (1.2, enc_out, (EA0,)),
        (1.6, attention_pairs(0, pairs // 2), ()),
        (1.6, attention_pairs(pairs // 2, pairs), ()),
        (0.6, enc_in(0), (EA1,)),
        (0.6, enc_in(1), (EA2,)),
        (1.0, enc_in(2), (EA3,)),
    ]
    if not chunks:
        for _, run, _ in work:
            run()
            if run is quantizer:
                all_books()
        return
    actions = plan(chunks, work, bits, rows * code_width * 2)

    def finish(name, stage):
        if name == BOOKS:
            finish_books(stage)
        else:
            sums.finish(name, stage, r.recv[name][stage - 1] if stage else t[name])

    for (_, run, made), acts in zip(work, actions):
        run()
        for name in made:
            if name != BOOKS:
                sums.send_half(name, 0, t[name])
        for name, stage in acts:
            finish(name, stage)
    for name, stage in actions[-1]:
        finish(name, stage)
    sums.drain()


POUT, PIN, CODES = 1, 2, 3
DISTILL_GRAD = "di"
DD0, DD1, DU0, DU1, DA0, DA1, DA2, MISC = "dd0", "dd1", "du0", "du1", "da0", "da1", "da2", "misc"
EU0, EU1, ED0, ED1, ED2 = "eu0", "eu1", "ed0", "ed1", "ed2"
EA0, EA1, EA2, EA3 = "ea0", "ea1", "ea2", "ea3"


def step(given, devices, with_sums):
    rows, width = given.tokens.shape
    ff = given.enc_up.shape[1]
    levels, entries, code_width = given.books.shape
    given.books = given.books.reshape(levels, -1, rows, code_width)
    bits = devices.bit_length() - 1
    vmem, hbm = pl.BlockSpec(memory_space=pltpu.VMEM), pl.BlockSpec(memory_space=pl.ANY)
    scratch = layer_scratch(rows, width, ff)
    scratch.update(
        w_qkv_e=pltpu.VMEM((width, 3 * width), BF16),
        w_out_e=pltpu.VMEM((width, width), BF16),
        cos=pltpu.VMEM((rows, PAIR), F32),
        sin=pltpu.VMEM((rows, PAIR), F32),
        bias=pltpu.VMEM((rows, rows), F32),
        ring=pltpu.VMEM((4,) + given.books.shape[1:], BF16),
        code_rows=pltpu.VMEM((levels, 8, rows), jnp.int32),
        chosen=pltpu.VMEM((levels, rows, code_width), BF16),
        ac=pltpu.VMEM((rows, code_width), BF16),
        gquant=pltpu.VMEM((rows, width), BF16),
        gy=pltpu.VMEM((rows, width), F32),
        latent=pltpu.VMEM((rows, width), BF16),
        pin_v=pltpu.VMEM((2, width, code_width), BF16),
        pout_v=pltpu.VMEM((2, code_width, width), BF16),
        distill_v=pltpu.VMEM(given.distill.shape, BF16),
        wavlm_v=pltpu.VMEM((rows, given.wavlm.shape[1]), BF16),
        tokens_v=pltpu.VMEM((rows, width), BF16),
        cotangent_v=pltpu.VMEM((rows, width), BF16),
        sem_move=pltpu.SemaphoreType.DMA((14,)),
        sem_book=pltpu.SemaphoreType.DMA((4,)),
    )
    outs = Refs(decoded=shaped((rows, width), BF16), grad_tokens=shaped((rows, width), F32))
    chunks, first_rows = {}, {}
    params = dict(vmem_limit_bytes=60 * 2**20)
    if with_sums:
        params.update(collective_id=0, has_side_effects=True)
        c, x, y = bits - 2, bits - 1, bits - 3
        b, a = range(y)
        share = width // devices
        low, high = ff // devices, share
        wide, half, blocks = ff // 128, ff // 256, width // 128
        third, quarter = 3 * blocks, blocks // 4
        chunks = dict(
            di=Chunk(
                high,
                width,
                [c, y, x, a, b],
                [
                    Segment(8, 0, 2 * blocks, 0, blocks, 0, high // 2),
                    Segment(8, blocks, 2 * blocks, 0, blocks, high // 2, high // 2),
                ],
            ),
            du0=Chunk(high, ff // 2, [c, y, a, x, b], [Segment(2, 0, wide, 0, half, 0, high)]),
            dd0=Chunk(low, width // 2, [c, a, y, b, x], [Segment(3, 0, blocks, 0, 2 * quarter, 0, low)]),
            dd1=Chunk(low, width // 2, [c, y, x, a, b], [Segment(3, 2 * quarter, blocks, 0, 2 * quarter, 0, low)]),
            du1=Chunk(high, ff // 2, [c, x, y, a, b], [Segment(2, half, wide, 0, half, 0, high)]),
            da0=Chunk(
                high,
                2 * width,
                [c, x, y, a, b],
                [Segment(1, 0, blocks, 0, blocks, 0, high), Segment(0, 0, third, width, blocks, 0, high)],
            ),
            da1=Chunk(high, width, [c, a, x, y, b], [Segment(0, blocks, third, 0, blocks, 0, high)]),
            da2=Chunk(high, width, [c, y, x, a, b], [Segment(0, 2 * blocks, third, 0, blocks, 0, high)]),
            misc=Chunk(
                high,
                2 * width,
                [c, x, y, a, b],
                [
                    Segment(9, 0, blocks, 0, blocks, 0, high),
                    Segment(10, 0, blocks // 2, width, blocks // 2, 0, high),
                    Segment(10, high * blocks // 2, blocks // 2, width + code_width, blocks // 2, 0, high),
                ],
            ),
            eu0=Chunk(high, ff // 2, [c, x, a, y, b], [Segment(6, 0, wide, 0, half, 0, high)]),
            eu1=Chunk(high, ff // 2, [c, x, y, a, b], [Segment(6, half, wide, 0, half, 0, high)]),
            ed0=Chunk(low, width // 2, [c, x, y, a, b], [Segment(7, 0, blocks, 0, 2 * quarter, 0, low)]),
            ed1=Chunk(low, width // 4, [c, y, x, a, b], [Segment(7, 2 * quarter, blocks, 0, quarter, 0, low)]),
            ed2=Chunk(low, width // 4, [c, y, a, b, x], [Segment(7, 3 * quarter, blocks, 0, quarter, 0, low)]),
            ea0=Chunk(high, width, [c, x, y, a, b], [Segment(5, 0, blocks, 0, blocks, 0, high)]),
            ea1=Chunk(high, width, [c, y, x, a, b], [Segment(4, 0, third, 0, blocks, 0, high)]),
            ea2=Chunk(high, width, [c, x, a, y, b], [Segment(4, blocks, third, 0, blocks, 0, high)]),
            ea3=Chunk(
                high,
                width + 128,
                [c, x, y, a, b],
                [Segment(4, 2 * blocks, third, 0, blocks, 0, high), Segment(11, 0, 1, width, 1, 0, 8)],
            ),
        )
        rows_of = [high * 3 * blocks, high * blocks, high * wide, low * blocks] * 2
        rows_of += [high * blocks, high * blocks, high * blocks, 8, entries // 4 * code_width // 128]
        first_rows = {i: sum(rows_of[:i]) for i in range(len(rows_of))}
        first_rows[BOOKS] = first_rows[len(rows_of) - 1]
        copies = len(chunks) * bits + 2 * levels + 2
        scratch.update(
            t={name: pltpu.VMEM(c.shape(bits), BF16) for name, c in chunks.items()},
            recv={
                name: [pltpu.VMEM(c.shape(bits - 1 - stage), BF16) for stage in range(bits)]
                for name, c in chunks.items()
            },
            gains=pltpu.VMEM((4, width), F32),
            dec_gains=pltpu.VMEM((4, width), F32),
            code_got=pltpu.VMEM((levels, 8, rows), jnp.int32),
                book_sum=pltpu.VMEM((entries // 4, code_width), F32),
            book_send=pltpu.VMEM((2, entries // 4, code_width), BF16),
            book_got=pltpu.VMEM((2, entries // 4, code_width), BF16),
            book_last=pltpu.VMEM((entries // 4, code_width), BF16),
            send_sem=pltpu.SemaphoreType.DMA((copies,)),
            recv_sem=pltpu.SemaphoreType.DMA((copies,)),
        )
        outs.packed = shaped((sum(rows_of), 128), F32)
    else:
        outs.update(gains=shaped((4, width), F32), dec_gains=shaped((4, width), F32))
        outs.t = dict(
            enc_qkv=shaped(given.enc_qkv.shape, BF16),
            enc_out=shaped(given.enc_out.shape, BF16),
            enc_up=shaped(given.enc_up.shape, BF16),
            enc_down=shaped(given.enc_down.shape, BF16),
            dec_qkv=shaped(given.enc_qkv.shape, BF16),
            dec_out=shaped(given.enc_out.shape, BF16),
            dec_up=shaped(given.enc_up.shape, BF16),
            dec_down=shaped(given.enc_down.shape, BF16),
            pin=shaped((2 * width, code_width), BF16),
            pout=shaped((2 * code_width, width), BF16),
            books=shaped((levels, entries, code_width), BF16),
            distill=shaped(given.distill.shape, BF16),
        )
    in_specs = dict.fromkeys(given, hbm)
    in_specs.update(
        lengths=pl.BlockSpec(memory_space=pltpu.SMEM), codes=vmem, vectors=vmem
    )
    got = pl.pallas_call(
        functools.partial(step_kernel, chunks, first_rows, bits),
        out_shape={k: pltpu.VMEM(v.shape, v.dtype) for k, v in outs.items()} if with_sums else dict(outs),
        in_specs=[in_specs],
        out_specs=jax.tree.map(lambda _: vmem, dict(outs)),
        scratch_shapes=[dict(scratch)],
        compiler_params=pltpu.CompilerParams(**params),
        name="step",
    )(dict(given))
    got = Refs(got)
    if not with_sums:
        return got
    last = [shaped((rows, 128), F32) for rows in rows_of]
    last[11] = shaped((1, 128), F32)

    def hand_on(packed, decoded, grad, *refs):
        outs, moves = refs[:-1], Moves(refs[-1])
        parts = [packed.at[pl.ds(first_rows[i], ref.shape[0])] for i, ref in enumerate(outs[:-2])]
        leaving = [moves.start(part, ref) for part, ref in zip(parts + [decoded, grad], outs)]
        for move in leaving:
            move.wait()

    return pl.pallas_call(
        hand_on,
        out_shape=last + [outs.decoded, outs.grad_tokens],
        in_specs=[vmem] * 3,
        out_specs=[hbm] * (len(last) + 2),
        scratch_shapes=[pltpu.SemaphoreType.DMA((len(last) + 2,))],
        compiler_params=pltpu.CompilerParams(vmem_limit_bytes=16 * 2**20),
        name="results",
    )(got.packed, got.decoded, got.grad_tokens)


def body(
    tokens,
    wavlm,
    cotangent,
    lengths,
    codes,
    enc_qkv,
    enc_out,
    enc_up,
    enc_down,
    dec_qkv,
    dec_out,
    dec_up,
    dec_down,
    vectors,
    proj_in,
    proj_out,
    codebooks,
    distill_proj,
):
    width = tokens.shape[1]
    devices = lax.axis_size("dp") * lax.axis_size("branch")
    with_sums = devices == 4 * codebooks.shape[0] and width // devices % 16 == 0
    given = Refs(
        tokens=tokens,
        wavlm=wavlm,
        cotangent=cotangent,
        lengths=lengths,
        codes=codes.T,
        enc_qkv=enc_qkv,
        enc_out=enc_out,
        enc_up=enc_up,
        enc_down=enc_down,
        dec_qkv=dec_qkv,
        dec_out=dec_out,
        dec_up=dec_up,
        dec_down=dec_down,
        vectors=vectors,
        pin_own=proj_in,
        pout_own=proj_out,
        books=codebooks,
        distill=distill_proj,
    )
    if with_sums:
        *sums, decoded, grad_tokens = step(given, devices, True)
        sums = [part.reshape(-1) for part in sums]
        order = (4, 5, 6, 7, 0, 1, 2, 3, 11, 10, 9, 12, 8)
        return (decoded, grad_tokens, *[sums[i] for i in order])
    swap = [(0, 1), (1, 0)]
    given.pin_other = lax.ppermute(proj_in, "branch", swap)
    given.pout_other = lax.ppermute(proj_out, "branch", swap)
    s = step(given, devices, False)
    t = Refs(s.t)
    gains = jnp.concatenate([s.gains, s.dec_gains])
    local = [t.enc_qkv, t.enc_out, t.enc_up, t.enc_down, t.dec_qkv, t.dec_out, t.dec_up, t.dec_down]
    local += [gains, t.pin, t.pout, t.books, t.distill]
    sums = [
        lax.psum_scatter(part.astype(F32).reshape(-1), ("dp", "branch"), scatter_dimension=0, tiled=True)
        for part in local
    ]
    return (s.decoded, s.grad_tokens, *sums)


def solution(mesh):
    rows, whole = P(("dp", "branch"), None), P()
    placed = (rows, P("dp", None), rows, rows, P("dp", None)) + (whole,) * 9
    placed += (P("branch", None, None),) * 2 + (whole,) * 2
    return jax.shard_map(
        body,
        mesh=mesh,
        in_specs=placed,
        out_specs=(rows, rows) + (P(("dp", "branch")),) * 13,
        check_vma=False,
    )
```

```python
import functools
import math

import jax
import jax.numpy as jnp
from jax import lax
from jax.experimental import pallas as pl
from jax.experimental.pallas import tpu as pltpu
from jax.sharding import PartitionSpec as P

HEADS = 8
WINDOW = 250
EPS_NORM = 1e-05
EPS_COS = 1e-06
BETA = 0.25
DISTILL = 10.0
ROPE_BASE = 10000.0

MESH = pl.DeviceIdType.MESH
F32 = jnp.float32
BF16 = jnp.bfloat16
TILE = 512
PAIR = 128
HALF = 256


def dot(left, right):
    return lax.dot_general(left, right, (((1,), (0,)), ((), ())), preferred_element_type=F32)


def dot_t(left, right):
    return lax.dot_general(left, right, (((1,), (1,)), ((), ())), preferred_element_type=F32)


def t_dot(left, right):
    return lax.dot_general(left, right, (((0,), (0,)), ((), ())), preferred_element_type=F32)


def iota(shape, dim):
    return lax.broadcasted_iota(jnp.int32, shape, dim)


def aligned(index, size):
    return pl.ds(pl.multiple_of(index * size, size), size)


class Refs(dict):
    __getattr__ = dict.__getitem__
    __setattr__ = dict.__setitem__


class Moves:
    def __init__(self, semaphores):
        self.semaphores, self.count = semaphores, 0

    def start(self, source, target):
        move = pltpu.make_async_copy(source, target, self.semaphores.at[self.count])
        self.count += 1
        move.start()
        return move


def layer_scratch(rows, width, ff):
    return Refs(
        x=pltpu.VMEM((rows, width), F32),
        s1=pltpu.VMEM((rows, 1), F32),
        h=pltpu.VMEM((rows, width), BF16),
        h1t=pltpu.VMEM((width, rows), BF16),
        h2t=pltpu.VMEM((width, rows), BF16),
        rinv=pltpu.VMEM((rows, width), F32),
        qkv=pltpu.VMEM((rows, 3 * width), BF16),
        mix=pltpu.VMEM((rows, width), BF16),
        ao=pltpu.VMEM((rows, width), F32),
        x2=pltpu.VMEM((rows, width), F32),
        s2=pltpu.VMEM((rows, 1), F32),
        act=pltpu.VMEM((rows, ff), BF16),
        dg=pltpu.VMEM((rows, ff), BF16),
        fo=pltpu.VMEM((rows, width), F32),
        grad=pltpu.VMEM((rows, width), BF16),
        gx=pltpu.VMEM((rows, width), F32),
        acc=pltpu.VMEM((rows, width), F32),
        wide=pltpu.VMEM((4, rows, HALF), F32),
        change=pltpu.VMEM((2, rows, rows), BF16),
        w_qkv_v=pltpu.VMEM((width, 3 * width), BF16),
        w_out_v=pltpu.VMEM((width, width), BF16),
        w_up_v=pltpu.VMEM((width, ff), BF16),
        w_down_v=pltpu.VMEM((ff, width), BF16),
    )


def shaped(shape, kind):
    return jax.ShapeDtypeStruct(shape, kind)


def frame_tables(r):
    rows = r.cos.shape[0]
    place = iota((rows, PAIR), 0)
    query, key = iota((rows, rows), 0), iota((rows, rows), 1)
    begin, begin_query = jnp.zeros_like(place), jnp.zeros_like(query)
    edge = 0
    for clip in range(r.lengths.shape[1] - 1):
        edge = edge + r.lengths[0, clip]
        begin = jnp.where(place >= edge, edge, begin)
        begin_query = jnp.where(query >= edge, edge, begin_query)
    allowed = (key >= begin_query) & (key <= query) & (query - key < WINDOW)
    r.bias[...] = jnp.where(allowed, 0.0, -1e30)
    lane = iota((rows, PAIR), 1)
    rate = jnp.exp((lane % 32).astype(F32) * (-math.log(ROPE_BASE) / 32))
    angle = (place - begin).astype(F32) * rate
    r.cos[...] = jnp.cos(angle)
    sine = jnp.sin(angle)
    r.sin[...] = jnp.where(lane % 64 < 32, -sine, sine)


def rotated(value, cosine, sine):
    lane = iota(value.shape, 1)
    swapped = jnp.where(lane % 64 < 32, pltpu.roll(value, PAIR - 32, 1), pltpu.roll(value, 32, 1))
    return value * cosine + swapped * sine


def head_masks(rows):
    low = iota((rows, PAIR), 1) < 64
    return (jnp.where(low, 1.0, 0.0).astype(BF16), jnp.where(low, 0.0, 1.0).astype(BF16))


def row_blocks(rows, step):
    return [slice(i, i + step) for i in range(0, rows, step)]


def attention_project(r, w_qkv, gain):
    rows, width = r.x.shape
    scale = gain(0)
    for at in row_blocks(rows, 64):
        x = r.x[at, :]
        s1 = lax.rsqrt(jnp.mean(x * x, axis=1, keepdims=True) + EPS_NORM)
        r.s1[at, :] = s1
        r.h[at, :] = (x * s1 * scale).astype(BF16)
    for half in range(3 * width // HALF):
        slot, part = half % 4, half // (width // HALF)
        cols = slice(half * HALF, (half + 1) * HALF)
        r.wide[slot] = dot(r.h[...], w_qkv[:, cols])
        for at in row_blocks(rows, 64):
            for p in range(HALF // PAIR):
                value = r.wide[slot, at, p * PAIR : (p + 1) * PAIR]
                if part < 2:
                    value = rotated(value, r.cos[at, :], r.sin[at, :])
                low = value.astype(BF16)
                if part == 0:
                    low = (low.astype(F32) * 0.125).astype(BF16)
                r.qkv[at, half * HALF + p * PAIR : half * HALF + (p + 1) * PAIR] = low
    r.h1t[...] = r.h[...].T


def attention_mix(r, w_out, gain):
    rows, width = r.x.shape
    masks = head_masks(rows)
    low = iota((rows, PAIR), 1) < 64
    pairs = width // PAIR
    for p in range(pairs):
        query = r.qkv[:, p * PAIR : (p + 1) * PAIR]
        key = r.qkv[:, (p + pairs) * PAIR : (p + pairs + 1) * PAIR]
        value = r.qkv[:, (p + 2 * pairs) * PAIR : (p + 2 * pairs + 1) * PAIR]
        outs = []
        for h in range(2):
            head = 2 * p + h
            slot = head % 4
            r.wide[slot] = dot_t(query * masks[h], key)
            for at in row_blocks(rows, 64):
                seen = PAIR if at.stop <= PAIR else rows
                scores = r.wide[slot, at, :seen] + r.bias[at, :seen]
                weights = jnp.exp(scores - jnp.max(scores, axis=1, keepdims=True))
                r.att[head, at, :seen] = weights.astype(BF16)
                if seen < rows:
                    r.att[head, at, seen:] = jnp.zeros((64, rows - seen), BF16)
            outs.append(dot(r.att[head], value * masks[h] + masks[1 - h]))
        inverse = 1.0 / pltpu.roll(jnp.where(low, outs[1], outs[0]), 64, 1)
        r.rinv[:, p * PAIR : (p + 1) * PAIR] = inverse
        r.mix[:, p * PAIR : (p + 1) * PAIR] = (jnp.where(low, outs[0], outs[1]) * inverse).astype(BF16)
    r.ao[...] = dot(r.mix[...], w_out[...])
    scale_one, scale_two = gain(1), gain(2)
    for at in row_blocks(rows, 64):
        x2 = r.x[at, :] + scale_one * r.ao[at, :]
        r.x2[at, :] = x2
        s2 = lax.rsqrt(jnp.mean(x2 * x2, axis=1, keepdims=True) + EPS_NORM)
        r.s2[at, :] = s2
        r.h[at, :] = (x2 * s2 * scale_two).astype(BF16)
    r.h2t[...] = r.h[...].T


def gelu_parts(pre):
    slope = math.sqrt(2.0 / math.pi)
    square = pre * pre
    bent = jnp.tanh(slope * pre * (1.0 + 0.044715 * square))
    half = 0.5 * (1.0 + bent)
    turn = 0.5 * pre * (1.0 - bent * bent) * slope * (1.0 + 3.0 * 0.044715 * square)
    return (pre * half).astype(BF16), half + turn


def ffn_forward(r, w_up, w_down):
    rows, ff = r.act.shape
    for half in range(ff // HALF):
        slot, cols = half % 4, slice(half * HALF, (half + 1) * HALF)
        r.wide[slot] = dot(r.h[...], w_up[:, cols])
        for at in row_blocks(rows, 32):
            act, slope = gelu_parts(r.wide[slot, at, :])
            r.act[at, cols] = act
            r.dg[at, cols] = slope.astype(BF16)
    r.fo[...] = dot(r.act[...], w_down[...])


def ffn_both(r, w_up, w_down, grad_up, grad_down, first, last):
    rows = r.act.shape[0]
    for t in range(first, last):
        cols = slice(t * TILE, (t + 1) * TILE)
        for side in range(TILE // HALF):
            part = slice(t * TILE + side * HALF, t * TILE + (side + 1) * HALF)
            r.wide[side] = dot(r.h[...], w_up[:, part])
            r.wide[2 + side] = dot_t(r.grad[...], w_down[part, :])
            for at in row_blocks(rows, 32):
                act, slope = gelu_parts(r.wide[side, at, :])
                r.act[at, part] = act
                r.dg[at, part] = (r.wide[2 + side, at, :] * slope).astype(BF16)
        grad_up.shift((t - first) * TILE).put(dot(r.h2t[...], r.dg[:, cols]))
        put_rows(grad_down, t_dot(r.act[:, cols], r.grad[...]), t)


def ffn_back_sum(r, w_up):
    r.acc[...] = dot_t(r.dg[...], w_up[...])


def norm_back(stream, inverse, grad):
    mean = jnp.mean(grad * stream, axis=1, keepdims=True)
    return inverse * grad - stream * (inverse * inverse * inverse * mean)


def column_sum(value):
    return jnp.sum(value, axis=0, keepdims=True)


class Place:
    def __init__(self, ref, col=0, chunk=None):
        self.ref, self.col, self.chunk = ref, col, chunk

    def shift(self, by):
        return Place(self.ref, self.col + by, self.chunk)

    def put(self, value):
        value = value.astype(BF16)
        cols = slice(self.col, self.col + value.shape[1])
        if self.chunk is None:
            self.ref[:, cols] = value
            return
        blocks, rows = self.ref.shape[:2]
        for owner in range(blocks):
            self.ref[self.chunk.index(owner), :, cols] = value[owner * rows : (owner + 1) * rows]


def put_rows(places, value, tile):
    value = value.astype(BF16)
    begin = 0
    for place in places:
        part = value[:, begin : begin + place.ref.shape[-1]]
        begin += place.ref.shape[-1]
        if place.chunk is None:
            place.ref[tile * TILE : tile * TILE + TILE, :] = part
            continue
        rows = place.ref.shape[1]
        for i in range(TILE // rows):
            place.ref[place.chunk.index(tile * (TILE // rows) + i)] = part[i * rows : (i + 1) * rows]


def ffn_backward_begin(r, gain, gy_ref):
    scale = gain(3)
    for at in row_blocks(r.grad.shape[0], 64):
        r.grad[at, :] = (scale * gy_ref[at, :].astype(F32)).astype(BF16)


def ffn_backward_tiles(r, w_down, grad_up, grad_down, first, last):
    rows = r.act.shape[0]
    for t in range(first, last):
        cols = slice(t * TILE, (t + 1) * TILE)
        for side in range(TILE // HALF):
            part = slice(t * TILE + side * HALF, t * TILE + (side + 1) * HALF)
            slot = (2 * t + side) % 4
            r.wide[slot] = dot_t(r.grad[...], w_down[part, :])
            for at in row_blocks(rows, 64):
                r.dg[at, part] = (r.wide[slot, at, :] * r.dg[at, part].astype(F32)).astype(BF16)
        put_rows(grad_down, t_dot(r.act[:, cols], r.grad[...]), t)
        grad_up.shift((t - first) * TILE).put(dot(r.h2t[...], r.dg[:, cols]))


def ffn_backward_end(r, gain, gy_ref, gain_out):
    scale = gain(2)
    to_gain = to_scale = 0.0
    for at in row_blocks(r.x2.shape[0], 32):
        gy = gy_ref[at, :].astype(F32)
        to_scale = to_scale + column_sum(gy * r.fo[at, :])
        back, x2, s2 = r.acc[at, :], r.x2[at, :], r.s2[at, :]
        to_gain = to_gain + column_sum(back * x2 * s2)
        r.gx[at, :] = gy + norm_back(x2, s2, back * scale)
    gain_out[3:4, :] = to_scale
    gain_out[2:3, :] = to_gain


def attention_backward_out(r, w_out, gain, grad_out, gain_out):
    scale = gain(1)
    to_scale = 0.0
    for at in row_blocks(r.gx.shape[0], 64):
        gx = r.gx[at, :]
        to_scale = to_scale + column_sum(gx * r.ao[at, :])
        r.grad[at, :] = (scale * gx).astype(BF16)
    gain_out[1:2, :] = to_scale
    grad_out.put(t_dot(r.mix[...], r.grad[...]))
    r.grad[...] = dot_t(r.grad[...], w_out[...]).astype(BF16)


def attention_backward_pairs(r, first, last):
    rows, width = r.x.shape
    masks = head_masks(rows)
    masks_t = [jnp.where((iota((PAIR, rows), 0) < 64) == (h == 0), 1.0, 0.0).astype(BF16) for h in range(2)]
    pairs = width // PAIR
    for p in range(first, last):
        lanes = [slice((p + i * pairs) * PAIR, (p + i * pairs + 1) * PAIR) for i in range(3)]
        query, key, value = (r.qkv[:, at] for at in lanes)
        grad_mixed = (r.grad[:, lanes[0]].astype(F32) * r.rinv[:, lanes[0]]).astype(BF16)
        product = (grad_mixed.astype(F32) * r.mix[:, lanes[0]].astype(F32)).astype(BF16)
        beside = jnp.concatenate([value, jnp.full(value.shape, -1.0, BF16)], axis=1)
        query_t, grad_t = query.T, grad_mixed.T
        to_query = to_key = to_value = 0.0
        for h in range(2):
            head = 2 * p + h
            slot = head % 4
            both = jnp.concatenate([grad_mixed * masks[h], product * masks[h]], axis=1)
            r.wide[slot] = dot_t(both, beside)
            for at in row_blocks(rows, 64):
                r.change[h, at, :] = (r.att[head, at, :].astype(F32) * r.wide[slot, at, :]).astype(BF16)
            to_query = to_query + dot(r.change[h], key * masks[h])
            to_key = to_key + dot(query_t * masks_t[h], r.change[h])
            to_value = to_value + dot(grad_t * masks_t[h], r.att[head])
        cosine, sine = r.cos[...], -r.sin[...]
        r.qkv[:, lanes[0]] = rotated(to_query * 0.125, cosine, sine).astype(BF16)
        r.qkv[:, lanes[1]] = rotated(to_key.T, cosine, sine).astype(BF16)
        r.qkv[:, lanes[2]] = to_value.T.astype(BF16)


def attention_backward_in(r, grad_qkv, part):
    width = r.x.shape[1]
    grad_qkv.put(dot(r.h1t[...], r.qkv[:, part * width : (part + 1) * width]))


def attention_backward_end(r, w_qkv, gain, gain_out):
    r.acc[...] = dot_t(r.qkv[...], w_qkv[...])
    scale = gain(0)
    to_gain = 0.0
    for at in row_blocks(r.x.shape[0], 32):
        back, x, s1 = r.acc[at, :], r.x[at, :], r.s1[at, :]
        to_gain = to_gain + column_sum(back * x * s1)
        r.gx[at, :] = r.gx[at, :] + norm_back(x, s1, back * scale)
    gain_out[0:1, :] = to_gain


class Segment:
    def __init__(self, result, base, stride, col, blocks, row, rows):
        self.result, self.base, self.stride, self.col, self.blocks = result, base, stride, col, blocks
        self.row, self.rows = row, rows


class Chunk:
    def __init__(self, rows, columns, order, segments):
        self.rows, self.columns, self.order, self.segments = rows, columns, order, segments

    def index(self, owner):
        bits = len(self.order)
        return sum((owner >> (bits - 1 - dim) & 1) << (bits - 1 - stage) for stage, dim in enumerate(self.order))

    def shape(self, leading):
        return (2**leading, self.rows, self.columns)

    def bytes(self, bits):
        return 2**bits * self.rows * self.columns * 2


def plan(chunks, work, bits, book_bytes):
    core, x, y = bits - 2, bits - 1, bits - 3
    ends, middle = -1, -2
    free, pending, done = {}, [], []
    now = 0.0

    def carry(link, size, rate=42e3):
        free[link] = max(now, free.get(link, 0.0)) + size / rate
        return free[link]

    def begin(name, stage):
        if name == BOOKS:
            size = 1.2 * 2 ** (bits - 3) * book_bytes
            if stage == 0:
                there = max(carry(y, size), carry(ends, 1.5 * size), carry(middle, 2 * size))
            else:
                there = carry(core, 4 * book_bytes, 400e3) if stage == 1 else carry(x, 2 * book_bytes)
        else:
            dim = chunks[name].order[stage]
            size = chunks[name].bytes(bits) / 2 ** (stage + 1)
            if dim == core:
                there = carry(core, size, 400e3)
            elif dim == x or dim == y:
                there = carry(dim, size)
            else:
                there = carry(ends, size)
                if dim < y - 1:
                    there = max(there, carry(middle, 2 * size))
        pending.append((there + 1.5, name, stage))

    def finish(limit):
        nonlocal now
        acts = []
        while pending:
            pending.sort(key=lambda p: p[0])
            if pending[0][0] + (0.5 if limit < math.inf else 0.0) > limit:
                break
            at, name, stage = pending.pop(0)
            if name == BOOKS:
                cost = (6.0, 0.6, 0.3)[stage]
            else:
                cost = 0.25 + 0.3e-6 * chunks[name].bytes(bits) / 2 ** (stage + 1)
            now = max(now, at) + cost
            limit = max(limit, now)
            acts.append((name, stage))
            if stage + 1 < (3 if name == BOOKS else bits):
                begin(name, stage + 1)
        return acts

    for took, _, names in work:
        now += 0.95 * took
        for name in names:
            begin(name, 0)
        done.append(finish(now))
    done.append(finish(math.inf))
    return done


def store_segment(packed, first, segment, value):
    for i in range(segment.blocks):
        where = pl.ds(first + segment.base + i, segment.rows, stride=segment.stride)
        packed[where, :] = value[
            segment.row : segment.row + segment.rows, segment.col + i * 128 : segment.col + (i + 1) * 128
        ]


class Halving:
    def __init__(self, chunks, bits, recv, packed, first, send_sem, recv_sem):
        self.chunks = chunks
        self.bits, self.recv, self.packed, self.first = bits, recv, packed, first
        self.send_sem, self.recv_sem = send_sem, recv_sem
        self.copies = {}
        dp, branch = lax.axis_index("dp"), lax.axis_index("branch")
        self.mine, self.partner = [], []
        for dim in range(bits - 1):
            weight = 2 ** (bits - 2 - dim)
            bit = dp // weight % 2
            self.mine.append(bit)
            self.partner.append({"dp": dp + weight * (1 - 2 * bit), "branch": branch})
        self.mine.append(branch)
        self.partner.append({"dp": dp, "branch": 1 - branch})

    def near_level(self, other):
        dp = lax.axis_index("dp")
        for i in range(self.bits - 2):
            if other >> i & 1:
                dp = dp + 2 ** (i + 1) * (1 - 2 * self.mine[self.bits - 3 - i])
        return {"dp": dp, "branch": lax.axis_index("branch")}

    def barrier(self):
        semaphore = pltpu.get_barrier_semaphore()
        levels = 2 ** (self.bits - 2)
        targets = self.partner[self.bits - 2 :] + [self.near_level(other) for other in range(1, levels)]
        for target in targets:
            pl.semaphore_signal(semaphore, inc=1, device_id=target, device_id_type=MESH)
        return lambda: pl.semaphore_wait(semaphore, len(targets))

    def half(self, ref, name, stage, other):
        mine = self.mine[self.chunks[name].order[stage]]
        count = 2 ** (self.bits - 1 - stage)
        return ref.at[pl.ds((1 - mine if other else mine) * count, count)]

    def remote(self, source, target, device, *key):
        slot = len(self.copies)
        self.copies[key] = pltpu.make_async_remote_copy(
            src_ref=source,
            dst_ref=target,
            send_sem=self.send_sem.at[slot],
            recv_sem=self.recv_sem.at[slot],
            device_id=device,
            device_id_type=MESH,
        )
        self.copies[key].start()

    def send(self, name, stage, source):
        dim = self.chunks[name].order[stage]
        self.remote(source, self.recv[name][stage], self.partner[dim], name, stage)

    def send_half(self, name, stage, ref):
        self.send(name, stage, self.half(ref, name, stage, True))

    def arrived(self, *key):
        self.copies[key].wait_recv()

    def add(self, name, stage, own):
        chunk = self.chunks[name]
        got = self.recv[name][stage]
        if stage == self.bits - 1:
            value = own[0].astype(F32) + got[0].astype(F32)
            for segment in chunk.segments:
                store_segment(self.packed, self.first[segment.result], segment, value)
            return
        count = 2 ** (self.bits - 1 - stage)
        step = min(count, 4)

        def some(i, carry):
            at = pl.ds(i * step, step)
            got[at] = got[at] + own[at]
            return carry

        lax.fori_loop(0, count // step, some, 0)

    def finish(self, name, stage, before):
        self.arrived(name, stage)
        self.add(name, stage, self.half(before, name, stage, False))
        if stage + 1 < self.bits:
            self.send_half(name, stage + 1, self.recv[name][stage])

    def drain(self):
        for copy in self.copies.values():
            copy.wait_send()


BOOKS = "books"


def quantizer_semantic(r):
    sem_code = r.chosen[0]
    rows, code_width = sem_code.shape
    columns = [slice(i * HALF, (i + 1) * HALF) for i in range(r.distill_v.shape[1] // HALF)]
    for i, cols in enumerate(columns):
        r.wide[i] = dot(sem_code, r.distill_v[:, cols])

    def row_sum(parts):
        return jnp.sum(sum(parts), axis=1, keepdims=True)

    for at in row_blocks(rows, 32):
        prediction = [r.wide[i, at, :] for i in range(len(columns))]
        target = [r.wavlm_v[at, cols].astype(F32) for cols in columns]
        pred_norm = lax.rsqrt(row_sum([p * p for p in prediction]) + EPS_COS)
        target_norm = lax.rsqrt(row_sum([w * w for w in target]) + EPS_COS)
        cosine = row_sum([p * w for p, w in zip(prediction, target)]) * (pred_norm * target_norm)
        from_target = -DISTILL * pred_norm * target_norm
        from_prediction = DISTILL * cosine * pred_norm * pred_norm
        for p, w, cols in zip(prediction, target, columns):
            r.act[at, cols] = (w * from_target + p * from_prediction).astype(BF16)
    grad_pred = r.act[:, : r.distill_v.shape[1]]
    put_distill(r.places.distill, dot(sem_code.T, grad_pred))
    r.gy[:, :code_width] = dot_t(grad_pred, r.distill_v[...])


def quantizer_latent(r):
    levels, rows, code_width = r.chosen.shape
    latent_t = r.latent[...].T
    r.wide[0] = dot_t(r.gquant[...], r.pout_v[0])
    r.wide[1] = dot(r.latent[...], r.pin_v[0])
    r.wide[2] = dot_t(r.gquant[...], r.pout_v[1])
    r.wide[3] = dot(r.latent[...], r.pin_v[1])
    put_group(r.places.pout, 0, t_dot(r.chosen[0], r.gquant[...]))
    put_group(r.places.pout, 1, t_dot(r.ac[...], r.gquant[...]))
    for at in row_blocks(rows, 32):
        grad_sem = r.wide[0, at, :] + r.gy[at, :code_width]
        commit = 2.0 * BETA * (r.wide[1, at, :] - r.chosen[0, at, :].astype(F32))
        r.g_rows[0, at, :] = (grad_sem - commit).astype(BF16)
        r.grad[at, :code_width] = (grad_sem + commit).astype(BF16)
        grad_ac, residual = r.wide[2, at, :], r.wide[3, at, :]
        for level in range(1, levels):
            residual = residual - r.chosen[level, at, :].astype(F32)
        carry = jnp.zeros_like(residual)
        for level in range(levels - 1, 0, -1):
            carry = carry + 2.0 * BETA * residual
            r.g_rows[level, at, :] = (grad_ac - carry).astype(BF16)
            residual = residual + r.chosen[level, at, :].astype(F32)
        r.grad[at, code_width:] = (grad_ac + carry).astype(BF16)
    put_group(r.places.pin, 0, dot(latent_t, r.grad[:, :code_width]))
    put_group(r.places.pin, 1, dot(latent_t, r.grad[:, code_width:]))
    r.gy[...] = dot_t(r.grad[...], jnp.concatenate([r.pin_v[0], r.pin_v[1]], axis=1))


def put_group(place, group, value):
    target, total = place.ref, value.shape[0]
    value = value.astype(BF16)
    if place.chunk is None:
        target[group * total : (group + 1) * total, :] = value
        return
    blocks, height, columns = target.shape[0] // 2, target.shape[1], value.shape[1]
    for i in range(blocks):
        for part in range(total // blocks // height):
            first = i * (total // blocks) + part * height
            cols = slice(place.col + part * columns, place.col + (part + 1) * columns)
            target[place.chunk.index(group * blocks + i), :, cols] = value[first : first + height]


def put_distill(place, value):
    target = place.ref
    if place.chunk is None:
        target[...] = value.astype(BF16)
        return
    blocks, height = target.shape[:2]
    rows = value.shape[0] // blocks
    columns = value.shape[1] * rows // height
    for i in range(blocks):
        part = value[i * rows : (i + 1) * rows]
        part = jnp.concatenate([part[:, at : at + columns] for at in range(0, value.shape[1], columns)], axis=0)
        target[place.chunk.index(i), :, place.col : place.col + columns] = part.astype(BF16)


def one_hot_rows(codes, first, count):
    row = iota((count, codes.shape[1]), 0)
    return jnp.where(codes - first == row, 1.0, 0.0).astype(BF16)


def pick_codes(r):
    levels, _, entries, code_width = r.books.shape
    entries = entries * r.books.shape[1]
    rows = r.cos.shape[0]
    slots = r.ring.shape[0]
    branch = lax.axis_index("branch")
    own = r.codes[:, pl.ds(pl.multiple_of(branch * rows, rows), rows)]
    r.code_rows[...] = jnp.broadcast_to(own[:, None, :], r.code_rows.shape)
    columns = jnp.concatenate([own.astype(F32), jnp.zeros((PAIR - levels, rows), F32)], axis=0).T
    lane = iota(columns.shape, 1)
    entry = iota((rows, entries), 1)
    r.code_cols[...] = columns
    r.ac_sum[...] = jnp.zeros(r.ac_sum.shape, F32)

    def book(level):
        slot = level % slots
        return pltpu.make_async_copy(r.books.at[level], r.ring.at[slot], r.sem_book.at[slot])

    def pick(level, carry):
        code = jnp.sum(jnp.where(lane == level, r.code_cols[...], 0.0), axis=1, keepdims=True)
        one_hot = jnp.where(entry == code.astype(jnp.int32), 1.0, 0.0).astype(BF16)
        book(level).wait()
        got = dot(one_hot, r.ring[level % slots].reshape(entries, code_width))
        r.chosen[level] = got.astype(BF16)
        r.ac_sum[...] += jnp.where(level > 0, got, 0.0)

        @pl.when(level + slots < levels)
        def _():
            book(level + slots).start()

        return carry

    def begin():
        for level in range(slots):
            book(level).start()

    def run():
        lax.fori_loop(0, levels, pick, 0, unroll=4)
        r.ac[...] = r.ac_sum[...].astype(BF16)

    return begin, run


def step_kernel(chunks, first_rows, bits, ins, outs, scratch):
    r = Refs({**ins, **outs, **scratch})
    t = r.t = Refs(r.t)
    r.att, r.g_rows, r.g_got, r.book_own = (r.ring.at[i] for i in range(4))
    r.ac_sum, r.code_cols = r.acc.at[:, : r.ac.shape[1]], r.gx.at[:, :PAIR]
    branch = lax.axis_index("branch")
    rows, width = r.tokens.shape
    levels, parts, entries, code_width = r.books.shape
    entries = entries * parts
    tiles = r.w_up_v.shape[1] // TILE
    pairs = width // PAIR
    if chunks:
        sums = Halving(chunks, bits, r.recv, r.packed, first_rows, r.send_sem, r.recv_sem)
        mine, level = sums.mine[bits - 2], lax.axis_index("dp") // 2
        wait_barrier = sums.barrier()
    moves = Moves(r.sem_move)
    begin_pick, run_pick = pick_codes(r)
    begin_pick()
    got_pout = [moves.start(r.pout_own.at[0], r.pout_v.at[branch])]
    if chunks:
        wait_barrier()
        sums.remote(r.pout_own.at[0], r.pout_v.at[branch], sums.partner[bits - 1], POUT)
    else:
        got_pout.append(moves.start(r.pout_other.at[0], r.pout_v.at[1 - branch]))
    got_rest = [
        moves.start(r.distill, r.distill_v),
        moves.start(r.wavlm.at[pl.ds(pl.multiple_of(branch * rows, rows), rows)], r.wavlm_v),
    ]
    got_attention, got_ffn, got_cotangent, got_pin, got_tokens, got_attention_two = ([] for _ in range(6))
    frame_tables(r)

    def fetch_rest():
        got_attention.extend([moves.start(r.dec_qkv, r.w_qkv_v), moves.start(r.dec_out, r.w_out_v)])
        got_ffn.extend([moves.start(r.dec_up, r.w_up_v), moves.start(r.dec_down, r.w_down_v)])
        got_cotangent.append(moves.start(r.cotangent, r.cotangent_v))
        got_pin.append(moves.start(r.pin_own.at[0], r.pin_v.at[branch]))
        if not chunks:
            got_pin.append(moves.start(r.pin_other.at[0], r.pin_v.at[1 - branch]))
        got_tokens.append(moves.start(r.tokens, r.tokens_v))
        got_attention_two.extend([moves.start(r.enc_qkv, r.w_qkv_e), moves.start(r.enc_out, r.w_out_e)])

    if chunks:
        def at(name, col=0):
            return Place(t[name], col, chunks[name])

        dec_down, enc_down = [at(DD0), at(DD1)], [at(ED0), at(ED1), at(ED2)]
        place = r.places = Refs(
            dec_up=[at(DU0), at(DU1)],
            dec_out=at(DA0),
            dec_qkv=[at(DA0, width), at(DA1), at(DA2)],
            enc_up=[at(EU0), at(EU1)],
            enc_out=at(EA0),
            enc_qkv=[at(EA1), at(EA2), at(EA3)],
            distill=at(DISTILL_GRAD),
            pout=at(MISC),
            pin=at(MISC, width),
        )
    else:
        dec_down, enc_down = [Place(t.dec_down)], [Place(t.enc_down)]
        place = r.places = Refs(
            dec_up=[Place(t.dec_up, i * tiles // 2 * TILE) for i in range(2)],
            dec_out=Place(t.dec_out),
            dec_qkv=[Place(t.dec_qkv, i * width) for i in range(3)],
            enc_up=[Place(t.enc_up, i * tiles // 2 * TILE) for i in range(2)],
            enc_out=Place(t.enc_out),
            enc_qkv=[Place(t.enc_qkv, i * width) for i in range(3)],
            distill=Place(t.distill),
            pout=Place(t.pout),
            pin=Place(t.pin),
        )

    def wait(moves, other=None):
        for move in moves:
            move.wait()
        if chunks and other is not None:
            sums.arrived(other)

    def layer_value(target, gain):
        for at in row_blocks(rows, 64):
            target[at, :] = (r.x2[at, :] + gain(3) * r.fo[at, :]).astype(BF16)

    def dec_gain(i):
        return r.vectors[1, i : i + 1, :]

    def enc_gain(i):
        return r.vectors[0, i : i + 1, :]

    def pick():
        run_pick()
        fetch_rest()

    def semantic():
        wait(got_rest)
        quantizer_semantic(r)

    def quant():
        wait(got_pout, POUT)
        if chunks:
            sums.remote(r.pin_own.at[0], r.pin_v.at[branch], sums.partner[bits - 1], PIN)
        r.x[...] = dot(jnp.concatenate([r.chosen[0], r.ac[...]], axis=1), r.pout_v[...].reshape(-1, width))
        if chunks:
            for other in range(1, levels):
                target = sums.near_level(other)
                sums.remote(r.code_rows.at[target_level(target)], r.code_got.at[other], target, CODES, other)
            r.code_got[0] = r.code_rows[level]

    def target_level(target):
        return next(iter(target.values())) // 2

    def dec_project():
        wait(got_attention)
        attention_project(r, r.w_qkv_v, dec_gain)

    def dec_mix():
        attention_mix(r, r.w_out_v, dec_gain)

    def dec_ffn(half):
        def run():
            if half == 0:
                wait(got_ffn)
                wait(got_cotangent)
                ffn_backward_begin(r, dec_gain, r.cotangent_v)
            first, last = half * tiles // 2, (half + 1) * tiles // 2
            ffn_both(r, r.w_up_v, r.w_down_v, place.dec_up[half], dec_down, first, last)

        return run

    def dec_ffn_end():
        r.fo[...] = dot(r.act[...], r.w_down_v[...])
        layer_value(r.decoded, dec_gain)
        ffn_back_sum(r, r.w_up_v)
        ffn_backward_end(r, dec_gain, r.cotangent_v, r.dec_gains)
        got_ffn[:] = [moves.start(r.enc_up, r.w_up_v), moves.start(r.enc_down, r.w_down_v)]

    def dec_out():
        attention_backward_out(r, r.w_out_v, dec_gain, place.dec_out, r.dec_gains)

    def attention_pairs(first, last):
        return lambda: attention_backward_pairs(r, first, last)

    def dec_in(part):
        def run():
            attention_backward_in(r, place.dec_qkv[part], part)
            if part == 2:
                attention_backward_end(r, r.w_qkv_v, dec_gain, r.dec_gains)
                r.gquant[...] = r.gx[...].astype(BF16)

        return run

    def enc_project():
        wait(got_tokens)
        r.x[...] = r.tokens_v[...].astype(F32)
        wait(got_attention_two)
        attention_project(r, r.w_qkv_e, enc_gain)

    def enc_mix():
        attention_mix(r, r.w_out_e, enc_gain)

    def enc_ffn():
        wait(got_ffn)
        ffn_forward(r, r.w_up_v, r.w_down_v)
        layer_value(r.latent, enc_gain)

    def quantizer():
        wait(got_pin, PIN)
        quantizer_latent(r)
        if chunks:
            for other in reversed(range(1, levels)):
                target = sums.near_level(other)
                sums.arrived(CODES, other)
                sums.remote(r.g_rows.at[target_level(target)], r.g_got.at[other], target, BOOKS, 0, other)
            r.g_got[0] = r.g_rows[level]

    def book_half(core, put):
        quarter = entries // 4
        for side in range(2):
            r.book_sum[...] = jnp.zeros_like(r.book_sum)
            first = (core * 2 + side) * quarter

            def add(source, carry):
                one_hot = one_hot_rows(r.code_got[source, 0:1, :], first, quarter)
                r.book_sum[...] += dot(one_hot, r.g_got[source])
                return carry

            lax.fori_loop(0, levels, add, 0, unroll=4)
            put(side, r.book_sum[...])

    def finish_books(stage):
        blocks = entries // 4 // rows
        other_core, other_side = sums.partner[bits - 2], sums.partner[bits - 1]
        if stage == 0:
            for other in range(1, levels):
                sums.arrived(BOOKS, 0, other)

            def put(side, value):
                r.book_send[side] = value.astype(BF16)

            def keep(side, value):
                r.book_own[side * blocks : (side + 1) * blocks] = value.astype(BF16).reshape((blocks, rows, code_width))

            book_half(1 - mine, put)
            sums.remote(r.book_send, r.book_got, other_core, BOOKS, 1)
            book_half(mine, keep)
        elif stage == 1:
            sums.arrived(BOOKS, 1)
            for side in range(2):
                own = r.book_own[side * blocks : (side + 1) * blocks]
                r.book_got[side] = r.book_got[side] + own.reshape(r.book_got.shape[1:])
            sums.remote(r.book_got.at[1 - branch], r.book_last, other_side, BOOKS, 2)
        else:
            sums.arrived(BOOKS, 2)
            total = r.book_got[branch].astype(F32) + r.book_last[...].astype(F32)
            blocks = code_width // 128
            store_segment(r.packed, first_rows[BOOKS], Segment(BOOKS, 0, blocks, 0, blocks, 0, entries // 4), total)

    def all_books():
        parts = entries // TILE

        def one(step, carry):
            at = step // parts
            one_hot = one_hot_rows(r.code_rows[at, 0:1, :], step % parts * TILE, TILE)
            t.books[at, aligned(step % parts, TILE), :] = dot(one_hot, r.g_rows[at]).astype(BF16)
            return carry

        lax.fori_loop(0, levels * parts, one, 0)

    def enc_ffn_back(half):
        def run():
            first, last = half * tiles // 2, (half + 1) * tiles // 2
            if half == 0:
                ffn_backward_begin(r, enc_gain, r.gy)
            ffn_backward_tiles(r, r.w_down_v, place.enc_up[half], enc_down, first, last)
            if half == 1:
                ffn_back_sum(r, r.w_up_v)
                ffn_backward_end(r, enc_gain, r.gy, r.gains)

        return run

    def enc_out():
        attention_backward_out(r, r.w_out_e, enc_gain, place.enc_out, r.gains)

    def enc_in(part):
        def run():
            attention_backward_in(r, place.enc_qkv[part], part)
            if part == 2:
                attention_backward_end(r, r.w_qkv_e, enc_gain, r.gains)
                r.grad_tokens[...] = r.gx[...]
                if chunks:
                    spread_gains()

        return run

    def spread_gains():
        last, height = chunks[EA3], t.ea3.shape[1]
        for layer, ref in enumerate((r.gains, r.dec_gains)):
            for row in range(4):
                for block in range(width // 128):
                    owner = (layer * 4 + row) * (width // 128) + block
                    value = jnp.broadcast_to(ref[row : row + 1, block * 128 : (block + 1) * 128], (height, 128))
                    t.ea3[last.index(owner), :, width : width + 128] = value.astype(BF16)

    work = [
        (6.5, pick, ()),
        (2.0, semantic, (DISTILL_GRAD,)),
        (0.7, quant, ()),
        (1.5, dec_project, ()),
        (2.5, dec_mix, ()),
        (2.6, dec_ffn(0), (DU0,)),
        (2.0, dec_ffn(1), (DD0, DD1, DU1)),
        (0.7, dec_ffn_end, ()),
        (1.2, dec_out, ()),
        (1.6, attention_pairs(0, pairs // 2), ()),
        (1.6, attention_pairs(pairs // 2, pairs), ()),
        (0.6, dec_in(0), (DA0,)),
        (0.6, dec_in(1), (DA1,)),
        (0.8, dec_in(2), (DA2,)),
        (1.5, enc_project, ()),
        (2.5, enc_mix, ()),
        (2.2, enc_ffn, ()),
        (2.0, quantizer, (BOOKS, MISC)),
        (2.0, enc_ffn_back(0), (EU0,)),
        (2.0, enc_ffn_back(1), (EU1, ED0, ED1, ED2)),
        (1.2, enc_out, (EA0,)),
        (1.6, attention_pairs(0, pairs // 2), ()),
        (1.6, attention_pairs(pairs // 2, pairs), ()),
        (0.6, enc_in(0), (EA1,)),
        (0.6, enc_in(1), (EA2,)),
        (1.0, enc_in(2), (EA3,)),
    ]
    if not chunks:
        for _, run, _ in work:
            run()
            if run is quantizer:
                all_books()
        return
    actions = plan(chunks, work, bits, rows * code_width * 2)

    def finish(name, stage):
        if name == BOOKS:
            finish_books(stage)
        else:
            sums.finish(name, stage, r.recv[name][stage - 1] if stage else t[name])

    for (_, run, made), acts in zip(work, actions):
        run()
        for name in made:
            if name != BOOKS:
                sums.send_half(name, 0, t[name])
        for name, stage in acts:
            finish(name, stage)
    for name, stage in actions[-1]:
        finish(name, stage)
    sums.drain()


POUT, PIN, CODES = 1, 2, 3
DISTILL_GRAD = "di"
DD0, DD1, DU0, DU1, DA0, DA1, DA2, MISC = "dd0", "dd1", "du0", "du1", "da0", "da1", "da2", "misc"
EU0, EU1, ED0, ED1, ED2 = "eu0", "eu1", "ed0", "ed1", "ed2"
EA0, EA1, EA2, EA3 = "ea0", "ea1", "ea2", "ea3"


def step(given, devices, with_sums):
    rows, width = given.tokens.shape
    ff = given.enc_up.shape[1]
    levels, entries, code_width = given.books.shape
    given.books = given.books.reshape(levels, -1, rows, code_width)
    bits = devices.bit_length() - 1
    vmem, hbm = pl.BlockSpec(memory_space=pltpu.VMEM), pl.BlockSpec(memory_space=pl.ANY)
    scratch = layer_scratch(rows, width, ff)
    scratch.update(
        w_qkv_e=pltpu.VMEM((width, 3 * width), BF16),
        w_out_e=pltpu.VMEM((width, width), BF16),
        cos=pltpu.VMEM((rows, PAIR), F32),
        sin=pltpu.VMEM((rows, PAIR), F32),
        bias=pltpu.VMEM((rows, rows), F32),
        ring=pltpu.VMEM((4,) + given.books.shape[1:], BF16),
        code_rows=pltpu.VMEM((levels, 8, rows), jnp.int32),
        chosen=pltpu.VMEM((levels, rows, code_width), BF16),
        ac=pltpu.VMEM((rows, code_width), BF16),
        gquant=pltpu.VMEM((rows, width), BF16),
        gy=pltpu.VMEM((rows, width), F32),
        latent=pltpu.VMEM((rows, width), BF16),
        pin_v=pltpu.VMEM((2, width, code_width), BF16),
        pout_v=pltpu.VMEM((2, code_width, width), BF16),
        distill_v=pltpu.VMEM(given.distill.shape, BF16),
        wavlm_v=pltpu.VMEM((rows, given.wavlm.shape[1]), BF16),
        tokens_v=pltpu.VMEM((rows, width), BF16),
        cotangent_v=pltpu.VMEM((rows, width), BF16),
        sem_move=pltpu.SemaphoreType.DMA((14,)),
        sem_book=pltpu.SemaphoreType.DMA((4,)),
    )
    outs = Refs(decoded=shaped((rows, width), BF16), grad_tokens=shaped((rows, width), F32))
    chunks, first_rows = {}, {}
    params = dict(vmem_limit_bytes=60 * 2**20)
    if with_sums:
        params.update(collective_id=0, has_side_effects=True)
        c, x, y = bits - 2, bits - 1, bits - 3
        b, a = range(y)
        share = width // devices
        low, high = ff // devices, share
        wide, half, blocks = ff // 128, ff // 256, width // 128
        third, quarter = 3 * blocks, blocks // 4
        chunks = dict(
            di=Chunk(
                high,
                width,
                [c, y, x, a, b],
                [
                    Segment(8, 0, 2 * blocks, 0, blocks, 0, high // 2),
                    Segment(8, blocks, 2 * blocks, 0, blocks, high // 2, high // 2),
                ],
            ),
            du0=Chunk(high, ff // 2, [c, y, a, x, b], [Segment(2, 0, wide, 0, half, 0, high)]),
            dd0=Chunk(low, width // 2, [c, a, y, b, x], [Segment(3, 0, blocks, 0, 2 * quarter, 0, low)]),
            dd1=Chunk(low, width // 2, [c, y, x, a, b], [Segment(3, 2 * quarter, blocks, 0, 2 * quarter, 0, low)]),
            du1=Chunk(high, ff // 2, [c, x, y, a, b], [Segment(2, half, wide, 0, half, 0, high)]),
            da0=Chunk(
                high,
                2 * width,
                [c, x, y, a, b],
                [Segment(1, 0, blocks, 0, blocks, 0, high), Segment(0, 0, third, width, blocks, 0, high)],
            ),
            da1=Chunk(high, width, [c, a, x, y, b], [Segment(0, blocks, third, 0, blocks, 0, high)]),
            da2=Chunk(high, width, [c, y, x, a, b], [Segment(0, 2 * blocks, third, 0, blocks, 0, high)]),
            misc=Chunk(
                high,
                2 * width,
                [c, x, y, a, b],
                [
                    Segment(9, 0, blocks, 0, blocks, 0, high),
                    Segment(10, 0, blocks // 2, width, blocks // 2, 0, high),
                    Segment(10, high * blocks // 2, blocks // 2, width + code_width, blocks // 2, 0, high),
                ],
            ),
            eu0=Chunk(high, ff // 2, [c, x, a, y, b], [Segment(6, 0, wide, 0, half, 0, high)]),
            eu1=Chunk(high, ff // 2, [c, x, y, a, b], [Segment(6, half, wide, 0, half, 0, high)]),
            ed0=Chunk(low, width // 2, [c, x, y, a, b], [Segment(7, 0, blocks, 0, 2 * quarter, 0, low)]),
            ed1=Chunk(low, width // 4, [c, y, x, a, b], [Segment(7, 2 * quarter, blocks, 0, quarter, 0, low)]),
            ed2=Chunk(low, width // 4, [c, y, a, b, x], [Segment(7, 3 * quarter, blocks, 0, quarter, 0, low)]),
            ea0=Chunk(high, width, [c, x, y, a, b], [Segment(5, 0, blocks, 0, blocks, 0, high)]),
            ea1=Chunk(high, width, [c, y, x, a, b], [Segment(4, 0, third, 0, blocks, 0, high)]),
            ea2=Chunk(high, width, [c, x, a, y, b], [Segment(4, blocks, third, 0, blocks, 0, high)]),
            ea3=Chunk(
                high,
                width + 128,
                [c, x, y, a, b],
                [Segment(4, 2 * blocks, third, 0, blocks, 0, high), Segment(11, 0, 1, width, 1, 0, 8)],
            ),
        )
        rows_of = [high * 3 * blocks, high * blocks, high * wide, low * blocks] * 2
        rows_of += [high * blocks, high * blocks, high * blocks, 8, entries // 4 * code_width // 128]
        first_rows = {i: sum(rows_of[:i]) for i in range(len(rows_of))}
        first_rows[BOOKS] = first_rows[len(rows_of) - 1]
        copies = len(chunks) * bits + 2 * levels + 2
        scratch.update(
            t={name: pltpu.VMEM(c.shape(bits), BF16) for name, c in chunks.items()},
            recv={
                name: [pltpu.VMEM(c.shape(bits - 1 - stage), BF16) for stage in range(bits)]
                for name, c in chunks.items()
            },
            gains=pltpu.VMEM((4, width), F32),
            dec_gains=pltpu.VMEM((4, width), F32),
            code_got=pltpu.VMEM((levels, 8, rows), jnp.int32),
                book_sum=pltpu.VMEM((entries // 4, code_width), F32),
            book_send=pltpu.VMEM((2, entries // 4, code_width), BF16),
            book_got=pltpu.VMEM((2, entries // 4, code_width), BF16),
            book_last=pltpu.VMEM((entries // 4, code_width), BF16),
            send_sem=pltpu.SemaphoreType.DMA((copies,)),
            recv_sem=pltpu.SemaphoreType.DMA((copies,)),
        )
        outs.packed = shaped((sum(rows_of), 128), F32)
    else:
        outs.update(gains=shaped((4, width), F32), dec_gains=shaped((4, width), F32))
        outs.t = dict(
            enc_qkv=shaped(given.enc_qkv.shape, BF16),
            enc_out=shaped(given.enc_out.shape, BF16),
            enc_up=shaped(given.enc_up.shape, BF16),
            enc_down=shaped(given.enc_down.shape, BF16),
            dec_qkv=shaped(given.enc_qkv.shape, BF16),
            dec_out=shaped(given.enc_out.shape, BF16),
            dec_up=shaped(given.enc_up.shape, BF16),
            dec_down=shaped(given.enc_down.shape, BF16),
            pin=shaped((2 * width, code_width), BF16),
            pout=shaped((2 * code_width, width), BF16),
            books=shaped((levels, entries, code_width), BF16),
            distill=shaped(given.distill.shape, BF16),
        )
    in_specs = dict.fromkeys(given, hbm)
    in_specs.update(
        lengths=pl.BlockSpec(memory_space=pltpu.SMEM), codes=vmem, vectors=vmem
    )
    got = pl.pallas_call(
        functools.partial(step_kernel, chunks, first_rows, bits),
        out_shape={k: pltpu.VMEM(v.shape, v.dtype) for k, v in outs.items()} if with_sums else dict(outs),
        in_specs=[in_specs],
        out_specs=jax.tree.map(lambda _: vmem, dict(outs)),
        scratch_shapes=[dict(scratch)],
        compiler_params=pltpu.CompilerParams(**params),
        name="step",
    )(dict(given))
    got = Refs(got)
    if not with_sums:
        return got
    last = [shaped((rows, 128), F32) for rows in rows_of]
    last[11] = shaped((1, 128), F32)

    def hand_on(packed, decoded, grad, *refs):
        outs, moves = refs[:-1], Moves(refs[-1])
        parts = [packed.at[pl.ds(first_rows[i], ref.shape[0])] for i, ref in enumerate(outs[:-2])]
        leaving = [moves.start(part, ref) for part, ref in zip(parts + [decoded, grad], outs)]
        for move in leaving:
            move.wait()

    return pl.pallas_call(
        hand_on,
        out_shape=last + [outs.decoded, outs.grad_tokens],
        in_specs=[vmem] * 3,
        out_specs=[hbm] * (len(last) + 2),
        scratch_shapes=[pltpu.SemaphoreType.DMA((len(last) + 2,))],
        compiler_params=pltpu.CompilerParams(vmem_limit_bytes=16 * 2**20),
        name="results",
    )(got.packed, got.decoded, got.grad_tokens)


def body(
    tokens,
    wavlm,
    cotangent,
    lengths,
    codes,
    enc_qkv,
    enc_out,
    enc_up,
    enc_down,
    dec_qkv,
    dec_out,
    dec_up,
    dec_down,
    vectors,
    proj_in,
    proj_out,
    codebooks,
    distill_proj,
):
    width = tokens.shape[1]
    devices = lax.axis_size("dp") * lax.axis_size("branch")
    with_sums = devices == 4 * codebooks.shape[0] and width // devices % 16 == 0
    given = Refs(
        tokens=tokens,
        wavlm=wavlm,
        cotangent=cotangent,
        lengths=lengths,
        codes=codes.T,
        enc_qkv=enc_qkv,
        enc_out=enc_out,
        enc_up=enc_up,
        enc_down=enc_down,
        dec_qkv=dec_qkv,
        dec_out=dec_out,
        dec_up=dec_up,
        dec_down=dec_down,
        vectors=vectors,
        pin_own=proj_in,
        pout_own=proj_out,
        books=codebooks,
        distill=distill_proj,
    )
    if with_sums:
        *sums, decoded, grad_tokens = step(given, devices, True)
        sums = [part.reshape(-1) for part in sums]
        order = (4, 5, 6, 7, 0, 1, 2, 3, 11, 10, 9, 12, 8)
        return (decoded, grad_tokens, *[sums[i] for i in order])
    swap = [(0, 1), (1, 0)]
    given.pin_other = lax.ppermute(proj_in, "branch", swap)
    given.pout_other = lax.ppermute(proj_out, "branch", swap)
    s = step(given, devices, False)
    t = Refs(s.t)
    gains = jnp.concatenate([s.gains, s.dec_gains])
    local = [t.enc_qkv, t.enc_out, t.enc_up, t.enc_down, t.dec_qkv, t.dec_out, t.dec_up, t.dec_down]
    local += [gains, t.pin, t.pout, t.books, t.distill]
    sums = [
        lax.psum_scatter(part.astype(F32).reshape(-1), ("dp", "branch"), scatter_dimension=0, tiled=True)
        for part in local
    ]
    return (s.decoded, s.grad_tokens, *sums)


def solution(mesh):
    rows, whole = P(("dp", "branch"), None), P()
    placed = (rows, P("dp", None), rows, rows, P("dp", None)) + (whole,) * 9
    placed += (P("branch", None, None),) * 2 + (whole,) * 2
    return jax.shard_map(
        body,
        mesh=mesh,
        in_specs=placed,
        out_specs=(rows, rows) + (P(("dp", "branch")),) * 13,
        check_vma=False,
    )
```

```python
import functools
import math

import jax
import jax.numpy as jnp
from jax import lax
from jax.experimental import pallas as pl
from jax.experimental.pallas import tpu as pltpu
from jax.sharding import PartitionSpec as P

HEADS = 8
WINDOW = 250
EPS_NORM = 1e-05
EPS_COS = 1e-06
BETA = 0.25
DISTILL = 10.0
ROPE_BASE = 10000.0

MESH = pl.DeviceIdType.MESH
F32 = jnp.float32
BF16 = jnp.bfloat16
TILE = 512
PAIR = 128
HALF = 256


def dot(left, right):
    return lax.dot_general(left, right, (((1,), (0,)), ((), ())), preferred_element_type=F32)


def dot_t(left, right):
    return lax.dot_general(left, right, (((1,), (1,)), ((), ())), preferred_element_type=F32)


def t_dot(left, right):
    return lax.dot_general(left, right, (((0,), (0,)), ((), ())), preferred_element_type=F32)


def iota(shape, dim):
    return lax.broadcasted_iota(jnp.int32, shape, dim)


def aligned(index, size):
    return pl.ds(pl.multiple_of(index * size, size), size)


class Refs(dict):
    __getattr__ = dict.__getitem__
    __setattr__ = dict.__setitem__


class Moves:
    def __init__(self, semaphores):
        self.semaphores, self.count = semaphores, 0

    def start(self, source, target):
        move = pltpu.make_async_copy(source, target, self.semaphores.at[self.count])
        self.count += 1
        move.start()
        return move


def layer_scratch(rows, width, ff):
    return Refs(
        x=pltpu.VMEM((rows, width), F32),
        s1=pltpu.VMEM((rows, 1), F32),
        h=pltpu.VMEM((rows, width), BF16),
        h1t=pltpu.VMEM((width, rows), BF16),
        h2t=pltpu.VMEM((width, rows), BF16),
        rinv=pltpu.VMEM((rows, width), F32),
        qkv=pltpu.VMEM((rows, 3 * width), BF16),
        mix=pltpu.VMEM((rows, width), BF16),
        ao=pltpu.VMEM((rows, width), F32),
        x2=pltpu.VMEM((rows, width), F32),
        s2=pltpu.VMEM((rows, 1), F32),
        act=pltpu.VMEM((rows, ff), BF16),
        dg=pltpu.VMEM((rows, ff), BF16),
        fo=pltpu.VMEM((rows, width), F32),
        grad=pltpu.VMEM((rows, width), BF16),
        gx=pltpu.VMEM((rows, width), F32),
        acc=pltpu.VMEM((rows, width), F32),
        wide=pltpu.VMEM((4, rows, HALF), F32),
        change=pltpu.VMEM((2, rows, rows), BF16),
        w_qkv_v=pltpu.VMEM((width, 3 * width), BF16),
        w_out_v=pltpu.VMEM((width, width), BF16),
        w_up_v=pltpu.VMEM((width, ff), BF16),
        w_down_v=pltpu.VMEM((ff, width), BF16),
    )


def shaped(shape, kind):
    return jax.ShapeDtypeStruct(shape, kind)


def frame_tables(r):
    rows = r.cos.shape[0]
    place = iota((rows, PAIR), 0)
    query, key = iota((rows, rows), 0), iota((rows, rows), 1)
    begin, begin_query = jnp.zeros_like(place), jnp.zeros_like(query)
    edge = 0
    for clip in range(r.lengths.shape[1] - 1):
        edge = edge + r.lengths[0, clip]
        begin = jnp.where(place >= edge, edge, begin)
        begin_query = jnp.where(query >= edge, edge, begin_query)
    allowed = (key >= begin_query) & (key <= query) & (query - key < WINDOW)
    r.bias[...] = jnp.where(allowed, 0.0, -1e30)
    lane = iota((rows, PAIR), 1)
    rate = jnp.exp((lane % 32).astype(F32) * (-math.log(ROPE_BASE) / 32))
    angle = (place - begin).astype(F32) * rate
    r.cos[...] = jnp.cos(angle)
    sine = jnp.sin(angle)
    r.sin[...] = jnp.where(lane % 64 < 32, -sine, sine)


def rotated(value, cosine, sine):
    lane = iota(value.shape, 1)
    swapped = jnp.where(lane % 64 < 32, pltpu.roll(value, PAIR - 32, 1), pltpu.roll(value, 32, 1))
    return value * cosine + swapped * sine


def head_masks(rows):
    low = iota((rows, PAIR), 1) < 64
    return (jnp.where(low, 1.0, 0.0).astype(BF16), jnp.where(low, 0.0, 1.0).astype(BF16))


def row_blocks(rows, step):
    return [slice(i, i + step) for i in range(0, rows, step)]


def attention_project(r, w_qkv, gain):
    rows, width = r.x.shape
    scale = gain(0)
    for at in row_blocks(rows, 64):
        x = r.x[at, :]
        s1 = lax.rsqrt(jnp.mean(x * x, axis=1, keepdims=True) + EPS_NORM)
        r.s1[at, :] = s1
        r.h[at, :] = (x * s1 * scale).astype(BF16)
    for half in range(3 * width // HALF):
        slot, part = half % 4, half // (width // HALF)
        cols = slice(half * HALF, (half + 1) * HALF)
        r.wide[slot] = dot(r.h[...], w_qkv[:, cols])
        for at in row_blocks(rows, 64):
            for p in range(HALF // PAIR):
                value = r.wide[slot, at, p * PAIR : (p + 1) * PAIR]
                if part < 2:
                    value = rotated(value, r.cos[at, :], r.sin[at, :])
                low = value.astype(BF16)
                if part == 0:
                    low = (low.astype(F32) * 0.125).astype(BF16)
                r.qkv[at, half * HALF + p * PAIR : half * HALF + (p + 1) * PAIR] = low
    r.h1t[...] = r.h[...].T


def attention_mix(r, w_out, gain):
    rows, width = r.x.shape
    masks = head_masks(rows)
    low = iota((rows, PAIR), 1) < 64
    pairs = width // PAIR
    for p in range(pairs):
        query = r.qkv[:, p * PAIR : (p + 1) * PAIR]
        key = r.qkv[:, (p + pairs) * PAIR : (p + pairs + 1) * PAIR]
        value = r.qkv[:, (p + 2 * pairs) * PAIR : (p + 2 * pairs + 1) * PAIR]
        outs = []
        for h in range(2):
            head = 2 * p + h
            slot = head % 4
            r.wide[slot] = dot_t(query * masks[h], key)
            for at in row_blocks(rows, 64):
                seen = PAIR if at.stop <= PAIR else rows
                scores = r.wide[slot, at, :seen] + r.bias[at, :seen]
                weights = jnp.exp(scores - jnp.max(scores, axis=1, keepdims=True))
                r.att[head, at, :seen] = weights.astype(BF16)
                if seen < rows:
                    r.att[head, at, seen:] = jnp.zeros((64, rows - seen), BF16)
            outs.append(dot(r.att[head], value * masks[h] + masks[1 - h]))
        inverse = 1.0 / pltpu.roll(jnp.where(low, outs[1], outs[0]), 64, 1)
        r.rinv[:, p * PAIR : (p + 1) * PAIR] = inverse
        r.mix[:, p * PAIR : (p + 1) * PAIR] = (jnp.where(low, outs[0], outs[1]) * inverse).astype(BF16)
    r.ao[...] = dot(r.mix[...], w_out[...])
    scale_one, scale_two = gain(1), gain(2)
    for at in row_blocks(rows, 64):
        x2 = r.x[at, :] + scale_one * r.ao[at, :]
        r.x2[at, :] = x2
        s2 = lax.rsqrt(jnp.mean(x2 * x2, axis=1, keepdims=True) + EPS_NORM)
        r.s2[at, :] = s2
        r.h[at, :] = (x2 * s2 * scale_two).astype(BF16)
    r.h2t[...] = r.h[...].T


def gelu_parts(pre):
    slope = math.sqrt(2.0 / math.pi)
    square = pre * pre
    bent = jnp.tanh(slope * pre * (1.0 + 0.044715 * square))
    half = 0.5 * (1.0 + bent)
    turn = 0.5 * pre * (1.0 - bent * bent) * slope * (1.0 + 3.0 * 0.044715 * square)
    return (pre * half).astype(BF16), half + turn


def ffn_forward(r, w_up, w_down):
    rows, ff = r.act.shape
    for half in range(ff // HALF):
        slot, cols = half % 4, slice(half * HALF, (half + 1) * HALF)
        r.wide[slot] = dot(r.h[...], w_up[:, cols])
        for at in row_blocks(rows, 32):
            act, slope = gelu_parts(r.wide[slot, at, :])
            r.act[at, cols] = act
            r.dg[at, cols] = slope.astype(BF16)
    r.fo[...] = dot(r.act[...], w_down[...])


def ffn_both(r, w_up, w_down, grad_up, grad_down, first, last):
    rows = r.act.shape[0]
    for t in range(first, last):
        cols = slice(t * TILE, (t + 1) * TILE)
        for side in range(TILE // HALF):
            part = slice(t * TILE + side * HALF, t * TILE + (side + 1) * HALF)
            r.wide[side] = dot(r.h[...], w_up[:, part])
            r.wide[2 + side] = dot_t(r.grad[...], w_down[part, :])
            for at in row_blocks(rows, 32):
                act, slope = gelu_parts(r.wide[side, at, :])
                r.act[at, part] = act
                r.dg[at, part] = (r.wide[2 + side, at, :] * slope).astype(BF16)
        grad_up.shift((t - first) * TILE).put(dot(r.h2t[...], r.dg[:, cols]))
        put_rows(grad_down, t_dot(r.act[:, cols], r.grad[...]), t)


def ffn_back_sum(r, w_up):
    r.acc[...] = dot_t(r.dg[...], w_up[...])


def norm_back(stream, inverse, grad):
    mean = jnp.mean(grad * stream, axis=1, keepdims=True)
    return inverse * grad - stream * (inverse * inverse * inverse * mean)


def column_sum(value):
    return jnp.sum(value, axis=0, keepdims=True)


class Place:
    def __init__(self, ref, col=0, chunk=None):
        self.ref, self.col, self.chunk = ref, col, chunk

    def shift(self, by):
        return Place(self.ref, self.col + by, self.chunk)

    def put(self, value):
        value = value.astype(BF16)
        cols = slice(self.col, self.col + value.shape[1])
        if self.chunk is None:
            self.ref[:, cols] = value
            return
        blocks, rows = self.ref.shape[:2]
        for owner in range(blocks):
            self.ref[self.chunk.index(owner), :, cols] = value[owner * rows : (owner + 1) * rows]


def put_rows(places, value, tile):
    value = value.astype(BF16)
    begin = 0
    for place in places:
        part = value[:, begin : begin + place.ref.shape[-1]]
        begin += place.ref.shape[-1]
        if place.chunk is None:
            place.ref[tile * TILE : tile * TILE + TILE, :] = part
            continue
        rows = place.ref.shape[1]
        for i in range(TILE // rows):
            place.ref[place.chunk.index(tile * (TILE // rows) + i)] = part[i * rows : (i + 1) * rows]


def ffn_backward_begin(r, gain, gy_ref):
    scale = gain(3)
    for at in row_blocks(r.grad.shape[0], 64):
        r.grad[at, :] = (scale * gy_ref[at, :].astype(F32)).astype(BF16)


def ffn_backward_tiles(r, w_down, grad_up, grad_down, first, last):
    rows = r.act.shape[0]
    for t in range(first, last):
        cols = slice(t * TILE, (t + 1) * TILE)
        for side in range(TILE // HALF):
            part = slice(t * TILE + side * HALF, t * TILE + (side + 1) * HALF)
            slot = (2 * t + side) % 4
            r.wide[slot] = dot_t(r.grad[...], w_down[part, :])
            for at in row_blocks(rows, 64):
                r.dg[at, part] = (r.wide[slot, at, :] * r.dg[at, part].astype(F32)).astype(BF16)
        put_rows(grad_down, t_dot(r.act[:, cols], r.grad[...]), t)
        grad_up.shift((t - first) * TILE).put(dot(r.h2t[...], r.dg[:, cols]))


def ffn_backward_end(r, gain, gy_ref, gain_out):
    scale = gain(2)
    to_gain = to_scale = 0.0
    for at in row_blocks(r.x2.shape[0], 32):
        gy = gy_ref[at, :].astype(F32)
        to_scale = to_scale + column_sum(gy * r.fo[at, :])
        back, x2, s2 = r.acc[at, :], r.x2[at, :], r.s2[at, :]
        to_gain = to_gain + column_sum(back * x2 * s2)
        r.gx[at, :] = gy + norm_back(x2, s2, back * scale)
    gain_out[3:4, :] = to_scale
    gain_out[2:3, :] = to_gain


def attention_backward_out(r, w_out, gain, grad_out, gain_out):
    scale = gain(1)
    to_scale = 0.0
    for at in row_blocks(r.gx.shape[0], 64):
        gx = r.gx[at, :]
        to_scale = to_scale + column_sum(gx * r.ao[at, :])
        r.grad[at, :] = (scale * gx).astype(BF16)
    gain_out[1:2, :] = to_scale
    grad_out.put(t_dot(r.mix[...], r.grad[...]))
    r.grad[...] = dot_t(r.grad[...], w_out[...]).astype(BF16)


def attention_backward_pairs(r, first, last):
    rows, width = r.x.shape
    masks = head_masks(rows)
    masks_t = [jnp.where((iota((PAIR, rows), 0) < 64) == (h == 0), 1.0, 0.0).astype(BF16) for h in range(2)]
    pairs = width // PAIR
    for p in range(first, last):
        lanes = [slice((p + i * pairs) * PAIR, (p + i * pairs + 1) * PAIR) for i in range(3)]
        query, key, value = (r.qkv[:, at] for at in lanes)
        grad_mixed = (r.grad[:, lanes[0]].astype(F32) * r.rinv[:, lanes[0]]).astype(BF16)
        product = (grad_mixed.astype(F32) * r.mix[:, lanes[0]].astype(F32)).astype(BF16)
        beside = jnp.concatenate([value, jnp.full(value.shape, -1.0, BF16)], axis=1)
        query_t, grad_t = query.T, grad_mixed.T
        to_query = to_key = to_value = 0.0
        for h in range(2):
            head = 2 * p + h
            slot = head % 4
            both = jnp.concatenate([grad_mixed * masks[h], product * masks[h]], axis=1)
            r.wide[slot] = dot_t(both, beside)
            for at in row_blocks(rows, 64):
                r.change[h, at, :] = (r.att[head, at, :].astype(F32) * r.wide[slot, at, :]).astype(BF16)
            to_query = to_query + dot(r.change[h], key * masks[h])
            to_key = to_key + dot(query_t * masks_t[h], r.change[h])
            to_value = to_value + dot(grad_t * masks_t[h], r.att[head])
        cosine, sine = r.cos[...], -r.sin[...]
        r.qkv[:, lanes[0]] = rotated(to_query * 0.125, cosine, sine).astype(BF16)
        r.qkv[:, lanes[1]] = rotated(to_key.T, cosine, sine).astype(BF16)
        r.qkv[:, lanes[2]] = to_value.T.astype(BF16)


def attention_backward_in(r, grad_qkv, part):
    width = r.x.shape[1]
    grad_qkv.put(dot(r.h1t[...], r.qkv[:, part * width : (part + 1) * width]))


def attention_backward_end(r, w_qkv, gain, gain_out):
    r.acc[...] = dot_t(r.qkv[...], w_qkv[...])
    scale = gain(0)
    to_gain = 0.0
    for at in row_blocks(r.x.shape[0], 32):
        back, x, s1 = r.acc[at, :], r.x[at, :], r.s1[at, :]
        to_gain = to_gain + column_sum(back * x * s1)
        r.gx[at, :] = r.gx[at, :] + norm_back(x, s1, back * scale)
    gain_out[0:1, :] = to_gain


class Segment:
    def __init__(self, result, base, stride, col, blocks, row, rows):
        self.result, self.base, self.stride, self.col, self.blocks = result, base, stride, col, blocks
        self.row, self.rows = row, rows


class Chunk:
    def __init__(self, rows, columns, order, segments):
        self.rows, self.columns, self.order, self.segments = rows, columns, order, segments

    def index(self, owner):
        bits = len(self.order)
        return sum((owner >> (bits - 1 - dim) & 1) << (bits - 1 - stage) for stage, dim in enumerate(self.order))

    def shape(self, leading):
        return (2**leading, self.rows, self.columns)

    def bytes(self, bits):
        return 2**bits * self.rows * self.columns * 2


def plan(chunks, work, bits, book_bytes):
    core, x, y = bits - 2, bits - 1, bits - 3
    ends, middle = -1, -2
    free, pending, done = {}, [], []
    now = 0.0

    def carry(link, size, rate=42e3):
        free[link] = max(now, free.get(link, 0.0)) + size / rate
        return free[link]

    def begin(name, stage):
        if name == BOOKS:
            size = 1.2 * 2 ** (bits - 3) * book_bytes
            if stage == 0:
                there = max(carry(y, size), carry(ends, 1.5 * size), carry(middle, 2 * size))
            else:
                there = carry(core, 4 * book_bytes, 400e3) if stage == 1 else carry(x, 2 * book_bytes)
        else:
            dim = chunks[name].order[stage]
            size = chunks[name].bytes(bits) / 2 ** (stage + 1)
            if dim == core:
                there = carry(core, size, 400e3)
            elif dim == x or dim == y:
                there = carry(dim, size)
            else:
                there = carry(ends, size)
                if dim < y - 1:
                    there = max(there, carry(middle, 2 * size))
        pending.append((there + 1.5, name, stage))

    def finish(limit):
        nonlocal now
        acts = []
        while pending:
            pending.sort(key=lambda p: p[0])
            if pending[0][0] + (0.5 if limit < math.inf else 0.0) > limit:
                break
            at, name, stage = pending.pop(0)
            if name == BOOKS:
                cost = (6.0, 0.6, 0.3)[stage]
            else:
                cost = 0.25 + 0.3e-6 * chunks[name].bytes(bits) / 2 ** (stage + 1)
            now = max(now, at) + cost
            limit = max(limit, now)
            acts.append((name, stage))
            if stage + 1 < (3 if name == BOOKS else bits):
                begin(name, stage + 1)
        return acts

    for took, _, names in work:
        now += 0.95 * took
        for name in names:
            begin(name, 0)
        done.append(finish(now))
    done.append(finish(math.inf))
    return done


def store_segment(packed, first, segment, value):
    for i in range(segment.blocks):
        where = pl.ds(first + segment.base + i, segment.rows, stride=segment.stride)
        packed[where, :] = value[
            segment.row : segment.row + segment.rows, segment.col + i * 128 : segment.col + (i + 1) * 128
        ]


class Halving:
    def __init__(self, chunks, bits, recv, packed, first, send_sem, recv_sem):
        self.chunks = chunks
        self.bits, self.recv, self.packed, self.first = bits, recv, packed, first
        self.send_sem, self.recv_sem = send_sem, recv_sem
        self.copies = {}
        dp, branch = lax.axis_index("dp"), lax.axis_index("branch")
        self.mine, self.partner = [], []
        for dim in range(bits - 1):
            weight = 2 ** (bits - 2 - dim)
            bit = dp // weight % 2
            self.mine.append(bit)
            self.partner.append({"dp": dp + weight * (1 - 2 * bit), "branch": branch})
        self.mine.append(branch)
        self.partner.append({"dp": dp, "branch": 1 - branch})

    def near_level(self, other):
        dp = lax.axis_index("dp")
        for i in range(self.bits - 2):
            if other >> i & 1:
                dp = dp + 2 ** (i + 1) * (1 - 2 * self.mine[self.bits - 3 - i])
        return {"dp": dp, "branch": lax.axis_index("branch")}

    def barrier(self):
        semaphore = pltpu.get_barrier_semaphore()
        levels = 2 ** (self.bits - 2)
        targets = self.partner[self.bits - 2 :] + [self.near_level(other) for other in range(1, levels)]
        for target in targets:
            pl.semaphore_signal(semaphore, inc=1, device_id=target, device_id_type=MESH)
        return lambda: pl.semaphore_wait(semaphore, len(targets))

    def half(self, ref, name, stage, other):
        mine = self.mine[self.chunks[name].order[stage]]
        count = 2 ** (self.bits - 1 - stage)
        return ref.at[pl.ds((1 - mine if other else mine) * count, count)]

    def remote(self, source, target, device, *key):
        slot = len(self.copies)
        self.copies[key] = pltpu.make_async_remote_copy(
            src_ref=source,
            dst_ref=target,
            send_sem=self.send_sem.at[slot],
            recv_sem=self.recv_sem.at[slot],
            device_id=device,
            device_id_type=MESH,
        )
        self.copies[key].start()

    def send(self, name, stage, source):
        dim = self.chunks[name].order[stage]
        self.remote(source, self.recv[name][stage], self.partner[dim], name, stage)

    def send_half(self, name, stage, ref):
        self.send(name, stage, self.half(ref, name, stage, True))

    def arrived(self, *key):
        self.copies[key].wait_recv()

    def add(self, name, stage, own):
        chunk = self.chunks[name]
        got = self.recv[name][stage]
        if stage == self.bits - 1:
            value = own[0].astype(F32) + got[0].astype(F32)
            for segment in chunk.segments:
                store_segment(self.packed, self.first[segment.result], segment, value)
            return
        count = 2 ** (self.bits - 1 - stage)
        step = min(count, 4)

        def some(i, carry):
            at = pl.ds(i * step, step)
            got[at] = got[at] + own[at]
            return carry

        lax.fori_loop(0, count // step, some, 0)

    def finish(self, name, stage, before):
        self.arrived(name, stage)
        self.add(name, stage, self.half(before, name, stage, False))
        if stage + 1 < self.bits:
            self.send_half(name, stage + 1, self.recv[name][stage])

    def drain(self):
        for copy in self.copies.values():
            copy.wait_send()


BOOKS = "books"


def quantizer_semantic(r):
    sem_code = r.chosen[0]
    rows, code_width = sem_code.shape
    columns = [slice(i * HALF, (i + 1) * HALF) for i in range(r.distill_v.shape[1] // HALF)]
    for i, cols in enumerate(columns):
        r.wide[i] = dot(sem_code, r.distill_v[:, cols])

    def row_sum(parts):
        return jnp.sum(sum(parts), axis=1, keepdims=True)

    for at in row_blocks(rows, 32):
        prediction = [r.wide[i, at, :] for i in range(len(columns))]
        target = [r.wavlm_v[at, cols].astype(F32) for cols in columns]
        pred_norm = lax.rsqrt(row_sum([p * p for p in prediction]) + EPS_COS)
        target_norm = lax.rsqrt(row_sum([w * w for w in target]) + EPS_COS)
        cosine = row_sum([p * w for p, w in zip(prediction, target)]) * (pred_norm * target_norm)
        from_target = -DISTILL * pred_norm * target_norm
        from_prediction = DISTILL * cosine * pred_norm * pred_norm
        for p, w, cols in zip(prediction, target, columns):
            r.act[at, cols] = (w * from_target + p * from_prediction).astype(BF16)
    grad_pred = r.act[:, : r.distill_v.shape[1]]
    put_distill(r.places.distill, dot(sem_code.T, grad_pred))
    r.gy[:, :code_width] = dot_t(grad_pred, r.distill_v[...])


def quantizer_latent(r):
    levels, rows, code_width = r.chosen.shape
    latent_t = r.latent[...].T
    r.wide[0] = dot_t(r.gquant[...], r.pout_v[0])
    r.wide[1] = dot(r.latent[...], r.pin_v[0])
    r.wide[2] = dot_t(r.gquant[...], r.pout_v[1])
    r.wide[3] = dot(r.latent[...], r.pin_v[1])
    put_group(r.places.pout, 0, t_dot(r.chosen[0], r.gquant[...]))
    put_group(r.places.pout, 1, t_dot(r.ac[...], r.gquant[...]))
    for at in row_blocks(rows, 32):
        grad_sem = r.wide[0, at, :] + r.gy[at, :code_width]
        commit = 2.0 * BETA * (r.wide[1, at, :] - r.chosen[0, at, :].astype(F32))
        r.g_rows[0, at, :] = (grad_sem - commit).astype(BF16)
        r.grad[at, :code_width] = (grad_sem + commit).astype(BF16)
        grad_ac, residual = r.wide[2, at, :], r.wide[3, at, :]
        for level in range(1, levels):
            residual = residual - r.chosen[level, at, :].astype(F32)
        carry = jnp.zeros_like(residual)
        for level in range(levels - 1, 0, -1):
            carry = carry + 2.0 * BETA * residual
            r.g_rows[level, at, :] = (grad_ac - carry).astype(BF16)
            residual = residual + r.chosen[level, at, :].astype(F32)
        r.grad[at, code_width:] = (grad_ac + carry).astype(BF16)
    put_group(r.places.pin, 0, dot(latent_t, r.grad[:, :code_width]))
    put_group(r.places.pin, 1, dot(latent_t, r.grad[:, code_width:]))
    r.gy[...] = dot_t(r.grad[...], jnp.concatenate([r.pin_v[0], r.pin_v[1]], axis=1))


def put_group(place, group, value):
    target, total = place.ref, value.shape[0]
    value = value.astype(BF16)
    if place.chunk is None:
        target[group * total : (group + 1) * total, :] = value
        return
    blocks, height, columns = target.shape[0] // 2, target.shape[1], value.shape[1]
    for i in range(blocks):
        for part in range(total // blocks // height):
            first = i * (total // blocks) + part * height
            cols = slice(place.col + part * columns, place.col + (part + 1) * columns)
            target[place.chunk.index(group * blocks + i), :, cols] = value[first : first + height]


def put_distill(place, value):
    target = place.ref
    if place.chunk is None:
        target[...] = value.astype(BF16)
        return
    blocks, height = target.shape[:2]
    rows = value.shape[0] // blocks
    columns = value.shape[1] * rows // height
    for i in range(blocks):
        part = value[i * rows : (i + 1) * rows]
        part = jnp.concatenate([part[:, at : at + columns] for at in range(0, value.shape[1], columns)], axis=0)
        target[place.chunk.index(i), :, place.col : place.col + columns] = part.astype(BF16)


def one_hot_rows(codes, first, count):
    row = iota((count, codes.shape[1]), 0)
    return jnp.where(codes - first == row, 1.0, 0.0).astype(BF16)


def pick_codes(r):
    levels, _, entries, code_width = r.books.shape
    entries = entries * r.books.shape[1]
    rows = r.cos.shape[0]
    slots = r.ring.shape[0]
    branch = lax.axis_index("branch")
    own = r.codes[:, pl.ds(pl.multiple_of(branch * rows, rows), rows)]
    r.code_rows[...] = jnp.broadcast_to(own[:, None, :], r.code_rows.shape)
    columns = jnp.concatenate([own.astype(F32), jnp.zeros((PAIR - levels, rows), F32)], axis=0).T
    lane = iota(columns.shape, 1)
    entry = iota((rows, entries), 1)
    r.code_cols[...] = columns
    r.ac_sum[...] = jnp.zeros(r.ac_sum.shape, F32)

    def book(level):
        slot = level % slots
        return pltpu.make_async_copy(r.books.at[level], r.ring.at[slot], r.sem_book.at[slot])

    def pick(level, carry):
        code = jnp.sum(jnp.where(lane == level, r.code_cols[...], 0.0), axis=1, keepdims=True)
        one_hot = jnp.where(entry == code.astype(jnp.int32), 1.0, 0.0).astype(BF16)
        book(level).wait()
        got = dot(one_hot, r.ring[level % slots].reshape(entries, code_width))
        r.chosen[level] = got.astype(BF16)
        r.ac_sum[...] += jnp.where(level > 0, got, 0.0)

        @pl.when(level + slots < levels)
        def _():
            book(level + slots).start()

        return carry

    def begin():
        for level in range(slots):
            book(level).start()

    def run():
        lax.fori_loop(0, levels, pick, 0, unroll=4)
        r.ac[...] = r.ac_sum[...].astype(BF16)

    return begin, run


def step_kernel(chunks, first_rows, bits, ins, outs, scratch):
    r = Refs({**ins, **outs, **scratch})
    t = r.t = Refs(r.t)
    r.att, r.g_rows, r.g_got, r.book_own = (r.ring.at[i] for i in range(4))
    r.ac_sum, r.code_cols = r.acc.at[:, : r.ac.shape[1]], r.gx.at[:, :PAIR]
    branch = lax.axis_index("branch")
    rows, width = r.tokens.shape
    levels, parts, entries, code_width = r.books.shape
    entries = entries * parts
    tiles = r.w_up_v.shape[1] // TILE
    pairs = width // PAIR
    if chunks:
        sums = Halving(chunks, bits, r.recv, r.packed, first_rows, r.send_sem, r.recv_sem)
        mine, level = sums.mine[bits - 2], lax.axis_index("dp") // 2
        wait_barrier = sums.barrier()
    moves = Moves(r.sem_move)
    begin_pick, run_pick = pick_codes(r)
    begin_pick()
    got_pout = [moves.start(r.pout_own.at[0], r.pout_v.at[branch])]
    if chunks:
        wait_barrier()
        sums.remote(r.pout_own.at[0], r.pout_v.at[branch], sums.partner[bits - 1], POUT)
    else:
        got_pout.append(moves.start(r.pout_other.at[0], r.pout_v.at[1 - branch]))
    got_rest = [
        moves.start(r.distill, r.distill_v),
        moves.start(r.wavlm.at[pl.ds(pl.multiple_of(branch * rows, rows), rows)], r.wavlm_v),
    ]
    got_attention, got_ffn, got_cotangent, got_pin, got_tokens, got_attention_two = ([] for _ in range(6))
    frame_tables(r)

    def fetch_rest():
        got_attention.extend([moves.start(r.dec_qkv, r.w_qkv_v), moves.start(r.dec_out, r.w_out_v)])
        got_ffn.extend([moves.start(r.dec_up, r.w_up_v), moves.start(r.dec_down, r.w_down_v)])
        got_cotangent.append(moves.start(r.cotangent, r.cotangent_v))
        got_pin.append(moves.start(r.pin_own.at[0], r.pin_v.at[branch]))
        if not chunks:
            got_pin.append(moves.start(r.pin_other.at[0], r.pin_v.at[1 - branch]))
        got_tokens.append(moves.start(r.tokens, r.tokens_v))
        got_attention_two.extend([moves.start(r.enc_qkv, r.w_qkv_e), moves.start(r.enc_out, r.w_out_e)])

    if chunks:
        def at(name, col=0):
            return Place(t[name], col, chunks[name])

        dec_down, enc_down = [at(DD0), at(DD1)], [at(ED0), at(ED1), at(ED2)]
        place = r.places = Refs(
            dec_up=[at(DU0), at(DU1)],
            dec_out=at(DA0),
            dec_qkv=[at(DA0, width), at(DA1), at(DA2)],
            enc_up=[at(EU0), at(EU1)],
            enc_out=at(EA0),
            enc_qkv=[at(EA1), at(EA2), at(EA3)],
            distill=at(DISTILL_GRAD),
            pout=at(MISC),
            pin=at(MISC, width),
        )
    else:
        dec_down, enc_down = [Place(t.dec_down)], [Place(t.enc_down)]
        place = r.places = Refs(
            dec_up=[Place(t.dec_up, i * tiles // 2 * TILE) for i in range(2)],
            dec_out=Place(t.dec_out),
            dec_qkv=[Place(t.dec_qkv, i * width) for i in range(3)],
            enc_up=[Place(t.enc_up, i * tiles // 2 * TILE) for i in range(2)],
            enc_out=Place(t.enc_out),
            enc_qkv=[Place(t.enc_qkv, i * width) for i in range(3)],
            distill=Place(t.distill),
            pout=Place(t.pout),
            pin=Place(t.pin),
        )

    def core_rows(ref):
        half = ref.shape[0] // 2
        return ref.at[pl.ds(pl.multiple_of(mine * half, half), half)]

    def wait(moves, *other):
        for move in moves:
            move.wait()
        if chunks and other:
            sums.arrived(*other)

    def layer_value(target, gain):
        for at in row_blocks(rows, 64):
            target[at, :] = (r.x2[at, :] + gain(3) * r.fo[at, :]).astype(BF16)

    def dec_gain(i):
        return r.vectors[1, i : i + 1, :]

    def enc_gain(i):
        return r.vectors[0, i : i + 1, :]

    def pick():
        run_pick()
        fetch_rest()

    def semantic():
        wait(got_rest)
        quantizer_semantic(r)

    def quant():
        wait(got_pout, POUT)
        if chunks:
            sums.remote(core_rows(r.pin_own.at[0]), core_rows(r.pin_v.at[branch]), sums.partner[bits - 1], PIN)
        r.x[...] = dot(jnp.concatenate([r.chosen[0], r.ac[...]], axis=1), r.pout_v[...].reshape(-1, width))
        if chunks:
            for other in range(1, levels):
                target = sums.near_level(other)
                sums.remote(r.code_rows.at[target_level(target)], r.code_got.at[other], target, CODES, other)
            r.code_got[0] = r.code_rows[level]

    def target_level(target):
        return next(iter(target.values())) // 2

    def dec_project():
        wait(got_attention)
        attention_project(r, r.w_qkv_v, dec_gain)

    def dec_mix():
        attention_mix(r, r.w_out_v, dec_gain)

    def dec_ffn(half):
        def run():
            if half == 0:
                wait(got_ffn)
                wait(got_cotangent)
                ffn_backward_begin(r, dec_gain, r.cotangent_v)
            first, last = half * tiles // 2, (half + 1) * tiles // 2
            ffn_both(r, r.w_up_v, r.w_down_v, place.dec_up[half], dec_down, first, last)

        return run

    def dec_ffn_end():
        r.fo[...] = dot(r.act[...], r.w_down_v[...])
        layer_value(r.decoded, dec_gain)
        ffn_back_sum(r, r.w_up_v)
        ffn_backward_end(r, dec_gain, r.cotangent_v, r.dec_gains)
        got_ffn[:] = [moves.start(r.enc_up, r.w_up_v), moves.start(r.enc_down, r.w_down_v)]

    def dec_out():
        if chunks:
            sums.arrived(PIN)
            there = core_rows(r.pin_v.at[1 - branch])
            sums.remote(there, there, sums.partner[bits - 2], PIN, 1)
        attention_backward_out(r, r.w_out_v, dec_gain, place.dec_out, r.dec_gains)

    def attention_pairs(first, last):
        return lambda: attention_backward_pairs(r, first, last)

    def dec_in(part):
        def run():
            attention_backward_in(r, place.dec_qkv[part], part)
            if part == 2:
                attention_backward_end(r, r.w_qkv_v, dec_gain, r.dec_gains)
                r.gquant[...] = r.gx[...].astype(BF16)

        return run

    def enc_project():
        wait(got_tokens)
        r.x[...] = r.tokens_v[...].astype(F32)
        wait(got_attention_two)
        attention_project(r, r.w_qkv_e, enc_gain)

    def enc_mix():
        attention_mix(r, r.w_out_e, enc_gain)

    def enc_ffn():
        wait(got_ffn)
        ffn_forward(r, r.w_up_v, r.w_down_v)
        layer_value(r.latent, enc_gain)

    def quantizer():
        wait(got_pin, PIN, 1)
        quantizer_latent(r)
        if chunks:
            for other in reversed(range(1, levels)):
                target = sums.near_level(other)
                sums.arrived(CODES, other)
                sums.remote(r.g_rows.at[target_level(target)], r.g_got.at[other], target, BOOKS, 0, other)
            r.g_got[0] = r.g_rows[level]

    def book_half(core, put):
        quarter = entries // 4
        for side in range(2):
            r.book_sum[...] = jnp.zeros_like(r.book_sum)
            first = (core * 2 + side) * quarter

            def add(source, carry):
                one_hot = one_hot_rows(r.code_got[source, 0:1, :], first, quarter)
                r.book_sum[...] += dot(one_hot, r.g_got[source])
                return carry

            lax.fori_loop(0, levels, add, 0, unroll=4)
            put(side, r.book_sum[...])

    def finish_books(stage):
        blocks = entries // 4 // rows
        other_core, other_side = sums.partner[bits - 2], sums.partner[bits - 1]
        if stage == 0:
            for other in range(1, levels):
                sums.arrived(BOOKS, 0, other)

            def put(side, value):
                r.book_send[side] = value.astype(BF16)

            def keep(side, value):
                r.book_own[side * blocks : (side + 1) * blocks] = value.astype(BF16).reshape((blocks, rows, code_width))

            book_half(1 - mine, put)
            sums.remote(r.book_send, r.book_got, other_core, BOOKS, 1)
            book_half(mine, keep)
        elif stage == 1:
            sums.arrived(BOOKS, 1)
            for side in range(2):
                own = r.book_own[side * blocks : (side + 1) * blocks]
                r.book_got[side] = r.book_got[side] + own.reshape(r.book_got.shape[1:])
            sums.remote(r.book_got.at[1 - branch], r.book_last, other_side, BOOKS, 2)
        else:
            sums.arrived(BOOKS, 2)
            total = r.book_got[branch].astype(F32) + r.book_last[...].astype(F32)
            blocks = code_width // 128
            store_segment(r.packed, first_rows[BOOKS], Segment(BOOKS, 0, blocks, 0, blocks, 0, entries // 4), total)

    def all_books():
        parts = entries // TILE

        def one(step, carry):
            at = step // parts
            one_hot = one_hot_rows(r.code_rows[at, 0:1, :], step % parts * TILE, TILE)
            t.books[at, aligned(step % parts, TILE), :] = dot(one_hot, r.g_rows[at]).astype(BF16)
            return carry

        lax.fori_loop(0, levels * parts, one, 0)

    def enc_ffn_back(half):
        def run():
            first, last = half * tiles // 2, (half + 1) * tiles // 2
            if half == 0:
                ffn_backward_begin(r, enc_gain, r.gy)
            ffn_backward_tiles(r, r.w_down_v, place.enc_up[half], enc_down, first, last)

        return run

    def enc_ffn_back_end():
        ffn_back_sum(r, r.w_up_v)
        ffn_backward_end(r, enc_gain, r.gy, r.gains)

    def enc_out():
        attention_backward_out(r, r.w_out_e, enc_gain, place.enc_out, r.gains)

    def enc_in(part):
        def run():
            attention_backward_in(r, place.enc_qkv[part], part)
            if part == 2:
                attention_backward_end(r, r.w_qkv_e, enc_gain, r.gains)
                r.grad_tokens[...] = r.gx[...]
                if chunks:
                    spread_gains()

        return run

    def spread_gains():
        last, height = chunks[EA3], t.ea3.shape[1]
        for layer, ref in enumerate((r.gains, r.dec_gains)):
            for row in range(4):
                for block in range(width // 128):
                    owner = (layer * 4 + row) * (width // 128) + block
                    value = jnp.broadcast_to(ref[row : row + 1, block * 128 : (block + 1) * 128], (height, 128))
                    t.ea3[last.index(owner), :, width : width + 128] = value.astype(BF16)

    work = [
        (6.5, pick, ()),
        (2.0, semantic, (DISTILL_GRAD,)),
        (0.7, quant, ()),
        (1.5, dec_project, ()),
        (2.5, dec_mix, ()),
        (2.6, dec_ffn(0), (DU0,)),
        (2.0, dec_ffn(1), (DD0, DD1, DU1)),
        (0.7, dec_ffn_end, ()),
        (1.2, dec_out, ()),
        (1.6, attention_pairs(0, pairs // 2), ()),
        (1.6, attention_pairs(pairs // 2, pairs), ()),
        (0.6, dec_in(0), (DA0,)),
        (0.6, dec_in(1), (DA1,)),
        (0.8, dec_in(2), (DA2,)),
        (1.5, enc_project, ()),
        (2.5, enc_mix, ()),
        (2.2, enc_ffn, ()),
        (2.0, quantizer, (BOOKS, MISC)),
        (2.0, enc_ffn_back(0), (EU0,)),
        (1.6, enc_ffn_back(1), (EU1, ED0, ED1, ED2)),
        (0.4, enc_ffn_back_end, ()),
        (1.2, enc_out, (EA0,)),
        (1.6, attention_pairs(0, pairs // 2), ()),
        (1.6, attention_pairs(pairs // 2, pairs), ()),
        (0.6, enc_in(0), (EA1,)),
        (0.6, enc_in(1), (EA2,)),
        (1.0, enc_in(2), (EA3,)),
    ]
    if not chunks:
        for _, run, _ in work:
            run()
            if run is quantizer:
                all_books()
        return
    actions = plan(chunks, work, bits, rows * code_width * 2)

    def finish(name, stage):
        if name == BOOKS:
            finish_books(stage)
        else:
            sums.finish(name, stage, r.recv[name][stage - 1] if stage else t[name])

    for (_, run, made), acts in zip(work, actions):
        run()
        for name in made:
            if name != BOOKS:
                sums.send_half(name, 0, t[name])
        for name, stage in acts:
            finish(name, stage)
    for name, stage in actions[-1]:
        finish(name, stage)
    sums.drain()


POUT, PIN, CODES = 1, 2, 3
DISTILL_GRAD = "di"
DD0, DD1, DU0, DU1, DA0, DA1, DA2, MISC = "dd0", "dd1", "du0", "du1", "da0", "da1", "da2", "misc"
EU0, EU1, ED0, ED1, ED2 = "eu0", "eu1", "ed0", "ed1", "ed2"
EA0, EA1, EA2, EA3 = "ea0", "ea1", "ea2", "ea3"


def step(given, devices, with_sums):
    rows, width = given.tokens.shape
    ff = given.enc_up.shape[1]
    levels, entries, code_width = given.books.shape
    given.books = given.books.reshape(levels, -1, rows, code_width)
    bits = devices.bit_length() - 1
    vmem, hbm = pl.BlockSpec(memory_space=pltpu.VMEM), pl.BlockSpec(memory_space=pl.ANY)
    scratch = layer_scratch(rows, width, ff)
    scratch.update(
        w_qkv_e=pltpu.VMEM((width, 3 * width), BF16),
        w_out_e=pltpu.VMEM((width, width), BF16),
        cos=pltpu.VMEM((rows, PAIR), F32),
        sin=pltpu.VMEM((rows, PAIR), F32),
        bias=pltpu.VMEM((rows, rows), F32),
        ring=pltpu.VMEM((4,) + given.books.shape[1:], BF16),
        code_rows=pltpu.VMEM((levels, 8, rows), jnp.int32),
        chosen=pltpu.VMEM((levels, rows, code_width), BF16),
        ac=pltpu.VMEM((rows, code_width), BF16),
        gquant=pltpu.VMEM((rows, width), BF16),
        gy=pltpu.VMEM((rows, width), F32),
        latent=pltpu.VMEM((rows, width), BF16),
        pin_v=pltpu.VMEM((2, width, code_width), BF16),
        pout_v=pltpu.VMEM((2, code_width, width), BF16),
        distill_v=pltpu.VMEM(given.distill.shape, BF16),
        wavlm_v=pltpu.VMEM((rows, given.wavlm.shape[1]), BF16),
        tokens_v=pltpu.VMEM((rows, width), BF16),
        cotangent_v=pltpu.VMEM((rows, width), BF16),
        sem_move=pltpu.SemaphoreType.DMA((14,)),
        sem_book=pltpu.SemaphoreType.DMA((4,)),
    )
    outs = Refs(decoded=shaped((rows, width), BF16), grad_tokens=shaped((rows, width), F32))
    chunks, first_rows = {}, {}
    params = dict(vmem_limit_bytes=60 * 2**20)
    if with_sums:
        params.update(collective_id=0, has_side_effects=True)
        c, x, y = bits - 2, bits - 1, bits - 3
        b, a = range(y)
        share = width // devices
        low, high = ff // devices, share
        wide, half, blocks = ff // 128, ff // 256, width // 128
        third, quarter = 3 * blocks, blocks // 4
        chunks = dict(
            di=Chunk(
                high,
                width,
                [c, y, x, a, b],
                [
                    Segment(8, 0, 2 * blocks, 0, blocks, 0, high // 2),
                    Segment(8, blocks, 2 * blocks, 0, blocks, high // 2, high // 2),
                ],
            ),
            du0=Chunk(high, ff // 2, [c, y, a, x, b], [Segment(2, 0, wide, 0, half, 0, high)]),
            dd0=Chunk(low, width // 2, [c, a, y, b, x], [Segment(3, 0, blocks, 0, 2 * quarter, 0, low)]),
            dd1=Chunk(low, width // 2, [c, y, x, a, b], [Segment(3, 2 * quarter, blocks, 0, 2 * quarter, 0, low)]),
            du1=Chunk(high, ff // 2, [c, x, y, a, b], [Segment(2, half, wide, 0, half, 0, high)]),
            da0=Chunk(
                high,
                2 * width,
                [c, x, y, a, b],
                [Segment(1, 0, blocks, 0, blocks, 0, high), Segment(0, 0, third, width, blocks, 0, high)],
            ),
            da1=Chunk(high, width, [c, a, x, y, b], [Segment(0, blocks, third, 0, blocks, 0, high)]),
            da2=Chunk(high, width, [c, y, x, a, b], [Segment(0, 2 * blocks, third, 0, blocks, 0, high)]),
            misc=Chunk(
                high,
                2 * width,
                [c, x, y, a, b],
                [
                    Segment(9, 0, blocks, 0, blocks, 0, high),
                    Segment(10, 0, blocks // 2, width, blocks // 2, 0, high),
                    Segment(10, high * blocks // 2, blocks // 2, width + code_width, blocks // 2, 0, high),
                ],
            ),
            eu0=Chunk(high, ff // 2, [c, x, a, y, b], [Segment(6, 0, wide, 0, half, 0, high)]),
            eu1=Chunk(high, ff // 2, [c, x, y, a, b], [Segment(6, half, wide, 0, half, 0, high)]),
            ed0=Chunk(low, width // 2, [c, x, y, a, b], [Segment(7, 0, blocks, 0, 2 * quarter, 0, low)]),
            ed1=Chunk(low, width // 4, [c, y, x, a, b], [Segment(7, 2 * quarter, blocks, 0, quarter, 0, low)]),
            ed2=Chunk(low, width // 4, [c, y, a, b, x], [Segment(7, 3 * quarter, blocks, 0, quarter, 0, low)]),
            ea0=Chunk(high, width, [c, x, y, a, b], [Segment(5, 0, blocks, 0, blocks, 0, high)]),
            ea1=Chunk(high, width, [c, y, x, a, b], [Segment(4, 0, third, 0, blocks, 0, high)]),
            ea2=Chunk(high, width, [c, x, a, y, b], [Segment(4, blocks, third, 0, blocks, 0, high)]),
            ea3=Chunk(
                high,
                width + 128,
                [c, x, y, a, b],
                [Segment(4, 2 * blocks, third, 0, blocks, 0, high), Segment(11, 0, 1, width, 1, 0, 8)],
            ),
        )
        rows_of = [high * 3 * blocks, high * blocks, high * wide, low * blocks] * 2
        rows_of += [high * blocks, high * blocks, high * blocks, 8, entries // 4 * code_width // 128]
        first_rows = {i: sum(rows_of[:i]) for i in range(len(rows_of))}
        first_rows[BOOKS] = first_rows[len(rows_of) - 1]
        copies = len(chunks) * bits + 2 * levels + 3
        scratch.update(
            t={name: pltpu.VMEM(c.shape(bits), BF16) for name, c in chunks.items()},
            recv={
                name: [pltpu.VMEM(c.shape(bits - 1 - stage), BF16) for stage in range(bits)]
                for name, c in chunks.items()
            },
            gains=pltpu.VMEM((4, width), F32),
            dec_gains=pltpu.VMEM((4, width), F32),
            code_got=pltpu.VMEM((levels, 8, rows), jnp.int32),
                book_sum=pltpu.VMEM((entries // 4, code_width), F32),
            book_send=pltpu.VMEM((2, entries // 4, code_width), BF16),
            book_got=pltpu.VMEM((2, entries // 4, code_width), BF16),
            book_last=pltpu.VMEM((entries // 4, code_width), BF16),
            send_sem=pltpu.SemaphoreType.DMA((copies,)),
            recv_sem=pltpu.SemaphoreType.DMA((copies,)),
        )
        outs.packed = shaped((sum(rows_of), 128), F32)
    else:
        outs.update(gains=shaped((4, width), F32), dec_gains=shaped((4, width), F32))
        outs.t = dict(
            enc_qkv=shaped(given.enc_qkv.shape, BF16),
            enc_out=shaped(given.enc_out.shape, BF16),
            enc_up=shaped(given.enc_up.shape, BF16),
            enc_down=shaped(given.enc_down.shape, BF16),
            dec_qkv=shaped(given.enc_qkv.shape, BF16),
            dec_out=shaped(given.enc_out.shape, BF16),
            dec_up=shaped(given.enc_up.shape, BF16),
            dec_down=shaped(given.enc_down.shape, BF16),
            pin=shaped((2 * width, code_width), BF16),
            pout=shaped((2 * code_width, width), BF16),
            books=shaped((levels, entries, code_width), BF16),
            distill=shaped(given.distill.shape, BF16),
        )
    in_specs = dict.fromkeys(given, hbm)
    in_specs.update(
        lengths=pl.BlockSpec(memory_space=pltpu.SMEM), codes=vmem, vectors=vmem
    )
    got = pl.pallas_call(
        functools.partial(step_kernel, chunks, first_rows, bits),
        out_shape={k: pltpu.VMEM(v.shape, v.dtype) for k, v in outs.items()} if with_sums else dict(outs),
        in_specs=[in_specs],
        out_specs=jax.tree.map(lambda _: vmem, dict(outs)),
        scratch_shapes=[dict(scratch)],
        compiler_params=pltpu.CompilerParams(**params),
        name="step",
    )(dict(given))
    got = Refs(got)
    if not with_sums:
        return got
    last = [shaped((rows, 128), F32) for rows in rows_of]
    last[11] = shaped((1, 128), F32)

    def hand_on(packed, decoded, grad, *refs):
        outs, moves = refs[:-1], Moves(refs[-1])
        parts = [packed.at[pl.ds(first_rows[i], ref.shape[0])] for i, ref in enumerate(outs[:-2])]
        leaving = [moves.start(part, ref) for part, ref in zip(parts + [decoded, grad], outs)]
        for move in leaving:
            move.wait()

    return pl.pallas_call(
        hand_on,
        out_shape=last + [outs.decoded, outs.grad_tokens],
        in_specs=[vmem] * 3,
        out_specs=[hbm] * (len(last) + 2),
        scratch_shapes=[pltpu.SemaphoreType.DMA((len(last) + 2,))],
        compiler_params=pltpu.CompilerParams(vmem_limit_bytes=16 * 2**20),
        name="results",
    )(got.packed, got.decoded, got.grad_tokens)


def body(
    tokens,
    wavlm,
    cotangent,
    lengths,
    codes,
    enc_qkv,
    enc_out,
    enc_up,
    enc_down,
    dec_qkv,
    dec_out,
    dec_up,
    dec_down,
    vectors,
    proj_in,
    proj_out,
    codebooks,
    distill_proj,
):
    width = tokens.shape[1]
    devices = lax.axis_size("dp") * lax.axis_size("branch")
    with_sums = devices == 4 * codebooks.shape[0] and width // devices % 16 == 0
    given = Refs(
        tokens=tokens,
        wavlm=wavlm,
        cotangent=cotangent,
        lengths=lengths,
        codes=codes.T,
        enc_qkv=enc_qkv,
        enc_out=enc_out,
        enc_up=enc_up,
        enc_down=enc_down,
        dec_qkv=dec_qkv,
        dec_out=dec_out,
        dec_up=dec_up,
        dec_down=dec_down,
        vectors=vectors,
        pin_own=proj_in,
        pout_own=proj_out,
        books=codebooks,
        distill=distill_proj,
    )
    if with_sums:
        *sums, decoded, grad_tokens = step(given, devices, True)
        sums = [part.reshape(-1) for part in sums]
        order = (4, 5, 6, 7, 0, 1, 2, 3, 11, 10, 9, 12, 8)
        return (decoded, grad_tokens, *[sums[i] for i in order])
    swap = [(0, 1), (1, 0)]
    given.pin_other = lax.ppermute(proj_in, "branch", swap)
    given.pout_other = lax.ppermute(proj_out, "branch", swap)
    s = step(given, devices, False)
    t = Refs(s.t)
    gains = jnp.concatenate([s.gains, s.dec_gains])
    local = [t.enc_qkv, t.enc_out, t.enc_up, t.enc_down, t.dec_qkv, t.dec_out, t.dec_up, t.dec_down]
    local += [gains, t.pin, t.pout, t.books, t.distill]
    sums = [
        lax.psum_scatter(part.astype(F32).reshape(-1), ("dp", "branch"), scatter_dimension=0, tiled=True)
        for part in local
    ]
    return (s.decoded, s.grad_tokens, *sums)


def solution(mesh):
    rows, whole = P(("dp", "branch"), None), P()
    placed = (rows, P("dp", None), rows, rows, P("dp", None)) + (whole,) * 9
    placed += (P("branch", None, None),) * 2 + (whole,) * 2
    return jax.shard_map(
        body,
        mesh=mesh,
        in_specs=placed,
        out_specs=(rows, rows) + (P(("dp", "branch")),) * 13,
        check_vma=False,
    )
```

```python
import functools
import math

import jax
import jax.numpy as jnp
from jax import lax
from jax.experimental import pallas as pl
from jax.experimental.pallas import tpu as pltpu
from jax.sharding import PartitionSpec as P

HEADS = 8
WINDOW = 250
EPS_NORM = 1e-05
EPS_COS = 1e-06
BETA = 0.25
DISTILL = 10.0
ROPE_BASE = 10000.0

MESH = pl.DeviceIdType.MESH
F32 = jnp.float32
BF16 = jnp.bfloat16
TILE = 512
PAIR = 128
HALF = 256


def dot(left, right):
    return lax.dot_general(left, right, (((1,), (0,)), ((), ())), preferred_element_type=F32)


def dot_t(left, right):
    return lax.dot_general(left, right, (((1,), (1,)), ((), ())), preferred_element_type=F32)


def t_dot(left, right):
    return lax.dot_general(left, right, (((0,), (0,)), ((), ())), preferred_element_type=F32)


def iota(shape, dim):
    return lax.broadcasted_iota(jnp.int32, shape, dim)


def aligned(index, size):
    return pl.ds(pl.multiple_of(index * size, size), size)


class Refs(dict):
    __getattr__ = dict.__getitem__
    __setattr__ = dict.__setitem__


class Moves:
    def __init__(self, semaphores):
        self.semaphores, self.count = semaphores, 0

    def start(self, source, target):
        move = pltpu.make_async_copy(source, target, self.semaphores.at[self.count])
        self.count += 1
        move.start()
        return move


def layer_scratch(rows, width, ff):
    return Refs(
        x=pltpu.VMEM((rows, width), F32),
        s1=pltpu.VMEM((rows, 1), F32),
        h=pltpu.VMEM((rows, width), BF16),
        h1t=pltpu.VMEM((width, rows), BF16),
        h2t=pltpu.VMEM((width, rows), BF16),
        rinv=pltpu.VMEM((rows, width), F32),
        qkv=pltpu.VMEM((rows, 3 * width), BF16),
        mix=pltpu.VMEM((rows, width), BF16),
        ao=pltpu.VMEM((rows, width), F32),
        x2=pltpu.VMEM((rows, width), F32),
        s2=pltpu.VMEM((rows, 1), F32),
        act=pltpu.VMEM((rows, ff), BF16),
        dg=pltpu.VMEM((rows, ff), BF16),
        fo=pltpu.VMEM((rows, width), F32),
        grad=pltpu.VMEM((rows, width), BF16),
        gx=pltpu.VMEM((rows, width), F32),
        acc=pltpu.VMEM((rows, width), F32),
        wide=pltpu.VMEM((4, rows, HALF), F32),
        change=pltpu.VMEM((2, rows, rows), BF16),
        w_qkv_v=pltpu.VMEM((width, 3 * width), BF16),
        w_out_v=pltpu.VMEM((width, width), BF16),
        w_up_v=pltpu.VMEM((width, ff), BF16),
        w_down_v=pltpu.VMEM((ff, width), BF16),
    )


def shaped(shape, kind):
    return jax.ShapeDtypeStruct(shape, kind)


def frame_tables(r):
    rows = r.cos.shape[0]
    place = iota((rows, PAIR), 0)
    query, key = iota((rows, rows), 0), iota((rows, rows), 1)
    begin, begin_query = jnp.zeros_like(place), jnp.zeros_like(query)
    edge = 0
    for clip in range(r.lengths.shape[1] - 1):
        edge = edge + r.lengths[0, clip]
        begin = jnp.where(place >= edge, edge, begin)
        begin_query = jnp.where(query >= edge, edge, begin_query)
    allowed = (key >= begin_query) & (key <= query) & (query - key < WINDOW)
    r.bias[...] = jnp.where(allowed, 0.0, -1e30)
    lane = iota((rows, PAIR), 1)
    rate = jnp.exp((lane % 32).astype(F32) * (-math.log(ROPE_BASE) / 32))
    angle = (place - begin).astype(F32) * rate
    r.cos[...] = jnp.cos(angle)
    sine = jnp.sin(angle)
    r.sin[...] = jnp.where(lane % 64 < 32, -sine, sine)


def rotated(value, cosine, sine):
    lane = iota(value.shape, 1)
    swapped = jnp.where(lane % 64 < 32, pltpu.roll(value, PAIR - 32, 1), pltpu.roll(value, 32, 1))
    return value * cosine + swapped * sine


def head_masks(rows):
    low = iota((rows, PAIR), 1) < 64
    return (jnp.where(low, 1.0, 0.0).astype(BF16), jnp.where(low, 0.0, 1.0).astype(BF16))


def row_blocks(rows, step):
    return [slice(i, i + step) for i in range(0, rows, step)]


def attention_project(r, w_qkv, gain):
    rows, width = r.x.shape
    scale = gain(0)
    for at in row_blocks(rows, 64):
        x = r.x[at, :]
        s1 = lax.rsqrt(jnp.mean(x * x, axis=1, keepdims=True) + EPS_NORM)
        r.s1[at, :] = s1
        r.h[at, :] = (x * s1 * scale).astype(BF16)
    for half in range(3 * width // HALF):
        slot, part = half % 4, half // (width // HALF)
        cols = slice(half * HALF, (half + 1) * HALF)
        r.wide[slot] = dot(r.h[...], w_qkv[:, cols])
        for at in row_blocks(rows, 64):
            for p in range(HALF // PAIR):
                value = r.wide[slot, at, p * PAIR : (p + 1) * PAIR]
                if part < 2:
                    value = rotated(value, r.cos[at, :], r.sin[at, :])
                low = value.astype(BF16)
                if part == 0:
                    low = (low.astype(F32) * 0.125).astype(BF16)
                r.qkv[at, half * HALF + p * PAIR : half * HALF + (p + 1) * PAIR] = low
    r.h1t[...] = r.h[...].T


def attention_mix(r, w_out, gain):
    rows, width = r.x.shape
    masks = head_masks(rows)
    low = iota((rows, PAIR), 1) < 64
    pairs = width // PAIR
    for p in range(pairs):
        query = r.qkv[:, p * PAIR : (p + 1) * PAIR]
        key = r.qkv[:, (p + pairs) * PAIR : (p + pairs + 1) * PAIR]
        value = r.qkv[:, (p + 2 * pairs) * PAIR : (p + 2 * pairs + 1) * PAIR]
        outs = []
        for h in range(2):
            head = 2 * p + h
            slot = head % 4
            r.wide[slot] = dot_t(query * masks[h], key)
            for at in row_blocks(rows, 64):
                seen = PAIR if at.stop <= PAIR else rows
                scores = r.wide[slot, at, :seen] + r.bias[at, :seen]
                weights = jnp.exp(scores - jnp.max(scores, axis=1, keepdims=True))
                r.att[head, at, :seen] = weights.astype(BF16)
                if seen < rows:
                    r.att[head, at, seen:] = jnp.zeros((64, rows - seen), BF16)
            outs.append(dot(r.att[head], value * masks[h] + masks[1 - h]))
        inverse = 1.0 / pltpu.roll(jnp.where(low, outs[1], outs[0]), 64, 1)
        r.rinv[:, p * PAIR : (p + 1) * PAIR] = inverse
        r.mix[:, p * PAIR : (p + 1) * PAIR] = (jnp.where(low, outs[0], outs[1]) * inverse).astype(BF16)
    r.ao[...] = dot(r.mix[...], w_out[...])
    scale_one, scale_two = gain(1), gain(2)
    for at in row_blocks(rows, 64):
        x2 = r.x[at, :] + scale_one * r.ao[at, :]
        r.x2[at, :] = x2
        s2 = lax.rsqrt(jnp.mean(x2 * x2, axis=1, keepdims=True) + EPS_NORM)
        r.s2[at, :] = s2
        r.h[at, :] = (x2 * s2 * scale_two).astype(BF16)
    r.h2t[...] = r.h[...].T


def gelu_parts(pre):
    slope = math.sqrt(2.0 / math.pi)
    square = pre * pre
    bent = jnp.tanh(slope * pre * (1.0 + 0.044715 * square))
    half = 0.5 * (1.0 + bent)
    turn = 0.5 * pre * (1.0 - bent * bent) * slope * (1.0 + 3.0 * 0.044715 * square)
    return (pre * half).astype(BF16), half + turn


def ffn_forward(r, w_up, w_down):
    rows, ff = r.act.shape
    for half in range(ff // HALF):
        slot, cols = half % 4, slice(half * HALF, (half + 1) * HALF)
        r.wide[slot] = dot(r.h[...], w_up[:, cols])
        for at in row_blocks(rows, 32):
            act, slope = gelu_parts(r.wide[slot, at, :])
            r.act[at, cols] = act
            r.dg[at, cols] = slope.astype(BF16)
    r.fo[...] = dot(r.act[...], w_down[...])


def ffn_both(r, w_up, w_down, grad_up, grad_down, first, last):
    rows = r.act.shape[0]
    for t in range(first, last):
        cols = slice(t * TILE, (t + 1) * TILE)
        for side in range(TILE // HALF):
            part = slice(t * TILE + side * HALF, t * TILE + (side + 1) * HALF)
            r.wide[side] = dot(r.h[...], w_up[:, part])
            r.wide[2 + side] = dot_t(r.grad[...], w_down[part, :])
            for at in row_blocks(rows, 32):
                act, slope = gelu_parts(r.wide[side, at, :])
                r.act[at, part] = act
                r.dg[at, part] = (r.wide[2 + side, at, :] * slope).astype(BF16)
        grad_up.shift((t - first) * TILE).put(dot(r.h2t[...], r.dg[:, cols]))
        put_rows(grad_down, t_dot(r.act[:, cols], r.grad[...]), t)


def ffn_back_sum(r, w_up):
    r.acc[...] = dot_t(r.dg[...], w_up[...])


def norm_back(stream, inverse, grad):
    mean = jnp.mean(grad * stream, axis=1, keepdims=True)
    return inverse * grad - stream * (inverse * inverse * inverse * mean)


def column_sum(value):
    return jnp.sum(value, axis=0, keepdims=True)


class Place:
    def __init__(self, ref, col=0, chunk=None):
        self.ref, self.col, self.chunk = ref, col, chunk

    def shift(self, by):
        return Place(self.ref, self.col + by, self.chunk)

    def put(self, value):
        value = value.astype(BF16)
        cols = slice(self.col, self.col + value.shape[1])
        if self.chunk is None:
            self.ref[:, cols] = value
            return
        blocks, rows = self.ref.shape[:2]
        for owner in range(blocks):
            self.ref[self.chunk.index(owner), :, cols] = value[owner * rows : (owner + 1) * rows]


def put_rows(places, value, tile):
    value = value.astype(BF16)
    begin = 0
    for place in places:
        part = value[:, begin : begin + place.ref.shape[-1]]
        begin += place.ref.shape[-1]
        if place.chunk is None:
            place.ref[tile * TILE : tile * TILE + TILE, :] = part
            continue
        rows = place.ref.shape[1]
        for i in range(TILE // rows):
            place.ref[place.chunk.index(tile * (TILE // rows) + i)] = part[i * rows : (i + 1) * rows]


def ffn_backward_begin(r, gain, gy_ref):
    scale = gain(3)
    for at in row_blocks(r.grad.shape[0], 64):
        r.grad[at, :] = (scale * gy_ref[at, :].astype(F32)).astype(BF16)


def ffn_backward_tiles(r, w_down, grad_up, grad_down, first, last):
    rows = r.act.shape[0]
    for t in range(first, last):
        cols = slice(t * TILE, (t + 1) * TILE)
        for side in range(TILE // HALF):
            part = slice(t * TILE + side * HALF, t * TILE + (side + 1) * HALF)
            slot = (2 * t + side) % 4
            r.wide[slot] = dot_t(r.grad[...], w_down[part, :])
            for at in row_blocks(rows, 64):
                r.dg[at, part] = (r.wide[slot, at, :] * r.dg[at, part].astype(F32)).astype(BF16)
        put_rows(grad_down, t_dot(r.act[:, cols], r.grad[...]), t)
        grad_up.shift((t - first) * TILE).put(dot(r.h2t[...], r.dg[:, cols]))


def ffn_backward_end(r, gain, gy_ref, gain_out):
    scale = gain(2)
    to_gain = to_scale = 0.0
    for at in row_blocks(r.x2.shape[0], 32):
        gy = gy_ref[at, :].astype(F32)
        to_scale = to_scale + column_sum(gy * r.fo[at, :])
        back, x2, s2 = r.acc[at, :], r.x2[at, :], r.s2[at, :]
        to_gain = to_gain + column_sum(back * x2 * s2)
        r.gx[at, :] = gy + norm_back(x2, s2, back * scale)
    gain_out[3:4, :] = to_scale
    gain_out[2:3, :] = to_gain


def attention_backward_out(r, w_out, gain, grad_out, gain_out):
    scale = gain(1)
    to_scale = 0.0
    for at in row_blocks(r.gx.shape[0], 64):
        gx = r.gx[at, :]
        to_scale = to_scale + column_sum(gx * r.ao[at, :])
        r.grad[at, :] = (scale * gx).astype(BF16)
    gain_out[1:2, :] = to_scale
    grad_out.put(t_dot(r.mix[...], r.grad[...]))
    r.grad[...] = dot_t(r.grad[...], w_out[...]).astype(BF16)


def attention_backward_pairs(r, first, last):
    rows, width = r.x.shape
    masks = head_masks(rows)
    masks_t = [jnp.where((iota((PAIR, rows), 0) < 64) == (h == 0), 1.0, 0.0).astype(BF16) for h in range(2)]
    pairs = width // PAIR
    for p in range(first, last):
        lanes = [slice((p + i * pairs) * PAIR, (p + i * pairs + 1) * PAIR) for i in range(3)]
        query, key, value = (r.qkv[:, at] for at in lanes)
        grad_mixed = (r.grad[:, lanes[0]].astype(F32) * r.rinv[:, lanes[0]]).astype(BF16)
        product = (grad_mixed.astype(F32) * r.mix[:, lanes[0]].astype(F32)).astype(BF16)
        beside = jnp.concatenate([value, jnp.full(value.shape, -1.0, BF16)], axis=1)
        query_t, grad_t = query.T, grad_mixed.T
        to_query = to_key = to_value = 0.0
        for h in range(2):
            head = 2 * p + h
            slot = head % 4
            both = jnp.concatenate([grad_mixed * masks[h], product * masks[h]], axis=1)
            r.wide[slot] = dot_t(both, beside)
            for at in row_blocks(rows, 64):
                r.change[h, at, :] = (r.att[head, at, :].astype(F32) * r.wide[slot, at, :]).astype(BF16)
            to_query = to_query + dot(r.change[h], key * masks[h])
            to_key = to_key + dot(query_t * masks_t[h], r.change[h])
            to_value = to_value + dot(grad_t * masks_t[h], r.att[head])
        cosine, sine = r.cos[...], -r.sin[...]
        r.qkv[:, lanes[0]] = rotated(to_query * 0.125, cosine, sine).astype(BF16)
        r.qkv[:, lanes[1]] = rotated(to_key.T, cosine, sine).astype(BF16)
        r.qkv[:, lanes[2]] = to_value.T.astype(BF16)


def attention_backward_in(r, grad_qkv, part):
    width = r.x.shape[1]
    grad_qkv.put(dot(r.h1t[...], r.qkv[:, part * width : (part + 1) * width]))


def attention_backward_end(r, w_qkv, gain, gain_out):
    r.acc[...] = dot_t(r.qkv[...], w_qkv[...])
    scale = gain(0)
    to_gain = 0.0
    for at in row_blocks(r.x.shape[0], 32):
        back, x, s1 = r.acc[at, :], r.x[at, :], r.s1[at, :]
        to_gain = to_gain + column_sum(back * x * s1)
        r.gx[at, :] = r.gx[at, :] + norm_back(x, s1, back * scale)
    gain_out[0:1, :] = to_gain


class Segment:
    def __init__(self, result, base, stride, col, blocks, row, rows):
        self.result, self.base, self.stride, self.col, self.blocks = result, base, stride, col, blocks
        self.row, self.rows = row, rows


class Chunk:
    def __init__(self, rows, columns, order, segments):
        self.rows, self.columns, self.order, self.segments = rows, columns, order, segments

    def index(self, owner):
        bits = len(self.order)
        return sum((owner >> (bits - 1 - dim) & 1) << (bits - 1 - stage) for stage, dim in enumerate(self.order))

    def shape(self, leading):
        return (2**leading, self.rows, self.columns)

    def bytes(self, bits):
        return 2**bits * self.rows * self.columns * 2


def plan(chunks, work, bits, book_bytes):
    core, x, y = bits - 2, bits - 1, bits - 3
    ends, middle = -1, -2
    free, pending, done = {}, [], []
    now = 0.0

    def carry(link, size, rate=42e3):
        free[link] = max(now, free.get(link, 0.0)) + size / rate
        return free[link]

    def begin(name, stage):
        if name == BOOKS:
            size = 1.2 * 2 ** (bits - 3) * book_bytes
            if stage == 0:
                there = max(carry(y, size), carry(ends, 1.5 * size), carry(middle, 2 * size))
            else:
                there = carry(core, 4 * book_bytes, 400e3) if stage == 1 else carry(x, 2 * book_bytes)
        else:
            dim = chunks[name].order[stage]
            size = chunks[name].bytes(bits) / 2 ** (stage + 1)
            if dim == core:
                there = carry(core, size, 400e3)
            elif dim == x or dim == y:
                there = carry(dim, size)
            else:
                there = carry(ends, size)
                if dim < y - 1:
                    there = max(there, carry(middle, 2 * size))
        pending.append((there + 1.5, name, stage))

    def finish(limit):
        nonlocal now
        acts = []
        while pending:
            pending.sort(key=lambda p: p[0])
            if pending[0][0] + (0.5 if limit < math.inf else 0.0) > limit:
                break
            at, name, stage = pending.pop(0)
            if name == BOOKS:
                cost = (6.0, 0.6, 0.3)[stage]
            else:
                cost = 0.25 + 0.3e-6 * chunks[name].bytes(bits) / 2 ** (stage + 1)
            now = max(now, at) + cost
            limit = max(limit, now)
            acts.append((name, stage))
            if stage + 1 < (3 if name == BOOKS else bits):
                begin(name, stage + 1)
        return acts

    for took, _, names in work:
        now += 0.95 * took
        for name in names:
            begin(name, 0)
        done.append(finish(now))
    done.append(finish(math.inf))
    return done


def store_segment(packed, first, segment, value):
    for i in range(segment.blocks):
        where = pl.ds(first + segment.base + i, segment.rows, stride=segment.stride)
        packed[where, :] = value[
            segment.row : segment.row + segment.rows, segment.col + i * 128 : segment.col + (i + 1) * 128
        ]


class Halving:
    def __init__(self, chunks, bits, recv, packed, first, send_sem, recv_sem):
        self.chunks = chunks
        self.bits, self.recv, self.packed, self.first = bits, recv, packed, first
        self.send_sem, self.recv_sem = send_sem, recv_sem
        self.copies = {}
        dp, branch = lax.axis_index("dp"), lax.axis_index("branch")
        self.mine, self.partner = [], []
        for dim in range(bits - 1):
            weight = 2 ** (bits - 2 - dim)
            bit = dp // weight % 2
            self.mine.append(bit)
            self.partner.append({"dp": dp + weight * (1 - 2 * bit), "branch": branch})
        self.mine.append(branch)
        self.partner.append({"dp": dp, "branch": 1 - branch})

    def near_level(self, other):
        dp = lax.axis_index("dp")
        for i in range(self.bits - 2):
            if other >> i & 1:
                dp = dp + 2 ** (i + 1) * (1 - 2 * self.mine[self.bits - 3 - i])
        return {"dp": dp, "branch": lax.axis_index("branch")}

    def barrier(self):
        semaphore = pltpu.get_barrier_semaphore()
        levels = 2 ** (self.bits - 2)
        targets = self.partner[self.bits - 2 :] + [self.near_level(other) for other in range(1, levels)]
        for target in targets:
            pl.semaphore_signal(semaphore, inc=1, device_id=target, device_id_type=MESH)
        return lambda: pl.semaphore_wait(semaphore, len(targets))

    def half(self, ref, name, stage, other):
        mine = self.mine[self.chunks[name].order[stage]]
        count = 2 ** (self.bits - 1 - stage)
        return ref.at[pl.ds((1 - mine if other else mine) * count, count)]

    def remote(self, source, target, device, *key):
        slot = len(self.copies)
        self.copies[key] = pltpu.make_async_remote_copy(
            src_ref=source,
            dst_ref=target,
            send_sem=self.send_sem.at[slot],
            recv_sem=self.recv_sem.at[slot],
            device_id=device,
            device_id_type=MESH,
        )
        self.copies[key].start()

    def send(self, name, stage, source):
        dim = self.chunks[name].order[stage]
        self.remote(source, self.recv[name][stage], self.partner[dim], name, stage)

    def send_half(self, name, stage, ref):
        self.send(name, stage, self.half(ref, name, stage, True))

    def arrived(self, *key):
        self.copies[key].wait_recv()

    def add(self, name, stage, own):
        chunk = self.chunks[name]
        got = self.recv[name][stage]
        if stage == self.bits - 1:
            value = own[0].astype(F32) + got[0].astype(F32)
            for segment in chunk.segments:
                store_segment(self.packed, self.first[segment.result], segment, value)
            return
        count = 2 ** (self.bits - 1 - stage)
        step = min(count, 4)

        def some(i, carry):
            at = pl.ds(i * step, step)
            got[at] = got[at] + own[at]
            return carry

        lax.fori_loop(0, count // step, some, 0)

    def finish(self, name, stage, before):
        self.arrived(name, stage)
        self.add(name, stage, self.half(before, name, stage, False))
        if stage + 1 < self.bits:
            self.send_half(name, stage + 1, self.recv[name][stage])

    def drain(self):
        for copy in self.copies.values():
            copy.wait_send()


BOOKS = "books"


def quantizer_semantic(r):
    sem_code = r.chosen[0]
    rows, code_width = sem_code.shape
    columns = [slice(i * HALF, (i + 1) * HALF) for i in range(r.distill_v.shape[1] // HALF)]
    for i, cols in enumerate(columns):
        r.wide[i] = dot(sem_code, r.distill_v[:, cols])

    def row_sum(parts):
        return jnp.sum(sum(parts), axis=1, keepdims=True)

    for at in row_blocks(rows, 32):
        prediction = [r.wide[i, at, :] for i in range(len(columns))]
        target = [r.wavlm_v[at, cols].astype(F32) for cols in columns]
        pred_norm = lax.rsqrt(row_sum([p * p for p in prediction]) + EPS_COS)
        target_norm = lax.rsqrt(row_sum([w * w for w in target]) + EPS_COS)
        cosine = row_sum([p * w for p, w in zip(prediction, target)]) * (pred_norm * target_norm)
        from_target = -DISTILL * pred_norm * target_norm
        from_prediction = DISTILL * cosine * pred_norm * pred_norm
        for p, w, cols in zip(prediction, target, columns):
            r.act[at, cols] = (w * from_target + p * from_prediction).astype(BF16)
    grad_pred = r.act[:, : r.distill_v.shape[1]]
    put_distill(r.places.distill, dot(sem_code.T, grad_pred))
    r.gy[:, :code_width] = dot_t(grad_pred, r.distill_v[...])


def quantizer_latent(r):
    levels, rows, code_width = r.chosen.shape
    r.wide[0] = dot_t(r.gquant[...], r.pout_v[0])
    r.wide[1] = dot(r.latent[...], r.pin_v[0])
    r.wide[2] = dot_t(r.gquant[...], r.pout_v[1])
    r.wide[3] = dot(r.latent[...], r.pin_v[1])
    for at in row_blocks(rows, 32):
        grad_sem = r.wide[0, at, :] + r.gy[at, :code_width]
        commit = 2.0 * BETA * (r.wide[1, at, :] - r.chosen[0, at, :].astype(F32))
        r.g_rows[0, at, :] = (grad_sem - commit).astype(BF16)
        r.grad[at, :code_width] = (grad_sem + commit).astype(BF16)
        grad_ac, residual = r.wide[2, at, :], r.wide[3, at, :]
        for level in range(1, levels):
            residual = residual - r.chosen[level, at, :].astype(F32)
        carry = jnp.zeros_like(residual)
        for level in range(levels - 1, 0, -1):
            carry = carry + 2.0 * BETA * residual
            r.g_rows[level, at, :] = (grad_ac - carry).astype(BF16)
            residual = residual + r.chosen[level, at, :].astype(F32)
        r.grad[at, code_width:] = (grad_ac + carry).astype(BF16)


def quantizer_rest(r):
    code_width = r.ac.shape[1]
    latent_t = r.latent[...].T
    put_group(r.places.pout, 0, t_dot(r.chosen[0], r.gquant[...]))
    put_group(r.places.pout, 1, t_dot(r.ac[...], r.gquant[...]))
    put_group(r.places.pin, 0, dot(latent_t, r.grad[:, :code_width]))
    put_group(r.places.pin, 1, dot(latent_t, r.grad[:, code_width:]))
    r.gy[...] = dot_t(r.grad[...], jnp.concatenate([r.pin_v[0], r.pin_v[1]], axis=1))


def put_group(place, group, value):
    target, total = place.ref, value.shape[0]
    value = value.astype(BF16)
    if place.chunk is None:
        target[group * total : (group + 1) * total, :] = value
        return
    blocks, height, columns = target.shape[0] // 2, target.shape[1], value.shape[1]
    for i in range(blocks):
        for part in range(total // blocks // height):
            first = i * (total // blocks) + part * height
            cols = slice(place.col + part * columns, place.col + (part + 1) * columns)
            target[place.chunk.index(group * blocks + i), :, cols] = value[first : first + height]


def put_distill(place, value):
    target = place.ref
    if place.chunk is None:
        target[...] = value.astype(BF16)
        return
    blocks, height = target.shape[:2]
    rows = value.shape[0] // blocks
    columns = value.shape[1] * rows // height
    for i in range(blocks):
        part = value[i * rows : (i + 1) * rows]
        part = jnp.concatenate([part[:, at : at + columns] for at in range(0, value.shape[1], columns)], axis=0)
        target[place.chunk.index(i), :, place.col : place.col + columns] = part.astype(BF16)


def one_hot_rows(codes, first, count):
    row = iota((count, codes.shape[1]), 0)
    return jnp.where(codes - first == row, 1.0, 0.0).astype(BF16)


def pick_codes(r):
    levels, _, entries, code_width = r.books.shape
    entries = entries * r.books.shape[1]
    rows = r.cos.shape[0]
    slots = r.ring.shape[0]
    branch = lax.axis_index("branch")
    own = r.codes[:, pl.ds(pl.multiple_of(branch * rows, rows), rows)]
    r.code_rows[...] = jnp.broadcast_to(own[:, None, :], r.code_rows.shape)
    columns = jnp.concatenate([own.astype(F32), jnp.zeros((PAIR - levels, rows), F32)], axis=0).T
    lane = iota(columns.shape, 1)
    entry = iota((rows, entries), 1)
    r.code_cols[...] = columns
    r.ac_sum[...] = jnp.zeros(r.ac_sum.shape, F32)

    def book(level):
        slot = level % slots
        return pltpu.make_async_copy(r.books.at[level], r.ring.at[slot], r.sem_book.at[slot])

    def pick(level, carry):
        code = jnp.sum(jnp.where(lane == level, r.code_cols[...], 0.0), axis=1, keepdims=True)
        one_hot = jnp.where(entry == code.astype(jnp.int32), 1.0, 0.0).astype(BF16)
        book(level).wait()
        got = dot(one_hot, r.ring[level % slots].reshape(entries, code_width))
        r.chosen[level] = got.astype(BF16)
        r.ac_sum[...] += jnp.where(level > 0, got, 0.0)

        @pl.when(level + slots < levels)
        def _():
            book(level + slots).start()

        return carry

    def begin():
        for level in range(slots):
            book(level).start()

    def run():
        lax.fori_loop(0, levels, pick, 0, unroll=4)
        r.ac[...] = r.ac_sum[...].astype(BF16)

    return begin, run


def step_kernel(chunks, first_rows, bits, ins, outs, scratch):
    r = Refs({**ins, **outs, **scratch})
    t = r.t = Refs(r.t)
    r.att, r.g_rows, r.g_got, r.book_own = (r.ring.at[i] for i in range(4))
    r.ac_sum, r.code_cols = r.acc.at[:, : r.ac.shape[1]], r.gx.at[:, :PAIR]
    branch = lax.axis_index("branch")
    rows, width = r.tokens.shape
    levels, parts, entries, code_width = r.books.shape
    entries = entries * parts
    tiles = r.w_up_v.shape[1] // TILE
    pairs = width // PAIR
    if chunks:
        sums = Halving(chunks, bits, r.recv, r.packed, first_rows, r.send_sem, r.recv_sem)
        mine, level = sums.mine[bits - 2], lax.axis_index("dp") // 2
        wait_barrier = sums.barrier()
    moves = Moves(r.sem_move)
    begin_pick, run_pick = pick_codes(r)
    begin_pick()
    got_pout = [moves.start(r.pout_own.at[0], r.pout_v.at[branch])]
    if chunks:
        wait_barrier()
        sums.remote(r.pout_own.at[0], r.pout_v.at[branch], sums.partner[bits - 1], POUT)
    else:
        got_pout.append(moves.start(r.pout_other.at[0], r.pout_v.at[1 - branch]))
    got_rest = [
        moves.start(r.distill, r.distill_v),
        moves.start(r.wavlm.at[pl.ds(pl.multiple_of(branch * rows, rows), rows)], r.wavlm_v),
    ]
    got_attention, got_ffn, got_cotangent, got_pin, got_tokens, got_attention_two = ([] for _ in range(6))
    frame_tables(r)

    def fetch_rest():
        got_attention.extend([moves.start(r.dec_qkv, r.w_qkv_v), moves.start(r.dec_out, r.w_out_v)])
        got_ffn.extend([moves.start(r.dec_up, r.w_up_v), moves.start(r.dec_down, r.w_down_v)])
        got_cotangent.append(moves.start(r.cotangent, r.cotangent_v))
        got_pin.append(moves.start(r.pin_own.at[0], r.pin_v.at[branch]))
        if not chunks:
            got_pin.append(moves.start(r.pin_other.at[0], r.pin_v.at[1 - branch]))
        got_tokens.append(moves.start(r.tokens, r.tokens_v))
        got_attention_two.extend([moves.start(r.enc_qkv, r.w_qkv_e), moves.start(r.enc_out, r.w_out_e)])

    if chunks:
        def at(name, col=0):
            return Place(t[name], col, chunks[name])

        dec_down, enc_down = [at(DD0), at(DD1)], [at(ED0), at(ED1), at(ED2)]
        place = r.places = Refs(
            dec_up=[at(DU0), at(DU1)],
            dec_out=at(DA0),
            dec_qkv=[at(DA0, width), at(DA1), at(DA2)],
            enc_up=[at(EU0), at(EU1)],
            enc_out=at(EA0),
            enc_qkv=[at(EA1), at(EA2), at(EA3)],
            distill=at(DISTILL_GRAD),
            pout=at(MISC),
            pin=at(MISC, width),
        )
    else:
        dec_down, enc_down = [Place(t.dec_down)], [Place(t.enc_down)]
        place = r.places = Refs(
            dec_up=[Place(t.dec_up, i * tiles // 2 * TILE) for i in range(2)],
            dec_out=Place(t.dec_out),
            dec_qkv=[Place(t.dec_qkv, i * width) for i in range(3)],
            enc_up=[Place(t.enc_up, i * tiles // 2 * TILE) for i in range(2)],
            enc_out=Place(t.enc_out),
            enc_qkv=[Place(t.enc_qkv, i * width) for i in range(3)],
            distill=Place(t.distill),
            pout=Place(t.pout),
            pin=Place(t.pin),
        )

    def core_rows(ref):
        half = ref.shape[0] // 2
        return ref.at[pl.ds(pl.multiple_of(mine * half, half), half)]

    def wait(moves, *other):
        for move in moves:
            move.wait()
        if chunks and other:
            sums.arrived(*other)

    def layer_value(target, gain):
        for at in row_blocks(rows, 64):
            target[at, :] = (r.x2[at, :] + gain(3) * r.fo[at, :]).astype(BF16)

    def dec_gain(i):
        return r.vectors[1, i : i + 1, :]

    def enc_gain(i):
        return r.vectors[0, i : i + 1, :]

    def pick():
        run_pick()
        fetch_rest()

    def semantic():
        wait(got_rest)
        quantizer_semantic(r)

    def quant():
        wait(got_pout, POUT)
        if chunks:
            sums.remote(core_rows(r.pin_own.at[0]), core_rows(r.pin_v.at[branch]), sums.partner[bits - 1], PIN)
        r.x[...] = dot(jnp.concatenate([r.chosen[0], r.ac[...]], axis=1), r.pout_v[...].reshape(-1, width))
        if chunks:
            for other in range(1, levels):
                target = sums.near_level(other)
                sums.remote(r.code_rows.at[target_level(target)], r.code_got.at[other], target, CODES, other)
            r.code_got[0] = r.code_rows[level]

    def target_level(target):
        return next(iter(target.values())) // 2

    def dec_project():
        wait(got_attention)
        attention_project(r, r.w_qkv_v, dec_gain)

    def dec_mix():
        attention_mix(r, r.w_out_v, dec_gain)

    def dec_ffn(half):
        def run():
            if half == 0:
                wait(got_ffn)
                wait(got_cotangent)
                ffn_backward_begin(r, dec_gain, r.cotangent_v)
            first, last = half * tiles // 2, (half + 1) * tiles // 2
            ffn_both(r, r.w_up_v, r.w_down_v, place.dec_up[half], dec_down, first, last)

        return run

    def dec_ffn_end():
        r.fo[...] = dot(r.act[...], r.w_down_v[...])
        layer_value(r.decoded, dec_gain)
        ffn_back_sum(r, r.w_up_v)
        ffn_backward_end(r, dec_gain, r.cotangent_v, r.dec_gains)
        got_ffn[:] = [moves.start(r.enc_up, r.w_up_v), moves.start(r.enc_down, r.w_down_v)]

    def dec_out():
        if chunks:
            sums.arrived(PIN)
            there = core_rows(r.pin_v.at[1 - branch])
            sums.remote(there, there, sums.partner[bits - 2], PIN, 1)
        attention_backward_out(r, r.w_out_v, dec_gain, place.dec_out, r.dec_gains)

    def attention_pairs(first, last):
        return lambda: attention_backward_pairs(r, first, last)

    def dec_in(part):
        return lambda: attention_backward_in(r, place.dec_qkv[part], part)

    def dec_in_end():
        attention_backward_end(r, r.w_qkv_v, dec_gain, r.dec_gains)
        r.gquant[...] = r.gx[...].astype(BF16)

    def enc_project():
        wait(got_tokens)
        r.x[...] = r.tokens_v[...].astype(F32)
        wait(got_attention_two)
        attention_project(r, r.w_qkv_e, enc_gain)

    def enc_mix():
        attention_mix(r, r.w_out_e, enc_gain)

    def enc_ffn():
        wait(got_ffn)
        ffn_forward(r, r.w_up_v, r.w_down_v)
        layer_value(r.latent, enc_gain)

    def quantizer():
        wait(got_pin, PIN, 1)
        quantizer_latent(r)
        if chunks:
            for other in reversed(range(1, levels)):
                target = sums.near_level(other)
                sums.arrived(CODES, other)
                sums.remote(r.g_rows.at[target_level(target)], r.g_got.at[other], target, BOOKS, 0, other)
            r.g_got[0] = r.g_rows[level]
        quantizer_rest(r)

    def book_half(core, put):
        quarter = entries // 4
        for side in range(2):
            r.book_sum[...] = jnp.zeros_like(r.book_sum)
            first = (core * 2 + side) * quarter

            def add(source, carry):
                one_hot = one_hot_rows(r.code_got[source, 0:1, :], first, quarter)
                r.book_sum[...] += dot(one_hot, r.g_got[source])
                return carry

            lax.fori_loop(0, levels, add, 0, unroll=4)
            put(side, r.book_sum[...])

    def finish_books(stage):
        blocks = entries // 4 // rows
        other_core, other_side = sums.partner[bits - 2], sums.partner[bits - 1]
        if stage == 0:
            for other in range(1, levels):
                sums.arrived(BOOKS, 0, other)

            def put(side, value):
                r.book_send[side] = value.astype(BF16)

            def keep(side, value):
                r.book_own[side * blocks : (side + 1) * blocks] = value.astype(BF16).reshape((blocks, rows, code_width))

            book_half(1 - mine, put)
            sums.remote(r.book_send, r.book_got, other_core, BOOKS, 1)
            book_half(mine, keep)
        elif stage == 1:
            sums.arrived(BOOKS, 1)
            for side in range(2):
                own = r.book_own[side * blocks : (side + 1) * blocks]
                r.book_got[side] = r.book_got[side] + own.reshape(r.book_got.shape[1:])
            sums.remote(r.book_got.at[1 - branch], r.book_last, other_side, BOOKS, 2)
        else:
            sums.arrived(BOOKS, 2)
            total = r.book_got[branch].astype(F32) + r.book_last[...].astype(F32)
            blocks = code_width // 128
            store_segment(r.packed, first_rows[BOOKS], Segment(BOOKS, 0, blocks, 0, blocks, 0, entries // 4), total)

    def all_books():
        parts = entries // TILE

        def one(step, carry):
            at = step // parts
            one_hot = one_hot_rows(r.code_rows[at, 0:1, :], step % parts * TILE, TILE)
            t.books[at, aligned(step % parts, TILE), :] = dot(one_hot, r.g_rows[at]).astype(BF16)
            return carry

        lax.fori_loop(0, levels * parts, one, 0)

    def enc_ffn_back(half):
        def run():
            first, last = half * tiles // 2, (half + 1) * tiles // 2
            if half == 0:
                ffn_backward_begin(r, enc_gain, r.gy)
            ffn_backward_tiles(r, r.w_down_v, place.enc_up[half], enc_down, first, last)

        return run

    def enc_ffn_back_end():
        ffn_back_sum(r, r.w_up_v)
        ffn_backward_end(r, enc_gain, r.gy, r.gains)

    def enc_out():
        attention_backward_out(r, r.w_out_e, enc_gain, place.enc_out, r.gains)

    def enc_in(part):
        def run():
            attention_backward_in(r, place.enc_qkv[part], part)
            if part == 2:
                attention_backward_end(r, r.w_qkv_e, enc_gain, r.gains)
                r.grad_tokens[...] = r.gx[...]
                if chunks:
                    spread_gains()

        return run

    def spread_gains():
        last, height = chunks[EA3], t.ea3.shape[1]
        for layer, ref in enumerate((r.gains, r.dec_gains)):
            for row in range(4):
                for block in range(width // 128):
                    owner = (layer * 4 + row) * (width // 128) + block
                    value = jnp.broadcast_to(ref[row : row + 1, block * 128 : (block + 1) * 128], (height, 128))
                    t.ea3[last.index(owner), :, width : width + 128] = value.astype(BF16)

    work = [
        (6.5, pick, ()),
        (2.0, semantic, (DISTILL_GRAD,)),
        (0.7, quant, ()),
        (1.5, dec_project, ()),
        (2.5, dec_mix, ()),
        (2.6, dec_ffn(0), (DU0,)),
        (2.0, dec_ffn(1), (DD0, DD1, DU1)),
        (0.7, dec_ffn_end, ()),
        (1.2, dec_out, ()),
        (1.6, attention_pairs(0, pairs // 2), ()),
        (1.6, attention_pairs(pairs // 2, pairs), ()),
        (0.6, dec_in(0), (DA0,)),
        (0.6, dec_in(1), (DA1,)),
        (0.4, dec_in(2), (DA2,)),
        (0.4, dec_in_end, ()),
        (1.5, enc_project, ()),
        (2.5, enc_mix, ()),
        (2.2, enc_ffn, ()),
        (2.0, quantizer, (BOOKS, MISC)),
        (2.0, enc_ffn_back(0), (EU0,)),
        (1.6, enc_ffn_back(1), (EU1, ED0, ED1, ED2)),
        (0.4, enc_ffn_back_end, ()),
        (1.2, enc_out, (EA0,)),
        (1.6, attention_pairs(0, pairs // 2), ()),
        (1.6, attention_pairs(pairs // 2, pairs), ()),
        (0.6, enc_in(0), (EA1,)),
        (0.6, enc_in(1), (EA2,)),
        (1.0, enc_in(2), (EA3,)),
    ]
    if not chunks:
        for _, run, _ in work:
            run()
            if run is quantizer:
                all_books()
        return
    actions = plan(chunks, work, bits, rows * code_width * 2)

    def finish(name, stage):
        if name == BOOKS:
            finish_books(stage)
        else:
            sums.finish(name, stage, r.recv[name][stage - 1] if stage else t[name])

    for (_, run, made), acts in zip(work, actions):
        run()
        for name in made:
            if name != BOOKS:
                sums.send_half(name, 0, t[name])
        for name, stage in acts:
            finish(name, stage)
    for name, stage in actions[-1]:
        finish(name, stage)
    sums.drain()


POUT, PIN, CODES = 1, 2, 3
DISTILL_GRAD = "di"
DD0, DD1, DU0, DU1, DA0, DA1, DA2, MISC = "dd0", "dd1", "du0", "du1", "da0", "da1", "da2", "misc"
EU0, EU1, ED0, ED1, ED2 = "eu0", "eu1", "ed0", "ed1", "ed2"
EA0, EA1, EA2, EA3 = "ea0", "ea1", "ea2", "ea3"


def step(given, devices, with_sums):
    rows, width = given.tokens.shape
    ff = given.enc_up.shape[1]
    levels, entries, code_width = given.books.shape
    given.books = given.books.reshape(levels, -1, rows, code_width)
    bits = devices.bit_length() - 1
    vmem, hbm = pl.BlockSpec(memory_space=pltpu.VMEM), pl.BlockSpec(memory_space=pl.ANY)
    scratch = layer_scratch(rows, width, ff)
    scratch.update(
        w_qkv_e=pltpu.VMEM((width, 3 * width), BF16),
        w_out_e=pltpu.VMEM((width, width), BF16),
        cos=pltpu.VMEM((rows, PAIR), F32),
        sin=pltpu.VMEM((rows, PAIR), F32),
        bias=pltpu.VMEM((rows, rows), F32),
        ring=pltpu.VMEM((4,) + given.books.shape[1:], BF16),
        code_rows=pltpu.VMEM((levels, 8, rows), jnp.int32),
        chosen=pltpu.VMEM((levels, rows, code_width), BF16),
        ac=pltpu.VMEM((rows, code_width), BF16),
        gquant=pltpu.VMEM((rows, width), BF16),
        gy=pltpu.VMEM((rows, width), F32),
        latent=pltpu.VMEM((rows, width), BF16),
        pin_v=pltpu.VMEM((2, width, code_width), BF16),
        pout_v=pltpu.VMEM((2, code_width, width), BF16),
        distill_v=pltpu.VMEM(given.distill.shape, BF16),
        wavlm_v=pltpu.VMEM((rows, given.wavlm.shape[1]), BF16),
        tokens_v=pltpu.VMEM((rows, width), BF16),
        cotangent_v=pltpu.VMEM((rows, width), BF16),
        sem_move=pltpu.SemaphoreType.DMA((14,)),
        sem_book=pltpu.SemaphoreType.DMA((4,)),
    )
    outs = Refs(decoded=shaped((rows, width), BF16), grad_tokens=shaped((rows, width), F32))
    chunks, first_rows = {}, {}
    params = dict(vmem_limit_bytes=60 * 2**20)
    if with_sums:
        params.update(collective_id=0, has_side_effects=True)
        c, x, y = bits - 2, bits - 1, bits - 3
        b, a = range(y)
        share = width // devices
        low, high = ff // devices, share
        wide, half, blocks = ff // 128, ff // 256, width // 128
        third, quarter = 3 * blocks, blocks // 4
        chunks = dict(
            di=Chunk(
                high,
                width,
                [c, y, x, a, b],
                [
                    Segment(8, 0, 2 * blocks, 0, blocks, 0, high // 2),
                    Segment(8, blocks, 2 * blocks, 0, blocks, high // 2, high // 2),
                ],
            ),
            du0=Chunk(high, ff // 2, [c, y, a, x, b], [Segment(2, 0, wide, 0, half, 0, high)]),
            dd0=Chunk(low, width // 2, [c, a, y, b, x], [Segment(3, 0, blocks, 0, 2 * quarter, 0, low)]),
            dd1=Chunk(low, width // 2, [c, y, x, a, b], [Segment(3, 2 * quarter, blocks, 0, 2 * quarter, 0, low)]),
            du1=Chunk(high, ff // 2, [c, x, y, a, b], [Segment(2, half, wide, 0, half, 0, high)]),
            da0=Chunk(
                high,
                2 * width,
                [c, x, y, a, b],
                [Segment(1, 0, blocks, 0, blocks, 0, high), Segment(0, 0, third, width, blocks, 0, high)],
            ),
            da1=Chunk(high, width, [c, a, x, y, b], [Segment(0, blocks, third, 0, blocks, 0, high)]),
            da2=Chunk(high, width, [c, y, x, a, b], [Segment(0, 2 * blocks, third, 0, blocks, 0, high)]),
            misc=Chunk(
                high,
                2 * width,
                [c, x, y, a, b],
                [
                    Segment(9, 0, blocks, 0, blocks, 0, high),
                    Segment(10, 0, blocks // 2, width, blocks // 2, 0, high),
                    Segment(10, high * blocks // 2, blocks // 2, width + code_width, blocks // 2, 0, high),
                ],
            ),
            eu0=Chunk(high, ff // 2, [c, x, a, y, b], [Segment(6, 0, wide, 0, half, 0, high)]),
            eu1=Chunk(high, ff // 2, [c, x, y, a, b], [Segment(6, half, wide, 0, half, 0, high)]),
            ed0=Chunk(low, width // 2, [c, x, y, a, b], [Segment(7, 0, blocks, 0, 2 * quarter, 0, low)]),
            ed1=Chunk(low, width // 4, [c, y, x, a, b], [Segment(7, 2 * quarter, blocks, 0, quarter, 0, low)]),
            ed2=Chunk(low, width // 4, [c, y, a, b, x], [Segment(7, 3 * quarter, blocks, 0, quarter, 0, low)]),
            ea0=Chunk(high, width, [c, x, y, a, b], [Segment(5, 0, blocks, 0, blocks, 0, high)]),
            ea1=Chunk(high, width, [c, y, x, a, b], [Segment(4, 0, third, 0, blocks, 0, high)]),
            ea2=Chunk(high, width, [c, x, a, y, b], [Segment(4, blocks, third, 0, blocks, 0, high)]),
            ea3=Chunk(
                high,
                width + 128,
                [c, x, y, a, b],
                [Segment(4, 2 * blocks, third, 0, blocks, 0, high), Segment(11, 0, 1, width, 1, 0, 8)],
            ),
        )
        rows_of = [high * 3 * blocks, high * blocks, high * wide, low * blocks] * 2
        rows_of += [high * blocks, high * blocks, high * blocks, 8, entries // 4 * code_width // 128]
        first_rows = {i: sum(rows_of[:i]) for i in range(len(rows_of))}
        first_rows[BOOKS] = first_rows[len(rows_of) - 1]
        copies = len(chunks) * bits + 2 * levels + 3
        scratch.update(
            t={name: pltpu.VMEM(c.shape(bits), BF16) for name, c in chunks.items()},
            recv={
                name: [pltpu.VMEM(c.shape(bits - 1 - stage), BF16) for stage in range(bits)]
                for name, c in chunks.items()
            },
            gains=pltpu.VMEM((4, width), F32),
            dec_gains=pltpu.VMEM((4, width), F32),
            code_got=pltpu.VMEM((levels, 8, rows), jnp.int32),
                book_sum=pltpu.VMEM((entries // 4, code_width), F32),
            book_send=pltpu.VMEM((2, entries // 4, code_width), BF16),
            book_got=pltpu.VMEM((2, entries // 4, code_width), BF16),
            book_last=pltpu.VMEM((entries // 4, code_width), BF16),
            send_sem=pltpu.SemaphoreType.DMA((copies,)),
            recv_sem=pltpu.SemaphoreType.DMA((copies,)),
        )
        outs.packed = shaped((sum(rows_of), 128), F32)
    else:
        outs.update(gains=shaped((4, width), F32), dec_gains=shaped((4, width), F32))
        outs.t = dict(
            enc_qkv=shaped(given.enc_qkv.shape, BF16),
            enc_out=shaped(given.enc_out.shape, BF16),
            enc_up=shaped(given.enc_up.shape, BF16),
            enc_down=shaped(given.enc_down.shape, BF16),
            dec_qkv=shaped(given.enc_qkv.shape, BF16),
            dec_out=shaped(given.enc_out.shape, BF16),
            dec_up=shaped(given.enc_up.shape, BF16),
            dec_down=shaped(given.enc_down.shape, BF16),
            pin=shaped((2 * width, code_width), BF16),
            pout=shaped((2 * code_width, width), BF16),
            books=shaped((levels, entries, code_width), BF16),
            distill=shaped(given.distill.shape, BF16),
        )
    in_specs = dict.fromkeys(given, hbm)
    in_specs.update(
        lengths=pl.BlockSpec(memory_space=pltpu.SMEM), codes=vmem, vectors=vmem
    )
    got = pl.pallas_call(
        functools.partial(step_kernel, chunks, first_rows, bits),
        out_shape={k: pltpu.VMEM(v.shape, v.dtype) for k, v in outs.items()} if with_sums else dict(outs),
        in_specs=[in_specs],
        out_specs=jax.tree.map(lambda _: vmem, dict(outs)),
        scratch_shapes=[dict(scratch)],
        compiler_params=pltpu.CompilerParams(**params),
        name="step",
    )(dict(given))
    got = Refs(got)
    if not with_sums:
        return got
    last = [shaped((rows, 128), F32) for rows in rows_of]
    last[11] = shaped((1, 128), F32)

    def hand_on(packed, decoded, grad, *refs):
        outs, moves = refs[:-1], Moves(refs[-1])
        parts = [packed.at[pl.ds(first_rows[i], ref.shape[0])] for i, ref in enumerate(outs[:-2])]
        leaving = [moves.start(part, ref) for part, ref in zip(parts + [decoded, grad], outs)]
        for move in leaving:
            move.wait()

    return pl.pallas_call(
        hand_on,
        out_shape=last + [outs.decoded, outs.grad_tokens],
        in_specs=[vmem] * 3,
        out_specs=[hbm] * (len(last) + 2),
        scratch_shapes=[pltpu.SemaphoreType.DMA((len(last) + 2,))],
        compiler_params=pltpu.CompilerParams(vmem_limit_bytes=16 * 2**20),
        name="results",
    )(got.packed, got.decoded, got.grad_tokens)


def body(
    tokens,
    wavlm,
    cotangent,
    lengths,
    codes,
    enc_qkv,
    enc_out,
    enc_up,
    enc_down,
    dec_qkv,
    dec_out,
    dec_up,
    dec_down,
    vectors,
    proj_in,
    proj_out,
    codebooks,
    distill_proj,
):
    width = tokens.shape[1]
    devices = lax.axis_size("dp") * lax.axis_size("branch")
    with_sums = devices == 4 * codebooks.shape[0] and width // devices % 16 == 0
    given = Refs(
        tokens=tokens,
        wavlm=wavlm,
        cotangent=cotangent,
        lengths=lengths,
        codes=codes.T,
        enc_qkv=enc_qkv,
        enc_out=enc_out,
        enc_up=enc_up,
        enc_down=enc_down,
        dec_qkv=dec_qkv,
        dec_out=dec_out,
        dec_up=dec_up,
        dec_down=dec_down,
        vectors=vectors,
        pin_own=proj_in,
        pout_own=proj_out,
        books=codebooks,
        distill=distill_proj,
    )
    if with_sums:
        *sums, decoded, grad_tokens = step(given, devices, True)
        sums = [part.reshape(-1) for part in sums]
        order = (4, 5, 6, 7, 0, 1, 2, 3, 11, 10, 9, 12, 8)
        return (decoded, grad_tokens, *[sums[i] for i in order])
    swap = [(0, 1), (1, 0)]
    given.pin_other = lax.ppermute(proj_in, "branch", swap)
    given.pout_other = lax.ppermute(proj_out, "branch", swap)
    s = step(given, devices, False)
    t = Refs(s.t)
    gains = jnp.concatenate([s.gains, s.dec_gains])
    local = [t.enc_qkv, t.enc_out, t.enc_up, t.enc_down, t.dec_qkv, t.dec_out, t.dec_up, t.dec_down]
    local += [gains, t.pin, t.pout, t.books, t.distill]
    sums = [
        lax.psum_scatter(part.astype(F32).reshape(-1), ("dp", "branch"), scatter_dimension=0, tiled=True)
        for part in local
    ]
    return (s.decoded, s.grad_tokens, *sums)


def solution(mesh):
    rows, whole = P(("dp", "branch"), None), P()
    placed = (rows, P("dp", None), rows, rows, P("dp", None)) + (whole,) * 9
    placed += (P("branch", None, None),) * 2 + (whole,) * 2
    return jax.shard_map(
        body,
        mesh=mesh,
        in_specs=placed,
        out_specs=(rows, rows) + (P(("dp", "branch")),) * 13,
        check_vma=False,
    )
```
